32 devices in a mesh: seq: 2 (over x), dp: 16 (over z, y, core).
Axes of the slice: x: 2, y: 2, z: 4, core: 2. Of those that a mesh axis runs over, the one named last changes fastest.
Arguments:
- layer_in: bfloat16 [32, 768, 768], P('dp', 'seq'), may hold values from -6 to 6
- segment: int32 [32, 768], P('dp', 'seq'), may hold values from -1 to 32, as said below
- key_mask: int32 [32, 768], P('dp', 'seq'), may hold values from 0 to 1, as said below
- position: int32 [32, 768], P('dp', 'seq'), may hold values from 0 to 196, as said below
- layout_x: int32 [32, 768], P('dp', 'seq'), may hold values from 0 to 47
- layout_y: int32 [32, 768], P('dp', 'seq'), may hold values from 0 to 47
- qkv_weight: bfloat16 [768, 2304], replicated, may hold values from -0.21875 to 0.21875
- query_bias: bfloat16 [768], replicated, may hold values from -3 to 3
- value_bias: bfloat16 [768], replicated, may hold values from -3 to 3
- out_weight: bfloat16 [768, 768], replicated, may hold values from -0.875 to 0.875
- out_bias: bfloat16 [768], replicated, may hold values from -3 to 3
- attn_gain: bfloat16 [768], replicated, may hold values from 0.5 to 1.5
- attn_shift: bfloat16 [768], replicated, may hold values from -3 to 3
- up_weight: bfloat16 [768, 3072], replicated, may hold values from -0.21875 to 0.21875
- up_bias: bfloat16 [3072], replicated, may hold values from -3 to 3
- down_weight: bfloat16 [3072, 768], replicated, may hold values from -0.109375 to 0.109375
- down_bias: bfloat16 [768], replicated, may hold values from -3 to 3
- ffn_gain: bfloat16 [768], replicated, may hold values from 0.5 to 1.5
- ffn_shift: bfloat16 [768], replicated, may hold values from -3 to 3
- text_table: bfloat16 [33, 12], replicated, may hold values from -3 to 3
- horiz_table: bfloat16 [33, 12], replicated, may hold values from -3 to 3
- vert_table: bfloat16 [33, 12], replicated, may hold values from -3 to 3
- cotangent: bfloat16 [32, 768, 768], P('dp', 'seq'), may hold values from -6 to 6
Outputs:
- layer_out: bfloat16 [32, 768, 768], P('dp', 'seq')
- grad_input: float32 [32, 768, 768], P('dp', 'seq')
- grad_qkv: float32 [768, 2304], replicated
- grad_query_bias: float32 [768], replicated
- grad_value_bias: float32 [768], replicated
- grad_out_weight: float32 [768, 768], replicated
- grad_out_bias: float32 [768], replicated
- grad_attn_gain: float32 [768], replicated
- grad_attn_shift: float32 [768], replicated
- grad_up_weight: float32 [768, 3072], replicated
- grad_up_bias: float32 [3072], replicated
- grad_down_weight: float32 [3072, 768], replicated
- grad_down_bias: float32 [768], replicated
- grad_ffn_gain: float32 [768], replicated
- grad_ffn_shift: float32 [768], replicated
- grad_text_table: float32 [33, 12], replicated
- grad_horiz_table: float32 [33, 12], replicated
- grad_vert_table: float32 [33, 12], replicated
The draws below stay inside these ranges and needn't reach their ends.
Inputs may be any that keep to these rules, and one draw needn't show every extreme that they name: `segment`: rows 0 to 511 of an item hold forms with consecutive positive numbers rising in row order, each form of at most 64 rows, the last used form of every item numbered 512 // 16; then unused text rows marked -1; at least 448 text rows are used. Rows 512 to 708 are image patches marked 0, the remaining rows are padding marked -1. `key_mask`: 1 exactly where segment is not -1. `position`: the row's index within its form on text rows, the patch index on image rows, 0 on unused rows.
All inputs are finite; a program needn't handle non-finite values.
Results may differ from the reference program's by a relative error of at most 0.014.
Values may be sent and summed in bfloat16 or wider, within the bound.
A program may use at most 320 MiB of HBM per device.

```python
import jax
import jax.numpy as jnp
from jax import lax

D = 768
HEADS = 12
HEAD = 64
FF = 3072
TEXT = 512
IMG = 197
ROWS = 768
FORM = 64
REACH1 = 16
REACH2 = 16
ITEMS = 32
NB1 = 33
NB2 = 33


def layout(key):
    first_key, second_key = jax.random.split(key)
    used_rows = TEXT - jax.random.randint(first_key, (ITEMS, 1), 0, TEXT // 8 + 1)
    form_count = TEXT // (FORM // 4) + 1
    top_number = TEXT // (FORM // 4)
    lengths = jax.random.randint(second_key, (ITEMS, form_count), FORM // 4, FORM + 1)
    form_ends = jnp.cumsum(lengths, axis=1)
    form_starts = form_ends - lengths
    row_index = jnp.arange(ROWS, dtype=jnp.int32)[None, :]
    form_number = jnp.sum((form_ends[:, None, :] <= row_index[:, :, None]).astype(jnp.int32), axis=2)
    form_number = jnp.minimum(form_number, form_count - 1)
    form_begin = jnp.take_along_axis(form_starts, form_number, axis=1)
    last_number = jnp.take_along_axis(form_number, used_rows - 1, axis=1)
    is_text = row_index < used_rows
    is_image = (row_index >= TEXT) & (row_index < TEXT + IMG)
    text_number = form_number + top_number - last_number
    segment = jnp.where(is_text, text_number, jnp.where(is_image, 0, -1))
    position = jnp.where(is_text, row_index - form_begin, jnp.where(is_image, row_index - TEXT, 0))
    return (segment.astype(jnp.int32), position.astype(jnp.int32))


def draw_segment(key, part):
    segment, position = layout(key)
    return segment


def draw_key_mask(key, part):
    segment, position = layout(key)
    return (segment >= 0).astype(jnp.int32)


def draw_position(key, part):
    segment, position = layout(key)
    return position


def with_ends(values, stream_key, least, top_value):
    spot = [jax.random.randint(jax.random.fold_in(stream_key, axis), (), 0, length) for axis, length in enumerate(values.shape)]
    longest = values.shape.index(max(values.shape))
    beside = spot[:longest] + [(spot[longest] + 1) % values.shape[longest]] + spot[longest + 1:]
    return values.at[tuple(spot)].set(least).at[tuple(beside)].set(top_value)


def steps_of(stream_key, shape, shards, low, top_value):
    loudness = 1.0
    for dim, blocks in shards:
        draws = jax.random.uniform(jax.random.fold_in(jax.random.fold_in(stream_key, 6), dim), (blocks,), jnp.float32, low / len(shards), top_value / len(shards))
        loudness = loudness * jnp.repeat(jnp.exp(draws), shape[dim] // blocks).reshape((-1,) + (1,) * (len(shape) - 1 - dim))
    return loudness


def gaussian(key, extent, scale, reach, shards=(), held_as=jnp.bfloat16):
    values = jax.random.normal(key, extent, jnp.float32) * scale
    if len(shards) > 0:
        values = steps_of(key, extent, shards, -0.22, 0.18) * values
    return jnp.clip(values, min=-reach, max=reach).astype(held_as)


def setup_inputs(seed: int = 0) -> dict:
    arg_keys = jax.random.split(jax.random.key(seed), 24)
    return {
        "layer_in": gaussian(arg_keys[0], (ITEMS, ROWS, D), 1.0, 6.0, ((0, 16), (1, 2))),
        "segment": draw_segment(jax.random.fold_in(arg_keys[23], 71), 0),
        "key_mask": draw_key_mask(jax.random.fold_in(arg_keys[23], 71), 0),
        "position": draw_position(jax.random.fold_in(arg_keys[23], 71), 0),
        "layout_x": with_ends(jax.random.randint(arg_keys[4], (ITEMS, ROWS), 0, 48), jax.random.fold_in(arg_keys[4], 1), 0, 47).astype(jnp.int32),
        "layout_y": with_ends(jax.random.randint(arg_keys[5], (ITEMS, ROWS), 0, 48), jax.random.fold_in(arg_keys[5], 1), 0, 47).astype(jnp.int32),
        "qkv_weight": gaussian(arg_keys[6], (D, 3 * D), D ** -0.5, 0.21875),
        "query_bias": gaussian(arg_keys[7], (D,), 0.5, 3.0),
        "value_bias": gaussian(arg_keys[8], (D,), 0.5, 3.0),
        "out_weight": gaussian(arg_keys[9], (D, D), (D // 16) ** -0.5, 0.875),
        "out_bias": gaussian(arg_keys[10], (D,), 0.5, 3.0),
        "attn_gain": jnp.clip(1.0 + 0.1 * jax.random.normal(arg_keys[11], (D,), jnp.float32), 0.5, 1.5).astype(jnp.bfloat16),
        "attn_shift": gaussian(arg_keys[12], (D,), 0.5, 3.0),
        "up_weight": gaussian(arg_keys[13], (D, FF), D ** -0.5, 0.21875),
        "up_bias": gaussian(arg_keys[14], (FF,), 0.5, 3.0),
        "down_weight": gaussian(arg_keys[15], (FF, D), FF ** -0.5, 0.109375),
        "down_bias": gaussian(arg_keys[16], (D,), 0.5, 3.0),
        "ffn_gain": jnp.clip(1.0 + 0.1 * jax.random.normal(arg_keys[17], (D,), jnp.float32), 0.5, 1.5).astype(jnp.bfloat16),
        "ffn_shift": gaussian(arg_keys[18], (D,), 0.5, 3.0),
        "text_table": gaussian(arg_keys[19], (NB1, HEADS), 0.5, 3.0),
        "horiz_table": gaussian(arg_keys[20], (NB2, HEADS), 0.5, 3.0),
        "vert_table": gaussian(arg_keys[21], (NB2, HEADS), 0.5, 3.0),
        "cotangent": gaussian(arg_keys[22], (ITEMS, ROWS, D), 1.0, 6.0, ((0, 16), (1, 2))),
    }


@jax.custom_vjp
def low(v):
    return lax.optimization_barrier(v.astype(jnp.bfloat16)).astype(jnp.float32)

@jax.custom_vjp
def low_back(v):
    return v

def low_keep(v):
    return (low(v), None)

def low_pass(kept, grad):
    return (grad,)

def back_keep(v):
    return (v, None)

def back_low(kept, grad):
    return (low(grad),)
low.defvjp(low_keep, low_pass)
low_back.defvjp(back_keep, back_low)
EPSILON = 1e-05
MASKED = -1e+30
PRECISE = lax.Precision.HIGHEST

def norm_rows(hidden, gain, shift):
    center = hidden - lax.optimization_barrier(jnp.mean(hidden, axis=-1, keepdims=True))
    spread = lax.optimization_barrier(jnp.mean(center * center, axis=-1, keepdims=True))
    return center * lax.rsqrt(spread + EPSILON) * gain + shift

def buckets(coord, radius):
    return jnp.clip(coord[:, :, None] - coord[:, None, :], -radius, radius) + radius

def layer(inputs, segment, key_mask, position, layout_x, layout_y, weights):
    qkv_weight, query_bias, value_bias, out_weight, out_bias, attn_gain, attn_shift, up_weight, up_bias, down_weight, down_bias, ffn_gain, ffn_shift, text_table, horiz_table, vert_table = weights
    group_size, row_count, model_width = inputs.shape
    projected = jnp.einsum('grd,de->gre', inputs, qkv_weight, precision=PRECISE)
    queries = low_back(low(projected[..., :D] + query_bias))
    keys_all = low_back(low(projected[..., D:2 * D]))
    values = low_back(low(projected[..., 2 * D:] + value_bias))
    queries = queries.reshape(group_size, row_count, HEADS, HEAD)
    keys_all = keys_all.reshape(group_size, row_count, HEADS, HEAD)
    values = values.reshape(group_size, row_count, HEADS, HEAD)
    raw_dots = low_back(jnp.einsum('gqhe,gkhe->ghqk', queries, keys_all, precision=PRECISE) * HEAD ** (-0.5))
    relative = text_table[buckets(position, REACH1)] + horiz_table[buckets(layout_x, REACH2)] + vert_table[buckets(layout_y, REACH2)]
    scores = raw_dots + jnp.transpose(relative, (0, 3, 1, 2))
    own_seg = segment[:, :, None]
    key_seg = segment[:, None, :]
    allowed = (key_mask[:, None, :] > 0) & ((own_seg == key_seg) | (own_seg == 0) | (key_seg == 0))
    scores = jnp.where(allowed[:, None], scores, MASKED)
    probabilities = jax.nn.softmax(scores, axis=-1)
    mixed_heads = jnp.einsum('ghqk,gkhe->gqhe', low(probabilities), values, precision=PRECISE)
    mixed_rows = low_back(low(mixed_heads.reshape(group_size, row_count, D)))
    attn_out = low_back(jnp.einsum('grd,de->gre', mixed_rows, out_weight, precision=PRECISE) + out_bias)
    normed_one = norm_rows(inputs + attn_out, attn_gain, attn_shift)
    up_pre = low_back(jnp.einsum('grd,df->grf', low(normed_one), up_weight, precision=PRECISE) + up_bias)
    activated = low(jax.nn.gelu(up_pre, approximate=False))
    branch = low_back(jnp.einsum('grf,fd->grd', activated, down_weight, precision=PRECISE) + down_bias)
    return norm_rows(normed_one + branch, ffn_gain, ffn_shift)

def reference(layer_in, segment, key_mask, position, layout_x, layout_y, qkv_weight, query_bias, value_bias, out_weight, out_bias, attn_gain, attn_shift, up_weight, up_bias, down_weight, down_bias, ffn_gain, ffn_shift, text_table, horiz_table, vert_table, cotangent):
    weights = tuple((w.astype(jnp.float32) for w in (qkv_weight, query_bias, value_bias, out_weight, out_bias, attn_gain, attn_shift, up_weight, up_bias, down_weight, down_bias, ffn_gain, ffn_shift, text_table, horiz_table, vert_table)))
    inputs = layer_in.astype(jnp.float32)

    def paired(array):
        return array.reshape((ITEMS // 2, 2) + array.shape[1:])
    integers = tuple((paired(a) for a in (segment, key_mask, position, layout_x, layout_y)))

    def forward(inputs, *weights):

        def one_group(pieces):
            return layer(pieces[0], pieces[1], pieces[2], pieces[3], pieces[4], pieces[5], weights)
        result = lax.map(jax.checkpoint(one_group), (paired(inputs),) + integers)
        return result.reshape(inputs.shape)
    layer_out, pullback = jax.vjp(forward, inputs, *weights)
    grads = pullback(cotangent.astype(jnp.float32))
    return (layer_out.astype(jnp.bfloat16), grads[0], grads[1], grads[2], grads[3], grads[4], grads[5], grads[6], grads[7], grads[8], grads[9], grads[10], grads[11], grads[12], grads[13], grads[14], grads[15], grads[16])
```

```python
import functools

import jax
import jax.numpy as jnp
from jax import lax
from jax.experimental import pallas as pl
from jax.experimental.pallas import tpu as pltpu
from jax.sharding import PartitionSpec as P

BF = jnp.bfloat16
F32 = jnp.float32
BIG = 1e30
LANES = 128
HEAD = 64
TEXT = 512
POS = 64
COORD = 48
Y0 = 64
GROUP0 = 112
MEMBER0 = 116
FLAG = 124
LOG0 = 125
X_TABLE = 33
Y_TABLE = 66
NOTHING = 127


def dot_nt(a, b):
    return lax.dot_general(a, b, (((1,), (1,)), ((), ())), preferred_element_type=F32)


def dot_nn(a, b):
    return lax.dot_general(a, b, (((1,), (0,)), ((), ())), preferred_element_type=F32)


def looked_up(table_row, index):
    rows = index.shape[0]
    return jnp.take_along_axis(jnp.broadcast_to(table_row, (rows, LANES)), index, axis=1)


def bucket(distance):
    return jnp.clip(distance, -16, 16) + 16


def between(lane, low, high):
    return (lane >= low) & (lane < high)


def columns_of(meta_ref):
    return tuple(meta_ref[:, field : field + 1] for field in range(5))


def marks(meta_ref):
    segment, key_mask, position, across, down = columns_of(meta_ref)
    rows = segment.shape[0]
    lane = lax.broadcasted_iota(jnp.int32, (rows, LANES), 1)
    row = lax.broadcasted_iota(jnp.int32, (rows, LANES), 0)
    even = between(lane, HEAD, HEAD + COORD) & (lane - HEAD == across)
    odd = (lane < COORD) & (lane == across)
    group = (segment - 1) >> 3
    member = (segment - 1) & 7
    named = segment > 0
    shared = (
        ((row < TEXT) & (lane < POS) & (lane == position))
        | (between(lane, Y0, Y0 + COORD) & (lane - Y0 == down))
        | (named & between(lane, GROUP0, MEMBER0) & (lane - GROUP0 == group))
        | (named & between(lane, MEMBER0, FLAG) & (lane - MEMBER0 == member))
        | ((lane == FLAG) & (key_mask <= 0))
        | (lane >= LOG0)
    )
    return tuple(jnp.where(m, 1.0, 0.0).astype(BF) for m in (even, odd, shared))


def barred(meta_ref):
    segment = meta_ref[:, 0:1]
    rows = segment.shape[0]
    lane = lax.broadcasted_iota(jnp.int32, (rows, LANES), 1)
    group = (segment - 1) >> 3
    member = (segment - 1) & 7
    shut = (
        ((segment > 0) & between(lane, GROUP0, MEMBER0) & (lane - GROUP0 != group))
        | ((segment < 0) & between(lane, GROUP0, MEMBER0))
        | ((segment > 0) & between(lane, MEMBER0, FLAG) & (lane - MEMBER0 != member))
        | (lane == FLAG)
    )
    return jnp.where(shut, -BIG, 0.0).astype(F32)


def query_index(meta_ref):
    segment, key_mask, position, across, down = columns_of(meta_ref)
    rows = segment.shape[0]
    lane = lax.broadcasted_iota(jnp.int32, (rows, LANES), 1)
    x_even = bucket(across - (lane - HEAD)) + X_TABLE
    x_odd = bucket(across - lane) + X_TABLE
    even = jnp.where(between(lane, HEAD, HEAD + COORD), x_even, NOTHING)
    odd = jnp.where(lane < COORD, x_odd, NOTHING)
    shared = jnp.where(
        lane < POS,
        bucket(position - lane),
        jnp.where(between(lane, Y0, Y0 + COORD), bucket(down - (lane - Y0)) + Y_TABLE, NOTHING),
    )
    return even, odd, shared


def image_key_index(meta_ref):
    position = meta_ref[TEXT:, 2:3]
    lane = lax.broadcasted_iota(jnp.int32, (position.shape[0], LANES), 1)
    return jnp.where(lane < POS, bucket(lane - position), NOTHING)


def prepare(meta_ref, mark_refs, bar_ref, index_refs, key_index_ref):
    for ref, value in zip(mark_refs, marks(meta_ref)):
        ref[...] = value
    bar_ref[...] = barred(meta_ref)
    for ref, value in zip(index_refs, query_index(meta_ref)):
        ref[...] = value
    key_index_ref[...] = image_key_index(meta_ref)


def image_offsets(row_positions, column_positions):
    return bucket(column_positions - row_positions)


def widened(parity, q, k, table_row, mark_refs, bar_ref, index_refs, key_index_ref, logs):
    rows = q.shape[0]
    lane = lax.broadcasted_iota(jnp.int32, (rows, LANES), 1)
    own = (lane < HEAD) if parity == 0 else (lane >= HEAD)
    first = jnp.where(own, q.astype(F32) * 0.125, looked_up(table_row, index_refs[parity][...]))
    second = looked_up(table_row, index_refs[2][...]) + bar_ref[...]
    if logs is not None:
        high = logs.astype(BF).astype(F32)
        middle = (logs - high).astype(BF).astype(F32)
        lowest = logs - high - middle
        second = jnp.where(
            lane == LOG0,
            -high,
            jnp.where(lane == LOG0 + 1, -middle, jnp.where(lane == LOG0 + 2, -lowest, second)),
        )
    first = first.astype(BF)
    second = second.astype(BF)
    mark_second = mark_refs[2][...]
    to_image = jnp.where(lane < POS, mark_second, second)
    key_first = jnp.where(own, k, mark_refs[parity][...])
    image_lane = lane[TEXT:]
    key_image = jnp.where(
        image_lane < POS,
        looked_up(table_row, key_index_ref[...]).astype(BF),
        mark_second[TEXT:],
    )
    q_text = jnp.concatenate([first, second], axis=1)
    q_image = jnp.concatenate([first, to_image], axis=1)
    k_text = jnp.concatenate([key_first[:TEXT], mark_second[:TEXT]], axis=1)
    k_image = jnp.concatenate([key_first[TEXT:], key_image], axis=1)
    return q_text, q_image, k_text, k_image


def image_bias(table_row, offsets):
    return jnp.concatenate(
        [looked_up(table_row, offsets[:, :LANES]), looked_up(table_row, offsets[:, LANES:])], axis=1
    )


def forward_kernel(
    meta_ref, rows_ref, table_ref, q_ref, k_ref, v_ref, mixed_ref, log_ref,
    even_ref, odd_ref, shared_ref, bar_ref, index_even, index_odd, index_shared, key_index_ref,
):
    mark_refs = (even_ref, odd_ref, shared_ref)
    index_refs = (index_even, index_odd, index_shared)

    @pl.when(pl.program_id(0) == 0)
    def _():
        prepare(meta_ref, mark_refs, bar_ref, index_refs, key_index_ref)

    rows = q_ref.shape[0]
    images = rows - TEXT
    q, k, v = q_ref[...], k_ref[...], v_ref[...]
    offsets = bucket(meta_ref[TEXT:, 2:3] - rows_ref[2:3, TEXT:])
    tile = 256
    parts = []
    for parity in range(2):
        table_row = table_ref[parity]
        q_text, q_image, k_text, k_image = widened(
            parity, q, k, table_row, mark_refs, bar_ref, index_refs, key_index_ref, None
        )
        bias = image_bias(table_row, offsets)
        outs = []
        logs = []
        for start in range(0, rows, tile):
            here = slice(start, start + tile)
            on_text = dot_nt(q_text[here], k_text)
            on_image = dot_nt(q_image[here], k_image)
            if start >= TEXT:
                on_image = on_image + bias[start - TEXT : start - TEXT + tile]
            top = jnp.maximum(
                jnp.max(on_text, axis=1, keepdims=True), jnp.max(on_image, axis=1, keepdims=True)
            )
            on_text = jnp.exp(on_text - top)
            on_image = jnp.exp(on_image - top)
            total = jnp.sum(on_text, axis=1, keepdims=True) + jnp.sum(
                on_image, axis=1, keepdims=True
            )
            out = dot_nn(on_text.astype(BF), v[:TEXT]) + dot_nn(on_image.astype(BF), v[TEXT:])
            outs.append(out / total)
            logs.append(jnp.broadcast_to(top + jnp.log(total), (tile, LANES)))
        parts.append((jnp.concatenate(outs, axis=0), jnp.concatenate(logs, axis=0)))
    lane = lax.broadcasted_iota(jnp.int32, (rows, LANES), 1)
    mixed_ref[...] = jnp.where(lane < HEAD, parts[0][0], parts[1][0])
    log_ref[0] = jnp.where(lane < HEAD, parts[0][1], parts[1][1])


def static_scratch(rows):
    return [
        pltpu.VMEM((rows, LANES), BF),
        pltpu.VMEM((rows, LANES), BF),
        pltpu.VMEM((rows, LANES), BF),
        pltpu.VMEM((rows, LANES), F32),
        pltpu.VMEM((rows, LANES), jnp.int32),
        pltpu.VMEM((rows, LANES), jnp.int32),
        pltpu.VMEM((rows, LANES), jnp.int32),
        pltpu.VMEM((rows - TEXT, LANES), jnp.int32),
    ]


def attention_forward(meta_columns, meta_rows, table_rows, projected, width):
    rows = projected.shape[0]
    pairs = width // LANES

    def block(part):
        return pl.BlockSpec((rows, LANES), lambda p: (0, part * pairs + p))

    whole = lambda shape: pl.BlockSpec(shape, lambda p: (0,) * len(shape))
    return pl.pallas_call(
        forward_kernel,
        grid=(pairs,),
        in_specs=[
            whole(meta_columns.shape),
            whole(meta_rows.shape),
            pl.BlockSpec((2, 1, LANES), lambda p: (p, 0, 0)),
            block(0), block(1), block(2),
        ],
        out_specs=[
            pl.BlockSpec((rows, LANES), lambda p: (0, p)),
            pl.BlockSpec((1, rows, LANES), lambda p: (p, 0, 0)),
        ],
        out_shape=[
            jax.ShapeDtypeStruct((rows, width), F32),
            jax.ShapeDtypeStruct((pairs, rows, LANES), F32),
        ],
        scratch_shapes=static_scratch(rows),
        compiler_params=pltpu.CompilerParams(vmem_limit_bytes=48 * 1024 * 1024),
        name="attention_forward",
    )(meta_columns, meta_rows, table_rows, projected, projected, projected)


def skewed(block):
    size = block.shape[0]
    lane = lax.broadcasted_iota(jnp.int32, (size, LANES), 1)
    row = lax.broadcasted_iota(jnp.int32, (size, LANES), 0)
    turned = jnp.take_along_axis(block, (lane + row) & (LANES - 1), axis=1)
    straight = lane + row < LANES
    above = jnp.sum(jnp.where(straight, turned, 0.0), axis=0, keepdims=True)
    below = jnp.sum(jnp.where(straight, 0.0, turned), axis=0, keepdims=True)
    return above, below


def transposed(array):
    return jnp.transpose(array.astype(F32)).astype(array.dtype)


def backward_kernel(
    meta_ref, rows_ref, table_ref, q_ref, k_ref, v_ref, mixed_ref, grad_ref, log_ref,
    dq_ref, dk_ref, dv_ref, diag_ref,
    even_ref, odd_ref, shared_ref, bar_ref, index_even, index_odd, index_shared, key_index_ref,
    even_t, odd_t, shared_t,
):
    mark_refs = (even_ref, odd_ref, shared_ref)
    index_refs = (index_even, index_odd, index_shared)
    turned_refs = (even_t, odd_t, shared_t)

    @pl.when(pl.program_id(0) == 0)
    def _():
        prepare(meta_ref, mark_refs, bar_ref, index_refs, key_index_ref)
        for ref, turned in zip(mark_refs, turned_refs):
            turned[...] = transposed(ref[...])

    rows = q_ref.shape[0]
    images = rows - TEXT
    tile = 256
    q, k, v, grad = q_ref[...], k_ref[...], v_ref[...], grad_ref[...]
    lane = lax.broadcasted_iota(jnp.int32, (rows, LANES), 1)
    products = grad.astype(F32) * mixed_ref[...].astype(F32)
    k_turned = transposed(k)
    offsets = bucket(rows_ref[2:3, TEXT:] - meta_ref[TEXT:, 2:3])
    is_image = rows_ref[1:2, TEXT:] > 0
    dq_parts = []
    dk_parts = []
    dv_parts = []
    for parity in range(2):
        own = (lane < HEAD) if parity == 0 else (lane >= HEAD)
        spare = HEAD if parity == 0 else 0
        table_row = table_ref[parity]
        logs = log_ref[0, :, parity * HEAD : parity * HEAD + 1]
        q_text, q_image, k_text, k_image = widened(
            parity, q, k, table_row, mark_refs, bar_ref, index_refs, key_index_ref, logs
        )
        bias = image_bias(table_row, offsets)
        delta = jnp.sum(jnp.where(own, products, 0.0), axis=1, keepdims=True)
        high = delta.astype(BF).astype(F32)
        middle = (delta - high).astype(BF).astype(F32)
        lowest = delta - high - middle
        grad_wide = jnp.where(
            own,
            grad.astype(F32),
            jnp.where(
                lane == spare,
                -high,
                jnp.where(lane == spare + 1, -middle, jnp.where(lane == spare + 2, -lowest, 0.0)),
            ),
        ).astype(BF)
        v_wide = jnp.where(
            own, v.astype(F32), jnp.where(between(lane, spare, spare + 3), 1.0, 0.0)
        ).astype(BF)
        q_marked = jnp.concatenate(
            [
                jnp.where(own, q.astype(F32) * 0.125, mark_refs[parity][...].astype(F32)).astype(BF),
                shared_ref[...],
            ],
            axis=1,
        )
        dq = jnp.zeros((HEAD, rows), F32)
        dks = []
        dvs = []
        first_sum = jnp.zeros((LANES, LANES), F32)
        second_sum = jnp.zeros((LANES, LANES), F32)
        text_image = jnp.zeros((LANES, images), F32)
        for start in range(0, rows, tile):
            here = slice(start, start + tile)
            if start < TEXT:
                scores = dot_nt(k_text[here], q_text)
            else:
                scores = dot_nt(k_image[start - TEXT : start - TEXT + tile], q_image)
                scores = jnp.concatenate([scores[:, :TEXT], scores[:, TEXT:] + bias], axis=1)
            soft = jnp.exp(scores)
            score_grad = soft * dot_nt(v_wide[here], grad_wide)
            low = score_grad.astype(BF)
            dvs.append(dot_nn(soft.astype(BF), grad))
            wide = dot_nn(low, q_marked)
            dks.append(wide[:, :LANES])
            dq = dq + dot_nn(k_turned[parity * HEAD : parity * HEAD + HEAD, here], low)
            rounded = wide.astype(BF)
            first_sum = first_sum + dot_nn(turned_refs[parity][:, here], rounded[:, :LANES])
            second_sum = second_sum + dot_nn(shared_t[:, here], rounded[:, LANES:])
            if start < TEXT:
                text_image = text_image + dot_nn(shared_t[:, here], low[:, TEXT:])
            else:
                by_position = wide[:, LANES:]
                on_image = score_grad[:, TEXT:]
        small = lax.broadcasted_iota(jnp.int32, (LANES, LANES), 1)
        small_row = lax.broadcasted_iota(jnp.int32, (LANES, LANES), 0)
        x0 = HEAD if parity == 0 else 0
        x_block = jnp.where(
            between(small, x0, x0 + COORD) & between(small_row, x0, x0 + COORD), first_sum, 0.0
        )
        y_block = jnp.where(
            between(small, Y0, Y0 + COORD) & between(small_row, Y0, Y0 + COORD), second_sum, 0.0
        )
        p_block = jnp.where((small < POS) & (small_row < POS), second_sum, 0.0)
        wide_lane = lax.broadcasted_iota(jnp.int32, (images, images), 1)
        outside = jnp.sum(jnp.where(is_image, 0.0, on_image), axis=1, keepdims=True)
        pairs = jnp.where(is_image, on_image, 0.0) + jnp.where(wide_lane == 0, outside, 0.0)
        outside_text = jnp.sum(jnp.where(is_image, 0.0, text_image), axis=1, keepdims=True)
        text_lane = lax.broadcasted_iota(jnp.int32, (LANES, images), 1)
        text_row = lax.broadcasted_iota(jnp.int32, (LANES, images), 0)
        text_image = jnp.where(is_image, text_image, 0.0) + jnp.where(
            text_lane == 0, outside_text, 0.0
        )
        text_image = jnp.where(text_row < POS, text_image, 0.0)
        first_lane = lax.broadcasted_iota(jnp.int32, (images, LANES), 1)
        left = pairs[:, :LANES] + jnp.where(first_lane < POS, by_position, 0.0)
        right = pairs[:, LANES:]
        a00, b00 = skewed(left[:LANES] + text_image[:, :LANES] + p_block)
        a01, b01 = skewed(right[:LANES] + text_image[:, LANES:])
        a10, b10 = skewed(left[LANES:])
        a11, b11 = skewed(right[LANES:])
        ax, bx = skewed(x_block)
        ay, by = skewed(y_block)
        diag_ref[parity] = jnp.concatenate(
            [b10, b00 + b11 + a10, a00 + a11 + b01, a01, bx, ax, by, ay], axis=0
        )
        dq_parts.append(dq)
        dk_parts.append(jnp.concatenate(dks, axis=0))
        dv_parts.append(jnp.concatenate(dvs, axis=0))
    dq_ref[...] = jnp.transpose(jnp.concatenate(dq_parts, axis=0) * 0.125).astype(BF)
    dk_ref[...] = jnp.where(lane < HEAD, dk_parts[0], dk_parts[1]).astype(BF)
    dv_ref[...] = jnp.where(lane < HEAD, dv_parts[0], dv_parts[1]).astype(BF)


def attention_backward(meta_columns, meta_rows, table_rows, projected, mixed, grad, logs):
    rows, width = mixed.shape
    pairs = width // LANES

    def block(part):
        return pl.BlockSpec((rows, LANES), lambda p: (0, part * pairs + p))

    whole = lambda shape: pl.BlockSpec(shape, lambda p: (0,) * len(shape))
    heads = 2 * pairs
    return pl.pallas_call(
        backward_kernel,
        grid=(pairs,),
        in_specs=[
            whole(meta_columns.shape),
            whole(meta_rows.shape),
            pl.BlockSpec((2, 1, LANES), lambda p: (p, 0, 0)),
            block(0), block(1), block(2), block(0), block(0),
            pl.BlockSpec((1, rows, LANES), lambda p: (p, 0, 0)),
        ],
        out_specs=[block(0)] * 3 + [pl.BlockSpec((2, 8, LANES), lambda p: (p, 0, 0))],
        out_shape=[jax.ShapeDtypeStruct((rows, width), BF)] * 3
        + [jax.ShapeDtypeStruct((heads, 8, LANES), F32)],
        scratch_shapes=static_scratch(rows) + [pltpu.VMEM((LANES, rows), BF)] * 3,
        compiler_params=pltpu.CompilerParams(vmem_limit_bytes=56 * 1024 * 1024),
        name="attention_backward",
    )(meta_columns, meta_rows, table_rows, projected, projected, projected, mixed, grad, logs)


def table_rows_of(tables):
    heads = tables[0].shape[1]
    stacked = jnp.concatenate([t.astype(F32).T for t in tables], axis=1)
    return jnp.pad(stacked, ((0, 0), (0, LANES - stacked.shape[1]))).reshape(heads, 1, LANES)


def diagonal_buckets():
    distance = lax.broadcasted_iota(jnp.int32, (4, LANES), 1) + LANES * (
        lax.broadcasted_iota(jnp.int32, (4, LANES), 0) - 2
    )
    return bucket(distance)


def table_grads_of(diagonals):
    heads = diagonals.shape[0]
    level = lax.broadcasted_iota(jnp.int32, (33, 4, LANES), 0)
    chosen = (diagonal_buckets()[None] == level).astype(F32)
    sums = []
    for first, count, skip in ((0, 4, 0), (4, 2, 1), (6, 2, 1)):
        rows = diagonals[:, first : first + count]
        picks = chosen[:, skip : skip + count]
        sums.append(jnp.sum(picks[:, None] * rows[None], axis=(2, 3)))
    return tuple(sums)


MESH = pl.DeviceIdType.MESH
PIECE = 16


def remote(src, dst, send, receive, device):
    return pltpu.make_async_remote_copy(
        src_ref=src, dst_ref=dst, send_sem=send, recv_sem=receive, device_id=device,
        device_id_type=MESH,
    )


def sync_kernel(
    depth, counts, hops, *refs,
):
    inputs = refs[: len(counts)]
    (small_ref, out_ref, small_out,
     work, fresh, from_first, from_second, from_line, final, small_in,
     pair_sems, plane_sems, line_sems, gather_sems, small_sems, local_sems) = refs[len(counts):]
    width = out_ref.shape[1]
    chunks = sum(counts)
    rows = 4 * 4 * PIECE * depth
    half, quarter, eighth, part = rows // 2, rows // 4, rows // 8, rows // 16
    x = lax.axis_index("seq")
    place = lax.axis_index("dp")
    core = lax.rem(place, 2)
    y = lax.rem(lax.div(place, 2), 2)
    z = lax.div(place, 4)

    def at(new_x, new_core, new_y, new_z):
        return (new_x, new_z * 4 + new_y * 2 + new_core)

    over_core = at(x, 1 - core, y, z)
    over_x = at(1 - x, core, y, z)
    over_y = at(x, core, 1 - y, z)
    on_line = [at(x, core, y, lax.rem(z + step, depth)) for step in range(1, depth)]
    barrier = pltpu.get_barrier_semaphore()
    for device in [over_core, over_x, over_y] + on_line:
        pl.semaphore_signal(barrier, inc=1, device_id=device, device_id_type=MESH)
    pl.semaphore_wait(barrier, 2 + depth)

    small_out[...] = small_ref[...]

    def small_copy(hop):
        if hop == 0:
            device = over_core
        elif hop == 1:
            device = over_x
        elif hop == 2:
            device = over_y
        else:
            reach = 2 ** (hop - 3)
            up = lax.rem(lax.div(z, reach), 2)
            device = at(x, core, y, z + reach - 2 * reach * up)
        return remote(
            small_out, small_in.at[hop], small_sems.at[0, hop], small_sems.at[1, hop], device
        )

    def pair_start(chunk):
        first = 0
        for source, count in zip(inputs, counts):
            @pl.when((chunk >= first) & (chunk < first + count))
            def _(source=source, first=first):
                begin = (chunk - first) * rows
                remote(
                    source.at[pl.ds(begin + (1 - core) * half, half)], fresh.at[chunk],
                    pair_sems.at[0, 0, chunk], pair_sems.at[0, 1, chunk], over_core,
                ).start()
                pltpu.make_async_copy(
                    source.at[pl.ds(begin + core * half, half)], work.at[chunk],
                    local_sems.at[0, chunk],
                ).start()
            first += count

    def pair_wait(chunk):
        remote(
            work.at[chunk], fresh.at[chunk], pair_sems.at[0, 0, chunk],
            pair_sems.at[0, 1, chunk], over_core,
        ).wait()
        pltpu.make_async_copy(work.at[chunk], work.at[chunk], local_sems.at[0, chunk]).wait()

    def first_copies(chunk):
        return [
            remote(
                work.at[chunk, pl.ds((1 - x) * eighth, eighth)], from_first.at[chunk, 0],
                plane_sems.at[0, 0, 0, chunk], plane_sems.at[0, 1, 0, chunk], over_x,
            ),
            remote(
                work.at[chunk, pl.ds(quarter + (1 - y) * eighth, eighth)],
                from_first.at[chunk, 1],
                plane_sems.at[0, 0, 1, chunk], plane_sems.at[0, 1, 1, chunk], over_y,
            ),
        ]

    def second_copies(chunk):
        return [
            remote(
                work.at[chunk, pl.ds(x * eighth + (1 - y) * part, part)],
                from_second.at[chunk, 0],
                plane_sems.at[1, 0, 0, chunk], plane_sems.at[1, 1, 0, chunk], over_y,
            ),
            remote(
                work.at[chunk, pl.ds(quarter + y * eighth + (1 - x) * part, part)],
                from_second.at[chunk, 1],
                plane_sems.at[1, 0, 1, chunk], plane_sems.at[1, 1, 1, chunk], over_x,
            ),
        ]

    own_a = x * eighth + y * part
    own_b = quarter + y * eighth + x * part

    def line_copies(chunk):
        copies = []
        for step in range(1, depth):
            target = lax.rem(z + step, depth)
            for side, begin in enumerate((own_a, own_b)):
                copies.append(
                    remote(
                        work.at[chunk, pl.ds(begin + target * PIECE, PIECE)],
                        from_line.at[chunk, step - 1, side],
                        line_sems.at[0, side, step - 1, chunk],
                        line_sems.at[1, side, step - 1, chunk],
                        on_line[step - 1],
                    )
                )
        return copies

    def out_rows(chunk, begin, size):
        return out_ref.at[pl.ds(chunk * rows + core * half + begin, size)]

    def line_gathers(chunk, arriving):
        copies = []
        for step in range(1, depth):
            owner = lax.rem(z + depth - step, depth) if arriving else z
            for side, begin in enumerate((own_a, own_b)):
                copies.append(
                    remote(
                        final.at[chunk, side], out_rows(chunk, begin + owner * PIECE, PIECE),
                        gather_sems.at[0, side, step - 1, chunk],
                        gather_sems.at[1, side, step - 1, chunk],
                        on_line[step - 1],
                    )
                )
        return copies

    def final_copies(chunk):
        return [
            pltpu.make_async_copy(
                final.at[chunk, side], out_rows(chunk, begin + z * PIECE, PIECE),
                local_sems.at[1 + side, chunk],
            )
            for side, begin in enumerate((own_a, own_b))
        ]

    def block_gather(chunk, begin, landing, size, device, level, side):
        return remote(
            out_rows(chunk, begin, size), out_rows(chunk, landing, size),
            plane_sems.at[level, 0, side, chunk], plane_sems.at[level, 1, side, chunk], device,
        )

    def second_gathers(chunk, arriving):
        other_a = x * eighth + (1 - y) * part
        other_b = quarter + y * eighth + (1 - x) * part
        return [
            block_gather(chunk, own_a, other_a if arriving else own_a, part, over_y, 2, 0),
            block_gather(chunk, own_b, other_b if arriving else own_b, part, over_x, 2, 1),
        ]

    def first_gathers(chunk, arriving):
        mine_a, mine_b = x * eighth, quarter + y * eighth
        other_a, other_b = (1 - x) * eighth, quarter + (1 - y) * eighth
        return [
            block_gather(chunk, mine_a, other_a if arriving else mine_a, eighth, over_x, 3, 0),
            block_gather(chunk, mine_b, other_b if arriving else mine_b, eighth, over_y, 3, 1),
        ]

    def pair_gather(chunk, arriving):
        mine = chunk * rows + core * half
        other = chunk * rows + (1 - core) * half
        return remote(
            out_ref.at[pl.ds(mine, half)], out_ref.at[pl.ds(other if arriving else mine, half)],
            pair_sems.at[1, 0, chunk], pair_sems.at[1, 1, chunk], over_core,
        )

    def add_rows(chunk, begin, source, size):
        block = min(size, 64)

        def body(index, carry):
            offset = pl.multiple_of(index * block, block)
            there = pl.ds(pl.multiple_of(begin + offset, PIECE), block)
            work[chunk, there] = work[chunk, there] + source[pl.ds(offset, block)]
            return carry

        lax.fori_loop(0, size // block, body, 0)

    def stage(number, chunk):
        if number == 0:
            pair_start(chunk)
        elif number == 1:
            pair_wait(chunk)
            add_rows(chunk, 0, fresh.at[chunk], half)
            for copy in first_copies(chunk):
                copy.start()
        elif number == 2:
            for copy in first_copies(chunk):
                copy.wait()
            add_rows(chunk, x * eighth, from_first.at[chunk, 0], eighth)
            add_rows(chunk, quarter + y * eighth, from_first.at[chunk, 1], eighth)
            for copy in second_copies(chunk):
                copy.start()
        elif number == 3:
            for copy in second_copies(chunk):
                copy.wait()
            add_rows(chunk, own_a, from_second.at[chunk, 0], part)
            add_rows(chunk, own_b, from_second.at[chunk, 1], part)
            for copy in line_copies(chunk):
                copy.start()
        elif number == 4:
            for copy in line_copies(chunk):
                copy.wait()
            for side, begin in enumerate((own_a, own_b)):
                there = pl.ds(pl.multiple_of(begin + z * PIECE, PIECE), PIECE)
                total = work[chunk, there].astype(F32)
                for step in range(depth - 1):
                    total = total + from_line[chunk, step, side].astype(F32)
                final[chunk, side] = total.astype(BF)
            for copy in line_gathers(chunk, False) + final_copies(chunk):
                copy.start()
        elif number == 5:
            for copy in line_gathers(chunk, True) + final_copies(chunk):
                copy.wait()
            for copy in second_gathers(chunk, False):
                copy.start()
        elif number == 6:
            for copy in second_gathers(chunk, True):
                copy.wait()
            for copy in first_gathers(chunk, False):
                copy.start()
        elif number == 7:
            for copy in first_gathers(chunk, True):
                copy.wait()
            pair_gather(chunk, False).start()
        else:
            pair_gather(chunk, True).wait()

    def tick(index, carry):
        for number in range(8, -1, -1):
            chunk = index - number
            pl.when((chunk >= 0) & (chunk < chunks))(functools.partial(stage, number, chunk))
        for hop in range(hops + 1):
            @pl.when(index == hop)
            def _(hop=hop):
                if hop > 0:
                    small_copy(hop - 1).wait()
                    small_out[...] = small_out[...] + small_in[hop - 1]
                if hop < hops:
                    small_copy(hop).start()
        return carry

    lax.fori_loop(0, max(chunks + 8, hops + 1), tick, 0)


def synced(grads, small, depth):
    rows = 16 * PIECE * depth
    if any(g.shape[0] % rows for g in grads):
        grads = (jnp.concatenate(grads, axis=0),)
        short = -grads[0].shape[0] % rows
        grads = (jnp.pad(grads[0], ((0, short), (0, 0))),)
    width = grads[0].shape[1]
    counts = tuple(g.shape[0] // rows for g in grads)
    chunks = sum(counts)
    hops = 3 + (depth - 1).bit_length()
    dma = pltpu.SemaphoreType.DMA
    anywhere = pl.BlockSpec(memory_space=pl.ANY)
    vmem = pl.BlockSpec(memory_space=pltpu.VMEM)
    return pl.pallas_call(
        functools.partial(sync_kernel, depth, counts, hops),
        in_specs=[anywhere] * len(grads) + [vmem],
        out_specs=[anywhere, vmem],
        out_shape=[
            jax.ShapeDtypeStruct((chunks * rows, width), BF),
            jax.ShapeDtypeStruct(small.shape, F32),
        ],
        scratch_shapes=[
            pltpu.VMEM((chunks, rows // 2, width), BF),
            pltpu.VMEM((chunks, rows // 2, width), BF),
            pltpu.VMEM((chunks, 2, rows // 8, width), BF),
            pltpu.VMEM((chunks, 2, rows // 16, width), BF),
            pltpu.VMEM((chunks, max(depth - 1, 1), 2, PIECE, width), BF),
            pltpu.VMEM((chunks, 2, PIECE, width), BF),
            pltpu.VMEM((hops,) + small.shape, F32),
            dma((2, 2, chunks)),
            dma((4, 2, 2, chunks)),
            dma((2, 2, max(depth - 1, 1), chunks)),
            dma((2, 2, max(depth - 1, 1), chunks)),
            dma((2, hops)),
            dma((3, chunks)),
        ],
        compiler_params=pltpu.CompilerParams(
            collective_id=0, has_side_effects=True, vmem_limit_bytes=58 * 1024 * 1024
        ),
        name="summed_over_devices",
    )(*grads, small)


EPSILON = 1e-05


def norm_rows(hidden, gain, shift):
    center = hidden - jnp.mean(hidden, axis=-1, keepdims=True)
    spread = jnp.mean(center * center, axis=-1, keepdims=True)
    return center * lax.rsqrt(spread + EPSILON) * gain + shift


def exact_gelu(hidden):
    return jax.nn.gelu(hidden, approximate=False)


def swapped(block):
    return lax.ppermute(block, "seq", [(0, 1), (1, 0)])


def whole_item(halves):
    mine = lax.axis_index("seq")
    kept = lax.dynamic_index_in_dim(halves, mine, 0, keepdims=False)
    other = swapped(lax.dynamic_index_in_dim(halves, 1 - mine, 0, keepdims=False))
    return jnp.where(
        mine == 0,
        jnp.concatenate([kept, other], axis=0),
        jnp.concatenate([other, kept], axis=0),
    )


def back_in_halves(rows):
    mine = lax.axis_index("seq")
    count = rows.shape[0] // 2
    other = swapped(lax.dynamic_slice_in_dim(rows, (1 - mine) * count, count, 0))
    kept = lax.dynamic_slice_in_dim(rows, mine * count, count, 0)
    return jnp.where(mine == 0, jnp.stack([kept, other]), jnp.stack([other, kept]))


def per_device(
    layer_in, segment, key_mask, position, layout_x, layout_y,
    qkv_weight, query_bias, value_bias, out_weight, out_bias, attn_gain, attn_shift,
    up_weight, up_bias, down_weight, down_bias, ffn_gain, ffn_shift,
    text_table, horiz_table, vert_table, cotangent,
):
    depth = lax.axis_size("dp") // 4
    width = layer_in.shape[-1]
    inputs = whole_item(layer_in)
    fields = jnp.stack([segment, key_mask, position, layout_x, layout_y], axis=-1)
    fields = whole_item(jnp.pad(fields, ((0, 0), (0, 0), (0, 3))))
    cotangent_rows = whole_item(cotangent)
    meta_rows = fields.T
    table_rows = table_rows_of((text_table, horiz_table, vert_table))

    projected = jnp.dot(inputs, qkv_weight, preferred_element_type=F32)
    biases = jnp.concatenate([query_bias, jnp.zeros_like(query_bias), value_bias])
    projected = (projected + biases.astype(F32)).astype(BF)
    mixed, logs = attention_forward(fields, meta_rows, table_rows, projected, width)
    mixed_low = mixed.astype(BF)
    attn_out = jnp.dot(mixed_low, out_weight, preferred_element_type=F32) + out_bias.astype(F32)
    hidden_one = inputs.astype(F32) + attn_out
    normed_one, pull_one = jax.vjp(
        norm_rows, hidden_one, attn_gain.astype(F32), attn_shift.astype(F32)
    )
    normed_low = normed_one.astype(BF)
    up_pre = jnp.dot(normed_low, up_weight, preferred_element_type=F32) + up_bias.astype(F32)
    activated, pull_gelu = jax.vjp(exact_gelu, up_pre)
    activated_low = activated.astype(BF)
    branch = jnp.dot(activated_low, down_weight, preferred_element_type=F32) + down_bias.astype(F32)
    normed_two, pull_two = jax.vjp(
        norm_rows, normed_one + branch, ffn_gain.astype(F32), ffn_shift.astype(F32)
    )
    layer_out = back_in_halves(normed_two.astype(BF))

    d_hidden_two, d_ffn_gain, d_ffn_shift = pull_two(cotangent_rows.astype(F32))
    d_branch = d_hidden_two.astype(BF)
    grad_down = jnp.einsum("rf,rd->fd", activated_low, d_branch, preferred_element_type=F32)
    grad_down_bias = jnp.sum(d_branch.astype(F32), axis=0)
    d_activated = jnp.einsum("rd,fd->rf", d_branch, down_weight, preferred_element_type=F32)
    d_up = pull_gelu(d_activated)[0].astype(BF)
    grad_up = jnp.einsum("rf,rd->fd", d_up, normed_low, preferred_element_type=F32)
    grad_up_bias = jnp.sum(d_up.astype(F32), axis=0)
    d_normed = (
        jnp.einsum("rf,df->rd", d_up, up_weight, preferred_element_type=F32) + d_hidden_two
    )
    d_hidden_one, d_attn_gain, d_attn_shift = pull_one(d_normed)
    d_attn = d_hidden_one.astype(BF)
    grad_out = jnp.einsum("rd,re->de", mixed_low, d_attn, preferred_element_type=F32)
    grad_out_bias = jnp.sum(d_attn.astype(F32), axis=0)
    d_mixed = jnp.einsum("re,de->rd", d_attn, out_weight, preferred_element_type=F32).astype(BF)

    d_queries, d_keys, d_values, diagonals = attention_backward(
        fields, meta_rows, table_rows, projected, mixed, d_mixed, logs
    )
    table_grads = table_grads_of(diagonals)
    d_project = jnp.concatenate([d_queries, d_keys, d_values], axis=1)
    grad_qkv = jnp.einsum("re,rd->ed", d_project, inputs, preferred_element_type=F32)
    grad_query_bias = jnp.sum(d_queries.astype(F32), axis=0)
    grad_value_bias = jnp.sum(d_values.astype(F32), axis=0)
    grad_input = d_hidden_one + jnp.einsum(
        "re,de->rd", d_project, qkv_weight, preferred_element_type=F32
    )
    grad_input = back_in_halves(grad_input.astype(BF)).astype(F32)

    singles = (
        grad_query_bias, grad_value_bias, grad_out_bias, d_attn_gain, d_attn_shift,
        grad_down_bias, d_ffn_gain, d_ffn_shift, grad_up_bias,
    ) + tuple(t.reshape(-1) for t in table_grads)
    flat = jnp.concatenate(singles)
    flat = jnp.pad(flat, (0, -flat.size % (8 * width))).reshape(-1, width)
    tail = jnp.concatenate([grad_out.astype(BF), grad_qkv.astype(BF)], axis=0)
    summed, flat = synced((grad_down.astype(BF), grad_up.astype(BF), tail), flat, depth)
    flat = flat.reshape(-1)
    small = []
    begin = 0
    for single in singles:
        small.append(flat[begin : begin + single.size])
        begin += single.size
    hidden = up_weight.shape[1]

    def part(begin, size):
        return summed[begin : begin + size].astype(F32)

    sum_down = part(0, hidden)
    sum_up = part(hidden, hidden).T
    sum_out = part(2 * hidden, width)
    sum_qkv = part(2 * hidden + width, 3 * width).T
    tables = [t.reshape(text_table.shape) for t in small[9:]]
    return (
        layer_out, grad_input, sum_qkv, small[0], small[1], sum_out, small[2], small[3], small[4],
        sum_up, small[8], sum_down, small[5], small[6], small[7], tables[0], tables[1], tables[2],
    )


def solution(mesh):
    rows = P("dp", "seq", None)
    marks_spec = P("dp", "seq")
    return jax.shard_map(
        per_device,
        mesh=mesh,
        in_specs=(rows,) + (marks_spec,) * 5 + (P(),) * 16 + (rows,),
        out_specs=(rows, rows) + (P(),) * 16,
        check_vma=False,
    )
```

```python
import functools

import jax
import jax.numpy as jnp
from jax import lax
from jax.experimental import pallas as pl
from jax.experimental.pallas import tpu as pltpu
from jax.sharding import PartitionSpec as P

BF = jnp.bfloat16
F32 = jnp.float32
BIG = 1e30
LANES = 128
HEAD = 64
TEXT = 512
POS = 64
COORD = 48
Y0 = 64
GROUP0 = 112
MEMBER0 = 116
FLAG = 124
LOG0 = 125
X_TABLE = 33
Y_TABLE = 66
NOTHING = 127


def dot_nt(a, b):
    return lax.dot_general(a, b, (((1,), (1,)), ((), ())), preferred_element_type=F32)


def dot_nn(a, b):
    return lax.dot_general(a, b, (((1,), (0,)), ((), ())), preferred_element_type=F32)


def looked_up(table_row, index):
    rows = index.shape[0]
    return jnp.take_along_axis(jnp.broadcast_to(table_row, (rows, LANES)), index, axis=1)


def bucket(distance):
    return jnp.clip(distance, -16, 16) + 16


def between(lane, low, high):
    return (lane >= low) & (lane < high)


def columns_of(meta_ref):
    return tuple(meta_ref[:, field : field + 1] for field in range(5))


def marks(meta_ref):
    segment, key_mask, position, across, down = columns_of(meta_ref)
    rows = segment.shape[0]
    lane = lax.broadcasted_iota(jnp.int32, (rows, LANES), 1)
    row = lax.broadcasted_iota(jnp.int32, (rows, LANES), 0)
    even = between(lane, HEAD, HEAD + COORD) & (lane - HEAD == across)
    odd = (lane < COORD) & (lane == across)
    group = (segment - 1) >> 3
    member = (segment - 1) & 7
    named = segment > 0
    shared = (
        ((row < TEXT) & (lane < POS) & (lane == position))
        | (between(lane, Y0, Y0 + COORD) & (lane - Y0 == down))
        | (named & between(lane, GROUP0, MEMBER0) & (lane - GROUP0 == group))
        | (named & between(lane, MEMBER0, FLAG) & (lane - MEMBER0 == member))
        | ((lane == FLAG) & (key_mask <= 0))
        | (lane >= LOG0)
    )
    return tuple(jnp.where(m, 1.0, 0.0).astype(BF) for m in (even, odd, shared))


def barred(meta_ref):
    segment = meta_ref[:, 0:1]
    rows = segment.shape[0]
    lane = lax.broadcasted_iota(jnp.int32, (rows, LANES), 1)
    group = (segment - 1) >> 3
    member = (segment - 1) & 7
    shut = (
        ((segment > 0) & between(lane, GROUP0, MEMBER0) & (lane - GROUP0 != group))
        | ((segment < 0) & between(lane, GROUP0, MEMBER0))
        | ((segment > 0) & between(lane, MEMBER0, FLAG) & (lane - MEMBER0 != member))
        | (lane == FLAG)
    )
    return jnp.where(shut, -BIG, 0.0).astype(F32)


def query_index(meta_ref):
    segment, key_mask, position, across, down = columns_of(meta_ref)
    rows = segment.shape[0]
    lane = lax.broadcasted_iota(jnp.int32, (rows, LANES), 1)
    x_even = bucket(across - (lane - HEAD)) + X_TABLE
    x_odd = bucket(across - lane) + X_TABLE
    even = jnp.where(between(lane, HEAD, HEAD + COORD), x_even, NOTHING)
    odd = jnp.where(lane < COORD, x_odd, NOTHING)
    shared = jnp.where(
        lane < POS,
        bucket(position - lane),
        jnp.where(between(lane, Y0, Y0 + COORD), bucket(down - (lane - Y0)) + Y_TABLE, NOTHING),
    )
    return even, odd, shared


def image_key_index(meta_ref):
    position = meta_ref[TEXT:, 2:3]
    lane = lax.broadcasted_iota(jnp.int32, (position.shape[0], LANES), 1)
    return jnp.where(lane < POS, bucket(lane - position), NOTHING)


def prepare(meta_ref, mark_refs, bar_ref, index_refs, key_index_ref):
    for ref, value in zip(mark_refs, marks(meta_ref)):
        ref[...] = value
    bar_ref[...] = barred(meta_ref)
    for ref, value in zip(index_refs, query_index(meta_ref)):
        ref[...] = value
    key_index_ref[...] = image_key_index(meta_ref)


def image_offsets(row_positions, column_positions):
    return bucket(column_positions - row_positions)


def widened(parity, q, k, table_row, mark_refs, bar_ref, index_refs, key_index_ref, logs):
    rows = q.shape[0]
    lane = lax.broadcasted_iota(jnp.int32, (rows, LANES), 1)
    own = (lane < HEAD) if parity == 0 else (lane >= HEAD)
    first = jnp.where(own, q.astype(F32) * 0.125, looked_up(table_row, index_refs[parity][...]))
    second = looked_up(table_row, index_refs[2][...]) + bar_ref[...]
    if logs is not None:
        high = logs.astype(BF).astype(F32)
        middle = (logs - high).astype(BF).astype(F32)
        lowest = logs - high - middle
        second = jnp.where(
            lane == LOG0,
            -high,
            jnp.where(lane == LOG0 + 1, -middle, jnp.where(lane == LOG0 + 2, -lowest, second)),
        )
    first = first.astype(BF)
    second = second.astype(BF)
    mark_second = mark_refs[2][...]
    to_image = jnp.where(lane < POS, mark_second, second)
    key_first = jnp.where(own, k, mark_refs[parity][...])
    image_lane = lane[TEXT:]
    key_image = jnp.where(
        image_lane < POS,
        looked_up(table_row, key_index_ref[...]).astype(BF),
        mark_second[TEXT:],
    )
    q_text = jnp.concatenate([first, second], axis=1)
    q_image = jnp.concatenate([first, to_image], axis=1)
    k_text = jnp.concatenate([key_first[:TEXT], mark_second[:TEXT]], axis=1)
    k_image = jnp.concatenate([key_first[TEXT:], key_image], axis=1)
    return q_text, q_image, k_text, k_image


def image_bias(table_row, offsets):
    return jnp.concatenate(
        [looked_up(table_row, offsets[:, :LANES]), looked_up(table_row, offsets[:, LANES:])], axis=1
    )


def forward_kernel(
    meta_ref, rows_ref, table_ref, q_ref, k_ref, v_ref, mixed_ref, log_ref,
    even_ref, odd_ref, shared_ref, bar_ref, index_even, index_odd, index_shared, key_index_ref,
):
    mark_refs = (even_ref, odd_ref, shared_ref)
    index_refs = (index_even, index_odd, index_shared)

    @pl.when(pl.program_id(0) == 0)
    def _():
        prepare(meta_ref, mark_refs, bar_ref, index_refs, key_index_ref)

    rows = q_ref.shape[0]
    images = rows - TEXT
    q, k, v = q_ref[...], k_ref[...], v_ref[...]
    offsets = bucket(meta_ref[TEXT:, 2:3] - rows_ref[2:3, TEXT:])
    tile = 256
    parts = []
    for parity in range(2):
        table_row = table_ref[pl.ds(2 * pl.program_id(0) + parity, 1), :]
        q_text, q_image, k_text, k_image = widened(
            parity, q, k, table_row, mark_refs, bar_ref, index_refs, key_index_ref, None
        )
        bias = image_bias(table_row, offsets)
        outs = []
        logs = []
        for start in range(0, rows, tile):
            here = slice(start, start + tile)
            on_text = dot_nt(q_text[here], k_text)
            on_image = dot_nt(q_image[here], k_image)
            if start >= TEXT:
                on_image = on_image + bias[start - TEXT : start - TEXT + tile]
            top = jnp.maximum(
                jnp.max(on_text, axis=1, keepdims=True), jnp.max(on_image, axis=1, keepdims=True)
            )
            on_text = jnp.exp(on_text - top)
            on_image = jnp.exp(on_image - top)
            total = jnp.sum(on_text, axis=1, keepdims=True) + jnp.sum(
                on_image, axis=1, keepdims=True
            )
            out = dot_nn(on_text.astype(BF), v[:TEXT]) + dot_nn(on_image.astype(BF), v[TEXT:])
            outs.append(out / total)
            logs.append(jnp.broadcast_to(top + jnp.log(total), (tile, LANES)))
        parts.append((jnp.concatenate(outs, axis=0), jnp.concatenate(logs, axis=0)))
    lane = lax.broadcasted_iota(jnp.int32, (rows, LANES), 1)
    mixed_ref[...] = jnp.where(lane < HEAD, parts[0][0], parts[1][0])
    log_ref[0] = jnp.where(lane < HEAD, parts[0][1], parts[1][1])


def static_scratch(rows):
    return [
        pltpu.VMEM((rows, LANES), BF),
        pltpu.VMEM((rows, LANES), BF),
        pltpu.VMEM((rows, LANES), BF),
        pltpu.VMEM((rows, LANES), F32),
        pltpu.VMEM((rows, LANES), jnp.int32),
        pltpu.VMEM((rows, LANES), jnp.int32),
        pltpu.VMEM((rows, LANES), jnp.int32),
        pltpu.VMEM((rows - TEXT, LANES), jnp.int32),
    ]


def attention_forward(meta_columns, meta_rows, table_rows, projected, width):
    rows = projected.shape[0]
    pairs = width // LANES

    def block(part):
        return pl.BlockSpec((rows, LANES), lambda p: (0, part * pairs + p))

    whole = lambda shape: pl.BlockSpec(shape, lambda p: (0,) * len(shape))
    return pl.pallas_call(
        forward_kernel,
        grid=(pairs,),
        in_specs=[
            whole(meta_columns.shape),
            whole(meta_rows.shape),
            whole(table_rows.shape),
            block(0), block(1), block(2),
        ],
        out_specs=[
            pl.BlockSpec((rows, LANES), lambda p: (0, p)),
            pl.BlockSpec((1, rows, LANES), lambda p: (p, 0, 0)),
        ],
        out_shape=[
            jax.ShapeDtypeStruct((rows, width), F32),
            jax.ShapeDtypeStruct((pairs, rows, LANES), F32),
        ],
        scratch_shapes=static_scratch(rows),
        compiler_params=pltpu.CompilerParams(vmem_limit_bytes=48 * 1024 * 1024),
        name="attention_forward",
    )(meta_columns, meta_rows, table_rows, projected, projected, projected)


def skewed(block):
    size = block.shape[0]
    lane = lax.broadcasted_iota(jnp.int32, (size, LANES), 1)
    row = lax.broadcasted_iota(jnp.int32, (size, LANES), 0)
    turned = jnp.take_along_axis(block, (lane + row) & (LANES - 1), axis=1)
    straight = lane + row < LANES
    above = jnp.sum(jnp.where(straight, turned, 0.0), axis=0, keepdims=True)
    below = jnp.sum(jnp.where(straight, 0.0, turned), axis=0, keepdims=True)
    return above, below


def transposed(array):
    return jnp.transpose(array.astype(F32)).astype(array.dtype)


def backward_kernel(
    meta_ref, rows_ref, table_ref, q_ref, k_ref, v_ref, mixed_ref, grad_ref, log_ref,
    dq_ref, dk_ref, dv_ref, diag_ref,
    even_ref, odd_ref, shared_ref, bar_ref, index_even, index_odd, index_shared, key_index_ref,
    even_t, odd_t, shared_t,
):
    mark_refs = (even_ref, odd_ref, shared_ref)
    index_refs = (index_even, index_odd, index_shared)
    turned_refs = (even_t, odd_t, shared_t)

    @pl.when(pl.program_id(0) == 0)
    def _():
        prepare(meta_ref, mark_refs, bar_ref, index_refs, key_index_ref)
        for ref, turned in zip(mark_refs, turned_refs):
            turned[...] = transposed(ref[...])

    rows = q_ref.shape[0]
    images = rows - TEXT
    tile = 256
    q, k, v, grad = q_ref[...], k_ref[...], v_ref[...], grad_ref[...]
    lane = lax.broadcasted_iota(jnp.int32, (rows, LANES), 1)
    products = grad.astype(F32) * mixed_ref[...].astype(F32)
    k_turned = transposed(k)
    offsets = bucket(rows_ref[2:3, TEXT:] - meta_ref[TEXT:, 2:3])
    is_image = rows_ref[1:2, TEXT:] > 0
    dq_parts = []
    dk_parts = []
    dv_parts = []
    for parity in range(2):
        own = (lane < HEAD) if parity == 0 else (lane >= HEAD)
        spare = HEAD if parity == 0 else 0
        table_row = table_ref[pl.ds(2 * pl.program_id(0) + parity, 1), :]
        logs = log_ref[0, :, parity * HEAD : parity * HEAD + 1]
        q_text, q_image, k_text, k_image = widened(
            parity, q, k, table_row, mark_refs, bar_ref, index_refs, key_index_ref, logs
        )
        bias = image_bias(table_row, offsets)
        delta = jnp.sum(jnp.where(own, products, 0.0), axis=1, keepdims=True)
        high = delta.astype(BF).astype(F32)
        middle = (delta - high).astype(BF).astype(F32)
        lowest = delta - high - middle
        grad_wide = jnp.where(
            own,
            grad.astype(F32),
            jnp.where(
                lane == spare,
                -high,
                jnp.where(lane == spare + 1, -middle, jnp.where(lane == spare + 2, -lowest, 0.0)),
            ),
        ).astype(BF)
        v_wide = jnp.where(
            own, v.astype(F32), jnp.where(between(lane, spare, spare + 3), 1.0, 0.0)
        ).astype(BF)
        q_marked = jnp.concatenate(
            [
                jnp.where(own, q.astype(F32) * 0.125, mark_refs[parity][...].astype(F32)).astype(BF),
                shared_ref[...],
            ],
            axis=1,
        )
        dq = jnp.zeros((HEAD, rows), F32)
        dks = []
        dvs = []
        first_sum = jnp.zeros((LANES, LANES), F32)
        second_sum = jnp.zeros((LANES, LANES), F32)
        text_image = jnp.zeros((LANES, images), F32)
        for start in range(0, rows, tile):
            here = slice(start, start + tile)
            if start < TEXT:
                scores = dot_nt(k_text[here], q_text)
            else:
                scores = dot_nt(k_image[start - TEXT : start - TEXT + tile], q_image)
                scores = jnp.concatenate([scores[:, :TEXT], scores[:, TEXT:] + bias], axis=1)
            soft = jnp.exp(scores)
            score_grad = soft * dot_nt(v_wide[here], grad_wide)
            low = score_grad.astype(BF)
            dvs.append(dot_nn(soft.astype(BF), grad))
            wide = dot_nn(low, q_marked)
            dks.append(wide[:, :LANES])
            dq = dq + dot_nn(k_turned[parity * HEAD : parity * HEAD + HEAD, here], low)
            rounded = wide.astype(BF)
            first_sum = first_sum + dot_nn(turned_refs[parity][:, here], rounded[:, :LANES])
            second_sum = second_sum + dot_nn(shared_t[:, here], rounded[:, LANES:])
            if start < TEXT:
                text_image = text_image + dot_nn(shared_t[:, here], low[:, TEXT:])
            else:
                by_position = wide[:, LANES:]
                on_image = score_grad[:, TEXT:]
        small = lax.broadcasted_iota(jnp.int32, (LANES, LANES), 1)
        small_row = lax.broadcasted_iota(jnp.int32, (LANES, LANES), 0)
        x0 = HEAD if parity == 0 else 0
        x_block = jnp.where(
            between(small, x0, x0 + COORD) & between(small_row, x0, x0 + COORD), first_sum, 0.0
        )
        y_block = jnp.where(
            between(small, Y0, Y0 + COORD) & between(small_row, Y0, Y0 + COORD), second_sum, 0.0
        )
        p_block = jnp.where((small < POS) & (small_row < POS), second_sum, 0.0)
        wide_lane = lax.broadcasted_iota(jnp.int32, (images, images), 1)
        outside = jnp.sum(jnp.where(is_image, 0.0, on_image), axis=1, keepdims=True)
        pairs = jnp.where(is_image, on_image, 0.0) + jnp.where(wide_lane == 0, outside, 0.0)
        outside_text = jnp.sum(jnp.where(is_image, 0.0, text_image), axis=1, keepdims=True)
        text_lane = lax.broadcasted_iota(jnp.int32, (LANES, images), 1)
        text_row = lax.broadcasted_iota(jnp.int32, (LANES, images), 0)
        text_image = jnp.where(is_image, text_image, 0.0) + jnp.where(
            text_lane == 0, outside_text, 0.0
        )
        text_image = jnp.where(text_row < POS, text_image, 0.0)
        first_lane = lax.broadcasted_iota(jnp.int32, (images, LANES), 1)
        left = pairs[:, :LANES] + jnp.where(first_lane < POS, by_position, 0.0)
        right = pairs[:, LANES:]
        a00, b00 = skewed(left[:LANES] + text_image[:, :LANES] + p_block)
        a01, b01 = skewed(right[:LANES] + text_image[:, LANES:])
        a10, b10 = skewed(left[LANES:])
        a11, b11 = skewed(right[LANES:])
        ax, bx = skewed(x_block)
        ay, by = skewed(y_block)
        diag_ref[parity] = jnp.concatenate(
            [b10, b00 + b11 + a10, a00 + a11 + b01, a01, bx, ax, by, ay], axis=0
        )
        dq_parts.append(dq)
        dk_parts.append(jnp.concatenate(dks, axis=0))
        dv_parts.append(jnp.concatenate(dvs, axis=0))
    dq_ref[...] = jnp.transpose(jnp.concatenate(dq_parts, axis=0) * 0.125).astype(BF)
    dk_ref[...] = jnp.where(lane < HEAD, dk_parts[0], dk_parts[1]).astype(BF)
    dv_ref[...] = jnp.where(lane < HEAD, dv_parts[0], dv_parts[1]).astype(BF)


def attention_backward(meta_columns, meta_rows, table_rows, projected, mixed, grad, logs):
    rows, width = mixed.shape
    pairs = width // LANES

    def block(part):
        return pl.BlockSpec((rows, LANES), lambda p: (0, part * pairs + p))

    whole = lambda shape: pl.BlockSpec(shape, lambda p: (0,) * len(shape))
    heads = 2 * pairs
    return pl.pallas_call(
        backward_kernel,
        grid=(pairs,),
        in_specs=[
            whole(meta_columns.shape),
            whole(meta_rows.shape),
            whole(table_rows.shape),
            block(0), block(1), block(2), block(0), block(0),
            pl.BlockSpec((1, rows, LANES), lambda p: (p, 0, 0)),
        ],
        out_specs=[block(0)] * 3 + [pl.BlockSpec((2, 8, LANES), lambda p: (p, 0, 0))],
        out_shape=[jax.ShapeDtypeStruct((rows, width), BF)] * 3
        + [jax.ShapeDtypeStruct((heads, 8, LANES), F32)],
        scratch_shapes=static_scratch(rows) + [pltpu.VMEM((LANES, rows), BF)] * 3,
        compiler_params=pltpu.CompilerParams(vmem_limit_bytes=56 * 1024 * 1024),
        name="attention_backward",
    )(meta_columns, meta_rows, table_rows, projected, projected, projected, mixed, grad, logs)


MESH = pl.DeviceIdType.MESH
VMEM = pl.BlockSpec(memory_space=pltpu.VMEM)
MIB = 1024 * 1024


def remote(src, dst, send, receive, device):
    return pltpu.make_async_remote_copy(
        src_ref=src, dst_ref=dst, send_sem=send, recv_sem=receive, device_id=device,
        device_id_type=MESH,
    )


def project_kernel(
    layer_ref, segment_ref, mask_ref, position_ref, across_ref, down_ref, weight_ref,
    query_bias_ref, value_bias_ref, text_ref, horiz_ref, vert_ref,
    item_ref, projected_ref, columns_ref, rows_ref, table_ref,
    meta_send, bias_ref, sems,
):
    mine = lax.axis_index("seq")
    partner = (1 - mine, lax.axis_index("dp"))
    count, width = layer_ref.shape[1:]
    barrier = pltpu.get_barrier_semaphore()
    pl.semaphore_signal(barrier, inc=1, device_id=partner, device_id_type=MESH)
    pl.semaphore_wait(barrier, 1)
    own = pl.ds(pl.multiple_of(mine * count, LANES), count)
    other = pl.ds(pl.multiple_of((1 - mine) * count, LANES), count)
    rows_out = remote(layer_ref.at[1 - mine], item_ref.at[own], sems.at[0], sems.at[1], partner)
    rows_out.start()

    fields = (segment_ref, mask_ref, position_ref, across_ref, down_ref)
    blocks = [
        jnp.concatenate(
            [field[item : item + 1, :] for field in fields] + [jnp.zeros((3, count), jnp.int32)],
            axis=0,
        )
        for item in range(2)
    ]
    meta_send[...] = jnp.where(mine == 0, blocks[1], blocks[0])
    meta_out = remote(meta_send, rows_ref.at[:, own], sems.at[2], sems.at[3], partner)
    meta_out.start()
    rows_ref[:, own] = jnp.where(mine == 0, blocks[0], blocks[1])
    item_ref[own] = layer_ref[mine]
    bias_ref[:, :width] = query_bias_ref[...].astype(F32).reshape(1, width)
    bias_ref[:, width : 2 * width] = jnp.zeros((1, width), F32)
    bias_ref[:, 2 * width :] = value_bias_ref[...].astype(F32).reshape(1, width)
    heads, levels = text_ref.shape
    spot = lax.broadcasted_iota(jnp.int32, (levels, LANES), 1)
    level = lax.broadcasted_iota(jnp.int32, (levels, LANES), 0)
    table = jnp.zeros((heads, LANES), F32)
    for source, begin in ((text_ref, 0), (horiz_ref, X_TABLE), (vert_ref, Y_TABLE)):
        table = table + dot_nn(source[...], (spot == level + begin).astype(BF))
    table_ref[...] = jnp.concatenate([table, jnp.zeros((16 - heads, LANES), F32)], axis=0)

    def project(there):
        step = 256

        def body(index, carry):
            columns = pl.ds(pl.multiple_of(index * step, step), step)
            product = dot_nn(item_ref[there], weight_ref[:, columns])
            projected_ref[there, columns] = (product + bias_ref[:, columns]).astype(BF)
            return carry

        lax.fori_loop(0, 3 * width // step, body, 0)

    project(own)
    rows_out.wait()
    project(other)
    meta_out.wait()
    meta = rows_ref[...].astype(F32)
    tall = jnp.concatenate([meta, jnp.zeros((LANES - 8, meta.shape[1]), F32)], axis=0)
    columns_ref[...] = jnp.transpose(tall).astype(jnp.int32)


def projected_item(layer_in, fields, qkv_weight, query_bias, value_bias, tables):
    rows = 2 * layer_in.shape[1]
    width = layer_in.shape[2]
    return pl.pallas_call(
        project_kernel,
        in_specs=[VMEM] * 12,
        out_specs=[VMEM] * 5,
        out_shape=[
            jax.ShapeDtypeStruct((rows, width), BF),
            jax.ShapeDtypeStruct((rows, 3 * width), BF),
            jax.ShapeDtypeStruct((rows, LANES), jnp.int32),
            jax.ShapeDtypeStruct((8, rows), jnp.int32),
            jax.ShapeDtypeStruct((16, LANES), F32),
        ],
        scratch_shapes=[
            pltpu.VMEM((8, rows // 2), jnp.int32),
            pltpu.VMEM((1, 3 * width), F32),
            pltpu.SemaphoreType.DMA((4,)),
        ],
        compiler_params=pltpu.CompilerParams(
            collective_id=1, has_side_effects=True, vmem_limit_bytes=40 * MIB
        ),
        name="projected_item",
    )(layer_in, *fields, qkv_weight, query_bias, value_bias, *(t.T for t in tables))


EPSILON = 1e-05
TILE = 256


def vector(ref):
    return ref[...].astype(F32).reshape(1, ref.shape[0])


def gelu_and_slope(x):
    bell = jnp.exp(-0.5 * x * x)
    t = 1.0 / (1.0 + 0.23164188826 * jnp.abs(x))
    series = t * (
        0.127414796
        + t * (-0.142248368 + t * (0.7107068705 + t * (-0.7265760135 + t * 0.5307027145)))
    )
    tail = bell * series
    below = jnp.where(x >= 0.0, 1.0 - tail, tail)
    return x * below, below + x * (0.3989422804014327 * bell)


def row_mean(block):
    return jnp.mean(block, axis=1, keepdims=True)


def normalized(hidden):
    center = hidden - row_mean(hidden)
    scale = lax.rsqrt(row_mean(center * center) + EPSILON)
    return center * scale, scale


def norm_pulled(grad, unit, scale):
    return scale * (grad - row_mean(grad) - unit * row_mean(grad * unit))


def column_sum(block):
    return jnp.sum(block, axis=0, keepdims=True)


def feed_kernel(
    item_ref, mixed_ref, cotangent_ref, out_weight_ref, up_ref, down_ref,
    out_bias_ref, attn_gain_ref, attn_shift_ref, up_bias_ref, down_bias_ref,
    ffn_gain_ref, ffn_shift_ref,
    layer_ref, d_hidden_ref, d_mixed_ref, grad_out_ref, grad_down_ref, grad_up_ref, small_ref,
    cotangent_all, active, slope, unit, scale_ref, normed, normed_t, total, d_branch, d_branch_t,
    sems,
):
    step = pl.program_id(0)
    blocks = pl.num_programs(0) // 2
    rows, width = item_ref.shape
    count = rows // 2
    mine = lax.axis_index("seq")
    partner = (1 - mine, lax.axis_index("dp"))
    own = pl.ds(pl.multiple_of(mine * count, LANES), count)
    tiles = rows // TILE

    def sent():
        return remote(
            cotangent_ref.at[1 - mine], cotangent_all.at[own], sems.at[0], sems.at[1], partner
        )

    def over_tiles(size, body, carry):
        def run(index, state):
            return body(pl.ds(pl.multiple_of(index * size, size), size), state)

        return lax.fori_loop(0, rows // size, run, carry)

    @pl.when(step == 0)
    def _():
        barrier = pltpu.get_barrier_semaphore()
        pl.semaphore_signal(barrier, inc=1, device_id=partner, device_id_type=MESH)
        pl.semaphore_wait(barrier, 1)
        sent().start()
        small_ref[...] = jnp.zeros_like(small_ref)
        cotangent_all[own] = cotangent_ref[mine]
        out_bias, gain, shift = vector(out_bias_ref), vector(attn_gain_ref), vector(attn_shift_ref)

        def tile(there, carry):
            attn = dot_nn(mixed_ref[there].astype(BF), out_weight_ref[...]) + out_bias
            standard, scale = normalized(item_ref[there].astype(F32) + attn)
            unit[there] = standard
            scale_ref[there] = jnp.broadcast_to(scale, (scale.shape[0], LANES))
            result = standard * gain + shift
            normed[there] = result.astype(BF)
            normed_t[:, there] = jnp.transpose(result).astype(BF)
            return carry

        over_tiles(TILE, tile, 0)
        total[...] = jnp.zeros_like(total)

    @pl.when(step < blocks)
    def _():
        bias = up_bias_ref[pl.ds(pl.multiple_of(step * width, LANES), width)]
        bias = bias.astype(F32).reshape(1, width)

        def tile(there, carry):
            value, grade = gelu_and_slope(dot_nn(normed[there], up_ref[...]) + bias)
            active[step, there] = value.astype(BF)
            slope[step, there] = grade
            return carry

        over_tiles(TILE, tile, 0)

        def tile(there, carry):
            total[there] += dot_nn(active[step, there], down_ref[...])
            return carry

        over_tiles(TILE, tile, 0)

    @pl.when(step == blocks)
    def _():
        sent().wait()
        gain, shift, bias = vector(ffn_gain_ref), vector(ffn_shift_ref), vector(down_bias_ref)
        first_gain, first_shift = vector(attn_gain_ref), vector(attn_shift_ref)

        def tile(there, sums):
            hidden = unit[there] * first_gain + first_shift + (total[there] + bias)
            standard, scale = normalized(hidden)
            layer_ref[there] = (standard * gain + shift).astype(BF)
            cotangent = cotangent_all[there].astype(F32)
            pulled = norm_pulled(cotangent * gain, standard, scale)
            total[there] = pulled
            low = pulled.astype(BF)
            d_branch[there] = low
            return (
                sums[0] + column_sum(low.astype(F32)),
                sums[1] + column_sum(cotangent * standard),
                sums[2] + column_sum(cotangent),
            )

        zero = jnp.zeros((1, width), F32)
        sums = over_tiles(64, tile, (zero, zero, zero))
        for row, value in zip((5, 6, 7), sums):
            small_ref[row : row + 1] = value

        def turn(there, carry):
            d_branch_t[:, there] = jnp.transpose(d_branch[there].astype(F32)).astype(BF)
            return carry

        over_tiles(TILE, turn, 0)

    @pl.when(step >= blocks)
    def _():
        block = step - blocks

        def tile(there, carry):
            grad_down_ref[there] = dot_nn(d_branch_t[there], active[block]).astype(BF)
            return carry

        over_tiles(TILE, tile, 0)

        def tile(there, carry):
            d_up = (dot_nt(d_branch[there], down_ref[...]) * slope[block, there]).astype(BF)
            active[block, there] = d_up
            return carry + column_sum(d_up.astype(F32))

        sums = over_tiles(TILE, tile, jnp.zeros((1, width), F32))
        small_ref[pl.ds(8 + block, 1)] = sums

        def tile(there, carry):
            grad_up_ref[there] = dot_nn(normed_t[there], active[block]).astype(BF)
            total[there] += dot_nt(active[block, there], up_ref[...])
            return carry

        over_tiles(TILE, tile, 0)

    @pl.when(step == 2 * blocks - 1)
    def _():
        gain = vector(attn_gain_ref)

        def tile(there, sums):
            d_normed = total[there]
            standard = unit[there]
            d_hidden = norm_pulled(d_normed * gain, standard, scale_ref[there, :1])
            d_hidden_ref[there] = d_hidden
            low = d_hidden.astype(BF)
            d_branch[there] = low
            return (
                sums[0] + column_sum(low.astype(F32)),
                sums[1] + column_sum(d_normed * standard),
                sums[2] + column_sum(d_normed),
            )

        zero = jnp.zeros((1, width), F32)
        sums = over_tiles(64, tile, (zero, zero, zero))
        for row, value in zip((2, 3, 4), sums):
            small_ref[row : row + 1] = value

        def turn(there, carry):
            normed_t[:, there] = jnp.transpose(mixed_ref[there]).astype(BF)
            return carry

        over_tiles(TILE, turn, 0)

        def tile(there, carry):
            d_mixed_ref[there] = dot_nt(d_branch[there], out_weight_ref[...]).astype(BF)
            grad_out_ref[there] = dot_nn(normed_t[there], d_branch[...]).astype(BF)
            return carry

        over_tiles(TILE, tile, 0)


def fed_forward_and_back(
    item, mixed, cotangent, out_weight, up_weight, down_weight, vectors,
):
    rows, width = item.shape
    blocks = up_weight.shape[1] // width
    whole = pl.BlockSpec(memory_space=pltpu.VMEM)
    square = lambda kind: jax.ShapeDtypeStruct((rows, width), kind)
    later = lambda i: jnp.maximum(i - blocks, 0)
    return pl.pallas_call(
        feed_kernel,
        grid=(2 * blocks,),
        in_specs=[whole] * 4
        + [
            pl.BlockSpec((width, width), lambda i: (0, lax.rem(i, blocks))),
            pl.BlockSpec((width, width), lambda i: (lax.rem(i, blocks), 0)),
        ]
        + [whole] * 7,
        out_specs=[whole] * 4
        + [
            pl.BlockSpec((width, width), lambda i: (later(i), 0)),
            pl.BlockSpec((width, width), lambda i: (later(i), 0)),
            whole,
        ],
        out_shape=[
            square(BF), square(F32), square(BF), jax.ShapeDtypeStruct((width, width), BF),
            jax.ShapeDtypeStruct((blocks * width, width), BF),
            jax.ShapeDtypeStruct((blocks * width, width), BF),
            jax.ShapeDtypeStruct((16, width), F32),
        ],
        scratch_shapes=[
            pltpu.VMEM((rows, width), BF),
            pltpu.VMEM((blocks, rows, width), BF),
            pltpu.VMEM((blocks, rows, width), F32),
            pltpu.VMEM((rows, width), F32),
            pltpu.VMEM((rows, LANES), F32),
            pltpu.VMEM((rows, width), BF),
            pltpu.VMEM((width, rows), BF),
            pltpu.VMEM((rows, width), F32),
            pltpu.VMEM((rows, width), BF),
            pltpu.VMEM((width, rows), BF),
            pltpu.SemaphoreType.DMA((2,)),
        ],
        compiler_params=pltpu.CompilerParams(
            collective_id=2, has_side_effects=True, vmem_limit_bytes=60 * MIB
        ),
        name="feed_forward",
    )(item, mixed, cotangent, out_weight, up_weight, down_weight, *vectors)


def input_kernel(
    item_ref, d_query_ref, d_key_ref, d_value_ref, weight_ref, d_hidden_ref,
    grad_ref, grad_input_ref, sums_ref, item_t,
):
    rows, width = item_ref.shape
    tiles = rows // TILE
    for tile in range(tiles):
        there = slice(tile * TILE, tile * TILE + TILE)
        item_t[:, there] = jnp.transpose(item_ref[there].astype(F32)).astype(BF)
    pieces = (d_query_ref, d_key_ref, d_value_ref)

    def body(tile, sums):
        there = pl.ds(pl.multiple_of(tile * TILE, TILE), TILE)
        total = d_hidden_ref[there]
        for part, piece in enumerate(pieces):
            columns = slice(part * width, part * width + width)
            total = total + dot_nt(piece[there], weight_ref[:, columns])
            grad_ref[pl.ds(pl.multiple_of(part * width + tile * TILE, TILE), TILE)] = dot_nn(
                item_t[there], piece[...]
            ).astype(BF)
        grad_input_ref[there] = total.astype(BF)
        return (
            sums[0] + column_sum(d_query_ref[there].astype(F32)),
            sums[1] + column_sum(d_value_ref[there].astype(F32)),
        )

    zero = jnp.zeros((1, width), F32)
    sums = lax.fori_loop(0, tiles, body, (zero, zero))
    sums_ref[0:1] = sums[0]
    sums_ref[1:2] = sums[1]
    sums_ref[2:] = jnp.zeros((6, width), F32)


def projection_grads(item, d_queries, d_keys, d_values, qkv_weight, d_hidden):
    rows, width = item.shape
    return pl.pallas_call(
        input_kernel,
        in_specs=[VMEM] * 6,
        out_specs=[VMEM] * 3,
        out_shape=[
            jax.ShapeDtypeStruct((3 * width, width), BF),
            jax.ShapeDtypeStruct((rows, width), BF),
            jax.ShapeDtypeStruct((8, width), F32),
        ],
        scratch_shapes=[pltpu.VMEM((width, rows), BF)],
        compiler_params=pltpu.CompilerParams(vmem_limit_bytes=56 * MIB),
        name="projection_grads",
    )(item, d_queries, d_keys, d_values, qkv_weight, d_hidden)


def finish_kernel(
    summed_ref, grad_input_ref, small_ref, diagonal_ref,
    down_ref, up_ref, out_ref, qkv_ref, input_ref, *singles,
):
    step = pl.program_id(0)
    piece = summed_ref[...].astype(F32)

    @pl.when(step < 4)
    def _():
        down_ref[...] = jnp.transpose(piece)

    @pl.when((step >= 4) & (step < 8))
    def _():
        up_ref[...] = piece

    @pl.when(step == 8)
    def _():
        out_ref[...] = piece

    @pl.when(step > 8)
    def _():
        qkv_ref[...] = piece

    @pl.when(step == 0)
    def _():
        input_ref[...] = grad_input_ref[...].astype(F32)
        for row in range(8):
            singles[row][...] = small_ref[row]
        width = small_ref.shape[1]
        for row in range(4):
            singles[8][row * width : row * width + width] = small_ref[8 + row]
        heads, levels = singles[9].shape
        diagonals = diagonal_ref[...]
        level = lax.broadcasted_iota(jnp.int32, (LANES, LANES), 1)
        lane = lax.broadcasted_iota(jnp.int32, (LANES, LANES), 0)
        for table, (first, size, skip) in enumerate(((0, 4, 0), (4, 2, 1), (6, 2, 1))):
            total = jnp.zeros((heads, LANES), F32)
            for row in range(size):
                distance = lane + LANES * (row + skip - 2)
                chosen = (bucket(distance) == level).astype(F32)
                total = total + jnp.dot(
                    diagonals[:, first + row, :], chosen, preferred_element_type=F32,
                    precision=lax.Precision.HIGHEST,
                )
            singles[9 + table][...] = total[:, :levels]


def finished(summed, grad_input, small, diagonals, hidden, levels):
    width = summed.shape[1]
    heads = diagonals.shape[0]
    blocks = hidden // width
    whole = pl.BlockSpec(memory_space=pltpu.VMEM)
    held = lambda i, first, count: jnp.clip(i - first, 0, count - 1)
    square = (width, width)
    single = jax.ShapeDtypeStruct((width,), F32)
    table = jax.ShapeDtypeStruct((heads, levels), F32)
    return pl.pallas_call(
        finish_kernel,
        grid=(2 * blocks + 4,),
        in_specs=[pl.BlockSpec(square, lambda i: (i, 0)), whole, whole, whole],
        out_specs=[
            pl.BlockSpec(square, lambda i: (held(i, 0, blocks), 0)),
            pl.BlockSpec(square, lambda i: (0, held(i, blocks, blocks))),
            pl.BlockSpec(square, lambda i: (0, 0)),
            pl.BlockSpec(square, lambda i: (0, held(i, 2 * blocks + 1, 3))),
        ]
        + [whole] * 13,
        out_shape=[
            jax.ShapeDtypeStruct((hidden, width), F32),
            jax.ShapeDtypeStruct((width, hidden), F32),
            jax.ShapeDtypeStruct((width, width), F32),
            jax.ShapeDtypeStruct((width, 3 * width), F32),
            jax.ShapeDtypeStruct(grad_input.shape, F32),
        ]
        + [single] * 8
        + [jax.ShapeDtypeStruct((hidden,), F32)]
        + [table] * 3,
        compiler_params=pltpu.CompilerParams(vmem_limit_bytes=56 * MIB),
        name="finished",
    )(summed, grad_input, small, diagonals)


PIECE = 16


def sync_kernel(
    depth, counts, hops, *refs,
):
    inputs = refs[: len(counts)]
    (small_ref, diagonal_ref, layer_ref, grad_ref,
     out_ref, small_out, diagonal_out, layer_out, grad_out,
     work, fresh, from_first, from_second, from_line, final, small_in, diagonal_in,
     pair_sems, plane_sems, line_sems, gather_sems, small_sems, local_sems, item_sems) = refs[len(counts):]
    width = out_ref.shape[1]
    chunks = sum(counts)
    rows = 4 * 4 * PIECE * depth
    half, quarter, eighth, part = rows // 2, rows // 4, rows // 8, rows // 16
    x = lax.axis_index("seq")
    place = lax.axis_index("dp")
    core = lax.rem(place, 2)
    y = lax.rem(lax.div(place, 2), 2)
    z = lax.div(place, 4)

    def at(new_x, new_core, new_y, new_z):
        return (new_x, new_z * 4 + new_y * 2 + new_core)

    over_core = at(x, 1 - core, y, z)
    over_x = at(1 - x, core, y, z)
    over_y = at(x, core, 1 - y, z)
    on_line = [at(x, core, y, lax.rem(z + step, depth)) for step in range(1, depth)]
    barrier = pltpu.get_barrier_semaphore()
    for device in [over_core, over_x, over_y] + on_line:
        pl.semaphore_signal(barrier, inc=1, device_id=device, device_id_type=MESH)
    pl.semaphore_wait(barrier, 2 + depth)

    small_out[...] = small_ref[...]
    diagonal_out[...] = diagonal_ref[...]
    count = layer_ref.shape[0] // 2

    def item_copies():
        copies = []
        for index, (source, target) in enumerate(((layer_ref, layer_out), (grad_ref, grad_out))):
            copies.append(
                pltpu.make_async_copy(
                    source.at[pl.ds(x * count, count)], target.at[x], item_sems.at[0, index]
                )
            )
            copies.append(
                remote(
                    source.at[pl.ds((1 - x) * count, count)], target.at[x],
                    item_sems.at[1, index], item_sems.at[2, index], over_x,
                )
            )
        return copies

    for copy in item_copies():
        copy.start()

    def small_copies(hop):
        if hop == 0:
            device = over_core
        elif hop == 1:
            device = over_x
        elif hop == 2:
            device = over_y
        else:
            reach = 2 ** (hop - 3)
            up = lax.rem(lax.div(z, reach), 2)
            device = at(x, core, y, z + reach - 2 * reach * up)
        return [
            remote(
                small_out, small_in.at[hop], small_sems.at[0, 0, hop], small_sems.at[0, 1, hop],
                device,
            ),
            remote(
                diagonal_out, diagonal_in.at[hop], small_sems.at[1, 0, hop],
                small_sems.at[1, 1, hop], device,
            ),
        ]

    def pair_start(chunk):
        first = 0
        for source, count in zip(inputs, counts):
            @pl.when((chunk >= first) & (chunk < first + count))
            def _(source=source, first=first):
                begin = (chunk - first) * rows
                remote(
                    source.at[pl.ds(begin + (1 - core) * half, half)], fresh.at[chunk],
                    pair_sems.at[0, 0, chunk], pair_sems.at[0, 1, chunk], over_core,
                ).start()
                pltpu.make_async_copy(
                    source.at[pl.ds(begin + core * half, half)], work.at[chunk],
                    local_sems.at[0, chunk],
                ).start()
            first += count

    def pair_wait(chunk):
        remote(
            work.at[chunk], fresh.at[chunk], pair_sems.at[0, 0, chunk],
            pair_sems.at[0, 1, chunk], over_core,
        ).wait()
        pltpu.make_async_copy(work.at[chunk], work.at[chunk], local_sems.at[0, chunk]).wait()

    def first_copies(chunk):
        return [
            remote(
                work.at[chunk, pl.ds((1 - x) * eighth, eighth)], from_first.at[chunk, 0],
                plane_sems.at[0, 0, 0, chunk], plane_sems.at[0, 1, 0, chunk], over_x,
            ),
            remote(
                work.at[chunk, pl.ds(quarter + (1 - y) * eighth, eighth)],
                from_first.at[chunk, 1],
                plane_sems.at[0, 0, 1, chunk], plane_sems.at[0, 1, 1, chunk], over_y,
            ),
        ]

    def second_copies(chunk):
        return [
            remote(
                work.at[chunk, pl.ds(x * eighth + (1 - y) * part, part)],
                from_second.at[chunk, 0],
                plane_sems.at[1, 0, 0, chunk], plane_sems.at[1, 1, 0, chunk], over_y,
            ),
            remote(
                work.at[chunk, pl.ds(quarter + y * eighth + (1 - x) * part, part)],
                from_second.at[chunk, 1],
                plane_sems.at[1, 0, 1, chunk], plane_sems.at[1, 1, 1, chunk], over_x,
            ),
        ]

    own_a = x * eighth + y * part
    own_b = quarter + y * eighth + x * part

    def line_copies(chunk):
        copies = []
        for step in range(1, depth):
            target = lax.rem(z + step, depth)
            for side, begin in enumerate((own_a, own_b)):
                copies.append(
                    remote(
                        work.at[chunk, pl.ds(begin + target * PIECE, PIECE)],
                        from_line.at[chunk, step - 1, side],
                        line_sems.at[0, side, step - 1, chunk],
                        line_sems.at[1, side, step - 1, chunk],
                        on_line[step - 1],
                    )
                )
        return copies

    def out_rows(chunk, begin, size):
        return out_ref.at[pl.ds(chunk * rows + core * half + begin, size)]

    def line_gathers(chunk, arriving):
        copies = []
        for step in range(1, depth):
            owner = lax.rem(z + depth - step, depth) if arriving else z
            for side, begin in enumerate((own_a, own_b)):
                copies.append(
                    remote(
                        final.at[chunk, side], out_rows(chunk, begin + owner * PIECE, PIECE),
                        gather_sems.at[0, side, step - 1, chunk],
                        gather_sems.at[1, side, step - 1, chunk],
                        on_line[step - 1],
                    )
                )
        return copies

    def final_copies(chunk):
        return [
            pltpu.make_async_copy(
                final.at[chunk, side], out_rows(chunk, begin + z * PIECE, PIECE),
                local_sems.at[1 + side, chunk],
            )
            for side, begin in enumerate((own_a, own_b))
        ]

    def block_gather(chunk, begin, landing, size, device, level, side):
        return remote(
            out_rows(chunk, begin, size), out_rows(chunk, landing, size),
            plane_sems.at[level, 0, side, chunk], plane_sems.at[level, 1, side, chunk], device,
        )

    def second_gathers(chunk, arriving):
        other_a = x * eighth + (1 - y) * part
        other_b = quarter + y * eighth + (1 - x) * part
        return [
            block_gather(chunk, own_a, other_a if arriving else own_a, part, over_y, 2, 0),
            block_gather(chunk, own_b, other_b if arriving else own_b, part, over_x, 2, 1),
        ]

    def first_gathers(chunk, arriving):
        mine_a, mine_b = x * eighth, quarter + y * eighth
        other_a, other_b = (1 - x) * eighth, quarter + (1 - y) * eighth
        return [
            block_gather(chunk, mine_a, other_a if arriving else mine_a, eighth, over_x, 3, 0),
            block_gather(chunk, mine_b, other_b if arriving else mine_b, eighth, over_y, 3, 1),
        ]

    def pair_gather(chunk, arriving):
        mine = chunk * rows + core * half
        other = chunk * rows + (1 - core) * half
        return remote(
            out_ref.at[pl.ds(mine, half)], out_ref.at[pl.ds(other if arriving else mine, half)],
            pair_sems.at[1, 0, chunk], pair_sems.at[1, 1, chunk], over_core,
        )

    def add_rows(chunk, begin, source, size):
        block = min(size, 64)

        def body(index, carry):
            offset = pl.multiple_of(index * block, block)
            there = pl.ds(pl.multiple_of(begin + offset, PIECE), block)
            work[chunk, there] = work[chunk, there] + source[pl.ds(offset, block)]
            return carry

        lax.fori_loop(0, size // block, body, 0)

    def stage(number, chunk):
        if number == 0:
            pair_start(chunk)
        elif number == 1:
            pair_wait(chunk)
            add_rows(chunk, 0, fresh.at[chunk], half)
            for copy in first_copies(chunk):
                copy.start()
        elif number == 2:
            for copy in first_copies(chunk):
                copy.wait()
            add_rows(chunk, x * eighth, from_first.at[chunk, 0], eighth)
            add_rows(chunk, quarter + y * eighth, from_first.at[chunk, 1], eighth)
            for copy in second_copies(chunk):
                copy.start()
        elif number == 3:
            for copy in second_copies(chunk):
                copy.wait()
            add_rows(chunk, own_a, from_second.at[chunk, 0], part)
            add_rows(chunk, own_b, from_second.at[chunk, 1], part)
            for copy in line_copies(chunk):
                copy.start()
        elif number == 4:
            for copy in line_copies(chunk):
                copy.wait()
            for side, begin in enumerate((own_a, own_b)):
                there = pl.ds(pl.multiple_of(begin + z * PIECE, PIECE), PIECE)
                total = work[chunk, there].astype(F32)
                for step in range(depth - 1):
                    total = total + from_line[chunk, step, side].astype(F32)
                final[chunk, side] = total.astype(BF)
            for copy in line_gathers(chunk, False) + final_copies(chunk):
                copy.start()
        elif number == 5:
            for copy in line_gathers(chunk, True) + final_copies(chunk):
                copy.wait()
            for copy in second_gathers(chunk, False):
                copy.start()
        elif number == 6:
            for copy in second_gathers(chunk, True):
                copy.wait()
            for copy in first_gathers(chunk, False):
                copy.start()
        elif number == 7:
            for copy in first_gathers(chunk, True):
                copy.wait()
            pair_gather(chunk, False).start()
        else:
            pair_gather(chunk, True).wait()

    def tick(index, carry):
        for number in range(8, -1, -1):
            chunk = index - number
            pl.when((chunk >= 0) & (chunk < chunks))(functools.partial(stage, number, chunk))
        for hop in range(hops + 1):
            @pl.when(index == hop)
            def _(hop=hop):
                if hop > 0:
                    for copy in small_copies(hop - 1):
                        copy.wait()
                    small_out[...] = small_out[...] + small_in[hop - 1]
                    diagonal_out[...] = diagonal_out[...] + diagonal_in[hop - 1]
                if hop < hops:
                    for copy in small_copies(hop):
                        copy.start()
        return carry

    lax.fori_loop(0, max(chunks + 8, hops + 1), tick, 0)
    for copy in item_copies():
        copy.wait()


def synced(grads, small, diagonals, layer, grad_input, depth):
    rows = 16 * PIECE * depth
    if any(g.shape[0] % rows for g in grads):
        grads = (jnp.concatenate(grads, axis=0),)
        short = -grads[0].shape[0] % rows
        grads = (jnp.pad(grads[0], ((0, short), (0, 0))),)
    width = grads[0].shape[1]
    counts = tuple(g.shape[0] // rows for g in grads)
    chunks = sum(counts)
    hops = 3 + (depth - 1).bit_length()
    halves = jax.ShapeDtypeStruct((2, layer.shape[0] // 2, width), BF)
    dma = pltpu.SemaphoreType.DMA
    anywhere = pl.BlockSpec(memory_space=pl.ANY)
    vmem = pl.BlockSpec(memory_space=pltpu.VMEM)
    return pl.pallas_call(
        functools.partial(sync_kernel, depth, counts, hops),
        in_specs=[anywhere] * len(grads) + [vmem, vmem, anywhere, anywhere],
        out_specs=[anywhere, vmem, vmem, anywhere, anywhere],
        out_shape=[
            jax.ShapeDtypeStruct((chunks * rows, width), BF),
            jax.ShapeDtypeStruct(small.shape, F32),
            jax.ShapeDtypeStruct(diagonals.shape, F32),
            halves, halves,
        ],
        scratch_shapes=[
            pltpu.VMEM((chunks, rows // 2, width), BF),
            pltpu.VMEM((chunks, rows // 2, width), BF),
            pltpu.VMEM((chunks, 2, rows // 8, width), BF),
            pltpu.VMEM((chunks, 2, rows // 16, width), BF),
            pltpu.VMEM((chunks, max(depth - 1, 1), 2, PIECE, width), BF),
            pltpu.VMEM((chunks, 2, PIECE, width), BF),
            pltpu.VMEM((hops,) + small.shape, F32),
            pltpu.VMEM((hops,) + diagonals.shape, F32),
            dma((2, 2, chunks)),
            dma((4, 2, 2, chunks)),
            dma((2, 2, max(depth - 1, 1), chunks)),
            dma((2, 2, max(depth - 1, 1), chunks)),
            dma((2, 2, hops)),
            dma((3, chunks)),
            dma((3, 2)),
        ],
        compiler_params=pltpu.CompilerParams(
            collective_id=0, has_side_effects=True, vmem_limit_bytes=58 * 1024 * 1024
        ),
        name="summed_over_devices",
    )(*grads, small, diagonals, layer, grad_input)


def per_device(
    layer_in, segment, key_mask, position, layout_x, layout_y,
    qkv_weight, query_bias, value_bias, out_weight, out_bias, attn_gain, attn_shift,
    up_weight, up_bias, down_weight, down_bias, ffn_gain, ffn_shift,
    text_table, horiz_table, vert_table, cotangent,
):
    depth = lax.axis_size("dp") // 4
    width = layer_in.shape[-1]
    item, projected, meta_columns, meta_rows, table_rows = projected_item(
        layer_in, (segment, key_mask, position, layout_x, layout_y),
        qkv_weight, query_bias, value_bias, (text_table, horiz_table, vert_table),
    )
    mixed, logs = attention_forward(meta_columns, meta_rows, table_rows, projected, width)
    layer, d_hidden, d_mixed, grad_out, grad_down, grad_up, small = fed_forward_and_back(
        item, mixed, cotangent, out_weight, up_weight, down_weight,
        (out_bias, attn_gain, attn_shift, up_bias, down_bias, ffn_gain, ffn_shift),
    )
    d_queries, d_keys, d_values, diagonals = attention_backward(
        meta_columns, meta_rows, table_rows, projected, mixed, d_mixed, logs
    )
    grad_qkv, grad_input, sums = projection_grads(
        item, d_queries, d_keys, d_values, qkv_weight, d_hidden
    )
    small = jnp.concatenate([sums[:2], small[2:]], axis=0)
    tail = jnp.concatenate([grad_out, grad_qkv], axis=0)
    summed, small, diagonals, layer_out, grad_input = synced(
        (grad_down, grad_up, tail), small, diagonals, layer, grad_input, depth
    )
    done = finished(
        summed, grad_input, small, diagonals, up_weight.shape[1], text_table.shape[0]
    )
    sum_down, sum_up, sum_out, sum_qkv, grad_input = done[:5]
    singles, tables = done[5:14], [t.T for t in done[14:]]
    return (
        layer_out, grad_input, sum_qkv, singles[0], singles[1], sum_out, singles[2], singles[3],
        singles[4], sum_up, singles[8], sum_down, singles[5], singles[6], singles[7],
        tables[0], tables[1], tables[2],
    )


def solution(mesh):
    rows = P("dp", "seq", None)
    marks_spec = P("dp", "seq")
    return jax.shard_map(
        per_device,
        mesh=mesh,
        in_specs=(rows,) + (marks_spec,) * 5 + (P(),) * 16 + (rows,),
        out_specs=(rows, rows) + (P(),) * 16,
        check_vma=False,
    )
```

```python
import functools

import jax
import jax.numpy as jnp
from jax import lax
from jax.experimental import pallas as pl
from jax.experimental.pallas import tpu as pltpu
from jax.sharding import PartitionSpec as P

BF = jnp.bfloat16
F32 = jnp.float32
BIG = 1e30
LANES = 128
HEAD = 64
TEXT = 512
POS = 64
COORD = 48
Y0 = 64
GROUP0 = 112
MEMBER0 = 116
FLAG = 124
LOG0 = 125
X_TABLE = 33
Y_TABLE = 66
NOTHING = 127


def dot_nt(a, b):
    return lax.dot_general(a, b, (((1,), (1,)), ((), ())), preferred_element_type=F32)


def dot_nn(a, b):
    return lax.dot_general(a, b, (((1,), (0,)), ((), ())), preferred_element_type=F32)


def looked_up(table_row, index):
    rows = index.shape[0]
    return jnp.take_along_axis(jnp.broadcast_to(table_row, (rows, LANES)), index, axis=1)


def bucket(distance):
    return jnp.clip(distance, -16, 16) + 16


def between(lane, low, high):
    return (lane >= low) & (lane < high)


def columns_of(meta_ref):
    return tuple(meta_ref[:, field : field + 1] for field in range(5))


def marks(meta_ref):
    segment, key_mask, position, across, down = columns_of(meta_ref)
    rows = segment.shape[0]
    lane = lax.broadcasted_iota(jnp.int32, (rows, LANES), 1)
    row = lax.broadcasted_iota(jnp.int32, (rows, LANES), 0)
    even = between(lane, HEAD, HEAD + COORD) & (lane - HEAD == across)
    odd = (lane < COORD) & (lane == across)
    group = (segment - 1) >> 3
    member = (segment - 1) & 7
    named = segment > 0
    shared = (
        ((row < TEXT) & (lane < POS) & (lane == position))
        | (between(lane, Y0, Y0 + COORD) & (lane - Y0 == down))
        | (named & between(lane, GROUP0, MEMBER0) & (lane - GROUP0 == group))
        | (named & between(lane, MEMBER0, FLAG) & (lane - MEMBER0 == member))
        | ((lane == FLAG) & (key_mask <= 0))
        | (lane >= LOG0)
    )
    return tuple(jnp.where(m, 1.0, 0.0).astype(BF) for m in (even, odd, shared))


def barred(meta_ref):
    segment = meta_ref[:, 0:1]
    rows = segment.shape[0]
    lane = lax.broadcasted_iota(jnp.int32, (rows, LANES), 1)
    group = (segment - 1) >> 3
    member = (segment - 1) & 7
    shut = (
        ((segment > 0) & between(lane, GROUP0, MEMBER0) & (lane - GROUP0 != group))
        | ((segment < 0) & between(lane, GROUP0, MEMBER0))
        | ((segment > 0) & between(lane, MEMBER0, FLAG) & (lane - MEMBER0 != member))
        | (lane == FLAG)
    )
    return jnp.where(shut, -BIG, 0.0).astype(F32)


def query_index(meta_ref):
    segment, key_mask, position, across, down = columns_of(meta_ref)
    rows = segment.shape[0]
    lane = lax.broadcasted_iota(jnp.int32, (rows, LANES), 1)
    x_even = bucket(across - (lane - HEAD)) + X_TABLE
    x_odd = bucket(across - lane) + X_TABLE
    even = jnp.where(between(lane, HEAD, HEAD + COORD), x_even, NOTHING)
    odd = jnp.where(lane < COORD, x_odd, NOTHING)
    shared = jnp.where(
        lane < POS,
        bucket(position - lane),
        jnp.where(between(lane, Y0, Y0 + COORD), bucket(down - (lane - Y0)) + Y_TABLE, NOTHING),
    )
    return even, odd, shared


def image_key_index(meta_ref):
    position = meta_ref[TEXT:, 2:3]
    lane = lax.broadcasted_iota(jnp.int32, (position.shape[0], LANES), 1)
    return jnp.where(lane < POS, bucket(lane - position), NOTHING)


def prepare(meta_ref, mark_refs, bar_ref, index_refs, key_index_ref):
    for ref, value in zip(mark_refs, marks(meta_ref)):
        ref[...] = value
    bar_ref[...] = barred(meta_ref)
    for ref, value in zip(index_refs, query_index(meta_ref)):
        ref[...] = value
    key_index_ref[...] = image_key_index(meta_ref)


def image_offsets(row_positions, column_positions):
    return bucket(column_positions - row_positions)


def widened(parity, q, k, table_row, mark_refs, bar_ref, index_refs, key_index_ref, logs):
    rows = q.shape[0]
    lane = lax.broadcasted_iota(jnp.int32, (rows, LANES), 1)
    own = (lane < HEAD) if parity == 0 else (lane >= HEAD)
    first = jnp.where(own, q.astype(F32) * 0.125, looked_up(table_row, index_refs[parity][...]))
    second = looked_up(table_row, index_refs[2][...]) + bar_ref[...]
    if logs is not None:
        high = logs.astype(BF).astype(F32)
        middle = (logs - high).astype(BF).astype(F32)
        lowest = logs - high - middle
        second = jnp.where(
            lane == LOG0,
            -high,
            jnp.where(lane == LOG0 + 1, -middle, jnp.where(lane == LOG0 + 2, -lowest, second)),
        )
    first = first.astype(BF)
    second = second.astype(BF)
    mark_second = mark_refs[2][...]
    to_image = jnp.where(lane < POS, mark_second, second)
    key_first = jnp.where(own, k, mark_refs[parity][...])
    image_lane = lane[TEXT:]
    key_image = jnp.where(
        image_lane < POS,
        looked_up(table_row, key_index_ref[...]).astype(BF),
        mark_second[TEXT:],
    )
    q_text = jnp.concatenate([first, second], axis=1)
    q_image = jnp.concatenate([first, to_image], axis=1)
    k_text = jnp.concatenate([key_first[:TEXT], mark_second[:TEXT]], axis=1)
    k_image = jnp.concatenate([key_first[TEXT:], key_image], axis=1)
    return q_text, q_image, k_text, k_image


def image_bias(table_row, offsets):
    return jnp.concatenate(
        [looked_up(table_row, offsets[:, :LANES]), looked_up(table_row, offsets[:, LANES:])], axis=1
    )


def forward_kernel(
    meta_ref, rows_ref, table_ref, q_ref, k_ref, v_ref, mixed_ref, log_ref,
    even_ref, odd_ref, shared_ref, bar_ref, index_even, index_odd, index_shared, key_index_ref,
):
    mark_refs = (even_ref, odd_ref, shared_ref)
    index_refs = (index_even, index_odd, index_shared)

    @pl.when(pl.program_id(0) == 0)
    def _():
        prepare(meta_ref, mark_refs, bar_ref, index_refs, key_index_ref)

    rows = q_ref.shape[0]
    images = rows - TEXT
    q, k, v = q_ref[...], k_ref[...], v_ref[...]
    offsets = bucket(meta_ref[TEXT:, 2:3] - rows_ref[2:3, TEXT:])
    tile = 256
    parts = []
    for parity in range(2):
        table_row = table_ref[pl.ds(2 * pl.program_id(0) + parity, 1), :]
        q_text, q_image, k_text, k_image = widened(
            parity, q, k, table_row, mark_refs, bar_ref, index_refs, key_index_ref, None
        )
        bias = image_bias(table_row, offsets)
        outs = []
        logs = []
        for start in range(0, rows, tile):
            here = slice(start, start + tile)
            on_text = dot_nt(q_text[here], k_text)
            on_image = dot_nt(q_image[here], k_image)
            if start >= TEXT:
                on_image = on_image + bias[start - TEXT : start - TEXT + tile]
            top = jnp.maximum(
                jnp.max(on_text, axis=1, keepdims=True), jnp.max(on_image, axis=1, keepdims=True)
            )
            on_text = jnp.exp(on_text - top)
            on_image = jnp.exp(on_image - top)
            total = jnp.sum(on_text, axis=1, keepdims=True) + jnp.sum(
                on_image, axis=1, keepdims=True
            )
            out = dot_nn(on_text.astype(BF), v[:TEXT]) + dot_nn(on_image.astype(BF), v[TEXT:])
            outs.append(out / total)
            logs.append(jnp.broadcast_to(top + jnp.log(total), (tile, LANES)))
        parts.append((jnp.concatenate(outs, axis=0), jnp.concatenate(logs, axis=0)))
    lane = lax.broadcasted_iota(jnp.int32, (rows, LANES), 1)
    mixed_ref[...] = jnp.where(lane < HEAD, parts[0][0], parts[1][0])
    log_ref[0] = jnp.where(lane < HEAD, parts[0][1], parts[1][1])


def static_scratch(rows):
    return [
        pltpu.VMEM((rows, LANES), BF),
        pltpu.VMEM((rows, LANES), BF),
        pltpu.VMEM((rows, LANES), BF),
        pltpu.VMEM((rows, LANES), F32),
        pltpu.VMEM((rows, LANES), jnp.int32),
        pltpu.VMEM((rows, LANES), jnp.int32),
        pltpu.VMEM((rows, LANES), jnp.int32),
        pltpu.VMEM((rows - TEXT, LANES), jnp.int32),
    ]


def attention_forward(meta_columns, meta_rows, table_rows, projected, width):
    rows = projected.shape[0]
    pairs = width // LANES

    def block(part):
        return pl.BlockSpec((rows, LANES), lambda p: (0, part * pairs + p))

    whole = lambda shape: pl.BlockSpec(shape, lambda p: (0,) * len(shape))
    return pl.pallas_call(
        forward_kernel,
        grid=(pairs,),
        in_specs=[
            whole(meta_columns.shape),
            whole(meta_rows.shape),
            whole(table_rows.shape),
            block(0), block(1), block(2),
        ],
        out_specs=[
            pl.BlockSpec((rows, LANES), lambda p: (0, p)),
            pl.BlockSpec((1, rows, LANES), lambda p: (p, 0, 0)),
        ],
        out_shape=[
            jax.ShapeDtypeStruct((rows, width), F32),
            jax.ShapeDtypeStruct((pairs, rows, LANES), F32),
        ],
        scratch_shapes=static_scratch(rows),
        compiler_params=pltpu.CompilerParams(vmem_limit_bytes=48 * 1024 * 1024),
        name="attention_forward",
    )(meta_columns, meta_rows, table_rows, projected, projected, projected)


def skewed(block):
    size = block.shape[0]
    lane = lax.broadcasted_iota(jnp.int32, (size, LANES), 1)
    row = lax.broadcasted_iota(jnp.int32, (size, LANES), 0)
    turned = jnp.take_along_axis(block, (lane + row) & (LANES - 1), axis=1)
    straight = lane + row < LANES
    above = jnp.sum(jnp.where(straight, turned, 0.0), axis=0, keepdims=True)
    below = jnp.sum(jnp.where(straight, 0.0, turned), axis=0, keepdims=True)
    return above, below


def transposed(array):
    return jnp.transpose(array.astype(F32)).astype(array.dtype)


def static_prepare(meta_ref, static):
    (even_ref, odd_ref, shared_ref, bar_ref, index_even, index_odd, index_shared, key_index_ref,
     even_t, odd_t, shared_t) = static
    mark_refs = (even_ref, odd_ref, shared_ref)
    prepare(meta_ref, mark_refs, bar_ref, (index_even, index_odd, index_shared), key_index_ref)
    for ref, turned in zip(mark_refs, (even_t, odd_t, shared_t)):
        turned[...] = transposed(ref[...])


def head_back(
    parity, pair, meta_ref, rows_ref, table_ref, q_ref, k_ref, v_ref, mixed_ref, grad_ref, log_ref,
    static, d_query, d_key, d_value, diag_ref,
):
    (even_ref, odd_ref, shared_ref, bar_ref, index_even, index_odd, index_shared, key_index_ref,
     even_t, odd_t, shared_t) = static
    mark_refs = (even_ref, odd_ref, shared_ref)
    index_refs = (index_even, index_odd, index_shared)
    turned_refs = (even_t, odd_t, shared_t)
    rows = q_ref.shape[0]
    images = rows - TEXT
    tile = 256
    q, k, v, grad = q_ref[...], k_ref[...], v_ref[...], grad_ref[...]
    lane = lax.broadcasted_iota(jnp.int32, (rows, LANES), 1)
    products = grad.astype(F32) * mixed_ref[...].astype(F32)
    k_turned = transposed(k)
    offsets = bucket(rows_ref[2:3, TEXT:] - meta_ref[TEXT:, 2:3])
    is_image = rows_ref[1:2, TEXT:] > 0
    own = (lane < HEAD) if parity == 0 else (lane >= HEAD)
    spare = HEAD if parity == 0 else 0
    table_row = table_ref[pl.ds(2 * pair + parity, 1), :]
    logs = log_ref[0, :, parity * HEAD : parity * HEAD + 1]
    q_text, q_image, k_text, k_image = widened(
        parity, q, k, table_row, mark_refs, bar_ref, index_refs, key_index_ref, logs
    )
    bias = image_bias(table_row, offsets)
    delta = jnp.sum(jnp.where(own, products, 0.0), axis=1, keepdims=True)
    high = delta.astype(BF).astype(F32)
    middle = (delta - high).astype(BF).astype(F32)
    lowest = delta - high - middle
    grad_wide = jnp.where(
        own,
        grad.astype(F32),
        jnp.where(
            lane == spare,
            -high,
            jnp.where(lane == spare + 1, -middle, jnp.where(lane == spare + 2, -lowest, 0.0)),
        ),
    ).astype(BF)
    v_wide = jnp.where(
        own, v.astype(F32), jnp.where(between(lane, spare, spare + 3), 1.0, 0.0)
    ).astype(BF)
    q_marked = jnp.concatenate(
        [
            jnp.where(own, q.astype(F32) * 0.125, mark_refs[parity][...].astype(F32)).astype(BF),
            shared_ref[...],
        ],
        axis=1,
    )
    dq = jnp.zeros((HEAD, rows), F32)
    dks = []
    dvs = []
    first_sum = jnp.zeros((LANES, LANES), F32)
    second_sum = jnp.zeros((LANES, LANES), F32)
    text_image = jnp.zeros((LANES, images), F32)
    for start in range(0, rows, tile):
        here = slice(start, start + tile)
        if start < TEXT:
            scores = dot_nt(k_text[here], q_text)
        else:
            scores = dot_nt(k_image[start - TEXT : start - TEXT + tile], q_image)
            scores = jnp.concatenate([scores[:, :TEXT], scores[:, TEXT:] + bias], axis=1)
        soft = jnp.exp(scores)
        score_grad = soft * dot_nt(v_wide[here], grad_wide)
        low = score_grad.astype(BF)
        dvs.append(dot_nn(soft.astype(BF), grad))
        wide = dot_nn(low, q_marked)
        dks.append(wide[:, :LANES])
        dq = dq + dot_nn(k_turned[parity * HEAD : parity * HEAD + HEAD, here], low)
        rounded = wide.astype(BF)
        first_sum = first_sum + dot_nn(turned_refs[parity][:, here], rounded[:, :LANES])
        second_sum = second_sum + dot_nn(shared_t[:, here], rounded[:, LANES:])
        if start < TEXT:
            text_image = text_image + dot_nn(shared_t[:, here], low[:, TEXT:])
        else:
            by_position = wide[:, LANES:]
            on_image = score_grad[:, TEXT:]
    small = lax.broadcasted_iota(jnp.int32, (LANES, LANES), 1)
    small_row = lax.broadcasted_iota(jnp.int32, (LANES, LANES), 0)
    x0 = HEAD if parity == 0 else 0
    x_block = jnp.where(
        between(small, x0, x0 + COORD) & between(small_row, x0, x0 + COORD), first_sum, 0.0
    )
    y_block = jnp.where(
        between(small, Y0, Y0 + COORD) & between(small_row, Y0, Y0 + COORD), second_sum, 0.0
    )
    p_block = jnp.where((small < POS) & (small_row < POS), second_sum, 0.0)
    wide_lane = lax.broadcasted_iota(jnp.int32, (images, images), 1)
    outside = jnp.sum(jnp.where(is_image, 0.0, on_image), axis=1, keepdims=True)
    pairs = jnp.where(is_image, on_image, 0.0) + jnp.where(wide_lane == 0, outside, 0.0)
    outside_text = jnp.sum(jnp.where(is_image, 0.0, text_image), axis=1, keepdims=True)
    text_lane = lax.broadcasted_iota(jnp.int32, (LANES, images), 1)
    text_row = lax.broadcasted_iota(jnp.int32, (LANES, images), 0)
    text_image = jnp.where(is_image, text_image, 0.0) + jnp.where(
        text_lane == 0, outside_text, 0.0
    )
    text_image = jnp.where(text_row < POS, text_image, 0.0)
    first_lane = lax.broadcasted_iota(jnp.int32, (images, LANES), 1)
    left = pairs[:, :LANES] + jnp.where(first_lane < POS, by_position, 0.0)
    right = pairs[:, LANES:]
    a00, b00 = skewed(left[:LANES] + text_image[:, :LANES] + p_block)
    a01, b01 = skewed(right[:LANES] + text_image[:, LANES:])
    a10, b10 = skewed(left[LANES:])
    a11, b11 = skewed(right[LANES:])
    ax, bx = skewed(x_block)
    ay, by = skewed(y_block)
    diag_ref[2 * pair + parity] = jnp.concatenate(
        [b10, b00 + b11 + a10, a00 + a11 + b01, a01, bx, ax, by, ay], axis=0
    )
    empty = jnp.zeros_like(dq)
    both = [dq * 0.125, empty] if parity == 0 else [empty, dq * 0.125]
    results = (
        (d_query, jnp.transpose(jnp.concatenate(both, axis=0))),
        (d_key, jnp.concatenate(dks, axis=0)),
        (d_value, jnp.concatenate(dvs, axis=0)),
    )
    for ref, value in results:
        if parity == 1:
            value = jnp.where(own, value, ref[pair].astype(F32))
        ref[pair] = value.astype(BF)


MESH = pl.DeviceIdType.MESH
VMEM = pl.BlockSpec(memory_space=pltpu.VMEM)
MIB = 1024 * 1024


def remote(src, dst, send, receive, device):
    return pltpu.make_async_remote_copy(
        src_ref=src, dst_ref=dst, send_sem=send, recv_sem=receive, device_id=device,
        device_id_type=MESH,
    )


def project_kernel(
    layer_ref, segment_ref, mask_ref, position_ref, across_ref, down_ref, weight_ref,
    query_bias_ref, value_bias_ref, text_ref, horiz_ref, vert_ref,
    item_ref, projected_ref, columns_ref, rows_ref, table_ref,
    meta_send, bias_ref, sems,
):
    mine = lax.axis_index("seq")
    partner = (1 - mine, lax.axis_index("dp"))
    count, width = layer_ref.shape[1:]
    barrier = pltpu.get_barrier_semaphore()
    pl.semaphore_signal(barrier, inc=1, device_id=partner, device_id_type=MESH)
    pl.semaphore_wait(barrier, 1)
    own = pl.ds(pl.multiple_of(mine * count, LANES), count)
    other = pl.ds(pl.multiple_of((1 - mine) * count, LANES), count)
    rows_out = remote(layer_ref.at[1 - mine], item_ref.at[own], sems.at[0], sems.at[1], partner)
    rows_out.start()

    fields = (segment_ref, mask_ref, position_ref, across_ref, down_ref)
    blocks = [
        jnp.concatenate(
            [field[item : item + 1, :] for field in fields] + [jnp.zeros((3, count), jnp.int32)],
            axis=0,
        )
        for item in range(2)
    ]
    meta_send[...] = jnp.where(mine == 0, blocks[1], blocks[0])
    meta_out = remote(meta_send, rows_ref.at[:, own], sems.at[2], sems.at[3], partner)
    meta_out.start()
    rows_ref[:, own] = jnp.where(mine == 0, blocks[0], blocks[1])
    item_ref[own] = layer_ref[mine]
    bias_ref[:, :width] = query_bias_ref[...].astype(F32).reshape(1, width)
    bias_ref[:, width : 2 * width] = jnp.zeros((1, width), F32)
    bias_ref[:, 2 * width :] = value_bias_ref[...].astype(F32).reshape(1, width)
    heads, levels = text_ref.shape
    spot = lax.broadcasted_iota(jnp.int32, (levels, LANES), 1)
    level = lax.broadcasted_iota(jnp.int32, (levels, LANES), 0)
    table = jnp.zeros((heads, LANES), F32)
    for source, begin in ((text_ref, 0), (horiz_ref, X_TABLE), (vert_ref, Y_TABLE)):
        table = table + dot_nn(source[...], (spot == level + begin).astype(BF))
    table_ref[...] = jnp.concatenate([table, jnp.zeros((16 - heads, LANES), F32)], axis=0)

    def project(there):
        step = 256

        def body(index, carry):
            columns = pl.ds(pl.multiple_of(index * step, step), step)
            product = dot_nn(item_ref[there], weight_ref[:, columns])
            projected_ref[there, columns] = (product + bias_ref[:, columns]).astype(BF)
            return carry

        lax.fori_loop(0, 3 * width // step, body, 0)

    project(own)
    rows_out.wait()
    project(other)
    meta_out.wait()
    meta = rows_ref[...].astype(F32)
    tall = jnp.concatenate([meta, jnp.zeros((LANES - 8, meta.shape[1]), F32)], axis=0)
    columns_ref[...] = jnp.transpose(tall).astype(jnp.int32)


def projected_item(layer_in, fields, qkv_weight, query_bias, value_bias, tables):
    rows = 2 * layer_in.shape[1]
    width = layer_in.shape[2]
    return pl.pallas_call(
        project_kernel,
        in_specs=[VMEM] * 12,
        out_specs=[VMEM] * 5,
        out_shape=[
            jax.ShapeDtypeStruct((rows, width), BF),
            jax.ShapeDtypeStruct((rows, 3 * width), BF),
            jax.ShapeDtypeStruct((rows, LANES), jnp.int32),
            jax.ShapeDtypeStruct((8, rows), jnp.int32),
            jax.ShapeDtypeStruct((16, LANES), F32),
        ],
        scratch_shapes=[
            pltpu.VMEM((8, rows // 2), jnp.int32),
            pltpu.VMEM((1, 3 * width), F32),
            pltpu.SemaphoreType.DMA((4,)),
        ],
        compiler_params=pltpu.CompilerParams(
            collective_id=1, has_side_effects=True, vmem_limit_bytes=40 * MIB
        ),
        name="projected_item",
    )(layer_in, *fields, qkv_weight, query_bias, value_bias, *(t.T for t in tables))


EPSILON = 1e-05
TILE = 256


def vector(ref):
    return ref[...].astype(F32).reshape(1, ref.shape[0])


def gelu_and_slope(x):
    bell = jnp.exp(-0.5 * x * x)
    t = 1.0 / (1.0 + 0.23164188826 * jnp.abs(x))
    series = t * (
        0.127414796
        + t * (-0.142248368 + t * (0.7107068705 + t * (-0.7265760135 + t * 0.5307027145)))
    )
    tail = bell * series
    below = jnp.where(x >= 0.0, 1.0 - tail, tail)
    return x * below, below + x * (0.3989422804014327 * bell)


def row_mean(block):
    return jnp.mean(block, axis=1, keepdims=True)


def normalized(hidden):
    center = hidden - row_mean(hidden)
    scale = lax.rsqrt(row_mean(center * center) + EPSILON)
    return center * scale, scale


def norm_pulled(grad, unit, scale):
    return scale * (grad - row_mean(grad) - unit * row_mean(grad * unit))


def column_sum(block):
    return jnp.sum(block, axis=0, keepdims=True)


def feed_kernel(
    item_ref, mixed_ref, cotangent_ref, out_weight_ref, up_ref, down_ref,
    out_bias_ref, attn_gain_ref, attn_shift_ref, up_bias_ref, down_bias_ref,
    ffn_gain_ref, ffn_shift_ref,
    layer_ref, d_hidden_ref, d_mixed_ref, grad_out_ref, grad_down_ref, grad_up_ref, small_ref,
    cotangent_all, active, slope, unit, scale_ref, normed, normed_t, total, d_branch, d_branch_t,
    sems,
):
    step = pl.program_id(0)
    blocks = pl.num_programs(0) // 2
    rows, width = item_ref.shape
    count = rows // 2
    mine = lax.axis_index("seq")
    partner = (1 - mine, lax.axis_index("dp"))
    own = pl.ds(pl.multiple_of(mine * count, LANES), count)
    tiles = rows // TILE

    def sent():
        return remote(
            cotangent_ref.at[1 - mine], cotangent_all.at[own], sems.at[0], sems.at[1], partner
        )

    def over_tiles(size, body, carry):
        def run(index, state):
            return body(pl.ds(pl.multiple_of(index * size, size), size), state)

        return lax.fori_loop(0, rows // size, run, carry)

    @pl.when(step == 0)
    def _():
        barrier = pltpu.get_barrier_semaphore()
        pl.semaphore_signal(barrier, inc=1, device_id=partner, device_id_type=MESH)
        pl.semaphore_wait(barrier, 1)
        sent().start()
        small_ref[...] = jnp.zeros_like(small_ref)
        cotangent_all[own] = cotangent_ref[mine]
        out_bias, gain, shift = vector(out_bias_ref), vector(attn_gain_ref), vector(attn_shift_ref)

        def tile(there, carry):
            attn = dot_nn(mixed_ref[there].astype(BF), out_weight_ref[...]) + out_bias
            standard, scale = normalized(item_ref[there].astype(F32) + attn)
            unit[there] = standard
            scale_ref[there] = jnp.broadcast_to(scale, (scale.shape[0], LANES))
            result = standard * gain + shift
            normed[there] = result.astype(BF)
            normed_t[:, there] = jnp.transpose(result).astype(BF)
            return carry

        over_tiles(TILE, tile, 0)
        total[...] = jnp.zeros_like(total)

    @pl.when(step < blocks)
    def _():
        bias = up_bias_ref[pl.ds(pl.multiple_of(step * width, LANES), width)]
        bias = bias.astype(F32).reshape(1, width)

        def tile(there, carry):
            value, grade = gelu_and_slope(dot_nn(normed[there], up_ref[...]) + bias)
            active[step, there] = value.astype(BF)
            slope[step, there] = grade
            return carry

        over_tiles(TILE, tile, 0)

        def tile(there, carry):
            total[there] += dot_nn(active[step, there], down_ref[...])
            return carry

        over_tiles(TILE, tile, 0)

    @pl.when(step == blocks)
    def _():
        sent().wait()
        gain, shift, bias = vector(ffn_gain_ref), vector(ffn_shift_ref), vector(down_bias_ref)
        first_gain, first_shift = vector(attn_gain_ref), vector(attn_shift_ref)

        def tile(there, sums):
            hidden = unit[there] * first_gain + first_shift + (total[there] + bias)
            standard, scale = normalized(hidden)
            layer_ref[there] = (standard * gain + shift).astype(BF)
            cotangent = cotangent_all[there].astype(F32)
            pulled = norm_pulled(cotangent * gain, standard, scale)
            total[there] = pulled
            low = pulled.astype(BF)
            d_branch[there] = low
            return (
                sums[0] + column_sum(low.astype(F32)),
                sums[1] + column_sum(cotangent * standard),
                sums[2] + column_sum(cotangent),
            )

        zero = jnp.zeros((1, width), F32)
        sums = over_tiles(64, tile, (zero, zero, zero))
        for row, value in zip((5, 6, 7), sums):
            small_ref[row : row + 1] = value

        def turn(there, carry):
            d_branch_t[:, there] = jnp.transpose(d_branch[there].astype(F32)).astype(BF)
            return carry

        over_tiles(TILE, turn, 0)

    @pl.when(step >= blocks)
    def _():
        block = step - blocks

        def tile(there, carry):
            grad_down_ref[there] = dot_nn(d_branch_t[there], active[block]).astype(BF)
            return carry

        over_tiles(TILE, tile, 0)

        def tile(there, carry):
            d_up = (dot_nt(d_branch[there], down_ref[...]) * slope[block, there]).astype(BF)
            active[block, there] = d_up
            return carry + column_sum(d_up.astype(F32))

        sums = over_tiles(TILE, tile, jnp.zeros((1, width), F32))
        small_ref[pl.ds(8 + block, 1)] = sums

        def tile(there, carry):
            grad_up_ref[there] = dot_nn(normed_t[there], active[block]).astype(BF)
            total[there] += dot_nt(active[block, there], up_ref[...])
            return carry

        over_tiles(TILE, tile, 0)

    @pl.when(step == 2 * blocks - 1)
    def _():
        gain = vector(attn_gain_ref)

        def tile(there, sums):
            d_normed = total[there]
            standard = unit[there]
            d_hidden = norm_pulled(d_normed * gain, standard, scale_ref[there, :1])
            d_hidden_ref[there] = d_hidden
            low = d_hidden.astype(BF)
            d_branch[there] = low
            return (
                sums[0] + column_sum(low.astype(F32)),
                sums[1] + column_sum(d_normed * standard),
                sums[2] + column_sum(d_normed),
            )

        zero = jnp.zeros((1, width), F32)
        sums = over_tiles(64, tile, (zero, zero, zero))
        for row, value in zip((2, 3, 4), sums):
            small_ref[row : row + 1] = value

        def turn(there, carry):
            normed_t[:, there] = jnp.transpose(mixed_ref[there]).astype(BF)
            return carry

        over_tiles(TILE, turn, 0)

        def tile(there, carry):
            d_mixed_ref[there] = dot_nt(d_branch[there], out_weight_ref[...]).astype(BF)
            grad_out_ref[there] = dot_nn(normed_t[there], d_branch[...]).astype(BF)
            return carry

        over_tiles(TILE, tile, 0)


def fed_forward_and_back(
    item, mixed, cotangent, out_weight, up_weight, down_weight, vectors,
):
    rows, width = item.shape
    blocks = up_weight.shape[1] // width
    whole = pl.BlockSpec(memory_space=pltpu.VMEM)
    square = lambda kind: jax.ShapeDtypeStruct((rows, width), kind)
    later = lambda i: jnp.maximum(i - blocks, 0)
    return pl.pallas_call(
        feed_kernel,
        grid=(2 * blocks,),
        in_specs=[whole] * 4
        + [
            pl.BlockSpec((width, width), lambda i: (0, lax.rem(i, blocks))),
            pl.BlockSpec((width, width), lambda i: (lax.rem(i, blocks), 0)),
        ]
        + [whole] * 7,
        out_specs=[whole] * 4
        + [
            pl.BlockSpec((width, width), lambda i: (later(i), 0)),
            pl.BlockSpec((width, width), lambda i: (later(i), 0)),
            whole,
        ],
        out_shape=[
            square(BF), square(F32), square(BF), jax.ShapeDtypeStruct((width, width), BF),
            jax.ShapeDtypeStruct((blocks * width, width), BF),
            jax.ShapeDtypeStruct((blocks * width, width), BF),
            jax.ShapeDtypeStruct((16, width), F32),
        ],
        scratch_shapes=[
            pltpu.VMEM((rows, width), BF),
            pltpu.VMEM((blocks, rows, width), BF),
            pltpu.VMEM((blocks, rows, width), F32),
            pltpu.VMEM((rows, width), F32),
            pltpu.VMEM((rows, LANES), F32),
            pltpu.VMEM((rows, width), BF),
            pltpu.VMEM((width, rows), BF),
            pltpu.VMEM((rows, width), F32),
            pltpu.VMEM((rows, width), BF),
            pltpu.VMEM((width, rows), BF),
            pltpu.SemaphoreType.DMA((2,)),
        ],
        compiler_params=pltpu.CompilerParams(
            collective_id=2, has_side_effects=True, vmem_limit_bytes=60 * MIB
        ),
        name="feed_forward",
    )(item, mixed, cotangent, out_weight, up_weight, down_weight, *vectors)


def finish_kernel(
    summed_ref, grad_input_ref, small_ref, diagonal_ref,
    down_ref, up_ref, out_ref, qkv_ref, input_ref, *singles,
):
    step = pl.program_id(0)
    piece = summed_ref[...].astype(F32)

    @pl.when(step < 4)
    def _():
        down_ref[...] = jnp.transpose(piece)

    @pl.when((step >= 4) & (step < 8))
    def _():
        up_ref[...] = piece

    @pl.when(step == 8)
    def _():
        out_ref[...] = piece

    @pl.when(step > 8)
    def _():
        qkv_ref[...] = piece

    @pl.when(step == 0)
    def _():
        input_ref[...] = grad_input_ref[...].astype(F32)
        for row in range(8):
            singles[row][...] = small_ref[row]
        width = small_ref.shape[1]
        for row in range(4):
            singles[8][row * width : row * width + width] = small_ref[8 + row]
        heads, levels = singles[9].shape
        diagonals = diagonal_ref[...]
        level = lax.broadcasted_iota(jnp.int32, (LANES, LANES), 1)
        lane = lax.broadcasted_iota(jnp.int32, (LANES, LANES), 0)
        for table, (first, size, skip) in enumerate(((0, 4, 0), (4, 2, 1), (6, 2, 1))):
            total = jnp.zeros((heads, LANES), F32)
            for row in range(size):
                distance = lane + LANES * (row + skip - 2)
                chosen = (bucket(distance) == level).astype(F32)
                total = total + jnp.dot(
                    diagonals[:, first + row, :], chosen, preferred_element_type=F32,
                    precision=lax.Precision.HIGHEST,
                )
            singles[9 + table][...] = total[:, :levels]


def finished(summed, grad_input, small, diagonals, hidden, levels):
    width = summed.shape[1]
    heads = diagonals.shape[0]
    blocks = hidden // width
    whole = pl.BlockSpec(memory_space=pltpu.VMEM)
    held = lambda i, first, count: jnp.clip(i - first, 0, count - 1)
    square = (width, width)
    single = jax.ShapeDtypeStruct((width,), F32)
    table = jax.ShapeDtypeStruct((heads, levels), F32)
    return pl.pallas_call(
        finish_kernel,
        grid=(2 * blocks + 4,),
        in_specs=[pl.BlockSpec(square, lambda i: (i, 0)), whole, whole, whole],
        out_specs=[
            pl.BlockSpec(square, lambda i: (held(i, 0, blocks), 0)),
            pl.BlockSpec(square, lambda i: (0, held(i, blocks, blocks))),
            pl.BlockSpec(square, lambda i: (0, 0)),
            pl.BlockSpec(square, lambda i: (0, held(i, 2 * blocks + 1, 3))),
        ]
        + [whole] * 13,
        out_shape=[
            jax.ShapeDtypeStruct((hidden, width), F32),
            jax.ShapeDtypeStruct((width, hidden), F32),
            jax.ShapeDtypeStruct((width, width), F32),
            jax.ShapeDtypeStruct((width, 3 * width), F32),
            jax.ShapeDtypeStruct(grad_input.shape, F32),
        ]
        + [single] * 8
        + [jax.ShapeDtypeStruct((hidden,), F32)]
        + [table] * 3,
        compiler_params=pltpu.CompilerParams(vmem_limit_bytes=56 * MIB),
        name="finished",
    )(summed, grad_input, small, diagonals)


PIECE = 16
HALVES = 2


def device_at(seq, core, y, z, depth, group):
    return (seq, (group * depth + z) * 4 + y * 2 + core)


class Summing:
    def __init__(self, depth, out_ref, scratch):
        (self.work, self.fresh, self.first_in, self.second_a, self.second_b, self.third_a,
         self.third_b, self.final, self.pair_sems, self.block_sems, self.line_sems,
         self.local_sems) = scratch
        self.depth, self.out_ref = depth, out_ref
        self.columns = self.work.shape[2]
        self.rows = 16 * PIECE * depth
        self.half, self.quarter, self.eighth = self.rows // 2, self.rows // 4, self.rows // 8
        self.part = self.rows // 16
        place = lax.axis_index("dp")
        self.x = x = lax.axis_index("seq")
        self.core = core = lax.rem(place, 2)
        self.y = y = lax.rem(lax.div(place, 2), 2)
        self.z = z = lax.rem(lax.div(place, 4), depth)
        group = lax.div(place, 4 * depth)
        at = lambda *spot: device_at(*spot, depth, group)
        self.over_core = at(x, 1 - core, y, z)
        self.over_x = at(1 - x, core, y, z)
        self.over_y = at(x, core, 1 - y, z)
        self.on_line = [at(x, core, y, lax.rem(z + s, depth)) for s in range(1, depth)]
        self.hop_devices = [self.over_core, self.over_x, self.over_y]
        reach = 1
        while reach < depth:
            up = lax.rem(lax.div(z, reach), 2)
            self.hop_devices.append(at(x, core, y, z + reach - 2 * reach * up))
            reach *= 2

    def greet(self):
        barrier = pltpu.get_barrier_semaphore()
        devices = [self.over_core, self.over_x, self.over_y] + self.on_line
        for device in devices:
            pl.semaphore_signal(barrier, inc=1, device_id=device, device_id_type=MESH)
        pl.semaphore_wait(barrier, len(devices))

    def block(self, source, target, level, side, chunk, device):
        sems = self.block_sems
        return remote(
            source, target, sems.at[0, level, side, chunk], sems.at[1, level, side, chunk], device
        )

    def spread(self, level, chunk, source, target):
        sems = self.line_sems
        return [
            remote(
                source(step), target(step), sems.at[0, level, step - 1, chunk],
                sems.at[1, level, step - 1, chunk], self.on_line[step - 1],
            )
            for step in range(1, self.depth)
        ]

    def after(self, step):
        return lax.rem(self.z + step, self.depth)

    def before(self, step):
        return lax.rem(self.z + self.depth - step, self.depth)

    def held(self, chunk, begin, size):
        return self.work.at[chunk, pl.ds(begin, size)]

    def out(self, chunk, begin, size, core=None):
        core = self.core if core is None else core
        start = lax.div(chunk, HALVES) * self.rows + core * self.half + begin
        return self.out_ref.at[
            pl.ds(pl.multiple_of(start, PIECE), size), pl.ds(self.column(chunk), self.columns)
        ]

    def column(self, chunk):
        return pl.multiple_of(lax.rem(chunk, HALVES) * self.columns, LANES)

    def own_a(self):
        return self.x * self.eighth + self.y * self.part

    def own_b(self):
        return self.quarter + self.y * self.eighth

    def first(self, chunk):
        return [
            self.block(
                self.held(chunk, (1 - self.x) * self.eighth, self.eighth),
                self.first_in.at[chunk, 0], 0, 0, chunk, self.over_x,
            ),
            self.block(
                self.held(chunk, self.quarter + (1 - self.y) * self.eighth, self.eighth),
                self.first_in.at[chunk, 1], 0, 1, chunk, self.over_y,
            ),
        ]

    def second(self, chunk):
        return [
            self.block(
                self.held(chunk, self.x * self.eighth + (1 - self.y) * self.part, self.part),
                self.second_a.at[chunk], 1, 0, chunk, self.over_y,
            )
        ] + self.spread(
            0, chunk,
            lambda s: self.held(chunk, self.own_b() + self.after(s) * 2 * PIECE, 2 * PIECE),
            lambda s: self.second_b.at[chunk, s - 1],
        )

    def third(self, chunk):
        start = self.own_b() + self.z * 2 * PIECE + (1 - self.x) * PIECE
        return [
            self.block(
                self.held(chunk, start, PIECE), self.third_b.at[chunk], 1, 1, chunk, self.over_x
            )
        ] + self.spread(
            1, chunk,
            lambda s: self.held(chunk, self.own_a() + self.after(s) * PIECE, PIECE),
            lambda s: self.third_a.at[chunk, s - 1],
        )

    def last_spots(self):
        return (
            self.own_a() + self.z * PIECE,
            self.own_b() + self.z * 2 * PIECE + self.x * PIECE,
        )

    def kept(self, chunk):
        return [
            pltpu.make_async_copy(
                self.final.at[chunk, side], self.out(chunk, begin, PIECE),
                self.local_sems.at[1 + side, chunk],
            )
            for side, begin in enumerate(self.last_spots())
        ]

    def third_back(self, chunk, arriving):
        x = 1 - self.x if arriving else self.x
        owner = self.before if arriving else (lambda s: self.z)
        return [
            self.block(
                self.final.at[chunk, 1],
                self.out(chunk, self.own_b() + self.z * 2 * PIECE + x * PIECE, PIECE),
                2, 1, chunk, self.over_x,
            )
        ] + self.spread(
            2, chunk,
            lambda s: self.final.at[chunk, 0],
            lambda s: self.out(chunk, self.own_a() + owner(s) * PIECE, PIECE),
        )

    def second_back(self, chunk, arriving):
        y = 1 - self.y if arriving else self.y
        owner = self.before if arriving else (lambda s: self.z)
        mine = self.out(chunk, self.own_b() + self.z * 2 * PIECE, 2 * PIECE)
        return [
            self.block(
                self.out(chunk, self.own_a(), self.part),
                self.out(chunk, self.x * self.eighth + y * self.part, self.part),
                2, 0, chunk, self.over_y,
            )
        ] + self.spread(
            3, chunk,
            lambda s: mine,
            lambda s: self.out(chunk, self.own_b() + owner(s) * 2 * PIECE, 2 * PIECE),
        )

    def first_back(self, chunk, arriving):
        x = 1 - self.x if arriving else self.x
        y = 1 - self.y if arriving else self.y
        return [
            self.block(
                self.out(chunk, self.x * self.eighth, self.eighth),
                self.out(chunk, x * self.eighth, self.eighth), 3, 0, chunk, self.over_x,
            ),
            self.block(
                self.out(chunk, self.own_b(), self.eighth),
                self.out(chunk, self.quarter + y * self.eighth, self.eighth),
                3, 1, chunk, self.over_y,
            ),
        ]

    def pair_back(self, chunk, arriving):
        core = 1 - self.core if arriving else self.core
        return [
            remote(
                self.out(chunk, 0, self.half), self.out(chunk, 0, self.half, core),
                self.pair_sems.at[0, 1, chunk], self.pair_sems.at[1, 1, chunk], self.over_core,
            )
        ]

    def pair_copies(self, chunk, source, begin):
        columns = pl.ds(self.column(chunk), self.columns)
        at = lambda core: source.at[
            pl.ds(pl.multiple_of(begin + core * self.half, PIECE), self.half), columns
        ]
        return [
            remote(
                at(1 - self.core), self.fresh.at[chunk], self.pair_sems.at[0, 0, chunk],
                self.pair_sems.at[1, 0, chunk], self.over_core,
            ),
            pltpu.make_async_copy(at(self.core), self.work.at[chunk], self.local_sems.at[0, chunk]),
        ]

    def add(self, chunk, begin, sources, size):
        step = min(size, 64)

        def body(index, carry):
            offset = pl.multiple_of(index * step, PIECE)
            there = pl.ds(pl.multiple_of(begin + offset, PIECE), step)
            total = self.work[chunk, there].astype(F32)
            for source in sources:
                total = total + source[pl.ds(offset, step)].astype(F32)
            self.work[chunk, there] = total.astype(BF)
            return carry

        lax.fori_loop(0, size // step, body, 0)

    def stage(self, number, chunk, start_pair, wait_pair):
        def wait(copies):
            for copy in copies:
                copy.wait()

        def start(copies):
            for copy in copies:
                copy.start()

        x, y = self.x, self.y
        if number == 0:
            start_pair(chunk)
        elif number == 1:
            wait_pair(chunk)
            self.add(chunk, 0, [self.fresh.at[chunk]], self.half)
            start(self.first(chunk))
        elif number == 2:
            wait(self.first(chunk))
            self.add(chunk, x * self.eighth, [self.first_in.at[chunk, 0]], self.eighth)
            self.add(chunk, self.own_b(), [self.first_in.at[chunk, 1]], self.eighth)
            start(self.second(chunk))
        elif number == 3:
            wait(self.second(chunk))
            self.add(chunk, self.own_a(), [self.second_a.at[chunk]], self.part)
            self.add(
                chunk, self.own_b() + self.z * 2 * PIECE,
                [self.second_b.at[chunk, s] for s in range(self.depth - 1)], 2 * PIECE,
            )
            start(self.third(chunk))
        elif number == 4:
            wait(self.third(chunk))
            spot_a, spot_b = self.last_spots()
            self.add(
                chunk, spot_a, [self.third_a.at[chunk, s] for s in range(self.depth - 1)], PIECE
            )
            self.add(chunk, spot_b, [self.third_b.at[chunk]], PIECE)
            for side, spot in enumerate((spot_a, spot_b)):
                self.final[chunk, side] = self.work[chunk, pl.ds(pl.multiple_of(spot, PIECE), PIECE)]
            start(self.third_back(chunk, False) + self.kept(chunk))
        elif number == 5:
            wait(self.third_back(chunk, True) + self.kept(chunk))
            start(self.second_back(chunk, False))
        elif number == 6:
            wait(self.second_back(chunk, True))
            start(self.first_back(chunk, False))
        elif number == 7:
            wait(self.first_back(chunk, True))
            start(self.pair_back(chunk, False))
        else:
            wait(self.pair_back(chunk, True))

    def tick(self, index, chunks, start_pair, wait_pair):
        for number in range(8, -1, -1):
            chunk = index - number

            @pl.when((chunk >= 0) & (chunk < chunks))
            def _(number=number, chunk=chunk):
                self.stage(number, chunk, start_pair, wait_pair)


def summing_scratch(depth, chunks, columns):
    rows = 16 * PIECE * depth
    others = max(depth - 1, 1)
    dma = pltpu.SemaphoreType.DMA
    return [
        pltpu.VMEM((chunks, rows // 2, columns), BF),
        pltpu.VMEM((chunks, rows // 2, columns), BF),
        pltpu.VMEM((chunks, 2, rows // 8, columns), BF),
        pltpu.VMEM((chunks, rows // 16, columns), BF),
        pltpu.VMEM((chunks, others, 2 * PIECE, columns), BF),
        pltpu.VMEM((chunks, others, PIECE, columns), BF),
        pltpu.VMEM((chunks, PIECE, columns), BF),
        pltpu.VMEM((chunks, 2, PIECE, columns), BF),
        dma((2, 2, chunks)),
        dma((2, 4, 2, chunks)),
        dma((2, 4, others, chunks)),
        dma((3, chunks)),
    ]


def last_kernel(
    depth, chunks, steps, *refs,
):
    (meta_ref, rows_ref, table_ref, q_ref, k_ref, v_ref, mixed_ref, grad_ref, log_ref,
     item_ref, weight_ref, d_hidden_ref, small_ref, grad_down_ref, grad_up_ref, grad_out_ref,
     layer_ref,
     out_ref, small_out, diagonal_out, layer_out, input_out,
     *scratch) = refs
    static, scratch = scratch[:11], scratch[11:]
    (d_query, d_key, d_value, item_t, tail, input_grad, small_in, diagonal_in, small_sems,
     item_sems, *scratch) = scratch
    summing = Summing(depth, out_ref, scratch)
    step = pl.program_id(0)
    pairs = d_query.shape[0]
    rows, width = item_ref.shape
    count = rows // 2
    hidden = grad_down_ref.shape[0]
    per_source = hidden // summing.rows * HALVES
    hops = len(summing.hop_devices)
    x = summing.x
    first_hop = 2 * pairs + 2

    def out_copy():
        return pltpu.make_async_copy(
            grad_out_ref, tail.at[pl.ds(0, width)], item_sems.at[0, 2]
        )

    def item_copies(index, source, target):
        return [
            pltpu.make_async_copy(
                source.at[pl.ds(x * count, count)], target.at[x], item_sems.at[0, index]
            ),
            remote(
                source.at[pl.ds((1 - x) * count, count)], target.at[x], item_sems.at[1, index],
                item_sems.at[2, index], summing.over_x,
            ),
        ]

    def layer_copies():
        return item_copies(0, layer_ref, layer_out)

    def input_copies():
        return item_copies(1, input_grad, input_out)

    def small_copies(hop):
        device = summing.hop_devices[hop]
        return [
            remote(source, landing.at[hop], small_sems.at[0, kind, hop],
                   small_sems.at[1, kind, hop], device)
            for kind, (source, landing) in enumerate(
                ((small_out, small_in), (diagonal_out, diagonal_in))
            )
        ]

    @pl.when(step == 0)
    def _():
        summing.greet()
        out_copy().start()
        for copy in layer_copies():
            copy.start()
        small_out[...] = small_ref[...]
        static_prepare(meta_ref, static)
        for tile in range(rows // TILE):
            there = slice(tile * TILE, tile * TILE + TILE)
            item_t[:, there] = jnp.transpose(item_ref[there].astype(F32)).astype(BF)

    sources = (grad_down_ref, grad_up_ref, tail)

    def start_pair(chunk):
        for index, source in enumerate(sources):
            @pl.when(lax.div(chunk, per_source) == index)
            def _(index=index, source=source):
                begin = lax.div(chunk - index * per_source, HALVES) * summing.rows
                for copy in summing.pair_copies(chunk, source, begin):
                    copy.start()

    def wait_pair(chunk):
        for copy in summing.pair_copies(chunk, tail, 0):
            copy.wait()

    def tick(index):
        summing.tick(index, chunks, start_pair, wait_pair)
        for hop in range(hops + 1):
            @pl.when(index == first_hop + hop)
            def _(hop=hop):
                if hop > 0:
                    for copy in small_copies(hop - 1):
                        copy.wait()
                    small_out[...] = small_out[...] + small_in[hop - 1]
                    diagonal_out[...] = diagonal_out[...] + diagonal_in[hop - 1]
                if hop < hops:
                    for copy in small_copies(hop):
                        copy.start()

    def slab(part, source):
        def body(tile, carry):
            there = pl.ds(pl.multiple_of(tile * TILE, TILE), TILE)
            target = pl.ds(pl.multiple_of((1 + part) * width + tile * TILE, TILE), TILE)
            for pair in range(pairs):
                columns = slice(pair * LANES, pair * LANES + LANES)
                tail[target, columns] = dot_nn(item_t[there], source[pair]).astype(BF)
            return carry

        lax.fori_loop(0, width // TILE, body, 0)

    for parity in range(2):
        tick(2 * step + parity)

        @pl.when(step < pairs)
        def _(parity=parity):
            head_back(
                parity, step, meta_ref, rows_ref, table_ref, q_ref, k_ref, v_ref, mixed_ref,
                grad_ref, log_ref, static, d_query, d_key, d_value, diagonal_out,
            )

        if parity == 0:
            @pl.when(step == pairs)
            def _():
                slab(1, d_key)

        if parity == 1:
            @pl.when(step == pairs - 1)
            def _():
                out_copy().wait()
                slab(0, d_query)

            @pl.when(step == pairs)
            def _():
                slab(2, d_value)

                def body(tile, carry):
                    there = pl.ds(pl.multiple_of(tile * TILE, TILE), TILE)
                    total = d_hidden_ref[there]
                    for pair in range(pairs):
                        for part, piece in enumerate((d_query, d_key, d_value)):
                            begin = part * width + pair * LANES
                            value = piece[pair, there]
                            total = total + dot_nt(value, weight_ref[:, begin : begin + LANES])
                    input_grad[there] = total.astype(BF)
                    return carry

                lax.fori_loop(0, rows // TILE, body, 0)
                for pair in range(pairs):
                    columns = slice(pair * LANES, pair * LANES + LANES)
                    small_out[0:1, columns] = column_sum(d_query[pair].astype(F32))
                    small_out[1:2, columns] = column_sum(d_value[pair].astype(F32))
                for copy in input_copies():
                    copy.start()

    @pl.when(step == steps - 1)
    def _():
        for copy in layer_copies() + input_copies():
            copy.wait()


def summed_with_attention_back(
    meta_columns, meta_rows, table_rows, projected, mixed, d_mixed, logs, item, qkv_weight,
    d_hidden, small, grad_down, grad_up, grad_out, layer,
):
    size = lax.axis_size("dp")
    depth = 4 if size % 16 == 0 else size // 4
    rows, width = item.shape
    pairs = width // LANES
    hidden = grad_down.shape[0]
    chunks = 3 * hidden // (16 * PIECE * depth) * HALVES
    steps = (max(chunks + 9, 2 * pairs + 10) + 1) // 2
    held = lambda p: jnp.minimum(p, pairs - 1)
    hops = 3 + (depth - 1).bit_length()

    def block(part):
        return pl.BlockSpec((rows, LANES), lambda p: (0, part * pairs + held(p)))

    whole = pl.BlockSpec(memory_space=pltpu.VMEM)
    anywhere = pl.BlockSpec(memory_space=pl.ANY)
    halves = jax.ShapeDtypeStruct((2, rows // 2, width), BF)
    diagonals = jax.ShapeDtypeStruct((2 * pairs, 8, LANES), F32)
    dma = pltpu.SemaphoreType.DMA
    summed, small, diagonals, layer_out, grad_input = pl.pallas_call(
        functools.partial(last_kernel, depth, chunks, steps),
        grid=(steps,),
        in_specs=[whole] * 3
        + [block(0), block(1), block(2), block(0), block(0)]
        + [pl.BlockSpec((1, rows, LANES), lambda p: (held(p), 0, 0))]
        + [whole] * 4
        + [anywhere] * 4,
        out_specs=[anywhere, whole, whole, anywhere, anywhere],
        out_shape=[
            jax.ShapeDtypeStruct((3 * hidden, width), BF),
            jax.ShapeDtypeStruct(small.shape, F32),
            diagonals, halves, halves,
        ],
        scratch_shapes=static_scratch(rows)
        + [pltpu.VMEM((LANES, rows), BF)] * 3
        + [pltpu.VMEM((pairs, rows, LANES), BF)] * 3
        + [
            pltpu.VMEM((width, rows), BF),
            pltpu.VMEM((hidden, width), BF),
            pltpu.VMEM((rows, width), BF),
            pltpu.VMEM((hops,) + small.shape, F32),
            pltpu.VMEM((hops,) + diagonals.shape, F32),
            dma((2, 2, hops)),
            dma((3, 3)),
        ]
        + summing_scratch(depth, chunks, width // HALVES),
        compiler_params=pltpu.CompilerParams(
            collective_id=0, has_side_effects=True, vmem_limit_bytes=62 * MIB
        ),
        name="summed_with_attention_back",
    )(meta_columns, meta_rows, table_rows, projected, projected, projected, mixed, d_mixed, logs,
      item, qkv_weight, d_hidden, small, grad_down, grad_up, grad_out, layer)
    span = 4 * depth
    if size > span:
        groups = [list(range(first, size, span)) for first in range(span)]
        summed, small, diagonals = lax.psum(
            (summed.astype(F32), small, diagonals), "dp", axis_index_groups=groups
        )
        summed = summed.astype(BF)
    return summed, small, diagonals, layer_out, grad_input


def per_device(
    layer_in, segment, key_mask, position, layout_x, layout_y,
    qkv_weight, query_bias, value_bias, out_weight, out_bias, attn_gain, attn_shift,
    up_weight, up_bias, down_weight, down_bias, ffn_gain, ffn_shift,
    text_table, horiz_table, vert_table, cotangent,
):
    width = layer_in.shape[-1]
    item, projected, meta_columns, meta_rows, table_rows = projected_item(
        layer_in, (segment, key_mask, position, layout_x, layout_y),
        qkv_weight, query_bias, value_bias, (text_table, horiz_table, vert_table),
    )
    mixed, logs = attention_forward(meta_columns, meta_rows, table_rows, projected, width)
    layer, d_hidden, d_mixed, grad_out, grad_down, grad_up, small = fed_forward_and_back(
        item, mixed, cotangent, out_weight, up_weight, down_weight,
        (out_bias, attn_gain, attn_shift, up_bias, down_bias, ffn_gain, ffn_shift),
    )
    summed, small, diagonals, layer_out, grad_input = summed_with_attention_back(
        meta_columns, meta_rows, table_rows, projected, mixed, d_mixed, logs, item, qkv_weight,
        d_hidden, small, grad_down, grad_up, grad_out, layer,
    )
    done = finished(
        summed, grad_input, small, diagonals, up_weight.shape[1], text_table.shape[0]
    )
    sum_down, sum_up, sum_out, sum_qkv, grad_input = done[:5]
    singles, tables = done[5:14], [t.T for t in done[14:]]
    return (
        layer_out, grad_input, sum_qkv, singles[0], singles[1], sum_out, singles[2], singles[3],
        singles[4], sum_up, singles[8], sum_down, singles[5], singles[6], singles[7],
        tables[0], tables[1], tables[2],
    )


def solution(mesh):
    rows = P("dp", "seq", None)
    marks_spec = P("dp", "seq")
    return jax.shard_map(
        per_device,
        mesh=mesh,
        in_specs=(rows,) + (marks_spec,) * 5 + (P(),) * 16 + (rows,),
        out_specs=(rows, rows) + (P(),) * 16,
        check_vma=False,
    )
```

```python
import functools

import jax
import jax.numpy as jnp
from jax import lax
from jax.experimental import pallas as pl
from jax.experimental.pallas import tpu as pltpu
from jax.sharding import PartitionSpec as P

BF = jnp.bfloat16
F32 = jnp.float32
BIG = 1e30
LANES = 128
HEAD = 64
TEXT = 512
POS = 64
COORD = 48
Y0 = 64
GROUP0 = 112
MEMBER0 = 116
FLAG = 124
LOG0 = 125
X_TABLE = 33
Y_TABLE = 66
NOTHING = 127


def dot_nt(a, b):
    return lax.dot_general(a, b, (((1,), (1,)), ((), ())), preferred_element_type=F32)


def dot_nn(a, b):
    return lax.dot_general(a, b, (((1,), (0,)), ((), ())), preferred_element_type=F32)


def looked_up(table_row, index):
    rows = index.shape[0]
    return jnp.take_along_axis(jnp.broadcast_to(table_row, (rows, LANES)), index, axis=1)


def bucket(distance):
    return jnp.clip(distance, -16, 16) + 16


def between(lane, low, high):
    return (lane >= low) & (lane < high)


def columns_of(meta_ref):
    return tuple(meta_ref[:, field : field + 1] for field in range(5))


def marks(meta_ref):
    segment, key_mask, position, across, down = columns_of(meta_ref)
    rows = segment.shape[0]
    lane = lax.broadcasted_iota(jnp.int32, (rows, LANES), 1)
    row = lax.broadcasted_iota(jnp.int32, (rows, LANES), 0)
    even = between(lane, HEAD, HEAD + COORD) & (lane - HEAD == across)
    odd = (lane < COORD) & (lane == across)
    group = (segment - 1) >> 3
    member = (segment - 1) & 7
    named = segment > 0
    shared = (
        ((row < TEXT) & (lane < POS) & (lane == position))
        | (between(lane, Y0, Y0 + COORD) & (lane - Y0 == down))
        | (named & between(lane, GROUP0, MEMBER0) & (lane - GROUP0 == group))
        | (named & between(lane, MEMBER0, FLAG) & (lane - MEMBER0 == member))
        | ((lane == FLAG) & (key_mask <= 0))
        | (lane >= LOG0)
    )
    return tuple(jnp.where(m, 1.0, 0.0).astype(BF) for m in (even, odd, shared))


def barred(meta_ref):
    segment = meta_ref[:, 0:1]
    rows = segment.shape[0]
    lane = lax.broadcasted_iota(jnp.int32, (rows, LANES), 1)
    group = (segment - 1) >> 3
    member = (segment - 1) & 7
    shut = (
        ((segment > 0) & between(lane, GROUP0, MEMBER0) & (lane - GROUP0 != group))
        | ((segment < 0) & between(lane, GROUP0, MEMBER0))
        | ((segment > 0) & between(lane, MEMBER0, FLAG) & (lane - MEMBER0 != member))
        | (lane == FLAG)
    )
    return jnp.where(shut, -BIG, 0.0).astype(F32)


def query_index(meta_ref):
    segment, key_mask, position, across, down = columns_of(meta_ref)
    rows = segment.shape[0]
    lane = lax.broadcasted_iota(jnp.int32, (rows, LANES), 1)
    x_even = bucket(across - (lane - HEAD)) + X_TABLE
    x_odd = bucket(across - lane) + X_TABLE
    even = jnp.where(between(lane, HEAD, HEAD + COORD), x_even, NOTHING)
    odd = jnp.where(lane < COORD, x_odd, NOTHING)
    shared = jnp.where(
        lane < POS,
        bucket(position - lane),
        jnp.where(between(lane, Y0, Y0 + COORD), bucket(down - (lane - Y0)) + Y_TABLE, NOTHING),
    )
    return even, odd, shared


def image_key_index(meta_ref):
    position = meta_ref[TEXT:, 2:3]
    lane = lax.broadcasted_iota(jnp.int32, (position.shape[0], LANES), 1)
    return jnp.where(lane < POS, bucket(lane - position), NOTHING)


def prepare(meta_ref, mark_refs, bar_ref, index_refs, key_index_ref):
    for ref, value in zip(mark_refs, marks(meta_ref)):
        ref[...] = value
    bar_ref[...] = barred(meta_ref)
    for ref, value in zip(index_refs, query_index(meta_ref)):
        ref[...] = value
    key_index_ref[...] = image_key_index(meta_ref)


def image_offsets(row_positions, column_positions):
    return bucket(column_positions - row_positions)


def widened(parity, q, k, table_row, mark_refs, bar_ref, index_refs, key_index_ref, logs):
    rows = q.shape[0]
    lane = lax.broadcasted_iota(jnp.int32, (rows, LANES), 1)
    own = (lane < HEAD) if parity == 0 else (lane >= HEAD)
    first = jnp.where(own, q.astype(F32) * 0.125, looked_up(table_row, index_refs[parity][...]))
    second = looked_up(table_row, index_refs[2][...]) + bar_ref[...]
    if logs is not None:
        high = logs.astype(BF).astype(F32)
        middle = (logs - high).astype(BF).astype(F32)
        lowest = logs - high - middle
        second = jnp.where(
            lane == LOG0,
            -high,
            jnp.where(lane == LOG0 + 1, -middle, jnp.where(lane == LOG0 + 2, -lowest, second)),
        )
    first = first.astype(BF)
    second = second.astype(BF)
    mark_second = mark_refs[2][...]
    to_image = jnp.where(lane < POS, mark_second, second)
    key_first = jnp.where(own, k, mark_refs[parity][...])
    image_lane = lane[TEXT:]
    key_image = jnp.where(
        image_lane < POS,
        looked_up(table_row, key_index_ref[...]).astype(BF),
        mark_second[TEXT:],
    )
    q_text = jnp.concatenate([first, second], axis=1)
    q_image = jnp.concatenate([first, to_image], axis=1)
    k_text = jnp.concatenate([key_first[:TEXT], mark_second[:TEXT]], axis=1)
    k_image = jnp.concatenate([key_first[TEXT:], key_image], axis=1)
    return q_text, q_image, k_text, k_image


def image_bias(table_row, offsets):
    return jnp.concatenate(
        [looked_up(table_row, offsets[:, :LANES]), looked_up(table_row, offsets[:, LANES:])], axis=1
    )


def forward_kernel(
    meta_ref, rows_ref, table_ref, q_ref, k_ref, v_ref, mixed_ref, log_ref,
    even_ref, odd_ref, shared_ref, bar_ref, index_even, index_odd, index_shared, key_index_ref,
):
    mark_refs = (even_ref, odd_ref, shared_ref)
    index_refs = (index_even, index_odd, index_shared)

    @pl.when(pl.program_id(0) == 0)
    def _():
        prepare(meta_ref, mark_refs, bar_ref, index_refs, key_index_ref)

    rows = q_ref.shape[0]
    images = rows - TEXT
    q, k, v = q_ref[...], k_ref[...], v_ref[...]
    offsets = bucket(meta_ref[TEXT:, 2:3] - rows_ref[2:3, TEXT:])
    tile = 256
    parts = []
    for parity in range(2):
        table_row = table_ref[pl.ds(2 * pl.program_id(0) + parity, 1), :]
        q_text, q_image, k_text, k_image = widened(
            parity, q, k, table_row, mark_refs, bar_ref, index_refs, key_index_ref, None
        )
        bias = image_bias(table_row, offsets)
        outs = []
        logs = []
        for start in range(0, rows, tile):
            here = slice(start, start + tile)
            on_text = dot_nt(q_text[here], k_text)
            on_image = dot_nt(q_image[here], k_image)
            if start >= TEXT:
                on_image = on_image + bias[start - TEXT : start - TEXT + tile]
            top = jnp.maximum(
                jnp.max(on_text, axis=1, keepdims=True), jnp.max(on_image, axis=1, keepdims=True)
            )
            on_text = jnp.exp(on_text - top)
            on_image = jnp.exp(on_image - top)
            total = jnp.sum(on_text, axis=1, keepdims=True) + jnp.sum(
                on_image, axis=1, keepdims=True
            )
            out = dot_nn(on_text.astype(BF), v[:TEXT]) + dot_nn(on_image.astype(BF), v[TEXT:])
            outs.append(out / total)
            logs.append(jnp.broadcast_to(top + jnp.log(total), (tile, LANES)))
        parts.append((jnp.concatenate(outs, axis=0), jnp.concatenate(logs, axis=0)))
    lane = lax.broadcasted_iota(jnp.int32, (rows, LANES), 1)
    mixed_ref[...] = jnp.where(lane < HEAD, parts[0][0], parts[1][0])
    log_ref[0] = jnp.where(lane < HEAD, parts[0][1], parts[1][1])


def static_scratch(rows):
    return [
        pltpu.VMEM((rows, LANES), BF),
        pltpu.VMEM((rows, LANES), BF),
        pltpu.VMEM((rows, LANES), BF),
        pltpu.VMEM((rows, LANES), F32),
        pltpu.VMEM((rows, LANES), jnp.int32),
        pltpu.VMEM((rows, LANES), jnp.int32),
        pltpu.VMEM((rows, LANES), jnp.int32),
        pltpu.VMEM((rows - TEXT, LANES), jnp.int32),
    ]


def attention_forward(meta_columns, meta_rows, table_rows, projected, width):
    rows = projected.shape[0]
    pairs = width // LANES

    def block(part):
        return pl.BlockSpec((rows, LANES), lambda p: (0, part * pairs + p))

    whole = lambda shape: pl.BlockSpec(shape, lambda p: (0,) * len(shape))
    return pl.pallas_call(
        forward_kernel,
        grid=(pairs,),
        in_specs=[
            whole(meta_columns.shape),
            whole(meta_rows.shape),
            whole(table_rows.shape),
            block(0), block(1), block(2),
        ],
        out_specs=[
            pl.BlockSpec((rows, LANES), lambda p: (0, p)),
            pl.BlockSpec((1, rows, LANES), lambda p: (p, 0, 0)),
        ],
        out_shape=[
            jax.ShapeDtypeStruct((rows, width), F32),
            jax.ShapeDtypeStruct((pairs, rows, LANES), F32),
        ],
        scratch_shapes=static_scratch(rows),
        compiler_params=pltpu.CompilerParams(vmem_limit_bytes=48 * 1024 * 1024),
        name="attention_forward",
    )(meta_columns, meta_rows, table_rows, projected, projected, projected)


def skewed(block):
    size = block.shape[0]
    lane = lax.broadcasted_iota(jnp.int32, (size, LANES), 1)
    row = lax.broadcasted_iota(jnp.int32, (size, LANES), 0)
    turned = jnp.take_along_axis(block, (lane + row) & (LANES - 1), axis=1)
    straight = lane + row < LANES
    above = jnp.sum(jnp.where(straight, turned, 0.0), axis=0, keepdims=True)
    below = jnp.sum(jnp.where(straight, 0.0, turned), axis=0, keepdims=True)
    return above, below


def transposed(array):
    return jnp.transpose(array.astype(F32)).astype(array.dtype)


def static_prepare(meta_ref, static):
    (even_ref, odd_ref, shared_ref, bar_ref, index_even, index_odd, index_shared, key_index_ref,
     even_t, odd_t, shared_t) = static
    mark_refs = (even_ref, odd_ref, shared_ref)
    prepare(meta_ref, mark_refs, bar_ref, (index_even, index_odd, index_shared), key_index_ref)
    for ref, turned in zip(mark_refs, (even_t, odd_t, shared_t)):
        turned[...] = transposed(ref[...])


def head_back(
    parity, pair, meta_ref, rows_ref, table_ref, q_ref, k_ref, v_ref, mixed_ref, grad_ref, log_ref,
    static, d_query, d_key, d_value, diag_ref,
):
    (even_ref, odd_ref, shared_ref, bar_ref, index_even, index_odd, index_shared, key_index_ref,
     even_t, odd_t, shared_t) = static
    mark_refs = (even_ref, odd_ref, shared_ref)
    index_refs = (index_even, index_odd, index_shared)
    turned_refs = (even_t, odd_t, shared_t)
    rows = q_ref.shape[0]
    images = rows - TEXT
    tile = 256
    q, k, v, grad = q_ref[...], k_ref[...], v_ref[...], grad_ref[...]
    lane = lax.broadcasted_iota(jnp.int32, (rows, LANES), 1)
    products = grad.astype(F32) * mixed_ref[...].astype(F32)
    k_turned = transposed(k)
    offsets = bucket(rows_ref[2:3, TEXT:] - meta_ref[TEXT:, 2:3])
    is_image = rows_ref[1:2, TEXT:] > 0
    own = (lane < HEAD) if parity == 0 else (lane >= HEAD)
    spare = HEAD if parity == 0 else 0
    table_row = table_ref[pl.ds(2 * pair + parity, 1), :]
    logs = log_ref[0, :, parity * HEAD : parity * HEAD + 1]
    q_text, q_image, k_text, k_image = widened(
        parity, q, k, table_row, mark_refs, bar_ref, index_refs, key_index_ref, logs
    )
    bias = image_bias(table_row, offsets)
    delta = jnp.sum(jnp.where(own, products, 0.0), axis=1, keepdims=True)
    high = delta.astype(BF).astype(F32)
    middle = (delta - high).astype(BF).astype(F32)
    lowest = delta - high - middle
    grad_wide = jnp.where(
        own,
        grad.astype(F32),
        jnp.where(
            lane == spare,
            -high,
            jnp.where(lane == spare + 1, -middle, jnp.where(lane == spare + 2, -lowest, 0.0)),
        ),
    ).astype(BF)
    v_wide = jnp.where(
        own, v.astype(F32), jnp.where(between(lane, spare, spare + 3), 1.0, 0.0)
    ).astype(BF)
    q_marked = jnp.concatenate(
        [
            jnp.where(own, q.astype(F32) * 0.125, mark_refs[parity][...].astype(F32)).astype(BF),
            shared_ref[...],
        ],
        axis=1,
    )
    dq = jnp.zeros((HEAD, rows), F32)
    dks = []
    dvs = []
    first_sum = jnp.zeros((LANES, LANES), F32)
    second_sum = jnp.zeros((LANES, LANES), F32)
    text_image = jnp.zeros((LANES, images), F32)
    for start in range(0, rows, tile):
        here = slice(start, start + tile)
        if start < TEXT:
            scores = dot_nt(k_text[here], q_text)
        else:
            scores = dot_nt(k_image[start - TEXT : start - TEXT + tile], q_image)
            scores = jnp.concatenate([scores[:, :TEXT], scores[:, TEXT:] + bias], axis=1)
        soft = jnp.exp(scores)
        score_grad = soft * dot_nt(v_wide[here], grad_wide)
        low = score_grad.astype(BF)
        dvs.append(dot_nn(soft.astype(BF), grad))
        wide = dot_nn(low, q_marked)
        dks.append(wide[:, :LANES])
        dq = dq + dot_nn(k_turned[parity * HEAD : parity * HEAD + HEAD, here], low)
        rounded = wide.astype(BF)
        first_sum = first_sum + dot_nn(turned_refs[parity][:, here], rounded[:, :LANES])
        second_sum = second_sum + dot_nn(shared_t[:, here], rounded[:, LANES:])
        if start < TEXT:
            text_image = text_image + dot_nn(shared_t[:, here], low[:, TEXT:])
        else:
            by_position = wide[:, LANES:]
            on_image = score_grad[:, TEXT:]
    small = lax.broadcasted_iota(jnp.int32, (LANES, LANES), 1)
    small_row = lax.broadcasted_iota(jnp.int32, (LANES, LANES), 0)
    x0 = HEAD if parity == 0 else 0
    x_block = jnp.where(
        between(small, x0, x0 + COORD) & between(small_row, x0, x0 + COORD), first_sum, 0.0
    )
    y_block = jnp.where(
        between(small, Y0, Y0 + COORD) & between(small_row, Y0, Y0 + COORD), second_sum, 0.0
    )
    p_block = jnp.where((small < POS) & (small_row < POS), second_sum, 0.0)
    wide_lane = lax.broadcasted_iota(jnp.int32, (images, images), 1)
    outside = jnp.sum(jnp.where(is_image, 0.0, on_image), axis=1, keepdims=True)
    pairs = jnp.where(is_image, on_image, 0.0) + jnp.where(wide_lane == 0, outside, 0.0)
    outside_text = jnp.sum(jnp.where(is_image, 0.0, text_image), axis=1, keepdims=True)
    text_lane = lax.broadcasted_iota(jnp.int32, (LANES, images), 1)
    text_row = lax.broadcasted_iota(jnp.int32, (LANES, images), 0)
    text_image = jnp.where(is_image, text_image, 0.0) + jnp.where(
        text_lane == 0, outside_text, 0.0
    )
    text_image = jnp.where(text_row < POS, text_image, 0.0)
    first_lane = lax.broadcasted_iota(jnp.int32, (images, LANES), 1)
    left = pairs[:, :LANES] + jnp.where(first_lane < POS, by_position, 0.0)
    right = pairs[:, LANES:]
    a00, b00 = skewed(left[:LANES] + text_image[:, :LANES] + p_block)
    a01, b01 = skewed(right[:LANES] + text_image[:, LANES:])
    a10, b10 = skewed(left[LANES:])
    a11, b11 = skewed(right[LANES:])
    ax, bx = skewed(x_block)
    ay, by = skewed(y_block)
    diag_ref[2 * pair + parity] = jnp.concatenate(
        [b10, b00 + b11 + a10, a00 + a11 + b01, a01, bx, ax, by, ay], axis=0
    )
    empty = jnp.zeros_like(dq)
    both = [dq * 0.125, empty] if parity == 0 else [empty, dq * 0.125]
    results = (
        (d_query, jnp.transpose(jnp.concatenate(both, axis=0))),
        (d_key, jnp.concatenate(dks, axis=0)),
        (d_value, jnp.concatenate(dvs, axis=0)),
    )
    for ref, value in results:
        if parity == 1:
            value = jnp.where(own, value, ref[pair].astype(F32))
        ref[pair] = value.astype(BF)


MESH = pl.DeviceIdType.MESH
VMEM = pl.BlockSpec(memory_space=pltpu.VMEM)
HBM = pl.BlockSpec(memory_space=pltpu.HBM)
MIB = 1024 * 1024


def remote(src, dst, send, receive, device):
    return pltpu.make_async_remote_copy(
        src_ref=src, dst_ref=dst, send_sem=send, recv_sem=receive, device_id=device,
        device_id_type=MESH,
    )


def project_kernel(
    layer_ref, weight_hbm, *refs,
):
    small_hbm, refs = refs[:10], refs[10:]
    (item_ref, projected_out, columns_ref, rows_ref, table_ref,
     projected_ref, weight_ref, meta_send, bias_ref, sems, load_sems, store_sems), small = (
        refs[:12], refs[12:],
    )
    (segment_ref, mask_ref, position_ref, across_ref, down_ref, query_bias_ref, value_bias_ref,
     text_ref, horiz_ref, vert_ref) = small
    mine = lax.axis_index("seq")
    partner = (1 - mine, lax.axis_index("dp"))
    count, width = layer_ref.shape[1:]
    own = pl.ds(pl.multiple_of(mine * count, LANES), count)
    loads = [
        pltpu.make_async_copy(source, target, load_sems.at[index])
        for index, (source, target) in enumerate(
            list(zip(small_hbm, small))
            + [(layer_ref.at[mine], item_ref.at[own]), (weight_hbm, weight_ref)]
        )
    ]
    for load in loads:
        load.start()
    barrier = pltpu.get_barrier_semaphore()
    pl.semaphore_signal(barrier, inc=1, device_id=partner, device_id_type=MESH)
    pl.semaphore_wait(barrier, 1)
    pieces = count // LANES
    rows_out = [
        remote(
            layer_ref.at[1 - mine, pl.ds(piece * LANES, LANES)],
            item_ref.at[pl.ds(pl.multiple_of(mine * count + piece * LANES, LANES), LANES)],
            sems.at[0, piece], sems.at[1, piece], partner,
        )
        for piece in range(pieces)
    ]
    for copy in rows_out:
        copy.start()
    for load in loads[:-2]:
        load.wait()

    fields = (segment_ref, mask_ref, position_ref, across_ref, down_ref)
    blocks = [
        jnp.concatenate(
            [field[item : item + 1, :] for field in fields] + [jnp.zeros((3, count), jnp.int32)],
            axis=0,
        )
        for item in range(2)
    ]
    meta_send[...] = jnp.where(mine == 0, blocks[1], blocks[0])
    meta_out = remote(
        meta_send, rows_ref.at[:, own], sems.at[0, pieces], sems.at[1, pieces], partner
    )
    meta_out.start()
    rows_ref[:, own] = jnp.where(mine == 0, blocks[0], blocks[1])
    bias_ref[:, :width] = query_bias_ref[...].astype(F32).reshape(1, width)
    bias_ref[:, width : 2 * width] = jnp.zeros((1, width), F32)
    bias_ref[:, 2 * width :] = value_bias_ref[...].astype(F32).reshape(1, width)
    heads, levels = text_ref.shape
    spot = lax.broadcasted_iota(jnp.int32, (levels, LANES), 1)
    level = lax.broadcasted_iota(jnp.int32, (levels, LANES), 0)
    table = jnp.zeros((heads, LANES), F32)
    for source, begin in ((text_ref, 0), (horiz_ref, X_TABLE), (vert_ref, Y_TABLE)):
        table = table + dot_nn(source[...], (spot == level + begin).astype(BF))
    table_ref[...] = jnp.concatenate([table, jnp.zeros((16 - heads, LANES), F32)], axis=0)

    def project(there):
        step = 256

        def body(index, carry):
            columns = pl.ds(pl.multiple_of(index * step, step), step)
            product = dot_nn(item_ref[there], weight_ref[:, columns])
            projected_ref[there, columns] = (product + bias_ref[:, columns]).astype(BF)
            return carry

        lax.fori_loop(0, 3 * width // step, body, 0)

    def stored(index, there):
        return pltpu.make_async_copy(
            projected_ref.at[there], projected_out.at[there], store_sems.at[index]
        )

    for load in loads[-2:]:
        load.wait()
    project(own)
    stored(0, own).start()
    for piece in range(pieces):
        rows_out[piece].wait()
        there = pl.ds(pl.multiple_of((1 - mine) * count + piece * LANES, LANES), LANES)
        project(there)
        stored(1 + piece, there).start()
    meta_out.wait()
    meta = rows_ref[...].astype(F32)
    tall = jnp.concatenate([meta, jnp.zeros((LANES - 8, meta.shape[1]), F32)], axis=0)
    columns_ref[...] = jnp.transpose(tall).astype(jnp.int32)
    stored(0, own).wait()
    for piece in range(pieces):
        there = pl.ds(pl.multiple_of((1 - mine) * count + piece * LANES, LANES), LANES)
        stored(1 + piece, there).wait()


def projected_item(layer_in, fields, qkv_weight, query_bias, value_bias, tables):
    rows = 2 * layer_in.shape[1]
    width = layer_in.shape[2]
    pieces = rows // 2 // LANES
    small = list(fields) + [query_bias, value_bias] + [t.T for t in tables]
    return pl.pallas_call(
        project_kernel,
        in_specs=[HBM] * (2 + len(small)),
        out_specs=[VMEM, HBM, VMEM, VMEM, VMEM],
        out_shape=[
            jax.ShapeDtypeStruct((rows, width), BF),
            jax.ShapeDtypeStruct((rows, 3 * width), BF),
            jax.ShapeDtypeStruct((rows, LANES), jnp.int32),
            jax.ShapeDtypeStruct((8, rows), jnp.int32),
            jax.ShapeDtypeStruct((16, LANES), F32),
        ],
        scratch_shapes=[
            pltpu.VMEM((rows, 3 * width), BF),
            pltpu.VMEM((width, 3 * width), BF),
            pltpu.VMEM((8, rows // 2), jnp.int32),
            pltpu.VMEM((1, 3 * width), F32),
            pltpu.SemaphoreType.DMA((2, pieces + 1)),
            pltpu.SemaphoreType.DMA((len(small) + 2,)),
            pltpu.SemaphoreType.DMA((pieces + 1,)),
        ]
        + [pltpu.VMEM(array.shape, array.dtype) for array in small],
        compiler_params=pltpu.CompilerParams(
            collective_id=1, has_side_effects=True, vmem_limit_bytes=60 * MIB
        ),
        name="projected_item",
    )(layer_in, qkv_weight, *small)


EPSILON = 1e-05
TILE = 256


def vector(ref):
    return ref[...].astype(F32).reshape(1, ref.shape[0])


def gelu_and_slope(x):
    bell = jnp.exp(-0.5 * x * x)
    t = 1.0 / (1.0 + 0.23164188826 * jnp.abs(x))
    series = t * (
        0.127414796
        + t * (-0.142248368 + t * (0.7107068705 + t * (-0.7265760135 + t * 0.5307027145)))
    )
    tail = bell * series
    below = jnp.where(x >= 0.0, 1.0 - tail, tail)
    return x * below, below + x * (0.3989422804014327 * bell)


def row_mean(block):
    return jnp.mean(block, axis=1, keepdims=True)


def normalized(hidden):
    center = hidden - row_mean(hidden)
    scale = lax.rsqrt(row_mean(center * center) + EPSILON)
    return center * scale, scale


def norm_pulled(grad, unit, scale):
    return scale * (grad - row_mean(grad) - unit * row_mean(grad * unit))


def column_sum(block):
    return jnp.sum(block, axis=0, keepdims=True)


def feed_kernel(
    item_ref, mixed_ref, cotangent_ref, out_weight_ref, up_ref, down_ref, *refs,
):
    vectors_hbm, refs = refs[:7], refs[7:]
    (layer_ref, d_hidden_ref, d_mixed_ref, grad_out_ref, grad_down_ref, grad_up_ref, small_ref,
     cotangent_all, active, slope, unit, scale_ref, normed, normed_t, total, d_branch, d_branch_t,
     sems, load_sems) = refs[:19]
    vectors = refs[19:]
    (out_bias_ref, attn_gain_ref, attn_shift_ref, up_bias_ref, down_bias_ref, ffn_gain_ref,
     ffn_shift_ref) = vectors
    step = pl.program_id(0)
    blocks = pl.num_programs(0) // 2
    rows, width = item_ref.shape
    count = rows // 2
    mine = lax.axis_index("seq")
    partner = (1 - mine, lax.axis_index("dp"))
    own = pl.ds(pl.multiple_of(mine * count, LANES), count)
    tiles = rows // TILE

    def sent():
        return remote(
            cotangent_ref.at[1 - mine], cotangent_all.at[own], sems.at[0], sems.at[1], partner
        )

    def loads():
        copies = list(zip(vectors_hbm, vectors)) + [(cotangent_ref.at[mine], cotangent_all.at[own])]
        return [
            pltpu.make_async_copy(source, target, load_sems.at[index])
            for index, (source, target) in enumerate(copies)
        ]

    def over_columns(body, carry):
        def run(index, state):
            return body(pl.ds(pl.multiple_of(index * TILE, TILE), TILE), state)

        return lax.fori_loop(0, width // TILE, run, carry)

    def over_tiles(size, body, carry):
        def run(index, state):
            return body(pl.ds(pl.multiple_of(index * size, size), size), state)

        return lax.fori_loop(0, rows // size, run, carry)

    @pl.when(step == 0)
    def _():
        for load in loads():
            load.start()
        barrier = pltpu.get_barrier_semaphore()
        pl.semaphore_signal(barrier, inc=1, device_id=partner, device_id_type=MESH)
        pl.semaphore_wait(barrier, 1)
        sent().start()
        small_ref[...] = jnp.zeros_like(small_ref)
        for load in loads():
            load.wait()
        out_bias, gain, shift = vector(out_bias_ref), vector(attn_gain_ref), vector(attn_shift_ref)

        def tile(there, carry):
            attn = dot_nn(mixed_ref[there].astype(BF), out_weight_ref[...]) + out_bias
            standard, scale = normalized(item_ref[there].astype(F32) + attn)
            unit[there] = standard
            scale_ref[there] = jnp.broadcast_to(scale, (scale.shape[0], LANES))
            result = standard * gain + shift
            normed[there] = result.astype(BF)
            normed_t[:, there] = jnp.transpose(result).astype(BF)
            return carry

        over_tiles(TILE, tile, 0)
        total[...] = jnp.zeros_like(total)

    @pl.when(step < blocks)
    def _():
        def tile(here, carry):
            bias = up_bias_ref[pl.ds(pl.multiple_of(step * width + here.start, LANES), TILE)]
            bias = bias.astype(F32).reshape(1, TILE)
            value, grade = gelu_and_slope(dot_nn(normed[...], up_ref[:, here]) + bias)
            active[step, :, here] = value.astype(BF)
            slope[step, :, here] = grade
            return carry

        over_columns(tile, 0)

        def tile(here, carry):
            total[:, here] += dot_nn(active[step], down_ref[:, here])
            return carry

        over_columns(tile, 0)

    @pl.when(step == blocks)
    def _():
        sent().wait()
        gain, shift, bias = vector(ffn_gain_ref), vector(ffn_shift_ref), vector(down_bias_ref)
        first_gain, first_shift = vector(attn_gain_ref), vector(attn_shift_ref)

        def tile(there, sums):
            hidden = unit[there] * first_gain + first_shift + (total[there] + bias)
            standard, scale = normalized(hidden)
            layer_ref[there] = (standard * gain + shift).astype(BF)
            cotangent = cotangent_all[there].astype(F32)
            pulled = norm_pulled(cotangent * gain, standard, scale)
            total[there] = pulled
            low = pulled.astype(BF)
            d_branch[there] = low
            return (
                sums[0] + column_sum(low.astype(F32)),
                sums[1] + column_sum(cotangent * standard),
                sums[2] + column_sum(cotangent),
            )

        zero = jnp.zeros((1, width), F32)
        sums = over_tiles(64, tile, (zero, zero, zero))
        for row, value in zip((5, 6, 7), sums):
            small_ref[row : row + 1] = value

        def turn(there, carry):
            d_branch_t[:, there] = jnp.transpose(d_branch[there].astype(F32)).astype(BF)
            return carry

        over_tiles(TILE, turn, 0)

    @pl.when(step >= blocks)
    def _():
        block = step - blocks

        def tile(here, carry):
            grad_down_ref[:, here] = dot_nn(d_branch_t[...], active[block, :, here]).astype(BF)
            return carry

        over_columns(tile, 0)

        def tile(here, carry):
            d_up = (dot_nt(d_branch[...], down_ref[here]) * slope[block, :, here]).astype(BF)
            active[block, :, here] = d_up
            small_ref[pl.ds(8 + block, 1), here] = column_sum(d_up.astype(F32))
            return carry

        over_columns(tile, 0)

        def tile(here, carry):
            grad_up_ref[:, here] = dot_nn(normed_t[...], active[block, :, here]).astype(BF)
            total[:, here] += dot_nt(active[block], up_ref[here])
            return carry

        over_columns(tile, 0)

    @pl.when(step == 2 * blocks - 1)
    def _():
        gain = vector(attn_gain_ref)

        def tile(there, sums):
            d_normed = total[there]
            standard = unit[there]
            d_hidden = norm_pulled(d_normed * gain, standard, scale_ref[there, :1])
            d_hidden_ref[there] = d_hidden
            low = d_hidden.astype(BF)
            d_branch[there] = low
            return (
                sums[0] + column_sum(low.astype(F32)),
                sums[1] + column_sum(d_normed * standard),
                sums[2] + column_sum(d_normed),
            )

        zero = jnp.zeros((1, width), F32)
        sums = over_tiles(64, tile, (zero, zero, zero))
        for row, value in zip((2, 3, 4), sums):
            small_ref[row : row + 1] = value

        def turn(there, carry):
            normed_t[:, there] = jnp.transpose(mixed_ref[there]).astype(BF)
            return carry

        over_tiles(TILE, turn, 0)

        def tile(here, carry):
            d_mixed_ref[:, here] = dot_nt(d_branch[...], out_weight_ref[here]).astype(BF)
            grad_out_ref[:, here] = dot_nn(normed_t[...], d_branch[:, here]).astype(BF)
            return carry

        over_columns(tile, 0)


def fed_forward_and_back(
    item, mixed, cotangent, out_weight, up_weight, down_weight, vectors,
):
    rows, width = item.shape
    blocks = up_weight.shape[1] // width
    whole = pl.BlockSpec(memory_space=pltpu.VMEM)
    square = lambda kind: jax.ShapeDtypeStruct((rows, width), kind)
    later = lambda i: jnp.maximum(i - blocks, 0)
    return pl.pallas_call(
        feed_kernel,
        grid=(2 * blocks,),
        in_specs=[whole, whole, HBM, whole]
        + [
            pl.BlockSpec((width, width), lambda i: (0, lax.rem(i, blocks))),
            pl.BlockSpec((width, width), lambda i: (lax.rem(i, blocks), 0)),
        ]
        + [HBM] * 7,
        out_specs=[whole] * 4
        + [
            pl.BlockSpec((width, width), lambda i: (later(i), 0)),
            pl.BlockSpec((width, width), lambda i: (later(i), 0)),
            whole,
        ],
        out_shape=[
            square(BF), square(F32), square(BF), jax.ShapeDtypeStruct((width, width), BF),
            jax.ShapeDtypeStruct((blocks * width, width), BF),
            jax.ShapeDtypeStruct((blocks * width, width), BF),
            jax.ShapeDtypeStruct((16, width), F32),
        ],
        scratch_shapes=[
            pltpu.VMEM((rows, width), BF),
            pltpu.VMEM((blocks, rows, width), BF),
            pltpu.VMEM((blocks, rows, width), F32),
            pltpu.VMEM((rows, width), F32),
            pltpu.VMEM((rows, LANES), F32),
            pltpu.VMEM((rows, width), BF),
            pltpu.VMEM((width, rows), BF),
            pltpu.VMEM((rows, width), F32),
            pltpu.VMEM((rows, width), BF),
            pltpu.VMEM((width, rows), BF),
            pltpu.SemaphoreType.DMA((2,)),
            pltpu.SemaphoreType.DMA((8,)),
        ]
        + [pltpu.VMEM(vector.shape, vector.dtype) for vector in vectors],
        compiler_params=pltpu.CompilerParams(
            collective_id=2, has_side_effects=True, vmem_limit_bytes=60 * MIB
        ),
        name="feed_forward",
    )(item, mixed, cotangent, out_weight, up_weight, down_weight, *vectors)


SLOTS = 4


def finish_kernel(
    summed_ref, input_hbm, small_ref, diagonal_ref,
    down_ref, up_ref, out_ref, qkv_ref, input_ref, *refs,
):
    singles, (blocks_in, slots, input_in, input_slot, in_sems, out_sems, item_sems) = (
        refs[:12], refs[12:],
    )
    blocks, width = blocks_in.shape[0], blocks_in.shape[2]
    hidden = down_ref.shape[0] // width

    def load(block):
        return pltpu.make_async_copy(
            summed_ref.at[pl.ds(block * width, width)], blocks_in.at[block], in_sems.at[block]
        )

    def store(block):
        if block < hidden:
            target = down_ref.at[pl.ds(block * width, width)]
        elif block < 2 * hidden:
            target = up_ref.at[:, pl.ds((block - hidden) * width, width)]
        elif block == 2 * hidden:
            target = out_ref
        else:
            target = qkv_ref.at[:, pl.ds((block - 2 * hidden - 1) * width, width)]
        return pltpu.make_async_copy(
            slots.at[block % SLOTS], target, out_sems.at[block % SLOTS]
        )

    load_input = pltpu.make_async_copy(input_hbm, input_in, item_sems.at[0])
    store_input = pltpu.make_async_copy(input_slot, input_ref, item_sems.at[1])
    for block in range(blocks):
        load(block).start()
    load_input.start()
    for block in range(blocks):
        load(block).wait()
        if block >= SLOTS:
            store(block - SLOTS).wait()
        piece = blocks_in[block].astype(F32)
        slots[block % SLOTS] = jnp.transpose(piece) if block < hidden else piece
        store(block).start()
    load_input.wait()
    input_slot[...] = input_in[...].astype(F32)
    store_input.start()
    for row in range(8):
        singles[row][...] = small_ref[row]
    for row in range(hidden):
        singles[8][row * width : row * width + width] = small_ref[8 + row]
    heads, levels = singles[9].shape
    diagonals = diagonal_ref[...]
    level = lax.broadcasted_iota(jnp.int32, (LANES, LANES), 1)
    lane = lax.broadcasted_iota(jnp.int32, (LANES, LANES), 0)
    for table, (first, size, skip) in enumerate(((0, 4, 0), (4, 2, 1), (6, 2, 1))):
        total = jnp.zeros((heads, LANES), F32)
        for row in range(size):
            distance = lane + LANES * (row + skip - 2)
            chosen = (bucket(distance) == level).astype(F32)
            total = total + jnp.dot(
                diagonals[:, first + row, :], chosen, preferred_element_type=F32,
                precision=lax.Precision.HIGHEST,
            )
        singles[9 + table][...] = total[:, :levels]
    for block in range(blocks - SLOTS, blocks):
        store(block).wait()
    store_input.wait()


def finished(summed, grad_input, small, diagonals, hidden, levels):
    width = summed.shape[1]
    heads = diagonals.shape[0]
    blocks = summed.shape[0] // width
    single = jax.ShapeDtypeStruct((width,), F32)
    table = jax.ShapeDtypeStruct((heads, levels), F32)
    dma = pltpu.SemaphoreType.DMA
    return pl.pallas_call(
        finish_kernel,
        in_specs=[HBM, HBM, VMEM, VMEM],
        out_specs=[HBM] * 5 + [VMEM] * 12,
        out_shape=[
            jax.ShapeDtypeStruct((hidden, width), F32),
            jax.ShapeDtypeStruct((width, hidden), F32),
            jax.ShapeDtypeStruct((width, width), F32),
            jax.ShapeDtypeStruct((width, 3 * width), F32),
            jax.ShapeDtypeStruct(grad_input.shape, F32),
        ]
        + [single] * 8
        + [jax.ShapeDtypeStruct((hidden,), F32)]
        + [table] * 3,
        scratch_shapes=[
            pltpu.VMEM((blocks, width, width), BF),
            pltpu.VMEM((SLOTS, width, width), F32),
            pltpu.VMEM(grad_input.shape, BF),
            pltpu.VMEM(grad_input.shape, F32),
            dma((blocks,)),
            dma((SLOTS,)),
            dma((2,)),
        ],
        compiler_params=pltpu.CompilerParams(vmem_limit_bytes=56 * MIB),
        name="finished",
    )(summed, grad_input, small, diagonals)


PIECE = 16
HALVES = 2
SLACK = 2


def device_at(seq, core, y, z, depth, group):
    return (seq, (group * depth + z) * 4 + y * 2 + core)


class Summing:
    def __init__(self, depth, out_ref, scratch):
        (self.work, self.fresh, self.first_in, self.second_a, self.second_b, self.third_a,
         self.third_b, self.final, self.pair_sems, self.block_sems, self.line_sems,
         self.local_sems) = scratch
        self.depth, self.out_ref = depth, out_ref
        self.columns = self.work.shape[2]
        self.rows = 16 * PIECE * depth
        self.half, self.quarter, self.eighth = self.rows // 2, self.rows // 4, self.rows // 8
        self.part = self.rows // 16
        place = lax.axis_index("dp")
        self.x = x = lax.axis_index("seq")
        self.core = core = lax.rem(place, 2)
        self.y = y = lax.rem(lax.div(place, 2), 2)
        self.z = z = lax.rem(lax.div(place, 4), depth)
        group = lax.div(place, 4 * depth)
        at = lambda *spot: device_at(*spot, depth, group)
        self.over_core = at(x, 1 - core, y, z)
        self.over_x = at(1 - x, core, y, z)
        self.over_y = at(x, core, 1 - y, z)
        self.on_line = [at(x, core, y, lax.rem(z + s, depth)) for s in range(1, depth)]
        self.hop_devices = [self.over_core, self.over_x, self.over_y]
        reach = 1
        while reach < depth:
            up = lax.rem(lax.div(z, reach), 2)
            self.hop_devices.append(at(x, core, y, z + reach - 2 * reach * up))
            reach *= 2

    def greet(self):
        barrier = pltpu.get_barrier_semaphore()
        devices = [self.over_core, self.over_x, self.over_y] + self.on_line
        for device in devices:
            pl.semaphore_signal(barrier, inc=1, device_id=device, device_id_type=MESH)
        pl.semaphore_wait(barrier, len(devices))

    def block(self, source, target, level, side, chunk, device):
        sems = self.block_sems
        return remote(
            source, target, sems.at[0, level, side, chunk], sems.at[1, level, side, chunk], device
        )

    def spread(self, level, chunk, source, target):
        sems = self.line_sems
        return [
            remote(
                source(step), target(step), sems.at[0, level, step - 1, chunk],
                sems.at[1, level, step - 1, chunk], self.on_line[step - 1],
            )
            for step in range(1, self.depth)
        ]

    def after(self, step):
        return lax.rem(self.z + step, self.depth)

    def before(self, step):
        return lax.rem(self.z + self.depth - step, self.depth)

    def held(self, chunk, begin, size):
        return self.work.at[chunk, pl.ds(begin, size)]

    def out(self, chunk, begin, size, core=None):
        core = self.core if core is None else core
        start = lax.div(chunk, HALVES) * self.rows + core * self.half + begin
        return self.out_ref.at[
            pl.ds(pl.multiple_of(start, PIECE), size), pl.ds(self.column(chunk), self.columns)
        ]

    def column(self, chunk):
        return pl.multiple_of(lax.rem(chunk, HALVES) * self.columns, LANES)

    def own_a(self):
        return self.x * self.eighth + self.y * self.part

    def own_b(self):
        return self.quarter + self.y * self.eighth

    def first(self, chunk):
        return [
            self.block(
                self.held(chunk, (1 - self.x) * self.eighth, self.eighth),
                self.first_in.at[chunk, 0], 0, 0, chunk, self.over_x,
            ),
            self.block(
                self.held(chunk, self.quarter + (1 - self.y) * self.eighth, self.eighth),
                self.first_in.at[chunk, 1], 0, 1, chunk, self.over_y,
            ),
        ]

    def second(self, chunk):
        return [
            self.block(
                self.held(chunk, self.x * self.eighth + (1 - self.y) * self.part, self.part),
                self.second_a.at[chunk], 1, 0, chunk, self.over_y,
            )
        ] + self.spread(
            0, chunk,
            lambda s: self.held(chunk, self.own_b() + self.after(s) * 2 * PIECE, 2 * PIECE),
            lambda s: self.second_b.at[chunk, s - 1],
        )

    def third(self, chunk):
        start = self.own_b() + self.z * 2 * PIECE + (1 - self.x) * PIECE
        return [
            self.block(
                self.held(chunk, start, PIECE), self.third_b.at[chunk], 1, 1, chunk, self.over_x
            )
        ] + self.spread(
            1, chunk,
            lambda s: self.held(chunk, self.own_a() + self.after(s) * PIECE, PIECE),
            lambda s: self.third_a.at[chunk, s - 1],
        )

    def last_spots(self):
        return (
            self.own_a() + self.z * PIECE,
            self.own_b() + self.z * 2 * PIECE + self.x * PIECE,
        )

    def kept(self, chunk):
        return [
            pltpu.make_async_copy(
                self.final.at[chunk, side], self.out(chunk, begin, PIECE),
                self.local_sems.at[1 + side, chunk],
            )
            for side, begin in enumerate(self.last_spots())
        ]

    def third_back(self, chunk, arriving):
        x = 1 - self.x if arriving else self.x
        owner = self.before if arriving else (lambda s: self.z)
        return [
            self.block(
                self.final.at[chunk, 1],
                self.out(chunk, self.own_b() + self.z * 2 * PIECE + x * PIECE, PIECE),
                2, 1, chunk, self.over_x,
            )
        ] + self.spread(
            2, chunk,
            lambda s: self.final.at[chunk, 0],
            lambda s: self.out(chunk, self.own_a() + owner(s) * PIECE, PIECE),
        )

    def second_back(self, chunk, arriving):
        y = 1 - self.y if arriving else self.y
        owner = self.before if arriving else (lambda s: self.z)
        mine = self.out(chunk, self.own_b() + self.z * 2 * PIECE, 2 * PIECE)
        return [
            self.block(
                self.out(chunk, self.own_a(), self.part),
                self.out(chunk, self.x * self.eighth + y * self.part, self.part),
                2, 0, chunk, self.over_y,
            )
        ] + self.spread(
            3, chunk,
            lambda s: mine,
            lambda s: self.out(chunk, self.own_b() + owner(s) * 2 * PIECE, 2 * PIECE),
        )

    def first_back(self, chunk, arriving):
        x = 1 - self.x if arriving else self.x
        y = 1 - self.y if arriving else self.y
        return [
            self.block(
                self.out(chunk, self.x * self.eighth, self.eighth),
                self.out(chunk, x * self.eighth, self.eighth), 3, 0, chunk, self.over_x,
            ),
            self.block(
                self.out(chunk, self.own_b(), self.eighth),
                self.out(chunk, self.quarter + y * self.eighth, self.eighth),
                3, 1, chunk, self.over_y,
            ),
        ]

    def pair_back(self, chunk, arriving):
        core = 1 - self.core if arriving else self.core
        return [
            remote(
                self.out(chunk, 0, self.half), self.out(chunk, 0, self.half, core),
                self.pair_sems.at[0, 1, chunk], self.pair_sems.at[1, 1, chunk], self.over_core,
            )
        ]

    def pair_copies(self, chunk, source, begin):
        columns = pl.ds(self.column(chunk), self.columns)
        at = lambda core: source.at[
            pl.ds(pl.multiple_of(begin + core * self.half, PIECE), self.half), columns
        ]
        return [
            remote(
                at(1 - self.core), self.fresh.at[chunk], self.pair_sems.at[0, 0, chunk],
                self.pair_sems.at[1, 0, chunk], self.over_core,
            ),
            pltpu.make_async_copy(at(self.core), self.work.at[chunk], self.local_sems.at[0, chunk]),
        ]

    def add(self, chunk, begin, sources, size):
        step = min(size, 64)

        def body(index, carry):
            offset = pl.multiple_of(index * step, PIECE)
            there = pl.ds(pl.multiple_of(begin + offset, PIECE), step)
            total = self.work[chunk, there].astype(F32)
            for source in sources:
                total = total + source[pl.ds(offset, step)].astype(F32)
            self.work[chunk, there] = total.astype(BF)
            return carry

        lax.fori_loop(0, size // step, body, 0)

    def stage(self, number, chunk, start_pair, wait_pair):
        def wait(copies):
            for copy in copies:
                copy.wait()

        def start(copies):
            for copy in copies:
                copy.start()

        x, y = self.x, self.y
        if number == 0:
            start_pair(chunk)
        elif number == 1:
            wait_pair(chunk)
            self.add(chunk, 0, [self.fresh.at[chunk]], self.half)
            start(self.first(chunk))
        elif number == 2:
            wait(self.first(chunk))
            self.add(chunk, x * self.eighth, [self.first_in.at[chunk, 0]], self.eighth)
            self.add(chunk, self.own_b(), [self.first_in.at[chunk, 1]], self.eighth)
            start(self.second(chunk))
        elif number == 3:
            wait(self.second(chunk))
            self.add(chunk, self.own_a(), [self.second_a.at[chunk]], self.part)
            self.add(
                chunk, self.own_b() + self.z * 2 * PIECE,
                [self.second_b.at[chunk, s] for s in range(self.depth - 1)], 2 * PIECE,
            )
            start(self.third(chunk))
        elif number == 4:
            wait(self.third(chunk))
            spot_a, spot_b = self.last_spots()
            self.add(
                chunk, spot_a, [self.third_a.at[chunk, s] for s in range(self.depth - 1)], PIECE
            )
            self.add(chunk, spot_b, [self.third_b.at[chunk]], PIECE)
            for side, spot in enumerate((spot_a, spot_b)):
                self.final[chunk, side] = self.work[chunk, pl.ds(pl.multiple_of(spot, PIECE), PIECE)]
            start(self.third_back(chunk, False) + self.kept(chunk))
        elif number == 5:
            wait(self.third_back(chunk, True) + self.kept(chunk))
            start(self.second_back(chunk, False))
        elif number == 6:
            wait(self.second_back(chunk, True))
            start(self.first_back(chunk, False))
        elif number == 7:
            wait(self.first_back(chunk, True))
            start(self.pair_back(chunk, False))
        else:
            wait(self.pair_back(chunk, True))

    def tick(self, index, chunks, start_pair, wait_pair):
        for number in range(8, -1, -1):
            chunk = index - SLACK * number

            @pl.when((chunk >= 0) & (chunk < chunks))
            def _(number=number, chunk=chunk):
                self.stage(number, chunk, start_pair, wait_pair)


def summing_scratch(depth, chunks, columns):
    rows = 16 * PIECE * depth
    others = max(depth - 1, 1)
    dma = pltpu.SemaphoreType.DMA
    return [
        pltpu.VMEM((chunks, rows // 2, columns), BF),
        pltpu.VMEM((chunks, rows // 2, columns), BF),
        pltpu.VMEM((chunks, 2, rows // 8, columns), BF),
        pltpu.VMEM((chunks, rows // 16, columns), BF),
        pltpu.VMEM((chunks, others, 2 * PIECE, columns), BF),
        pltpu.VMEM((chunks, others, PIECE, columns), BF),
        pltpu.VMEM((chunks, PIECE, columns), BF),
        pltpu.VMEM((chunks, 2, PIECE, columns), BF),
        dma((2, 2, chunks)),
        dma((2, 4, 2, chunks)),
        dma((2, 4, others, chunks)),
        dma((3, chunks)),
    ]


def last_kernel(
    depth, chunks, steps, *refs,
):
    (meta_ref, rows_ref, table_ref, q_ref, k_ref, v_ref, mixed_ref, grad_ref, log_ref,
     small_ref, item_hbm, weight_hbm, d_hidden_hbm, grad_down_ref, grad_up_ref, grad_out_ref,
     layer_ref,
     out_ref, small_out, diagonal_out, layer_out, input_out,
     *scratch) = refs
    static, scratch = scratch[:11], scratch[11:]
    (item_ref, weight_ref, d_hidden_ref, load_sems,
     d_query, d_key, d_value, item_t, tail, input_grad, small_in, diagonal_in, small_sems,
     item_sems, *scratch) = scratch
    summing = Summing(depth, out_ref, scratch)
    step = pl.program_id(0)
    pairs = d_query.shape[0]
    rows, width = item_hbm.shape
    count = rows // 2
    hidden = grad_down_ref.shape[0]
    per_source = hidden // summing.rows * HALVES
    hops = len(summing.hop_devices)
    x = summing.x
    first_hop = 2 * pairs + 2

    def out_copy():
        return pltpu.make_async_copy(
            grad_out_ref, tail.at[pl.ds(0, width)], item_sems.at[0, 2]
        )

    def loads():
        pairs_of = ((item_hbm, item_ref), (weight_hbm, weight_ref), (d_hidden_hbm, d_hidden_ref))
        return [
            pltpu.make_async_copy(source, target, load_sems.at[index])
            for index, (source, target) in enumerate(pairs_of)
        ]

    def item_copies(index, source, target):
        return [
            pltpu.make_async_copy(
                source.at[pl.ds(x * count, count)], target.at[x], item_sems.at[0, index]
            ),
            remote(
                source.at[pl.ds((1 - x) * count, count)], target.at[x], item_sems.at[1, index],
                item_sems.at[2, index], summing.over_x,
            ),
        ]

    def layer_copies():
        return item_copies(0, layer_ref, layer_out)

    def input_copies():
        return item_copies(1, input_grad, input_out)

    def small_copies(hop):
        device = summing.hop_devices[hop]
        return [
            remote(source, landing.at[hop], small_sems.at[0, kind, hop],
                   small_sems.at[1, kind, hop], device)
            for kind, (source, landing) in enumerate(
                ((small_out, small_in), (diagonal_out, diagonal_in))
            )
        ]

    @pl.when(step == 0)
    def _():
        summing.greet()
        out_copy().start()
        for copy in layer_copies():
            copy.start()
        small_out[...] = small_ref[...]
        for copy in loads():
            copy.start()
        static_prepare(meta_ref, static)

    sources = (grad_down_ref, grad_up_ref, tail)

    def start_pair(chunk):
        for index, source in enumerate(sources):
            @pl.when(lax.div(chunk, per_source) == index)
            def _(index=index, source=source):
                begin = lax.div(chunk - index * per_source, HALVES) * summing.rows
                for copy in summing.pair_copies(chunk, source, begin):
                    copy.start()

    def wait_pair(chunk):
        for copy in summing.pair_copies(chunk, tail, 0):
            copy.wait()

    def tick(index):
        summing.tick(index, chunks, start_pair, wait_pair)
        for hop in range(hops + 1):
            @pl.when(index == first_hop + SLACK * hop)
            def _(hop=hop):
                if hop > 0:
                    for copy in small_copies(hop - 1):
                        copy.wait()
                    small_out[...] = small_out[...] + small_in[hop - 1]
                    diagonal_out[...] = diagonal_out[...] + diagonal_in[hop - 1]
                if hop < hops:
                    for copy in small_copies(hop):
                        copy.start()

    def slab(part, source):
        def body(tile, carry):
            there = pl.ds(pl.multiple_of(tile * TILE, TILE), TILE)
            target = pl.ds(pl.multiple_of((1 + part) * width + tile * TILE, TILE), TILE)
            for pair in range(pairs):
                columns = slice(pair * LANES, pair * LANES + LANES)
                tail[target, columns] = dot_nn(item_t[there], source[pair]).astype(BF)
            return carry

        lax.fori_loop(0, width // TILE, body, 0)

    for parity in range(2):
        tick(2 * step + parity)

        @pl.when(step < pairs)
        def _(parity=parity):
            head_back(
                parity, step, meta_ref, rows_ref, table_ref, q_ref, k_ref, v_ref, mixed_ref,
                grad_ref, log_ref, static, d_query, d_key, d_value, diagonal_out,
            )

        if parity == 0:
            @pl.when(step == pairs)
            def _():
                slab(1, d_key)

        if parity == 1:
            @pl.when(step == pairs - 1)
            def _():
                out_copy().wait()
                for copy in loads():
                    copy.wait()
                for tile in range(rows // TILE):
                    there = slice(tile * TILE, tile * TILE + TILE)
                    item_t[:, there] = jnp.transpose(item_ref[there].astype(F32)).astype(BF)
                slab(0, d_query)

            @pl.when(step == pairs)
            def _():
                slab(2, d_value)

                def body(tile, carry):
                    there = pl.ds(pl.multiple_of(tile * TILE, TILE), TILE)
                    total = d_hidden_ref[there]
                    for pair in range(pairs):
                        for part, piece in enumerate((d_query, d_key, d_value)):
                            begin = part * width + pair * LANES
                            value = piece[pair, there]
                            total = total + dot_nt(value, weight_ref[:, begin : begin + LANES])
                    input_grad[there] = total.astype(BF)
                    return carry

                lax.fori_loop(0, rows // TILE, body, 0)
                for pair in range(pairs):
                    columns = slice(pair * LANES, pair * LANES + LANES)
                    small_out[0:1, columns] = column_sum(d_query[pair].astype(F32))
                    small_out[1:2, columns] = column_sum(d_value[pair].astype(F32))
                for copy in input_copies():
                    copy.start()

    @pl.when(step == steps - 1)
    def _():
        for copy in layer_copies() + input_copies():
            copy.wait()


def summed_with_attention_back(
    meta_columns, meta_rows, table_rows, projected, mixed, d_mixed, logs, item, qkv_weight,
    d_hidden, small, grad_down, grad_up, grad_out, layer,
):
    size = lax.axis_size("dp")
    depth = 4 if size % 16 == 0 else size // 4
    rows, width = item.shape
    pairs = width // LANES
    hidden = grad_down.shape[0]
    chunks = 3 * hidden // (16 * PIECE * depth) * HALVES
    hops = 3 + (depth - 1).bit_length()
    ticks = max(chunks + 8 * SLACK + 1, 2 * pairs + 3 + hops * SLACK)
    steps = (ticks + 1) // 2
    held = lambda p: jnp.minimum(p, pairs - 1)

    def block(part):
        return pl.BlockSpec((rows, LANES), lambda p: (0, part * pairs + held(p)))

    whole = pl.BlockSpec(memory_space=pltpu.VMEM)
    anywhere = pl.BlockSpec(memory_space=pltpu.HBM)
    halves = jax.ShapeDtypeStruct((2, rows // 2, width), BF)
    diagonals = jax.ShapeDtypeStruct((2 * pairs, 8, LANES), F32)
    dma = pltpu.SemaphoreType.DMA
    summed, small, diagonals, layer_out, grad_input = pl.pallas_call(
        functools.partial(last_kernel, depth, chunks, steps),
        grid=(steps,),
        in_specs=[whole] * 3
        + [block(0), block(1), block(2), block(0), block(0)]
        + [pl.BlockSpec((1, rows, LANES), lambda p: (held(p), 0, 0))]
        + [whole]
        + [anywhere] * 7,
        out_specs=[anywhere, whole, whole, anywhere, anywhere],
        out_shape=[
            jax.ShapeDtypeStruct((3 * hidden, width), BF),
            jax.ShapeDtypeStruct(small.shape, F32),
            diagonals, halves, halves,
        ],
        scratch_shapes=static_scratch(rows)
        + [pltpu.VMEM((LANES, rows), BF)] * 3
        + [
            pltpu.VMEM((rows, width), BF),
            pltpu.VMEM((width, 3 * width), BF),
            pltpu.VMEM((rows, width), F32),
            dma((3,)),
        ]
        + [pltpu.VMEM((pairs, rows, LANES), BF)] * 3
        + [
            pltpu.VMEM((width, rows), BF),
            pltpu.VMEM((hidden, width), BF),
            pltpu.VMEM((rows, width), BF),
            pltpu.VMEM((hops,) + small.shape, F32),
            pltpu.VMEM((hops,) + diagonals.shape, F32),
            dma((2, 2, hops)),
            dma((3, 3)),
        ]
        + summing_scratch(depth, chunks, width // HALVES),
        compiler_params=pltpu.CompilerParams(
            collective_id=0, has_side_effects=True, vmem_limit_bytes=62 * MIB
        ),
        name="summed_with_attention_back",
    )(meta_columns, meta_rows, table_rows, projected, projected, projected, mixed, d_mixed, logs,
      small, item, qkv_weight, d_hidden, grad_down, grad_up, grad_out, layer)
    span = 4 * depth
    if size > span:
        groups = [list(range(first, size, span)) for first in range(span)]
        summed, small, diagonals = lax.psum(
            (summed.astype(F32), small, diagonals), "dp", axis_index_groups=groups
        )
        summed = summed.astype(BF)
    return summed, small, diagonals, layer_out, grad_input


def per_device(
    layer_in, segment, key_mask, position, layout_x, layout_y,
    qkv_weight, query_bias, value_bias, out_weight, out_bias, attn_gain, attn_shift,
    up_weight, up_bias, down_weight, down_bias, ffn_gain, ffn_shift,
    text_table, horiz_table, vert_table, cotangent,
):
    width = layer_in.shape[-1]
    item, projected, meta_columns, meta_rows, table_rows = projected_item(
        layer_in, (segment, key_mask, position, layout_x, layout_y),
        qkv_weight, query_bias, value_bias, (text_table, horiz_table, vert_table),
    )
    mixed, logs = attention_forward(meta_columns, meta_rows, table_rows, projected, width)
    layer, d_hidden, d_mixed, grad_out, grad_down, grad_up, small = fed_forward_and_back(
        item, mixed, cotangent, out_weight, up_weight, down_weight,
        (out_bias, attn_gain, attn_shift, up_bias, down_bias, ffn_gain, ffn_shift),
    )
    summed, small, diagonals, layer_out, grad_input = summed_with_attention_back(
        meta_columns, meta_rows, table_rows, projected, mixed, d_mixed, logs, item, qkv_weight,
        d_hidden, small, grad_down, grad_up, grad_out, layer,
    )
    done = finished(
        summed, grad_input, small, diagonals, up_weight.shape[1], text_table.shape[0]
    )
    sum_down, sum_up, sum_out, sum_qkv, grad_input = done[:5]
    singles, tables = done[5:14], [t.T for t in done[14:]]
    return (
        layer_out, grad_input, sum_qkv, singles[0], singles[1], sum_out, singles[2], singles[3],
        singles[4], sum_up, singles[8], sum_down, singles[5], singles[6], singles[7],
        tables[0], tables[1], tables[2],
    )


def solution(mesh):
    rows = P("dp", "seq", None)
    marks_spec = P("dp", "seq")
    return jax.shard_map(
        per_device,
        mesh=mesh,
        in_specs=(rows,) + (marks_spec,) * 5 + (P(),) * 16 + (rows,),
        out_specs=(rows, rows) + (P(),) * 16,
        check_vma=False,
    )
```

```python
import functools

import jax
import jax.numpy as jnp
from jax import lax
from jax.experimental import pallas as pl
from jax.experimental.pallas import tpu as pltpu
from jax.sharding import PartitionSpec as P

BF = jnp.bfloat16
F32 = jnp.float32
BIG = 1e30
LANES = 128
HEAD = 64
TEXT = 512
POS = 64
COORD = 48
Y0 = 64
GROUP0 = 112
MEMBER0 = 116
FLAG = 124
LOG0 = 125
X_TABLE = 33
Y_TABLE = 66
NOTHING = 127


def dot_nt(a, b):
    return lax.dot_general(a, b, (((1,), (1,)), ((), ())), preferred_element_type=F32)


def dot_nn(a, b):
    return lax.dot_general(a, b, (((1,), (0,)), ((), ())), preferred_element_type=F32)


def looked_up(table_row, index):
    rows = index.shape[0]
    return jnp.take_along_axis(jnp.broadcast_to(table_row, (rows, LANES)), index, axis=1)


def bucket(distance):
    return jnp.clip(distance, -16, 16) + 16


def between(lane, low, high):
    return (lane >= low) & (lane < high)


def columns_of(meta_ref):
    return tuple(meta_ref[:, field : field + 1] for field in range(5))


def marks(meta_ref):
    segment, key_mask, position, across, down = columns_of(meta_ref)
    rows = segment.shape[0]
    lane = lax.broadcasted_iota(jnp.int32, (rows, LANES), 1)
    row = lax.broadcasted_iota(jnp.int32, (rows, LANES), 0)
    even = between(lane, HEAD, HEAD + COORD) & (lane - HEAD == across)
    odd = (lane < COORD) & (lane == across)
    group = (segment - 1) >> 3
    member = (segment - 1) & 7
    named = segment > 0
    shared = (
        ((row < TEXT) & (lane < POS) & (lane == position))
        | (between(lane, Y0, Y0 + COORD) & (lane - Y0 == down))
        | (named & between(lane, GROUP0, MEMBER0) & (lane - GROUP0 == group))
        | (named & between(lane, MEMBER0, FLAG) & (lane - MEMBER0 == member))
        | ((lane == FLAG) & (key_mask <= 0))
        | (lane >= LOG0)
    )
    return tuple(jnp.where(m, 1.0, 0.0).astype(BF) for m in (even, odd, shared))


def barred(meta_ref):
    segment = meta_ref[:, 0:1]
    rows = segment.shape[0]
    lane = lax.broadcasted_iota(jnp.int32, (rows, LANES), 1)
    group = (segment - 1) >> 3
    member = (segment - 1) & 7
    shut = (
        ((segment > 0) & between(lane, GROUP0, MEMBER0) & (lane - GROUP0 != group))
        | ((segment < 0) & between(lane, GROUP0, MEMBER0))
        | ((segment > 0) & between(lane, MEMBER0, FLAG) & (lane - MEMBER0 != member))
        | (lane == FLAG)
    )
    return jnp.where(shut, -BIG, 0.0).astype(F32)


def query_index(meta_ref):
    segment, key_mask, position, across, down = columns_of(meta_ref)
    rows = segment.shape[0]
    lane = lax.broadcasted_iota(jnp.int32, (rows, LANES), 1)
    x_even = bucket(across - (lane - HEAD)) + X_TABLE
    x_odd = bucket(across - lane) + X_TABLE
    even = jnp.where(between(lane, HEAD, HEAD + COORD), x_even, NOTHING)
    odd = jnp.where(lane < COORD, x_odd, NOTHING)
    shared = jnp.where(
        lane < POS,
        bucket(position - lane),
        jnp.where(between(lane, Y0, Y0 + COORD), bucket(down - (lane - Y0)) + Y_TABLE, NOTHING),
    )
    return even, odd, shared


def image_key_index(meta_ref):
    position = meta_ref[TEXT:, 2:3]
    lane = lax.broadcasted_iota(jnp.int32, (position.shape[0], LANES), 1)
    return jnp.where(lane < POS, bucket(lane - position), NOTHING)


def prepare(meta_ref, mark_refs, bar_ref, index_refs, key_index_ref):
    for ref, value in zip(mark_refs, marks(meta_ref)):
        ref[...] = value
    bar_ref[...] = barred(meta_ref)
    for ref, value in zip(index_refs, query_index(meta_ref)):
        ref[...] = value
    key_index_ref[...] = image_key_index(meta_ref)


def image_offsets(row_positions, column_positions):
    return bucket(column_positions - row_positions)


def widened(parity, q, k, table_row, mark_refs, bar_ref, index_refs, key_index_ref, logs):
    rows = q.shape[0]
    lane = lax.broadcasted_iota(jnp.int32, (rows, LANES), 1)
    own = (lane < HEAD) if parity == 0 else (lane >= HEAD)
    first = jnp.where(own, q.astype(F32) * 0.125, looked_up(table_row, index_refs[parity][...]))
    second = looked_up(table_row, index_refs[2][...]) + bar_ref[...]
    if logs is not None:
        high = logs.astype(BF).astype(F32)
        middle = (logs - high).astype(BF).astype(F32)
        lowest = logs - high - middle
        second = jnp.where(
            lane == LOG0,
            -high,
            jnp.where(lane == LOG0 + 1, -middle, jnp.where(lane == LOG0 + 2, -lowest, second)),
        )
    first = first.astype(BF)
    second = second.astype(BF)
    mark_second = mark_refs[2][...]
    to_image = jnp.where(lane < POS, mark_second, second)
    key_first = jnp.where(own, k, mark_refs[parity][...])
    image_lane = lane[TEXT:]
    key_image = jnp.where(
        image_lane < POS,
        looked_up(table_row, key_index_ref[...]).astype(BF),
        mark_second[TEXT:],
    )
    q_text = jnp.concatenate([first, second], axis=1)
    q_image = jnp.concatenate([first, to_image], axis=1)
    k_text = jnp.concatenate([key_first[:TEXT], mark_second[:TEXT]], axis=1)
    k_image = jnp.concatenate([key_first[TEXT:], key_image], axis=1)
    return q_text, q_image, k_text, k_image


def image_bias(table_row, offsets):
    return jnp.concatenate(
        [looked_up(table_row, offsets[:, :LANES]), looked_up(table_row, offsets[:, LANES:])], axis=1
    )


def forward_kernel(
    meta_ref, rows_ref, table_ref, q_ref, k_ref, v_ref, mixed_ref, log_ref,
    even_ref, odd_ref, shared_ref, bar_ref, index_even, index_odd, index_shared, key_index_ref,
):
    mark_refs = (even_ref, odd_ref, shared_ref)
    index_refs = (index_even, index_odd, index_shared)

    @pl.when(pl.program_id(0) == 0)
    def _():
        prepare(meta_ref, mark_refs, bar_ref, index_refs, key_index_ref)

    rows = q_ref.shape[0]
    images = rows - TEXT
    q, k, v = q_ref[...], k_ref[...], v_ref[...]
    offsets = bucket(meta_ref[TEXT:, 2:3] - rows_ref[2:3, TEXT:])
    tile = 256
    parts = []
    for parity in range(2):
        table_row = table_ref[pl.ds(2 * pl.program_id(0) + parity, 1), :]
        q_text, q_image, k_text, k_image = widened(
            parity, q, k, table_row, mark_refs, bar_ref, index_refs, key_index_ref, None
        )
        bias = image_bias(table_row, offsets)
        outs = []
        logs = []
        for start in range(0, rows, tile):
            here = slice(start, start + tile)
            on_text = dot_nt(q_text[here], k_text)
            on_image = dot_nt(q_image[here], k_image)
            if start >= TEXT:
                on_image = on_image + bias[start - TEXT : start - TEXT + tile]
            top = jnp.maximum(
                jnp.max(on_text, axis=1, keepdims=True), jnp.max(on_image, axis=1, keepdims=True)
            )
            on_text = jnp.exp(on_text - top)
            on_image = jnp.exp(on_image - top)
            total = jnp.sum(on_text, axis=1, keepdims=True) + jnp.sum(
                on_image, axis=1, keepdims=True
            )
            out = dot_nn(on_text.astype(BF), v[:TEXT]) + dot_nn(on_image.astype(BF), v[TEXT:])
            outs.append(out / total)
            logs.append(jnp.broadcast_to(top + jnp.log(total), (tile, LANES)))
        parts.append((jnp.concatenate(outs, axis=0), jnp.concatenate(logs, axis=0)))
    lane = lax.broadcasted_iota(jnp.int32, (rows, LANES), 1)
    mixed_ref[...] = jnp.where(lane < HEAD, parts[0][0], parts[1][0])
    log_ref[0] = jnp.where(lane < HEAD, parts[0][1], parts[1][1])


def static_scratch(rows):
    return [
        pltpu.VMEM((rows, LANES), BF),
        pltpu.VMEM((rows, LANES), BF),
        pltpu.VMEM((rows, LANES), BF),
        pltpu.VMEM((rows, LANES), F32),
        pltpu.VMEM((rows, LANES), jnp.int32),
        pltpu.VMEM((rows, LANES), jnp.int32),
        pltpu.VMEM((rows, LANES), jnp.int32),
        pltpu.VMEM((rows - TEXT, LANES), jnp.int32),
    ]


def attention_forward(meta_columns, meta_rows, table_rows, projected, width):
    rows = projected.shape[0]
    pairs = width // LANES

    def block(part):
        return pl.BlockSpec((rows, LANES), lambda p: (0, part * pairs + p))

    whole = lambda shape: pl.BlockSpec(shape, lambda p: (0,) * len(shape))
    return pl.pallas_call(
        forward_kernel,
        grid=(pairs,),
        in_specs=[
            whole(meta_columns.shape),
            whole(meta_rows.shape),
            whole(table_rows.shape),
            block(0), block(1), block(2),
        ],
        out_specs=[
            pl.BlockSpec((rows, LANES), lambda p: (0, p)),
            pl.BlockSpec((1, rows, LANES), lambda p: (p, 0, 0)),
        ],
        out_shape=[
            jax.ShapeDtypeStruct((rows, width), F32),
            jax.ShapeDtypeStruct((pairs, rows, LANES), F32),
        ],
        scratch_shapes=static_scratch(rows),
        compiler_params=pltpu.CompilerParams(vmem_limit_bytes=48 * 1024 * 1024),
        name="attention_forward",
    )(meta_columns, meta_rows, table_rows, projected, projected, projected)


def skewed(block):
    size = block.shape[0]
    lane = lax.broadcasted_iota(jnp.int32, (size, LANES), 1)
    row = lax.broadcasted_iota(jnp.int32, (size, LANES), 0)
    turned = jnp.take_along_axis(block, (lane + row) & (LANES - 1), axis=1)
    straight = lane + row < LANES
    above = jnp.sum(jnp.where(straight, turned, 0.0), axis=0, keepdims=True)
    below = jnp.sum(jnp.where(straight, 0.0, turned), axis=0, keepdims=True)
    return above, below


def transposed(array):
    return jnp.transpose(array.astype(F32)).astype(array.dtype)


def static_prepare(meta_ref, static):
    (even_ref, odd_ref, shared_ref, bar_ref, index_even, index_odd, index_shared, key_index_ref,
     even_t, odd_t, shared_t) = static
    mark_refs = (even_ref, odd_ref, shared_ref)
    prepare(meta_ref, mark_refs, bar_ref, (index_even, index_odd, index_shared), key_index_ref)
    for ref, turned in zip(mark_refs, (even_t, odd_t, shared_t)):
        turned[...] = transposed(ref[...])


def head_back(
    parity, pair, meta_ref, rows_ref, table_ref, q_ref, k_ref, v_ref, mixed_ref, grad_ref, log_ref,
    static, d_query, d_key, d_value, diag_ref,
):
    (even_ref, odd_ref, shared_ref, bar_ref, index_even, index_odd, index_shared, key_index_ref,
     even_t, odd_t, shared_t) = static
    mark_refs = (even_ref, odd_ref, shared_ref)
    index_refs = (index_even, index_odd, index_shared)
    turned_refs = (even_t, odd_t, shared_t)
    rows = q_ref.shape[0]
    images = rows - TEXT
    tile = 256
    q, k, v, grad = q_ref[...], k_ref[...], v_ref[...], grad_ref[...]
    lane = lax.broadcasted_iota(jnp.int32, (rows, LANES), 1)
    products = grad.astype(F32) * mixed_ref[...].astype(F32)
    k_turned = transposed(k)
    offsets = bucket(rows_ref[2:3, TEXT:] - meta_ref[TEXT:, 2:3])
    is_image = rows_ref[1:2, TEXT:] > 0
    own = (lane < HEAD) if parity == 0 else (lane >= HEAD)
    spare = HEAD if parity == 0 else 0
    table_row = table_ref[pl.ds(2 * pair + parity, 1), :]
    logs = log_ref[0, :, parity * HEAD : parity * HEAD + 1]
    q_text, q_image, k_text, k_image = widened(
        parity, q, k, table_row, mark_refs, bar_ref, index_refs, key_index_ref, logs
    )
    bias = image_bias(table_row, offsets)
    delta = jnp.sum(jnp.where(own, products, 0.0), axis=1, keepdims=True)
    high = delta.astype(BF).astype(F32)
    middle = (delta - high).astype(BF).astype(F32)
    lowest = delta - high - middle
    grad_wide = jnp.where(
        own,
        grad.astype(F32),
        jnp.where(
            lane == spare,
            -high,
            jnp.where(lane == spare + 1, -middle, jnp.where(lane == spare + 2, -lowest, 0.0)),
        ),
    ).astype(BF)
    v_wide = jnp.where(
        own, v.astype(F32), jnp.where(between(lane, spare, spare + 3), 1.0, 0.0)
    ).astype(BF)
    q_marked = jnp.concatenate(
        [
            jnp.where(own, q.astype(F32) * 0.125, mark_refs[parity][...].astype(F32)).astype(BF),
            shared_ref[...],
        ],
        axis=1,
    )
    dq = jnp.zeros((HEAD, rows), F32)
    dks = []
    dvs = []
    first_sum = jnp.zeros((LANES, LANES), F32)
    second_sum = jnp.zeros((LANES, LANES), F32)
    text_image = jnp.zeros((LANES, images), F32)
    for start in range(0, rows, tile):
        here = slice(start, start + tile)
        if start < TEXT:
            scores = dot_nt(k_text[here], q_text)
        else:
            scores = dot_nt(k_image[start - TEXT : start - TEXT + tile], q_image)
            scores = jnp.concatenate([scores[:, :TEXT], scores[:, TEXT:] + bias], axis=1)
        soft = jnp.exp(scores)
        score_grad = soft * dot_nt(v_wide[here], grad_wide)
        low = score_grad.astype(BF)
        dvs.append(dot_nn(soft.astype(BF), grad))
        wide = dot_nn(low, q_marked)
        dks.append(wide[:, :LANES])
        dq = dq + dot_nn(k_turned[parity * HEAD : parity * HEAD + HEAD, here], low)
        rounded = wide.astype(BF)
        first_sum = first_sum + dot_nn(turned_refs[parity][:, here], rounded[:, :LANES])
        second_sum = second_sum + dot_nn(shared_t[:, here], rounded[:, LANES:])
        if start < TEXT:
            text_image = text_image + dot_nn(shared_t[:, here], low[:, TEXT:])
        else:
            by_position = wide[:, LANES:]
            on_image = score_grad[:, TEXT:]
    small = lax.broadcasted_iota(jnp.int32, (LANES, LANES), 1)
    small_row = lax.broadcasted_iota(jnp.int32, (LANES, LANES), 0)
    x0 = HEAD if parity == 0 else 0
    x_block = jnp.where(
        between(small, x0, x0 + COORD) & between(small_row, x0, x0 + COORD), first_sum, 0.0
    )
    y_block = jnp.where(
        between(small, Y0, Y0 + COORD) & between(small_row, Y0, Y0 + COORD), second_sum, 0.0
    )
    p_block = jnp.where((small < POS) & (small_row < POS), second_sum, 0.0)
    wide_lane = lax.broadcasted_iota(jnp.int32, (images, images), 1)
    outside = jnp.sum(jnp.where(is_image, 0.0, on_image), axis=1, keepdims=True)
    pairs = jnp.where(is_image, on_image, 0.0) + jnp.where(wide_lane == 0, outside, 0.0)
    outside_text = jnp.sum(jnp.where(is_image, 0.0, text_image), axis=1, keepdims=True)
    text_lane = lax.broadcasted_iota(jnp.int32, (LANES, images), 1)
    text_row = lax.broadcasted_iota(jnp.int32, (LANES, images), 0)
    text_image = jnp.where(is_image, text_image, 0.0) + jnp.where(
        text_lane == 0, outside_text, 0.0
    )
    text_image = jnp.where(text_row < POS, text_image, 0.0)
    first_lane = lax.broadcasted_iota(jnp.int32, (images, LANES), 1)
    left = pairs[:, :LANES] + jnp.where(first_lane < POS, by_position, 0.0)
    right = pairs[:, LANES:]
    a00, b00 = skewed(left[:LANES] + text_image[:, :LANES] + p_block)
    a01, b01 = skewed(right[:LANES] + text_image[:, LANES:])
    a10, b10 = skewed(left[LANES:])
    a11, b11 = skewed(right[LANES:])
    ax, bx = skewed(x_block)
    ay, by = skewed(y_block)
    diag_ref[2 * pair + parity] = jnp.concatenate(
        [b10, b00 + b11 + a10, a00 + a11 + b01, a01, bx, ax, by, ay], axis=0
    )
    empty = jnp.zeros_like(dq)
    both = [dq * 0.125, empty] if parity == 0 else [empty, dq * 0.125]
    results = (
        (d_query, jnp.transpose(jnp.concatenate(both, axis=0))),
        (d_key, jnp.concatenate(dks, axis=0)),
        (d_value, jnp.concatenate(dvs, axis=0)),
    )
    for ref, value in results:
        if parity == 1:
            value = jnp.where(own, value, ref[pair].astype(F32))
        ref[pair] = value.astype(BF)


MESH = pl.DeviceIdType.MESH
VMEM = pl.BlockSpec(memory_space=pltpu.VMEM)
HBM = pl.BlockSpec(memory_space=pltpu.HBM)
MIB = 1024 * 1024


def remote(src, dst, send, receive, device):
    return pltpu.make_async_remote_copy(
        src_ref=src, dst_ref=dst, send_sem=send, recv_sem=receive, device_id=device,
        device_id_type=MESH,
    )


def project_kernel(
    layer_ref, weight_hbm, *refs,
):
    small_hbm, refs = refs[:10], refs[10:]
    (item_ref, projected_out, columns_ref, rows_ref, table_ref,
     projected_ref, weight_ref, meta_send, bias_ref, sems, load_sems, store_sems), small = (
        refs[:12], refs[12:],
    )
    (segment_ref, mask_ref, position_ref, across_ref, down_ref, query_bias_ref, value_bias_ref,
     text_ref, horiz_ref, vert_ref) = small
    mine = lax.axis_index("seq")
    partner = (1 - mine, lax.axis_index("dp"))
    count, width = layer_ref.shape[1:]
    own = pl.ds(pl.multiple_of(mine * count, LANES), count)
    loads = [
        pltpu.make_async_copy(source, target, load_sems.at[index])
        for index, (source, target) in enumerate(
            list(zip(small_hbm, small))
            + [(layer_ref.at[mine], item_ref.at[own]), (weight_hbm, weight_ref)]
        )
    ]
    for load in loads:
        load.start()
    barrier = pltpu.get_barrier_semaphore()
    pl.semaphore_signal(barrier, inc=1, device_id=partner, device_id_type=MESH)
    pl.semaphore_wait(barrier, 1)
    pieces = count // LANES
    rows_out = [
        remote(
            layer_ref.at[1 - mine, pl.ds(piece * LANES, LANES)],
            item_ref.at[pl.ds(pl.multiple_of(mine * count + piece * LANES, LANES), LANES)],
            sems.at[0, piece], sems.at[1, piece], partner,
        )
        for piece in range(pieces)
    ]
    for copy in rows_out:
        copy.start()
    for load in loads[:-2]:
        load.wait()

    fields = (segment_ref, mask_ref, position_ref, across_ref, down_ref)
    blocks = [
        jnp.concatenate(
            [field[item : item + 1, :] for field in fields] + [jnp.zeros((3, count), jnp.int32)],
            axis=0,
        )
        for item in range(2)
    ]
    meta_send[...] = jnp.where(mine == 0, blocks[1], blocks[0])
    meta_out = remote(
        meta_send, rows_ref.at[:, own], sems.at[0, pieces], sems.at[1, pieces], partner
    )
    meta_out.start()
    rows_ref[:, own] = jnp.where(mine == 0, blocks[0], blocks[1])
    bias_ref[:, :width] = query_bias_ref[...].astype(F32).reshape(1, width)
    bias_ref[:, width : 2 * width] = jnp.zeros((1, width), F32)
    bias_ref[:, 2 * width :] = value_bias_ref[...].astype(F32).reshape(1, width)
    heads, levels = text_ref.shape
    spot = lax.broadcasted_iota(jnp.int32, (levels, LANES), 1)
    level = lax.broadcasted_iota(jnp.int32, (levels, LANES), 0)
    table = jnp.zeros((heads, LANES), F32)
    for source, begin in ((text_ref, 0), (horiz_ref, X_TABLE), (vert_ref, Y_TABLE)):
        table = table + dot_nn(source[...], (spot == level + begin).astype(BF))
    table_ref[...] = jnp.concatenate([table, jnp.zeros((16 - heads, LANES), F32)], axis=0)

    def project(there):
        step = 256

        def body(index, carry):
            columns = pl.ds(pl.multiple_of(index * step, step), step)
            product = dot_nn(item_ref[there], weight_ref[:, columns])
            projected_ref[there, columns] = (product + bias_ref[:, columns]).astype(BF)
            return carry

        lax.fori_loop(0, 3 * width // step, body, 0)

    def stored(index, there):
        return pltpu.make_async_copy(
            projected_ref.at[there], projected_out.at[there], store_sems.at[index]
        )

    for load in loads[-2:]:
        load.wait()
    project(own)
    stored(0, own).start()
    for piece in range(pieces):
        rows_out[piece].wait()
        there = pl.ds(pl.multiple_of((1 - mine) * count + piece * LANES, LANES), LANES)
        project(there)
        stored(1 + piece, there).start()
    meta_out.wait()
    meta = rows_ref[...].astype(F32)
    tall = jnp.concatenate([meta, jnp.zeros((LANES - 8, meta.shape[1]), F32)], axis=0)
    columns_ref[...] = jnp.transpose(tall).astype(jnp.int32)
    stored(0, own).wait()
    for piece in range(pieces):
        there = pl.ds(pl.multiple_of((1 - mine) * count + piece * LANES, LANES), LANES)
        stored(1 + piece, there).wait()


def projected_item(layer_in, fields, qkv_weight, query_bias, value_bias, tables):
    rows = 2 * layer_in.shape[1]
    width = layer_in.shape[2]
    pieces = rows // 2 // LANES
    small = list(fields) + [query_bias, value_bias] + [t.T for t in tables]
    return pl.pallas_call(
        project_kernel,
        in_specs=[HBM] * (2 + len(small)),
        out_specs=[VMEM, HBM, VMEM, VMEM, VMEM],
        out_shape=[
            jax.ShapeDtypeStruct((rows, width), BF),
            jax.ShapeDtypeStruct((rows, 3 * width), BF),
            jax.ShapeDtypeStruct((rows, LANES), jnp.int32),
            jax.ShapeDtypeStruct((8, rows), jnp.int32),
            jax.ShapeDtypeStruct((16, LANES), F32),
        ],
        scratch_shapes=[
            pltpu.VMEM((rows, 3 * width), BF),
            pltpu.VMEM((width, 3 * width), BF),
            pltpu.VMEM((8, rows // 2), jnp.int32),
            pltpu.VMEM((1, 3 * width), F32),
            pltpu.SemaphoreType.DMA((2, pieces + 1)),
            pltpu.SemaphoreType.DMA((len(small) + 2,)),
            pltpu.SemaphoreType.DMA((pieces + 1,)),
        ]
        + [pltpu.VMEM(array.shape, array.dtype) for array in small],
        compiler_params=pltpu.CompilerParams(
            collective_id=1, has_side_effects=True, vmem_limit_bytes=60 * MIB
        ),
        name="projected_item",
    )(layer_in, qkv_weight, *small)


EPSILON = 1e-05
TILE = 256


def vector(ref):
    return ref[...].astype(F32).reshape(1, ref.shape[0])


def gelu_and_slope(x):
    bell = jnp.exp(-0.5 * x * x)
    t = 1.0 / (1.0 + 0.23164188826 * jnp.abs(x))
    series = t * (
        0.127414796
        + t * (-0.142248368 + t * (0.7107068705 + t * (-0.7265760135 + t * 0.5307027145)))
    )
    tail = bell * series
    below = jnp.where(x >= 0.0, 1.0 - tail, tail)
    return x * below, below + x * (0.3989422804014327 * bell)


def row_mean(block):
    return jnp.mean(block, axis=1, keepdims=True)


def normalized(hidden):
    center = hidden - row_mean(hidden)
    scale = lax.rsqrt(row_mean(center * center) + EPSILON)
    return center * scale, scale


def norm_pulled(grad, unit, scale):
    return scale * (grad - row_mean(grad) - unit * row_mean(grad * unit))


def column_sum(block):
    return jnp.sum(block, axis=0, keepdims=True)


def feed_kernel(
    item_ref, mixed_ref, cotangent_ref, out_weight_ref, up_ref, down_ref, *refs,
):
    vectors_hbm, refs = refs[:7], refs[7:]
    (layer_out, d_hidden_ref, d_mixed_ref, grad_out_ref, grad_down_ref, grad_up_ref, small_ref,
     layer_ref, cotangent_all, active, slope, unit, scale_ref, normed, normed_t, total, d_branch, d_branch_t,
     sems, load_sems) = refs[:20]
    vectors = refs[20:]
    (out_bias_ref, attn_gain_ref, attn_shift_ref, up_bias_ref, down_bias_ref, ffn_gain_ref,
     ffn_shift_ref) = vectors
    step = pl.program_id(0)
    blocks = pl.num_programs(0) // 2
    rows, width = item_ref.shape
    count = rows // 2
    mine = lax.axis_index("seq")
    partner = (1 - mine, lax.axis_index("dp"))
    own = pl.ds(pl.multiple_of(mine * count, LANES), count)
    tiles = rows // TILE

    def sent():
        return remote(
            cotangent_ref.at[1 - mine], cotangent_all.at[own], sems.at[0], sems.at[1], partner
        )

    def returned():
        theirs = pl.ds(pl.multiple_of((1 - mine) * count, LANES), count)
        return [
            pltpu.make_async_copy(layer_ref.at[own], layer_out.at[mine], load_sems.at[8]),
            remote(
                layer_ref.at[theirs], layer_out.at[mine], sems.at[2], sems.at[3], partner
            ),
        ]

    def loads():
        copies = list(zip(vectors_hbm, vectors)) + [(cotangent_ref.at[mine], cotangent_all.at[own])]
        return [
            pltpu.make_async_copy(source, target, load_sems.at[index])
            for index, (source, target) in enumerate(copies)
        ]

    def over_columns(body, carry):
        def run(index, state):
            return body(pl.ds(pl.multiple_of(index * TILE, TILE), TILE), state)

        return lax.fori_loop(0, width // TILE, run, carry)

    def over_tiles(size, body, carry):
        def run(index, state):
            return body(pl.ds(pl.multiple_of(index * size, size), size), state)

        return lax.fori_loop(0, rows // size, run, carry)

    @pl.when(step == 0)
    def _():
        for load in loads():
            load.start()
        barrier = pltpu.get_barrier_semaphore()
        pl.semaphore_signal(barrier, inc=1, device_id=partner, device_id_type=MESH)
        pl.semaphore_wait(barrier, 1)
        sent().start()
        small_ref[...] = jnp.zeros_like(small_ref)
        for load in loads():
            load.wait()
        out_bias, gain, shift = vector(out_bias_ref), vector(attn_gain_ref), vector(attn_shift_ref)

        def tile(there, carry):
            attn = dot_nn(mixed_ref[there].astype(BF), out_weight_ref[...]) + out_bias
            standard, scale = normalized(item_ref[there].astype(F32) + attn)
            unit[there] = standard
            scale_ref[there] = jnp.broadcast_to(scale, (scale.shape[0], LANES))
            result = standard * gain + shift
            normed[there] = result.astype(BF)
            normed_t[:, there] = jnp.transpose(result).astype(BF)
            return carry

        over_tiles(TILE, tile, 0)
        total[...] = jnp.zeros_like(total)

    @pl.when(step < blocks)
    def _():
        def tile(here, carry):
            bias = up_bias_ref[pl.ds(pl.multiple_of(step * width + here.start, LANES), TILE)]
            bias = bias.astype(F32).reshape(1, TILE)
            value, grade = gelu_and_slope(dot_nn(normed[...], up_ref[:, here]) + bias)
            active[step, :, here] = value.astype(BF)
            slope[step, :, here] = grade
            return carry

        over_columns(tile, 0)

        def tile(here, carry):
            total[:, here] += dot_nn(active[step], down_ref[:, here])
            return carry

        over_columns(tile, 0)

    @pl.when(step == blocks)
    def _():
        sent().wait()
        gain, shift, bias = vector(ffn_gain_ref), vector(ffn_shift_ref), vector(down_bias_ref)
        first_gain, first_shift = vector(attn_gain_ref), vector(attn_shift_ref)

        def tile(there, sums):
            hidden = unit[there] * first_gain + first_shift + (total[there] + bias)
            standard, scale = normalized(hidden)
            layer_ref[there] = (standard * gain + shift).astype(BF)
            cotangent = cotangent_all[there].astype(F32)
            pulled = norm_pulled(cotangent * gain, standard, scale)
            total[there] = pulled
            low = pulled.astype(BF)
            d_branch[there] = low
            return (
                sums[0] + column_sum(low.astype(F32)),
                sums[1] + column_sum(cotangent * standard),
                sums[2] + column_sum(cotangent),
            )

        zero = jnp.zeros((1, width), F32)
        sums = over_tiles(64, tile, (zero, zero, zero))
        for row, value in zip((5, 6, 7), sums):
            small_ref[row : row + 1] = value

        for copy in returned():
            copy.start()

        def turn(there, carry):
            d_branch_t[:, there] = jnp.transpose(d_branch[there].astype(F32)).astype(BF)
            return carry

        over_tiles(TILE, turn, 0)

    @pl.when(step >= blocks)
    def _():
        block = step - blocks

        def tile(here, carry):
            grad_down_ref[:, here] = dot_nn(d_branch_t[...], active[block, :, here]).astype(BF)
            return carry

        over_columns(tile, 0)

        def tile(here, carry):
            d_up = (dot_nt(d_branch[...], down_ref[here]) * slope[block, :, here]).astype(BF)
            active[block, :, here] = d_up
            small_ref[pl.ds(8 + block, 1), here] = column_sum(d_up.astype(F32))
            return carry

        over_columns(tile, 0)

        def tile(here, carry):
            grad_up_ref[:, here] = dot_nn(normed_t[...], active[block, :, here]).astype(BF)
            total[:, here] += dot_nt(active[block], up_ref[here])
            return carry

        over_columns(tile, 0)

    @pl.when(step == 2 * blocks - 1)
    def _():
        gain = vector(attn_gain_ref)

        def tile(there, sums):
            d_normed = total[there]
            standard = unit[there]
            d_hidden = norm_pulled(d_normed * gain, standard, scale_ref[there, :1])
            d_hidden_ref[there] = d_hidden
            low = d_hidden.astype(BF)
            d_branch[there] = low
            return (
                sums[0] + column_sum(low.astype(F32)),
                sums[1] + column_sum(d_normed * standard),
                sums[2] + column_sum(d_normed),
            )

        zero = jnp.zeros((1, width), F32)
        sums = over_tiles(64, tile, (zero, zero, zero))
        for row, value in zip((2, 3, 4), sums):
            small_ref[row : row + 1] = value

        def turn(there, carry):
            normed_t[:, there] = jnp.transpose(mixed_ref[there]).astype(BF)
            return carry

        over_tiles(TILE, turn, 0)

        def tile(here, carry):
            d_mixed_ref[:, here] = dot_nt(d_branch[...], out_weight_ref[here]).astype(BF)
            grad_out_ref[:, here] = dot_nn(normed_t[...], d_branch[:, here]).astype(BF)
            return carry

        over_columns(tile, 0)
        for copy in returned():
            copy.wait()


def fed_forward_and_back(
    item, mixed, cotangent, out_weight, up_weight, down_weight, vectors,
):
    rows, width = item.shape
    blocks = up_weight.shape[1] // width
    whole = pl.BlockSpec(memory_space=pltpu.VMEM)
    square = lambda kind: jax.ShapeDtypeStruct((rows, width), kind)
    later = lambda i: jnp.maximum(i - blocks, 0)
    return pl.pallas_call(
        feed_kernel,
        grid=(2 * blocks,),
        in_specs=[whole, whole, HBM, whole]
        + [
            pl.BlockSpec((width, width), lambda i: (0, lax.rem(i, blocks))),
            pl.BlockSpec((width, width), lambda i: (lax.rem(i, blocks), 0)),
        ]
        + [HBM] * 7,
        out_specs=[HBM] + [whole] * 3
        + [
            pl.BlockSpec((width, width), lambda i: (later(i), 0)),
            pl.BlockSpec((width, width), lambda i: (later(i), 0)),
            whole,
        ],
        out_shape=[
            jax.ShapeDtypeStruct((2, rows // 2, width), BF), square(F32), square(BF),
            jax.ShapeDtypeStruct((width, width), BF),
            jax.ShapeDtypeStruct((blocks * width, width), BF),
            jax.ShapeDtypeStruct((blocks * width, width), BF),
            jax.ShapeDtypeStruct((16, width), F32),
        ],
        scratch_shapes=[
            pltpu.VMEM((rows, width), BF),
            pltpu.VMEM((rows, width), BF),
            pltpu.VMEM((blocks, rows, width), BF),
            pltpu.VMEM((blocks, rows, width), F32),
            pltpu.VMEM((rows, width), F32),
            pltpu.VMEM((rows, LANES), F32),
            pltpu.VMEM((rows, width), BF),
            pltpu.VMEM((width, rows), BF),
            pltpu.VMEM((rows, width), F32),
            pltpu.VMEM((rows, width), BF),
            pltpu.VMEM((width, rows), BF),
            pltpu.SemaphoreType.DMA((4,)),
            pltpu.SemaphoreType.DMA((9,)),
        ]
        + [pltpu.VMEM(vector.shape, vector.dtype) for vector in vectors],
        compiler_params=pltpu.CompilerParams(
            collective_id=2, has_side_effects=True, vmem_limit_bytes=60 * MIB
        ),
        name="feed_forward",
    )(item, mixed, cotangent, out_weight, up_weight, down_weight, *vectors)


SLOTS = 4


def finish_kernel(
    summed_ref, input_hbm, small_ref, diagonal_ref,
    down_ref, up_ref, out_ref, qkv_ref, input_ref, *refs,
):
    singles, (blocks_in, slots, input_in, input_slot, in_sems, out_sems, item_sems) = (
        refs[:12], refs[12:],
    )
    blocks, width = blocks_in.shape[0], blocks_in.shape[2]
    hidden = down_ref.shape[0] // width

    def load(block):
        return pltpu.make_async_copy(
            summed_ref.at[pl.ds(block * width, width)], blocks_in.at[block], in_sems.at[block]
        )

    def stores(block):
        slot, sem = slots.at[block % SLOTS], out_sems.at[block % SLOTS]
        if block < hidden:
            targets = [(slot, down_ref.at[pl.ds(block * width, width)])]
        elif block < 2 * hidden:
            targets = [(slot, up_ref.at[:, pl.ds((block - hidden) * width, width)])]
        elif block == 2 * hidden:
            targets = [(slot, out_ref)]
        else:
            first = 2 * (block - 2 * hidden - 1)
            targets = [
                (
                    slot.at[:, pl.ds((3 * pair + part) * LANES, LANES)],
                    qkv_ref.at[:, pl.ds(part * width + (first + pair) * LANES, LANES)],
                )
                for pair in range(2) for part in range(3)
            ]
        return [
            pltpu.make_async_copy(source, target, sem.at[index])
            for index, (source, target) in enumerate(targets)
        ]

    load_input = pltpu.make_async_copy(input_hbm, input_in, item_sems.at[0])
    store_input = pltpu.make_async_copy(input_slot, input_ref, item_sems.at[1])
    for block in range(blocks):
        load(block).start()
    load_input.start()
    for block in range(blocks):
        load(block).wait()
        if block >= SLOTS:
            for copy in stores(block - SLOTS):
                copy.wait()
        piece = blocks_in[block].astype(F32)
        slots[block % SLOTS] = jnp.transpose(piece) if block < hidden else piece
        for copy in stores(block):
            copy.start()
    load_input.wait()
    input_slot[...] = input_in[...].astype(F32)
    store_input.start()
    for row in range(8):
        singles[row][...] = small_ref[row]
    for row in range(hidden):
        singles[8][row * width : row * width + width] = small_ref[8 + row]
    heads, levels = singles[9].shape
    diagonals = diagonal_ref[...]
    level = lax.broadcasted_iota(jnp.int32, (LANES, LANES), 1)
    lane = lax.broadcasted_iota(jnp.int32, (LANES, LANES), 0)
    for table, (first, size, skip) in enumerate(((0, 4, 0), (4, 2, 1), (6, 2, 1))):
        total = jnp.zeros((heads, LANES), F32)
        for row in range(size):
            distance = lane + LANES * (row + skip - 2)
            chosen = (bucket(distance) == level).astype(F32)
            total = total + jnp.dot(
                diagonals[:, first + row, :], chosen, preferred_element_type=F32,
                precision=lax.Precision.HIGHEST,
            )
        singles[9 + table][...] = total[:, :levels]
    for block in range(blocks - SLOTS, blocks):
        for copy in stores(block):
            copy.wait()
    store_input.wait()


def finished(summed, grad_input, small, diagonals, hidden, levels):
    width = summed.shape[1]
    heads = diagonals.shape[0]
    blocks = summed.shape[0] // width
    single = jax.ShapeDtypeStruct((width,), F32)
    table = jax.ShapeDtypeStruct((heads, levels), F32)
    dma = pltpu.SemaphoreType.DMA
    return pl.pallas_call(
        finish_kernel,
        in_specs=[HBM, HBM, VMEM, VMEM],
        out_specs=[HBM] * 5 + [VMEM] * 12,
        out_shape=[
            jax.ShapeDtypeStruct((hidden, width), F32),
            jax.ShapeDtypeStruct((width, hidden), F32),
            jax.ShapeDtypeStruct((width, width), F32),
            jax.ShapeDtypeStruct((width, 3 * width), F32),
            jax.ShapeDtypeStruct(grad_input.shape, F32),
        ]
        + [single] * 8
        + [jax.ShapeDtypeStruct((hidden,), F32)]
        + [table] * 3,
        scratch_shapes=[
            pltpu.VMEM((blocks, width, width), BF),
            pltpu.VMEM((SLOTS, width, width), F32),
            pltpu.VMEM(grad_input.shape, BF),
            pltpu.VMEM(grad_input.shape, F32),
            dma((blocks,)),
            dma((SLOTS, 6)),
            dma((2,)),
        ],
        compiler_params=pltpu.CompilerParams(vmem_limit_bytes=56 * MIB),
        name="finished",
    )(summed, grad_input, small, diagonals)


PIECE = 16


def hop_names(depth):
    names = ["x", "y"]
    reach = 1
    while reach < depth:
        names.append(f"z{reach}")
        reach *= 2
    return names


def routes(depth):
    line = hop_names(depth)[2:]
    return (["x", "y"] + line, ["y"] + line + ["x"])


class Place:
    def __init__(self, depth):
        place = lax.axis_index("dp")
        x = lax.axis_index("seq")
        core = lax.rem(place, 2)
        y = lax.rem(lax.div(place, 2), 2)
        z = lax.rem(lax.div(place, 4), depth)
        group = lax.div(place, 4 * depth)
        at = lambda sx, sc, sy, sz: (sx, (group * depth + sz) * 4 + sy * 2 + sc)
        self.bits = {"core": core, "x": x, "y": y}
        self.partners = {
            "core": at(x, 1 - core, y, z), "x": at(1 - x, core, y, z), "y": at(x, core, 1 - y, z),
        }
        reach = 1
        while reach < depth:
            up = lax.rem(lax.div(z, reach), 2)
            self.bits[f"z{reach}"] = up
            self.partners[f"z{reach}"] = at(x, core, y, z + reach - 2 * reach * up)
            reach *= 2

    def greet(self):
        barrier = pltpu.get_barrier_semaphore()
        for device in self.partners.values():
            pl.semaphore_signal(barrier, inc=1, device_id=device, device_id_type=MESH)
        pl.semaphore_wait(barrier, len(self.partners))


class Chunk:
    def __init__(self, place, depth, source, out_ref, offset, spot, scratch):
        _, self.begin, rows, first, columns, _ = spot
        self.place, self.source, self.columns = place, source, pl.ds(first, columns)
        self.out_ref, self.out_begin = out_ref, offset + self.begin
        self.half, self.quarter = rows // 2, rows // 4
        self.routes = routes(depth)
        self.hops = len(self.routes[0])
        self.stages = 2 * self.hops + 3
        self.work, self.fresh, *self.landing, self.sends, self.receives, self.locals = scratch

    def aligned(self, value):
        return pl.multiple_of(value, PIECE)

    def size(self, hop):
        return self.quarter >> (hop + 1)

    def base(self, part, hops):
        start = part * self.quarter
        for hop in range(hops):
            start = start + self.place.bits[self.routes[part][hop]] * self.size(hop)
        return start

    def across(self, part, hop):
        bit = self.place.bits[self.routes[part][hop]]
        return self.base(part, hop) + (1 - bit) * self.size(hop)

    def partner(self, part, hop):
        return self.place.partners[self.routes[part][hop]]

    def out(self, begin, size, core=None):
        core = self.place.bits["core"] if core is None else core
        return self.out_ref.at[
            pl.ds(self.aligned(self.out_begin + core * self.half + begin), size), self.columns
        ]

    def copy(self, index, source, target, device):
        return remote(source, target, self.sends.at[index], self.receives.at[index], device)

    def pair_down(self):
        core = self.place.bits["core"]
        at = lambda c: self.source.at[
            pl.ds(self.aligned(self.begin + c * self.half), self.half), self.columns
        ]
        return [
            self.copy(0, at(1 - core), self.fresh, self.place.partners["core"]),
            pltpu.make_async_copy(at(core), self.work, self.locals.at[0]),
        ]

    def pair_up(self, arriving):
        core = self.place.bits["core"]
        target = self.out(0, self.half, 1 - core if arriving else core)
        return [self.copy(1, self.out(0, self.half), target, self.place.partners["core"])]

    def down(self, hop):
        return [
            self.copy(
                2 + 2 * hop + part,
                self.work.at[pl.ds(self.aligned(self.across(part, hop)), self.size(hop))],
                self.landing[hop].at[part], self.partner(part, hop),
            )
            for part in range(2)
        ]

    def kept(self):
        size = self.size(self.hops - 1)
        copies = []
        for part in range(2):
            begin = self.aligned(self.base(part, self.hops))
            copies.append(
                pltpu.make_async_copy(
                    self.work.at[pl.ds(begin, size)], self.out(begin, size),
                    self.locals.at[1 + part],
                )
            )
        return copies

    def up(self, hop, arriving):
        copies = []
        for part in range(2):
            mine = self.base(part, hop + 1)
            size = self.size(hop)
            if hop == self.hops - 1:
                source = self.work.at[pl.ds(self.aligned(mine), size)]
            else:
                source = self.out(mine, size)
            target = self.out(self.across(part, hop) if arriving else mine, size)
            index = 2 + 2 * self.hops + 2 * hop + part
            copies.append(self.copy(index, source, target, self.partner(part, hop)))
        return copies

    def add(self, begin, source, size):
        step = 64 if size % 64 == 0 else min(size, PIECE)

        def body(index, carry):
            offset = self.aligned(index * step)
            there = pl.ds(self.aligned(begin + offset), step)
            total = self.work[there].astype(F32) + source[pl.ds(offset, step)].astype(F32)
            self.work[there] = total.astype(BF)
            return carry

        lax.fori_loop(0, size // step, body, 0)

    def stage(self, number):
        hops = self.hops
        ended, started = [], []
        if number == 0:
            started = self.pair_down()
        elif number == 1:
            ended = self.pair_down()
            started = self.down(0)
        elif number <= hops:
            ended = self.down(number - 2)
            started = self.down(number - 1)
        elif number == hops + 1:
            ended = self.down(hops - 1)
            started = self.up(hops - 1, False) + self.kept()
        elif number <= 2 * hops:
            level = 2 * hops + 1 - number
            ended = self.up(level, True) + (self.kept() if level == hops - 1 else [])
            started = self.up(level - 1, False)
        elif number == 2 * hops + 1:
            ended = self.up(0, True)
            started = self.pair_up(False)
        else:
            ended = self.pair_up(True)
        for copy in ended:
            copy.wait()
        if number == 1:
            self.add(0, self.fresh, self.half)
        elif 2 <= number <= hops + 1:
            hop = number - 2
            for part in range(2):
                self.add(self.base(part, hop + 1), self.landing[hop].at[part], self.size(hop))
        for copy in started:
            copy.start()


def chunk_scratch(rows, width, depth):
    hops = len(routes(depth)[0])
    dma = pltpu.SemaphoreType.DMA
    return (
        [pltpu.VMEM((rows // 2, width), BF)] * 2
        + [pltpu.VMEM((2, rows // 4 >> (hop + 1), width), BF) for hop in range(hops)]
        + [dma((2 + 4 * hops,)), dma((2 + 4 * hops,)), dma((3,))]
    )


def planned(chunks, work, depth, hop_count):
    latency, issue, link, pair = 2.0, 0.2, 100e3, 600e3
    free = {}
    now = 0.0

    def sent(name, rows, columns):
        nonlocal now
        now += issue
        row_bytes = 2 * columns
        share = {"core": [("core", rows * row_bytes / pair)]}.get(name)
        if share is None:
            time = 2 * rows * row_bytes / link
            share = [(name, time)]
            if name[0] == "z":
                reach = int(name[1:])
                share = [("z end", time), ("z middle", 0.0 if reach == 1 else reach * time)]
        end = now
        for lane, time in share:
            free[lane] = max(now, free.get(lane, 0.0)) + time
            end = max(end, free[lane])
        return end + latency

    paths = routes(depth)
    chains = []
    for rows, columns, need in chunks:
        down = []
        size = rows // 4
        for hop in range(len(paths[0])):
            size //= 2
            down.append([(path[hop], size, columns) for path in paths])
        pair_step = [[("core", rows // 2, columns)]]
        chains.append((need, pair_step + down + down[::-1] + pair_step))
    chains.append((len(work), [[("core", 16, 768)]] * hop_count))
    position = [0] * len(chains)
    ready = [0.0] * len(chains)
    order = [[] for _ in range(len(work) + 1)]
    done = 0
    while True:
        open_ones = [
            (ready[i], i) for i, (need, chain) in enumerate(chains)
            if position[i] <= len(chain) and need <= done
        ]
        due = [entry for entry in open_ones if entry[0] <= now + 0.3]
        if not due and done < len(work):
            now += work[done]
            done += 1
            continue
        if not open_ones:
            return order
        when, index = min(due or open_ones)
        now = max(now, when)
        chain = chains[index][1]
        stage = position[index]
        order[done].append((index, stage))
        if 0 < stage <= len(chain) // 2:
            now += 2e-6 * sum(rows * wide for _, rows, wide in chain[stage - 1])
        if stage < len(chain):
            ready[index] = max(sent(*entry) for entry in chain[stage])
        position[index] += 1


def last_kernel(
    depth, plan, orders, *refs,
):
    (meta_ref, rows_ref, table_ref, q_ref, k_ref, v_ref, mixed_ref, grad_ref, log_ref,
     small_ref, item_hbm, weight_hbm, d_hidden_hbm, grad_down_ref, grad_up_ref, grad_out_ref,
     out_ref, small_out, diagonal_out, input_out,
     *scratch) = refs
    static, scratch = scratch[:11], scratch[11:]
    (item_ref, weight_ref, total_ref, load_sems, d_query, d_key, d_value, item_t, tail, input_grad,
     small_in, diagonal_in, small_sems, item_sems, *scratch) = scratch
    place = Place(depth)
    step = pl.program_id(0)
    pairs = d_query.shape[0]
    rows, width = item_hbm.shape
    count = rows // 2
    x = place.bits["x"]
    sources = (grad_down_ref, grad_up_ref, tail)
    each = len(scratch) // len(plan)
    chunks = []
    for index, spot in enumerate(plan):
        offset = spot[0] * grad_down_ref.shape[0]
        chunks.append(
            Chunk(place, depth, sources[spot[0]], out_ref, offset, spot,
                  scratch[index * each : index * each + each])
        )
    hop_devices = list(place.partners.values())

    def loads():
        pairs_of = (
            (item_hbm, item_ref), (weight_hbm, weight_ref), (d_hidden_hbm, total_ref),
            (grad_out_ref, tail.at[pl.ds(0, width)]),
        )
        return [
            pltpu.make_async_copy(source, target, load_sems.at[index])
            for index, (source, target) in enumerate(pairs_of)
        ]

    def input_copies():
        return [
            pltpu.make_async_copy(
                input_grad.at[pl.ds(pl.multiple_of(x * count, LANES), count)], input_out.at[x],
                item_sems.at[0],
            ),
            remote(
                input_grad.at[pl.ds(pl.multiple_of((1 - x) * count, LANES), count)],
                input_out.at[x], item_sems.at[1], item_sems.at[2], place.partners["x"],
            ),
        ]

    def small_copies(hop):
        return [
            remote(source, landing.at[hop], small_sems.at[0, kind, hop],
                   small_sems.at[1, kind, hop], hop_devices[hop])
            for kind, (source, landing) in enumerate(
                ((small_out, small_in), (diagonal_out, diagonal_in))
            )
        ]

    def small_stage(hop):
        if hop > 0:
            for copy in small_copies(hop - 1):
                copy.wait()
            small_out[...] = small_out[...] + small_in[hop - 1]
            diagonal_out[...] = diagonal_out[...] + diagonal_in[hop - 1]
        if hop < len(hop_devices):
            for copy in small_copies(hop):
                copy.start()

    def perform(slot):
        for index, stage in orders[slot]:
            if index == len(chunks):
                small_stage(stage)
            else:
                chunks[index].stage(stage)

    @pl.when(step == 0)
    def _():
        place.greet()
        for copy in loads():
            copy.start()
        small_out[...] = small_ref[...]
        static_prepare(meta_ref, static)

    def slab(first):
        pieces = [
            (pair, part) for pair in (first, first + 1) for part in range(3)
        ]
        held = (d_query, d_key, d_value)
        base = width + first // 2 * width
        for left, right in zip(pieces[::2], pieces[1::2]):
            both = jnp.concatenate([held[part][pair] for pair, part in (left, right)], axis=1)
            weights = jnp.concatenate(
                [
                    weight_ref[:, part * width + pair * LANES : part * width + (pair + 1) * LANES]
                    for pair, part in (left, right)
                ],
                axis=1,
            )
            at = pieces.index(left) * LANES
            tail[base : base + width, at : at + 2 * LANES] = dot_nn(item_t[...], both).astype(BF)
            total_ref[...] += dot_nt(both, weights)
        for pair in (first, first + 1):
            columns = slice(pair * LANES, pair * LANES + LANES)
            small_out[0:1, columns] = column_sum(d_query[pair].astype(F32))
            small_out[1:2, columns] = column_sum(d_value[pair].astype(F32))

    @pl.when(step == 1)
    def _():
        for copy in loads():
            copy.wait()
        for tile in range(rows // TILE):
            there = slice(tile * TILE, tile * TILE + TILE)
            item_t[:, there] = jnp.transpose(item_ref[there].astype(F32)).astype(BF)

    for parity in range(2):
        for pair in range(pairs):
            @pl.when(step == pair)
            def _(pair=pair):
                perform(2 * pair + pair // 2 + parity)

        head_back(
            parity, step, meta_ref, rows_ref, table_ref, q_ref, k_ref, v_ref, mixed_ref,
            grad_ref, log_ref, static, d_query, d_key, d_value, diagonal_out,
        )

    for pair in range(1, pairs, 2):
        @pl.when(step == pair)
        def _(pair=pair):
            perform(2 * pair + 2 + pair // 2)
            slab(pair - 1)

    @pl.when(step == pairs - 1)
    def _():
        input_grad[...] = total_ref[...].astype(BF)
        for copy in input_copies():
            copy.start()
        perform(len(orders) - 1)
        for copy in input_copies():
            copy.wait()


def summed_with_attention_back(
    meta_columns, meta_rows, table_rows, projected, mixed, d_mixed, logs, item, qkv_weight,
    d_hidden, small, grad_down, grad_up, grad_out,
):
    size = lax.axis_size("dp")
    depth = 4 if size % 16 == 0 else size // 4
    rows, width = item.shape
    pairs = width // LANES
    hidden = grad_down.shape[0]
    hops = len(hop_names(depth)) + 1
    work = ([3.2] * 4 + [4.2]) * (pairs // 2)
    wide = width // 2
    plan = [(source, 0, hidden, first, wide, 0) for source in (0, 1) for first in (0, wide)]
    plan += [(2, 0, 1024, 0, width, 5), (2, 1024, 1024, 0, width, 10)]
    plan += [(2, 2048, 1024, first, wide, 15) for first in (0, wide)]
    orders = planned([(spot[2], spot[4], spot[5]) for spot in plan], work, depth, hops)

    def block(part):
        return pl.BlockSpec((rows, LANES), lambda p: (0, part * pairs + p))

    whole = pl.BlockSpec(memory_space=pltpu.VMEM)
    diagonals = jax.ShapeDtypeStruct((2 * pairs, 8, LANES), F32)
    dma = pltpu.SemaphoreType.DMA
    scratch = []
    for spot in plan:
        scratch += chunk_scratch(spot[2], spot[4], depth)
    summed, small, diagonals, grad_input = pl.pallas_call(
        functools.partial(last_kernel, depth, plan, orders),
        grid=(pairs,),
        in_specs=[whole] * 3
        + [block(0), block(1), block(2), block(0), block(0)]
        + [pl.BlockSpec((1, rows, LANES), lambda p: (p, 0, 0))]
        + [whole]
        + [HBM] * 6,
        out_specs=[HBM, whole, whole, HBM],
        out_shape=[
            jax.ShapeDtypeStruct((3 * hidden, width), BF),
            jax.ShapeDtypeStruct(small.shape, F32),
            diagonals,
            jax.ShapeDtypeStruct((2, rows // 2, width), BF),
        ],
        scratch_shapes=static_scratch(rows)
        + [pltpu.VMEM((LANES, rows), BF)] * 3
        + [
            pltpu.VMEM((rows, width), BF),
            pltpu.VMEM((width, 3 * width), BF),
            pltpu.VMEM((rows, width), F32),
            dma((4,)),
        ]
        + [pltpu.VMEM((pairs, rows, LANES), BF)] * 3
        + [
            pltpu.VMEM((width, rows), BF),
            pltpu.VMEM((hidden, width), BF),
            pltpu.VMEM((rows, width), BF),
            pltpu.VMEM((hops,) + small.shape, F32),
            pltpu.VMEM((hops,) + diagonals.shape, F32),
            dma((2, 2, hops)),
            dma((3,)),
        ]
        + scratch,
        compiler_params=pltpu.CompilerParams(
            collective_id=0, has_side_effects=True, vmem_limit_bytes=62 * MIB
        ),
        name="summed_with_attention_back",
    )(meta_columns, meta_rows, table_rows, projected, projected, projected, mixed, d_mixed, logs,
      small, item, qkv_weight, d_hidden, grad_down, grad_up, grad_out)
    span = 4 * depth
    if size > span:
        groups = [list(range(first, size, span)) for first in range(span)]
        summed, small, diagonals = lax.psum(
            (summed.astype(F32), small, diagonals), "dp", axis_index_groups=groups
        )
        summed = summed.astype(BF)
    return summed, small, diagonals, grad_input


def per_device(
    layer_in, segment, key_mask, position, layout_x, layout_y,
    qkv_weight, query_bias, value_bias, out_weight, out_bias, attn_gain, attn_shift,
    up_weight, up_bias, down_weight, down_bias, ffn_gain, ffn_shift,
    text_table, horiz_table, vert_table, cotangent,
):
    width = layer_in.shape[-1]
    item, projected, meta_columns, meta_rows, table_rows = projected_item(
        layer_in, (segment, key_mask, position, layout_x, layout_y),
        qkv_weight, query_bias, value_bias, (text_table, horiz_table, vert_table),
    )
    mixed, logs = attention_forward(meta_columns, meta_rows, table_rows, projected, width)
    layer_out, d_hidden, d_mixed, grad_out, grad_down, grad_up, small = fed_forward_and_back(
        item, mixed, cotangent, out_weight, up_weight, down_weight,
        (out_bias, attn_gain, attn_shift, up_bias, down_bias, ffn_gain, ffn_shift),
    )
    summed, small, diagonals, grad_input = summed_with_attention_back(
        meta_columns, meta_rows, table_rows, projected, mixed, d_mixed, logs, item, qkv_weight,
        d_hidden, small, grad_down, grad_up, grad_out,
    )
    done = finished(
        summed, grad_input, small, diagonals, up_weight.shape[1], text_table.shape[0]
    )
    sum_down, sum_up, sum_out, sum_qkv, grad_input = done[:5]
    singles, tables = done[5:14], [t.T for t in done[14:]]
    return (
        layer_out, grad_input, sum_qkv, singles[0], singles[1], sum_out, singles[2], singles[3],
        singles[4], sum_up, singles[8], sum_down, singles[5], singles[6], singles[7],
        tables[0], tables[1], tables[2],
    )


def solution(mesh):
    rows = P("dp", "seq", None)
    marks_spec = P("dp", "seq")
    return jax.shard_map(
        per_device,
        mesh=mesh,
        in_specs=(rows,) + (marks_spec,) * 5 + (P(),) * 16 + (rows,),
        out_specs=(rows, rows) + (P(),) * 16,
        check_vma=False,
    )
```

```python
import functools

import jax
import jax.numpy as jnp
from jax import lax
from jax.experimental import pallas as pl
from jax.experimental.pallas import tpu as pltpu
from jax.sharding import PartitionSpec as P

BF = jnp.bfloat16
F32 = jnp.float32
BIG = 1e30
LANES = 128
HEAD = 64
TEXT = 512
POS = 64
COORD = 48
Y0 = 64
GROUP0 = 112
MEMBER0 = 116
FLAG = 124
LOG0 = 125
X_TABLE = 33
Y_TABLE = 66
NOTHING = 127


def dot_nt(a, b):
    return lax.dot_general(a, b, (((1,), (1,)), ((), ())), preferred_element_type=F32)


def dot_nn(a, b):
    return lax.dot_general(a, b, (((1,), (0,)), ((), ())), preferred_element_type=F32)


def looked_up(table_row, index):
    rows = index.shape[0]
    return jnp.take_along_axis(
        jnp.broadcast_to(table_row, (rows, LANES)), index, axis=1, mode="promise_in_bounds"
    )


def bucket(distance):
    return jnp.clip(distance, -16, 16) + 16


def between(lane, low, high):
    return (lane >= low) & (lane < high)


def columns_of(meta_ref):
    return tuple(meta_ref[:, field : field + 1] for field in range(5))


def marks(meta_ref):
    segment, key_mask, position, across, down = columns_of(meta_ref)
    rows = segment.shape[0]
    lane = lax.broadcasted_iota(jnp.int32, (rows, LANES), 1)
    row = lax.broadcasted_iota(jnp.int32, (rows, LANES), 0)
    even = between(lane, HEAD, HEAD + COORD) & (lane - HEAD == across)
    odd = (lane < COORD) & (lane == across)
    group = (segment - 1) >> 3
    member = (segment - 1) & 7
    named = segment > 0
    shared = (
        ((row < TEXT) & (lane < POS) & (lane == position))
        | (between(lane, Y0, Y0 + COORD) & (lane - Y0 == down))
        | (named & between(lane, GROUP0, MEMBER0) & (lane - GROUP0 == group))
        | (named & between(lane, MEMBER0, FLAG) & (lane - MEMBER0 == member))
        | ((lane == FLAG) & (key_mask <= 0))
        | (lane >= LOG0)
    )
    return tuple(jnp.where(m, 1.0, 0.0).astype(BF) for m in (even, odd, shared))


def barred(meta_ref):
    segment = meta_ref[:, 0:1]
    rows = segment.shape[0]
    lane = lax.broadcasted_iota(jnp.int32, (rows, LANES), 1)
    group = (segment - 1) >> 3
    member = (segment - 1) & 7
    shut = (
        ((segment > 0) & between(lane, GROUP0, MEMBER0) & (lane - GROUP0 != group))
        | ((segment < 0) & between(lane, GROUP0, MEMBER0))
        | ((segment > 0) & between(lane, MEMBER0, FLAG) & (lane - MEMBER0 != member))
        | (lane == FLAG)
    )
    return jnp.where(shut, -BIG, 0.0).astype(F32)


def query_index(meta_ref):
    segment, key_mask, position, across, down = columns_of(meta_ref)
    rows = segment.shape[0]
    lane = lax.broadcasted_iota(jnp.int32, (rows, LANES), 1)
    x_even = bucket(across - (lane - HEAD)) + X_TABLE
    x_odd = bucket(across - lane) + X_TABLE
    even = jnp.where(between(lane, HEAD, HEAD + COORD), x_even, NOTHING)
    odd = jnp.where(lane < COORD, x_odd, NOTHING)
    shared = jnp.where(
        lane < POS,
        bucket(position - lane),
        jnp.where(between(lane, Y0, Y0 + COORD), bucket(down - (lane - Y0)) + Y_TABLE, NOTHING),
    )
    return even, odd, shared


def image_key_index(meta_ref):
    position = meta_ref[TEXT:, 2:3]
    lane = lax.broadcasted_iota(jnp.int32, (position.shape[0], LANES), 1)
    return jnp.where(lane < POS, bucket(lane - position), NOTHING)


def prepare(meta_ref, mark_refs, bar_ref, index_refs, key_index_ref):
    for ref, value in zip(mark_refs, marks(meta_ref)):
        ref[...] = value
    bar_ref[...] = barred(meta_ref)
    for ref, value in zip(index_refs, query_index(meta_ref)):
        ref[...] = value
    key_index_ref[...] = image_key_index(meta_ref)


def image_offsets(row_positions, column_positions):
    return bucket(column_positions - row_positions)


def widened(parity, q, k, table_row, mark_refs, bar_ref, index_refs, key_index_ref, logs):
    rows = q.shape[0]
    lane = lax.broadcasted_iota(jnp.int32, (rows, LANES), 1)
    own = (lane < HEAD) if parity == 0 else (lane >= HEAD)
    first = jnp.where(own, q.astype(F32) * 0.125, looked_up(table_row, index_refs[parity][...]))
    second = looked_up(table_row, index_refs[2][...]) + bar_ref[...]
    if logs is not None:
        high = logs.astype(BF).astype(F32)
        middle = (logs - high).astype(BF).astype(F32)
        lowest = logs - high - middle
        second = jnp.where(
            lane == LOG0,
            -high,
            jnp.where(lane == LOG0 + 1, -middle, jnp.where(lane == LOG0 + 2, -lowest, second)),
        )
    first = first.astype(BF)
    second = second.astype(BF)
    mark_second = mark_refs[2][...]
    to_image = jnp.where(lane < POS, mark_second, second)
    key_first = jnp.where(own, k, mark_refs[parity][...])
    image_lane = lane[TEXT:]
    key_image = jnp.where(
        image_lane < POS,
        looked_up(table_row, key_index_ref[...]).astype(BF),
        mark_second[TEXT:],
    )
    q_text = jnp.concatenate([first, second], axis=1)
    q_image = jnp.concatenate([first, to_image], axis=1)
    k_text = jnp.concatenate([key_first[:TEXT], mark_second[:TEXT]], axis=1)
    k_image = jnp.concatenate([key_first[TEXT:], key_image], axis=1)
    return q_text, q_image, k_text, k_image


def image_bias(table_row, offsets):
    return jnp.concatenate(
        [looked_up(table_row, offsets[:, :LANES]), looked_up(table_row, offsets[:, LANES:])], axis=1
    )


def forward_kernel(
    meta_ref, rows_ref, table_ref, q_ref, k_ref, v_ref, mixed_ref, log_ref,
    even_ref, odd_ref, shared_ref, bar_ref, index_even, index_odd, index_shared, key_index_ref,
):
    mark_refs = (even_ref, odd_ref, shared_ref)
    index_refs = (index_even, index_odd, index_shared)

    @pl.when(pl.program_id(0) == 0)
    def _():
        prepare(meta_ref, mark_refs, bar_ref, index_refs, key_index_ref)

    rows = q_ref.shape[0]
    images = rows - TEXT
    q, k, v = q_ref[...], k_ref[...], v_ref[...]
    offsets = bucket(meta_ref[TEXT:, 2:3] - rows_ref[2:3, TEXT:])
    tile = 256
    heads = []
    for parity in range(2):
        table_row = table_ref[pl.ds(2 * pl.program_id(0) + parity, 1), :]
        wide = widened(
            parity, q, k, table_row, mark_refs, bar_ref, index_refs, key_index_ref, None
        )
        heads.append(wide + (image_bias(table_row, offsets),))

    def scored(parity, start):
        q_text, q_image, k_text, k_image, bias = heads[parity]
        here = slice(start, start + tile)
        on_image = dot_nt(q_image[here], k_image)
        if start >= TEXT:
            on_image = on_image + bias[start - TEXT : start - TEXT + tile]
        return dot_nt(q_text[here], k_text), on_image

    spots = [(parity, start) for parity in range(2) for start in range(0, rows, tile)]
    outs = ([], [])
    logs = ([], [])
    following = scored(*spots[0])
    for index, (parity, start) in enumerate(spots):
        on_text, on_image = following
        if index + 1 < len(spots):
            following = scored(*spots[index + 1])
        top = jnp.maximum(
            jnp.max(on_text, axis=1, keepdims=True), jnp.max(on_image, axis=1, keepdims=True)
        )
        on_text = jnp.exp(on_text - top)
        on_image = jnp.exp(on_image - top)
        total = jnp.sum(on_text, axis=1, keepdims=True) + jnp.sum(on_image, axis=1, keepdims=True)
        out = dot_nn(on_text.astype(BF), v[:TEXT]) + dot_nn(on_image.astype(BF), v[TEXT:])
        outs[parity].append(out / total)
        logs[parity].append(jnp.broadcast_to(top + jnp.log(total), (tile, LANES)))
    parts = [
        (jnp.concatenate(outs[parity], axis=0), jnp.concatenate(logs[parity], axis=0))
        for parity in range(2)
    ]
    lane = lax.broadcasted_iota(jnp.int32, (rows, LANES), 1)
    mixed_ref[...] = jnp.where(lane < HEAD, parts[0][0], parts[1][0])
    log_ref[0] = jnp.where(lane < HEAD, parts[0][1], parts[1][1])


def static_scratch(rows):
    return [
        pltpu.VMEM((rows, LANES), BF),
        pltpu.VMEM((rows, LANES), BF),
        pltpu.VMEM((rows, LANES), BF),
        pltpu.VMEM((rows, LANES), F32),
        pltpu.VMEM((rows, LANES), jnp.int32),
        pltpu.VMEM((rows, LANES), jnp.int32),
        pltpu.VMEM((rows, LANES), jnp.int32),
        pltpu.VMEM((rows - TEXT, LANES), jnp.int32),
    ]


def attention_forward(meta_columns, meta_rows, table_rows, projected, width):
    rows = projected.shape[0]
    pairs = width // LANES

    def block(part):
        return pl.BlockSpec((rows, LANES), lambda p: (0, part * pairs + p))

    whole = lambda shape: pl.BlockSpec(shape, lambda p: (0,) * len(shape))
    return pl.pallas_call(
        forward_kernel,
        grid=(pairs,),
        in_specs=[
            whole(meta_columns.shape),
            whole(meta_rows.shape),
            whole(table_rows.shape),
            block(0), block(1), block(2),
        ],
        out_specs=[
            pl.BlockSpec((rows, LANES), lambda p: (0, p)),
            pl.BlockSpec((1, rows, LANES), lambda p: (p, 0, 0)),
        ],
        out_shape=[
            jax.ShapeDtypeStruct((rows, width), F32),
            jax.ShapeDtypeStruct((pairs, rows, LANES), F32),
        ],
        scratch_shapes=static_scratch(rows),
        compiler_params=pltpu.CompilerParams(vmem_limit_bytes=32 * 1024 * 1024),
        name="attention_forward",
    )(meta_columns, meta_rows, table_rows, projected, projected, projected)


def skewed(block):
    size = block.shape[0]
    lane = lax.broadcasted_iota(jnp.int32, (size, LANES), 1)
    row = lax.broadcasted_iota(jnp.int32, (size, LANES), 0)
    turned = jnp.take_along_axis(
        block, (lane + row) & (LANES - 1), axis=1, mode="promise_in_bounds"
    )
    straight = lane + row < LANES
    above = jnp.sum(jnp.where(straight, turned, 0.0), axis=0, keepdims=True)
    below = jnp.sum(jnp.where(straight, 0.0, turned), axis=0, keepdims=True)
    return above, below


def transposed(array):
    return jnp.transpose(array.astype(F32)).astype(array.dtype)


def static_prepare(meta_ref, static):
    (even_ref, odd_ref, shared_ref, bar_ref, index_even, index_odd, index_shared, key_index_ref,
     even_t, odd_t, shared_t) = static
    mark_refs = (even_ref, odd_ref, shared_ref)
    prepare(meta_ref, mark_refs, bar_ref, (index_even, index_odd, index_shared), key_index_ref)
    for ref, turned in zip(mark_refs, (even_t, odd_t, shared_t)):
        turned[...] = transposed(ref[...])


def head_back(
    parity, pair, meta_ref, rows_ref, table_ref, q_ref, k_ref, v_ref, mixed_ref, grad_ref, log_ref,
    static, d_query, d_key, d_value, diag_ref,
):
    (even_ref, odd_ref, shared_ref, bar_ref, index_even, index_odd, index_shared, key_index_ref,
     even_t, odd_t, shared_t) = static
    mark_refs = (even_ref, odd_ref, shared_ref)
    index_refs = (index_even, index_odd, index_shared)
    turned_refs = (even_t, odd_t, shared_t)
    rows = q_ref.shape[0]
    images = rows - TEXT
    tile = 256
    q, k, v, grad = q_ref[...], k_ref[...], v_ref[...], grad_ref[...]
    lane = lax.broadcasted_iota(jnp.int32, (rows, LANES), 1)
    products = grad.astype(F32) * mixed_ref[...].astype(F32)
    k_turned = transposed(k)
    offsets = bucket(rows_ref[2:3, TEXT:] - meta_ref[TEXT:, 2:3])
    is_image = rows_ref[1:2, TEXT:] > 0
    own = (lane < HEAD) if parity == 0 else (lane >= HEAD)
    spare = HEAD if parity == 0 else 0
    table_row = table_ref[pl.ds(2 * pair + parity, 1), :]
    logs = log_ref[0, :, parity * HEAD : parity * HEAD + 1]
    q_text, q_image, k_text, k_image = widened(
        parity, q, k, table_row, mark_refs, bar_ref, index_refs, key_index_ref, logs
    )
    bias = image_bias(table_row, offsets)
    delta = jnp.sum(jnp.where(own, products, 0.0), axis=1, keepdims=True)
    high = delta.astype(BF).astype(F32)
    middle = (delta - high).astype(BF).astype(F32)
    lowest = delta - high - middle
    grad_wide = jnp.where(
        own,
        grad.astype(F32),
        jnp.where(
            lane == spare,
            -high,
            jnp.where(lane == spare + 1, -middle, jnp.where(lane == spare + 2, -lowest, 0.0)),
        ),
    ).astype(BF)
    v_wide = jnp.where(
        own, v.astype(F32), jnp.where(between(lane, spare, spare + 3), 1.0, 0.0)
    ).astype(BF)
    q_marked = jnp.concatenate(
        [
            jnp.where(own, q.astype(F32) * 0.125, mark_refs[parity][...].astype(F32)).astype(BF),
            shared_ref[...],
        ],
        axis=1,
    )
    dq = jnp.zeros((HEAD, rows), F32)
    dks = []
    dvs = []
    first_sum = jnp.zeros((LANES, LANES), F32)
    second_sum = jnp.zeros((LANES, LANES), F32)
    text_image = jnp.zeros((LANES, images), F32)
    def scored(start):
        here = slice(start, start + tile)
        if start < TEXT:
            scores = dot_nt(k_text[here], q_text)
        else:
            scores = dot_nt(k_image[start - TEXT : start - TEXT + tile], q_image)
            scores = jnp.concatenate([scores[:, :TEXT], scores[:, TEXT:] + bias], axis=1)
        return scores, dot_nt(v_wide[here], grad_wide)

    following = scored(0)
    for start in range(0, rows, tile):
        here = slice(start, start + tile)
        scores, prob_grad = following
        if start + tile < rows:
            following = scored(start + tile)
        soft = jnp.exp(scores)
        score_grad = soft * prob_grad
        low = score_grad.astype(BF)
        dvs.append(dot_nn(soft.astype(BF), grad))
        wide = dot_nn(low, q_marked)
        dks.append(wide[:, :LANES])
        dq = dq + dot_nn(k_turned[parity * HEAD : parity * HEAD + HEAD, here], low)
        rounded = wide.astype(BF)
        first_sum = first_sum + dot_nn(turned_refs[parity][:, here], rounded[:, :LANES])
        second_sum = second_sum + dot_nn(shared_t[:, here], rounded[:, LANES:])
        if start < TEXT:
            text_image = text_image + dot_nn(shared_t[:, here], low[:, TEXT:])
        else:
            by_position = wide[:, LANES:]
            on_image = score_grad[:, TEXT:]
    small = lax.broadcasted_iota(jnp.int32, (LANES, LANES), 1)
    small_row = lax.broadcasted_iota(jnp.int32, (LANES, LANES), 0)
    x0 = HEAD if parity == 0 else 0
    x_block = jnp.where(
        between(small, x0, x0 + COORD) & between(small_row, x0, x0 + COORD), first_sum, 0.0
    )
    y_block = jnp.where(
        between(small, Y0, Y0 + COORD) & between(small_row, Y0, Y0 + COORD), second_sum, 0.0
    )
    p_block = jnp.where((small < POS) & (small_row < POS), second_sum, 0.0)
    wide_lane = lax.broadcasted_iota(jnp.int32, (images, images), 1)
    outside = jnp.sum(jnp.where(is_image, 0.0, on_image), axis=1, keepdims=True)
    pairs = jnp.where(is_image, on_image, 0.0) + jnp.where(wide_lane == 0, outside, 0.0)
    outside_text = jnp.sum(jnp.where(is_image, 0.0, text_image), axis=1, keepdims=True)
    text_lane = lax.broadcasted_iota(jnp.int32, (LANES, images), 1)
    text_row = lax.broadcasted_iota(jnp.int32, (LANES, images), 0)
    text_image = jnp.where(is_image, text_image, 0.0) + jnp.where(
        text_lane == 0, outside_text, 0.0
    )
    text_image = jnp.where(text_row < POS, text_image, 0.0)
    first_lane = lax.broadcasted_iota(jnp.int32, (images, LANES), 1)
    left = pairs[:, :LANES] + jnp.where(first_lane < POS, by_position, 0.0)
    right = pairs[:, LANES:]
    a00, b00 = skewed(left[:LANES] + text_image[:, :LANES] + p_block)
    a01, b01 = skewed(right[:LANES] + text_image[:, LANES:])
    a10, b10 = skewed(left[LANES:])
    a11, b11 = skewed(right[LANES:])
    ax, bx = skewed(x_block)
    ay, by = skewed(y_block)
    diag_ref[2 * pair + parity] = jnp.concatenate(
        [b10, b00 + b11 + a10, a00 + a11 + b01, a01, bx, ax, by, ay], axis=0
    )
    empty = jnp.zeros_like(dq)
    both = [dq * 0.125, empty] if parity == 0 else [empty, dq * 0.125]
    results = (
        (d_query, jnp.transpose(jnp.concatenate(both, axis=0))),
        (d_key, jnp.concatenate(dks, axis=0)),
        (d_value, jnp.concatenate(dvs, axis=0)),
    )
    for ref, value in results:
        if parity == 1:
            value = jnp.where(own, value, ref[pair].astype(F32))
        ref[pair] = value.astype(BF)


MESH = pl.DeviceIdType.MESH
VMEM = pl.BlockSpec(memory_space=pltpu.VMEM)
HBM = pl.BlockSpec(memory_space=pltpu.HBM)
MIB = 1024 * 1024


def remote(src, dst, send, receive, device):
    return pltpu.make_async_remote_copy(
        src_ref=src, dst_ref=dst, send_sem=send, recv_sem=receive, device_id=device,
        device_id_type=MESH,
    )


def project_kernel(
    layer_ref, weight_hbm, *refs,
):
    small_hbm, refs = refs[:10], refs[10:]
    (item_ref, projected_out, columns_ref, rows_ref, table_ref,
     projected_ref, weight_ref, meta_send, bias_ref, sems, load_sems, store_sems), small = (
        refs[:12], refs[12:],
    )
    (segment_ref, mask_ref, position_ref, across_ref, down_ref, query_bias_ref, value_bias_ref,
     text_ref, horiz_ref, vert_ref) = small
    mine = lax.axis_index("seq")
    partner = (1 - mine, lax.axis_index("dp"))
    count, width = layer_ref.shape[1:]
    own = pl.ds(pl.multiple_of(mine * count, LANES), count)
    loads = [
        pltpu.make_async_copy(source, target, load_sems.at[index])
        for index, (source, target) in enumerate(
            list(zip(small_hbm, small))
            + [(layer_ref.at[mine], item_ref.at[own]), (weight_hbm, weight_ref)]
        )
    ]
    for load in loads:
        load.start()
    barrier = pltpu.get_barrier_semaphore()
    pl.semaphore_signal(barrier, inc=1, device_id=partner, device_id_type=MESH)
    pl.semaphore_wait(barrier, 1)
    pieces = count // LANES
    rows_out = [
        remote(
            layer_ref.at[1 - mine, pl.ds(piece * LANES, LANES)],
            item_ref.at[pl.ds(pl.multiple_of(mine * count + piece * LANES, LANES), LANES)],
            sems.at[0, piece], sems.at[1, piece], partner,
        )
        for piece in range(pieces)
    ]
    for copy in rows_out:
        copy.start()
    for load in loads[:-2]:
        load.wait()

    fields = (segment_ref, mask_ref, position_ref, across_ref, down_ref)
    blocks = [
        jnp.concatenate(
            [field[item : item + 1, :] for field in fields] + [jnp.zeros((3, count), jnp.int32)],
            axis=0,
        )
        for item in range(2)
    ]
    meta_send[...] = jnp.where(mine == 0, blocks[1], blocks[0])
    meta_out = remote(
        meta_send, rows_ref.at[:, own], sems.at[0, pieces], sems.at[1, pieces], partner
    )
    meta_out.start()
    rows_ref[:, own] = jnp.where(mine == 0, blocks[0], blocks[1])
    bias_ref[:, :width] = query_bias_ref[...].astype(F32).reshape(1, width)
    bias_ref[:, width : 2 * width] = jnp.zeros((1, width), F32)
    bias_ref[:, 2 * width :] = value_bias_ref[...].astype(F32).reshape(1, width)
    heads, levels = text_ref.shape
    spot = lax.broadcasted_iota(jnp.int32, (levels, LANES), 1)
    level = lax.broadcasted_iota(jnp.int32, (levels, LANES), 0)
    table = jnp.zeros((heads, LANES), F32)
    for source, begin in ((text_ref, 0), (horiz_ref, X_TABLE), (vert_ref, Y_TABLE)):
        table = table + dot_nn(source[...], (spot == level + begin).astype(BF))
    table_ref[...] = jnp.concatenate([table, jnp.zeros((16 - heads, LANES), F32)], axis=0)

    def project(there):
        step = 256

        def body(index, carry):
            columns = pl.ds(pl.multiple_of(index * step, step), step)
            product = dot_nn(item_ref[there], weight_ref[:, columns])
            projected_ref[there, columns] = (product + bias_ref[:, columns]).astype(BF)
            return carry

        lax.fori_loop(0, 3 * width // step, body, 0)

    def stored(index, there):
        return pltpu.make_async_copy(
            projected_ref.at[there], projected_out.at[there], store_sems.at[index]
        )

    for load in loads[-2:]:
        load.wait()
    project(own)
    stored(0, own).start()
    for piece in range(pieces):
        rows_out[piece].wait()
        there = pl.ds(pl.multiple_of((1 - mine) * count + piece * LANES, LANES), LANES)
        project(there)
        stored(1 + piece, there).start()
    meta_out.wait()
    meta = rows_ref[...].astype(F32)
    tall = jnp.concatenate([meta, jnp.zeros((LANES - 8, meta.shape[1]), F32)], axis=0)
    columns_ref[...] = jnp.transpose(tall).astype(jnp.int32)
    stored(0, own).wait()
    for piece in range(pieces):
        there = pl.ds(pl.multiple_of((1 - mine) * count + piece * LANES, LANES), LANES)
        stored(1 + piece, there).wait()


def projected_item(layer_in, fields, qkv_weight, query_bias, value_bias, tables):
    rows = 2 * layer_in.shape[1]
    width = layer_in.shape[2]
    pieces = rows // 2 // LANES
    small = list(fields) + [query_bias, value_bias] + [t.T for t in tables]
    return pl.pallas_call(
        project_kernel,
        in_specs=[HBM] * (2 + len(small)),
        out_specs=[VMEM, HBM, VMEM, VMEM, VMEM],
        out_shape=[
            jax.ShapeDtypeStruct((rows, width), BF),
            jax.ShapeDtypeStruct((rows, 3 * width), BF),
            jax.ShapeDtypeStruct((rows, LANES), jnp.int32),
            jax.ShapeDtypeStruct((8, rows), jnp.int32),
            jax.ShapeDtypeStruct((16, LANES), F32),
        ],
        scratch_shapes=[
            pltpu.VMEM((rows, 3 * width), BF),
            pltpu.VMEM((width, 3 * width), BF),
            pltpu.VMEM((8, rows // 2), jnp.int32),
            pltpu.VMEM((1, 3 * width), F32),
            pltpu.SemaphoreType.DMA((2, pieces + 1)),
            pltpu.SemaphoreType.DMA((len(small) + 2,)),
            pltpu.SemaphoreType.DMA((pieces + 1,)),
        ]
        + [pltpu.VMEM(array.shape, array.dtype) for array in small],
        compiler_params=pltpu.CompilerParams(
            collective_id=1, has_side_effects=True, vmem_limit_bytes=24 * MIB
        ),
        name="projected_item",
    )(layer_in, qkv_weight, *small)


EPSILON = 1e-05
TILE = 256


def vector(ref):
    return ref[...].astype(F32).reshape(1, ref.shape[0])


def gelu_and_slope(x):
    bell = jnp.exp(-0.5 * x * x)
    t = 1.0 / (1.0 + 0.23164188826 * jnp.abs(x))
    series = t * (
        0.127414796
        + t * (-0.142248368 + t * (0.7107068705 + t * (-0.7265760135 + t * 0.5307027145)))
    )
    tail = bell * series
    below = jnp.where(x >= 0.0, 1.0 - tail, tail)
    return x * below, below + x * (0.3989422804014327 * bell)


def row_mean(block):
    return jnp.mean(block, axis=1, keepdims=True)


def normalized(hidden):
    center = hidden - row_mean(hidden)
    scale = lax.rsqrt(row_mean(center * center) + EPSILON)
    return center * scale, scale


def norm_pulled(grad, unit, scale):
    return scale * (grad - row_mean(grad) - unit * row_mean(grad * unit))


def column_sum(block):
    return jnp.sum(block, axis=0, keepdims=True)


def feed_kernel(
    item_ref, mixed_ref, cotangent_ref, out_weight_ref, up_ref, down_ref, *refs,
):
    vectors_hbm, refs = refs[:7], refs[7:]
    (layer_out, d_hidden_ref, d_mixed_ref, grad_out_ref, grad_down_ref, grad_up_ref, small_ref,
     layer_ref, cotangent_all, active, slope, unit, scale_ref, normed, normed_t, total, d_branch, d_branch_t,
     sems, load_sems) = refs[:20]
    vectors = refs[20:]
    (out_bias_ref, attn_gain_ref, attn_shift_ref, up_bias_ref, down_bias_ref, ffn_gain_ref,
     ffn_shift_ref) = vectors
    step = pl.program_id(0)
    blocks = pl.num_programs(0) // 2
    rows, width = item_ref.shape
    count = rows // 2
    mine = lax.axis_index("seq")
    partner = (1 - mine, lax.axis_index("dp"))
    own = pl.ds(pl.multiple_of(mine * count, LANES), count)
    tiles = rows // TILE

    def sent():
        return remote(
            cotangent_ref.at[1 - mine], cotangent_all.at[own], sems.at[0], sems.at[1], partner
        )

    def returned():
        theirs = pl.ds(pl.multiple_of((1 - mine) * count, LANES), count)
        return [
            pltpu.make_async_copy(layer_ref.at[own], layer_out.at[mine], load_sems.at[8]),
            remote(
                layer_ref.at[theirs], layer_out.at[mine], sems.at[2], sems.at[3], partner
            ),
        ]

    def loads():
        copies = list(zip(vectors_hbm, vectors)) + [(cotangent_ref.at[mine], cotangent_all.at[own])]
        return [
            pltpu.make_async_copy(source, target, load_sems.at[index])
            for index, (source, target) in enumerate(copies)
        ]

    def over_tiles(size, body, carry):
        def run(index, state):
            return body(pl.ds(pl.multiple_of(index * size, size), size), state)

        return lax.fori_loop(0, rows // size, run, carry)

    @pl.when(step == 0)
    def _():
        for load in loads():
            load.start()
        barrier = pltpu.get_barrier_semaphore()
        pl.semaphore_signal(barrier, inc=1, device_id=partner, device_id_type=MESH)
        pl.semaphore_wait(barrier, 1)
        sent().start()
        small_ref[...] = jnp.zeros_like(small_ref)
        for load in loads():
            load.wait()
        out_bias, gain, shift = vector(out_bias_ref), vector(attn_gain_ref), vector(attn_shift_ref)

        def tile(there, carry):
            attn = dot_nn(mixed_ref[there].astype(BF), out_weight_ref[...]) + out_bias
            standard, scale = normalized(item_ref[there].astype(F32) + attn)
            unit[there] = standard
            scale_ref[there] = jnp.broadcast_to(scale, (scale.shape[0], LANES))
            result = standard * gain + shift
            normed[there] = result.astype(BF)
            normed_t[:, there] = jnp.transpose(result).astype(BF)
            return carry

        over_tiles(TILE, tile, 0)
        total[...] = jnp.zeros_like(total)

    @pl.when(step < blocks)
    def _():
        columns = [slice(begin, begin + TILE) for begin in range(0, width, TILE)]
        low = normed[...]
        following = dot_nn(low, up_ref[:, columns[0]])
        values = []
        for index, here in enumerate(columns):
            product = following
            if index + 1 < len(columns):
                following = dot_nn(low, up_ref[:, columns[index + 1]])
            bias = up_bias_ref[pl.ds(pl.multiple_of(step * width + here.start, LANES), TILE)]
            value, grade = gelu_and_slope(product + bias.astype(F32).reshape(1, TILE))
            values.append(value.astype(BF))
            active[step, :, here] = values[-1]
            slope[step, :, here] = grade
        values = jnp.concatenate(values, axis=1)
        for here in columns:
            total[:, here] += dot_nn(values, down_ref[:, here])

    @pl.when(step == blocks)
    def _():
        sent().wait()
        gain, shift, bias = vector(ffn_gain_ref), vector(ffn_shift_ref), vector(down_bias_ref)
        first_gain, first_shift = vector(attn_gain_ref), vector(attn_shift_ref)

        def tile(there, sums):
            hidden = unit[there] * first_gain + first_shift + (total[there] + bias)
            standard, scale = normalized(hidden)
            layer_ref[there] = (standard * gain + shift).astype(BF)
            cotangent = cotangent_all[there].astype(F32)
            pulled = norm_pulled(cotangent * gain, standard, scale)
            total[there] = pulled
            low = pulled.astype(BF)
            d_branch[there] = low
            return (
                sums[0] + column_sum(low.astype(F32)),
                sums[1] + column_sum(cotangent * standard),
                sums[2] + column_sum(cotangent),
            )

        zero = jnp.zeros((1, width), F32)
        sums = over_tiles(64, tile, (zero, zero, zero))
        for row, value in zip((5, 6, 7), sums):
            small_ref[row : row + 1] = value

        for copy in returned():
            copy.start()

        def turn(there, carry):
            d_branch_t[:, there] = jnp.transpose(d_branch[there].astype(F32)).astype(BF)
            return carry

        over_tiles(TILE, turn, 0)

    @pl.when(step >= blocks)
    def _():
        block = step - blocks

        columns = [slice(begin, begin + TILE) for begin in range(0, width, TILE)]
        branch = d_branch[...]
        turned = d_branch_t[...]
        following = dot_nt(branch, down_ref[columns[0]])
        values = []
        for index, here in enumerate(columns):
            product = following
            if index + 1 < len(columns):
                following = dot_nt(branch, down_ref[columns[index + 1]])
            grad_down_ref[:, here] = dot_nn(turned, active[block, :, here]).astype(BF)
            d_up = (product * slope[block, :, here]).astype(BF)
            small_ref[pl.ds(8 + block, 1), here] = column_sum(d_up.astype(F32))
            values.append(d_up)
        values = jnp.concatenate(values, axis=1)
        turned = normed_t[...]
        for here in columns:
            grad_up_ref[:, here] = dot_nn(turned, values[:, here]).astype(BF)
            total[:, here] += dot_nt(values, up_ref[here])

    @pl.when(step == 2 * blocks - 1)
    def _():
        gain = vector(attn_gain_ref)

        def tile(there, sums):
            d_normed = total[there]
            standard = unit[there]
            d_hidden = norm_pulled(d_normed * gain, standard, scale_ref[there, :1])
            d_hidden_ref[there] = d_hidden
            low = d_hidden.astype(BF)
            d_branch[there] = low
            return (
                sums[0] + column_sum(low.astype(F32)),
                sums[1] + column_sum(d_normed * standard),
                sums[2] + column_sum(d_normed),
            )

        zero = jnp.zeros((1, width), F32)
        sums = over_tiles(64, tile, (zero, zero, zero))
        for row, value in zip((2, 3, 4), sums):
            small_ref[row : row + 1] = value

        def turn(there, carry):
            normed_t[:, there] = jnp.transpose(mixed_ref[there]).astype(BF)
            return carry

        over_tiles(TILE, turn, 0)

        for begin in range(0, width, TILE):
            here = slice(begin, begin + TILE)
            d_mixed_ref[:, here] = dot_nt(d_branch[...], out_weight_ref[here]).astype(BF)
            grad_out_ref[:, here] = dot_nn(normed_t[...], d_branch[:, here]).astype(BF)

        for copy in returned():
            copy.wait()


def fed_forward_and_back(
    item, mixed, cotangent, out_weight, up_weight, down_weight, vectors,
):
    rows, width = item.shape
    blocks = up_weight.shape[1] // width
    whole = pl.BlockSpec(memory_space=pltpu.VMEM)
    square = lambda kind: jax.ShapeDtypeStruct((rows, width), kind)
    later = lambda i: jnp.maximum(i - blocks, 0)
    return pl.pallas_call(
        feed_kernel,
        grid=(2 * blocks,),
        in_specs=[whole, whole, HBM, whole]
        + [
            pl.BlockSpec((width, width), lambda i: (0, lax.rem(i, blocks))),
            pl.BlockSpec((width, width), lambda i: (lax.rem(i, blocks), 0)),
        ]
        + [HBM] * 7,
        out_specs=[HBM] + [whole] * 3
        + [
            pl.BlockSpec((width, width), lambda i: (later(i), 0)),
            pl.BlockSpec((width, width), lambda i: (later(i), 0)),
            whole,
        ],
        out_shape=[
            jax.ShapeDtypeStruct((2, rows // 2, width), BF), square(F32), square(BF),
            jax.ShapeDtypeStruct((width, width), BF),
            jax.ShapeDtypeStruct((blocks * width, width), BF),
            jax.ShapeDtypeStruct((blocks * width, width), BF),
            jax.ShapeDtypeStruct((16, width), F32),
        ],
        scratch_shapes=[
            pltpu.VMEM((rows, width), BF),
            pltpu.VMEM((rows, width), BF),
            pltpu.VMEM((blocks, rows, width), BF),
            pltpu.VMEM((blocks, rows, width), F32),
            pltpu.VMEM((rows, width), F32),
            pltpu.VMEM((rows, LANES), F32),
            pltpu.VMEM((rows, width), BF),
            pltpu.VMEM((width, rows), BF),
            pltpu.VMEM((rows, width), F32),
            pltpu.VMEM((rows, width), BF),
            pltpu.VMEM((width, rows), BF),
            pltpu.SemaphoreType.DMA((4,)),
            pltpu.SemaphoreType.DMA((9,)),
        ]
        + [pltpu.VMEM(vector.shape, vector.dtype) for vector in vectors],
        compiler_params=pltpu.CompilerParams(
            collective_id=2, has_side_effects=True, vmem_limit_bytes=60 * MIB
        ),
        name="feed_forward",
    )(item, mixed, cotangent, out_weight, up_weight, down_weight, *vectors)


SLOTS = 4


def finish_kernel(
    summed_ref, input_hbm, small_ref, diagonal_ref,
    down_ref, up_ref, out_ref, qkv_ref, input_ref, *refs,
):
    singles, (blocks_in, slots, input_in, input_slot, in_sems, out_sems, item_sems) = (
        refs[:12], refs[12:],
    )
    blocks, width = blocks_in.shape[0], blocks_in.shape[2]
    hidden = down_ref.shape[0] // width

    def load(block):
        return pltpu.make_async_copy(
            summed_ref.at[pl.ds(block * width, width)], blocks_in.at[block], in_sems.at[block]
        )

    def stores(block):
        slot, sem = slots.at[block % SLOTS], out_sems.at[block % SLOTS]
        if block < hidden:
            targets = [(slot, down_ref.at[pl.ds(block * width, width)])]
        elif block < 2 * hidden:
            targets = [(slot, up_ref.at[:, pl.ds((block - hidden) * width, width)])]
        elif block == 2 * hidden:
            targets = [(slot, out_ref)]
        else:
            first = 2 * (block - 2 * hidden - 1)
            targets = [
                (
                    slot.at[:, pl.ds((3 * pair + part) * LANES, LANES)],
                    qkv_ref.at[:, pl.ds(part * width + (first + pair) * LANES, LANES)],
                )
                for pair in range(2) for part in range(3)
            ]
        return [
            pltpu.make_async_copy(source, target, sem.at[index])
            for index, (source, target) in enumerate(targets)
        ]

    load_input = pltpu.make_async_copy(input_hbm, input_in, item_sems.at[0])
    store_input = pltpu.make_async_copy(input_slot, input_ref, item_sems.at[1])
    for block in range(blocks):
        load(block).start()
    load_input.start()
    for block in range(blocks):
        load(block).wait()
        if block >= SLOTS:
            for copy in stores(block - SLOTS):
                copy.wait()
        piece = blocks_in[block].astype(F32)
        slots[block % SLOTS] = jnp.transpose(piece) if block < hidden else piece
        for copy in stores(block):
            copy.start()
    load_input.wait()
    input_slot[...] = input_in[...].astype(F32)
    store_input.start()
    for row in range(8):
        singles[row][...] = small_ref[row]
    for row in range(hidden):
        singles[8][row * width : row * width + width] = small_ref[8 + row]
    heads, levels = singles[9].shape
    diagonals = diagonal_ref[...]
    level = lax.broadcasted_iota(jnp.int32, (LANES, LANES), 1)
    lane = lax.broadcasted_iota(jnp.int32, (LANES, LANES), 0)
    for table, (first, size, skip) in enumerate(((0, 4, 0), (4, 2, 1), (6, 2, 1))):
        total = jnp.zeros((heads, LANES), F32)
        for row in range(size):
            distance = lane + LANES * (row + skip - 2)
            chosen = (bucket(distance) == level).astype(F32)
            total = total + jnp.dot(
                diagonals[:, first + row, :], chosen, preferred_element_type=F32,
                precision=lax.Precision.HIGHEST,
            )
        singles[9 + table][...] = total[:, :levels]
    for block in range(blocks - SLOTS, blocks):
        for copy in stores(block):
            copy.wait()
    store_input.wait()


def finished(summed, grad_input, small, diagonals, hidden, levels):
    width = summed.shape[1]
    heads = diagonals.shape[0]
    blocks = summed.shape[0] // width
    single = jax.ShapeDtypeStruct((width,), F32)
    table = jax.ShapeDtypeStruct((heads, levels), F32)
    dma = pltpu.SemaphoreType.DMA
    return pl.pallas_call(
        finish_kernel,
        in_specs=[HBM, HBM, VMEM, VMEM],
        out_specs=[HBM] * 5 + [VMEM] * 12,
        out_shape=[
            jax.ShapeDtypeStruct((hidden, width), F32),
            jax.ShapeDtypeStruct((width, hidden), F32),
            jax.ShapeDtypeStruct((width, width), F32),
            jax.ShapeDtypeStruct((width, 3 * width), F32),
            jax.ShapeDtypeStruct(grad_input.shape, F32),
        ]
        + [single] * 8
        + [jax.ShapeDtypeStruct((hidden,), F32)]
        + [table] * 3,
        scratch_shapes=[
            pltpu.VMEM((blocks, width, width), BF),
            pltpu.VMEM((SLOTS, width, width), F32),
            pltpu.VMEM(grad_input.shape, BF),
            pltpu.VMEM(grad_input.shape, F32),
            dma((blocks,)),
            dma((SLOTS, 6)),
            dma((2,)),
        ],
        compiler_params=pltpu.CompilerParams(vmem_limit_bytes=56 * MIB),
        name="finished",
    )(summed, grad_input, small, diagonals)


PIECE = 16


def hop_names(depth):
    names = ["x", "y"]
    reach = 1
    while reach < depth:
        names.append(f"z{reach}")
        reach *= 2
    return names


def route(depth, letters):
    names = hop_names(depth)
    line = {"a": names[2:3], "b": names[3:]}
    return [name for letter in letters for name in line.get(letter, [letter])]


class Place:
    def __init__(self, depth):
        place = lax.axis_index("dp")
        x = lax.axis_index("seq")
        core = lax.rem(place, 2)
        y = lax.rem(lax.div(place, 2), 2)
        z = lax.rem(lax.div(place, 4), depth)
        group = lax.div(place, 4 * depth)
        at = lambda sx, sc, sy, sz: (sx, (group * depth + sz) * 4 + sy * 2 + sc)
        self.bits = {"core": core, "x": x, "y": y}
        self.partners = {
            "core": at(x, 1 - core, y, z), "x": at(1 - x, core, y, z), "y": at(x, core, 1 - y, z),
        }
        reach = 1
        while reach < depth:
            up = lax.rem(lax.div(z, reach), 2)
            self.bits[f"z{reach}"] = up
            self.partners[f"z{reach}"] = at(x, core, y, z + reach - 2 * reach * up)
            reach *= 2

    def greet(self):
        barrier = pltpu.get_barrier_semaphore()
        for device in self.partners.values():
            pl.semaphore_signal(barrier, inc=1, device_id=device, device_id_type=MESH)
        pl.semaphore_wait(barrier, len(self.partners))


class Chunk:
    def __init__(self, place, depth, source, out_ref, offset, spot, scratch):
        _, self.begin, rows, first, columns, _, paths, _ = spot
        self.place, self.source, self.columns = place, source, pl.ds(first, columns)
        self.out_ref, self.out_begin = out_ref, offset + self.begin
        self.half, self.quarter = rows // 2, rows // 4
        self.routes = [route(depth, letters) for letters in paths.split()]
        self.hops = len(self.routes[0])
        self.stages = 2 * self.hops + 3
        self.work, self.fresh, *self.landing, self.sends, self.receives, self.locals = scratch

    def aligned(self, value):
        return pl.multiple_of(value, PIECE)

    def size(self, hop):
        return self.quarter >> (hop + 1)

    def base(self, part, hops):
        start = part * self.quarter
        for hop in range(hops):
            start = start + self.place.bits[self.routes[part][hop]] * self.size(hop)
        return start

    def across(self, part, hop):
        bit = self.place.bits[self.routes[part][hop]]
        return self.base(part, hop) + (1 - bit) * self.size(hop)

    def partner(self, part, hop):
        return self.place.partners[self.routes[part][hop]]

    def out(self, begin, size, core=None):
        core = self.place.bits["core"] if core is None else core
        return self.out_ref.at[
            pl.ds(self.aligned(self.out_begin + core * self.half + begin), size), self.columns
        ]

    def copy(self, index, source, target, device):
        return remote(source, target, self.sends.at[index], self.receives.at[index], device)

    def pair_down(self):
        core = self.place.bits["core"]
        at = lambda c: self.source.at[
            pl.ds(self.aligned(self.begin + c * self.half), self.half), self.columns
        ]
        return [
            self.copy(0, at(1 - core), self.fresh, self.place.partners["core"]),
            pltpu.make_async_copy(at(core), self.work, self.locals.at[0]),
        ]

    def pair_up(self, arriving):
        core = self.place.bits["core"]
        target = self.out(0, self.half, 1 - core if arriving else core)
        return [self.copy(1, self.out(0, self.half), target, self.place.partners["core"])]

    def down(self, hop):
        return [
            self.copy(
                2 + 2 * hop + part,
                self.work.at[pl.ds(self.aligned(self.across(part, hop)), self.size(hop))],
                self.landing[hop].at[part], self.partner(part, hop),
            )
            for part in range(2)
        ]

    def kept(self):
        size = self.size(self.hops - 1)
        copies = []
        for part in range(2):
            begin = self.aligned(self.base(part, self.hops))
            copies.append(
                pltpu.make_async_copy(
                    self.work.at[pl.ds(begin, size)], self.out(begin, size),
                    self.locals.at[1 + part],
                )
            )
        return copies

    def up(self, hop, arriving):
        copies = []
        for part in range(2):
            mine = self.base(part, hop + 1)
            size = self.size(hop)
            if hop == self.hops - 1:
                source = self.work.at[pl.ds(self.aligned(mine), size)]
            else:
                source = self.out(mine, size)
            target = self.out(self.across(part, hop) if arriving else mine, size)
            index = 2 + 2 * self.hops + 2 * hop + part
            copies.append(self.copy(index, source, target, self.partner(part, hop)))
        return copies

    def add(self, begin, source, size):
        step = 64 if size % 64 == 0 else min(size, PIECE)

        def body(index, carry):
            offset = self.aligned(index * step)
            there = pl.ds(self.aligned(begin + offset), step)
            total = self.work[there].astype(F32) + source[pl.ds(offset, step)].astype(F32)
            self.work[there] = total.astype(BF)
            return carry

        lax.fori_loop(0, size // step, body, 0)

    def stage(self, number):
        hops = self.hops
        ended, started = [], []
        if number == 0:
            started = self.pair_down()
        elif number == 1:
            ended = self.pair_down()
            started = self.down(0)
        elif number <= hops:
            ended = self.down(number - 2)
            started = self.down(number - 1)
        elif number == hops + 1:
            ended = self.down(hops - 1)
            started = self.up(hops - 1, False) + self.kept()
        elif number <= 2 * hops:
            level = 2 * hops + 1 - number
            ended = self.up(level, True) + (self.kept() if level == hops - 1 else [])
            started = self.up(level - 1, False)
        elif number == 2 * hops + 1:
            ended = self.up(0, True)
            started = self.pair_up(False)
        else:
            ended = self.pair_up(True)
        for copy in ended:
            copy.wait()
        if number == 1:
            self.add(0, self.fresh, self.half)
        elif 2 <= number <= hops + 1:
            hop = number - 2
            for part in range(2):
                self.add(self.base(part, hop + 1), self.landing[hop].at[part], self.size(hop))
        for copy in started:
            copy.start()


def chunk_scratch(rows, width, depth):
    hops = len(hop_names(depth))
    dma = pltpu.SemaphoreType.DMA
    return (
        [pltpu.VMEM((rows // 2, width), BF)] * 2
        + [pltpu.VMEM((2, rows // 4 >> (hop + 1), width), BF) for hop in range(hops)]
        + [dma((2 + 4 * hops,)), dma((2 + 4 * hops,)), dma((3,))]
    )


def planned(chunks, work, depth, hop_count):
    latency, issue, link, pair = 2.5, 0.2, 100e3, 350e3
    free = {}
    now = 0.0

    def sent(name, rows, columns):
        nonlocal now
        now += issue
        row_bytes = 2 * columns
        share = {"core": [("core", rows * row_bytes / pair)]}.get(name)
        if share is None:
            time = 2 * rows * row_bytes / link
            share = [(name, time)]
            if name[0] == "z":
                reach = int(name[1:])
                share = [("z end", time), ("z middle", 0.0 if reach == 1 else reach * time)]
        end = now
        for lane, time in share:
            free[lane] = max(now, free.get(lane, 0.0)) + time
            end = max(end, free[lane])
        return end + latency

    chains = []
    for rows, columns, need, paths, _ in chunks:
        paths = [route(depth, letters) for letters in paths.split()]
        down = []
        size = rows // 4
        for hop in range(len(paths[0])):
            size //= 2
            down.append([(path[hop], size, columns) for path in paths])
        pair_step = [[("core", rows // 2, columns)]]
        chains.append((need, pair_step + down + down[::-1] + pair_step))
    chains.append((len(work), [[("core", 16, 768)]] * hop_count))
    position = [0] * len(chains)
    ready = [0.0] * len(chains)
    ranks = [chunk[4] for chunk in chunks] + [0]
    order = [[] for _ in range(len(work) + 1)]
    done = 0
    while True:
        open_ones = [
            (ranks[i], ready[i], i) for i, (need, chain) in enumerate(chains)
            if position[i] <= len(chain) and need <= done
        ]
        due = [entry for entry in open_ones if entry[1] <= now]
        if not due and done < len(work):
            now += work[done]
            done += 1
            continue
        if not open_ones:
            return order
        _, when, index = min(due) if due else min(open_ones, key=lambda entry: entry[1])
        now = max(now, when)
        chain = chains[index][1]
        stage = position[index]
        order[done].append((index, stage))
        if 0 < stage <= len(chain) // 2:
            now += 2e-6 * sum(rows * wide for _, rows, wide in chain[stage - 1])
        if stage < len(chain):
            ready[index] = max(sent(*entry) for entry in chain[stage])
        position[index] += 1


def last_kernel(
    depth, plan, orders, *refs,
):
    (meta_ref, rows_ref, table_ref, q_ref, k_ref, v_ref, mixed_ref, grad_ref, log_ref,
     small_ref, item_hbm, weight_hbm, d_hidden_hbm, grad_down_ref, grad_up_ref, grad_out_ref,
     out_ref, small_out, diagonal_out, input_out,
     *scratch) = refs
    static, scratch = scratch[:11], scratch[11:]
    (item_ref, weight_ref, total_ref, load_sems, d_query, d_key, d_value, item_t, tail, input_grad,
     small_in, diagonal_in, small_sems, item_sems, *scratch) = scratch
    place = Place(depth)
    step = pl.program_id(0)
    pairs = d_query.shape[0]
    rows, width = item_hbm.shape
    count = rows // 2
    x = place.bits["x"]
    sources = (grad_down_ref, grad_up_ref, tail)
    each = len(scratch) // len(plan)
    chunks = []
    for index, spot in enumerate(plan):
        offset = spot[0] * grad_down_ref.shape[0]
        chunks.append(
            Chunk(place, depth, sources[spot[0]], out_ref, offset, spot,
                  scratch[index * each : index * each + each])
        )
    hop_devices = list(place.partners.values())

    def loads():
        pairs_of = (
            (item_hbm, item_ref), (weight_hbm, weight_ref), (d_hidden_hbm, total_ref),
            (grad_out_ref, tail.at[pl.ds(0, width)]),
        )
        return [
            pltpu.make_async_copy(source, target, load_sems.at[index])
            for index, (source, target) in enumerate(pairs_of)
        ]

    def input_copies():
        return [
            pltpu.make_async_copy(
                input_grad.at[pl.ds(pl.multiple_of(x * count, LANES), count)], input_out.at[x],
                item_sems.at[0],
            ),
            remote(
                input_grad.at[pl.ds(pl.multiple_of((1 - x) * count, LANES), count)],
                input_out.at[x], item_sems.at[1], item_sems.at[2], place.partners["x"],
            ),
        ]

    def small_copies(hop):
        return [
            remote(source, landing.at[hop], small_sems.at[0, kind, hop],
                   small_sems.at[1, kind, hop], hop_devices[hop])
            for kind, (source, landing) in enumerate(
                ((small_out, small_in), (diagonal_out, diagonal_in))
            )
        ]

    def small_stage(hop):
        if hop > 0:
            for copy in small_copies(hop - 1):
                copy.wait()
            small_out[...] = small_out[...] + small_in[hop - 1]
            diagonal_out[...] = diagonal_out[...] + diagonal_in[hop - 1]
        if hop < len(hop_devices):
            for copy in small_copies(hop):
                copy.start()

    def perform(slot):
        for index, stage in orders[slot]:
            if index == len(chunks):
                small_stage(stage)
            else:
                chunks[index].stage(stage)

    @pl.when(step == 0)
    def _():
        place.greet()
        for copy in loads():
            copy.start()
        small_out[...] = small_ref[...]
        static_prepare(meta_ref, static)

    def slab(first):
        pieces = [
            (pair, part) for pair in (first, first + 1) for part in range(3)
        ]
        held = (d_query, d_key, d_value)
        base = width + first // 2 * width
        for left, right in zip(pieces[::2], pieces[1::2]):
            both = jnp.concatenate([held[part][pair] for pair, part in (left, right)], axis=1)
            weights = jnp.concatenate(
                [
                    weight_ref[:, part * width + pair * LANES : part * width + (pair + 1) * LANES]
                    for pair, part in (left, right)
                ],
                axis=1,
            )
            at = pieces.index(left) * LANES
            tail[base : base + width, at : at + 2 * LANES] = dot_nn(item_t[...], both).astype(BF)
            total_ref[...] += dot_nt(both, weights)
        for pair in (first, first + 1):
            columns = slice(pair * LANES, pair * LANES + LANES)
            small_out[0:1, columns] = column_sum(d_query[pair].astype(F32))
            small_out[1:2, columns] = column_sum(d_value[pair].astype(F32))

    @pl.when(step == 1)
    def _():
        for copy in loads():
            copy.wait()
        for tile in range(rows // TILE):
            there = slice(tile * TILE, tile * TILE + TILE)
            item_t[:, there] = jnp.transpose(item_ref[there].astype(F32)).astype(BF)

    for parity in range(2):
        for pair in range(pairs):
            @pl.when(step == pair)
            def _(pair=pair):
                perform(2 * pair + pair // 2 + parity)

        head_back(
            parity, step, meta_ref, rows_ref, table_ref, q_ref, k_ref, v_ref, mixed_ref,
            grad_ref, log_ref, static, d_query, d_key, d_value, diagonal_out,
        )

    for pair in range(1, pairs, 2):
        @pl.when(step == pair)
        def _(pair=pair):
            perform(2 * pair + 2 + pair // 2)
            slab(pair - 1)

    @pl.when(step == pairs - 1)
    def _():
        input_grad[...] = total_ref[...].astype(BF)
        for copy in input_copies():
            copy.start()
        perform(len(orders) - 1)
        for copy in input_copies():
            copy.wait()


def summed_with_attention_back(
    meta_columns, meta_rows, table_rows, projected, mixed, d_mixed, logs, item, qkv_weight,
    d_hidden, small, grad_down, grad_up, grad_out,
):
    size = lax.axis_size("dp")
    depth = 4 if size % 16 == 0 else size // 4
    rows, width = item.shape
    pairs = width // LANES
    hidden = grad_down.shape[0]
    hops = len(hop_names(depth)) + 1
    work = ([3.2] * 4 + [4.2]) * (pairs // 2)
    wide, slim = width // 2, width // 3
    plan = [
        (0, 0, 3072, 0, slim, 0, "xaby yabx", 0),
        (0, 0, 3072, slim, slim, 0, "xayb yxab", 0),
        (0, 0, 3072, 2 * slim, slim, 0, "yaxb xayb", 0),
        (1, 0, 2048, 0, width, 0, "yabx xyab", 1),
        (1, 2048, 1024, 0, width, 0, "abyx yaxb", 0),
        (2, 0, 1024, 0, wide, 5, "yabx xayb", 2),
        (2, 0, 1024, wide, wide, 5, "xyab yabx", 2),
        (2, 1024, 1024, 0, width, 10, "xyab yaxb", 1),
        (2, 2048, 1024, 0, wide, 15, "xayb yaxb", 2),
        (2, 2048, 1024, wide, wide, 15, "abyx yabx", 0),
    ]
    orders = planned([(spot[2],) + spot[4:] for spot in plan], work, depth, hops)

    def block(part):
        return pl.BlockSpec((rows, LANES), lambda p: (0, part * pairs + p))

    whole = pl.BlockSpec(memory_space=pltpu.VMEM)
    diagonals = jax.ShapeDtypeStruct((2 * pairs, 8, LANES), F32)
    dma = pltpu.SemaphoreType.DMA
    scratch = []
    for spot in plan:
        scratch += chunk_scratch(spot[2], spot[4], depth)
    summed, small, diagonals, grad_input = pl.pallas_call(
        functools.partial(last_kernel, depth, plan, orders),
        grid=(pairs,),
        in_specs=[whole] * 3
        + [block(0), block(1), block(2), block(0), block(0)]
        + [pl.BlockSpec((1, rows, LANES), lambda p: (p, 0, 0))]
        + [whole]
        + [HBM] * 6,
        out_specs=[HBM, whole, whole, HBM],
        out_shape=[
            jax.ShapeDtypeStruct((3 * hidden, width), BF),
            jax.ShapeDtypeStruct(small.shape, F32),
            diagonals,
            jax.ShapeDtypeStruct((2, rows // 2, width), BF),
        ],
        scratch_shapes=static_scratch(rows)
        + [pltpu.VMEM((LANES, rows), BF)] * 3
        + [
            pltpu.VMEM((rows, width), BF),
            pltpu.VMEM((width, 3 * width), BF),
            pltpu.VMEM((rows, width), F32),
            dma((4,)),
        ]
        + [pltpu.VMEM((pairs, rows, LANES), BF)] * 3
        + [
            pltpu.VMEM((width, rows), BF),
            pltpu.VMEM((hidden, width), BF),
            pltpu.VMEM((rows, width), BF),
            pltpu.VMEM((hops,) + small.shape, F32),
            pltpu.VMEM((hops,) + diagonals.shape, F32),
            dma((2, 2, hops)),
            dma((3,)),
        ]
        + scratch,
        compiler_params=pltpu.CompilerParams(
            collective_id=0, has_side_effects=True, vmem_limit_bytes=62 * MIB
        ),
        name="summed_with_attention_back",
    )(meta_columns, meta_rows, table_rows, projected, projected, projected, mixed, d_mixed, logs,
      small, item, qkv_weight, d_hidden, grad_down, grad_up, grad_out)
    span = 4 * depth
    if size > span:
        groups = [list(range(first, size, span)) for first in range(span)]
        summed, small, diagonals = lax.psum(
            (summed.astype(F32), small, diagonals), "dp", axis_index_groups=groups
        )
        summed = summed.astype(BF)
    return summed, small, diagonals, grad_input


def per_device(
    layer_in, segment, key_mask, position, layout_x, layout_y,
    qkv_weight, query_bias, value_bias, out_weight, out_bias, attn_gain, attn_shift,
    up_weight, up_bias, down_weight, down_bias, ffn_gain, ffn_shift,
    text_table, horiz_table, vert_table, cotangent,
):
    width = layer_in.shape[-1]
    item, projected, meta_columns, meta_rows, table_rows = projected_item(
        layer_in, (segment, key_mask, position, layout_x, layout_y),
        qkv_weight, query_bias, value_bias, (text_table, horiz_table, vert_table),
    )
    mixed, logs = attention_forward(meta_columns, meta_rows, table_rows, projected, width)
    layer_out, d_hidden, d_mixed, grad_out, grad_down, grad_up, small = fed_forward_and_back(
        item, mixed, cotangent, out_weight, up_weight, down_weight,
        (out_bias, attn_gain, attn_shift, up_bias, down_bias, ffn_gain, ffn_shift),
    )
    summed, small, diagonals, grad_input = summed_with_attention_back(
        meta_columns, meta_rows, table_rows, projected, mixed, d_mixed, logs, item, qkv_weight,
        d_hidden, small, grad_down, grad_up, grad_out,
    )
    done = finished(
        summed, grad_input, small, diagonals, up_weight.shape[1], text_table.shape[0]
    )
    sum_down, sum_up, sum_out, sum_qkv, grad_input = done[:5]
    singles, tables = done[5:14], [t.T for t in done[14:]]
    return (
        layer_out, grad_input, sum_qkv, singles[0], singles[1], sum_out, singles[2], singles[3],
        singles[4], sum_up, singles[8], sum_down, singles[5], singles[6], singles[7],
        tables[0], tables[1], tables[2],
    )


def solution(mesh):
    rows = P("dp", "seq", None)
    marks_spec = P("dp", "seq")
    return jax.shard_map(
        per_device,
        mesh=mesh,
        in_specs=(rows,) + (marks_spec,) * 5 + (P(),) * 16 + (rows,),
        out_specs=(rows, rows) + (P(),) * 16,
        check_vma=False,
    )
```

```python
import functools

import jax
import jax.numpy as jnp
from jax import lax
from jax.experimental import pallas as pl
from jax.experimental.pallas import tpu as pltpu
from jax.sharding import PartitionSpec as P

BF = jnp.bfloat16
F32 = jnp.float32
BIG = 1e30
LANES = 128
HEAD = 64
TEXT = 512
POS = 64
COORD = 48
Y0 = 64
GROUP0 = 112
MEMBER0 = 116
FLAG = 124
LOG0 = 125
X_TABLE = 33
Y_TABLE = 66
NOTHING = 127


def dot_nt(a, b):
    return lax.dot_general(a, b, (((1,), (1,)), ((), ())), preferred_element_type=F32)


def dot_nn(a, b):
    return lax.dot_general(a, b, (((1,), (0,)), ((), ())), preferred_element_type=F32)


def looked_up(table_row, index):
    rows = index.shape[0]
    return jnp.take_along_axis(
        jnp.broadcast_to(table_row, (rows, LANES)), index, axis=1, mode="promise_in_bounds"
    )


def bucket(distance):
    return jnp.clip(distance, -16, 16) + 16


def between(lane, low, high):
    return (lane >= low) & (lane < high)


def columns_of(meta_ref):
    return tuple(meta_ref[:, field : field + 1] for field in range(5))


def marks(meta_ref):
    segment, key_mask, position, across, down = columns_of(meta_ref)
    rows = segment.shape[0]
    lane = lax.broadcasted_iota(jnp.int32, (rows, LANES), 1)
    row = lax.broadcasted_iota(jnp.int32, (rows, LANES), 0)
    even = between(lane, HEAD, HEAD + COORD) & (lane - HEAD == across)
    odd = (lane < COORD) & (lane == across)
    group = (segment - 1) >> 3
    member = (segment - 1) & 7
    named = segment > 0
    shared = (
        ((row < TEXT) & (lane < POS) & (lane == position))
        | (between(lane, Y0, Y0 + COORD) & (lane - Y0 == down))
        | (named & between(lane, GROUP0, MEMBER0) & (lane - GROUP0 == group))
        | (named & between(lane, MEMBER0, FLAG) & (lane - MEMBER0 == member))
        | ((lane == FLAG) & (key_mask <= 0))
        | (lane >= LOG0)
    )
    return tuple(jnp.where(m, 1.0, 0.0).astype(BF) for m in (even, odd, shared))


def barred(meta_ref):
    segment = meta_ref[:, 0:1]
    rows = segment.shape[0]
    lane = lax.broadcasted_iota(jnp.int32, (rows, LANES), 1)
    group = (segment - 1) >> 3
    member = (segment - 1) & 7
    shut = (
        ((segment > 0) & between(lane, GROUP0, MEMBER0) & (lane - GROUP0 != group))
        | ((segment < 0) & between(lane, GROUP0, MEMBER0))
        | ((segment > 0) & between(lane, MEMBER0, FLAG) & (lane - MEMBER0 != member))
        | (lane == FLAG)
    )
    return jnp.where(shut, -BIG, 0.0).astype(F32)


def query_index(meta_ref):
    segment, key_mask, position, across, down = columns_of(meta_ref)
    rows = segment.shape[0]
    lane = lax.broadcasted_iota(jnp.int32, (rows, LANES), 1)
    x_even = bucket(across - (lane - HEAD)) + X_TABLE
    x_odd = bucket(across - lane) + X_TABLE
    even = jnp.where(between(lane, HEAD, HEAD + COORD), x_even, NOTHING)
    odd = jnp.where(lane < COORD, x_odd, NOTHING)
    shared = jnp.where(
        lane < POS,
        bucket(position - lane),
        jnp.where(between(lane, Y0, Y0 + COORD), bucket(down - (lane - Y0)) + Y_TABLE, NOTHING),
    )
    return even, odd, shared


def image_key_index(meta_ref):
    position = meta_ref[TEXT:, 2:3]
    lane = lax.broadcasted_iota(jnp.int32, (position.shape[0], LANES), 1)
    return jnp.where(lane < POS, bucket(lane - position), NOTHING)


def prepare(meta_ref, mark_refs, bar_ref, index_refs, key_index_ref):
    for ref, value in zip(mark_refs, marks(meta_ref)):
        ref[...] = value
    bar_ref[...] = barred(meta_ref)
    for ref, value in zip(index_refs, query_index(meta_ref)):
        ref[...] = value
    key_index_ref[...] = image_key_index(meta_ref)


def image_offsets(row_positions, column_positions):
    return bucket(column_positions - row_positions)


def widened(parity, q, k, table_row, mark_refs, bar_ref, index_refs, key_index_ref, logs):
    rows = q.shape[0]
    lane = lax.broadcasted_iota(jnp.int32, (rows, LANES), 1)
    own = (lane < HEAD) if parity == 0 else (lane >= HEAD)
    first = jnp.where(own, q.astype(F32) * 0.125, looked_up(table_row, index_refs[parity][...]))
    second = looked_up(table_row, index_refs[2][...]) + bar_ref[...]
    if logs is not None:
        high = logs.astype(BF).astype(F32)
        middle = (logs - high).astype(BF).astype(F32)
        lowest = logs - high - middle
        second = jnp.where(
            lane == LOG0,
            -high,
            jnp.where(lane == LOG0 + 1, -middle, jnp.where(lane == LOG0 + 2, -lowest, second)),
        )
    first = first.astype(BF)
    second = second.astype(BF)
    mark_second = mark_refs[2][...]
    to_image = jnp.where(lane < POS, mark_second, second)
    key_first = jnp.where(own, k, mark_refs[parity][...])
    image_lane = lane[TEXT:]
    key_image = jnp.where(
        image_lane < POS,
        looked_up(table_row, key_index_ref[...]).astype(BF),
        mark_second[TEXT:],
    )
    q_text = jnp.concatenate([first, second], axis=1)
    q_image = jnp.concatenate([first, to_image], axis=1)
    k_text = jnp.concatenate([key_first[:TEXT], mark_second[:TEXT]], axis=1)
    k_image = jnp.concatenate([key_first[TEXT:], key_image], axis=1)
    return q_text, q_image, k_text, k_image


def image_bias(table_row, offsets):
    return jnp.concatenate(
        [looked_up(table_row, offsets[:, :LANES]), looked_up(table_row, offsets[:, LANES:])], axis=1
    )


def forward_kernel(
    meta_ref, rows_ref, table_ref, q_ref, k_ref, v_ref, mixed_ref, log_ref,
    even_ref, odd_ref, shared_ref, bar_ref, index_even, index_odd, index_shared, key_index_ref,
):
    mark_refs = (even_ref, odd_ref, shared_ref)
    index_refs = (index_even, index_odd, index_shared)

    @pl.when(pl.program_id(0) == 0)
    def _():
        prepare(meta_ref, mark_refs, bar_ref, index_refs, key_index_ref)

    rows = q_ref.shape[0]
    images = rows - TEXT
    q, k, v = q_ref[...], k_ref[...], v_ref[...]
    offsets = bucket(rows_ref[2:3, TEXT:] - meta_ref[TEXT:, 2:3])
    tile = 256
    v_turned = transposed(v)
    heads = []
    for parity in range(2):
        table_row = table_ref[pl.ds(2 * pl.program_id(0) + parity, 1), :]
        wide = widened(
            parity, q, k, table_row, mark_refs, bar_ref, index_refs, key_index_ref, None
        )
        heads.append(wide + (image_bias(table_row, offsets),))

    def scored(parity, start):
        q_text, q_image, k_text, k_image, bias = heads[parity]
        here = slice(start, start + tile)
        on_image = dot_nt(k_image, q_image[here])
        if start >= TEXT:
            on_image = on_image + bias[:, start - TEXT : start - TEXT + tile]
        return dot_nt(k_text, q_text[here]), on_image

    spots = [(parity, start) for parity in range(2) for start in range(0, rows, tile)]
    outs = ([], [])
    logs = ([], [])
    following = scored(*spots[0])
    for index, (parity, start) in enumerate(spots):
        on_text, on_image = following
        if index + 1 < len(spots):
            following = scored(*spots[index + 1])
        top = jnp.maximum(
            jnp.max(on_text, axis=0, keepdims=True), jnp.max(on_image, axis=0, keepdims=True)
        )
        on_text = jnp.exp(on_text - top)
        on_image = jnp.exp(on_image - top)
        total = jnp.sum(on_text, axis=0, keepdims=True) + jnp.sum(on_image, axis=0, keepdims=True)
        own = slice(parity * HEAD, parity * HEAD + HEAD)
        out = dot_nn(v_turned[own, :TEXT], on_text.astype(BF)) + dot_nn(
            v_turned[own, TEXT:], on_image.astype(BF)
        )
        outs[parity].append(out * (1.0 / total))
        logs[parity].append(jnp.broadcast_to(top + jnp.log(total), (HEAD, tile)))
    both = [
        jnp.concatenate([jnp.concatenate(kind[parity], axis=1) for parity in range(2)], axis=0)
        for kind in (outs, logs)
    ]
    mixed_ref[...] = jnp.transpose(both[0])
    log_ref[0] = jnp.transpose(both[1])


def static_scratch(rows):
    return [
        pltpu.VMEM((rows, LANES), BF),
        pltpu.VMEM((rows, LANES), BF),
        pltpu.VMEM((rows, LANES), BF),
        pltpu.VMEM((rows, LANES), F32),
        pltpu.VMEM((rows, LANES), jnp.int32),
        pltpu.VMEM((rows, LANES), jnp.int32),
        pltpu.VMEM((rows, LANES), jnp.int32),
        pltpu.VMEM((rows - TEXT, LANES), jnp.int32),
    ]


def attention_forward(meta_columns, meta_rows, table_rows, projected, width):
    rows = projected.shape[0]
    pairs = width // LANES

    def block(part):
        return pl.BlockSpec((rows, LANES), lambda p: (0, part * pairs + p))

    whole = lambda shape: pl.BlockSpec(shape, lambda p: (0,) * len(shape))
    return pl.pallas_call(
        forward_kernel,
        grid=(pairs,),
        in_specs=[
            whole(meta_columns.shape),
            whole(meta_rows.shape),
            whole(table_rows.shape),
            block(0), block(1), block(2),
        ],
        out_specs=[
            pl.BlockSpec((rows, LANES), lambda p: (0, p)),
            pl.BlockSpec((1, rows, LANES), lambda p: (p, 0, 0)),
        ],
        out_shape=[
            jax.ShapeDtypeStruct((rows, width), F32),
            jax.ShapeDtypeStruct((pairs, rows, LANES), F32),
        ],
        scratch_shapes=static_scratch(rows),
        compiler_params=pltpu.CompilerParams(vmem_limit_bytes=60 * 1024 * 1024),
        name="attention_forward",
    )(meta_columns, meta_rows, table_rows, projected, projected, projected)


def skewed(block):
    size = block.shape[0]
    lane = lax.broadcasted_iota(jnp.int32, (size, LANES), 1)
    row = lax.broadcasted_iota(jnp.int32, (size, LANES), 0)
    turned = jnp.take_along_axis(
        block, (lane + row) & (LANES - 1), axis=1, mode="promise_in_bounds"
    )
    straight = lane + row < LANES
    above = jnp.sum(jnp.where(straight, turned, 0.0), axis=0, keepdims=True)
    below = jnp.sum(jnp.where(straight, 0.0, turned), axis=0, keepdims=True)
    return above, below


def transposed(array):
    return jnp.transpose(array.astype(F32)).astype(array.dtype)


def static_prepare(meta_ref, static):
    (even_ref, odd_ref, shared_ref, bar_ref, index_even, index_odd, index_shared, key_index_ref,
     even_t, odd_t, shared_t) = static
    mark_refs = (even_ref, odd_ref, shared_ref)
    prepare(meta_ref, mark_refs, bar_ref, (index_even, index_odd, index_shared), key_index_ref)
    for ref, turned in zip(mark_refs, (even_t, odd_t, shared_t)):
        turned[...] = transposed(ref[...])


def head_back(
    parity, pair, meta_ref, rows_ref, table_ref, q_ref, k_ref, v_ref, mixed_ref, grad_ref, log_ref,
    static, d_query, d_key, d_value, diag_ref,
):
    (even_ref, odd_ref, shared_ref, bar_ref, index_even, index_odd, index_shared, key_index_ref,
     even_t, odd_t, shared_t) = static
    mark_refs = (even_ref, odd_ref, shared_ref)
    index_refs = (index_even, index_odd, index_shared)
    turned_refs = (even_t, odd_t, shared_t)
    rows = q_ref.shape[1]
    images = rows - TEXT
    tile = 256
    q, k, v, grad = q_ref[pair], k_ref[pair], v_ref[pair], grad_ref[pair]
    lane = lax.broadcasted_iota(jnp.int32, (rows, LANES), 1)
    products = grad.astype(F32) * mixed_ref[pair]
    k_turned = transposed(k)
    offsets = bucket(rows_ref[2:3, TEXT:] - meta_ref[TEXT:, 2:3])
    is_image = rows_ref[1:2, TEXT:] > 0
    own = (lane < HEAD) if parity == 0 else (lane >= HEAD)
    spare = HEAD if parity == 0 else 0
    table_row = table_ref[pl.ds(2 * pair + parity, 1), :]
    logs = log_ref[pair, :, parity * HEAD : parity * HEAD + 1]
    q_text, q_image, k_text, k_image = widened(
        parity, q, k, table_row, mark_refs, bar_ref, index_refs, key_index_ref, logs
    )
    bias = image_bias(table_row, offsets)
    half = lax.broadcasted_iota(jnp.int32, (LANES, LANES), 0)
    ones = jnp.where((half < HEAD) if parity == 0 else (half >= HEAD), 1.0, 0.0).astype(BF)
    delta = jnp.zeros((rows, LANES), F32)
    rest = products
    for _ in range(3):
        piece = rest.astype(BF)
        delta = delta + dot_nn(piece, ones)
        rest = rest - piece.astype(F32)
    high = delta.astype(BF).astype(F32)
    middle = (delta - high).astype(BF).astype(F32)
    lowest = delta - high - middle
    grad_wide = jnp.where(
        own,
        grad.astype(F32),
        jnp.where(
            lane == spare,
            -high,
            jnp.where(lane == spare + 1, -middle, jnp.where(lane == spare + 2, -lowest, 0.0)),
        ),
    ).astype(BF)
    v_wide = jnp.where(
        own, v.astype(F32), jnp.where(between(lane, spare, spare + 3), 1.0, 0.0)
    ).astype(BF)
    q_marked = jnp.concatenate(
        [
            jnp.where(own, q.astype(F32) * 0.125, mark_refs[parity][...].astype(F32)).astype(BF),
            shared_ref[...],
        ],
        axis=1,
    )
    dq = jnp.zeros((HEAD, rows), F32)
    dks = []
    dvs = []
    first_sum = jnp.zeros((LANES, LANES), F32)
    second_sum = jnp.zeros((LANES, LANES), F32)
    text_image = jnp.zeros((LANES, images), F32)
    def scored(start):
        here = slice(start, start + tile)
        if start < TEXT:
            scores = dot_nt(k_text[here], q_text)
        else:
            scores = dot_nt(k_image[start - TEXT : start - TEXT + tile], q_image)
            scores = jnp.concatenate([scores[:, :TEXT], scores[:, TEXT:] + bias], axis=1)
        return scores, dot_nt(v_wide[here], grad_wide)

    following = scored(0)
    for start in range(0, rows, tile):
        here = slice(start, start + tile)
        scores, prob_grad = following
        if start + tile < rows:
            following = scored(start + tile)
        soft = jnp.exp(scores)
        score_grad = soft * prob_grad
        low = score_grad.astype(BF)
        dvs.append(dot_nn(soft.astype(BF), grad))
        wide = dot_nn(low, q_marked)
        dks.append(wide[:, :LANES])
        dq = dq + dot_nn(k_turned[parity * HEAD : parity * HEAD + HEAD, here], low)
        rounded = wide.astype(BF)
        first_sum = first_sum + dot_nn(turned_refs[parity][:, here], rounded[:, :LANES])
        second_sum = second_sum + dot_nn(shared_t[:, here], rounded[:, LANES:])
        if start < TEXT:
            text_image = text_image + dot_nn(shared_t[:, here], low[:, TEXT:])
        else:
            by_position = wide[:, LANES:]
            on_image = score_grad[:, TEXT:]
    small = lax.broadcasted_iota(jnp.int32, (LANES, LANES), 1)
    small_row = lax.broadcasted_iota(jnp.int32, (LANES, LANES), 0)
    x0 = HEAD if parity == 0 else 0
    x_block = jnp.where(
        between(small, x0, x0 + COORD) & between(small_row, x0, x0 + COORD), first_sum, 0.0
    )
    y_block = jnp.where(
        between(small, Y0, Y0 + COORD) & between(small_row, Y0, Y0 + COORD), second_sum, 0.0
    )
    p_block = jnp.where((small < POS) & (small_row < POS), second_sum, 0.0)
    wide_lane = lax.broadcasted_iota(jnp.int32, (images, images), 1)
    outside = jnp.sum(jnp.where(is_image, 0.0, on_image), axis=1, keepdims=True)
    pairs = jnp.where(is_image, on_image, 0.0) + jnp.where(wide_lane == 0, outside, 0.0)
    outside_text = jnp.sum(jnp.where(is_image, 0.0, text_image), axis=1, keepdims=True)
    text_lane = lax.broadcasted_iota(jnp.int32, (LANES, images), 1)
    text_row = lax.broadcasted_iota(jnp.int32, (LANES, images), 0)
    text_image = jnp.where(is_image, text_image, 0.0) + jnp.where(
        text_lane == 0, outside_text, 0.0
    )
    text_image = jnp.where(text_row < POS, text_image, 0.0)
    first_lane = lax.broadcasted_iota(jnp.int32, (images, LANES), 1)
    left = pairs[:, :LANES] + jnp.where(first_lane < POS, by_position, 0.0)
    right = pairs[:, LANES:]
    a00, b00 = skewed(left[:LANES] + text_image[:, :LANES] + p_block)
    a01, b01 = skewed(right[:LANES] + text_image[:, LANES:])
    a10, b10 = skewed(left[LANES:])
    a11, b11 = skewed(right[LANES:])
    ax, bx = skewed(x_block)
    ay, by = skewed(y_block)
    diag_ref[2 * pair + parity] = jnp.concatenate(
        [b10, b00 + b11 + a10, a00 + a11 + b01, a01, bx, ax, by, ay], axis=0
    )
    empty = jnp.zeros_like(dq)
    both = [dq * 0.125, empty] if parity == 0 else [empty, dq * 0.125]
    results = (
        (d_query, jnp.transpose(jnp.concatenate(both, axis=0))),
        (d_key, jnp.concatenate(dks, axis=0)),
        (d_value, jnp.concatenate(dvs, axis=0)),
    )
    for ref, value in results:
        if parity == 1:
            value = jnp.where(own, value, ref[pair].astype(F32))
        ref[pair] = value.astype(BF)


MESH = pl.DeviceIdType.MESH
VMEM = pl.BlockSpec(memory_space=pltpu.VMEM)
HBM = pl.BlockSpec(memory_space=pltpu.HBM)
MIB = 1024 * 1024


def remote(src, dst, send, receive, device):
    return pltpu.make_async_remote_copy(
        src_ref=src, dst_ref=dst, send_sem=send, recv_sem=receive, device_id=device,
        device_id_type=MESH,
    )


def project_kernel(
    layer_ref, weight_hbm, *refs,
):
    small_hbm, refs = refs[:10], refs[10:]
    (item_ref, projected_out, columns_ref, rows_ref, table_ref,
     projected_ref, weight_ref, meta_send, bias_ref, sems, load_sems, store_sems), small = (
        refs[:12], refs[12:],
    )
    (segment_ref, mask_ref, position_ref, across_ref, down_ref, query_bias_ref, value_bias_ref,
     text_ref, horiz_ref, vert_ref) = small
    mine = lax.axis_index("seq")
    partner = (1 - mine, lax.axis_index("dp"))
    count, width = layer_ref.shape[1:]
    own = pl.ds(pl.multiple_of(mine * count, LANES), count)
    loads = [
        pltpu.make_async_copy(source, target, load_sems.at[index])
        for index, (source, target) in enumerate(
            list(zip(small_hbm, small))
            + [(layer_ref.at[mine], item_ref.at[own]), (weight_hbm, weight_ref)]
        )
    ]
    for load in loads:
        load.start()
    barrier = pltpu.get_barrier_semaphore()
    pl.semaphore_signal(barrier, inc=1, device_id=partner, device_id_type=MESH)
    pl.semaphore_wait(barrier, 1)
    pieces = count // LANES
    rows_out = [
        remote(
            layer_ref.at[1 - mine, pl.ds(piece * LANES, LANES)],
            item_ref.at[pl.ds(pl.multiple_of(mine * count + piece * LANES, LANES), LANES)],
            sems.at[0, piece], sems.at[1, piece], partner,
        )
        for piece in range(pieces)
    ]
    for copy in rows_out:
        copy.start()
    for load in loads[:-2]:
        load.wait()

    fields = (segment_ref, mask_ref, position_ref, across_ref, down_ref)
    blocks = [
        jnp.concatenate(
            [field[item : item + 1, :] for field in fields] + [jnp.zeros((3, count), jnp.int32)],
            axis=0,
        )
        for item in range(2)
    ]
    meta_send[...] = jnp.where(mine == 0, blocks[1], blocks[0])
    meta_out = remote(
        meta_send, rows_ref.at[:, own], sems.at[0, pieces], sems.at[1, pieces], partner
    )
    meta_out.start()
    rows_ref[:, own] = jnp.where(mine == 0, blocks[0], blocks[1])
    bias_ref[:, :width] = query_bias_ref[...].astype(F32).reshape(1, width)
    bias_ref[:, width : 2 * width] = jnp.zeros((1, width), F32)
    bias_ref[:, 2 * width :] = value_bias_ref[...].astype(F32).reshape(1, width)
    heads, levels = text_ref.shape
    spot = lax.broadcasted_iota(jnp.int32, (levels, LANES), 1)
    level = lax.broadcasted_iota(jnp.int32, (levels, LANES), 0)
    table = jnp.zeros((heads, LANES), F32)
    for source, begin in ((text_ref, 0), (horiz_ref, X_TABLE), (vert_ref, Y_TABLE)):
        table = table + dot_nn(source[...], (spot == level + begin).astype(BF))
    table_ref[...] = jnp.concatenate([table, jnp.zeros((16 - heads, LANES), F32)], axis=0)

    def project(there):
        step = 256

        def body(index, carry):
            columns = pl.ds(pl.multiple_of(index * step, step), step)
            product = dot_nn(item_ref[there], weight_ref[:, columns])
            projected_ref[there, columns] = (product + bias_ref[:, columns]).astype(BF)
            return carry

        lax.fori_loop(0, 3 * width // step, body, 0)

    def stored(index, there):
        return pltpu.make_async_copy(
            projected_ref.at[there], projected_out.at[there], store_sems.at[index]
        )

    for load in loads[-2:]:
        load.wait()
    project(own)
    stored(0, own).start()
    for piece in range(pieces):
        rows_out[piece].wait()
        there = pl.ds(pl.multiple_of((1 - mine) * count + piece * LANES, LANES), LANES)
        project(there)
        stored(1 + piece, there).start()
    meta_out.wait()
    meta = rows_ref[...].astype(F32)
    tall = jnp.concatenate([meta, jnp.zeros((LANES - 8, meta.shape[1]), F32)], axis=0)
    columns_ref[...] = jnp.transpose(tall).astype(jnp.int32)
    stored(0, own).wait()
    for piece in range(pieces):
        there = pl.ds(pl.multiple_of((1 - mine) * count + piece * LANES, LANES), LANES)
        stored(1 + piece, there).wait()


def projected_item(layer_in, fields, qkv_weight, query_bias, value_bias, tables):
    rows = 2 * layer_in.shape[1]
    width = layer_in.shape[2]
    pieces = rows // 2 // LANES
    small = list(fields) + [query_bias, value_bias] + [t.T for t in tables]
    return pl.pallas_call(
        project_kernel,
        in_specs=[HBM] * (2 + len(small)),
        out_specs=[VMEM, HBM, VMEM, VMEM, VMEM],
        out_shape=[
            jax.ShapeDtypeStruct((rows, width), BF),
            jax.ShapeDtypeStruct((rows, 3 * width), BF),
            jax.ShapeDtypeStruct((rows, LANES), jnp.int32),
            jax.ShapeDtypeStruct((8, rows), jnp.int32),
            jax.ShapeDtypeStruct((16, LANES), F32),
        ],
        scratch_shapes=[
            pltpu.VMEM((rows, 3 * width), BF),
            pltpu.VMEM((width, 3 * width), BF),
            pltpu.VMEM((8, rows // 2), jnp.int32),
            pltpu.VMEM((1, 3 * width), F32),
            pltpu.SemaphoreType.DMA((2, pieces + 1)),
            pltpu.SemaphoreType.DMA((len(small) + 2,)),
            pltpu.SemaphoreType.DMA((pieces + 1,)),
        ]
        + [pltpu.VMEM(array.shape, array.dtype) for array in small],
        compiler_params=pltpu.CompilerParams(
            collective_id=1, has_side_effects=True, vmem_limit_bytes=60 * MIB
        ),
        name="projected_item",
    )(layer_in, qkv_weight, *small)


EPSILON = 1e-05
TILE = 256


def vector(ref):
    return ref[...].astype(F32).reshape(1, ref.shape[0])


def gelu_and_slope(x):
    bell = jnp.exp(-0.5 * x * x)
    t = 1.0 / (1.0 + 0.23164188826 * jnp.abs(x))
    series = t * (
        0.127414796
        + t * (-0.142248368 + t * (0.7107068705 + t * (-0.7265760135 + t * 0.5307027145)))
    )
    tail = bell * series
    below = jnp.where(x >= 0.0, 1.0 - tail, tail)
    return x * below, below + x * (0.3989422804014327 * bell)


def row_mean(block):
    return jnp.mean(block, axis=1, keepdims=True)


def normalized(hidden):
    center = hidden - row_mean(hidden)
    scale = lax.rsqrt(row_mean(center * center) + EPSILON)
    return center * scale, scale


def norm_pulled(grad, unit, scale):
    return scale * (grad - row_mean(grad) - unit * row_mean(grad * unit))


def column_sum(block):
    return jnp.sum(block, axis=0, keepdims=True)


def feed_kernel(
    item_ref, mixed_ref, cotangent_ref, out_weight_ref, up_ref, down_ref, *refs,
):
    vectors_hbm, refs = refs[:7], refs[7:]
    (layer_out, d_hidden_ref, d_mixed_ref, grad_out_ref, grad_down_ref, grad_up_ref, small_ref,
     layer_ref, cotangent_all, active, slope, unit, scale_ref, normed, normed_t, total, d_branch, d_branch_t,
     sems, load_sems) = refs[:20]
    vectors = refs[20:]
    (out_bias_ref, attn_gain_ref, attn_shift_ref, up_bias_ref, down_bias_ref, ffn_gain_ref,
     ffn_shift_ref) = vectors
    step = pl.program_id(0)
    blocks = pl.num_programs(0) // 2
    rows, width = item_ref.shape
    count = rows // 2
    mine = lax.axis_index("seq")
    partner = (1 - mine, lax.axis_index("dp"))
    own = pl.ds(pl.multiple_of(mine * count, LANES), count)
    tiles = rows // TILE

    def sent():
        return remote(
            cotangent_ref.at[1 - mine], cotangent_all.at[own], sems.at[0], sems.at[1], partner
        )

    def returned():
        theirs = pl.ds(pl.multiple_of((1 - mine) * count, LANES), count)
        return [
            pltpu.make_async_copy(layer_ref.at[own], layer_out.at[mine], load_sems.at[8]),
            remote(
                layer_ref.at[theirs], layer_out.at[mine], sems.at[2], sems.at[3], partner
            ),
        ]

    def loads():
        copies = list(zip(vectors_hbm, vectors)) + [(cotangent_ref.at[mine], cotangent_all.at[own])]
        return [
            pltpu.make_async_copy(source, target, load_sems.at[index])
            for index, (source, target) in enumerate(copies)
        ]

    def over_tiles(size, body, carry):
        def run(index, state):
            return body(pl.ds(pl.multiple_of(index * size, size), size), state)

        return lax.fori_loop(0, rows // size, run, carry)

    @pl.when(step == 0)
    def _():
        for load in loads():
            load.start()
        barrier = pltpu.get_barrier_semaphore()
        pl.semaphore_signal(barrier, inc=1, device_id=partner, device_id_type=MESH)
        pl.semaphore_wait(barrier, 1)
        sent().start()
        small_ref[...] = jnp.zeros_like(small_ref)
        for load in loads():
            load.wait()
        out_bias, gain, shift = vector(out_bias_ref), vector(attn_gain_ref), vector(attn_shift_ref)

        def tile(there, carry):
            attn = dot_nn(mixed_ref[there].astype(BF), out_weight_ref[...]) + out_bias
            standard, scale = normalized(item_ref[there].astype(F32) + attn)
            unit[there] = standard
            scale_ref[there] = jnp.broadcast_to(scale, (scale.shape[0], LANES))
            result = standard * gain + shift
            normed[there] = result.astype(BF)
            normed_t[:, there] = jnp.transpose(result).astype(BF)
            return carry

        over_tiles(TILE, tile, 0)
        total[...] = jnp.zeros_like(total)

    @pl.when(step < blocks)
    def _():
        columns = [slice(begin, begin + TILE) for begin in range(0, width, TILE)]
        low = normed[...]
        following = dot_nn(low, up_ref[:, columns[0]])
        values = []
        for index, here in enumerate(columns):
            product = following
            if index + 1 < len(columns):
                following = dot_nn(low, up_ref[:, columns[index + 1]])
            bias = up_bias_ref[pl.ds(pl.multiple_of(step * width + here.start, LANES), TILE)]
            value, grade = gelu_and_slope(product + bias.astype(F32).reshape(1, TILE))
            values.append(value.astype(BF))
            active[step, :, here] = values[-1]
            slope[step, :, here] = grade
        values = jnp.concatenate(values, axis=1)
        for here in columns:
            total[:, here] += dot_nn(values, down_ref[:, here])

    @pl.when(step == blocks)
    def _():
        sent().wait()
        gain, shift, bias = vector(ffn_gain_ref), vector(ffn_shift_ref), vector(down_bias_ref)
        first_gain, first_shift = vector(attn_gain_ref), vector(attn_shift_ref)

        def tile(there, sums):
            hidden = unit[there] * first_gain + first_shift + (total[there] + bias)
            standard, scale = normalized(hidden)
            layer_ref[there] = (standard * gain + shift).astype(BF)
            cotangent = cotangent_all[there].astype(F32)
            pulled = norm_pulled(cotangent * gain, standard, scale)
            total[there] = pulled
            low = pulled.astype(BF)
            d_branch[there] = low
            return (
                sums[0] + column_sum(low.astype(F32)),
                sums[1] + column_sum(cotangent * standard),
                sums[2] + column_sum(cotangent),
            )

        zero = jnp.zeros((1, width), F32)
        sums = over_tiles(64, tile, (zero, zero, zero))
        for row, value in zip((5, 6, 7), sums):
            small_ref[row : row + 1] = value

        for copy in returned():
            copy.start()

        def turn(there, carry):
            d_branch_t[:, there] = jnp.transpose(d_branch[there].astype(F32)).astype(BF)
            return carry

        over_tiles(TILE, turn, 0)

    @pl.when(step >= blocks)
    def _():
        block = step - blocks

        columns = [slice(begin, begin + TILE) for begin in range(0, width, TILE)]
        branch = d_branch[...]
        turned = d_branch_t[...]
        following = dot_nt(branch, down_ref[columns[0]])
        values = []
        for index, here in enumerate(columns):
            product = following
            if index + 1 < len(columns):
                following = dot_nt(branch, down_ref[columns[index + 1]])
            grad_down_ref[:, here] = dot_nn(turned, active[block, :, here]).astype(BF)
            d_up = (product * slope[block, :, here]).astype(BF)
            small_ref[pl.ds(8 + block, 1), here] = column_sum(d_up.astype(F32))
            values.append(d_up)
        values = jnp.concatenate(values, axis=1)
        turned = normed_t[...]
        for here in columns:
            grad_up_ref[:, here] = dot_nn(turned, values[:, here]).astype(BF)
            total[:, here] += dot_nt(values, up_ref[here])

    @pl.when(step == 2 * blocks - 1)
    def _():
        gain = vector(attn_gain_ref)

        def tile(there, sums):
            d_normed = total[there]
            standard = unit[there]
            d_hidden = norm_pulled(d_normed * gain, standard, scale_ref[there, :1])
            d_hidden_ref[there] = d_hidden
            low = d_hidden.astype(BF)
            d_branch[there] = low
            return (
                sums[0] + column_sum(low.astype(F32)),
                sums[1] + column_sum(d_normed * standard),
                sums[2] + column_sum(d_normed),
            )

        zero = jnp.zeros((1, width), F32)
        sums = over_tiles(64, tile, (zero, zero, zero))
        for row, value in zip((2, 3, 4), sums):
            small_ref[row : row + 1] = value

        def turn(there, carry):
            normed_t[:, there] = jnp.transpose(mixed_ref[there]).astype(BF)
            return carry

        over_tiles(TILE, turn, 0)

        for begin in range(0, width, TILE):
            here = slice(begin, begin + TILE)
            d_mixed_ref[:, here] = dot_nt(d_branch[...], out_weight_ref[here]).astype(BF)
            grad_out_ref[:, here] = dot_nn(normed_t[...], d_branch[:, here]).astype(BF)

        for copy in returned():
            copy.wait()


def fed_forward_and_back(
    item, mixed, cotangent, out_weight, up_weight, down_weight, vectors,
):
    rows, width = item.shape
    blocks = up_weight.shape[1] // width
    whole = pl.BlockSpec(memory_space=pltpu.VMEM)
    square = lambda kind: jax.ShapeDtypeStruct((rows, width), kind)
    later = lambda i: jnp.maximum(i - blocks, 0)
    return pl.pallas_call(
        feed_kernel,
        grid=(2 * blocks,),
        in_specs=[whole, whole, HBM, whole]
        + [
            pl.BlockSpec((width, width), lambda i: (0, lax.rem(i, blocks))),
            pl.BlockSpec((width, width), lambda i: (lax.rem(i, blocks), 0)),
        ]
        + [HBM] * 7,
        out_specs=[HBM] + [whole] * 3
        + [
            pl.BlockSpec((width, width), lambda i: (later(i), 0)),
            pl.BlockSpec((width, width), lambda i: (later(i), 0)),
            whole,
        ],
        out_shape=[
            jax.ShapeDtypeStruct((2, rows // 2, width), BF), square(F32), square(BF),
            jax.ShapeDtypeStruct((width, width), BF),
            jax.ShapeDtypeStruct((blocks * width, width), BF),
            jax.ShapeDtypeStruct((blocks * width, width), BF),
            jax.ShapeDtypeStruct((16, width), F32),
        ],
        scratch_shapes=[
            pltpu.VMEM((rows, width), BF),
            pltpu.VMEM((rows, width), BF),
            pltpu.VMEM((blocks, rows, width), BF),
            pltpu.VMEM((blocks, rows, width), F32),
            pltpu.VMEM((rows, width), F32),
            pltpu.VMEM((rows, LANES), F32),
            pltpu.VMEM((rows, width), BF),
            pltpu.VMEM((width, rows), BF),
            pltpu.VMEM((rows, width), F32),
            pltpu.VMEM((rows, width), BF),
            pltpu.VMEM((width, rows), BF),
            pltpu.SemaphoreType.DMA((4,)),
            pltpu.SemaphoreType.DMA((9,)),
        ]
        + [pltpu.VMEM(vector.shape, vector.dtype) for vector in vectors],
        compiler_params=pltpu.CompilerParams(
            collective_id=2, has_side_effects=True, vmem_limit_bytes=60 * MIB
        ),
        name="feed_forward",
    )(item, mixed, cotangent, out_weight, up_weight, down_weight, *vectors)


SLOTS = 4


def finish_kernel(
    summed_ref, input_hbm, small_ref, diagonal_ref,
    down_ref, up_ref, out_ref, qkv_ref, input_ref, *refs,
):
    singles, (blocks_in, slots, input_in, input_slot, in_sems, out_sems, item_sems) = (
        refs[:12], refs[12:],
    )
    blocks, width = blocks_in.shape[0], blocks_in.shape[2]
    hidden = down_ref.shape[0] // width

    def load(block):
        return pltpu.make_async_copy(
            summed_ref.at[pl.ds(block * width, width)], blocks_in.at[block], in_sems.at[block]
        )

    def stores(block):
        slot, sem = slots.at[block % SLOTS], out_sems.at[block % SLOTS]
        if block < hidden:
            targets = [(slot, down_ref.at[pl.ds(block * width, width)])]
        elif block < 2 * hidden:
            targets = [(slot, up_ref.at[:, pl.ds((block - hidden) * width, width)])]
        elif block == 2 * hidden:
            targets = [(slot, out_ref)]
        else:
            first = 2 * (block - 2 * hidden - 1)
            targets = [
                (
                    slot.at[:, pl.ds((3 * pair + part) * LANES, LANES)],
                    qkv_ref.at[:, pl.ds(part * width + (first + pair) * LANES, LANES)],
                )
                for pair in range(2) for part in range(3)
            ]
        return [
            pltpu.make_async_copy(source, target, sem.at[index])
            for index, (source, target) in enumerate(targets)
        ]

    load_input = pltpu.make_async_copy(input_hbm, input_in, item_sems.at[0])
    store_input = pltpu.make_async_copy(input_slot, input_ref, item_sems.at[1])
    for block in range(blocks):
        load(block).start()
    load_input.start()
    for block in range(blocks):
        load(block).wait()
        if block >= SLOTS:
            for copy in stores(block - SLOTS):
                copy.wait()
        piece = blocks_in[block].astype(F32)
        slots[block % SLOTS] = jnp.transpose(piece) if block < hidden else piece
        for copy in stores(block):
            copy.start()
    load_input.wait()
    input_slot[...] = input_in[...].astype(F32)
    store_input.start()
    for row in range(8):
        singles[row][...] = small_ref[row]
    for row in range(hidden):
        singles[8][row * width : row * width + width] = small_ref[8 + row]
    heads, levels = singles[9].shape
    diagonals = diagonal_ref[...]
    level = lax.broadcasted_iota(jnp.int32, (LANES, LANES), 1)
    lane = lax.broadcasted_iota(jnp.int32, (LANES, LANES), 0)
    for table, (first, size, skip) in enumerate(((0, 4, 0), (4, 2, 1), (6, 2, 1))):
        total = jnp.zeros((heads, LANES), F32)
        for row in range(size):
            distance = lane + LANES * (row + skip - 2)
            chosen = (bucket(distance) == level).astype(F32)
            total = total + jnp.dot(
                diagonals[:, first + row, :], chosen, preferred_element_type=F32,
                precision=lax.Precision.HIGHEST,
            )
        singles[9 + table][...] = total[:, :levels]
    for block in range(blocks - SLOTS, blocks):
        for copy in stores(block):
            copy.wait()
    store_input.wait()


def finished(summed, grad_input, small, diagonals, hidden, levels):
    width = summed.shape[1]
    heads = diagonals.shape[0]
    blocks = summed.shape[0] // width
    single = jax.ShapeDtypeStruct((width,), F32)
    table = jax.ShapeDtypeStruct((heads, levels), F32)
    dma = pltpu.SemaphoreType.DMA
    return pl.pallas_call(
        finish_kernel,
        in_specs=[HBM, HBM, VMEM, VMEM],
        out_specs=[HBM] * 5 + [VMEM] * 12,
        out_shape=[
            jax.ShapeDtypeStruct((hidden, width), F32),
            jax.ShapeDtypeStruct((width, hidden), F32),
            jax.ShapeDtypeStruct((width, width), F32),
            jax.ShapeDtypeStruct((width, 3 * width), F32),
            jax.ShapeDtypeStruct(grad_input.shape, F32),
        ]
        + [single] * 8
        + [jax.ShapeDtypeStruct((hidden,), F32)]
        + [table] * 3,
        scratch_shapes=[
            pltpu.VMEM((blocks, width, width), BF),
            pltpu.VMEM((SLOTS, width, width), F32),
            pltpu.VMEM(grad_input.shape, BF),
            pltpu.VMEM(grad_input.shape, F32),
            dma((blocks,)),
            dma((SLOTS, 6)),
            dma((2,)),
        ],
        compiler_params=pltpu.CompilerParams(vmem_limit_bytes=56 * MIB),
        name="finished",
    )(summed, grad_input, small, diagonals)


PIECE = 16


def hop_names(depth):
    names = ["x", "y"]
    reach = 1
    while reach < depth:
        names.append(f"z{reach}")
        reach *= 2
    return names


def route(depth, letters):
    names = hop_names(depth)
    line = {"a": names[2:3], "b": names[3:]}
    return [name for letter in letters for name in line.get(letter, [letter])]


class Place:
    def __init__(self, depth):
        place = lax.axis_index("dp")
        x = lax.axis_index("seq")
        core = lax.rem(place, 2)
        y = lax.rem(lax.div(place, 2), 2)
        z = lax.rem(lax.div(place, 4), depth)
        group = lax.div(place, 4 * depth)
        at = lambda sx, sc, sy, sz: (sx, (group * depth + sz) * 4 + sy * 2 + sc)
        self.bits = {"core": core, "x": x, "y": y}
        self.partners = {
            "core": at(x, 1 - core, y, z), "x": at(1 - x, core, y, z), "y": at(x, core, 1 - y, z),
        }
        reach = 1
        while reach < depth:
            up = lax.rem(lax.div(z, reach), 2)
            self.bits[f"z{reach}"] = up
            self.partners[f"z{reach}"] = at(x, core, y, z + reach - 2 * reach * up)
            reach *= 2

    def greet(self):
        barrier = pltpu.get_barrier_semaphore()
        for device in self.partners.values():
            pl.semaphore_signal(barrier, inc=1, device_id=device, device_id_type=MESH)
        pl.semaphore_wait(barrier, len(self.partners))


class Chunk:
    def __init__(self, place, depth, source, out_ref, offset, spot, scratch):
        _, self.begin, rows, first, columns, _, paths, _ = spot
        self.place, self.source, self.columns = place, source, pl.ds(first, columns)
        self.out_ref, self.out_begin = out_ref, offset + self.begin
        self.half, self.quarter = rows // 2, rows // 4
        self.routes = [route(depth, letters) for letters in paths.split()]
        self.hops = len(self.routes[0])
        self.stages = 2 * self.hops + 3
        self.work, self.fresh, *self.landing, self.sends, self.receives, self.locals = scratch

    def aligned(self, value):
        return pl.multiple_of(value, PIECE)

    def size(self, hop):
        return self.quarter >> (hop + 1)

    def base(self, part, hops):
        start = part * self.quarter
        for hop in range(hops):
            start = start + self.place.bits[self.routes[part][hop]] * self.size(hop)
        return start

    def across(self, part, hop):
        bit = self.place.bits[self.routes[part][hop]]
        return self.base(part, hop) + (1 - bit) * self.size(hop)

    def partner(self, part, hop):
        return self.place.partners[self.routes[part][hop]]

    def out(self, begin, size, core=None):
        core = self.place.bits["core"] if core is None else core
        return self.out_ref.at[
            pl.ds(self.aligned(self.out_begin + core * self.half + begin), size), self.columns
        ]

    def copy(self, index, source, target, device):
        return remote(source, target, self.sends.at[index], self.receives.at[index], device)

    def pair_down(self):
        core = self.place.bits["core"]
        at = lambda c: self.source.at[
            pl.ds(self.aligned(self.begin + c * self.half), self.half), self.columns
        ]
        return [
            self.copy(0, at(1 - core), self.fresh, self.place.partners["core"]),
            pltpu.make_async_copy(at(core), self.work, self.locals.at[0]),
        ]

    def pair_up(self, arriving):
        core = self.place.bits["core"]
        target = self.out(0, self.half, 1 - core if arriving else core)
        return [self.copy(1, self.out(0, self.half), target, self.place.partners["core"])]

    def down(self, hop):
        return [
            self.copy(
                2 + 2 * hop + part,
                self.work.at[pl.ds(self.aligned(self.across(part, hop)), self.size(hop))],
                self.landing[hop].at[part], self.partner(part, hop),
            )
            for part in range(2)
        ]

    def kept(self):
        size = self.size(self.hops - 1)
        copies = []
        for part in range(2):
            begin = self.aligned(self.base(part, self.hops))
            copies.append(
                pltpu.make_async_copy(
                    self.work.at[pl.ds(begin, size)], self.out(begin, size),
                    self.locals.at[1 + part],
                )
            )
        return copies

    def up(self, hop, arriving):
        copies = []
        for part in range(2):
            mine = self.base(part, hop + 1)
            size = self.size(hop)
            if hop == self.hops - 1:
                source = self.work.at[pl.ds(self.aligned(mine), size)]
            else:
                source = self.out(mine, size)
            target = self.out(self.across(part, hop) if arriving else mine, size)
            index = 2 + 2 * self.hops + 2 * hop + part
            copies.append(self.copy(index, source, target, self.partner(part, hop)))
        return copies

    def add(self, begin, source, size):
        step = 64 if size % 64 == 0 else min(size, PIECE)

        def body(index, carry):
            offset = self.aligned(index * step)
            there = pl.ds(self.aligned(begin + offset), step)
            total = self.work[there].astype(F32) + source[pl.ds(offset, step)].astype(F32)
            self.work[there] = total.astype(BF)
            return carry

        lax.fori_loop(0, size // step, body, 0)

    def stage(self, number):
        hops = self.hops
        ended, started = [], []
        if number == 0:
            started = self.pair_down()
        elif number == 1:
            ended = self.pair_down()
            started = self.down(0)
        elif number <= hops:
            ended = self.down(number - 2)
            started = self.down(number - 1)
        elif number == hops + 1:
            ended = self.down(hops - 1)
            started = self.up(hops - 1, False) + self.kept()
        elif number <= 2 * hops:
            level = 2 * hops + 1 - number
            ended = self.up(level, True) + (self.kept() if level == hops - 1 else [])
            started = self.up(level - 1, False)
        elif number == 2 * hops + 1:
            ended = self.up(0, True)
            started = self.pair_up(False)
        else:
            ended = self.pair_up(True)
        for copy in ended:
            copy.wait()
        if number == 1:
            self.add(0, self.fresh, self.half)
        elif 2 <= number <= hops + 1:
            hop = number - 2
            for part in range(2):
                self.add(self.base(part, hop + 1), self.landing[hop].at[part], self.size(hop))
        for copy in started:
            copy.start()


def chunk_scratch(rows, width, depth):
    hops = len(hop_names(depth))
    dma = pltpu.SemaphoreType.DMA
    return (
        [pltpu.VMEM((rows // 2, width), BF)] * 2
        + [pltpu.VMEM((2, rows // 4 >> (hop + 1), width), BF) for hop in range(hops)]
        + [dma((2 + 4 * hops,)), dma((2 + 4 * hops,)), dma((3,))]
    )


def planned(chunks, work, depth, hop_count):
    latency, issue, link, pair = 2.5, 0.2, 100e3, 350e3
    free = {}
    now = 0.0

    def sent(name, rows, columns):
        nonlocal now
        now += issue
        row_bytes = 2 * columns
        share = {"core": [("core", rows * row_bytes / pair)]}.get(name)
        if share is None:
            time = 2 * rows * row_bytes / link
            share = [(name, time)]
            if name[0] == "z":
                reach = int(name[1:])
                share = [("z end", time), ("z middle", 0.0 if reach == 1 else reach * time)]
        end = now
        for lane, time in share:
            free[lane] = max(now, free.get(lane, 0.0)) + time
            end = max(end, free[lane])
        return end + latency

    chains = []
    for rows, columns, need, paths, _ in chunks:
        paths = [route(depth, letters) for letters in paths.split()]
        down = []
        size = rows // 4
        for hop in range(len(paths[0])):
            size //= 2
            down.append([(path[hop], size, columns) for path in paths])
        pair_step = [[("core", rows // 2, columns)]]
        chains.append((need, pair_step + down + down[::-1] + pair_step))
    chains.append((len(work), [[("core", 16, 768)]] * hop_count))
    position = [0] * len(chains)
    ready = [0.0] * len(chains)
    ranks = [chunk[4] for chunk in chunks] + [0]
    order = [[] for _ in range(len(work) + 1)]
    done = 0
    while True:
        open_ones = [
            (ranks[i], ready[i], i) for i, (need, chain) in enumerate(chains)
            if position[i] <= len(chain) and need <= done
        ]
        due = [entry for entry in open_ones if entry[1] <= now]
        if not due and done < len(work):
            now += work[done]
            done += 1
            continue
        if not open_ones:
            return order
        _, when, index = min(due) if due else min(open_ones, key=lambda entry: entry[1])
        now = max(now, when)
        chain = chains[index][1]
        stage = position[index]
        order[done].append((index, stage))
        if 0 < stage <= len(chain) // 2:
            now += 2e-6 * sum(rows * wide for _, rows, wide in chain[stage - 1])
        if stage < len(chain):
            ready[index] = max(sent(*entry) for entry in chain[stage])
        position[index] += 1


def last_kernel(
    depth, plan, orders, *refs,
):
    (meta_ref, rows_ref, table_ref, projected_hbm, mixed_hbm, grad_hbm, log_hbm,
     small_ref, item_hbm, weight_hbm, d_hidden_hbm, grad_down_ref, grad_up_ref, grad_out_ref,
     out_ref, small_out, diagonal_out, input_out,
     *scratch) = refs
    static, scratch = scratch[:11], scratch[11:]
    (q_ref, k_ref, v_ref, mixed_ref, grad_ref, log_ref, pair_sems,
     item_ref, weight_ref, total_ref, load_sems, d_query, d_key, d_value, item_t, tail, input_grad,
     small_in, diagonal_in, small_sems, item_sems, *scratch) = scratch
    place = Place(depth)
    step = pl.program_id(0)
    pairs = d_query.shape[0]
    rows, width = item_hbm.shape
    count = rows // 2
    x = place.bits["x"]
    sources = (grad_down_ref, grad_up_ref, tail)
    each = len(scratch) // len(plan)
    chunks = []
    for index, spot in enumerate(plan):
        offset = spot[0] * grad_down_ref.shape[0]
        chunks.append(
            Chunk(place, depth, sources[spot[0]], out_ref, offset, spot,
                  scratch[index * each : index * each + each])
        )
    hop_devices = list(place.partners.values())

    def pair_loads(pair):
        copies = []
        held = (
            (projected_hbm, q_ref, 0), (projected_hbm, k_ref, width),
            (projected_hbm, v_ref, 2 * width), (mixed_hbm, mixed_ref, 0), (grad_hbm, grad_ref, 0),
        )
        for source, target, first in held:
            columns = pl.ds(pl.multiple_of(first + pair * LANES, LANES), LANES)
            copies.append((source.at[:, columns], target.at[pair]))
        copies.append((log_hbm.at[pair], log_ref.at[pair]))
        return [
            pltpu.make_async_copy(source, target, pair_sems.at[pair, index])
            for index, (source, target) in enumerate(copies)
        ]

    def loads():
        pairs_of = (
            (item_hbm, item_ref), (weight_hbm, weight_ref), (d_hidden_hbm, total_ref),
            (grad_out_ref, tail.at[pl.ds(0, width)]),
        )
        return [
            pltpu.make_async_copy(source, target, load_sems.at[index])
            for index, (source, target) in enumerate(pairs_of)
        ]

    def input_copies():
        return [
            pltpu.make_async_copy(
                input_grad.at[pl.ds(pl.multiple_of(x * count, LANES), count)], input_out.at[x],
                item_sems.at[0],
            ),
            remote(
                input_grad.at[pl.ds(pl.multiple_of((1 - x) * count, LANES), count)],
                input_out.at[x], item_sems.at[1], item_sems.at[2], place.partners["x"],
            ),
        ]

    def small_copies(hop):
        return [
            remote(source, landing.at[hop], small_sems.at[0, kind, hop],
                   small_sems.at[1, kind, hop], hop_devices[hop])
            for kind, (source, landing) in enumerate(
                ((small_out, small_in), (diagonal_out, diagonal_in))
            )
        ]

    def small_stage(hop):
        if hop > 0:
            for copy in small_copies(hop - 1):
                copy.wait()
            small_out[...] = small_out[...] + small_in[hop - 1]
            diagonal_out[...] = diagonal_out[...] + diagonal_in[hop - 1]
        if hop < len(hop_devices):
            for copy in small_copies(hop):
                copy.start()

    def perform(slot):
        for index, stage in orders[slot]:
            if index == len(chunks):
                small_stage(stage)
            else:
                chunks[index].stage(stage)

    @pl.when(step == 0)
    def _():
        for pair in range(pairs):
            for copy in pair_loads(pair):
                copy.start()
        for copy in loads():
            copy.start()
        place.greet()
        small_out[...] = small_ref[...]
        static_prepare(meta_ref, static)

    def slab(first):
        pieces = [
            (pair, part) for pair in (first, first + 1) for part in range(3)
        ]
        held = (d_query, d_key, d_value)
        base = width + first // 2 * width
        for left, right in zip(pieces[::2], pieces[1::2]):
            both = jnp.concatenate([held[part][pair] for pair, part in (left, right)], axis=1)
            weights = jnp.concatenate(
                [
                    weight_ref[:, part * width + pair * LANES : part * width + (pair + 1) * LANES]
                    for pair, part in (left, right)
                ],
                axis=1,
            )
            at = pieces.index(left) * LANES
            tail[base : base + width, at : at + 2 * LANES] = dot_nn(item_t[...], both).astype(BF)
            total_ref[...] += dot_nt(both, weights)
        for pair in (first, first + 1):
            columns = slice(pair * LANES, pair * LANES + LANES)
            small_out[0:1, columns] = column_sum(d_query[pair].astype(F32))
            small_out[1:2, columns] = column_sum(d_value[pair].astype(F32))

    @pl.when(step == 1)
    def _():
        for copy in loads():
            copy.wait()
        for tile in range(rows // TILE):
            there = slice(tile * TILE, tile * TILE + TILE)
            item_t[:, there] = jnp.transpose(item_ref[there].astype(F32)).astype(BF)

    for copy in pair_loads(step):
        copy.wait()
    for parity in range(2):
        for pair in range(pairs):
            @pl.when(step == pair)
            def _(pair=pair):
                perform(2 * pair + pair // 2 + parity)

        head_back(
            parity, step, meta_ref, rows_ref, table_ref, q_ref, k_ref, v_ref, mixed_ref,
            grad_ref, log_ref, static, d_query, d_key, d_value, diagonal_out,
        )

    for pair in range(1, pairs, 2):
        @pl.when(step == pair)
        def _(pair=pair):
            perform(2 * pair + 2 + pair // 2)
            slab(pair - 1)

    @pl.when(step == pairs - 1)
    def _():
        input_grad[...] = total_ref[...].astype(BF)
        for copy in input_copies():
            copy.start()
        perform(len(orders) - 1)
        for copy in input_copies():
            copy.wait()


def summed_with_attention_back(
    meta_columns, meta_rows, table_rows, projected, mixed, d_mixed, logs, item, qkv_weight,
    d_hidden, small, grad_down, grad_up, grad_out,
):
    size = lax.axis_size("dp")
    depth = 4 if size % 16 == 0 else size // 4
    rows, width = item.shape
    pairs = width // LANES
    hidden = grad_down.shape[0]
    hops = len(hop_names(depth)) + 1
    work = ([3.2] * 4 + [4.2]) * (pairs // 2)
    wide, slim = width // 2, width // 3
    plan = [
        (0, 0, 3072, 0, slim, 0, "xaby yabx", 0),
        (0, 0, 3072, slim, slim, 0, "xayb yxab", 0),
        (0, 0, 3072, 2 * slim, slim, 0, "yaxb xayb", 0),
        (1, 0, 2048, 0, width, 0, "yabx xyab", 1),
        (1, 2048, 1024, 0, width, 0, "abyx yaxb", 0),
        (2, 0, 1024, 0, wide, 5, "yabx xayb", 2),
        (2, 0, 1024, wide, wide, 5, "xyab yabx", 2),
        (2, 1024, 1024, 0, width, 10, "xyab yaxb", 1),
        (2, 2048, 1024, 0, wide, 15, "xayb yaxb", 2),
        (2, 2048, 1024, wide, wide, 15, "abyx yabx", 0),
    ]
    orders = planned([(spot[2],) + spot[4:] for spot in plan], work, depth, hops)

    whole = pl.BlockSpec(memory_space=pltpu.VMEM)
    diagonals = jax.ShapeDtypeStruct((2 * pairs, 8, LANES), F32)
    dma = pltpu.SemaphoreType.DMA
    scratch = []
    for spot in plan:
        scratch += chunk_scratch(spot[2], spot[4], depth)
    summed, small, diagonals, grad_input = pl.pallas_call(
        functools.partial(last_kernel, depth, plan, orders),
        grid=(pairs,),
        in_specs=[whole] * 3
        + [HBM] * 4
        + [whole]
        + [HBM] * 6,
        out_specs=[HBM, whole, whole, HBM],
        out_shape=[
            jax.ShapeDtypeStruct((3 * hidden, width), BF),
            jax.ShapeDtypeStruct(small.shape, F32),
            diagonals,
            jax.ShapeDtypeStruct((2, rows // 2, width), BF),
        ],
        scratch_shapes=static_scratch(rows)
        + [pltpu.VMEM((LANES, rows), BF)] * 3
        + [
            pltpu.VMEM((pairs, rows, LANES), kind) for kind in (BF, BF, BF, F32, BF, F32)
        ]
        + [
            dma((pairs, 6)),
            pltpu.VMEM((rows, width), BF),
            pltpu.VMEM((width, 3 * width), BF),
            pltpu.VMEM((rows, width), F32),
            dma((4,)),
        ]
        + [pltpu.VMEM((pairs, rows, LANES), BF)] * 3
        + [
            pltpu.VMEM((width, rows), BF),
            pltpu.VMEM((hidden, width), BF),
            pltpu.VMEM((rows, width), BF),
            pltpu.VMEM((hops,) + small.shape, F32),
            pltpu.VMEM((hops,) + diagonals.shape, F32),
            dma((2, 2, hops)),
            dma((3,)),
        ]
        + scratch,
        compiler_params=pltpu.CompilerParams(
            collective_id=0, has_side_effects=True, vmem_limit_bytes=62 * MIB
        ),
        name="summed_with_attention_back",
    )(meta_columns, meta_rows, table_rows, projected, mixed, d_mixed, logs,
      small, item, qkv_weight, d_hidden, grad_down, grad_up, grad_out)
    span = 4 * depth
    if size > span:
        groups = [list(range(first, size, span)) for first in range(span)]
        summed, small, diagonals = lax.psum(
            (summed.astype(F32), small, diagonals), "dp", axis_index_groups=groups
        )
        summed = summed.astype(BF)
    return summed, small, diagonals, grad_input


def per_device(
    layer_in, segment, key_mask, position, layout_x, layout_y,
    qkv_weight, query_bias, value_bias, out_weight, out_bias, attn_gain, attn_shift,
    up_weight, up_bias, down_weight, down_bias, ffn_gain, ffn_shift,
    text_table, horiz_table, vert_table, cotangent,
):
    width = layer_in.shape[-1]
    item, projected, meta_columns, meta_rows, table_rows = projected_item(
        layer_in, (segment, key_mask, position, layout_x, layout_y),
        qkv_weight, query_bias, value_bias, (text_table, horiz_table, vert_table),
    )
    mixed, logs = attention_forward(meta_columns, meta_rows, table_rows, projected, width)
    layer_out, d_hidden, d_mixed, grad_out, grad_down, grad_up, small = fed_forward_and_back(
        item, mixed, cotangent, out_weight, up_weight, down_weight,
        (out_bias, attn_gain, attn_shift, up_bias, down_bias, ffn_gain, ffn_shift),
    )
    summed, small, diagonals, grad_input = summed_with_attention_back(
        meta_columns, meta_rows, table_rows, projected, mixed, d_mixed, logs, item, qkv_weight,
        d_hidden, small, grad_down, grad_up, grad_out,
    )
    done = finished(
        summed, grad_input, small, diagonals, up_weight.shape[1], text_table.shape[0]
    )
    sum_down, sum_up, sum_out, sum_qkv, grad_input = done[:5]
    singles, tables = done[5:14], [t.T for t in done[14:]]
    return (
        layer_out, grad_input, sum_qkv, singles[0], singles[1], sum_out, singles[2], singles[3],
        singles[4], sum_up, singles[8], sum_down, singles[5], singles[6], singles[7],
        tables[0], tables[1], tables[2],
    )


def solution(mesh):
    rows = P("dp", "seq", None)
    marks_spec = P("dp", "seq")
    return jax.shard_map(
        per_device,
        mesh=mesh,
        in_specs=(rows,) + (marks_spec,) * 5 + (P(),) * 16 + (rows,),
        out_specs=(rows, rows) + (P(),) * 16,
        check_vma=False,
    )
```

```python
import functools

import jax
import jax.numpy as jnp
from jax import lax
from jax.experimental import pallas as pl
from jax.experimental.pallas import tpu as pltpu
from jax.sharding import PartitionSpec as P

BF = jnp.bfloat16
F32 = jnp.float32
BIG = 1e30
LANES = 128
HEAD = 64
TEXT = 512
POS = 64
COORD = 48
Y0 = 64
GROUP0 = 112
MEMBER0 = 116
FLAG = 124
LOG0 = 125
X_TABLE = 33
Y_TABLE = 66
NOTHING = 127


def dot_nt(a, b):
    return lax.dot_general(a, b, (((1,), (1,)), ((), ())), preferred_element_type=F32)


def dot_nn(a, b):
    return lax.dot_general(a, b, (((1,), (0,)), ((), ())), preferred_element_type=F32)


def looked_up(table_row, index):
    rows = index.shape[0]
    return jnp.take_along_axis(
        jnp.broadcast_to(table_row, (rows, LANES)), index, axis=1, mode="promise_in_bounds"
    )


def bucket(distance):
    return jnp.clip(distance, -16, 16) + 16


def between(lane, low, high):
    return (lane >= low) & (lane < high)


def columns_of(meta_ref):
    return tuple(meta_ref[:, field : field + 1] for field in range(5))


def marks(meta_ref):
    segment, key_mask, position, across, down = columns_of(meta_ref)
    rows = segment.shape[0]
    lane = lax.broadcasted_iota(jnp.int32, (rows, LANES), 1)
    row = lax.broadcasted_iota(jnp.int32, (rows, LANES), 0)
    even = between(lane, HEAD, HEAD + COORD) & (lane - HEAD == across)
    odd = (lane < COORD) & (lane == across)
    group = (segment - 1) >> 3
    member = (segment - 1) & 7
    named = segment > 0
    shared = (
        ((row < TEXT) & (lane < POS) & (lane == position))
        | (between(lane, Y0, Y0 + COORD) & (lane - Y0 == down))
        | (named & between(lane, GROUP0, MEMBER0) & (lane - GROUP0 == group))
        | (named & between(lane, MEMBER0, FLAG) & (lane - MEMBER0 == member))
        | ((lane == FLAG) & (key_mask <= 0))
        | (lane >= LOG0)
    )
    return tuple(jnp.where(m, 1.0, 0.0).astype(BF) for m in (even, odd, shared))


def barred(meta_ref):
    segment = meta_ref[:, 0:1]
    rows = segment.shape[0]
    lane = lax.broadcasted_iota(jnp.int32, (rows, LANES), 1)
    group = (segment - 1) >> 3
    member = (segment - 1) & 7
    shut = (
        ((segment > 0) & between(lane, GROUP0, MEMBER0) & (lane - GROUP0 != group))
        | ((segment < 0) & between(lane, GROUP0, MEMBER0))
        | ((segment > 0) & between(lane, MEMBER0, FLAG) & (lane - MEMBER0 != member))
        | (lane == FLAG)
    )
    return jnp.where(shut, -BIG, 0.0).astype(F32)


def query_index(meta_ref):
    segment, key_mask, position, across, down = columns_of(meta_ref)
    rows = segment.shape[0]
    lane = lax.broadcasted_iota(jnp.int32, (rows, LANES), 1)
    x_even = bucket(across - (lane - HEAD)) + X_TABLE
    x_odd = bucket(across - lane) + X_TABLE
    even = jnp.where(between(lane, HEAD, HEAD + COORD), x_even, NOTHING)
    odd = jnp.where(lane < COORD, x_odd, NOTHING)
    shared = jnp.where(
        lane < POS,
        bucket(position - lane),
        jnp.where(between(lane, Y0, Y0 + COORD), bucket(down - (lane - Y0)) + Y_TABLE, NOTHING),
    )
    return even, odd, shared


def image_key_index(meta_ref):
    position = meta_ref[TEXT:, 2:3]
    lane = lax.broadcasted_iota(jnp.int32, (position.shape[0], LANES), 1)
    return jnp.where(lane < POS, bucket(lane - position), NOTHING)


def prepare(meta_ref, mark_refs, bar_ref, index_refs, key_index_ref):
    for ref, value in zip(mark_refs, marks(meta_ref)):
        ref[...] = value
    bar_ref[...] = barred(meta_ref)
    for ref, value in zip(index_refs, query_index(meta_ref)):
        ref[...] = value
    key_index_ref[...] = image_key_index(meta_ref)


def image_offsets(row_positions, column_positions):
    return bucket(column_positions - row_positions)


def own_lanes(parity, rows):
    lane = lax.broadcasted_iota(jnp.int32, (rows, LANES), 1)
    return (lane < HEAD) if parity == 0 else (lane >= HEAD)


def widened(parity, q, table_row, bar_ref, index_refs, key_index_ref, shared_ref):
    rows = q.shape[0]
    images = key_index_ref.shape[0]
    first = jnp.where(
        own_lanes(parity, rows),
        q.astype(F32) * 0.125,
        looked_up(table_row, index_refs[parity][...]),
    )
    second = looked_up(table_row, index_refs[2][...]) + bar_ref[...]
    image_lane = lax.broadcasted_iota(jnp.int32, (images, LANES), 1)
    key_image = jnp.where(
        image_lane < POS, looked_up(table_row, key_index_ref[...]).astype(BF), shared_ref[TEXT:]
    )
    return first.astype(BF), second, key_image


def joined(parity, first, second, key_image, k, marks_own, shared):
    rows = k.shape[0]
    lane = lax.broadcasted_iota(jnp.int32, (rows, LANES), 1)
    to_image = jnp.where(lane < POS, shared, second)
    key_first = jnp.where(own_lanes(parity, rows), k, marks_own)
    q_text = jnp.concatenate([first, second], axis=1)
    q_image = jnp.concatenate([first, to_image], axis=1)
    k_text = jnp.concatenate([key_first[:TEXT], shared[:TEXT]], axis=1)
    k_image = jnp.concatenate([key_first[TEXT:], key_image], axis=1)
    return q_text, q_image, k_text, k_image


def in_three(value):
    high = value.astype(BF).astype(F32)
    middle = (value - high).astype(BF).astype(F32)
    return high, middle, value - high - middle


def with_pieces(lane, start, value, otherwise):
    high, middle, lowest = in_three(value)
    return jnp.where(
        lane == start,
        -high,
        jnp.where(lane == start + 1, -middle, jnp.where(lane == start + 2, -lowest, otherwise)),
    )


def image_bias(table_row, offsets):
    return jnp.concatenate(
        [looked_up(table_row, offsets[:, :LANES]), looked_up(table_row, offsets[:, LANES:])], axis=1
    )


def forward_kernel(
    meta_ref, rows_ref, table_ref, q_ref, k_ref, v_ref,
    mixed_ref, first_ref, second_ref, key_image_ref, bias_ref,
    even_ref, odd_ref, shared_ref, bar_ref, index_even, index_odd, index_shared, key_index_ref,
):
    mark_refs = (even_ref, odd_ref, shared_ref)
    index_refs = (index_even, index_odd, index_shared)

    @pl.when(pl.program_id(0) == 0)
    def _():
        prepare(meta_ref, mark_refs, bar_ref, index_refs, key_index_ref)

    rows = q_ref.shape[0]
    images = rows - TEXT
    q, k, v = q_ref[...], k_ref[...], v_ref[...]
    offsets = bucket(rows_ref[2:3, TEXT:] - meta_ref[TEXT:, 2:3])
    tile = 256
    v_turned = transposed(v)
    heads = []
    seconds = []
    for parity in range(2):
        table_row = table_ref[pl.ds(2 * pl.program_id(0) + parity, 1), :]
        first, second, key_image = widened(
            parity, q, table_row, bar_ref, index_refs, key_index_ref, shared_ref
        )
        bias = image_bias(table_row, offsets)
        first_ref[parity] = first
        key_image_ref[parity] = key_image
        bias_ref[parity] = bias.astype(BF)
        seconds.append(second)
        wide = joined(
            parity, first, second.astype(BF), key_image, k, mark_refs[parity][...], shared_ref[...]
        )
        heads.append(wide + (bias,))

    def scored(parity, start):
        q_text, q_image, k_text, k_image, bias = heads[parity]
        here = slice(start, start + tile)
        on_image = dot_nt(k_image, q_image[here])
        if start >= TEXT:
            on_image = on_image + bias[:, start - TEXT : start - TEXT + tile]
        return dot_nt(k_text, q_text[here]), on_image

    spots = [(parity, start) for parity in range(2) for start in range(0, rows, tile)]
    outs = ([], [])
    logs = ([], [])
    following = scored(*spots[0])
    for index, (parity, start) in enumerate(spots):
        on_text, on_image = following
        if index + 1 < len(spots):
            following = scored(*spots[index + 1])
        top = jnp.maximum(
            jnp.max(on_text, axis=0, keepdims=True), jnp.max(on_image, axis=0, keepdims=True)
        )
        on_text = jnp.exp(on_text - top)
        on_image = jnp.exp(on_image - top)
        total = jnp.sum(on_text, axis=0, keepdims=True) + jnp.sum(on_image, axis=0, keepdims=True)
        own = slice(parity * HEAD, parity * HEAD + HEAD)
        out = dot_nn(v_turned[own, :TEXT], on_text.astype(BF)) + dot_nn(
            v_turned[own, TEXT:], on_image.astype(BF)
        )
        outs[parity].append(out * (1.0 / total))
        logs[parity].append(jnp.broadcast_to(top + jnp.log(total), (LANES, tile)))
    mixed_ref[...] = jnp.transpose(
        jnp.concatenate([jnp.concatenate(outs[parity], axis=1) for parity in range(2)], axis=0)
    )
    lane = lax.broadcasted_iota(jnp.int32, (rows, LANES), 1)
    for parity in range(2):
        totals = jnp.transpose(jnp.concatenate(logs[parity], axis=1))
        second_ref[parity] = with_pieces(lane, LOG0, totals, seconds[parity]).astype(BF)


def static_scratch(rows):
    return [
        pltpu.VMEM((rows, LANES), BF),
        pltpu.VMEM((rows, LANES), BF),
        pltpu.VMEM((rows, LANES), BF),
        pltpu.VMEM((rows, LANES), F32),
        pltpu.VMEM((rows, LANES), jnp.int32),
        pltpu.VMEM((rows, LANES), jnp.int32),
        pltpu.VMEM((rows, LANES), jnp.int32),
        pltpu.VMEM((rows - TEXT, LANES), jnp.int32),
    ]


def attention_forward(meta_columns, meta_rows, table_rows, projected, width):
    rows = projected.shape[0]
    images = rows - TEXT
    pairs = width // LANES

    def block(part):
        return pl.BlockSpec((rows, LANES), lambda p: (0, part * pairs + p))

    whole = lambda shape: pl.BlockSpec(shape, lambda p: (0,) * len(shape))
    return pl.pallas_call(
        forward_kernel,
        grid=(pairs,),
        in_specs=[
            whole(meta_columns.shape),
            whole(meta_rows.shape),
            whole(table_rows.shape),
            block(0), block(1), block(2),
        ],
        out_specs=[
            pl.BlockSpec((rows, LANES), lambda p: (0, p)),
            pl.BlockSpec((2, rows, LANES), lambda p: (p, 0, 0)),
            pl.BlockSpec((2, rows, LANES), lambda p: (p, 0, 0)),
            pl.BlockSpec((2, images, LANES), lambda p: (p, 0, 0)),
            pl.BlockSpec((2, images, images), lambda p: (p, 0, 0)),
        ],
        out_shape=[
            jax.ShapeDtypeStruct((rows, width), F32),
            jax.ShapeDtypeStruct((2 * pairs, rows, LANES), BF),
            jax.ShapeDtypeStruct((2 * pairs, rows, LANES), BF),
            jax.ShapeDtypeStruct((2 * pairs, images, LANES), BF),
            jax.ShapeDtypeStruct((2 * pairs, images, images), BF),
        ],
        scratch_shapes=static_scratch(rows),
        compiler_params=pltpu.CompilerParams(vmem_limit_bytes=60 * 1024 * 1024),
        name="attention_forward",
    )(meta_columns, meta_rows, table_rows, projected, projected, projected)


def skewed(block):
    size = block.shape[0]
    lane = lax.broadcasted_iota(jnp.int32, (size, LANES), 1)
    row = lax.broadcasted_iota(jnp.int32, (size, LANES), 0)
    turned = jnp.take_along_axis(
        block, (lane + row) & (LANES - 1), axis=1, mode="promise_in_bounds"
    )
    straight = lane + row < LANES
    above = jnp.sum(jnp.where(straight, turned, 0.0), axis=0, keepdims=True)
    below = jnp.sum(jnp.where(straight, 0.0, turned), axis=0, keepdims=True)
    return above, below


def transposed(array):
    return jnp.transpose(array.astype(F32)).astype(array.dtype)


def static_prepare(meta_ref, static):
    for ref, turned, value in zip(static[:3], static[3:], marks(meta_ref)):
        ref[...] = value
        turned[...] = transposed(value)


def head_back(
    parity, pair, meta_ref, rows_ref, wide_refs, k_ref, v_ref, mixed_ref, grad_ref,
    static, d_query, d_key, d_value, diag_ref,
):
    mark_refs, turned_refs = static[:3], static[3:]
    first_ref, second_ref, key_image_ref, bias_ref = wide_refs
    head = 2 * pair + parity
    shared_t = turned_refs[2]
    rows = k_ref.shape[1]
    images = rows - TEXT
    tile = 256
    k, v, grad = k_ref[pair], v_ref[pair], grad_ref[pair]
    lane = lax.broadcasted_iota(jnp.int32, (rows, LANES), 1)
    products = grad.astype(F32) * mixed_ref[pair]
    k_turned = transposed(k)
    is_image = rows_ref[1:2, TEXT:] > 0
    own = (lane < HEAD) if parity == 0 else (lane >= HEAD)
    spare = HEAD if parity == 0 else 0
    first, shared = first_ref[head], mark_refs[2][...]
    q_text, q_image, k_text, k_image = joined(
        parity, first, second_ref[head], key_image_ref[head], k, mark_refs[parity][...], shared
    )
    bias = bias_ref[head].astype(F32)
    half = lax.broadcasted_iota(jnp.int32, (LANES, LANES), 0)
    ones = jnp.where((half < HEAD) if parity == 0 else (half >= HEAD), 1.0, 0.0).astype(BF)
    delta = jnp.zeros((rows, LANES), F32)
    rest = products
    for _ in range(3):
        piece = rest.astype(BF)
        delta = delta + dot_nn(piece, ones)
        rest = rest - piece.astype(F32)
    grad_wide = jnp.where(
        own, grad.astype(F32), with_pieces(lane, spare, delta, 0.0)
    ).astype(BF)
    v_wide = jnp.where(
        own, v.astype(F32), jnp.where(between(lane, spare, spare + 3), 1.0, 0.0)
    ).astype(BF)
    q_marked = jnp.concatenate(
        [jnp.where(own, first, mark_refs[parity][...]), shared], axis=1
    )
    dq = jnp.zeros((HEAD, rows), F32)
    dks = []
    dvs = []
    first_sum = jnp.zeros((LANES, LANES), F32)
    second_sum = jnp.zeros((LANES, LANES), F32)
    text_image = jnp.zeros((LANES, images), F32)
    def scored(start):
        here = slice(start, start + tile)
        if start < TEXT:
            scores = dot_nt(k_text[here], q_text)
        else:
            scores = dot_nt(k_image[start - TEXT : start - TEXT + tile], q_image)
            scores = jnp.concatenate([scores[:, :TEXT], scores[:, TEXT:] + bias], axis=1)
        return scores, dot_nt(v_wide[here], grad_wide)

    following = scored(0)
    for start in range(0, rows, tile):
        here = slice(start, start + tile)
        scores, prob_grad = following
        if start + tile < rows:
            following = scored(start + tile)
        soft = jnp.exp(scores)
        score_grad = soft * prob_grad
        low = score_grad.astype(BF)
        dvs.append(dot_nn(soft.astype(BF), grad))
        wide = dot_nn(low, q_marked)
        dks.append(wide[:, :LANES])
        dq = dq + dot_nn(k_turned[parity * HEAD : parity * HEAD + HEAD, here], low)
        rounded = wide.astype(BF)
        first_sum = first_sum + dot_nn(turned_refs[parity][:, here], rounded[:, :LANES])
        second_sum = second_sum + dot_nn(shared_t[:, here], rounded[:, LANES:])
        if start < TEXT:
            text_image = text_image + dot_nn(shared_t[:, here], low[:, TEXT:])
        else:
            by_position = wide[:, LANES:]
            on_image = score_grad[:, TEXT:]
    small = lax.broadcasted_iota(jnp.int32, (LANES, LANES), 1)
    small_row = lax.broadcasted_iota(jnp.int32, (LANES, LANES), 0)
    x0 = HEAD if parity == 0 else 0
    x_block = jnp.where(
        between(small, x0, x0 + COORD) & between(small_row, x0, x0 + COORD), first_sum, 0.0
    )
    y_block = jnp.where(
        between(small, Y0, Y0 + COORD) & between(small_row, Y0, Y0 + COORD), second_sum, 0.0
    )
    p_block = jnp.where((small < POS) & (small_row < POS), second_sum, 0.0)
    wide_lane = lax.broadcasted_iota(jnp.int32, (images, images), 1)
    outside = jnp.sum(jnp.where(is_image, 0.0, on_image), axis=1, keepdims=True)
    pairs = jnp.where(is_image, on_image, 0.0) + jnp.where(wide_lane == 0, outside, 0.0)
    outside_text = jnp.sum(jnp.where(is_image, 0.0, text_image), axis=1, keepdims=True)
    text_lane = lax.broadcasted_iota(jnp.int32, (LANES, images), 1)
    text_row = lax.broadcasted_iota(jnp.int32, (LANES, images), 0)
    text_image = jnp.where(is_image, text_image, 0.0) + jnp.where(
        text_lane == 0, outside_text, 0.0
    )
    text_image = jnp.where(text_row < POS, text_image, 0.0)
    first_lane = lax.broadcasted_iota(jnp.int32, (images, LANES), 1)
    left = pairs[:, :LANES] + jnp.where(first_lane < POS, by_position, 0.0)
    right = pairs[:, LANES:]
    a00, b00 = skewed(left[:LANES] + text_image[:, :LANES] + p_block)
    a01, b01 = skewed(right[:LANES] + text_image[:, LANES:])
    a10, b10 = skewed(left[LANES:])
    a11, b11 = skewed(right[LANES:])
    ax, bx = skewed(x_block)
    ay, by = skewed(y_block)
    diag_ref[head] = jnp.concatenate(
        [b10, b00 + b11 + a10, a00 + a11 + b01, a01, bx, ax, by, ay], axis=0
    )
    empty = jnp.zeros_like(dq)
    both = [dq * 0.125, empty] if parity == 0 else [empty, dq * 0.125]
    results = (
        (d_query, jnp.transpose(jnp.concatenate(both, axis=0))),
        (d_key, jnp.concatenate(dks, axis=0)),
        (d_value, jnp.concatenate(dvs, axis=0)),
    )
    for ref, value in results:
        if parity == 1:
            value = jnp.where(own, value, ref[pair].astype(F32))
        ref[pair] = value.astype(BF)


MESH = pl.DeviceIdType.MESH
VMEM = pl.BlockSpec(memory_space=pltpu.VMEM)
HBM = pl.BlockSpec(memory_space=pltpu.HBM)
MIB = 1024 * 1024


def remote(src, dst, send, receive, device):
    return pltpu.make_async_remote_copy(
        src_ref=src, dst_ref=dst, send_sem=send, recv_sem=receive, device_id=device,
        device_id_type=MESH,
    )


def project_kernel(
    layer_ref, weight_hbm, *refs,
):
    small_hbm, refs = refs[:10], refs[10:]
    (item_ref, projected_out, columns_ref, rows_ref, table_ref,
     projected_ref, weight_ref, meta_send, bias_ref, sems, load_sems, store_sems), small = (
        refs[:12], refs[12:],
    )
    (segment_ref, mask_ref, position_ref, across_ref, down_ref, query_bias_ref, value_bias_ref,
     text_ref, horiz_ref, vert_ref) = small
    mine = lax.axis_index("seq")
    partner = (1 - mine, lax.axis_index("dp"))
    count, width = layer_ref.shape[1:]
    own = pl.ds(pl.multiple_of(mine * count, LANES), count)
    loads = [
        pltpu.make_async_copy(source, target, load_sems.at[index])
        for index, (source, target) in enumerate(
            list(zip(small_hbm, small))
            + [(layer_ref.at[mine], item_ref.at[own]), (weight_hbm, weight_ref)]
        )
    ]
    for load in loads:
        load.start()
    barrier = pltpu.get_barrier_semaphore()
    pl.semaphore_signal(barrier, inc=1, device_id=partner, device_id_type=MESH)
    pl.semaphore_wait(barrier, 1)
    pieces = count // LANES
    rows_out = [
        remote(
            layer_ref.at[1 - mine, pl.ds(piece * LANES, LANES)],
            item_ref.at[pl.ds(pl.multiple_of(mine * count + piece * LANES, LANES), LANES)],
            sems.at[0, piece], sems.at[1, piece], partner,
        )
        for piece in range(pieces)
    ]
    for copy in rows_out:
        copy.start()
    for load in loads[:-2]:
        load.wait()

    fields = (segment_ref, mask_ref, position_ref, across_ref, down_ref)
    blocks = [
        jnp.concatenate(
            [field[item : item + 1, :] for field in fields] + [jnp.zeros((3, count), jnp.int32)],
            axis=0,
        )
        for item in range(2)
    ]
    meta_send[...] = jnp.where(mine == 0, blocks[1], blocks[0])
    meta_out = remote(
        meta_send, rows_ref.at[:, own], sems.at[0, pieces], sems.at[1, pieces], partner
    )
    meta_out.start()
    rows_ref[:, own] = jnp.where(mine == 0, blocks[0], blocks[1])
    bias_ref[:, :width] = query_bias_ref[...].astype(F32).reshape(1, width)
    bias_ref[:, width : 2 * width] = jnp.zeros((1, width), F32)
    bias_ref[:, 2 * width :] = value_bias_ref[...].astype(F32).reshape(1, width)
    heads, levels = text_ref.shape
    spot = lax.broadcasted_iota(jnp.int32, (levels, LANES), 1)
    level = lax.broadcasted_iota(jnp.int32, (levels, LANES), 0)
    table = jnp.zeros((heads, LANES), F32)
    for source, begin in ((text_ref, 0), (horiz_ref, X_TABLE), (vert_ref, Y_TABLE)):
        table = table + dot_nn(source[...], (spot == level + begin).astype(BF))
    table_ref[...] = jnp.concatenate([table, jnp.zeros((16 - heads, LANES), F32)], axis=0)

    def project(there):
        step = 256

        def body(index, carry):
            columns = pl.ds(pl.multiple_of(index * step, step), step)
            product = dot_nn(item_ref[there], weight_ref[:, columns])
            projected_ref[there, columns] = (product + bias_ref[:, columns]).astype(BF)
            return carry

        lax.fori_loop(0, 3 * width // step, body, 0)

    def stored(index, there):
        return pltpu.make_async_copy(
            projected_ref.at[there], projected_out.at[there], store_sems.at[index]
        )

    for load in loads[-2:]:
        load.wait()
    project(own)
    stored(0, own).start()
    for piece in range(pieces):
        rows_out[piece].wait()
        there = pl.ds(pl.multiple_of((1 - mine) * count + piece * LANES, LANES), LANES)
        project(there)
        stored(1 + piece, there).start()
    meta_out.wait()
    meta = rows_ref[...].astype(F32)
    tall = jnp.concatenate([meta, jnp.zeros((LANES - 8, meta.shape[1]), F32)], axis=0)
    columns_ref[...] = jnp.transpose(tall).astype(jnp.int32)
    stored(0, own).wait()
    for piece in range(pieces):
        there = pl.ds(pl.multiple_of((1 - mine) * count + piece * LANES, LANES), LANES)
        stored(1 + piece, there).wait()


def projected_item(layer_in, fields, qkv_weight, query_bias, value_bias, tables):
    rows = 2 * layer_in.shape[1]
    width = layer_in.shape[2]
    pieces = rows // 2 // LANES
    small = list(fields) + [query_bias, value_bias] + [t.T for t in tables]
    return pl.pallas_call(
        project_kernel,
        in_specs=[HBM] * (2 + len(small)),
        out_specs=[VMEM, HBM, VMEM, VMEM, VMEM],
        out_shape=[
            jax.ShapeDtypeStruct((rows, width), BF),
            jax.ShapeDtypeStruct((rows, 3 * width), BF),
            jax.ShapeDtypeStruct((rows, LANES), jnp.int32),
            jax.ShapeDtypeStruct((8, rows), jnp.int32),
            jax.ShapeDtypeStruct((16, LANES), F32),
        ],
        scratch_shapes=[
            pltpu.VMEM((rows, 3 * width), BF),
            pltpu.VMEM((width, 3 * width), BF),
            pltpu.VMEM((8, rows // 2), jnp.int32),
            pltpu.VMEM((1, 3 * width), F32),
            pltpu.SemaphoreType.DMA((2, pieces + 1)),
            pltpu.SemaphoreType.DMA((len(small) + 2,)),
            pltpu.SemaphoreType.DMA((pieces + 1,)),
        ]
        + [pltpu.VMEM(array.shape, array.dtype) for array in small],
        compiler_params=pltpu.CompilerParams(
            collective_id=1, has_side_effects=True, vmem_limit_bytes=60 * MIB
        ),
        name="projected_item",
    )(layer_in, qkv_weight, *small)


EPSILON = 1e-05
TILE = 256


def vector(ref):
    return ref[...].astype(F32).reshape(1, ref.shape[0])


def gelu_and_slope(x):
    bell = jnp.exp(-0.5 * x * x)
    t = 1.0 / (1.0 + 0.23164188826 * jnp.abs(x))
    series = t * (
        0.127414796
        + t * (-0.142248368 + t * (0.7107068705 + t * (-0.7265760135 + t * 0.5307027145)))
    )
    tail = bell * series
    below = jnp.where(x >= 0.0, 1.0 - tail, tail)
    return x * below, below + x * (0.3989422804014327 * bell)


def row_mean(block):
    return jnp.mean(block, axis=1, keepdims=True)


def normalized(hidden):
    center = hidden - row_mean(hidden)
    scale = lax.rsqrt(row_mean(center * center) + EPSILON)
    return center * scale, scale


def norm_pulled(grad, unit, scale):
    return scale * (grad - row_mean(grad) - unit * row_mean(grad * unit))


def column_sum(block):
    return jnp.sum(block, axis=0, keepdims=True)


def feed_kernel(
    item_ref, mixed_ref, cotangent_ref, out_weight_ref, up_ref, down_ref, *refs,
):
    vectors_hbm, refs = refs[:7], refs[7:]
    (layer_out, d_hidden_ref, d_mixed_ref, grad_out_ref, grad_down_ref, grad_up_ref, small_ref,
     layer_ref, cotangent_all, active, slope, unit, scale_ref, normed, normed_t, total, d_branch, d_branch_t,
     sems, load_sems) = refs[:20]
    vectors = refs[20:]
    (out_bias_ref, attn_gain_ref, attn_shift_ref, up_bias_ref, down_bias_ref, ffn_gain_ref,
     ffn_shift_ref) = vectors
    step = pl.program_id(0)
    blocks = pl.num_programs(0) // 2
    rows, width = item_ref.shape
    count = rows // 2
    mine = lax.axis_index("seq")
    partner = (1 - mine, lax.axis_index("dp"))
    own = pl.ds(pl.multiple_of(mine * count, LANES), count)
    tiles = rows // TILE

    def sent():
        return remote(
            cotangent_ref.at[1 - mine], cotangent_all.at[own], sems.at[0], sems.at[1], partner
        )

    def returned():
        theirs = pl.ds(pl.multiple_of((1 - mine) * count, LANES), count)
        return [
            pltpu.make_async_copy(layer_ref.at[own], layer_out.at[mine], load_sems.at[8]),
            remote(
                layer_ref.at[theirs], layer_out.at[mine], sems.at[2], sems.at[3], partner
            ),
        ]

    def loads():
        copies = list(zip(vectors_hbm, vectors)) + [(cotangent_ref.at[mine], cotangent_all.at[own])]
        return [
            pltpu.make_async_copy(source, target, load_sems.at[index])
            for index, (source, target) in enumerate(copies)
        ]

    def over_tiles(size, body, carry):
        def run(index, state):
            return body(pl.ds(pl.multiple_of(index * size, size), size), state)

        return lax.fori_loop(0, rows // size, run, carry)

    @pl.when(step == 0)
    def _():
        for load in loads():
            load.start()
        barrier = pltpu.get_barrier_semaphore()
        pl.semaphore_signal(barrier, inc=1, device_id=partner, device_id_type=MESH)
        pl.semaphore_wait(barrier, 1)
        sent().start()
        small_ref[...] = jnp.zeros_like(small_ref)
        for load in loads():
            load.wait()
        out_bias, gain, shift = vector(out_bias_ref), vector(attn_gain_ref), vector(attn_shift_ref)

        def tile(there, carry):
            attn = dot_nn(mixed_ref[there].astype(BF), out_weight_ref[...]) + out_bias
            standard, scale = normalized(item_ref[there].astype(F32) + attn)
            unit[there] = standard
            scale_ref[there] = jnp.broadcast_to(scale, (scale.shape[0], LANES))
            result = standard * gain + shift
            normed[there] = result.astype(BF)
            normed_t[:, there] = jnp.transpose(result).astype(BF)
            return carry

        over_tiles(TILE, tile, 0)
        total[...] = jnp.zeros_like(total)

    @pl.when(step < blocks)
    def _():
        columns = [slice(begin, begin + TILE) for begin in range(0, width, TILE)]
        low = normed[...]
        following = dot_nn(low, up_ref[:, columns[0]])
        values = []
        for index, here in enumerate(columns):
            product = following
            if index + 1 < len(columns):
                following = dot_nn(low, up_ref[:, columns[index + 1]])
            bias = up_bias_ref[pl.ds(pl.multiple_of(step * width + here.start, LANES), TILE)]
            value, grade = gelu_and_slope(product + bias.astype(F32).reshape(1, TILE))
            values.append(value.astype(BF))
            active[step, :, here] = values[-1]
            slope[step, :, here] = grade
        values = jnp.concatenate(values, axis=1)
        for here in columns:
            total[:, here] += dot_nn(values, down_ref[:, here])

    @pl.when(step == blocks)
    def _():
        sent().wait()
        gain, shift, bias = vector(ffn_gain_ref), vector(ffn_shift_ref), vector(down_bias_ref)
        first_gain, first_shift = vector(attn_gain_ref), vector(attn_shift_ref)

        def tile(there, sums):
            hidden = unit[there] * first_gain + first_shift + (total[there] + bias)
            standard, scale = normalized(hidden)
            layer_ref[there] = (standard * gain + shift).astype(BF)
            cotangent = cotangent_all[there].astype(F32)
            pulled = norm_pulled(cotangent * gain, standard, scale)
            total[there] = pulled
            low = pulled.astype(BF)
            d_branch[there] = low
            return (
                sums[0] + column_sum(low.astype(F32)),
                sums[1] + column_sum(cotangent * standard),
                sums[2] + column_sum(cotangent),
            )

        zero = jnp.zeros((1, width), F32)
        sums = over_tiles(64, tile, (zero, zero, zero))
        for row, value in zip((5, 6, 7), sums):
            small_ref[row : row + 1] = value

        for copy in returned():
            copy.start()

        def turn(there, carry):
            d_branch_t[:, there] = jnp.transpose(d_branch[there].astype(F32)).astype(BF)
            return carry

        over_tiles(TILE, turn, 0)

    @pl.when(step >= blocks)
    def _():
        block = step - blocks

        columns = [slice(begin, begin + TILE) for begin in range(0, width, TILE)]
        branch = d_branch[...]
        turned = d_branch_t[...]
        following = dot_nt(branch, down_ref[columns[0]])
        values = []
        for index, here in enumerate(columns):
            product = following
            if index + 1 < len(columns):
                following = dot_nt(branch, down_ref[columns[index + 1]])
            grad_down_ref[:, here] = dot_nn(turned, active[block, :, here]).astype(BF)
            d_up = (product * slope[block, :, here]).astype(BF)
            small_ref[pl.ds(8 + block, 1), here] = column_sum(d_up.astype(F32))
            values.append(d_up)
        values = jnp.concatenate(values, axis=1)
        turned = normed_t[...]
        for here in columns:
            grad_up_ref[:, here] = dot_nn(turned, values[:, here]).astype(BF)
            total[:, here] += dot_nt(values, up_ref[here])

    @pl.when(step == 2 * blocks - 1)
    def _():
        gain = vector(attn_gain_ref)

        def tile(there, sums):
            d_normed = total[there]
            standard = unit[there]
            d_hidden = norm_pulled(d_normed * gain, standard, scale_ref[there, :1])
            d_hidden_ref[there] = d_hidden
            low = d_hidden.astype(BF)
            d_branch[there] = low
            return (
                sums[0] + column_sum(low.astype(F32)),
                sums[1] + column_sum(d_normed * standard),
                sums[2] + column_sum(d_normed),
            )

        zero = jnp.zeros((1, width), F32)
        sums = over_tiles(64, tile, (zero, zero, zero))
        for row, value in zip((2, 3, 4), sums):
            small_ref[row : row + 1] = value

        def turn(there, carry):
            normed_t[:, there] = jnp.transpose(mixed_ref[there]).astype(BF)
            return carry

        over_tiles(TILE, turn, 0)

        for begin in range(0, width, TILE):
            here = slice(begin, begin + TILE)
            d_mixed_ref[:, here] = dot_nt(d_branch[...], out_weight_ref[here]).astype(BF)
            grad_out_ref[:, here] = dot_nn(normed_t[...], d_branch[:, here]).astype(BF)

        for copy in returned():
            copy.wait()


def fed_forward_and_back(
    item, mixed, cotangent, out_weight, up_weight, down_weight, vectors,
):
    rows, width = item.shape
    blocks = up_weight.shape[1] // width
    whole = pl.BlockSpec(memory_space=pltpu.VMEM)
    square = lambda kind: jax.ShapeDtypeStruct((rows, width), kind)
    later = lambda i: jnp.maximum(i - blocks, 0)
    return pl.pallas_call(
        feed_kernel,
        grid=(2 * blocks,),
        in_specs=[whole, whole, HBM, whole]
        + [
            pl.BlockSpec((width, width), lambda i: (0, lax.rem(i, blocks))),
            pl.BlockSpec((width, width), lambda i: (lax.rem(i, blocks), 0)),
        ]
        + [HBM] * 7,
        out_specs=[HBM] + [whole] * 3
        + [
            pl.BlockSpec((width, width), lambda i: (later(i), 0)),
            pl.BlockSpec((width, width), lambda i: (later(i), 0)),
            whole,
        ],
        out_shape=[
            jax.ShapeDtypeStruct((2, rows // 2, width), BF), square(F32), square(BF),
            jax.ShapeDtypeStruct((width, width), BF),
            jax.ShapeDtypeStruct((blocks * width, width), BF),
            jax.ShapeDtypeStruct((blocks * width, width), BF),
            jax.ShapeDtypeStruct((16, width), F32),
        ],
        scratch_shapes=[
            pltpu.VMEM((rows, width), BF),
            pltpu.VMEM((rows, width), BF),
            pltpu.VMEM((blocks, rows, width), BF),
            pltpu.VMEM((blocks, rows, width), F32),
            pltpu.VMEM((rows, width), F32),
            pltpu.VMEM((rows, LANES), F32),
            pltpu.VMEM((rows, width), BF),
            pltpu.VMEM((width, rows), BF),
            pltpu.VMEM((rows, width), F32),
            pltpu.VMEM((rows, width), BF),
            pltpu.VMEM((width, rows), BF),
            pltpu.SemaphoreType.DMA((4,)),
            pltpu.SemaphoreType.DMA((9,)),
        ]
        + [pltpu.VMEM(vector.shape, vector.dtype) for vector in vectors],
        compiler_params=pltpu.CompilerParams(
            collective_id=2, has_side_effects=True, vmem_limit_bytes=60 * MIB
        ),
        name="feed_forward",
    )(item, mixed, cotangent, out_weight, up_weight, down_weight, *vectors)


SLOTS = 4


def finish_kernel(
    summed_ref, input_hbm, small_ref, diagonal_ref,
    down_ref, up_ref, out_ref, qkv_ref, input_ref, *refs,
):
    singles, (blocks_in, slots, input_in, input_slot, in_sems, out_sems, item_sems) = (
        refs[:12], refs[12:],
    )
    blocks, width = blocks_in.shape[0], blocks_in.shape[2]
    hidden = down_ref.shape[0] // width

    def load(block):
        return pltpu.make_async_copy(
            summed_ref.at[pl.ds(block * width, width)], blocks_in.at[block], in_sems.at[block]
        )

    def stores(block):
        slot, sem = slots.at[block % SLOTS], out_sems.at[block % SLOTS]
        if block < hidden:
            targets = [(slot, down_ref.at[pl.ds(block * width, width)])]
        elif block < 2 * hidden:
            targets = [(slot, up_ref.at[:, pl.ds((block - hidden) * width, width)])]
        elif block == 2 * hidden:
            targets = [(slot, out_ref)]
        else:
            first = 2 * (block - 2 * hidden - 1)
            targets = [
                (
                    slot.at[:, pl.ds((3 * pair + part) * LANES, LANES)],
                    qkv_ref.at[:, pl.ds(part * width + (first + pair) * LANES, LANES)],
                )
                for pair in range(2) for part in range(3)
            ]
        return [
            pltpu.make_async_copy(source, target, sem.at[index])
            for index, (source, target) in enumerate(targets)
        ]

    load_input = pltpu.make_async_copy(input_hbm, input_in, item_sems.at[0])
    store_input = pltpu.make_async_copy(input_slot, input_ref, item_sems.at[1])
    for block in range(blocks):
        load(block).start()
    load_input.start()
    for block in range(blocks):
        load(block).wait()
        if block >= SLOTS:
            for copy in stores(block - SLOTS):
                copy.wait()
        piece = blocks_in[block].astype(F32)
        slots[block % SLOTS] = jnp.transpose(piece) if block < hidden else piece
        for copy in stores(block):
            copy.start()
    load_input.wait()
    input_slot[...] = input_in[...].astype(F32)
    store_input.start()
    for row in range(8):
        singles[row][...] = small_ref[row]
    for row in range(hidden):
        singles[8][row * width : row * width + width] = small_ref[8 + row]
    heads, levels = singles[9].shape
    diagonals = diagonal_ref[...]
    level = lax.broadcasted_iota(jnp.int32, (LANES, LANES), 1)
    lane = lax.broadcasted_iota(jnp.int32, (LANES, LANES), 0)
    for table, (first, size, skip) in enumerate(((0, 4, 0), (4, 2, 1), (6, 2, 1))):
        total = jnp.zeros((heads, LANES), F32)
        for row in range(size):
            distance = lane + LANES * (row + skip - 2)
            chosen = (bucket(distance) == level).astype(F32)
            total = total + jnp.dot(
                diagonals[:, first + row, :], chosen, preferred_element_type=F32,
                precision=lax.Precision.HIGHEST,
            )
        singles[9 + table][...] = total[:, :levels]
    for block in range(blocks - SLOTS, blocks):
        for copy in stores(block):
            copy.wait()
    store_input.wait()


def finished(summed, grad_input, small, diagonals, hidden, levels):
    width = summed.shape[1]
    heads = diagonals.shape[0]
    blocks = summed.shape[0] // width
    single = jax.ShapeDtypeStruct((width,), F32)
    table = jax.ShapeDtypeStruct((heads, levels), F32)
    dma = pltpu.SemaphoreType.DMA
    return pl.pallas_call(
        finish_kernel,
        in_specs=[HBM, HBM, VMEM, VMEM],
        out_specs=[HBM] * 5 + [VMEM] * 12,
        out_shape=[
            jax.ShapeDtypeStruct((hidden, width), F32),
            jax.ShapeDtypeStruct((width, hidden), F32),
            jax.ShapeDtypeStruct((width, width), F32),
            jax.ShapeDtypeStruct((width, 3 * width), F32),
            jax.ShapeDtypeStruct(grad_input.shape, F32),
        ]
        + [single] * 8
        + [jax.ShapeDtypeStruct((hidden,), F32)]
        + [table] * 3,
        scratch_shapes=[
            pltpu.VMEM((blocks, width, width), BF),
            pltpu.VMEM((SLOTS, width, width), F32),
            pltpu.VMEM(grad_input.shape, BF),
            pltpu.VMEM(grad_input.shape, F32),
            dma((blocks,)),
            dma((SLOTS, 6)),
            dma((2,)),
        ],
        compiler_params=pltpu.CompilerParams(vmem_limit_bytes=56 * MIB),
        name="finished",
    )(summed, grad_input, small, diagonals)


PIECE = 16


def hop_names(depth):
    names = ["x", "y"]
    reach = 1
    while reach < depth:
        names.append(f"z{reach}")
        reach *= 2
    return names


def route(depth, letters):
    names = hop_names(depth)
    line = {"a": names[2:3], "b": names[3:]}
    return [name for letter in letters for name in line.get(letter, [letter])]


class Place:
    def __init__(self, depth):
        place = lax.axis_index("dp")
        x = lax.axis_index("seq")
        core = lax.rem(place, 2)
        y = lax.rem(lax.div(place, 2), 2)
        z = lax.rem(lax.div(place, 4), depth)
        group = lax.div(place, 4 * depth)
        at = lambda sx, sc, sy, sz: (sx, (group * depth + sz) * 4 + sy * 2 + sc)
        self.bits = {"core": core, "x": x, "y": y}
        self.partners = {
            "core": at(x, 1 - core, y, z), "x": at(1 - x, core, y, z), "y": at(x, core, 1 - y, z),
        }
        reach = 1
        while reach < depth:
            up = lax.rem(lax.div(z, reach), 2)
            self.bits[f"z{reach}"] = up
            self.partners[f"z{reach}"] = at(x, core, y, z + reach - 2 * reach * up)
            reach *= 2

    def greet(self):
        barrier = pltpu.get_barrier_semaphore()
        for device in self.partners.values():
            pl.semaphore_signal(barrier, inc=1, device_id=device, device_id_type=MESH)
        pl.semaphore_wait(barrier, len(self.partners))


class Chunk:
    def __init__(self, place, depth, source, out_ref, offset, spot, scratch):
        _, self.begin, rows, first, columns, _, paths, _ = spot
        self.place, self.source, self.columns = place, source, pl.ds(first, columns)
        self.out_ref, self.out_begin = out_ref, offset + self.begin
        self.half, self.quarter = rows // 2, rows // 4
        self.routes = [route(depth, letters) for letters in paths.split()]
        self.hops = len(self.routes[0])
        self.stages = 2 * self.hops + 3
        self.work, self.fresh, *self.landing, self.sends, self.receives, self.locals = scratch

    def aligned(self, value):
        return pl.multiple_of(value, PIECE)

    def size(self, hop):
        return self.quarter >> (hop + 1)

    def base(self, part, hops):
        start = part * self.quarter
        for hop in range(hops):
            start = start + self.place.bits[self.routes[part][hop]] * self.size(hop)
        return start

    def across(self, part, hop):
        bit = self.place.bits[self.routes[part][hop]]
        return self.base(part, hop) + (1 - bit) * self.size(hop)

    def partner(self, part, hop):
        return self.place.partners[self.routes[part][hop]]

    def out(self, begin, size, core=None):
        core = self.place.bits["core"] if core is None else core
        return self.out_ref.at[
            pl.ds(self.aligned(self.out_begin + core * self.half + begin), size), self.columns
        ]

    def copy(self, index, source, target, device):
        return remote(source, target, self.sends.at[index], self.receives.at[index], device)

    def pair_down(self):
        core = self.place.bits["core"]
        at = lambda c: self.source.at[
            pl.ds(self.aligned(self.begin + c * self.half), self.half), self.columns
        ]
        return [
            self.copy(0, at(1 - core), self.fresh, self.place.partners["core"]),
            pltpu.make_async_copy(at(core), self.work, self.locals.at[0]),
        ]

    def pair_up(self, arriving):
        core = self.place.bits["core"]
        target = self.out(0, self.half, 1 - core if arriving else core)
        return [self.copy(1, self.out(0, self.half), target, self.place.partners["core"])]

    def down(self, hop):
        return [
            self.copy(
                2 + 2 * hop + part,
                self.work.at[pl.ds(self.aligned(self.across(part, hop)), self.size(hop))],
                self.landing[hop].at[part], self.partner(part, hop),
            )
            for part in range(2)
        ]

    def kept(self):
        size = self.size(self.hops - 1)
        copies = []
        for part in range(2):
            begin = self.aligned(self.base(part, self.hops))
            copies.append(
                pltpu.make_async_copy(
                    self.work.at[pl.ds(begin, size)], self.out(begin, size),
                    self.locals.at[1 + part],
                )
            )
        return copies

    def up(self, hop, arriving):
        copies = []
        for part in range(2):
            mine = self.base(part, hop + 1)
            size = self.size(hop)
            if hop == self.hops - 1:
                source = self.work.at[pl.ds(self.aligned(mine), size)]
            else:
                source = self.out(mine, size)
            target = self.out(self.across(part, hop) if arriving else mine, size)
            index = 2 + 2 * self.hops + 2 * hop + part
            copies.append(self.copy(index, source, target, self.partner(part, hop)))
        return copies

    def add(self, begin, source, size):
        step = 64 if size % 64 == 0 else min(size, PIECE)

        def body(index, carry):
            offset = self.aligned(index * step)
            there = pl.ds(self.aligned(begin + offset), step)
            total = self.work[there].astype(F32) + source[pl.ds(offset, step)].astype(F32)
            self.work[there] = total.astype(BF)
            return carry

        lax.fori_loop(0, size // step, body, 0)

    def stage(self, number):
        hops = self.hops
        ended, started = [], []
        if number == 0:
            started = self.pair_down()
        elif number == 1:
            ended = self.pair_down()
            started = self.down(0)
        elif number <= hops:
            ended = self.down(number - 2)
            started = self.down(number - 1)
        elif number == hops + 1:
            ended = self.down(hops - 1)
            started = self.up(hops - 1, False) + self.kept()
        elif number <= 2 * hops:
            level = 2 * hops + 1 - number
            ended = self.up(level, True) + (self.kept() if level == hops - 1 else [])
            started = self.up(level - 1, False)
        elif number == 2 * hops + 1:
            ended = self.up(0, True)
            started = self.pair_up(False)
        else:
            ended = self.pair_up(True)
        for copy in ended:
            copy.wait()
        if number == 1:
            self.add(0, self.fresh, self.half)
        elif 2 <= number <= hops + 1:
            hop = number - 2
            for part in range(2):
                self.add(self.base(part, hop + 1), self.landing[hop].at[part], self.size(hop))
        for copy in started:
            copy.start()


def chunk_scratch(rows, width, depth):
    hops = len(hop_names(depth))
    dma = pltpu.SemaphoreType.DMA
    return (
        [pltpu.VMEM((rows // 2, width), BF)] * 2
        + [pltpu.VMEM((2, rows // 4 >> (hop + 1), width), BF) for hop in range(hops)]
        + [dma((2 + 4 * hops,)), dma((2 + 4 * hops,)), dma((3,))]
    )


def planned(chunks, work, depth, hop_count):
    latency, issue, link, pair = 2.5, 0.2, 100e3, 350e3
    free = {}
    now = 0.0

    def sent(name, rows, columns):
        nonlocal now
        now += issue
        row_bytes = 2 * columns
        share = {"core": [("core", rows * row_bytes / pair)]}.get(name)
        if share is None:
            time = 2 * rows * row_bytes / link
            share = [(name, time)]
            if name[0] == "z":
                reach = int(name[1:])
                share = [("z end", time), ("z middle", 0.0 if reach == 1 else reach * time)]
        end = now
        for lane, time in share:
            free[lane] = max(now, free.get(lane, 0.0)) + time
            end = max(end, free[lane])
        return end + latency

    chains = []
    for rows, columns, need, paths, _ in chunks:
        paths = [route(depth, letters) for letters in paths.split()]
        down = []
        size = rows // 4
        for hop in range(len(paths[0])):
            size //= 2
            down.append([(path[hop], size, columns) for path in paths])
        pair_step = [[("core", rows // 2, columns)]]
        chains.append((need, pair_step + down + down[::-1] + pair_step))
    chains.append((len(work), [[("core", 16, 768)]] * hop_count))
    position = [0] * len(chains)
    ready = [0.0] * len(chains)
    ranks = [chunk[4] for chunk in chunks] + [0]
    order = [[] for _ in range(len(work) + 1)]
    done = 0
    while True:
        open_ones = [
            (ranks[i], ready[i], i) for i, (need, chain) in enumerate(chains)
            if position[i] <= len(chain) and need <= done
        ]
        due = [entry for entry in open_ones if entry[1] <= now]
        if not due and done < len(work):
            now += work[done]
            done += 1
            continue
        if not open_ones:
            return order
        _, when, index = min(due) if due else min(open_ones, key=lambda entry: entry[1])
        now = max(now, when)
        chain = chains[index][1]
        stage = position[index]
        order[done].append((index, stage))
        if 0 < stage <= len(chain) // 2:
            now += 2e-6 * sum(rows * wide for _, rows, wide in chain[stage - 1])
        if stage < len(chain):
            ready[index] = max(sent(*entry) for entry in chain[stage])
        position[index] += 1


def last_kernel(
    depth, plan, orders, *refs,
):
    (meta_ref, rows_ref, projected_hbm, mixed_hbm, grad_hbm, first_hbm, second_hbm, key_image_hbm,
     bias_hbm, small_ref, item_hbm, weight_hbm, d_hidden_hbm, grad_down_ref, grad_up_ref, grad_out_ref,
     out_ref, small_out, diagonal_out, input_out,
     *scratch) = refs
    static, scratch = scratch[:6], scratch[6:]
    (k_ref, v_ref, mixed_ref, grad_ref, first_ref, second_ref, key_image_ref, bias_ref, pair_sems,
     item_ref, weight_ref, total_ref, load_sems, d_query, d_key, d_value, item_t, tail, input_grad,
     small_in, diagonal_in, small_sems, item_sems, *scratch) = scratch
    place = Place(depth)
    step = pl.program_id(0)
    pairs = d_query.shape[0]
    rows, width = item_hbm.shape
    count = rows // 2
    x = place.bits["x"]
    sources = (grad_down_ref, grad_up_ref, tail)
    each = len(scratch) // len(plan)
    chunks = []
    for index, spot in enumerate(plan):
        offset = spot[0] * grad_down_ref.shape[0]
        chunks.append(
            Chunk(place, depth, sources[spot[0]], out_ref, offset, spot,
                  scratch[index * each : index * each + each])
        )
    hop_devices = list(place.partners.values())

    wide_hbm = (first_hbm, second_hbm, key_image_hbm, bias_hbm)
    wide_refs = (first_ref, second_ref, key_image_ref, bias_ref)

    def pair_loads(pair):
        copies = []
        held = (
            (projected_hbm, k_ref, width), (projected_hbm, v_ref, 2 * width),
            (mixed_hbm, mixed_ref, 0), (grad_hbm, grad_ref, 0),
        )
        for source, target, first in held:
            columns = pl.ds(pl.multiple_of(first + pair * LANES, LANES), LANES)
            copies.append((source.at[:, columns], target.at[pair]))
        heads = pl.ds(2 * pair, 2)
        for source, target in zip(wide_hbm, wide_refs):
            copies.append((source.at[heads], target.at[heads]))
        return [
            pltpu.make_async_copy(source, target, pair_sems.at[pair, index])
            for index, (source, target) in enumerate(copies)
        ]

    def loads():
        pairs_of = (
            (item_hbm, item_ref), (weight_hbm, weight_ref), (d_hidden_hbm, total_ref),
            (grad_out_ref, tail.at[pl.ds(0, width)]),
        )
        return [
            pltpu.make_async_copy(source, target, load_sems.at[index])
            for index, (source, target) in enumerate(pairs_of)
        ]

    def input_copies():
        return [
            pltpu.make_async_copy(
                input_grad.at[pl.ds(pl.multiple_of(x * count, LANES), count)], input_out.at[x],
                item_sems.at[0],
            ),
            remote(
                input_grad.at[pl.ds(pl.multiple_of((1 - x) * count, LANES), count)],
                input_out.at[x], item_sems.at[1], item_sems.at[2], place.partners["x"],
            ),
        ]

    def small_copies(hop):
        return [
            remote(source, landing.at[hop], small_sems.at[0, kind, hop],
                   small_sems.at[1, kind, hop], hop_devices[hop])
            for kind, (source, landing) in enumerate(
                ((small_out, small_in), (diagonal_out, diagonal_in))
            )
        ]

    def small_stage(hop):
        if hop > 0:
            for copy in small_copies(hop - 1):
                copy.wait()
            small_out[...] = small_out[...] + small_in[hop - 1]
            diagonal_out[...] = diagonal_out[...] + diagonal_in[hop - 1]
        if hop < len(hop_devices):
            for copy in small_copies(hop):
                copy.start()

    def perform(slot):
        for index, stage in orders[slot]:
            if index == len(chunks):
                small_stage(stage)
            else:
                chunks[index].stage(stage)

    @pl.when(step == 0)
    def _():
        for pair in range(pairs):
            for copy in pair_loads(pair):
                copy.start()
        for copy in loads():
            copy.start()
        place.greet()
        small_out[...] = small_ref[...]
        static_prepare(meta_ref, static)

    def slab(first):
        pieces = [
            (pair, part) for pair in (first, first + 1) for part in range(3)
        ]
        held = (d_query, d_key, d_value)
        base = width + first // 2 * width
        for left, right in zip(pieces[::2], pieces[1::2]):
            both = jnp.concatenate([held[part][pair] for pair, part in (left, right)], axis=1)
            weights = jnp.concatenate(
                [
                    weight_ref[:, part * width + pair * LANES : part * width + (pair + 1) * LANES]
                    for pair, part in (left, right)
                ],
                axis=1,
            )
            at = pieces.index(left) * LANES
            tail[base : base + width, at : at + 2 * LANES] = dot_nn(item_t[...], both).astype(BF)
            total_ref[...] += dot_nt(both, weights)
        for pair in (first, first + 1):
            columns = slice(pair * LANES, pair * LANES + LANES)
            small_out[0:1, columns] = column_sum(d_query[pair].astype(F32))
            small_out[1:2, columns] = column_sum(d_value[pair].astype(F32))

    @pl.when(step == 1)
    def _():
        for copy in loads():
            copy.wait()
        for tile in range(rows // TILE):
            there = slice(tile * TILE, tile * TILE + TILE)
            item_t[:, there] = jnp.transpose(item_ref[there].astype(F32)).astype(BF)

    for copy in pair_loads(step):
        copy.wait()
    for pair in range(pairs):
        @pl.when(step == pair)
        def _(pair=pair):
            perform(pair + pair // 2)

    for parity in range(2):
        head_back(
            parity, step, meta_ref, rows_ref, wide_refs, k_ref, v_ref, mixed_ref, grad_ref,
            static, d_query, d_key, d_value, diagonal_out,
        )

    for pair in range(1, pairs, 2):
        @pl.when(step == pair)
        def _(pair=pair):
            perform(pair + 1 + pair // 2)
            slab(pair - 1)

    @pl.when(step == pairs - 1)
    def _():
        input_grad[...] = total_ref[...].astype(BF)
        for copy in input_copies():
            copy.start()
        perform(len(orders) - 1)
        for copy in input_copies():
            copy.wait()


def summed_with_attention_back(
    meta_columns, meta_rows, projected, mixed, d_mixed, wide_arrays, item, qkv_weight,
    d_hidden, small, grad_down, grad_up, grad_out,
):
    size = lax.axis_size("dp")
    depth = 4 if size % 16 == 0 else size // 4
    rows, width = item.shape
    pairs = width // LANES
    hidden = grad_down.shape[0]
    hops = len(hop_names(depth)) + 1
    work = ([6.4] * 2 + [4.2]) * (pairs // 2)
    wide, slim = width // 2, width // 3
    plan = [
        (0, 0, 3072, 0, slim, 0, "xaby yabx", 0),
        (0, 0, 3072, slim, slim, 0, "xayb yxab", 0),
        (0, 0, 3072, 2 * slim, slim, 0, "yaxb xayb", 0),
        (1, 0, 2048, 0, width, 0, "yabx xyab", 1),
        (1, 2048, 1024, 0, width, 0, "abyx yaxb", 0),
        (2, 0, 1024, 0, wide, 3, "yabx xayb", 2),
        (2, 0, 1024, wide, wide, 3, "xyab yabx", 2),
        (2, 1024, 1024, 0, width, 6, "xyab yaxb", 1),
        (2, 2048, 1024, 0, wide, 9, "xayb yaxb", 2),
        (2, 2048, 1024, wide, wide, 9, "abyx yabx", 0),
    ]
    orders = planned([(spot[2],) + spot[4:] for spot in plan], work, depth, hops)

    whole = pl.BlockSpec(memory_space=pltpu.VMEM)
    diagonals = jax.ShapeDtypeStruct((2 * pairs, 8, LANES), F32)
    dma = pltpu.SemaphoreType.DMA
    scratch = []
    for spot in plan:
        scratch += chunk_scratch(spot[2], spot[4], depth)
    summed, small, diagonals, grad_input = pl.pallas_call(
        functools.partial(last_kernel, depth, plan, orders),
        grid=(pairs,),
        in_specs=[whole] * 2
        + [HBM] * 7
        + [whole]
        + [HBM] * 6,
        out_specs=[HBM, whole, whole, HBM],
        out_shape=[
            jax.ShapeDtypeStruct((3 * hidden, width), BF),
            jax.ShapeDtypeStruct(small.shape, F32),
            diagonals,
            jax.ShapeDtypeStruct((2, rows // 2, width), BF),
        ],
        scratch_shapes=[pltpu.VMEM((rows, LANES), BF)] * 3
        + [pltpu.VMEM((LANES, rows), BF)] * 3
        + [pltpu.VMEM((pairs, rows, LANES), kind) for kind in (BF, BF, F32, BF)]
        + [pltpu.VMEM(array.shape, BF) for array in wide_arrays]
        + [
            dma((pairs, 8)),
            pltpu.VMEM((rows, width), BF),
            pltpu.VMEM((width, 3 * width), BF),
            pltpu.VMEM((rows, width), F32),
            dma((4,)),
        ]
        + [pltpu.VMEM((pairs, rows, LANES), BF)] * 3
        + [
            pltpu.VMEM((width, rows), BF),
            pltpu.VMEM((hidden, width), BF),
            pltpu.VMEM((rows, width), BF),
            pltpu.VMEM((hops,) + small.shape, F32),
            pltpu.VMEM((hops,) + diagonals.shape, F32),
            dma((2, 2, hops)),
            dma((3,)),
        ]
        + scratch,
        compiler_params=pltpu.CompilerParams(
            collective_id=0, has_side_effects=True, vmem_limit_bytes=62 * MIB
        ),
        name="summed_with_attention_back",
    )(meta_columns, meta_rows, projected, mixed, d_mixed, *wide_arrays,
      small, item, qkv_weight, d_hidden, grad_down, grad_up, grad_out)
    span = 4 * depth
    if size > span:
        groups = [list(range(first, size, span)) for first in range(span)]
        summed, small, diagonals = lax.psum(
            (summed.astype(F32), small, diagonals), "dp", axis_index_groups=groups
        )
        summed = summed.astype(BF)
    return summed, small, diagonals, grad_input


def per_device(
    layer_in, segment, key_mask, position, layout_x, layout_y,
    qkv_weight, query_bias, value_bias, out_weight, out_bias, attn_gain, attn_shift,
    up_weight, up_bias, down_weight, down_bias, ffn_gain, ffn_shift,
    text_table, horiz_table, vert_table, cotangent,
):
    width = layer_in.shape[-1]
    item, projected, meta_columns, meta_rows, table_rows = projected_item(
        layer_in, (segment, key_mask, position, layout_x, layout_y),
        qkv_weight, query_bias, value_bias, (text_table, horiz_table, vert_table),
    )
    mixed, *wide_arrays = attention_forward(meta_columns, meta_rows, table_rows, projected, width)
    layer_out, d_hidden, d_mixed, grad_out, grad_down, grad_up, small = fed_forward_and_back(
        item, mixed, cotangent, out_weight, up_weight, down_weight,
        (out_bias, attn_gain, attn_shift, up_bias, down_bias, ffn_gain, ffn_shift),
    )
    summed, small, diagonals, grad_input = summed_with_attention_back(
        meta_columns, meta_rows, projected, mixed, d_mixed, wide_arrays, item, qkv_weight,
        d_hidden, small, grad_down, grad_up, grad_out,
    )
    done = finished(
        summed, grad_input, small, diagonals, up_weight.shape[1], text_table.shape[0]
    )
    sum_down, sum_up, sum_out, sum_qkv, grad_input = done[:5]
    singles, tables = done[5:14], [t.T for t in done[14:]]
    return (
        layer_out, grad_input, sum_qkv, singles[0], singles[1], sum_out, singles[2], singles[3],
        singles[4], sum_up, singles[8], sum_down, singles[5], singles[6], singles[7],
        tables[0], tables[1], tables[2],
    )


def solution(mesh):
    rows = P("dp", "seq", None)
    marks_spec = P("dp", "seq")
    return jax.shard_map(
        per_device,
        mesh=mesh,
        in_specs=(rows,) + (marks_spec,) * 5 + (P(),) * 16 + (rows,),
        out_specs=(rows, rows) + (P(),) * 16,
        check_vma=False,
    )
```

```python
import functools

import jax
import jax.numpy as jnp
from jax import lax
from jax.experimental import pallas as pl
from jax.experimental.pallas import tpu as pltpu
from jax.sharding import PartitionSpec as P

BF = jnp.bfloat16
F32 = jnp.float32
BIG = 1e30
LANES = 128
HEAD = 64
TEXT = 512
POS = 64
COORD = 48
Y0 = 64
GROUP0 = 112
MEMBER0 = 116
FLAG = 124
LOG0 = 125
X_TABLE = 33
Y_TABLE = 66
NOTHING = 127


def dot_nt(a, b):
    return lax.dot_general(a, b, (((1,), (1,)), ((), ())), preferred_element_type=F32)


def dot_nn(a, b):
    return lax.dot_general(a, b, (((1,), (0,)), ((), ())), preferred_element_type=F32)


def looked_up(table_row, index):
    rows = index.shape[0]
    return jnp.take_along_axis(
        jnp.broadcast_to(table_row, (rows, LANES)), index, axis=1, mode="promise_in_bounds"
    )


def bucket(distance):
    return jnp.clip(distance, -16, 16) + 16


def between(lane, low, high):
    return (lane >= low) & (lane < high)


def columns_of(meta_ref):
    return tuple(meta_ref[:, field : field + 1] for field in range(5))


def marks(meta_ref):
    segment, key_mask, position, across, down = columns_of(meta_ref)
    rows = segment.shape[0]
    lane = lax.broadcasted_iota(jnp.int32, (rows, LANES), 1)
    row = lax.broadcasted_iota(jnp.int32, (rows, LANES), 0)
    even = between(lane, HEAD, HEAD + COORD) & (lane - HEAD == across)
    odd = (lane < COORD) & (lane == across)
    group = (segment - 1) >> 3
    member = (segment - 1) & 7
    named = segment > 0
    shared = (
        ((row < TEXT) & (lane < POS) & (lane == position))
        | (between(lane, Y0, Y0 + COORD) & (lane - Y0 == down))
        | (named & between(lane, GROUP0, MEMBER0) & (lane - GROUP0 == group))
        | (named & between(lane, MEMBER0, FLAG) & (lane - MEMBER0 == member))
        | ((lane == FLAG) & (key_mask <= 0))
        | (lane >= LOG0)
    )
    return tuple(jnp.where(m, 1.0, 0.0).astype(BF) for m in (even, odd, shared))


def barred(meta_ref):
    segment = meta_ref[:, 0:1]
    rows = segment.shape[0]
    lane = lax.broadcasted_iota(jnp.int32, (rows, LANES), 1)
    group = (segment - 1) >> 3
    member = (segment - 1) & 7
    shut = (
        ((segment > 0) & between(lane, GROUP0, MEMBER0) & (lane - GROUP0 != group))
        | ((segment < 0) & between(lane, GROUP0, MEMBER0))
        | ((segment > 0) & between(lane, MEMBER0, FLAG) & (lane - MEMBER0 != member))
        | (lane == FLAG)
    )
    return jnp.where(shut, -BIG, 0.0).astype(F32)


def query_index(meta_ref):
    segment, key_mask, position, across, down = columns_of(meta_ref)
    rows = segment.shape[0]
    lane = lax.broadcasted_iota(jnp.int32, (rows, LANES), 1)
    x_even = bucket(across - (lane - HEAD)) + X_TABLE
    x_odd = bucket(across - lane) + X_TABLE
    even = jnp.where(between(lane, HEAD, HEAD + COORD), x_even, NOTHING)
    odd = jnp.where(lane < COORD, x_odd, NOTHING)
    shared = jnp.where(
        lane < POS,
        bucket(position - lane),
        jnp.where(between(lane, Y0, Y0 + COORD), bucket(down - (lane - Y0)) + Y_TABLE, NOTHING),
    )
    return even, odd, shared


def image_key_index(meta_ref):
    position = meta_ref[TEXT:, 2:3]
    lane = lax.broadcasted_iota(jnp.int32, (position.shape[0], LANES), 1)
    return jnp.where(lane < POS, bucket(lane - position), NOTHING)


def prepare(meta_ref, mark_refs, bar_ref, index_refs, key_index_ref):
    for ref, value in zip(mark_refs, marks(meta_ref)):
        ref[...] = value
    bar_ref[...] = barred(meta_ref)
    for ref, value in zip(index_refs, query_index(meta_ref)):
        ref[...] = value
    key_index_ref[...] = image_key_index(meta_ref)


def image_offsets(row_positions, column_positions):
    return bucket(column_positions - row_positions)


def own_lanes(parity, rows):
    lane = lax.broadcasted_iota(jnp.int32, (rows, LANES), 1)
    return (lane < HEAD) if parity == 0 else (lane >= HEAD)


def widened(parity, q, table_row, bar_ref, index_refs, key_index_ref, shared_ref):
    rows = q.shape[0]
    images = key_index_ref.shape[0]
    first = jnp.where(
        own_lanes(parity, rows),
        q.astype(F32) * 0.125,
        looked_up(table_row, index_refs[parity][...]),
    )
    second = looked_up(table_row, index_refs[2][...]) + bar_ref[...]
    image_lane = lax.broadcasted_iota(jnp.int32, (images, LANES), 1)
    key_image = jnp.where(
        image_lane < POS, looked_up(table_row, key_index_ref[...]).astype(BF), shared_ref[TEXT:]
    )
    return first.astype(BF), second, key_image


def joined(parity, first, second, key_image, k, marks_own, shared):
    rows = k.shape[0]
    lane = lax.broadcasted_iota(jnp.int32, (rows, LANES), 1)
    to_image = jnp.where(lane < POS, shared, second)
    key_first = jnp.where(own_lanes(parity, rows), k, marks_own)
    q_text = jnp.concatenate([first, second], axis=1)
    q_image = jnp.concatenate([first, to_image], axis=1)
    k_text = jnp.concatenate([key_first[:TEXT], shared[:TEXT]], axis=1)
    k_image = jnp.concatenate([key_first[TEXT:], key_image], axis=1)
    return q_text, q_image, k_text, k_image


def in_three(value):
    high = value.astype(BF).astype(F32)
    middle = (value - high).astype(BF).astype(F32)
    return high, middle, value - high - middle


def with_pieces(lane, start, value, otherwise):
    high, middle, lowest = in_three(value)
    return jnp.where(
        lane == start,
        -high,
        jnp.where(lane == start + 1, -middle, jnp.where(lane == start + 2, -lowest, otherwise)),
    )


def image_bias(table_row, offsets):
    return jnp.concatenate(
        [looked_up(table_row, offsets[:, :LANES]), looked_up(table_row, offsets[:, LANES:])], axis=1
    )


def forward_kernel(
    meta_ref, rows_ref, table_ref, q_ref, k_ref, v_ref,
    mixed_ref, first_ref, second_ref, key_image_ref, bias_ref,
    even_ref, odd_ref, shared_ref, bar_ref, index_even, index_odd, index_shared, key_index_ref,
):
    mark_refs = (even_ref, odd_ref, shared_ref)
    index_refs = (index_even, index_odd, index_shared)

    @pl.when(pl.program_id(0) == 0)
    def _():
        prepare(meta_ref, mark_refs, bar_ref, index_refs, key_index_ref)

    rows = q_ref.shape[0]
    images = rows - TEXT
    q, k, v = q_ref[...], k_ref[...], v_ref[...]
    offsets = bucket(rows_ref[2:3, TEXT:] - meta_ref[TEXT:, 2:3])
    tile = 256
    v_turned = transposed(v)
    heads = []
    seconds = []
    for parity in range(2):
        table_row = table_ref[pl.ds(2 * pl.program_id(0) + parity, 1), :]
        first, second, key_image = widened(
            parity, q, table_row, bar_ref, index_refs, key_index_ref, shared_ref
        )
        bias = image_bias(table_row, offsets)
        first_ref[parity] = first
        key_image_ref[parity] = key_image
        bias_ref[parity] = bias.astype(BF)
        seconds.append(second)
        wide = joined(
            parity, first, second.astype(BF), key_image, k, mark_refs[parity][...], shared_ref[...]
        )
        heads.append(wide + (bias,))

    def scored(parity, start):
        q_text, q_image, k_text, k_image, bias = heads[parity]
        here = slice(start, start + tile)
        on_image = dot_nt(k_image, q_image[here])
        if start >= TEXT:
            on_image = on_image + bias[:, start - TEXT : start - TEXT + tile]
        return dot_nt(k_text, q_text[here]), on_image

    spots = [(parity, start) for parity in range(2) for start in range(0, rows, tile)]
    outs = ([], [])
    logs = ([], [])
    following = scored(*spots[0])
    for index, (parity, start) in enumerate(spots):
        on_text, on_image = following
        if index + 1 < len(spots):
            following = scored(*spots[index + 1])
        top = jnp.maximum(
            jnp.max(on_text, axis=0, keepdims=True), jnp.max(on_image, axis=0, keepdims=True)
        )
        on_text = jnp.exp(on_text - top)
        on_image = jnp.exp(on_image - top)
        total = jnp.sum(on_text, axis=0, keepdims=True) + jnp.sum(on_image, axis=0, keepdims=True)
        own = slice(parity * HEAD, parity * HEAD + HEAD)
        out = dot_nn(v_turned[own, :TEXT], on_text.astype(BF)) + dot_nn(
            v_turned[own, TEXT:], on_image.astype(BF)
        )
        outs[parity].append(out * (1.0 / total))
        logs[parity].append(jnp.broadcast_to(top + jnp.log(total), (LANES, tile)))
    mixed_ref[...] = jnp.transpose(
        jnp.concatenate([jnp.concatenate(outs[parity], axis=1) for parity in range(2)], axis=0)
    )
    lane = lax.broadcasted_iota(jnp.int32, (rows, LANES), 1)
    for parity in range(2):
        totals = jnp.transpose(jnp.concatenate(logs[parity], axis=1))
        second_ref[parity] = with_pieces(lane, LOG0, totals, seconds[parity]).astype(BF)


def static_scratch(rows):
    return [
        pltpu.VMEM((rows, LANES), BF),
        pltpu.VMEM((rows, LANES), BF),
        pltpu.VMEM((rows, LANES), BF),
        pltpu.VMEM((rows, LANES), F32),
        pltpu.VMEM((rows, LANES), jnp.int32),
        pltpu.VMEM((rows, LANES), jnp.int32),
        pltpu.VMEM((rows, LANES), jnp.int32),
        pltpu.VMEM((rows - TEXT, LANES), jnp.int32),
    ]


def attention_forward(meta_columns, meta_rows, table_rows, projected, width):
    rows = projected.shape[0]
    images = rows - TEXT
    pairs = width // LANES

    def block(part):
        return pl.BlockSpec((rows, LANES), lambda p: (0, part * pairs + p))

    whole = lambda shape: pl.BlockSpec(shape, lambda p: (0,) * len(shape))
    return pl.pallas_call(
        forward_kernel,
        grid=(pairs,),
        in_specs=[
            whole(meta_columns.shape),
            whole(meta_rows.shape),
            whole(table_rows.shape),
            block(0), block(1), block(2),
        ],
        out_specs=[
            pl.BlockSpec((rows, LANES), lambda p: (0, p)),
            pl.BlockSpec((2, rows, LANES), lambda p: (p, 0, 0)),
            pl.BlockSpec((2, rows, LANES), lambda p: (p, 0, 0)),
            pl.BlockSpec((2, images, LANES), lambda p: (p, 0, 0)),
            pl.BlockSpec((2, images, images), lambda p: (p, 0, 0)),
        ],
        out_shape=[
            jax.ShapeDtypeStruct((rows, width), F32),
            jax.ShapeDtypeStruct((2 * pairs, rows, LANES), BF),
            jax.ShapeDtypeStruct((2 * pairs, rows, LANES), BF),
            jax.ShapeDtypeStruct((2 * pairs, images, LANES), BF),
            jax.ShapeDtypeStruct((2 * pairs, images, images), BF),
        ],
        scratch_shapes=static_scratch(rows),
        compiler_params=pltpu.CompilerParams(vmem_limit_bytes=60 * 1024 * 1024),
        name="attention_forward",
    )(meta_columns, meta_rows, table_rows, projected, projected, projected)


def skewed(block):
    size = block.shape[0]
    lane = lax.broadcasted_iota(jnp.int32, (size, LANES), 1)
    row = lax.broadcasted_iota(jnp.int32, (size, LANES), 0)
    turned = jnp.take_along_axis(
        block, (lane + row) & (LANES - 1), axis=1, mode="promise_in_bounds"
    )
    straight = lane + row < LANES
    above = jnp.sum(jnp.where(straight, turned, 0.0), axis=0, keepdims=True)
    below = jnp.sum(jnp.where(straight, 0.0, turned), axis=0, keepdims=True)
    return above, below


def transposed(array):
    return jnp.transpose(array.astype(F32)).astype(array.dtype)


def static_prepare(meta_ref, static):
    for ref, turned, value in zip(static[:3], static[3:], marks(meta_ref)):
        ref[...] = value
        turned[...] = transposed(value)


def head_back(
    parity, pair, rows_ref, wide_refs, k_ref, v_ref, mixed_ref, grad_ref, static, diag_ref,
):
    mark_refs, turned_refs = static[:3], static[3:]
    first_ref, second_ref, key_image_ref, bias_ref = wide_refs
    head = 2 * pair + parity
    shared_t = turned_refs[2]
    rows = k_ref.shape[1]
    images = rows - TEXT
    tile = 256
    k, v, grad = k_ref[pair], v_ref[pair], grad_ref[pair]
    lane = lax.broadcasted_iota(jnp.int32, (rows, LANES), 1)
    products = grad.astype(F32) * mixed_ref[pair]
    k_turned = transposed(k)
    is_image = rows_ref[1:2, TEXT:] > 0
    own = (lane < HEAD) if parity == 0 else (lane >= HEAD)
    spare = HEAD if parity == 0 else 0
    first, shared = first_ref[head], mark_refs[2][...]
    q_text, q_image, k_text, k_image = joined(
        parity, first, second_ref[head], key_image_ref[head], k, mark_refs[parity][...], shared
    )
    bias = bias_ref[head].astype(F32)
    half = lax.broadcasted_iota(jnp.int32, (LANES, LANES), 0)
    ones = jnp.where((half < HEAD) if parity == 0 else (half >= HEAD), 1.0, 0.0).astype(BF)
    delta = jnp.zeros((rows, LANES), F32)
    rest = products
    for _ in range(3):
        piece = rest.astype(BF)
        delta = delta + dot_nn(piece, ones)
        rest = rest - piece.astype(F32)
    grad_wide = jnp.where(
        own, grad.astype(F32), with_pieces(lane, spare, delta, 0.0)
    ).astype(BF)
    v_wide = jnp.where(
        own, v.astype(F32), jnp.where(between(lane, spare, spare + 3), 1.0, 0.0)
    ).astype(BF)
    q_marked = jnp.concatenate(
        [jnp.where(own, first, mark_refs[parity][...]), shared], axis=1
    )
    dq = jnp.zeros((HEAD, rows), F32)
    dks = []
    dvs = []
    first_sum = jnp.zeros((LANES, LANES), F32)
    second_sum = jnp.zeros((LANES, LANES), F32)
    text_image = jnp.zeros((LANES, images), F32)
    def scored(start):
        here = slice(start, start + tile)
        if start < TEXT:
            scores = dot_nt(k_text[here], q_text)
        else:
            scores = dot_nt(k_image[start - TEXT : start - TEXT + tile], q_image)
            scores = jnp.concatenate([scores[:, :TEXT], scores[:, TEXT:] + bias], axis=1)
        return scores, dot_nt(v_wide[here], grad_wide)

    following = scored(0)
    for start in range(0, rows, tile):
        here = slice(start, start + tile)
        scores, prob_grad = following
        if start + tile < rows:
            following = scored(start + tile)
        soft = jnp.exp(scores)
        score_grad = soft * prob_grad
        low = score_grad.astype(BF)
        dvs.append(dot_nn(soft.astype(BF), grad))
        wide = dot_nn(low, q_marked)
        dks.append(wide[:, :LANES])
        dq = dq + dot_nn(k_turned[parity * HEAD : parity * HEAD + HEAD, here], low)
        rounded = wide.astype(BF)
        first_sum = first_sum + dot_nn(turned_refs[parity][:, here], rounded[:, :LANES])
        second_sum = second_sum + dot_nn(shared_t[:, here], rounded[:, LANES:])
        if start < TEXT:
            text_image = text_image + dot_nn(shared_t[:, here], low[:, TEXT:])
        else:
            by_position = wide[:, LANES:]
            on_image = score_grad[:, TEXT:]
    small = lax.broadcasted_iota(jnp.int32, (LANES, LANES), 1)
    small_row = lax.broadcasted_iota(jnp.int32, (LANES, LANES), 0)
    x0 = HEAD if parity == 0 else 0
    x_block = jnp.where(
        between(small, x0, x0 + COORD) & between(small_row, x0, x0 + COORD), first_sum, 0.0
    )
    y_block = jnp.where(
        between(small, Y0, Y0 + COORD) & between(small_row, Y0, Y0 + COORD), second_sum, 0.0
    )
    p_block = jnp.where((small < POS) & (small_row < POS), second_sum, 0.0)
    wide_lane = lax.broadcasted_iota(jnp.int32, (images, images), 1)
    outside = jnp.sum(jnp.where(is_image, 0.0, on_image), axis=1, keepdims=True)
    pairs = jnp.where(is_image, on_image, 0.0) + jnp.where(wide_lane == 0, outside, 0.0)
    outside_text = jnp.sum(jnp.where(is_image, 0.0, text_image), axis=1, keepdims=True)
    text_lane = lax.broadcasted_iota(jnp.int32, (LANES, images), 1)
    text_row = lax.broadcasted_iota(jnp.int32, (LANES, images), 0)
    text_image = jnp.where(is_image, text_image, 0.0) + jnp.where(
        text_lane == 0, outside_text, 0.0
    )
    text_image = jnp.where(text_row < POS, text_image, 0.0)
    first_lane = lax.broadcasted_iota(jnp.int32, (images, LANES), 1)
    left = pairs[:, :LANES] + jnp.where(first_lane < POS, by_position, 0.0)
    right = pairs[:, LANES:]
    a00, b00 = skewed(left[:LANES] + text_image[:, :LANES] + p_block)
    a01, b01 = skewed(right[:LANES] + text_image[:, LANES:])
    a10, b10 = skewed(left[LANES:])
    a11, b11 = skewed(right[LANES:])
    ax, bx = skewed(x_block)
    ay, by = skewed(y_block)
    diag_ref[head] = jnp.concatenate(
        [b10, b00 + b11 + a10, a00 + a11 + b01, a01, bx, ax, by, ay], axis=0
    )
    return dq * 0.125, jnp.concatenate(dks, axis=0), jnp.concatenate(dvs, axis=0)


MESH = pl.DeviceIdType.MESH
VMEM = pl.BlockSpec(memory_space=pltpu.VMEM)
HBM = pl.BlockSpec(memory_space=pltpu.HBM)
MIB = 1024 * 1024


def remote(src, dst, send, receive, device):
    return pltpu.make_async_remote_copy(
        src_ref=src, dst_ref=dst, send_sem=send, recv_sem=receive, device_id=device,
        device_id_type=MESH,
    )


def project_kernel(
    layer_ref, weight_hbm, *refs,
):
    small_hbm, refs = refs[:10], refs[10:]
    (item_ref, projected_out, columns_ref, rows_ref, table_ref,
     projected_ref, weight_ref, meta_send, bias_ref, sems, load_sems, store_sems), small = (
        refs[:12], refs[12:],
    )
    (segment_ref, mask_ref, position_ref, across_ref, down_ref, query_bias_ref, value_bias_ref,
     text_ref, horiz_ref, vert_ref) = small
    mine = lax.axis_index("seq")
    partner = (1 - mine, lax.axis_index("dp"))
    count, width = layer_ref.shape[1:]
    own = pl.ds(pl.multiple_of(mine * count, LANES), count)
    loads = [
        pltpu.make_async_copy(source, target, load_sems.at[index])
        for index, (source, target) in enumerate(
            list(zip(small_hbm, small))
            + [(layer_ref.at[mine], item_ref.at[own]), (weight_hbm, weight_ref)]
        )
    ]
    for load in loads:
        load.start()
    barrier = pltpu.get_barrier_semaphore()
    pl.semaphore_signal(barrier, inc=1, device_id=partner, device_id_type=MESH)
    pl.semaphore_wait(barrier, 1)
    pieces = count // LANES
    rows_out = [
        remote(
            layer_ref.at[1 - mine, pl.ds(piece * LANES, LANES)],
            item_ref.at[pl.ds(pl.multiple_of(mine * count + piece * LANES, LANES), LANES)],
            sems.at[0, piece], sems.at[1, piece], partner,
        )
        for piece in range(pieces)
    ]
    for copy in rows_out:
        copy.start()
    for load in loads[:-2]:
        load.wait()

    fields = (segment_ref, mask_ref, position_ref, across_ref, down_ref)
    blocks = [
        jnp.concatenate(
            [field[item : item + 1, :] for field in fields] + [jnp.zeros((3, count), jnp.int32)],
            axis=0,
        )
        for item in range(2)
    ]
    meta_send[...] = jnp.where(mine == 0, blocks[1], blocks[0])
    meta_out = remote(
        meta_send, rows_ref.at[:, own], sems.at[0, pieces], sems.at[1, pieces], partner
    )
    meta_out.start()
    rows_ref[:, own] = jnp.where(mine == 0, blocks[0], blocks[1])
    bias_ref[:, :width] = query_bias_ref[...].astype(F32).reshape(1, width)
    bias_ref[:, width : 2 * width] = jnp.zeros((1, width), F32)
    bias_ref[:, 2 * width :] = value_bias_ref[...].astype(F32).reshape(1, width)
    heads, levels = text_ref.shape
    spot = lax.broadcasted_iota(jnp.int32, (levels, LANES), 1)
    level = lax.broadcasted_iota(jnp.int32, (levels, LANES), 0)
    table = jnp.zeros((heads, LANES), F32)
    for source, begin in ((text_ref, 0), (horiz_ref, X_TABLE), (vert_ref, Y_TABLE)):
        table = table + dot_nn(source[...], (spot == level + begin).astype(BF))
    table_ref[...] = jnp.concatenate([table, jnp.zeros((16 - heads, LANES), F32)], axis=0)

    def project(there):
        step = 256

        def body(index, carry):
            columns = pl.ds(pl.multiple_of(index * step, step), step)
            product = dot_nn(item_ref[there], weight_ref[:, columns])
            projected_ref[there, columns] = (product + bias_ref[:, columns]).astype(BF)
            return carry

        lax.fori_loop(0, 3 * width // step, body, 0)

    def stored(index, there):
        return pltpu.make_async_copy(
            projected_ref.at[there], projected_out.at[there], store_sems.at[index]
        )

    for load in loads[-2:]:
        load.wait()
    project(own)
    stored(0, own).start()
    for piece in range(pieces):
        rows_out[piece].wait()
        there = pl.ds(pl.multiple_of((1 - mine) * count + piece * LANES, LANES), LANES)
        project(there)
        stored(1 + piece, there).start()
    meta_out.wait()
    meta = rows_ref[...].astype(F32)
    tall = jnp.concatenate([meta, jnp.zeros((LANES - 8, meta.shape[1]), F32)], axis=0)
    columns_ref[...] = jnp.transpose(tall).astype(jnp.int32)
    stored(0, own).wait()
    for piece in range(pieces):
        there = pl.ds(pl.multiple_of((1 - mine) * count + piece * LANES, LANES), LANES)
        stored(1 + piece, there).wait()


def projected_item(layer_in, fields, qkv_weight, query_bias, value_bias, tables):
    rows = 2 * layer_in.shape[1]
    width = layer_in.shape[2]
    pieces = rows // 2 // LANES
    small = list(fields) + [query_bias, value_bias] + [t.T for t in tables]
    return pl.pallas_call(
        project_kernel,
        in_specs=[HBM] * (2 + len(small)),
        out_specs=[VMEM, HBM, VMEM, VMEM, VMEM],
        out_shape=[
            jax.ShapeDtypeStruct((rows, width), BF),
            jax.ShapeDtypeStruct((rows, 3 * width), BF),
            jax.ShapeDtypeStruct((rows, LANES), jnp.int32),
            jax.ShapeDtypeStruct((8, rows), jnp.int32),
            jax.ShapeDtypeStruct((16, LANES), F32),
        ],
        scratch_shapes=[
            pltpu.VMEM((rows, 3 * width), BF),
            pltpu.VMEM((width, 3 * width), BF),
            pltpu.VMEM((8, rows // 2), jnp.int32),
            pltpu.VMEM((1, 3 * width), F32),
            pltpu.SemaphoreType.DMA((2, pieces + 1)),
            pltpu.SemaphoreType.DMA((len(small) + 2,)),
            pltpu.SemaphoreType.DMA((pieces + 1,)),
        ]
        + [pltpu.VMEM(array.shape, array.dtype) for array in small],
        compiler_params=pltpu.CompilerParams(
            collective_id=1, has_side_effects=True, vmem_limit_bytes=60 * MIB
        ),
        name="projected_item",
    )(layer_in, qkv_weight, *small)


EPSILON = 1e-05
TILE = 256


def vector(ref):
    return ref[...].astype(F32).reshape(1, ref.shape[0])


def gelu_and_slope(x):
    bell = jnp.exp2(-0.7213475204444817 * (x * x))
    rough = 1.0 + 0.23164188826 * jnp.abs(x)
    t = pl.reciprocal(rough, approx=True)
    t = t * (2.0 - rough * t)
    series = t * (
        0.127414796
        + t * (-0.142248368 + t * (0.7107068705 + t * (-0.7265760135 + t * 0.5307027145)))
    )
    tail = bell * series
    below = jnp.where(x >= 0.0, 1.0 - tail, tail)
    return x * below, below + x * (0.3989422804014327 * bell)


def row_mean(block):
    return jnp.mean(block, axis=1, keepdims=True)


def normalized(hidden):
    center = hidden - row_mean(hidden)
    scale = lax.rsqrt(row_mean(center * center) + EPSILON)
    return center * scale, scale


def norm_pulled(grad, unit, scale):
    return scale * (grad - row_mean(grad) - unit * row_mean(grad * unit))


def column_sum(block):
    return jnp.sum(block, axis=0, keepdims=True)


def feed_kernel(
    item_ref, mixed_ref, cotangent_ref, out_weight_ref, up_ref, down_ref, *refs,
):
    vectors_hbm, refs = refs[:7], refs[7:]
    (layer_out, d_hidden_ref, d_mixed_ref, grad_out_ref, grad_down_ref, grad_up_ref, small_ref,
     layer_ref, cotangent_all, active, slope, unit, scale_ref, normed, normed_t, total, d_branch, d_branch_t,
     sems, load_sems) = refs[:20]
    vectors = refs[20:]
    (out_bias_ref, attn_gain_ref, attn_shift_ref, up_bias_ref, down_bias_ref, ffn_gain_ref,
     ffn_shift_ref) = vectors
    step = pl.program_id(0)
    blocks = pl.num_programs(0) // 2
    rows, width = item_ref.shape
    count = rows // 2
    mine = lax.axis_index("seq")
    partner = (1 - mine, lax.axis_index("dp"))
    own = pl.ds(pl.multiple_of(mine * count, LANES), count)
    tiles = rows // TILE

    def sent():
        return remote(
            cotangent_ref.at[1 - mine], cotangent_all.at[own], sems.at[0], sems.at[1], partner
        )

    def returned():
        theirs = pl.ds(pl.multiple_of((1 - mine) * count, LANES), count)
        return [
            pltpu.make_async_copy(layer_ref.at[own], layer_out.at[mine], load_sems.at[8]),
            remote(
                layer_ref.at[theirs], layer_out.at[mine], sems.at[2], sems.at[3], partner
            ),
        ]

    def loads():
        copies = list(zip(vectors_hbm, vectors)) + [(cotangent_ref.at[mine], cotangent_all.at[own])]
        return [
            pltpu.make_async_copy(source, target, load_sems.at[index])
            for index, (source, target) in enumerate(copies)
        ]

    def over_tiles(size, body, carry):
        def run(index, state):
            return body(pl.ds(pl.multiple_of(index * size, size), size), state)

        return lax.fori_loop(0, rows // size, run, carry)

    @pl.when(step == 0)
    def _():
        for load in loads():
            load.start()
        barrier = pltpu.get_barrier_semaphore()
        pl.semaphore_signal(barrier, inc=1, device_id=partner, device_id_type=MESH)
        pl.semaphore_wait(barrier, 1)
        sent().start()
        small_ref[...] = jnp.zeros_like(small_ref)
        for load in loads():
            load.wait()
        out_bias, gain, shift = vector(out_bias_ref), vector(attn_gain_ref), vector(attn_shift_ref)

        def tile(there, carry):
            attn = dot_nn(mixed_ref[there].astype(BF), out_weight_ref[...]) + out_bias
            standard, scale = normalized(item_ref[there].astype(F32) + attn)
            unit[there] = standard
            scale_ref[there] = jnp.broadcast_to(scale, (scale.shape[0], LANES))
            result = standard * gain + shift
            normed[there] = result.astype(BF)
            normed_t[:, there] = jnp.transpose(result).astype(BF)
            return carry

        over_tiles(TILE, tile, 0)
        total[...] = jnp.zeros_like(total)

    @pl.when(step < blocks)
    def _():
        columns = [slice(begin, begin + TILE) for begin in range(0, width, TILE)]
        low = normed[...]
        following = dot_nn(low, up_ref[:, columns[0]])
        values = []
        for index, here in enumerate(columns):
            product = following
            if index + 1 < len(columns):
                following = dot_nn(low, up_ref[:, columns[index + 1]])
            bias = up_bias_ref[pl.ds(pl.multiple_of(step * width + here.start, LANES), TILE)]
            value, grade = gelu_and_slope(product + bias.astype(F32).reshape(1, TILE))
            values.append(value.astype(BF))
            active[step, :, here] = values[-1]
            slope[step, :, here] = grade
        values = jnp.concatenate(values, axis=1)
        for here in columns:
            total[:, here] += dot_nn(values, down_ref[:, here])

    @pl.when(step == blocks)
    def _():
        sent().wait()
        gain, shift, bias = vector(ffn_gain_ref), vector(ffn_shift_ref), vector(down_bias_ref)
        first_gain, first_shift = vector(attn_gain_ref), vector(attn_shift_ref)

        def tile(there, sums):
            hidden = unit[there] * first_gain + first_shift + (total[there] + bias)
            standard, scale = normalized(hidden)
            layer_ref[there] = (standard * gain + shift).astype(BF)
            cotangent = cotangent_all[there].astype(F32)
            pulled = norm_pulled(cotangent * gain, standard, scale)
            total[there] = pulled
            low = pulled.astype(BF)
            d_branch[there] = low
            return (
                sums[0] + column_sum(low.astype(F32)),
                sums[1] + column_sum(cotangent * standard),
                sums[2] + column_sum(cotangent),
            )

        zero = jnp.zeros((1, width), F32)
        sums = over_tiles(64, tile, (zero, zero, zero))
        for row, value in zip((5, 6, 7), sums):
            small_ref[row : row + 1] = value

        for copy in returned():
            copy.start()

        def turn(there, carry):
            d_branch_t[:, there] = jnp.transpose(d_branch[there].astype(F32)).astype(BF)
            return carry

        over_tiles(TILE, turn, 0)

    @pl.when(step >= blocks)
    def _():
        block = step - blocks

        columns = [slice(begin, begin + TILE) for begin in range(0, width, TILE)]
        branch = d_branch[...]
        turned = d_branch_t[...]
        following = dot_nt(branch, down_ref[columns[0]])
        values = []
        for index, here in enumerate(columns):
            product = following
            if index + 1 < len(columns):
                following = dot_nt(branch, down_ref[columns[index + 1]])
            grad_down_ref[:, here] = dot_nn(turned, active[block, :, here]).astype(BF)
            d_up = (product * slope[block, :, here]).astype(BF)
            small_ref[pl.ds(8 + block, 1), here] = column_sum(d_up.astype(F32))
            values.append(d_up)
        values = jnp.concatenate(values, axis=1)
        turned = normed_t[...]
        for here in columns:
            grad_up_ref[:, here] = dot_nn(turned, values[:, here]).astype(BF)
            total[:, here] += dot_nt(values, up_ref[here])

    @pl.when(step == 2 * blocks - 1)
    def _():
        gain = vector(attn_gain_ref)

        def tile(there, sums):
            d_normed = total[there]
            standard = unit[there]
            d_hidden = norm_pulled(d_normed * gain, standard, scale_ref[there, :1])
            d_hidden_ref[there] = d_hidden
            low = d_hidden.astype(BF)
            d_branch[there] = low
            return (
                sums[0] + column_sum(low.astype(F32)),
                sums[1] + column_sum(d_normed * standard),
                sums[2] + column_sum(d_normed),
            )

        zero = jnp.zeros((1, width), F32)
        sums = over_tiles(64, tile, (zero, zero, zero))
        for row, value in zip((2, 3, 4), sums):
            small_ref[row : row + 1] = value

        def turn(there, carry):
            normed_t[:, there] = jnp.transpose(mixed_ref[there]).astype(BF)
            return carry

        over_tiles(TILE, turn, 0)

        for begin in range(0, width, TILE):
            here = slice(begin, begin + TILE)
            d_mixed_ref[:, here] = dot_nt(d_branch[...], out_weight_ref[here]).astype(BF)
            grad_out_ref[:, here] = dot_nn(normed_t[...], d_branch[:, here]).astype(BF)

        for copy in returned():
            copy.wait()


def fed_forward_and_back(
    item, mixed, cotangent, out_weight, up_weight, down_weight, vectors,
):
    rows, width = item.shape
    blocks = up_weight.shape[1] // width
    whole = pl.BlockSpec(memory_space=pltpu.VMEM)
    square = lambda kind: jax.ShapeDtypeStruct((rows, width), kind)
    later = lambda i: jnp.maximum(i - blocks, 0)
    return pl.pallas_call(
        feed_kernel,
        grid=(2 * blocks,),
        in_specs=[whole, whole, HBM, whole]
        + [
            pl.BlockSpec((width, width), lambda i: (0, lax.rem(i, blocks))),
            pl.BlockSpec((width, width), lambda i: (lax.rem(i, blocks), 0)),
        ]
        + [HBM] * 7,
        out_specs=[HBM] + [whole] * 3
        + [
            pl.BlockSpec((width, width), lambda i: (later(i), 0)),
            pl.BlockSpec((width, width), lambda i: (later(i), 0)),
            whole,
        ],
        out_shape=[
            jax.ShapeDtypeStruct((2, rows // 2, width), BF), square(F32), square(BF),
            jax.ShapeDtypeStruct((width, width), BF),
            jax.ShapeDtypeStruct((blocks * width, width), BF),
            jax.ShapeDtypeStruct((blocks * width, width), BF),
            jax.ShapeDtypeStruct((16, width), F32),
        ],
        scratch_shapes=[
            pltpu.VMEM((rows, width), BF),
            pltpu.VMEM((rows, width), BF),
            pltpu.VMEM((blocks, rows, width), BF),
            pltpu.VMEM((blocks, rows, width), F32),
            pltpu.VMEM((rows, width), F32),
            pltpu.VMEM((rows, LANES), F32),
            pltpu.VMEM((rows, width), BF),
            pltpu.VMEM((width, rows), BF),
            pltpu.VMEM((rows, width), F32),
            pltpu.VMEM((rows, width), BF),
            pltpu.VMEM((width, rows), BF),
            pltpu.SemaphoreType.DMA((4,)),
            pltpu.SemaphoreType.DMA((9,)),
        ]
        + [pltpu.VMEM(vector.shape, vector.dtype) for vector in vectors],
        compiler_params=pltpu.CompilerParams(
            collective_id=2, has_side_effects=True, vmem_limit_bytes=60 * MIB
        ),
        name="feed_forward",
    )(item, mixed, cotangent, out_weight, up_weight, down_weight, *vectors)


SLOTS = 4


def finish_kernel(
    main_ref, tail_ref, input_hbm, small_ref, diagonal_ref,
    down_ref, up_ref, out_ref, qkv_ref, input_ref, *refs,
):
    singles, (main_in, tail_in, slots, input_in, input_slot, in_sems, out_sems, item_sems) = (
        refs[:12], refs[12:],
    )
    mains, width = main_in.shape[0], main_in.shape[2]
    pairs, across = tail_in.shape[0], tail_in.shape[2]
    hidden = mains // 2
    blocks = mains + pairs

    def load(block):
        if block < mains:
            source, target = main_ref.at[pl.ds(block * width, width)], main_in.at[block]
        else:
            pair = block - mains
            source, target = tail_ref.at[pl.ds(pair * TAIL_ROWS, TAIL_ROWS)], tail_in.at[pair]
        return pltpu.make_async_copy(source, target, in_sems.at[block])

    def stores(block):
        slot, sem = slots.at[block % SLOTS], out_sems.at[block % SLOTS]
        if block < hidden:
            targets = [(slot, down_ref.at[pl.ds(block * width, width)])]
        elif block < mains:
            targets = [(slot, up_ref.at[:, pl.ds((block - hidden) * width, width)])]
        else:
            pair = block - mains
            targets = [
                (
                    slot.at[:, pl.ds(part * LANES, LANES)],
                    qkv_ref.at[:, pl.ds(part * width + pair * LANES, LANES)],
                )
                for part in range(3)
            ]
            down = pl.ds(0, TAIL_ROWS - width)
            targets.append(
                (slot.at[down, pl.ds(across, across)], out_ref.at[out_spot(pair, pairs, width)])
            )
        return [
            pltpu.make_async_copy(source, target, sem.at[index])
            for index, (source, target) in enumerate(targets)
        ]

    load_input = pltpu.make_async_copy(input_hbm, input_in, item_sems.at[0])
    store_input = pltpu.make_async_copy(input_slot, input_ref, item_sems.at[1])
    for block in range(blocks):
        load(block).start()
    load_input.start()
    for block in range(blocks):
        load(block).wait()
        if block >= SLOTS:
            for copy in stores(block - SLOTS):
                copy.wait()
        slot = block % SLOTS
        if block < hidden:
            slots[slot] = jnp.transpose(main_in[block].astype(F32))
        elif block < mains:
            slots[slot] = main_in[block].astype(F32)
        else:
            slots[slot, :, :across] = tail_in[block - mains, :width].astype(F32)
            slots[slot, : TAIL_ROWS - width, across:] = tail_in[block - mains, width:].astype(F32)
        for copy in stores(block):
            copy.start()
    load_input.wait()
    input_slot[...] = input_in[...].astype(F32)
    store_input.start()
    for row in range(8):
        singles[row][...] = small_ref[row]
    for row in range(hidden):
        singles[8][row * width : row * width + width] = small_ref[8 + row]
    heads, levels = singles[9].shape
    diagonals = diagonal_ref[...]
    level = lax.broadcasted_iota(jnp.int32, (LANES, LANES), 1)
    lane = lax.broadcasted_iota(jnp.int32, (LANES, LANES), 0)
    for table, (first, size, skip) in enumerate(((0, 4, 0), (4, 2, 1), (6, 2, 1))):
        total = jnp.zeros((heads, LANES), F32)
        for row in range(size):
            distance = lane + LANES * (row + skip - 2)
            chosen = (bucket(distance) == level).astype(F32)
            total = total + jnp.dot(
                diagonals[:, first + row, :], chosen, preferred_element_type=F32,
                precision=lax.Precision.HIGHEST,
            )
        singles[9 + table][...] = total[:, :levels]
    for block in range(blocks - SLOTS, blocks):
        for copy in stores(block):
            copy.wait()
    store_input.wait()


def finished(main, tail, grad_input, small, diagonals, hidden, levels):
    width = main.shape[1]
    heads = diagonals.shape[0]
    mains = main.shape[0] // width
    pairs = tail.shape[0] // TAIL_ROWS
    single = jax.ShapeDtypeStruct((width,), F32)
    table = jax.ShapeDtypeStruct((heads, levels), F32)
    dma = pltpu.SemaphoreType.DMA
    return pl.pallas_call(
        finish_kernel,
        in_specs=[HBM, HBM, HBM, VMEM, VMEM],
        out_specs=[HBM] * 5 + [VMEM] * 12,
        out_shape=[
            jax.ShapeDtypeStruct((hidden, width), F32),
            jax.ShapeDtypeStruct((width, hidden), F32),
            jax.ShapeDtypeStruct((width, width), F32),
            jax.ShapeDtypeStruct((width, 3 * width), F32),
            jax.ShapeDtypeStruct(grad_input.shape, F32),
        ]
        + [single] * 8
        + [jax.ShapeDtypeStruct((hidden,), F32)]
        + [table] * 3,
        scratch_shapes=[
            pltpu.VMEM((mains, width, width), BF),
            pltpu.VMEM((pairs, TAIL_ROWS, tail.shape[1]), BF),
            pltpu.VMEM((SLOTS, width, width), F32),
            pltpu.VMEM(grad_input.shape, BF),
            pltpu.VMEM(grad_input.shape, F32),
            dma((mains + pairs,)),
            dma((SLOTS, 4)),
            dma((2,)),
        ],
        compiler_params=pltpu.CompilerParams(vmem_limit_bytes=56 * MIB),
        name="finished",
    )(main, tail, grad_input, small, diagonals)


PIECE = 16


def hop_names(depth):
    names = ["x", "y"]
    reach = 1
    while reach < depth:
        names.append(f"z{reach}")
        reach *= 2
    return names


def route(depth, letters):
    names = hop_names(depth)
    line = {"a": names[2:3], "b": names[3:]}
    return [name for letter in letters for name in line.get(letter, [letter])]


class Place:
    def __init__(self, depth):
        place = lax.axis_index("dp")
        x = lax.axis_index("seq")
        core = lax.rem(place, 2)
        y = lax.rem(lax.div(place, 2), 2)
        z = lax.rem(lax.div(place, 4), depth)
        group = lax.div(place, 4 * depth)
        at = lambda sx, sc, sy, sz: (sx, (group * depth + sz) * 4 + sy * 2 + sc)
        self.bits = {"core": core, "x": x, "y": y}
        self.partners = {
            "core": at(x, 1 - core, y, z), "x": at(1 - x, core, y, z), "y": at(x, core, 1 - y, z),
        }
        reach = 1
        while reach < depth:
            up = lax.rem(lax.div(z, reach), 2)
            self.bits[f"z{reach}"] = up
            self.partners[f"z{reach}"] = at(x, core, y, z + reach - 2 * reach * up)
            reach *= 2

    def greet(self):
        barrier = pltpu.get_barrier_semaphore()
        for device in self.partners.values():
            pl.semaphore_signal(barrier, inc=1, device_id=device, device_id_type=MESH)
        pl.semaphore_wait(barrier, len(self.partners))


class Chunk:
    def __init__(self, place, depth, source, out_ref, offset, spot, scratch):
        _, self.begin, rows, first, columns, _, paths, _ = spot
        self.place, self.source, self.columns = place, source, pl.ds(first, columns)
        self.out_ref, self.out_begin = out_ref, offset + self.begin
        self.half, self.quarter = rows // 2, rows // 4
        self.routes = [route(depth, letters) for letters in paths.split()]
        self.hops = len(self.routes[0])
        self.stages = 2 * self.hops + 3
        self.work, self.fresh, *self.landing, self.sends, self.receives, self.locals = scratch

    def aligned(self, value):
        return pl.multiple_of(value, PIECE)

    def size(self, hop):
        return self.quarter >> (hop + 1)

    def base(self, part, hops):
        start = part * self.quarter
        for hop in range(hops):
            start = start + self.place.bits[self.routes[part][hop]] * self.size(hop)
        return start

    def across(self, part, hop):
        bit = self.place.bits[self.routes[part][hop]]
        return self.base(part, hop) + (1 - bit) * self.size(hop)

    def partner(self, part, hop):
        return self.place.partners[self.routes[part][hop]]

    def out(self, begin, size, core=None):
        core = self.place.bits["core"] if core is None else core
        return self.out_ref.at[
            pl.ds(self.aligned(self.out_begin + core * self.half + begin), size), self.columns
        ]

    def copy(self, index, source, target, device):
        return remote(source, target, self.sends.at[index], self.receives.at[index], device)

    def pair_down(self):
        core = self.place.bits["core"]
        at = lambda c: self.source.at[
            pl.ds(self.aligned(self.begin + c * self.half), self.half), self.columns
        ]
        return [
            self.copy(0, at(1 - core), self.fresh, self.place.partners["core"]),
            pltpu.make_async_copy(at(core), self.work, self.locals.at[0]),
        ]

    def pair_up(self, arriving):
        core = self.place.bits["core"]
        target = self.out(0, self.half, 1 - core if arriving else core)
        return [self.copy(1, self.out(0, self.half), target, self.place.partners["core"])]

    def down(self, hop):
        return [
            self.copy(
                2 + 2 * hop + part,
                self.work.at[pl.ds(self.aligned(self.across(part, hop)), self.size(hop))],
                self.landing[hop].at[part], self.partner(part, hop),
            )
            for part in range(2)
        ]

    def kept(self):
        size = self.size(self.hops - 1)
        copies = []
        for part in range(2):
            begin = self.aligned(self.base(part, self.hops))
            copies.append(
                pltpu.make_async_copy(
                    self.work.at[pl.ds(begin, size)], self.out(begin, size),
                    self.locals.at[1 + part],
                )
            )
        return copies

    def up(self, hop, arriving):
        copies = []
        for part in range(2):
            mine = self.base(part, hop + 1)
            size = self.size(hop)
            if hop == self.hops - 1:
                source = self.work.at[pl.ds(self.aligned(mine), size)]
            else:
                source = self.out(mine, size)
            target = self.out(self.across(part, hop) if arriving else mine, size)
            index = 2 + 2 * self.hops + 2 * hop + part
            copies.append(self.copy(index, source, target, self.partner(part, hop)))
        return copies

    def add(self, begin, source, size):
        step = 64 if size % 64 == 0 else min(size, PIECE)

        def body(index, carry):
            offset = self.aligned(index * step)
            there = pl.ds(self.aligned(begin + offset), step)
            self.work[there] = self.work[there] + source[pl.ds(offset, step)]
            return carry

        lax.fori_loop(0, size // step, body, 0)

    def stage(self, number):
        hops = self.hops
        ended, started = [], []
        if number == 0:
            started = self.pair_down()
        elif number == 1:
            ended = self.pair_down()
            started = self.down(0)
        elif number <= hops:
            ended = self.down(number - 2)
            started = self.down(number - 1)
        elif number == hops + 1:
            ended = self.down(hops - 1)
            started = self.up(hops - 1, False) + self.kept()
        elif number <= 2 * hops:
            level = 2 * hops + 1 - number
            ended = self.up(level, True) + (self.kept() if level == hops - 1 else [])
            started = self.up(level - 1, False)
        elif number == 2 * hops + 1:
            ended = self.up(0, True)
            started = self.pair_up(False)
        else:
            ended = self.pair_up(True)
        for copy in ended:
            copy.wait()
        if number == 1:
            self.add(0, self.fresh, self.half)
        elif 2 <= number <= hops + 1:
            hop = number - 2
            for part in range(2):
                self.add(self.base(part, hop + 1), self.landing[hop].at[part], self.size(hop))
        for copy in started:
            copy.start()


def chunk_scratch(rows, width, depth):
    hops = len(hop_names(depth))
    dma = pltpu.SemaphoreType.DMA
    return (
        [pltpu.VMEM((rows // 2, width), BF)] * 2
        + [pltpu.VMEM((2, rows // 4 >> (hop + 1), width), BF) for hop in range(hops)]
        + [dma((2 + 4 * hops,)), dma((2 + 4 * hops,)), dma((3,))]
    )


def planned(chunks, work, depth, hop_count):
    latency, issue, link, pair = 2.5, 0.08, 100e3, 600e3
    free = {}
    now = 0.0

    def sent(name, rows, columns):
        nonlocal now
        now += issue
        row_bytes = 2 * columns
        share = {"core": [("core", rows * row_bytes / pair)]}.get(name)
        if share is None:
            time = 2 * rows * row_bytes / link
            share = [(name, time)]
            if name[0] == "z":
                reach = int(name[1:])
                share = [("z end", time), ("z middle", 0.0 if reach == 1 else reach * time)]
        end = now
        for lane, time in share:
            free[lane] = max(now, free.get(lane, 0.0)) + time
            end = max(end, free[lane])
        return end + latency

    chains = []
    for rows, columns, need, paths, _ in chunks:
        paths = [route(depth, letters) for letters in paths.split()]
        down = []
        size = rows // 4
        for hop in range(len(paths[0])):
            size //= 2
            down.append([(path[hop], size, columns) for path in paths])
        pair_step = [[("core", rows // 2, columns)]]
        chains.append((need, pair_step + down + down[::-1] + pair_step))
    chains.append((len(work), [[("core", 16, 768)]] * hop_count))
    position = [0] * len(chains)
    ready = [0.0] * len(chains)
    ranks = [chunk[4] for chunk in chunks] + [0]
    order = [[] for _ in range(len(work) + 1)]
    done = 0
    while True:
        open_ones = [
            (ranks[i], ready[i], i) for i, (need, chain) in enumerate(chains)
            if position[i] <= len(chain) and need <= done
        ]
        due = [entry for entry in open_ones if entry[1] <= now]
        if not due and done < len(work):
            now += work[done]
            done += 1
            continue
        if not open_ones:
            return order
        _, when, index = min(due) if due else min(open_ones, key=lambda entry: entry[1])
        now = max(now, when)
        chain = chains[index][1]
        stage = position[index]
        order[done].append((index, stage))
        if 0 < stage <= len(chain) // 2:
            now += 2e-6 * sum(rows * wide for _, rows, wide in chain[stage - 1])
        if stage < len(chain):
            ready[index] = max(sent(*entry) for entry in chain[stage])
        position[index] += 1


def last_kernel(
    depth, plan, orders, *refs,
):
    (meta_ref, rows_ref, projected_hbm, mixed_hbm, grad_hbm, first_hbm, second_hbm, key_image_hbm,
     bias_hbm, small_ref, item_hbm, weight_hbm, d_hidden_hbm, grad_down_ref, grad_up_ref,
     grad_out_ref,
     main_out, tail_out, small_out, diagonal_out, input_out,
     *scratch) = refs
    static, scratch = scratch[:6], scratch[6:]
    (k_ref, v_ref, mixed_ref, grad_ref, first_ref, second_ref, key_image_ref, bias_ref, pair_sems,
     item_ref, weight_ref, d_hidden_ref, load_sems, d_project, item_t, tail, input_grad,
     small_in, diagonal_in, small_sems, item_sems, *scratch) = scratch
    place = Place(depth)
    step = pl.program_id(0)
    pairs = k_ref.shape[0]
    rows, width = item_hbm.shape
    count = rows // 2
    x = place.bits["x"]
    hidden = grad_down_ref.shape[0]
    sources = ((grad_down_ref, main_out, 0), (grad_up_ref, main_out, hidden), (tail, tail_out, 0))
    each = len(scratch) // len(plan)
    chunks = []
    for index, spot in enumerate(plan):
        chunks.append(
            Chunk(place, depth, *sources[spot[0]], spot, scratch[index * each : index * each + each])
        )
    hop_devices = list(place.partners.values())
    wide_hbm = (first_hbm, second_hbm, key_image_hbm, bias_hbm)
    wide_refs = (first_ref, second_ref, key_image_ref, bias_ref)

    def pair_loads(pair):
        copies = []
        held = (
            (projected_hbm, k_ref, width), (projected_hbm, v_ref, 2 * width),
            (mixed_hbm, mixed_ref, 0), (grad_hbm, grad_ref, 0),
        )
        for source, target, first in held:
            columns = pl.ds(pl.multiple_of(first + pair * LANES, LANES), LANES)
            copies.append((source.at[:, columns], target.at[pair]))
        heads = pl.ds(2 * pair, 2)
        for source, target in zip(wide_hbm, wide_refs):
            copies.append((source.at[heads], target.at[heads]))
        return [
            pltpu.make_async_copy(source, target, pair_sems.at[pair, index])
            for index, (source, target) in enumerate(copies)
        ]

    def loads():
        copies = [(item_hbm, item_ref), (weight_hbm, weight_ref), (d_hidden_hbm, d_hidden_ref)]
        for pair in range(pairs):
            down, across = out_spot(pair, pairs, width)
            copies.append(
                (
                    grad_out_ref.at[down, across],
                    tail.at[pl.ds(pair * TAIL_ROWS + width, TAIL_ROWS - width)],
                )
            )
        return [
            pltpu.make_async_copy(source, target, load_sems.at[index])
            for index, (source, target) in enumerate(copies)
        ]

    def input_copies():
        return [
            pltpu.make_async_copy(
                input_grad.at[pl.ds(pl.multiple_of(x * count, LANES), count)], input_out.at[x],
                item_sems.at[0],
            ),
            remote(
                input_grad.at[pl.ds(pl.multiple_of((1 - x) * count, LANES), count)],
                input_out.at[x], item_sems.at[1], item_sems.at[2], place.partners["x"],
            ),
        ]

    def small_copies(hop):
        return [
            remote(source, landing.at[hop], small_sems.at[0, kind, hop],
                   small_sems.at[1, kind, hop], hop_devices[hop])
            for kind, (source, landing) in enumerate(
                ((small_out, small_in), (diagonal_out, diagonal_in))
            )
        ]

    def small_stage(hop):
        if hop > 0:
            for copy in small_copies(hop - 1):
                copy.wait()
            small_out[...] = small_out[...] + small_in[hop - 1]
            diagonal_out[...] = diagonal_out[...] + diagonal_in[hop - 1]
        if hop < len(hop_devices):
            for copy in small_copies(hop):
                copy.start()

    def perform(slot):
        for index, stage in orders[slot]:
            if index == len(chunks):
                small_stage(stage)
            else:
                chunks[index].stage(stage)

    @pl.when(step == 0)
    def _():
        for pair in range(pairs):
            for copy in pair_loads(pair):
                copy.start()
        for copy in loads():
            copy.start()
        place.greet()
        small_out[...] = small_ref[...]

    for pair in range(pairs):
        @pl.when(step == pair)
        def _(pair=pair):
            perform(pair)

    @pl.when(step == 0)
    def _():
        static_prepare(meta_ref, static)
        for copy in loads():
            copy.wait()
        for tile in range(rows // TILE):
            there = slice(tile * TILE, tile * TILE + TILE)
            item_t[:, there] = jnp.transpose(item_ref[there].astype(F32)).astype(BF)

    for copy in pair_loads(step):
        copy.wait()
    (dq_even, dk_even, dv_even), (dq_odd, dk_odd, dv_odd) = [
        head_back(
            parity, step, rows_ref, wide_refs, k_ref, v_ref, mixed_ref, grad_ref, static,
            diagonal_out,
        )
        for parity in range(2)
    ]
    even = own_lanes(0, rows)
    pieces = [
        jnp.transpose(jnp.concatenate([dq_even, dq_odd], axis=0)).astype(BF),
        jnp.where(even, dk_even, dk_odd).astype(BF),
        jnp.where(even, dv_even, dv_odd).astype(BF),
    ]
    for part, piece in enumerate(pieces):
        d_project[:, pl.ds(pl.multiple_of(part * width + step * LANES, LANES), LANES)] = piece
    slab = pl.ds(pl.multiple_of(step * TAIL_ROWS, TAIL_ROWS), width)
    tail[slab] = dot_nn(item_t[...], jnp.concatenate(pieces, axis=1)).astype(BF)

    @pl.when(step == pairs - 1)
    def _():
        perform(pairs)
        for begin in range(0, width, TILE):
            here = slice(begin, begin + TILE)
            total = d_hidden_ref[:, here] + dot_nt(d_project[...], weight_ref[here])
            input_grad[:, here] = total.astype(BF)
        for copy in input_copies():
            copy.start()
        for begin in range(0, width, TILE):
            here = slice(begin, begin + TILE)
            there = slice(2 * width + begin, 2 * width + begin + TILE)
            small_out[0:1, here] = column_sum(d_project[:, here].astype(F32))
            small_out[1:2, here] = column_sum(d_project[:, there].astype(F32))
        perform(pairs + 1)
        for copy in input_copies():
            copy.wait()


TAIL_ROWS = 1024


def out_spot(pair, pairs, width):
    down = TAIL_ROWS - width
    across = width * width // (pairs * down)
    per_row = width // across
    return (
        pl.ds(pair // per_row * down, down),
        pl.ds(pair % per_row * across, across),
    )


def summed_with_attention_back(
    meta_columns, meta_rows, projected, mixed, d_mixed, wide_arrays, item, qkv_weight,
    d_hidden, small, grad_down, grad_up, grad_out,
):
    size = lax.axis_size("dp")
    depth = 4 if size % 16 == 0 else size // 4
    rows, width = item.shape
    pairs = width // LANES
    hidden = grad_down.shape[0]
    hops = len(hop_names(depth)) + 1
    work = [7.5] * pairs + [4.0]
    tall, wide = 1024, 3 * LANES
    plan = [
        (0, 0, tall, 0, width, 0, "yabx yxab", 1),
        (0, tall, tall, 0, width, 0, "yabx xaby", 0),
        (0, 2 * tall, tall, 0, width, 0, "yaxb xyab", 3),
        (1, 0, 2 * tall, 0, width, 0, "xaby axby", 2),
        (1, 2 * tall, tall, 0, width, 0, "xayb yaxb", 0),
        (2, 0, tall, 0, wide, 1, "xyab yxab", 0),
        (2, tall, tall, 0, wide, 2, "yaxb yxab", 3),
        (2, 2 * tall, tall, 0, wide, 3, "xyab yabx", 0),
        (2, 3 * tall, tall, 0, wide, 4, "xayb axby", 2),
        (2, 4 * tall, tall, 0, wide, 5, "yabx xyab", 1),
        (2, 5 * tall, tall, 0, wide, 6, "yxab xyab", 3),
    ]
    orders = planned([(spot[2],) + spot[4:] for spot in plan], work, depth, hops)

    whole = pl.BlockSpec(memory_space=pltpu.VMEM)
    diagonals = jax.ShapeDtypeStruct((2 * pairs, 8, LANES), F32)
    dma = pltpu.SemaphoreType.DMA
    scratch = []
    for spot in plan:
        scratch += chunk_scratch(spot[2], spot[4], depth)
    main, tail, small, diagonals, grad_input = pl.pallas_call(
        functools.partial(last_kernel, depth, plan, orders),
        grid=(pairs,),
        in_specs=[whole] * 2 + [HBM] * 7 + [whole] + [HBM] * 6,
        out_specs=[HBM, HBM, whole, whole, HBM],
        out_shape=[
            jax.ShapeDtypeStruct((2 * hidden, width), BF),
            jax.ShapeDtypeStruct((pairs * TAIL_ROWS, 3 * LANES), BF),
            jax.ShapeDtypeStruct(small.shape, F32),
            diagonals,
            jax.ShapeDtypeStruct((2, rows // 2, width), BF),
        ],
        scratch_shapes=[pltpu.VMEM((rows, LANES), BF)] * 3
        + [pltpu.VMEM((LANES, rows), BF)] * 3
        + [pltpu.VMEM((pairs, rows, LANES), kind) for kind in (BF, BF, F32, BF)]
        + [pltpu.VMEM(array.shape, BF) for array in wide_arrays]
        + [
            dma((pairs, 8)),
            pltpu.VMEM((rows, width), BF),
            pltpu.VMEM((width, 3 * width), BF),
            pltpu.VMEM((rows, width), F32),
            dma((3 + pairs,)),
            pltpu.VMEM((rows, 3 * width), BF),
            pltpu.VMEM((width, rows), BF),
            pltpu.VMEM((pairs * TAIL_ROWS, 3 * LANES), BF),
            pltpu.VMEM((rows, width), BF),
            pltpu.VMEM((hops,) + small.shape, F32),
            pltpu.VMEM((hops,) + diagonals.shape, F32),
            dma((2, 2, hops)),
            dma((3,)),
        ]
        + scratch,
        compiler_params=pltpu.CompilerParams(
            collective_id=0, has_side_effects=True, vmem_limit_bytes=62 * MIB
        ),
        name="summed_with_attention_back",
    )(meta_columns, meta_rows, projected, mixed, d_mixed, *wide_arrays,
      small, item, qkv_weight, d_hidden, grad_down, grad_up, grad_out)
    span = 4 * depth
    if size > span:
        groups = [list(range(first, size, span)) for first in range(span)]
        main, tail, small, diagonals = lax.psum(
            (main.astype(F32), tail.astype(F32), small, diagonals), "dp",
            axis_index_groups=groups,
        )
        main, tail = main.astype(BF), tail.astype(BF)
    return main, tail, small, diagonals, grad_input


def per_device(
    layer_in, segment, key_mask, position, layout_x, layout_y,
    qkv_weight, query_bias, value_bias, out_weight, out_bias, attn_gain, attn_shift,
    up_weight, up_bias, down_weight, down_bias, ffn_gain, ffn_shift,
    text_table, horiz_table, vert_table, cotangent,
):
    width = layer_in.shape[-1]
    item, projected, meta_columns, meta_rows, table_rows = projected_item(
        layer_in, (segment, key_mask, position, layout_x, layout_y),
        qkv_weight, query_bias, value_bias, (text_table, horiz_table, vert_table),
    )
    mixed, *wide_arrays = attention_forward(meta_columns, meta_rows, table_rows, projected, width)
    layer_out, d_hidden, d_mixed, grad_out, grad_down, grad_up, small = fed_forward_and_back(
        item, mixed, cotangent, out_weight, up_weight, down_weight,
        (out_bias, attn_gain, attn_shift, up_bias, down_bias, ffn_gain, ffn_shift),
    )
    main, tail, small, diagonals, grad_input = summed_with_attention_back(
        meta_columns, meta_rows, projected, mixed, d_mixed, wide_arrays, item, qkv_weight,
        d_hidden, small, grad_down, grad_up, grad_out,
    )
    done = finished(
        main, tail, grad_input, small, diagonals, up_weight.shape[1], text_table.shape[0]
    )
    sum_down, sum_up, sum_out, sum_qkv, grad_input = done[:5]
    singles, tables = done[5:14], [t.T for t in done[14:]]
    return (
        layer_out, grad_input, sum_qkv, singles[0], singles[1], sum_out, singles[2], singles[3],
        singles[4], sum_up, singles[8], sum_down, singles[5], singles[6], singles[7],
        tables[0], tables[1], tables[2],
    )


def solution(mesh):
    rows = P("dp", "seq", None)
    marks_spec = P("dp", "seq")
    return jax.shard_map(
        per_device,
        mesh=mesh,
        in_specs=(rows,) + (marks_spec,) * 5 + (P(),) * 16 + (rows,),
        out_specs=(rows, rows) + (P(),) * 16,
        check_vma=False,
    )
```

```python
import functools

import jax
import jax.numpy as jnp
from jax import lax
from jax.experimental import pallas as pl
from jax.experimental.pallas import tpu as pltpu
from jax.sharding import PartitionSpec as P

BF = jnp.bfloat16
F32 = jnp.float32
BIG = 1e30
LANES = 128
HEAD = 64
TEXT = 512
POS = 64
COORD = 48
Y0 = 64
GROUP0 = 112
MEMBER0 = 116
FLAG = 124
X_TABLE = 33
Y_TABLE = 66
NOTHING = 127


def dot_nt(a, b):
    return lax.dot_general(a, b, (((1,), (1,)), ((), ())), preferred_element_type=F32)


def dot_nn(a, b):
    return lax.dot_general(a, b, (((1,), (0,)), ((), ())), preferred_element_type=F32)


def looked_up(table_row, index):
    rows = index.shape[0]
    return jnp.take_along_axis(
        jnp.broadcast_to(table_row, (rows, LANES)), index, axis=1, mode="promise_in_bounds"
    )


def bucket(distance):
    return jnp.clip(distance, -16, 16) + 16


def between(lane, low, high):
    return (lane >= low) & (lane < high)


def columns_of(meta_ref):
    return tuple(meta_ref[:, field : field + 1] for field in range(5))


def marks(meta_ref):
    segment, key_mask, position, across, down = columns_of(meta_ref)
    rows = segment.shape[0]
    lane = lax.broadcasted_iota(jnp.int32, (rows, LANES), 1)
    row = lax.broadcasted_iota(jnp.int32, (rows, LANES), 0)
    even = between(lane, HEAD, HEAD + COORD) & (lane - HEAD == across)
    odd = (lane < COORD) & (lane == across)
    group = (segment - 1) >> 3
    member = (segment - 1) & 7
    named = segment > 0
    shared = (
        ((row < TEXT) & (lane < POS) & (lane == position))
        | (between(lane, Y0, Y0 + COORD) & (lane - Y0 == down))
        | (named & between(lane, GROUP0, MEMBER0) & (lane - GROUP0 == group))
        | (named & between(lane, MEMBER0, FLAG) & (lane - MEMBER0 == member))
        | ((lane == FLAG) & (key_mask <= 0))
    )
    return tuple(jnp.where(m, 1.0, 0.0).astype(BF) for m in (even, odd, shared))


def barred(meta_ref):
    segment = meta_ref[:, 0:1]
    rows = segment.shape[0]
    lane = lax.broadcasted_iota(jnp.int32, (rows, LANES), 1)
    group = (segment - 1) >> 3
    member = (segment - 1) & 7
    shut = (
        ((segment > 0) & between(lane, GROUP0, MEMBER0) & (lane - GROUP0 != group))
        | ((segment < 0) & between(lane, GROUP0, MEMBER0))
        | ((segment > 0) & between(lane, MEMBER0, FLAG) & (lane - MEMBER0 != member))
        | (lane == FLAG)
    )
    return jnp.where(shut, -BIG, 0.0).astype(F32)


def query_index(meta_ref):
    segment, key_mask, position, across, down = columns_of(meta_ref)
    rows = segment.shape[0]
    lane = lax.broadcasted_iota(jnp.int32, (rows, LANES), 1)
    x_even = bucket(across - (lane - HEAD)) + X_TABLE
    x_odd = bucket(across - lane) + X_TABLE
    even = jnp.where(between(lane, HEAD, HEAD + COORD), x_even, NOTHING)
    odd = jnp.where(lane < COORD, x_odd, NOTHING)
    shared = jnp.where(
        lane < POS,
        bucket(position - lane),
        jnp.where(between(lane, Y0, Y0 + COORD), bucket(down - (lane - Y0)) + Y_TABLE, NOTHING),
    )
    return even, odd, shared


def image_key_index(meta_ref):
    position = meta_ref[TEXT:, 2:3]
    lane = lax.broadcasted_iota(jnp.int32, (position.shape[0], LANES), 1)
    return jnp.where(lane < POS, bucket(lane - position), NOTHING)


def prepare(meta_ref, mark_refs, bar_ref, index_refs, key_index_ref):
    for ref, value in zip(mark_refs, marks(meta_ref)):
        ref[...] = value
    bar_ref[...] = barred(meta_ref)
    for ref, value in zip(index_refs, query_index(meta_ref)):
        ref[...] = value
    key_index_ref[...] = image_key_index(meta_ref)


def image_offsets(row_positions, column_positions):
    return bucket(column_positions - row_positions)


def own_lanes(parity, rows):
    lane = lax.broadcasted_iota(jnp.int32, (rows, LANES), 1)
    return (lane < HEAD) if parity == 0 else (lane >= HEAD)


def widened(parity, q, table_row, bar_ref, index_refs, key_index_ref, shared_ref):
    rows = q.shape[0]
    images = key_index_ref.shape[0]
    first = jnp.where(
        own_lanes(parity, rows),
        q.astype(F32) * 0.125,
        looked_up(table_row, index_refs[parity][...]),
    )
    second = (looked_up(table_row, index_refs[2][...]) + bar_ref[...]).astype(BF)
    image_lane = lax.broadcasted_iota(jnp.int32, (images, LANES), 1)
    key_image = jnp.where(
        image_lane < POS, looked_up(table_row, key_index_ref[...]).astype(BF), shared_ref[TEXT:]
    )
    return first.astype(BF), second, key_image


def joined(parity, first, second, key_image, k, marks_own, shared):
    rows = k.shape[0]
    lane = lax.broadcasted_iota(jnp.int32, (rows, LANES), 1)
    to_image = jnp.where(lane < POS, shared, second)
    key_first = jnp.where(own_lanes(parity, rows), k, marks_own)
    q_text = jnp.concatenate([first, second], axis=1)
    q_image = jnp.concatenate([first, to_image], axis=1)
    k_text = jnp.concatenate([key_first[:TEXT], shared[:TEXT]], axis=1)
    k_image = jnp.concatenate([key_first[TEXT:], key_image], axis=1)
    return q_text, q_image, k_text, k_image


def image_bias(table_row, offsets):
    return jnp.concatenate(
        [looked_up(table_row, offsets[:, :LANES]), looked_up(table_row, offsets[:, LANES:])], axis=1
    )


def forward_kernel(
    meta_ref, rows_ref, table_ref, q_ref, k_ref, v_ref,
    mixed_ref, log_ref, first_ref, second_ref, key_image_ref, bias_ref,
    even_ref, odd_ref, shared_ref, bar_ref, index_even, index_odd, index_shared, key_index_ref,
):
    mark_refs = (even_ref, odd_ref, shared_ref)
    index_refs = (index_even, index_odd, index_shared)

    @pl.when(pl.program_id(0) == 0)
    def _():
        prepare(meta_ref, mark_refs, bar_ref, index_refs, key_index_ref)

    rows = q_ref.shape[0]
    images = rows - TEXT
    q, k, v = q_ref[...], k_ref[...], v_ref[...]
    offsets = bucket(rows_ref[2:3, TEXT:] - meta_ref[TEXT:, 2:3])
    tile = 256
    v_turned = transposed(v)
    heads = [None, None]

    def prepared(parity):
        table_row = table_ref[pl.ds(2 * pl.program_id(0) + parity, 1), :]
        first, second, key_image = widened(
            parity, q, table_row, bar_ref, index_refs, key_index_ref, shared_ref
        )
        bias = image_bias(table_row, offsets)
        first_ref[parity] = first
        second_ref[parity] = second
        key_image_ref[parity] = key_image
        bias_ref[parity] = bias.astype(BF)
        wide = joined(
            parity, first, second, key_image, k, mark_refs[parity][...], shared_ref[...]
        )
        heads[parity] = wide + (bias,)

    def scored(parity, start):
        q_text, q_image, k_text, k_image, bias = heads[parity]
        here = slice(start, start + tile)
        on_image = dot_nt(k_image, q_image[here])
        if start >= TEXT:
            on_image = on_image + bias[:, start - TEXT : start - TEXT + tile]
        return dot_nt(k_text, q_text[here]), on_image

    spots = [(parity, start) for parity in range(2) for start in range(0, rows, tile)]
    outs = ([], [])
    prepared(0)
    following = scored(*spots[0])
    for index, (parity, start) in enumerate(spots):
        on_text, on_image = following
        if index == 1:
            prepared(1)
        if index + 1 < len(spots):
            following = scored(*spots[index + 1])
        top = jnp.maximum(
            jnp.max(on_text, axis=0, keepdims=True), jnp.max(on_image, axis=0, keepdims=True)
        )
        on_text = jnp.exp(on_text - top)
        on_image = jnp.exp(on_image - top)
        total = jnp.sum(on_text, axis=0, keepdims=True) + jnp.sum(on_image, axis=0, keepdims=True)
        own = slice(parity * HEAD, parity * HEAD + HEAD)
        out = dot_nn(v_turned[own, :TEXT], on_text.astype(BF)) + dot_nn(
            v_turned[own, TEXT:], on_image.astype(BF)
        )
        outs[parity].append(out * (1.0 / total))
        log_ref[0, parity : parity + 1, start : start + tile] = top + jnp.log(total)
    mixed_ref[...] = jnp.transpose(
        jnp.concatenate([jnp.concatenate(outs[parity], axis=1) for parity in range(2)], axis=0)
    )


def static_scratch(rows):
    return [
        pltpu.VMEM((rows, LANES), BF),
        pltpu.VMEM((rows, LANES), BF),
        pltpu.VMEM((rows, LANES), BF),
        pltpu.VMEM((rows, LANES), F32),
        pltpu.VMEM((rows, LANES), jnp.int32),
        pltpu.VMEM((rows, LANES), jnp.int32),
        pltpu.VMEM((rows, LANES), jnp.int32),
        pltpu.VMEM((rows - TEXT, LANES), jnp.int32),
    ]


def attention_forward(meta_columns, meta_rows, table_rows, projected, width):
    rows = projected.shape[0]
    images = rows - TEXT
    pairs = width // LANES

    def block(part):
        return pl.BlockSpec((rows, LANES), lambda p: (0, part * pairs + p))

    whole = lambda shape: pl.BlockSpec(shape, lambda p: (0,) * len(shape))
    return pl.pallas_call(
        forward_kernel,
        grid=(pairs,),
        in_specs=[
            whole(meta_columns.shape),
            whole(meta_rows.shape),
            whole(table_rows.shape),
            block(0), block(1), block(2),
        ],
        out_specs=[
            pl.BlockSpec((rows, LANES), lambda p: (0, p)),
            pl.BlockSpec((1, 2, rows), lambda p: (p, 0, 0)),
            pl.BlockSpec((2, rows, LANES), lambda p: (p, 0, 0)),
            pl.BlockSpec((2, rows, LANES), lambda p: (p, 0, 0)),
            pl.BlockSpec((2, images, LANES), lambda p: (p, 0, 0)),
            pl.BlockSpec((2, images, images), lambda p: (p, 0, 0)),
        ],
        out_shape=[
            jax.ShapeDtypeStruct((rows, width), F32),
            jax.ShapeDtypeStruct((pairs, 2, rows), F32),
            jax.ShapeDtypeStruct((2 * pairs, rows, LANES), BF),
            jax.ShapeDtypeStruct((2 * pairs, rows, LANES), BF),
            jax.ShapeDtypeStruct((2 * pairs, images, LANES), BF),
            jax.ShapeDtypeStruct((2 * pairs, images, images), BF),
        ],
        scratch_shapes=static_scratch(rows),
        compiler_params=pltpu.CompilerParams(vmem_limit_bytes=60 * 1024 * 1024),
        name="attention_forward",
    )(meta_columns, meta_rows, table_rows, projected, projected, projected)


def skewed(block):
    size = block.shape[0]
    lane = lax.broadcasted_iota(jnp.int32, (size, LANES), 1)
    row = lax.broadcasted_iota(jnp.int32, (size, LANES), 0)
    turned = jnp.take_along_axis(
        block, (lane + row) & (LANES - 1), axis=1, mode="promise_in_bounds"
    )
    straight = lane + row < LANES
    above = jnp.sum(jnp.where(straight, turned, 0.0), axis=0, keepdims=True)
    below = jnp.sum(jnp.where(straight, 0.0, turned), axis=0, keepdims=True)
    return above, below


def transposed(array):
    return jnp.transpose(array.astype(F32)).astype(array.dtype)


def static_prepare(meta_ref, static):
    for ref, turned, value in zip(static[:3], static[3:], marks(meta_ref)):
        ref[...] = value
        turned[...] = transposed(value)


def head_back(
    parity, pair, rows_ref, wide_refs, k_ref, v_ref, mixed_ref, grad_ref, log_ref, static, diag_ref,
):
    mark_refs, turned_refs = static[:3], static[3:]
    first_ref, second_ref, key_image_ref, bias_ref = wide_refs
    head = 2 * pair + parity
    shared_t = turned_refs[2]
    rows = k_ref.shape[1]
    images = rows - TEXT
    tile = 256
    k, v, grad = k_ref[pair], v_ref[pair], grad_ref[pair]
    products = grad.astype(F32) * mixed_ref[pair]
    k_turned = transposed(k)
    is_image = rows_ref[1:2, TEXT:] > 0
    own = own_lanes(parity, rows)
    log_row = log_ref[pair, parity : parity + 1, :]
    first, shared = first_ref[head], mark_refs[2][...]
    q_text, q_image, k_text, k_image = joined(
        parity, first, second_ref[head], key_image_ref[head], k, mark_refs[parity][...], shared
    )
    bias = bias_ref[head].astype(F32)
    ones = jnp.where(own_lanes(parity, 8), 1.0, 0.0).astype(BF)
    delta = jnp.zeros((8, rows), F32)
    rest = products
    for _ in range(3):
        piece = rest.astype(BF)
        delta = delta + dot_nt(ones, piece)
        rest = rest - piece.astype(F32)
    delta = delta[0:1]
    v_own = jnp.where(own, v, jnp.zeros_like(v))
    q_marked = jnp.concatenate(
        [jnp.where(own, first, mark_refs[parity][...]), shared], axis=1
    )
    dq = jnp.zeros((HEAD, rows), F32)
    dks = []
    dvs = []
    first_sum = jnp.zeros((LANES, LANES), F32)
    second_sum = jnp.zeros((LANES, LANES), F32)
    text_image = jnp.zeros((LANES, images), F32)
    def scored(start):
        here = slice(start, start + tile)
        if start < TEXT:
            scores = dot_nt(k_text[here], q_text)
        else:
            scores = dot_nt(k_image[start - TEXT : start - TEXT + tile], q_image)
            scores = jnp.concatenate([scores[:, :TEXT], scores[:, TEXT:] + bias], axis=1)
        return scores, dot_nt(v_own[here], grad)

    following = scored(0)
    for start in range(0, rows, tile):
        here = slice(start, start + tile)
        scores, prob_grad = following
        if start + tile < rows:
            following = scored(start + tile)
        soft = jnp.exp(scores - log_row)
        score_grad = soft * (prob_grad - delta)
        low = score_grad.astype(BF)
        dvs.append(dot_nn(soft.astype(BF), grad))
        wide = dot_nn(low, q_marked)
        dks.append(wide[:, :LANES])
        dq = dq + dot_nn(k_turned[parity * HEAD : parity * HEAD + HEAD, here], low)
        rounded = wide.astype(BF)
        first_sum = first_sum + dot_nn(turned_refs[parity][:, here], rounded[:, :LANES])
        second_sum = second_sum + dot_nn(shared_t[:, here], rounded[:, LANES:])
        if start < TEXT:
            text_image = text_image + dot_nn(shared_t[:, here], low[:, TEXT:])
        else:
            by_position = wide[:, LANES:]
            on_image = score_grad[:, TEXT:]
    small = lax.broadcasted_iota(jnp.int32, (LANES, LANES), 1)
    small_row = lax.broadcasted_iota(jnp.int32, (LANES, LANES), 0)
    x0 = HEAD if parity == 0 else 0
    x_block = jnp.where(
        between(small, x0, x0 + COORD) & between(small_row, x0, x0 + COORD), first_sum, 0.0
    )
    y_block = jnp.where(
        between(small, Y0, Y0 + COORD) & between(small_row, Y0, Y0 + COORD), second_sum, 0.0
    )
    p_block = jnp.where((small < POS) & (small_row < POS), second_sum, 0.0)
    wide_lane = lax.broadcasted_iota(jnp.int32, (images, images), 1)
    outside = jnp.sum(jnp.where(is_image, 0.0, on_image), axis=1, keepdims=True)
    pairs = jnp.where(is_image, on_image, 0.0) + jnp.where(wide_lane == 0, outside, 0.0)
    outside_text = jnp.sum(jnp.where(is_image, 0.0, text_image), axis=1, keepdims=True)
    text_lane = lax.broadcasted_iota(jnp.int32, (LANES, images), 1)
    text_row = lax.broadcasted_iota(jnp.int32, (LANES, images), 0)
    text_image = jnp.where(is_image, text_image, 0.0) + jnp.where(
        text_lane == 0, outside_text, 0.0
    )
    text_image = jnp.where(text_row < POS, text_image, 0.0)
    first_lane = lax.broadcasted_iota(jnp.int32, (images, LANES), 1)
    left = pairs[:, :LANES] + jnp.where(first_lane < POS, by_position, 0.0)
    right = pairs[:, LANES:]
    a00, b00 = skewed(left[:LANES] + text_image[:, :LANES] + p_block)
    a01, b01 = skewed(right[:LANES] + text_image[:, LANES:])
    a10, b10 = skewed(left[LANES:])
    a11, b11 = skewed(right[LANES:])
    ax, bx = skewed(x_block)
    ay, by = skewed(y_block)
    diag_ref[head] = jnp.concatenate(
        [b10, b00 + b11 + a10, a00 + a11 + b01, a01, bx, ax, by, ay], axis=0
    )
    return dq * 0.125, jnp.concatenate(dks, axis=0), jnp.concatenate(dvs, axis=0)


MESH = pl.DeviceIdType.MESH
VMEM = pl.BlockSpec(memory_space=pltpu.VMEM)
HBM = pl.BlockSpec(memory_space=pltpu.HBM)
MIB = 1024 * 1024


def remote(src, dst, send, receive, device):
    return pltpu.make_async_remote_copy(
        src_ref=src, dst_ref=dst, send_sem=send, recv_sem=receive, device_id=device,
        device_id_type=MESH,
    )


def project_kernel(
    layer_ref, weight_hbm, *refs,
):
    small_hbm, refs = refs[:10], refs[10:]
    (item_ref, projected_out, columns_ref, rows_ref, table_ref,
     projected_ref, weight_ref, meta_send, bias_ref, sems, load_sems, store_sems), small = (
        refs[:12], refs[12:],
    )
    (segment_ref, mask_ref, position_ref, across_ref, down_ref, query_bias_ref, value_bias_ref,
     text_ref, horiz_ref, vert_ref) = small
    mine = lax.axis_index("seq")
    partner = (1 - mine, lax.axis_index("dp"))
    count, width = layer_ref.shape[1:]
    own = pl.ds(pl.multiple_of(mine * count, LANES), count)
    loads = [
        pltpu.make_async_copy(source, target, load_sems.at[index])
        for index, (source, target) in enumerate(
            list(zip(small_hbm, small))
            + [(layer_ref.at[mine], item_ref.at[own]), (weight_hbm, weight_ref)]
        )
    ]
    for load in loads:
        load.start()
    barrier = pltpu.get_barrier_semaphore()
    pl.semaphore_signal(barrier, inc=1, device_id=partner, device_id_type=MESH)
    pl.semaphore_wait(barrier, 1)
    pieces = count // LANES
    rows_out = [
        remote(
            layer_ref.at[1 - mine, pl.ds(piece * LANES, LANES)],
            item_ref.at[pl.ds(pl.multiple_of(mine * count + piece * LANES, LANES), LANES)],
            sems.at[0, piece], sems.at[1, piece], partner,
        )
        for piece in range(pieces)
    ]
    for copy in rows_out:
        copy.start()
    for load in loads[:-2]:
        load.wait()

    fields = (segment_ref, mask_ref, position_ref, across_ref, down_ref)
    blocks = [
        jnp.concatenate(
            [field[item : item + 1, :] for field in fields] + [jnp.zeros((3, count), jnp.int32)],
            axis=0,
        )
        for item in range(2)
    ]
    meta_send[...] = jnp.where(mine == 0, blocks[1], blocks[0])
    meta_out = remote(
        meta_send, rows_ref.at[:, own], sems.at[0, pieces], sems.at[1, pieces], partner
    )
    meta_out.start()
    rows_ref[:, own] = jnp.where(mine == 0, blocks[0], blocks[1])
    bias_ref[:, :width] = query_bias_ref[...].astype(F32).reshape(1, width)
    bias_ref[:, width : 2 * width] = jnp.zeros((1, width), F32)
    bias_ref[:, 2 * width :] = value_bias_ref[...].astype(F32).reshape(1, width)
    heads, levels = text_ref.shape
    spot = lax.broadcasted_iota(jnp.int32, (levels, LANES), 1)
    level = lax.broadcasted_iota(jnp.int32, (levels, LANES), 0)
    table = jnp.zeros((heads, LANES), F32)
    for source, begin in ((text_ref, 0), (horiz_ref, X_TABLE), (vert_ref, Y_TABLE)):
        table = table + dot_nn(source[...], (spot == level + begin).astype(BF))
    table_ref[...] = jnp.concatenate([table, jnp.zeros((16 - heads, LANES), F32)], axis=0)

    def project(there):
        step = 256

        def body(index, carry):
            columns = pl.ds(pl.multiple_of(index * step, step), step)
            product = dot_nn(item_ref[there], weight_ref[:, columns])
            projected_ref[there, columns] = (product + bias_ref[:, columns]).astype(BF)
            return carry

        lax.fori_loop(0, 3 * width // step, body, 0)

    def stored(index, there):
        return pltpu.make_async_copy(
            projected_ref.at[there], projected_out.at[there], store_sems.at[index]
        )

    for load in loads[-2:]:
        load.wait()
    project(own)
    stored(0, own).start()
    for piece in range(pieces):
        rows_out[piece].wait()
        there = pl.ds(pl.multiple_of((1 - mine) * count + piece * LANES, LANES), LANES)
        project(there)
        stored(1 + piece, there).start()
    meta_out.wait()
    meta = rows_ref[...].astype(F32)
    tall = jnp.concatenate([meta, jnp.zeros((LANES - 8, meta.shape[1]), F32)], axis=0)
    columns_ref[...] = jnp.transpose(tall).astype(jnp.int32)
    stored(0, own).wait()
    for piece in range(pieces):
        there = pl.ds(pl.multiple_of((1 - mine) * count + piece * LANES, LANES), LANES)
        stored(1 + piece, there).wait()


def projected_item(layer_in, fields, qkv_weight, query_bias, value_bias, tables):
    rows = 2 * layer_in.shape[1]
    width = layer_in.shape[2]
    pieces = rows // 2 // LANES
    small = list(fields) + [query_bias, value_bias] + [t.T for t in tables]
    return pl.pallas_call(
        project_kernel,
        in_specs=[HBM] * (2 + len(small)),
        out_specs=[VMEM, HBM, VMEM, VMEM, VMEM],
        out_shape=[
            jax.ShapeDtypeStruct((rows, width), BF),
            jax.ShapeDtypeStruct((rows, 3 * width), BF),
            jax.ShapeDtypeStruct((rows, LANES), jnp.int32),
            jax.ShapeDtypeStruct((8, rows), jnp.int32),
            jax.ShapeDtypeStruct((16, LANES), F32),
        ],
        scratch_shapes=[
            pltpu.VMEM((rows, 3 * width), BF),
            pltpu.VMEM((width, 3 * width), BF),
            pltpu.VMEM((8, rows // 2), jnp.int32),
            pltpu.VMEM((1, 3 * width), F32),
            pltpu.SemaphoreType.DMA((2, pieces + 1)),
            pltpu.SemaphoreType.DMA((len(small) + 2,)),
            pltpu.SemaphoreType.DMA((pieces + 1,)),
        ]
        + [pltpu.VMEM(array.shape, array.dtype) for array in small],
        compiler_params=pltpu.CompilerParams(
            collective_id=1, has_side_effects=True, vmem_limit_bytes=60 * MIB
        ),
        name="projected_item",
    )(layer_in, qkv_weight, *small)


EPSILON = 1e-05
TILE = 256


def vector(ref):
    return ref[...].astype(F32).reshape(1, ref.shape[0])


def gelu_and_slope(x):
    bell = jnp.exp2(-0.7213475204444817 * (x * x))
    rough = 1.0 + 0.23164188826 * jnp.abs(x)
    t = pl.reciprocal(rough, approx=True)
    t = t * (2.0 - rough * t)
    series = t * (
        0.127414796
        + t * (-0.142248368 + t * (0.7107068705 + t * (-0.7265760135 + t * 0.5307027145)))
    )
    tail = bell * series
    below = jnp.where(x >= 0.0, 1.0 - tail, tail)
    return x * below, below + x * (0.3989422804014327 * bell)


def row_mean(block):
    return jnp.mean(block, axis=1, keepdims=True)


def normalized(hidden):
    center = hidden - row_mean(hidden)
    scale = lax.rsqrt(row_mean(center * center) + EPSILON)
    return center * scale, scale


def norm_pulled(grad, unit, scale):
    return scale * (grad - row_mean(grad) - unit * row_mean(grad * unit))


def column_sum(block):
    return jnp.sum(block, axis=0, keepdims=True)


def feed_kernel(
    item_ref, mixed_ref, cotangent_ref, out_weight_ref, up_ref, down_ref, *refs,
):
    vectors_hbm, refs = refs[:7], refs[7:]
    (layer_out, d_hidden_ref, d_mixed_ref, grad_out_ref, grad_down_ref, grad_up_ref, small_ref,
     layer_ref, cotangent_all, active, slope, unit, scale_ref, normed, normed_t, total, d_branch, d_branch_t,
     sems, load_sems) = refs[:20]
    vectors = refs[20:]
    (out_bias_ref, attn_gain_ref, attn_shift_ref, up_bias_ref, down_bias_ref, ffn_gain_ref,
     ffn_shift_ref) = vectors
    step = pl.program_id(0)
    blocks = pl.num_programs(0) // 2
    rows, width = item_ref.shape
    count = rows // 2
    mine = lax.axis_index("seq")
    partner = (1 - mine, lax.axis_index("dp"))
    own = pl.ds(pl.multiple_of(mine * count, LANES), count)
    tiles = rows // TILE

    def sent():
        return remote(
            cotangent_ref.at[1 - mine], cotangent_all.at[own], sems.at[0], sems.at[1], partner
        )

    def returned():
        theirs = pl.ds(pl.multiple_of((1 - mine) * count, LANES), count)
        return [
            pltpu.make_async_copy(layer_ref.at[own], layer_out.at[mine], load_sems.at[8]),
            remote(
                layer_ref.at[theirs], layer_out.at[mine], sems.at[2], sems.at[3], partner
            ),
        ]

    def loads():
        copies = list(zip(vectors_hbm, vectors)) + [(cotangent_ref.at[mine], cotangent_all.at[own])]
        return [
            pltpu.make_async_copy(source, target, load_sems.at[index])
            for index, (source, target) in enumerate(copies)
        ]

    def over_tiles(size, body, carry, unroll=1):
        def run(index, state):
            return body(pl.ds(pl.multiple_of(index * size, size), size), state)

        return lax.fori_loop(0, rows // size, run, carry, unroll=unroll)

    @pl.when(step == 0)
    def _():
        for load in loads():
            load.start()
        barrier = pltpu.get_barrier_semaphore()
        pl.semaphore_signal(barrier, inc=1, device_id=partner, device_id_type=MESH)
        pl.semaphore_wait(barrier, 1)
        sent().start()
        small_ref[...] = jnp.zeros_like(small_ref)
        for load in loads():
            load.wait()
        out_bias, gain, shift = vector(out_bias_ref), vector(attn_gain_ref), vector(attn_shift_ref)

        def tile(there, carry):
            attn = dot_nn(mixed_ref[there].astype(BF), out_weight_ref[...]) + out_bias
            standard, scale = normalized(item_ref[there].astype(F32) + attn)
            unit[there] = standard
            scale_ref[there] = jnp.broadcast_to(scale, (scale.shape[0], LANES))
            result = standard * gain + shift
            normed[there] = result.astype(BF)
            normed_t[:, there] = jnp.transpose(result).astype(BF)
            return carry

        over_tiles(TILE, tile, 0, 3)
        total[...] = jnp.zeros_like(total)

    @pl.when(step < blocks)
    def _():
        columns = [slice(begin, begin + TILE) for begin in range(0, width, TILE)]
        low = normed[...]
        following = dot_nn(low, up_ref[:, columns[0]])
        values = []
        for index, here in enumerate(columns):
            product = following
            if index + 1 < len(columns):
                following = dot_nn(low, up_ref[:, columns[index + 1]])
            bias = up_bias_ref[pl.ds(pl.multiple_of(step * width + here.start, LANES), TILE)]
            value, grade = gelu_and_slope(product + bias.astype(F32).reshape(1, TILE))
            values.append(value.astype(BF))
            active[step, :, here] = values[-1]
            slope[step, :, here] = grade
        values = jnp.concatenate(values, axis=1)
        for here in columns:
            total[:, here] += dot_nn(values, down_ref[:, here])

    @pl.when(step == blocks)
    def _():
        sent().wait()
        gain, shift, bias = vector(ffn_gain_ref), vector(ffn_shift_ref), vector(down_bias_ref)
        first_gain, first_shift = vector(attn_gain_ref), vector(attn_shift_ref)

        def tile(there, sums):
            hidden = unit[there] * first_gain + first_shift + (total[there] + bias)
            standard, scale = normalized(hidden)
            layer_ref[there] = (standard * gain + shift).astype(BF)
            cotangent = cotangent_all[there].astype(F32)
            pulled = norm_pulled(cotangent * gain, standard, scale)
            total[there] = pulled
            low = pulled.astype(BF)
            d_branch[there] = low
            return (
                sums[0] + column_sum(low.astype(F32)),
                sums[1] + column_sum(cotangent * standard),
                sums[2] + column_sum(cotangent),
            )

        zero = jnp.zeros((1, width), F32)
        sums = over_tiles(64, tile, (zero, zero, zero), 4)
        for row, value in zip((5, 6, 7), sums):
            small_ref[row : row + 1] = value

        for copy in returned():
            copy.start()

        def turn(there, carry):
            d_branch_t[:, there] = jnp.transpose(d_branch[there].astype(F32)).astype(BF)
            return carry

        over_tiles(TILE, turn, 0, 3)

    @pl.when(step >= blocks)
    def _():
        block = step - blocks

        columns = [slice(begin, begin + TILE) for begin in range(0, width, TILE)]
        branch = d_branch[...]
        turned = d_branch_t[...]
        following = dot_nt(branch, down_ref[columns[0]])
        values = []
        for index, here in enumerate(columns):
            product = following
            if index + 1 < len(columns):
                following = dot_nt(branch, down_ref[columns[index + 1]])
            grad_down_ref[:, here] = dot_nn(turned, active[block, :, here]).astype(BF)
            d_up = (product * slope[block, :, here]).astype(BF)
            small_ref[pl.ds(8 + block, 1), here] = column_sum(d_up.astype(F32))
            values.append(d_up)
        values = jnp.concatenate(values, axis=1)
        turned = normed_t[...]
        for here in columns:
            grad_up_ref[:, here] = dot_nn(turned, values[:, here]).astype(BF)
            total[:, here] += dot_nt(values, up_ref[here])

    @pl.when(step == 2 * blocks - 1)
    def _():
        gain = vector(attn_gain_ref)

        def tile(there, sums):
            d_normed = total[there]
            standard = unit[there]
            d_hidden = norm_pulled(d_normed * gain, standard, scale_ref[there, :1])
            d_hidden_ref[there] = d_hidden
            low = d_hidden.astype(BF)
            d_branch[there] = low
            return (
                sums[0] + column_sum(low.astype(F32)),
                sums[1] + column_sum(d_normed * standard),
                sums[2] + column_sum(d_normed),
            )

        zero = jnp.zeros((1, width), F32)
        sums = over_tiles(64, tile, (zero, zero, zero), 4)
        for row, value in zip((2, 3, 4), sums):
            small_ref[row : row + 1] = value

        def turn(there, carry):
            normed_t[:, there] = jnp.transpose(mixed_ref[there]).astype(BF)
            return carry

        over_tiles(TILE, turn, 0, 3)

        for begin in range(0, width, TILE):
            here = slice(begin, begin + TILE)
            d_mixed_ref[:, here] = dot_nt(d_branch[...], out_weight_ref[here]).astype(BF)
            grad_out_ref[:, here] = dot_nn(normed_t[...], d_branch[:, here]).astype(BF)

        for copy in returned():
            copy.wait()


def fed_forward_and_back(
    item, mixed, cotangent, out_weight, up_weight, down_weight, vectors,
):
    rows, width = item.shape
    blocks = up_weight.shape[1] // width
    whole = pl.BlockSpec(memory_space=pltpu.VMEM)
    square = lambda kind: jax.ShapeDtypeStruct((rows, width), kind)
    later = lambda i: jnp.maximum(i - blocks, 0)
    return pl.pallas_call(
        feed_kernel,
        grid=(2 * blocks,),
        in_specs=[whole, whole, HBM, whole]
        + [
            pl.BlockSpec((width, width), lambda i: (0, lax.rem(i, blocks))),
            pl.BlockSpec((width, width), lambda i: (lax.rem(i, blocks), 0)),
        ]
        + [HBM] * 7,
        out_specs=[HBM] + [whole] * 3
        + [
            pl.BlockSpec((width, width), lambda i: (later(i), 0)),
            pl.BlockSpec((width, width), lambda i: (later(i), 0)),
            whole,
        ],
        out_shape=[
            jax.ShapeDtypeStruct((2, rows // 2, width), BF), square(F32), square(BF),
            jax.ShapeDtypeStruct((width, width), BF),
            jax.ShapeDtypeStruct((blocks * width, width), BF),
            jax.ShapeDtypeStruct((blocks * width, width), BF),
            jax.ShapeDtypeStruct((16, width), F32),
        ],
        scratch_shapes=[
            pltpu.VMEM((rows, width), BF),
            pltpu.VMEM((rows, width), BF),
            pltpu.VMEM((blocks, rows, width), BF),
            pltpu.VMEM((blocks, rows, width), F32),
            pltpu.VMEM((rows, width), F32),
            pltpu.VMEM((rows, LANES), F32),
            pltpu.VMEM((rows, width), BF),
            pltpu.VMEM((width, rows), BF),
            pltpu.VMEM((rows, width), F32),
            pltpu.VMEM((rows, width), BF),
            pltpu.VMEM((width, rows), BF),
            pltpu.SemaphoreType.DMA((4,)),
            pltpu.SemaphoreType.DMA((9,)),
        ]
        + [pltpu.VMEM(vector.shape, vector.dtype) for vector in vectors],
        compiler_params=pltpu.CompilerParams(
            collective_id=2, has_side_effects=True, vmem_limit_bytes=60 * MIB
        ),
        name="feed_forward",
    )(item, mixed, cotangent, out_weight, up_weight, down_weight, *vectors)


SLOTS = 4


def finish_kernel(
    main_ref, tail_ref, input_hbm, small_ref, diagonal_ref,
    down_ref, up_ref, out_ref, qkv_ref, input_ref, *refs,
):
    singles, (main_in, tail_in, slots, input_in, input_slot, in_sems, out_sems, item_sems) = (
        refs[:12], refs[12:],
    )
    mains, width = main_in.shape[0], main_in.shape[2]
    pairs, across = tail_in.shape[0], tail_in.shape[2]
    hidden = mains // 2
    blocks = mains + pairs

    def load(block):
        if block < mains:
            source, target = main_ref.at[pl.ds(block * width, width)], main_in.at[block]
        else:
            pair = block - mains
            source, target = tail_ref.at[pl.ds(pair * TAIL_ROWS, TAIL_ROWS)], tail_in.at[pair]
        return pltpu.make_async_copy(source, target, in_sems.at[block])

    def stores(block):
        slot, sem = slots.at[block % SLOTS], out_sems.at[block % SLOTS]
        if block < hidden:
            targets = [(slot, down_ref.at[pl.ds(block * width, width)])]
        elif block < mains:
            targets = [(slot, up_ref.at[:, pl.ds((block - hidden) * width, width)])]
        else:
            pair = block - mains
            targets = [
                (
                    slot.at[:, pl.ds(part * LANES, LANES)],
                    qkv_ref.at[:, pl.ds(part * width + pair * LANES, LANES)],
                )
                for part in range(3)
            ]
            down = pl.ds(0, TAIL_ROWS - width)
            targets.append(
                (slot.at[down, pl.ds(across, across)], out_ref.at[out_spot(pair, pairs, width)])
            )
        return [
            pltpu.make_async_copy(source, target, sem.at[index])
            for index, (source, target) in enumerate(targets)
        ]

    load_input = pltpu.make_async_copy(input_hbm, input_in, item_sems.at[0])
    store_input = pltpu.make_async_copy(input_slot, input_ref, item_sems.at[1])
    for block in range(blocks):
        load(block).start()
    load_input.start()
    for block in range(blocks):
        load(block).wait()
        if block >= SLOTS:
            for copy in stores(block - SLOTS):
                copy.wait()
        slot = block % SLOTS
        if block < hidden:
            slots[slot] = jnp.transpose(main_in[block].astype(F32))
        elif block < mains:
            slots[slot] = main_in[block].astype(F32)
        else:
            slots[slot, :, :across] = tail_in[block - mains, :width].astype(F32)
            slots[slot, : TAIL_ROWS - width, across:] = tail_in[block - mains, width:].astype(F32)
        for copy in stores(block):
            copy.start()
    load_input.wait()
    input_slot[...] = input_in[...].astype(F32)
    store_input.start()
    for row in range(8):
        singles[row][...] = small_ref[row]
    for row in range(hidden):
        singles[8][row * width : row * width + width] = small_ref[8 + row]
    heads, levels = singles[9].shape
    diagonals = diagonal_ref[...]
    level = lax.broadcasted_iota(jnp.int32, (LANES, LANES), 1)
    lane = lax.broadcasted_iota(jnp.int32, (LANES, LANES), 0)
    for table, (first, size, skip) in enumerate(((0, 4, 0), (4, 2, 1), (6, 2, 1))):
        total = jnp.zeros((heads, LANES), F32)
        for row in range(size):
            distance = lane + LANES * (row + skip - 2)
            chosen = (bucket(distance) == level).astype(F32)
            total = total + jnp.dot(
                diagonals[:, first + row, :], chosen, preferred_element_type=F32,
                precision=lax.Precision.HIGHEST,
            )
        singles[9 + table][...] = total[:, :levels]
    for block in range(blocks - SLOTS, blocks):
        for copy in stores(block):
            copy.wait()
    store_input.wait()


def finished(main, tail, grad_input, small, diagonals, hidden, levels):
    width = main.shape[1]
    heads = diagonals.shape[0]
    mains = main.shape[0] // width
    pairs = tail.shape[0] // TAIL_ROWS
    single = jax.ShapeDtypeStruct((width,), F32)
    table = jax.ShapeDtypeStruct((heads, levels), F32)
    dma = pltpu.SemaphoreType.DMA
    return pl.pallas_call(
        finish_kernel,
        in_specs=[HBM, HBM, HBM, VMEM, VMEM],
        out_specs=[HBM] * 5 + [VMEM] * 12,
        out_shape=[
            jax.ShapeDtypeStruct((hidden, width), F32),
            jax.ShapeDtypeStruct((width, hidden), F32),
            jax.ShapeDtypeStruct((width, width), F32),
            jax.ShapeDtypeStruct((width, 3 * width), F32),
            jax.ShapeDtypeStruct(grad_input.shape, F32),
        ]
        + [single] * 8
        + [jax.ShapeDtypeStruct((hidden,), F32)]
        + [table] * 3,
        scratch_shapes=[
            pltpu.VMEM((mains, width, width), BF),
            pltpu.VMEM((pairs, TAIL_ROWS, tail.shape[1]), BF),
            pltpu.VMEM((SLOTS, width, width), F32),
            pltpu.VMEM(grad_input.shape, BF),
            pltpu.VMEM(grad_input.shape, F32),
            dma((mains + pairs,)),
            dma((SLOTS, 4)),
            dma((2,)),
        ],
        compiler_params=pltpu.CompilerParams(vmem_limit_bytes=56 * MIB),
        name="finished",
    )(main, tail, grad_input, small, diagonals)


PIECE = 16


def hop_names(depth):
    names = ["x", "y"]
    reach = 1
    while reach < depth:
        names.append(f"z{reach}")
        reach *= 2
    return names


def route(depth, letters):
    names = hop_names(depth)
    line = {"a": names[2:3], "b": names[3:]}
    return [name for letter in letters for name in line.get(letter, [letter])]


class Place:
    def __init__(self, depth):
        place = lax.axis_index("dp")
        x = lax.axis_index("seq")
        core = lax.rem(place, 2)
        y = lax.rem(lax.div(place, 2), 2)
        z = lax.rem(lax.div(place, 4), depth)
        group = lax.div(place, 4 * depth)
        at = lambda sx, sc, sy, sz: (sx, (group * depth + sz) * 4 + sy * 2 + sc)
        self.bits = {"core": core, "x": x, "y": y}
        self.partners = {
            "core": at(x, 1 - core, y, z), "x": at(1 - x, core, y, z), "y": at(x, core, 1 - y, z),
        }
        reach = 1
        while reach < depth:
            up = lax.rem(lax.div(z, reach), 2)
            self.bits[f"z{reach}"] = up
            self.partners[f"z{reach}"] = at(x, core, y, z + reach - 2 * reach * up)
            reach *= 2

    def greet(self):
        barrier = pltpu.get_barrier_semaphore()
        for device in self.partners.values():
            pl.semaphore_signal(barrier, inc=1, device_id=device, device_id_type=MESH)
        pl.semaphore_wait(barrier, len(self.partners))


class Chunk:
    def __init__(self, place, depth, source, out_ref, offset, spot, scratch):
        _, self.begin, rows, first, columns, _, paths, _ = spot
        self.place, self.source, self.columns = place, source, pl.ds(first, columns)
        self.out_ref, self.out_begin = out_ref, offset + self.begin
        self.half, self.quarter = rows // 2, rows // 4
        self.routes = [route(depth, letters) for letters in paths.split()]
        self.hops = len(self.routes[0])
        self.stages = 2 * self.hops + 3
        self.work, self.fresh, *self.landing, self.sends, self.receives, self.locals = scratch

    def aligned(self, value):
        return pl.multiple_of(value, PIECE)

    def size(self, hop):
        return self.quarter >> (hop + 1)

    def base(self, part, hops):
        start = part * self.quarter
        for hop in range(hops):
            start = start + self.place.bits[self.routes[part][hop]] * self.size(hop)
        return start

    def across(self, part, hop):
        bit = self.place.bits[self.routes[part][hop]]
        return self.base(part, hop) + (1 - bit) * self.size(hop)

    def partner(self, part, hop):
        return self.place.partners[self.routes[part][hop]]

    def out(self, begin, size, core=None):
        core = self.place.bits["core"] if core is None else core
        return self.out_ref.at[
            pl.ds(self.aligned(self.out_begin + core * self.half + begin), size), self.columns
        ]

    def copy(self, index, source, target, device):
        return remote(source, target, self.sends.at[index], self.receives.at[index], device)

    def pair_down(self):
        core = self.place.bits["core"]
        at = lambda c: self.source.at[
            pl.ds(self.aligned(self.begin + c * self.half), self.half), self.columns
        ]
        return [
            self.copy(0, at(1 - core), self.fresh, self.place.partners["core"]),
            pltpu.make_async_copy(at(core), self.work, self.locals.at[0]),
        ]

    def pair_up(self, arriving):
        core = self.place.bits["core"]
        target = self.out(0, self.half, 1 - core if arriving else core)
        return [self.copy(1, self.out(0, self.half), target, self.place.partners["core"])]

    def down(self, hop):
        return [
            self.copy(
                2 + 2 * hop + part,
                self.work.at[pl.ds(self.aligned(self.across(part, hop)), self.size(hop))],
                self.landing[hop].at[part], self.partner(part, hop),
            )
            for part in range(2)
        ]

    def kept(self):
        size = self.size(self.hops - 1)
        copies = []
        for part in range(2):
            begin = self.aligned(self.base(part, self.hops))
            copies.append(
                pltpu.make_async_copy(
                    self.work.at[pl.ds(begin, size)], self.out(begin, size),
                    self.locals.at[1 + part],
                )
            )
        return copies

    def up(self, hop, arriving):
        copies = []
        for part in range(2):
            mine = self.base(part, hop + 1)
            size = self.size(hop)
            if hop == self.hops - 1:
                source = self.work.at[pl.ds(self.aligned(mine), size)]
            else:
                source = self.out(mine, size)
            target = self.out(self.across(part, hop) if arriving else mine, size)
            index = 2 + 2 * self.hops + 2 * hop + part
            copies.append(self.copy(index, source, target, self.partner(part, hop)))
        return copies

    def add(self, begin, source, size):
        step = 64 if size % 64 == 0 else min(size, PIECE)

        def body(index, carry):
            offset = self.aligned(index * step)
            there = pl.ds(self.aligned(begin + offset), step)
            self.work[there] = self.work[there] + source[pl.ds(offset, step)]
            return carry

        lax.fori_loop(0, size // step, body, 0)

    def stage(self, number):
        hops = self.hops
        ended, started = [], []
        if number == 0:
            started = self.pair_down()
        elif number == 1:
            ended = self.pair_down()
            started = self.down(0)
        elif number <= hops:
            ended = self.down(number - 2)
            started = self.down(number - 1)
        elif number == hops + 1:
            ended = self.down(hops - 1)
            started = self.up(hops - 1, False) + self.kept()
        elif number <= 2 * hops:
            level = 2 * hops + 1 - number
            ended = self.up(level, True) + (self.kept() if level == hops - 1 else [])
            started = self.up(level - 1, False)
        elif number == 2 * hops + 1:
            ended = self.up(0, True)
            started = self.pair_up(False)
        else:
            ended = self.pair_up(True)
        for copy in ended:
            copy.wait()
        if number == 1:
            self.add(0, self.fresh, self.half)
        elif 2 <= number <= hops + 1:
            hop = number - 2
            for part in range(2):
                self.add(self.base(part, hop + 1), self.landing[hop].at[part], self.size(hop))
        for copy in started:
            copy.start()


def chunk_scratch(rows, width, depth):
    hops = len(hop_names(depth))
    dma = pltpu.SemaphoreType.DMA
    return (
        [pltpu.VMEM((rows // 2, width), BF)] * 2
        + [pltpu.VMEM((2, rows // 4 >> (hop + 1), width), BF) for hop in range(hops)]
        + [dma((2 + 4 * hops,)), dma((2 + 4 * hops,)), dma((3,))]
    )


def planned(chunks, work, depth, hop_count):
    latency, issue, link, pair = 4.0, 0.08, 100e3, 600e3
    free = {}
    now = 0.0

    def sent(name, rows, columns):
        nonlocal now
        now += issue
        row_bytes = 2 * columns
        share = {"core": [("core", rows * row_bytes / pair)]}.get(name)
        if share is None:
            time = 2 * rows * row_bytes / link
            share = [(name, time)]
            if name[0] == "z":
                reach = int(name[1:])
                share = [("z end", time), ("z middle", 0.0 if reach == 1 else reach * time)]
        end = now
        for lane, time in share:
            free[lane] = max(now, free.get(lane, 0.0)) + time
            end = max(end, free[lane])
        return end + latency

    chains = []
    for rows, columns, need, paths, _ in chunks:
        paths = [route(depth, letters) for letters in paths.split()]
        down = []
        size = rows // 4
        for hop in range(len(paths[0])):
            size //= 2
            down.append([(path[hop], size, columns) for path in paths])
        pair_step = [[("core", rows // 2, columns)]]
        chains.append((need, pair_step + down + down[::-1] + pair_step))
    chains.append((len(work), [[("core", 16, 768)]] * hop_count))
    position = [0] * len(chains)
    ready = [0.0] * len(chains)
    ranks = [chunk[4] for chunk in chunks] + [0]
    order = [[] for _ in range(len(work) + 1)]
    done = 0
    while True:
        open_ones = [
            (ranks[i], ready[i], i) for i, (need, chain) in enumerate(chains)
            if position[i] <= len(chain) and need <= done
        ]
        due = [entry for entry in open_ones if entry[1] <= now]
        if not due and done < len(work):
            now += work[done]
            done += 1
            continue
        if not open_ones:
            return order
        _, when, index = min(due) if due else min(open_ones, key=lambda entry: entry[1])
        now = max(now, when)
        chain = chains[index][1]
        stage = position[index]
        order[done].append((index, stage))
        if 0 < stage <= len(chain) // 2:
            now += 2e-6 * sum(rows * wide for _, rows, wide in chain[stage - 1])
        if stage < len(chain):
            ready[index] = max(sent(*entry) for entry in chain[stage])
        position[index] += 1


def last_kernel(
    depth, plan, orders, *refs,
):
    (meta_ref, rows_ref, projected_hbm, mixed_hbm, grad_hbm, log_ref, first_hbm, second_hbm,
     key_image_hbm, bias_hbm, small_ref, item_hbm, weight_hbm, d_hidden_hbm, grad_down_ref, grad_up_ref,
     grad_out_ref,
     main_out, tail_out, small_out, diagonal_out, input_out,
     *scratch) = refs
    static, scratch = scratch[:6], scratch[6:]
    (k_ref, v_ref, mixed_ref, grad_ref, first_ref, second_ref, key_image_ref, bias_ref, pair_sems,
     item_ref, weight_ref, d_hidden_ref, load_sems, d_project, item_t, tail, input_grad,
     small_in, diagonal_in, small_sems, item_sems, *scratch) = scratch
    place = Place(depth)
    step = pl.program_id(0)
    pairs = k_ref.shape[0]
    rows, width = item_hbm.shape
    count = rows // 2
    x = place.bits["x"]
    hidden = grad_down_ref.shape[0]
    sources = ((grad_down_ref, main_out, 0), (grad_up_ref, main_out, hidden), (tail, tail_out, 0))
    each = len(scratch) // len(plan)
    chunks = []
    for index, spot in enumerate(plan):
        chunks.append(
            Chunk(place, depth, *sources[spot[0]], spot, scratch[index * each : index * each + each])
        )
    hop_devices = list(place.partners.values())
    wide_hbm = (first_hbm, second_hbm, key_image_hbm, bias_hbm)
    wide_refs = (first_ref, second_ref, key_image_ref, bias_ref)

    def pair_loads(pair):
        copies = []
        held = (
            (projected_hbm, k_ref, width), (projected_hbm, v_ref, 2 * width),
            (mixed_hbm, mixed_ref, 0), (grad_hbm, grad_ref, 0),
        )
        for source, target, first in held:
            columns = pl.ds(pl.multiple_of(first + pair * LANES, LANES), LANES)
            copies.append((source.at[:, columns], target.at[pair]))
        heads = pl.ds(2 * pair, 2)
        for source, target in zip(wide_hbm, wide_refs):
            copies.append((source.at[heads], target.at[heads]))
        return [
            pltpu.make_async_copy(source, target, pair_sems.at[pair, index])
            for index, (source, target) in enumerate(copies)
        ]

    def loads():
        copies = [(item_hbm, item_ref), (weight_hbm, weight_ref), (d_hidden_hbm, d_hidden_ref)]
        for pair in range(pairs):
            down, across = out_spot(pair, pairs, width)
            copies.append(
                (
                    grad_out_ref.at[down, across],
                    tail.at[pl.ds(pair * TAIL_ROWS + width, TAIL_ROWS - width)],
                )
            )
        return [
            pltpu.make_async_copy(source, target, load_sems.at[index])
            for index, (source, target) in enumerate(copies)
        ]

    def input_copies():
        return [
            pltpu.make_async_copy(
                input_grad.at[pl.ds(pl.multiple_of(x * count, LANES), count)], input_out.at[x],
                item_sems.at[0],
            ),
            remote(
                input_grad.at[pl.ds(pl.multiple_of((1 - x) * count, LANES), count)],
                input_out.at[x], item_sems.at[1], item_sems.at[2], place.partners["x"],
            ),
        ]

    def small_copies(hop):
        return [
            remote(source, landing.at[hop], small_sems.at[0, kind, hop],
                   small_sems.at[1, kind, hop], hop_devices[hop])
            for kind, (source, landing) in enumerate(
                ((small_out, small_in), (diagonal_out, diagonal_in))
            )
        ]

    def small_stage(hop):
        if hop > 0:
            for copy in small_copies(hop - 1):
                copy.wait()
            small_out[...] = small_out[...] + small_in[hop - 1]
            diagonal_out[...] = diagonal_out[...] + diagonal_in[hop - 1]
        if hop < len(hop_devices):
            for copy in small_copies(hop):
                copy.start()

    def perform(slot):
        for index, stage in orders[slot]:
            if index == len(chunks):
                small_stage(stage)
            else:
                chunks[index].stage(stage)

    @pl.when(step == 0)
    def _():
        for pair in range(pairs):
            for copy in pair_loads(pair):
                copy.start()
        for copy in loads():
            copy.start()
        place.greet()
        small_out[...] = small_ref[...]

    for pair in range(pairs):
        @pl.when(step == pair)
        def _(pair=pair):
            perform(pair)

    @pl.when(step == 0)
    def _():
        static_prepare(meta_ref, static)
        for copy in loads():
            copy.wait()
        for tile in range(rows // TILE):
            there = slice(tile * TILE, tile * TILE + TILE)
            item_t[:, there] = jnp.transpose(item_ref[there].astype(F32)).astype(BF)

    for copy in pair_loads(step):
        copy.wait()
    (dq_even, dk_even, dv_even), (dq_odd, dk_odd, dv_odd) = [
        head_back(
            parity, step, rows_ref, wide_refs, k_ref, v_ref, mixed_ref, grad_ref, log_ref,
            static, diagonal_out,
        )
        for parity in range(2)
    ]
    even = own_lanes(0, rows)
    pieces = [
        jnp.transpose(jnp.concatenate([dq_even, dq_odd], axis=0)).astype(BF),
        jnp.where(even, dk_even, dk_odd).astype(BF),
        jnp.where(even, dv_even, dv_odd).astype(BF),
    ]
    for part, piece in enumerate(pieces):
        d_project[:, pl.ds(pl.multiple_of(part * width + step * LANES, LANES), LANES)] = piece
    slab = pl.ds(pl.multiple_of(step * TAIL_ROWS, TAIL_ROWS), width)
    tail[slab] = dot_nn(item_t[...], jnp.concatenate(pieces, axis=1)).astype(BF)

    @pl.when(step == pairs - 1)
    def _():
        perform(pairs)
        for begin in range(0, width, TILE):
            here = slice(begin, begin + TILE)
            total = d_hidden_ref[:, here] + dot_nt(d_project[...], weight_ref[here])
            input_grad[:, here] = total.astype(BF)
        for copy in input_copies():
            copy.start()
        for begin in range(0, width, TILE):
            here = slice(begin, begin + TILE)
            there = slice(2 * width + begin, 2 * width + begin + TILE)
            small_out[0:1, here] = column_sum(d_project[:, here].astype(F32))
            small_out[1:2, here] = column_sum(d_project[:, there].astype(F32))
        perform(pairs + 1)
        for copy in input_copies():
            copy.wait()


TAIL_ROWS = 1024


def out_spot(pair, pairs, width):
    down = TAIL_ROWS - width
    across = width * width // (pairs * down)
    per_row = width // across
    return (
        pl.ds(pair // per_row * down, down),
        pl.ds(pair % per_row * across, across),
    )


def summed_with_attention_back(
    meta_columns, meta_rows, projected, mixed, d_mixed, logs, wide_arrays, item, qkv_weight,
    d_hidden, small, grad_down, grad_up, grad_out,
):
    size = lax.axis_size("dp")
    depth = 4 if size % 16 == 0 else size // 4
    rows, width = item.shape
    pairs = width // LANES
    hidden = grad_down.shape[0]
    hops = len(hop_names(depth)) + 1
    work = [7.5] * pairs + [4.0]
    tall, wide = 1024, 3 * LANES
    plan = [
        (0, 0, tall, 0, width, 0, "yabx yxab", 1),
        (0, tall, tall, 0, width, 0, "yabx xaby", 0),
        (0, 2 * tall, tall, 0, width, 0, "yaxb xyab", 3),
        (1, 0, 2 * tall, 0, width, 0, "xaby axby", 2),
        (1, 2 * tall, tall, 0, width, 0, "xayb yaxb", 0),
        (2, 0, tall, 0, wide, 1, "xyab yxab", 0),
        (2, tall, tall, 0, wide, 2, "yaxb yxab", 3),
        (2, 2 * tall, tall, 0, wide, 3, "xyab yabx", 0),
        (2, 3 * tall, tall, 0, wide, 4, "xayb axby", 2),
        (2, 4 * tall, tall, 0, wide, 5, "yabx xyab", 1),
        (2, 5 * tall, tall, 0, wide, 6, "yxab xyab", 3),
    ]
    orders = planned([(spot[2],) + spot[4:] for spot in plan], work, depth, hops)

    whole = pl.BlockSpec(memory_space=pltpu.VMEM)
    diagonals = jax.ShapeDtypeStruct((2 * pairs, 8, LANES), F32)
    dma = pltpu.SemaphoreType.DMA
    scratch = []
    for spot in plan:
        scratch += chunk_scratch(spot[2], spot[4], depth)
    main, tail, small, diagonals, grad_input = pl.pallas_call(
        functools.partial(last_kernel, depth, plan, orders),
        grid=(pairs,),
        in_specs=[whole] * 2 + [HBM] * 3 + [whole] + [HBM] * 4 + [whole] + [HBM] * 6,
        out_specs=[HBM, HBM, whole, whole, HBM],
        out_shape=[
            jax.ShapeDtypeStruct((2 * hidden, width), BF),
            jax.ShapeDtypeStruct((pairs * TAIL_ROWS, 3 * LANES), BF),
            jax.ShapeDtypeStruct(small.shape, F32),
            diagonals,
            jax.ShapeDtypeStruct((2, rows // 2, width), BF),
        ],
        scratch_shapes=[pltpu.VMEM((rows, LANES), BF)] * 3
        + [pltpu.VMEM((LANES, rows), BF)] * 3
        + [pltpu.VMEM((pairs, rows, LANES), kind) for kind in (BF, BF, F32, BF)]
        + [pltpu.VMEM(array.shape, BF) for array in wide_arrays]
        + [
            dma((pairs, 8)),
            pltpu.VMEM((rows, width), BF),
            pltpu.VMEM((width, 3 * width), BF),
            pltpu.VMEM((rows, width), F32),
            dma((3 + pairs,)),
            pltpu.VMEM((rows, 3 * width), BF),
            pltpu.VMEM((width, rows), BF),
            pltpu.VMEM((pairs * TAIL_ROWS, 3 * LANES), BF),
            pltpu.VMEM((rows, width), BF),
            pltpu.VMEM((hops,) + small.shape, F32),
            pltpu.VMEM((hops,) + diagonals.shape, F32),
            dma((2, 2, hops)),
            dma((3,)),
        ]
        + scratch,
        compiler_params=pltpu.CompilerParams(
            collective_id=0, has_side_effects=True, vmem_limit_bytes=62 * MIB
        ),
        name="summed_with_attention_back",
    )(meta_columns, meta_rows, projected, mixed, d_mixed, logs, *wide_arrays,
      small, item, qkv_weight, d_hidden, grad_down, grad_up, grad_out)
    span = 4 * depth
    if size > span:
        groups = [list(range(first, size, span)) for first in range(span)]
        main, tail, small, diagonals = lax.psum(
            (main.astype(F32), tail.astype(F32), small, diagonals), "dp",
            axis_index_groups=groups,
        )
        main, tail = main.astype(BF), tail.astype(BF)
    return main, tail, small, diagonals, grad_input


def per_device(
    layer_in, segment, key_mask, position, layout_x, layout_y,
    qkv_weight, query_bias, value_bias, out_weight, out_bias, attn_gain, attn_shift,
    up_weight, up_bias, down_weight, down_bias, ffn_gain, ffn_shift,
    text_table, horiz_table, vert_table, cotangent,
):
    width = layer_in.shape[-1]
    item, projected, meta_columns, meta_rows, table_rows = projected_item(
        layer_in, (segment, key_mask, position, layout_x, layout_y),
        qkv_weight, query_bias, value_bias, (text_table, horiz_table, vert_table),
    )
    mixed, logs, *wide_arrays = attention_forward(meta_columns, meta_rows, table_rows, projected, width)
    layer_out, d_hidden, d_mixed, grad_out, grad_down, grad_up, small = fed_forward_and_back(
        item, mixed, cotangent, out_weight, up_weight, down_weight,
        (out_bias, attn_gain, attn_shift, up_bias, down_bias, ffn_gain, ffn_shift),
    )
    main, tail, small, diagonals, grad_input = summed_with_attention_back(
        meta_columns, meta_rows, projected, mixed, d_mixed, logs, wide_arrays, item, qkv_weight,
        d_hidden, small, grad_down, grad_up, grad_out,
    )
    done = finished(
        main, tail, grad_input, small, diagonals, up_weight.shape[1], text_table.shape[0]
    )
    sum_down, sum_up, sum_out, sum_qkv, grad_input = done[:5]
    singles, tables = done[5:14], [t.T for t in done[14:]]
    return (
        layer_out, grad_input, sum_qkv, singles[0], singles[1], sum_out, singles[2], singles[3],
        singles[4], sum_up, singles[8], sum_down, singles[5], singles[6], singles[7],
        tables[0], tables[1], tables[2],
    )


def solution(mesh):
    rows = P("dp", "seq", None)
    marks_spec = P("dp", "seq")
    return jax.shard_map(
        per_device,
        mesh=mesh,
        in_specs=(rows,) + (marks_spec,) * 5 + (P(),) * 16 + (rows,),
        out_specs=(rows, rows) + (P(),) * 16,
        check_vma=False,
    )
```

```python
import functools

import jax
import jax.numpy as jnp
from jax import lax
from jax.experimental import pallas as pl
from jax.experimental.pallas import tpu as pltpu
from jax.sharding import PartitionSpec as P

BF = jnp.bfloat16
F32 = jnp.float32
BIG = 1e30
LANES = 128
HEAD = 64
TEXT = 512
POS = 64
COORD = 48
Y0 = 64
GROUP0 = 112
MEMBER0 = 116
FLAG = 124
X_TABLE = 33
Y_TABLE = 66
NOTHING = 127


def dot_nt(a, b):
    return lax.dot_general(a, b, (((1,), (1,)), ((), ())), preferred_element_type=F32)


def dot_nn(a, b):
    return lax.dot_general(a, b, (((1,), (0,)), ((), ())), preferred_element_type=F32)


def looked_up(table_row, index):
    rows = index.shape[0]
    return jnp.take_along_axis(
        jnp.broadcast_to(table_row, (rows, LANES)), index, axis=1, mode="promise_in_bounds"
    )


def bucket(distance):
    return jnp.clip(distance, -16, 16) + 16


def between(lane, low, high):
    return (lane >= low) & (lane < high)


def columns_of(meta_ref):
    return tuple(meta_ref[:, field : field + 1] for field in range(5))


def marks(meta_ref):
    segment, key_mask, position, across, down = columns_of(meta_ref)
    rows = segment.shape[0]
    lane = lax.broadcasted_iota(jnp.int32, (rows, LANES), 1)
    row = lax.broadcasted_iota(jnp.int32, (rows, LANES), 0)
    even = between(lane, HEAD, HEAD + COORD) & (lane - HEAD == across)
    odd = (lane < COORD) & (lane == across)
    group = (segment - 1) >> 3
    member = (segment - 1) & 7
    named = segment > 0
    shared = (
        ((row < TEXT) & (lane < POS) & (lane == position))
        | (between(lane, Y0, Y0 + COORD) & (lane - Y0 == down))
        | (named & between(lane, GROUP0, MEMBER0) & (lane - GROUP0 == group))
        | (named & between(lane, MEMBER0, FLAG) & (lane - MEMBER0 == member))
        | ((lane == FLAG) & (key_mask <= 0))
    )
    return tuple(jnp.where(m, 1.0, 0.0).astype(BF) for m in (even, odd, shared))


def barred(meta_ref):
    segment = meta_ref[:, 0:1]
    rows = segment.shape[0]
    lane = lax.broadcasted_iota(jnp.int32, (rows, LANES), 1)
    group = (segment - 1) >> 3
    member = (segment - 1) & 7
    shut = (
        ((segment > 0) & between(lane, GROUP0, MEMBER0) & (lane - GROUP0 != group))
        | ((segment < 0) & between(lane, GROUP0, MEMBER0))
        | ((segment > 0) & between(lane, MEMBER0, FLAG) & (lane - MEMBER0 != member))
        | (lane == FLAG)
    )
    return jnp.where(shut, -BIG, 0.0).astype(F32)


def query_index(meta_ref):
    segment, key_mask, position, across, down = columns_of(meta_ref)
    rows = segment.shape[0]
    lane = lax.broadcasted_iota(jnp.int32, (rows, LANES), 1)
    x_even = bucket(across - (lane - HEAD)) + X_TABLE
    x_odd = bucket(across - lane) + X_TABLE
    even = jnp.where(between(lane, HEAD, HEAD + COORD), x_even, NOTHING)
    odd = jnp.where(lane < COORD, x_odd, NOTHING)
    shared = jnp.where(
        lane < POS,
        bucket(position - lane),
        jnp.where(between(lane, Y0, Y0 + COORD), bucket(down - (lane - Y0)) + Y_TABLE, NOTHING),
    )
    return even, odd, shared


def image_key_index(meta_ref):
    position = meta_ref[TEXT:, 2:3]
    lane = lax.broadcasted_iota(jnp.int32, (position.shape[0], LANES), 1)
    return jnp.where(lane < POS, bucket(lane - position), NOTHING)


def prepare(meta_ref, mark_refs, bar_ref, index_refs, key_index_ref):
    for ref, value in zip(mark_refs, marks(meta_ref)):
        ref[...] = value
    bar_ref[...] = barred(meta_ref)
    for ref, value in zip(index_refs, query_index(meta_ref)):
        ref[...] = value
    key_index_ref[...] = image_key_index(meta_ref)


def image_offsets(row_positions, column_positions):
    return bucket(column_positions - row_positions)


def own_lanes(parity, rows):
    lane = lax.broadcasted_iota(jnp.int32, (rows, LANES), 1)
    return (lane < HEAD) if parity == 0 else (lane >= HEAD)


def widened(parity, q, table_row, bar_ref, index_refs, key_index_ref, shared_ref):
    rows = q.shape[0]
    images = key_index_ref.shape[0]
    first = jnp.where(
        own_lanes(parity, rows),
        q.astype(F32) * 0.125,
        looked_up(table_row, index_refs[parity][...]),
    )
    second = (looked_up(table_row, index_refs[2][...]) + bar_ref[...]).astype(BF)
    image_lane = lax.broadcasted_iota(jnp.int32, (images, LANES), 1)
    key_image = jnp.where(
        image_lane < POS, looked_up(table_row, key_index_ref[...]).astype(BF), shared_ref[TEXT:]
    )
    return first.astype(BF), second, key_image


def joined(parity, first, second, key_image, k, marks_own, shared):
    rows = k.shape[0]
    lane = lax.broadcasted_iota(jnp.int32, (rows, LANES), 1)
    to_image = jnp.where(lane < POS, shared, second)
    key_first = jnp.where(own_lanes(parity, rows), k, marks_own)
    q_text = jnp.concatenate([first, second], axis=1)
    q_image = jnp.concatenate([first, to_image], axis=1)
    k_text = jnp.concatenate([key_first[:TEXT], shared[:TEXT]], axis=1)
    k_image = jnp.concatenate([key_first[TEXT:], key_image], axis=1)
    return q_text, q_image, k_text, k_image


def image_bias(table_row, offsets):
    return jnp.concatenate(
        [looked_up(table_row, offsets[:, :LANES]), looked_up(table_row, offsets[:, LANES:])], axis=1
    )


def forward_kernel(
    meta_ref, rows_ref, table_ref, q_ref, k_ref, v_ref,
    mixed_ref, log_ref, first_ref, second_ref, key_image_ref, bias_ref,
    even_ref, odd_ref, shared_ref, bar_ref, index_even, index_odd, index_shared, key_index_ref,
):
    mark_refs = (even_ref, odd_ref, shared_ref)
    index_refs = (index_even, index_odd, index_shared)

    @pl.when(pl.program_id(0) == 0)
    def _():
        prepare(meta_ref, mark_refs, bar_ref, index_refs, key_index_ref)

    rows = q_ref.shape[0]
    images = rows - TEXT
    q, k, v = q_ref[...], k_ref[...], v_ref[...]
    offsets = bucket(rows_ref[2:3, TEXT:] - meta_ref[TEXT:, 2:3])
    tile = 256
    v_turned = transposed(v)
    heads = [None, None]

    def prepared(parity):
        table_row = table_ref[pl.ds(2 * pl.program_id(0) + parity, 1), :]
        first, second, key_image = widened(
            parity, q, table_row, bar_ref, index_refs, key_index_ref, shared_ref
        )
        bias = image_bias(table_row, offsets)
        first_ref[parity] = first
        second_ref[parity] = second
        key_image_ref[parity] = key_image
        bias_ref[parity] = bias.astype(BF)
        wide = joined(
            parity, first, second, key_image, k, mark_refs[parity][...], shared_ref[...]
        )
        heads[parity] = wide + (bias,)

    def scored(parity, start):
        q_text, q_image, k_text, k_image, bias = heads[parity]
        here = slice(start, start + tile)
        on_image = dot_nt(k_image, q_image[here])
        if start >= TEXT:
            on_image = on_image + bias[:, start - TEXT : start - TEXT + tile]
        return dot_nt(k_text, q_text[here]), on_image

    spots = [(parity, start) for parity in range(2) for start in range(0, rows, tile)]
    outs = ([], [])
    prepared(0)
    following = scored(*spots[0])
    for index, (parity, start) in enumerate(spots):
        on_text, on_image = following
        if index == 1:
            prepared(1)
        if index + 1 < len(spots):
            following = scored(*spots[index + 1])
        top = jnp.maximum(
            jnp.max(on_text, axis=0, keepdims=True), jnp.max(on_image, axis=0, keepdims=True)
        )
        on_text = jnp.exp(on_text - top)
        on_image = jnp.exp(on_image - top)
        total = jnp.sum(on_text, axis=0, keepdims=True) + jnp.sum(on_image, axis=0, keepdims=True)
        own = slice(parity * HEAD, parity * HEAD + HEAD)
        out = dot_nn(v_turned[own, :TEXT], on_text.astype(BF)) + dot_nn(
            v_turned[own, TEXT:], on_image.astype(BF)
        )
        outs[parity].append(out * (1.0 / total))
        log_ref[0, parity : parity + 1, start : start + tile] = top + jnp.log(total)
    mixed_ref[...] = jnp.transpose(
        jnp.concatenate([jnp.concatenate(outs[parity], axis=1) for parity in range(2)], axis=0)
    )


def static_scratch(rows):
    return [
        pltpu.VMEM((rows, LANES), BF),
        pltpu.VMEM((rows, LANES), BF),
        pltpu.VMEM((rows, LANES), BF),
        pltpu.VMEM((rows, LANES), F32),
        pltpu.VMEM((rows, LANES), jnp.int32),
        pltpu.VMEM((rows, LANES), jnp.int32),
        pltpu.VMEM((rows, LANES), jnp.int32),
        pltpu.VMEM((rows - TEXT, LANES), jnp.int32),
    ]


def attention_forward(meta_columns, meta_rows, table_rows, projected, width):
    rows = projected.shape[0]
    images = rows - TEXT
    pairs = width // LANES

    def block(part):
        return pl.BlockSpec((rows, LANES), lambda p: (0, part * pairs + p))

    whole = lambda shape: pl.BlockSpec(shape, lambda p: (0,) * len(shape))
    return pl.pallas_call(
        forward_kernel,
        grid=(pairs,),
        in_specs=[
            whole(meta_columns.shape),
            whole(meta_rows.shape),
            whole(table_rows.shape),
            block(0), block(1), block(2),
        ],
        out_specs=[
            pl.BlockSpec((rows, LANES), lambda p: (0, p)),
            pl.BlockSpec((1, 2, rows), lambda p: (p, 0, 0)),
            pl.BlockSpec((2, rows, LANES), lambda p: (p, 0, 0)),
            pl.BlockSpec((2, rows, LANES), lambda p: (p, 0, 0)),
            pl.BlockSpec((2, images, LANES), lambda p: (p, 0, 0)),
            pl.BlockSpec((2, images, images), lambda p: (p, 0, 0)),
        ],
        out_shape=[
            jax.ShapeDtypeStruct((rows, width), F32),
            jax.ShapeDtypeStruct((pairs, 2, rows), F32),
            jax.ShapeDtypeStruct((2 * pairs, rows, LANES), BF),
            jax.ShapeDtypeStruct((2 * pairs, rows, LANES), BF),
            jax.ShapeDtypeStruct((2 * pairs, images, LANES), BF),
            jax.ShapeDtypeStruct((2 * pairs, images, images), BF),
        ],
        scratch_shapes=static_scratch(rows),
        compiler_params=pltpu.CompilerParams(vmem_limit_bytes=60 * 1024 * 1024),
        name="attention_forward",
    )(meta_columns, meta_rows, table_rows, projected, projected, projected)


def skewed(block):
    size = block.shape[0]
    lane = lax.broadcasted_iota(jnp.int32, (size, LANES), 1)
    row = lax.broadcasted_iota(jnp.int32, (size, LANES), 0)
    turned = jnp.take_along_axis(
        block, (lane + row) & (LANES - 1), axis=1, mode="promise_in_bounds"
    )
    straight = lane + row < LANES
    above = jnp.sum(jnp.where(straight, turned, 0.0), axis=0, keepdims=True)
    below = jnp.sum(jnp.where(straight, 0.0, turned), axis=0, keepdims=True)
    return above, below


def transposed(array):
    return jnp.transpose(array.astype(F32)).astype(array.dtype)


def static_prepare(meta_ref, static):
    for ref, turned, value in zip(static[:3], static[3:], marks(meta_ref)):
        ref[...] = value
        turned[...] = transposed(value)


def head_back(
    parity, pair, rows_ref, wide_refs, k_ref, v_ref, mixed_ref, grad_ref, log_ref, static, diag_ref,
):
    mark_refs, turned_refs = static[:3], static[3:]
    first_ref, second_ref, key_image_ref, bias_ref = wide_refs
    head = 2 * pair + parity
    shared_t = turned_refs[2]
    rows = k_ref.shape[1]
    images = rows - TEXT
    tile = 256
    k, v, grad = k_ref[pair], v_ref[pair], grad_ref[pair]
    products = grad.astype(F32) * mixed_ref[pair]
    k_turned = transposed(k)
    is_image = rows_ref[1:2, TEXT:] > 0
    own = own_lanes(parity, rows)
    log_row = log_ref[pair, parity : parity + 1, :]
    first, shared = first_ref[head], mark_refs[2][...]
    q_text, q_image, k_text, k_image = joined(
        parity, first, second_ref[head], key_image_ref[head], k, mark_refs[parity][...], shared
    )
    bias = bias_ref[head].astype(F32)
    ones = jnp.where(own_lanes(parity, 8), 1.0, 0.0).astype(BF)
    delta = jnp.zeros((8, rows), F32)
    rest = products
    for _ in range(3):
        piece = rest.astype(BF)
        delta = delta + dot_nt(ones, piece)
        rest = rest - piece.astype(F32)
    delta = delta[0:1]
    v_own = jnp.where(own, v, jnp.zeros_like(v))
    q_marked = jnp.concatenate(
        [jnp.where(own, first, mark_refs[parity][...]), shared], axis=1
    )
    dq = jnp.zeros((HEAD, rows), F32)
    dks = []
    dvs = []
    first_sum = jnp.zeros((LANES, LANES), F32)
    second_sum = jnp.zeros((LANES, LANES), F32)
    text_image = jnp.zeros((LANES, images), F32)
    def scored(start):
        here = slice(start, start + tile)
        if start < TEXT:
            scores = dot_nt(k_text[here], q_text)
        else:
            scores = dot_nt(k_image[start - TEXT : start - TEXT + tile], q_image)
            scores = jnp.concatenate([scores[:, :TEXT], scores[:, TEXT:] + bias], axis=1)
        return scores, dot_nt(v_own[here], grad)

    following = scored(0)
    for start in range(0, rows, tile):
        here = slice(start, start + tile)
        scores, prob_grad = following
        if start + tile < rows:
            following = scored(start + tile)
        soft = jnp.exp(scores - log_row)
        score_grad = soft * (prob_grad - delta)
        low = score_grad.astype(BF)
        dvs.append(dot_nn(soft.astype(BF), grad))
        wide = dot_nn(low, q_marked)
        dks.append(wide[:, :LANES])
        dq = dq + dot_nn(k_turned[parity * HEAD : parity * HEAD + HEAD, here], low)
        rounded = wide.astype(BF)
        first_sum = first_sum + dot_nn(turned_refs[parity][:, here], rounded[:, :LANES])
        second_sum = second_sum + dot_nn(shared_t[:, here], rounded[:, LANES:])
        if start < TEXT:
            text_image = text_image + dot_nn(shared_t[:, here], low[:, TEXT:])
        else:
            by_position = wide[:, LANES:]
            on_image = score_grad[:, TEXT:]
    small = lax.broadcasted_iota(jnp.int32, (LANES, LANES), 1)
    small_row = lax.broadcasted_iota(jnp.int32, (LANES, LANES), 0)
    x0 = HEAD if parity == 0 else 0
    x_block = jnp.where(
        between(small, x0, x0 + COORD) & between(small_row, x0, x0 + COORD), first_sum, 0.0
    )
    y_block = jnp.where(
        between(small, Y0, Y0 + COORD) & between(small_row, Y0, Y0 + COORD), second_sum, 0.0
    )
    p_block = jnp.where((small < POS) & (small_row < POS), second_sum, 0.0)
    wide_lane = lax.broadcasted_iota(jnp.int32, (images, images), 1)
    outside = jnp.sum(jnp.where(is_image, 0.0, on_image), axis=1, keepdims=True)
    pairs = jnp.where(is_image, on_image, 0.0) + jnp.where(wide_lane == 0, outside, 0.0)
    outside_text = jnp.sum(jnp.where(is_image, 0.0, text_image), axis=1, keepdims=True)
    text_lane = lax.broadcasted_iota(jnp.int32, (LANES, images), 1)
    text_row = lax.broadcasted_iota(jnp.int32, (LANES, images), 0)
    text_image = jnp.where(is_image, text_image, 0.0) + jnp.where(
        text_lane == 0, outside_text, 0.0
    )
    text_image = jnp.where(text_row < POS, text_image, 0.0)
    first_lane = lax.broadcasted_iota(jnp.int32, (images, LANES), 1)
    left = pairs[:, :LANES] + jnp.where(first_lane < POS, by_position, 0.0)
    right = pairs[:, LANES:]
    a00, b00 = skewed(left[:LANES] + text_image[:, :LANES] + p_block)
    a01, b01 = skewed(right[:LANES] + text_image[:, LANES:])
    a10, b10 = skewed(left[LANES:])
    a11, b11 = skewed(right[LANES:])
    ax, bx = skewed(x_block)
    ay, by = skewed(y_block)
    diag_ref[head] = jnp.concatenate(
        [b10, b00 + b11 + a10, a00 + a11 + b01, a01, bx, ax, by, ay], axis=0
    )
    return dq * 0.125, jnp.concatenate(dks, axis=0), jnp.concatenate(dvs, axis=0)


MESH = pl.DeviceIdType.MESH
VMEM = pl.BlockSpec(memory_space=pltpu.VMEM)
HBM = pl.BlockSpec(memory_space=pltpu.HBM)
MIB = 1024 * 1024


def remote(src, dst, send, receive, device):
    return pltpu.make_async_remote_copy(
        src_ref=src, dst_ref=dst, send_sem=send, recv_sem=receive, device_id=device,
        device_id_type=MESH,
    )


def project_kernel(
    layer_ref, weight_hbm, *refs,
):
    small_hbm, refs = refs[:10], refs[10:]
    (item_ref, projected_out, columns_ref, rows_ref, table_ref,
     projected_ref, weight_ref, meta_send, bias_ref, sems, load_sems, store_sems), small = (
        refs[:12], refs[12:],
    )
    (segment_ref, mask_ref, position_ref, across_ref, down_ref, query_bias_ref, value_bias_ref,
     text_ref, horiz_ref, vert_ref) = small
    mine = lax.axis_index("seq")
    partner = (1 - mine, lax.axis_index("dp"))
    count, width = layer_ref.shape[1:]
    own = pl.ds(pl.multiple_of(mine * count, LANES), count)
    loads = [
        pltpu.make_async_copy(source, target, load_sems.at[index])
        for index, (source, target) in enumerate(
            list(zip(small_hbm, small))
            + [(layer_ref.at[mine], item_ref.at[own]), (weight_hbm, weight_ref)]
        )
    ]
    for load in loads:
        load.start()
    barrier = pltpu.get_barrier_semaphore()
    pl.semaphore_signal(barrier, inc=1, device_id=partner, device_id_type=MESH)
    pl.semaphore_wait(barrier, 1)
    pieces = count // LANES
    rows_out = [
        remote(
            layer_ref.at[1 - mine, pl.ds(piece * LANES, LANES)],
            item_ref.at[pl.ds(pl.multiple_of(mine * count + piece * LANES, LANES), LANES)],
            sems.at[0, piece], sems.at[1, piece], partner,
        )
        for piece in range(pieces)
    ]
    for copy in rows_out:
        copy.start()
    for load in loads[:-2]:
        load.wait()

    fields = (segment_ref, mask_ref, position_ref, across_ref, down_ref)
    blocks = [
        jnp.concatenate(
            [field[item : item + 1, :] for field in fields] + [jnp.zeros((3, count), jnp.int32)],
            axis=0,
        )
        for item in range(2)
    ]
    meta_send[...] = jnp.where(mine == 0, blocks[1], blocks[0])
    meta_out = remote(
        meta_send, rows_ref.at[:, own], sems.at[0, pieces], sems.at[1, pieces], partner
    )
    meta_out.start()
    rows_ref[:, own] = jnp.where(mine == 0, blocks[0], blocks[1])
    bias_ref[:, :width] = query_bias_ref[...].astype(F32).reshape(1, width)
    bias_ref[:, width : 2 * width] = jnp.zeros((1, width), F32)
    bias_ref[:, 2 * width :] = value_bias_ref[...].astype(F32).reshape(1, width)
    heads, levels = text_ref.shape
    spot = lax.broadcasted_iota(jnp.int32, (levels, LANES), 1)
    level = lax.broadcasted_iota(jnp.int32, (levels, LANES), 0)
    table = jnp.zeros((heads, LANES), F32)
    for source, begin in ((text_ref, 0), (horiz_ref, X_TABLE), (vert_ref, Y_TABLE)):
        table = table + dot_nn(source[...], (spot == level + begin).astype(BF))
    table_ref[...] = jnp.concatenate([table, jnp.zeros((16 - heads, LANES), F32)], axis=0)

    def project(there):
        step = 256

        def body(index, carry):
            columns = pl.ds(pl.multiple_of(index * step, step), step)
            product = dot_nn(item_ref[there], weight_ref[:, columns])
            projected_ref[there, columns] = (product + bias_ref[:, columns]).astype(BF)
            return carry

        lax.fori_loop(0, 3 * width // step, body, 0)

    def stored(index, there):
        return pltpu.make_async_copy(
            projected_ref.at[there], projected_out.at[there], store_sems.at[index]
        )

    for load in loads[-2:]:
        load.wait()
    project(own)
    stored(0, own).start()
    for piece in range(pieces):
        rows_out[piece].wait()
        there = pl.ds(pl.multiple_of((1 - mine) * count + piece * LANES, LANES), LANES)
        project(there)
        stored(1 + piece, there).start()
    meta_out.wait()
    meta = rows_ref[...].astype(F32)
    tall = jnp.concatenate([meta, jnp.zeros((LANES - 8, meta.shape[1]), F32)], axis=0)
    columns_ref[...] = jnp.transpose(tall).astype(jnp.int32)
    stored(0, own).wait()
    for piece in range(pieces):
        there = pl.ds(pl.multiple_of((1 - mine) * count + piece * LANES, LANES), LANES)
        stored(1 + piece, there).wait()


def projected_item(layer_in, fields, qkv_weight, query_bias, value_bias, tables):
    rows = 2 * layer_in.shape[1]
    width = layer_in.shape[2]
    pieces = rows // 2 // LANES
    small = list(fields) + [query_bias, value_bias] + [t.T for t in tables]
    return pl.pallas_call(
        project_kernel,
        in_specs=[HBM] * (2 + len(small)),
        out_specs=[VMEM, HBM, VMEM, VMEM, VMEM],
        out_shape=[
            jax.ShapeDtypeStruct((rows, width), BF),
            jax.ShapeDtypeStruct((rows, 3 * width), BF),
            jax.ShapeDtypeStruct((rows, LANES), jnp.int32),
            jax.ShapeDtypeStruct((8, rows), jnp.int32),
            jax.ShapeDtypeStruct((16, LANES), F32),
        ],
        scratch_shapes=[
            pltpu.VMEM((rows, 3 * width), BF),
            pltpu.VMEM((width, 3 * width), BF),
            pltpu.VMEM((8, rows // 2), jnp.int32),
            pltpu.VMEM((1, 3 * width), F32),
            pltpu.SemaphoreType.DMA((2, pieces + 1)),
            pltpu.SemaphoreType.DMA((len(small) + 2,)),
            pltpu.SemaphoreType.DMA((pieces + 1,)),
        ]
        + [pltpu.VMEM(array.shape, array.dtype) for array in small],
        compiler_params=pltpu.CompilerParams(
            collective_id=1, has_side_effects=True, vmem_limit_bytes=60 * MIB
        ),
        name="projected_item",
    )(layer_in, qkv_weight, *small)


EPSILON = 1e-05
TILE = 256


def vector(ref):
    return ref[...].astype(F32).reshape(1, ref.shape[0])


def gelu_and_slope(x):
    bell = jnp.exp2(-0.7213475204444817 * (x * x))
    rough = 1.0 + 0.23164188826 * jnp.abs(x)
    t = pl.reciprocal(rough, approx=True)
    t = t * (2.0 - rough * t)
    series = t * (
        0.127414796
        + t * (-0.142248368 + t * (0.7107068705 + t * (-0.7265760135 + t * 0.5307027145)))
    )
    tail = bell * series
    below = jnp.where(x >= 0.0, 1.0 - tail, tail)
    return x * below, below + x * (0.3989422804014327 * bell)


def row_mean(block):
    return jnp.mean(block, axis=1, keepdims=True)


def normalized(hidden):
    center = hidden - row_mean(hidden)
    scale = lax.rsqrt(row_mean(center * center) + EPSILON)
    return center * scale, scale


def norm_pulled(grad, unit, scale):
    return scale * (grad - row_mean(grad) - unit * row_mean(grad * unit))


def column_sum(block):
    return jnp.sum(block, axis=0, keepdims=True)


def feed_kernel(
    item_ref, mixed_ref, cotangent_ref, out_weight_ref, up_ref, down_ref, *refs,
):
    vectors_hbm, refs = refs[:7], refs[7:]
    (layer_out, d_hidden_ref, d_mixed_ref, grad_out_ref, grad_down_ref, grad_up_ref, small_ref,
     layer_ref, cotangent_all, active, slope, unit, scale_ref, normed, normed_t, total, d_branch, d_branch_t,
     sems, load_sems) = refs[:20]
    vectors = refs[20:]
    (out_bias_ref, attn_gain_ref, attn_shift_ref, up_bias_ref, down_bias_ref, ffn_gain_ref,
     ffn_shift_ref) = vectors
    step = pl.program_id(0)
    blocks = pl.num_programs(0) // 2
    rows, width = item_ref.shape
    count = rows // 2
    mine = lax.axis_index("seq")
    partner = (1 - mine, lax.axis_index("dp"))
    own = pl.ds(pl.multiple_of(mine * count, LANES), count)
    tiles = rows // TILE

    def sent():
        return remote(
            cotangent_ref.at[1 - mine], cotangent_all.at[own], sems.at[0], sems.at[1], partner
        )

    def returned():
        theirs = pl.ds(pl.multiple_of((1 - mine) * count, LANES), count)
        return [
            pltpu.make_async_copy(layer_ref.at[own], layer_out.at[mine], load_sems.at[8]),
            remote(
                layer_ref.at[theirs], layer_out.at[mine], sems.at[2], sems.at[3], partner
            ),
        ]

    def loads():
        copies = list(zip(vectors_hbm, vectors)) + [(cotangent_ref.at[mine], cotangent_all.at[own])]
        return [
            pltpu.make_async_copy(source, target, load_sems.at[index])
            for index, (source, target) in enumerate(copies)
        ]

    def over_tiles(size, body, carry, unroll=1):
        def run(index, state):
            return body(pl.ds(pl.multiple_of(index * size, size), size), state)

        return lax.fori_loop(0, rows // size, run, carry, unroll=unroll)

    @pl.when(step == 0)
    def _():
        for load in loads():
            load.start()
        barrier = pltpu.get_barrier_semaphore()
        pl.semaphore_signal(barrier, inc=1, device_id=partner, device_id_type=MESH)
        pl.semaphore_wait(barrier, 1)
        sent().start()
        small_ref[...] = jnp.zeros_like(small_ref)
        for load in loads():
            load.wait()
        out_bias, gain, shift = vector(out_bias_ref), vector(attn_gain_ref), vector(attn_shift_ref)

        def tile(there, carry):
            attn = dot_nn(mixed_ref[there].astype(BF), out_weight_ref[...]) + out_bias
            standard, scale = normalized(item_ref[there].astype(F32) + attn)
            unit[there] = standard
            scale_ref[there] = jnp.broadcast_to(scale, (scale.shape[0], LANES))
            result = standard * gain + shift
            normed[there] = result.astype(BF)
            normed_t[:, there] = jnp.transpose(result).astype(BF)
            return carry

        over_tiles(TILE, tile, 0, 3)
        total[...] = jnp.zeros_like(total)

    @pl.when(step < blocks)
    def _():
        columns = [slice(begin, begin + TILE) for begin in range(0, width, TILE)]
        low = normed[...]
        following = dot_nn(low, up_ref[:, columns[0]])
        values = []
        for index, here in enumerate(columns):
            product = following
            if index + 1 < len(columns):
                following = dot_nn(low, up_ref[:, columns[index + 1]])
            bias = up_bias_ref[pl.ds(pl.multiple_of(step * width + here.start, LANES), TILE)]
            value, grade = gelu_and_slope(product + bias.astype(F32).reshape(1, TILE))
            values.append(value.astype(BF))
            active[step, :, here] = values[-1]
            slope[step, :, here] = grade
        values = jnp.concatenate(values, axis=1)
        for here in columns:
            total[:, here] += dot_nn(values, down_ref[:, here])

    @pl.when(step == blocks)
    def _():
        sent().wait()
        gain, shift, bias = vector(ffn_gain_ref), vector(ffn_shift_ref), vector(down_bias_ref)
        first_gain, first_shift = vector(attn_gain_ref), vector(attn_shift_ref)

        def tile(there, sums):
            hidden = unit[there] * first_gain + first_shift + (total[there] + bias)
            standard, scale = normalized(hidden)
            layer_ref[there] = (standard * gain + shift).astype(BF)
            cotangent = cotangent_all[there].astype(F32)
            pulled = norm_pulled(cotangent * gain, standard, scale)
            total[there] = pulled
            low = pulled.astype(BF)
            d_branch[there] = low
            return (
                sums[0] + column_sum(low.astype(F32)),
                sums[1] + column_sum(cotangent * standard),
                sums[2] + column_sum(cotangent),
            )

        zero = jnp.zeros((1, width), F32)
        sums = over_tiles(64, tile, (zero, zero, zero), 4)
        for row, value in zip((5, 6, 7), sums):
            small_ref[row : row + 1] = value

        for copy in returned():
            copy.start()

        def turn(there, carry):
            d_branch_t[:, there] = jnp.transpose(d_branch[there].astype(F32)).astype(BF)
            return carry

        over_tiles(TILE, turn, 0, 3)

    @pl.when(step >= blocks)
    def _():
        block = step - blocks

        columns = [slice(begin, begin + TILE) for begin in range(0, width, TILE)]
        branch = d_branch[...]
        turned = d_branch_t[...]
        following = dot_nt(branch, down_ref[columns[0]])
        values = []
        for index, here in enumerate(columns):
            product = following
            if index + 1 < len(columns):
                following = dot_nt(branch, down_ref[columns[index + 1]])
            grad_down_ref[:, here] = dot_nn(turned, active[block, :, here]).astype(BF)
            d_up = (product * slope[block, :, here]).astype(BF)
            small_ref[pl.ds(8 + block, 1), here] = column_sum(d_up.astype(F32))
            values.append(d_up)
        values = jnp.concatenate(values, axis=1)
        turned = normed_t[...]
        for here in columns:
            grad_up_ref[:, here] = dot_nn(turned, values[:, here]).astype(BF)
            total[:, here] += dot_nt(values, up_ref[here])

    @pl.when(step == 2 * blocks - 1)
    def _():
        gain = vector(attn_gain_ref)

        def tile(there, sums):
            d_normed = total[there]
            standard = unit[there]
            d_hidden = norm_pulled(d_normed * gain, standard, scale_ref[there, :1])
            d_hidden_ref[there] = d_hidden
            low = d_hidden.astype(BF)
            d_branch[there] = low
            return (
                sums[0] + column_sum(low.astype(F32)),
                sums[1] + column_sum(d_normed * standard),
                sums[2] + column_sum(d_normed),
            )

        zero = jnp.zeros((1, width), F32)
        sums = over_tiles(64, tile, (zero, zero, zero), 4)
        for row, value in zip((2, 3, 4), sums):
            small_ref[row : row + 1] = value

        def turn(there, carry):
            normed_t[:, there] = jnp.transpose(mixed_ref[there]).astype(BF)
            return carry

        over_tiles(TILE, turn, 0, 3)

        for begin in range(0, width, TILE):
            here = slice(begin, begin + TILE)
            d_mixed_ref[:, here] = dot_nt(d_branch[...], out_weight_ref[here]).astype(BF)
            grad_out_ref[:, here] = dot_nn(normed_t[...], d_branch[:, here]).astype(BF)

        for copy in returned():
            copy.wait()


def fed_forward_and_back(
    item, mixed, cotangent, out_weight, up_weight, down_weight, vectors,
):
    rows, width = item.shape
    blocks = up_weight.shape[1] // width
    whole = pl.BlockSpec(memory_space=pltpu.VMEM)
    square = lambda kind: jax.ShapeDtypeStruct((rows, width), kind)
    later = lambda i: jnp.maximum(i - blocks, 0)
    return pl.pallas_call(
        feed_kernel,
        grid=(2 * blocks,),
        in_specs=[whole, whole, HBM, whole]
        + [
            pl.BlockSpec((width, width), lambda i: (0, lax.rem(i, blocks))),
            pl.BlockSpec((width, width), lambda i: (lax.rem(i, blocks), 0)),
        ]
        + [HBM] * 7,
        out_specs=[HBM] + [whole] * 3
        + [
            pl.BlockSpec((width, width), lambda i: (later(i), 0)),
            pl.BlockSpec((width, width), lambda i: (later(i), 0)),
            whole,
        ],
        out_shape=[
            jax.ShapeDtypeStruct((2, rows // 2, width), BF), square(F32), square(BF),
            jax.ShapeDtypeStruct((width, width), BF),
            jax.ShapeDtypeStruct((blocks * width, width), BF),
            jax.ShapeDtypeStruct((blocks * width, width), BF),
            jax.ShapeDtypeStruct((16, width), F32),
        ],
        scratch_shapes=[
            pltpu.VMEM((rows, width), BF),
            pltpu.VMEM((rows, width), BF),
            pltpu.VMEM((blocks, rows, width), BF),
            pltpu.VMEM((blocks, rows, width), F32),
            pltpu.VMEM((rows, width), F32),
            pltpu.VMEM((rows, LANES), F32),
            pltpu.VMEM((rows, width), BF),
            pltpu.VMEM((width, rows), BF),
            pltpu.VMEM((rows, width), F32),
            pltpu.VMEM((rows, width), BF),
            pltpu.VMEM((width, rows), BF),
            pltpu.SemaphoreType.DMA((4,)),
            pltpu.SemaphoreType.DMA((9,)),
        ]
        + [pltpu.VMEM(vector.shape, vector.dtype) for vector in vectors],
        compiler_params=pltpu.CompilerParams(
            collective_id=2, has_side_effects=True, vmem_limit_bytes=60 * MIB
        ),
        name="feed_forward",
    )(item, mixed, cotangent, out_weight, up_weight, down_weight, *vectors)


SLOTS = 4


def finish_kernel(
    main_ref, tail_ref, input_hbm, small_ref, diagonal_ref,
    down_ref, up_ref, out_ref, qkv_ref, input_ref, *refs,
):
    singles, (main_in, tail_in, slots, input_in, input_slot, in_sems, out_sems, item_sems) = (
        refs[:12], refs[12:],
    )
    mains, width = main_in.shape[0], main_in.shape[2]
    pairs, across = tail_in.shape[0], tail_in.shape[2]
    hidden = mains // 2
    blocks = mains + pairs

    def load(block):
        if block < mains:
            source, target = main_ref.at[pl.ds(block * width, width)], main_in.at[block]
        else:
            pair = block - mains
            source, target = tail_ref.at[pl.ds(pair * TAIL_ROWS, TAIL_ROWS)], tail_in.at[pair]
        return pltpu.make_async_copy(source, target, in_sems.at[block])

    def stores(block):
        slot, sem = slots.at[block % SLOTS], out_sems.at[block % SLOTS]
        if block < hidden:
            targets = [(slot, down_ref.at[pl.ds(block * width, width)])]
        elif block < mains:
            targets = [(slot, up_ref.at[:, pl.ds((block - hidden) * width, width)])]
        else:
            pair = block - mains
            targets = [
                (
                    slot.at[:, pl.ds(part * LANES, LANES)],
                    qkv_ref.at[:, pl.ds(part * width + pair * LANES, LANES)],
                )
                for part in range(3)
            ]
            down = pl.ds(0, TAIL_ROWS - width)
            targets.append(
                (slot.at[down, pl.ds(across, across)], out_ref.at[out_spot(pair, pairs, width)])
            )
        return [
            pltpu.make_async_copy(source, target, sem.at[index])
            for index, (source, target) in enumerate(targets)
        ]

    load_input = pltpu.make_async_copy(input_hbm, input_in, item_sems.at[0])
    store_input = pltpu.make_async_copy(input_slot, input_ref, item_sems.at[1])
    for block in range(blocks):
        load(block).start()
    load_input.start()
    for block in range(blocks):
        load(block).wait()
        if block >= SLOTS:
            for copy in stores(block - SLOTS):
                copy.wait()
        slot = block % SLOTS
        if block < hidden:
            slots[slot] = jnp.transpose(main_in[block].astype(F32))
        elif block < mains:
            slots[slot] = main_in[block].astype(F32)
        else:
            slots[slot, :, :across] = tail_in[block - mains, :width].astype(F32)
            slots[slot, : TAIL_ROWS - width, across:] = tail_in[block - mains, width:].astype(F32)
        for copy in stores(block):
            copy.start()
    load_input.wait()
    input_slot[...] = input_in[...].astype(F32)
    store_input.start()
    for row in range(8):
        singles[row][...] = small_ref[row]
    for row in range(hidden):
        singles[8][row * width : row * width + width] = small_ref[8 + row]
    heads, levels = singles[9].shape
    diagonals = diagonal_ref[...]
    level = lax.broadcasted_iota(jnp.int32, (LANES, LANES), 1)
    lane = lax.broadcasted_iota(jnp.int32, (LANES, LANES), 0)
    for table, (first, size, skip) in enumerate(((0, 4, 0), (4, 2, 1), (6, 2, 1))):
        total = jnp.zeros((heads, LANES), F32)
        for row in range(size):
            distance = lane + LANES * (row + skip - 2)
            chosen = (bucket(distance) == level).astype(F32)
            total = total + jnp.dot(
                diagonals[:, first + row, :], chosen, preferred_element_type=F32,
                precision=lax.Precision.HIGHEST,
            )
        singles[9 + table][...] = total[:, :levels]
    for block in range(blocks - SLOTS, blocks):
        for copy in stores(block):
            copy.wait()
    store_input.wait()


def finished(main, tail, grad_input, small, diagonals, hidden, levels):
    width = main.shape[1]
    heads = diagonals.shape[0]
    mains = main.shape[0] // width
    pairs = tail.shape[0] // TAIL_ROWS
    single = jax.ShapeDtypeStruct((width,), F32)
    table = jax.ShapeDtypeStruct((heads, levels), F32)
    dma = pltpu.SemaphoreType.DMA
    return pl.pallas_call(
        finish_kernel,
        in_specs=[HBM, HBM, HBM, VMEM, VMEM],
        out_specs=[HBM] * 5 + [VMEM] * 12,
        out_shape=[
            jax.ShapeDtypeStruct((hidden, width), F32),
            jax.ShapeDtypeStruct((width, hidden), F32),
            jax.ShapeDtypeStruct((width, width), F32),
            jax.ShapeDtypeStruct((width, 3 * width), F32),
            jax.ShapeDtypeStruct(grad_input.shape, F32),
        ]
        + [single] * 8
        + [jax.ShapeDtypeStruct((hidden,), F32)]
        + [table] * 3,
        scratch_shapes=[
            pltpu.VMEM((mains, width, width), BF),
            pltpu.VMEM((pairs, TAIL_ROWS, tail.shape[1]), BF),
            pltpu.VMEM((SLOTS, width, width), F32),
            pltpu.VMEM(grad_input.shape, BF),
            pltpu.VMEM(grad_input.shape, F32),
            dma((mains + pairs,)),
            dma((SLOTS, 4)),
            dma((2,)),
        ],
        compiler_params=pltpu.CompilerParams(vmem_limit_bytes=56 * MIB),
        name="finished",
    )(main, tail, grad_input, small, diagonals)


PIECE = 16


class Place:
    def __init__(self, depth):
        place = lax.axis_index("dp")
        self.depth = depth
        self.group = lax.div(place, 4 * depth)
        self.z = lax.rem(lax.div(place, 4), depth)
        self.bits = {
            "x": lax.axis_index("seq"),
            "c": lax.rem(place, 2),
            "y": lax.rem(lax.div(place, 2), 2),
            "a": lax.rem(self.z, 2),
            "b": lax.div(self.z, 2),
        }

    def partner(self, letters):
        bit = {
            letter: 1 - value if letter in letters else value
            for letter, value in self.bits.items()
        }
        z = self.z
        for letter, reach in (("a", 1), ("b", 2)):
            if letter in letters:
                z = z + reach - 2 * reach * self.bits[letter]
        return (bit["x"], (self.group * self.depth + z) * 4 + bit["y"] * 2 + bit["c"])

    def greet(self, met):
        barrier = pltpu.get_barrier_semaphore()
        for letters in met:
            pl.semaphore_signal(
                barrier, inc=1, device_id=self.partner(letters), device_id_type=MESH
            )
        pl.semaphore_wait(barrier, len(met))


def letters_of(depth):
    return "xy" + "ab"[: (depth - 1).bit_length()]


def parsed(routes, depth):
    kept = letters_of(depth)
    parts = []
    for route in routes.split():
        hops = ["".join(letter for letter in hop if letter in kept) for hop in route.split(".")]
        parts.append([hop for hop in hops if hop])
    return parts


def subsets(hop):
    return [
        "".join(letter for index, letter in enumerate(hop) if mask >> index & 1)
        for mask in range(1, 2 ** len(hop))
    ]


class Chunk:
    def __init__(self, place, depth, source, out_ref, offset, spot, scratch):
        _, self.begin, rows, first, columns, _, routes, _ = spot
        self.place, self.source, self.columns = place, source, pl.ds(first, columns)
        self.out_ref, self.out_begin = out_ref, offset + self.begin
        self.parts = parsed(routes, depth)
        self.half = rows // 2
        self.share = self.half // len(self.parts)
        self.hops = max(len(part) for part in self.parts)
        self.work, self.fresh, *landing, self.sends, self.receives, self.locals = scratch
        self.landing = {}
        self.sems = {}
        count = 2
        for part, hops in enumerate(self.parts):
            for hop, letters in enumerate(hops):
                self.landing[part, hop] = landing.pop(0)
                for way in range(2):
                    for index in range(2 ** len(letters) - 1):
                        self.sems[way, part, hop, index] = count
                        count += 1

    def aligned(self, value):
        return pl.multiple_of(value, PIECE)

    def size(self, part, hop):
        return self.share >> sum(len(letters) for letters in self.parts[part][: hop + 1])

    def spot(self, part, hop, other=""):
        start = part * self.share
        for level in range(hop + 1):
            for index, letter in enumerate(self.parts[part][level]):
                bit = self.place.bits[letter]
                if level == hop and letter in other:
                    bit = 1 - bit
                start = start + bit * (self.size(part, level) << index)
        return start

    def out(self, begin, size, core=None):
        core = self.place.bits["c"] if core is None else core
        return self.out_ref.at[
            pl.ds(self.aligned(self.out_begin + core * self.half + begin), size), self.columns
        ]

    def copy(self, index, source, target, letters):
        return remote(
            source, target, self.sends.at[index], self.receives.at[index],
            self.place.partner(letters),
        )

    def pair_down(self):
        core = self.place.bits["c"]
        at = lambda c: self.source.at[
            pl.ds(self.aligned(self.begin + c * self.half), self.half), self.columns
        ]
        return [
            self.copy(0, at(1 - core), self.fresh, "c"),
            pltpu.make_async_copy(at(core), self.work, self.locals.at[0]),
        ]

    def pair_up(self, arriving):
        core = self.place.bits["c"]
        target = self.out(0, self.half, 1 - core if arriving else core)
        return [self.copy(1, self.out(0, self.half), target, "c")]

    def at_hop(self, hop):
        return [
            (part, hops[hop]) for part, hops in enumerate(self.parts) if hop < len(hops)
        ]

    def down(self, hop):
        copies = []
        for part, letters in self.at_hop(hop):
            size = self.size(part, hop)
            for index, other in enumerate(subsets(letters)):
                begin = self.aligned(self.spot(part, hop, other))
                copies.append(
                    self.copy(
                        self.sems[0, part, hop, index], self.work.at[pl.ds(begin, size)],
                        self.landing[part, hop].at[index], other,
                    )
                )
        return copies

    def kept(self):
        copies = []
        for part, hops in enumerate(self.parts):
            last = len(hops) - 1
            size = self.size(part, last)
            begin = self.aligned(self.spot(part, last))
            copies.append(
                pltpu.make_async_copy(
                    self.work.at[pl.ds(begin, size)], self.out(begin, size),
                    self.locals.at[1 + part],
                )
            )
        return copies

    def up(self, hop, arriving):
        copies = []
        for part, letters in self.at_hop(hop):
            mine = self.spot(part, hop)
            size = self.size(part, hop)
            if hop == len(self.parts[part]) - 1:
                source = self.work.at[pl.ds(self.aligned(mine), size)]
            else:
                source = self.out(mine, size)
            for index, other in enumerate(subsets(letters)):
                target = self.out(self.spot(part, hop, other) if arriving else mine, size)
                copies.append(self.copy(self.sems[1, part, hop, index], source, target, other))
        return copies

    def add(self, begin, sources, size):
        step = 64 if size % 64 == 0 else 32 if size % 32 == 0 else PIECE

        def body(index, carry):
            offset = self.aligned(index * step)
            there = pl.ds(self.aligned(begin + offset), step)
            total = self.work[there]
            if len(sources) == 1:
                total = total + sources[0][pl.ds(offset, step)]
            else:
                total = total.astype(F32)
                for source in sources:
                    total = total + source[pl.ds(offset, step)].astype(F32)
            self.work[there] = total.astype(BF)
            return carry

        lax.fori_loop(0, size // step, body, 0)

    def stage(self, number):
        hops = self.hops
        ended, started = [], []
        if number == 0:
            started = self.pair_down()
        elif number == 1:
            ended = self.pair_down()
            started = self.down(0)
        elif number <= hops:
            ended = self.down(number - 2)
            started = self.down(number - 1)
        elif number == hops + 1:
            ended = self.down(hops - 1)
            started = self.up(hops - 1, False) + self.kept()
        elif number <= 2 * hops:
            level = 2 * hops + 1 - number
            ended = self.up(level, True) + (self.kept() if level == hops - 1 else [])
            started = self.up(level - 1, False)
        elif number == 2 * hops + 1:
            ended = self.up(0, True)
            started = self.pair_up(False)
        else:
            ended = self.pair_up(True)
        for copy in ended:
            copy.wait()
        if number == 1:
            self.add(0, [self.fresh], self.half)
        elif 2 <= number <= hops + 1:
            hop = number - 2
            for part, letters in self.at_hop(hop):
                landing = self.landing[part, hop]
                sources = [landing.at[index] for index in range(2 ** len(letters) - 1)]
                self.add(self.spot(part, hop), sources, self.size(part, hop))
        for copy in started:
            copy.start()


def chunk_scratch(spot, depth):
    _, _, rows, _, columns, _, routes, _ = spot
    parts = parsed(routes, depth)
    landing = []
    copies = 2
    for hops in parts:
        size = rows // 2 // len(parts)
        for letters in hops:
            size >>= len(letters)
            others = 2 ** len(letters) - 1
            copies += 2 * others
            landing.append(pltpu.VMEM((others, size, columns), BF))
    dma = pltpu.SemaphoreType.DMA
    return (
        [pltpu.VMEM((rows // 2, columns), BF)] * 2
        + landing
        + [dma((copies,)), dma((copies,)), dma((1 + len(parts),))]
    )


def loads_of(hop, size):
    if "x" in hop and "y" in hop:
        return [("x", 2 * size), ("y", 2 * size)]
    if hop in ("x", "y"):
        return [(hop, size)]
    if "a" in hop and "b" in hop:
        return [("end", 3 * size), ("middle", 4 * size)]
    return [("end", size), ("middle", 2 * size)] if hop == "b" else [("end", size)]


def planned(chunks, work, depth, hop_count):
    latency, issue, link, pair = 3.5, 0.08, 100e3, 600e3
    free = {}
    now = 3.0
    chains = []
    for rows, columns, need, routes, _ in chunks:
        parts = parsed(routes, depth)
        sizes = [rows // 2 // len(parts)] * len(parts)
        down = []
        for hop in range(max(len(part) for part in parts)):
            loads, copies, added = [], 0, 0
            for index, part in enumerate(parts):
                if hop < len(part):
                    sizes[index] >>= len(part[hop])
                    others = 2 ** len(part[hop]) - 1
                    loads += loads_of(part[hop], sizes[index])
                    copies += others
                    added += sizes[index] * others
            down.append((loads, copies, added, columns))
        first = [([("core", rows // 2)], 1.5, rows // 2, columns)]
        last = [([("core", rows // 2)], 1, 0, columns)]
        chains.append((need, first + down + down[::-1] + last))
    chains.append((len(work), [([("core", 16)], 2, 0, 768)] * hop_count))
    ranks = [chunk[4] for chunk in chunks] + [0]
    position = [0] * len(chains)
    ready = [0.0] * len(chains)
    order = [[] for _ in range(len(work) + 1)]
    done = 0
    while True:
        open_ones = [
            (ranks[i], ready[i], i) for i, (need, chain) in enumerate(chains)
            if position[i] <= len(chain) and need <= done
        ]
        due = [entry for entry in open_ones if entry[1] <= now]
        if not due and done < len(work):
            now += work[done]
            done += 1
            continue
        if not open_ones:
            return order
        _, when, index = min(due) if due else min(open_ones, key=lambda entry: entry[1])
        now = max(now, when)
        chain = chains[index][1]
        stage = position[index]
        order[done].append((index, stage))
        if 0 < stage <= len(chain) // 2:
            now += 1e-6 * chain[stage - 1][2] * chain[stage - 1][3]
        if stage < len(chain):
            loads, copies, _, columns = chain[stage]
            now += issue * copies
            end = now
            for lane, rows in loads:
                rate = pair if lane == "core" else link / 2
                free[lane] = max(now, free.get(lane, 0.0)) + 2 * rows * columns / rate
                end = max(end, free[lane])
            ready[index] = end + latency
        position[index] += 1


def last_kernel(
    depth, plan, orders, counts, *refs,
):
    (meta_ref, rows_ref, projected_hbm, mixed_hbm, grad_hbm, log_ref, first_hbm, second_hbm,
     key_image_hbm, bias_hbm, small_ref, item_hbm, weight_hbm, d_hidden_hbm, grad_down_ref, grad_up_ref,
     grad_out_ref,
     main_out, tail_out, small_out, diagonal_out, input_out,
     *scratch) = refs
    static, scratch = scratch[:6], scratch[6:]
    (k_ref, v_ref, mixed_ref, grad_ref, first_ref, second_ref, key_image_ref, bias_ref, pair_sems,
     item_ref, weight_ref, d_hidden_ref, load_sems, d_project, item_t, tail, input_grad,
     small_in, diagonal_in, small_sems, item_sems, *scratch) = scratch
    place = Place(depth)
    step = pl.program_id(0)
    pairs = k_ref.shape[0]
    rows, width = item_hbm.shape
    count = rows // 2
    x = place.bits["x"]
    hidden = grad_down_ref.shape[0]
    sources = ((grad_down_ref, main_out, 0), (grad_up_ref, main_out, hidden), (tail, tail_out, 0))
    chunks = []
    for spot, pieces in zip(plan, counts):
        chunks.append(Chunk(place, depth, *sources[spot[0]], spot, scratch[:pieces]))
        scratch = scratch[pieces:]
    hop_letters = "c" + letters_of(depth)
    wide_hbm = (first_hbm, second_hbm, key_image_hbm, bias_hbm)
    wide_refs = (first_ref, second_ref, key_image_ref, bias_ref)

    def pair_loads(pair):
        copies = []
        held = (
            (projected_hbm, k_ref, width), (projected_hbm, v_ref, 2 * width),
            (mixed_hbm, mixed_ref, 0), (grad_hbm, grad_ref, 0),
        )
        for source, target, first in held:
            columns = pl.ds(pl.multiple_of(first + pair * LANES, LANES), LANES)
            copies.append((source.at[:, columns], target.at[pair]))
        heads = pl.ds(2 * pair, 2)
        for source, target in zip(wide_hbm, wide_refs):
            copies.append((source.at[heads], target.at[heads]))
        return [
            pltpu.make_async_copy(source, target, pair_sems.at[pair, index])
            for index, (source, target) in enumerate(copies)
        ]

    def loads():
        copies = [(item_hbm, item_ref), (weight_hbm, weight_ref), (d_hidden_hbm, d_hidden_ref)]
        for pair in range(pairs):
            down, across = out_spot(pair, pairs, width)
            copies.append(
                (
                    grad_out_ref.at[down, across],
                    tail.at[pl.ds(pair * TAIL_ROWS + width, TAIL_ROWS - width)],
                )
            )
        return [
            pltpu.make_async_copy(source, target, load_sems.at[index])
            for index, (source, target) in enumerate(copies)
        ]

    def input_copies():
        return [
            pltpu.make_async_copy(
                input_grad.at[pl.ds(pl.multiple_of(x * count, LANES), count)], input_out.at[x],
                item_sems.at[0],
            ),
            remote(
                input_grad.at[pl.ds(pl.multiple_of((1 - x) * count, LANES), count)],
                input_out.at[x], item_sems.at[1], item_sems.at[2], place.partner("x"),
            ),
        ]

    def small_copies(hop):
        return [
            remote(source, landing.at[hop], small_sems.at[0, kind, hop],
                   small_sems.at[1, kind, hop], place.partner(hop_letters[hop]))
            for kind, (source, landing) in enumerate(
                ((small_out, small_in), (diagonal_out, diagonal_in))
            )
        ]

    def small_stage(hop):
        if hop > 0:
            for copy in small_copies(hop - 1):
                copy.wait()
            small_out[...] = small_out[...] + small_in[hop - 1]
            diagonal_out[...] = diagonal_out[...] + diagonal_in[hop - 1]
        if hop < len(hop_letters):
            for copy in small_copies(hop):
                copy.start()

    def perform(slot):
        for index, stage in orders[slot]:
            if index == len(chunks):
                small_stage(stage)
            else:
                chunks[index].stage(stage)

    @pl.when(step == 0)
    def _():
        for pair in range(pairs):
            for copy in pair_loads(pair):
                copy.start()
        for copy in loads():
            copy.start()
        met = set(hop_letters)
        for chunk in chunks:
            for hops in chunk.parts:
                for letters in hops:
                    met.update(subsets(letters))
        place.greet(sorted(met))
        small_out[...] = small_ref[...]

    for pair in range(pairs):
        @pl.when(step == pair)
        def _(pair=pair):
            perform(pair)

    @pl.when(step == 0)
    def _():
        static_prepare(meta_ref, static)
        for copy in loads():
            copy.wait()
        for tile in range(rows // TILE):
            there = slice(tile * TILE, tile * TILE + TILE)
            item_t[:, there] = jnp.transpose(item_ref[there].astype(F32)).astype(BF)

    for copy in pair_loads(step):
        copy.wait()
    (dq_even, dk_even, dv_even), (dq_odd, dk_odd, dv_odd) = [
        head_back(
            parity, step, rows_ref, wide_refs, k_ref, v_ref, mixed_ref, grad_ref, log_ref,
            static, diagonal_out,
        )
        for parity in range(2)
    ]
    even = own_lanes(0, rows)
    pieces = [
        jnp.transpose(jnp.concatenate([dq_even, dq_odd], axis=0)).astype(BF),
        jnp.where(even, dk_even, dk_odd).astype(BF),
        jnp.where(even, dv_even, dv_odd).astype(BF),
    ]
    for part, piece in enumerate(pieces):
        d_project[:, pl.ds(pl.multiple_of(part * width + step * LANES, LANES), LANES)] = piece
    slab = pl.ds(pl.multiple_of(step * TAIL_ROWS, TAIL_ROWS), width)
    tail[slab] = dot_nn(item_t[...], jnp.concatenate(pieces, axis=1)).astype(BF)

    @pl.when(step == pairs - 1)
    def _():
        perform(pairs)
        for begin in range(0, width, TILE):
            here = slice(begin, begin + TILE)
            total = d_hidden_ref[:, here] + dot_nt(d_project[...], weight_ref[here])
            input_grad[:, here] = total.astype(BF)
        for copy in input_copies():
            copy.start()
        for begin in range(0, width, TILE):
            here = slice(begin, begin + TILE)
            there = slice(2 * width + begin, 2 * width + begin + TILE)
            small_out[0:1, here] = column_sum(d_project[:, here].astype(F32))
            small_out[1:2, here] = column_sum(d_project[:, there].astype(F32))
        perform(pairs + 1)
        for copy in input_copies():
            copy.wait()


TAIL_ROWS = 1024


def out_spot(pair, pairs, width):
    down = TAIL_ROWS - width
    across = width * width // (pairs * down)
    per_row = width // across
    return (
        pl.ds(pair // per_row * down, down),
        pl.ds(pair % per_row * across, across),
    )


def summed_with_attention_back(
    meta_columns, meta_rows, projected, mixed, d_mixed, logs, wide_arrays, item, qkv_weight,
    d_hidden, small, grad_down, grad_up, grad_out,
):
    size = lax.axis_size("dp")
    depth = 4 if size % 16 == 0 else size // 4
    rows, width = item.shape
    pairs = width // LANES
    hidden = grad_down.shape[0]
    hops = len(letters_of(depth)) + 1
    work = [6.8] * pairs + [4.0]
    tall, wide, slim = 1024, 3 * LANES, 2 * LANES
    plan = [
        (0, 0, 2 * tall, 0, width, 0, "a.b.x.y x.y.a.b", 1),
        (0, 2 * tall, tall, 0, width, 0, "x.a.y.b y.a.b.x", 2),
        (1, 0, 3 * tall, 0, slim, 0, "a.b.x.y y.x.a.b", 4),
        (1, 0, 3 * tall, slim, slim, 0, "y.a.x.b x.y.a.b", 0),
        (1, 0, 3 * tall, 2 * slim, slim, 0, "x.y.a.b y.x.a.b", 2),
        (2, 0, tall, 0, wide, 1, "y.x.a.b a.b.x.y", 3),
        (2, tall, tall, 0, wide, 2, "xy.a.b", 2),
        (2, 2 * tall, tall, 0, wide, 3, "x.y.ab y.ab.x", 3),
        (2, 3 * tall, tall, 0, wide, 4, "xy.a.b", 1),
        (2, 4 * tall, tall, 0, wide, 5, "xy.a.b", 1),
        (2, 5 * tall, tall, 0, wide, 6, "ab.y.x y.ab.x", 2),
    ]
    orders = planned([(spot[2],) + spot[4:] for spot in plan], work, depth, hops)

    whole = pl.BlockSpec(memory_space=pltpu.VMEM)
    diagonals = jax.ShapeDtypeStruct((2 * pairs, 8, LANES), F32)
    dma = pltpu.SemaphoreType.DMA
    scratch = []
    for spot in plan:
        scratch.append(chunk_scratch(spot, depth))
    main, tail, small, diagonals, grad_input = pl.pallas_call(
        functools.partial(last_kernel, depth, plan, orders, [len(pieces) for pieces in scratch]),
        grid=(pairs,),
        in_specs=[whole] * 2 + [HBM] * 3 + [whole] + [HBM] * 4 + [whole] + [HBM] * 6,
        out_specs=[HBM, HBM, whole, whole, HBM],
        out_shape=[
            jax.ShapeDtypeStruct((2 * hidden, width), BF),
            jax.ShapeDtypeStruct((pairs * TAIL_ROWS, 3 * LANES), BF),
            jax.ShapeDtypeStruct(small.shape, F32),
            diagonals,
            jax.ShapeDtypeStruct((2, rows // 2, width), BF),
        ],
        scratch_shapes=[pltpu.VMEM((rows, LANES), BF)] * 3
        + [pltpu.VMEM((LANES, rows), BF)] * 3
        + [pltpu.VMEM((pairs, rows, LANES), kind) for kind in (BF, BF, F32, BF)]
        + [pltpu.VMEM(array.shape, BF) for array in wide_arrays]
        + [
            dma((pairs, 8)),
            pltpu.VMEM((rows, width), BF),
            pltpu.VMEM((width, 3 * width), BF),
            pltpu.VMEM((rows, width), F32),
            dma((3 + pairs,)),
            pltpu.VMEM((rows, 3 * width), BF),
            pltpu.VMEM((width, rows), BF),
            pltpu.VMEM((pairs * TAIL_ROWS, 3 * LANES), BF),
            pltpu.VMEM((rows, width), BF),
            pltpu.VMEM((hops,) + small.shape, F32),
            pltpu.VMEM((hops,) + diagonals.shape, F32),
            dma((2, 2, hops)),
            dma((3,)),
        ]
        + [piece for pieces in scratch for piece in pieces],
        compiler_params=pltpu.CompilerParams(
            collective_id=0, has_side_effects=True, vmem_limit_bytes=62 * MIB
        ),
        name="summed_with_attention_back",
    )(meta_columns, meta_rows, projected, mixed, d_mixed, logs, *wide_arrays,
      small, item, qkv_weight, d_hidden, grad_down, grad_up, grad_out)
    span = 4 * depth
    if size > span:
        groups = [list(range(first, size, span)) for first in range(span)]
        main, tail, small, diagonals = lax.psum(
            (main.astype(F32), tail.astype(F32), small, diagonals), "dp",
            axis_index_groups=groups,
        )
        main, tail = main.astype(BF), tail.astype(BF)
    return main, tail, small, diagonals, grad_input


def per_device(
    layer_in, segment, key_mask, position, layout_x, layout_y,
    qkv_weight, query_bias, value_bias, out_weight, out_bias, attn_gain, attn_shift,
    up_weight, up_bias, down_weight, down_bias, ffn_gain, ffn_shift,
    text_table, horiz_table, vert_table, cotangent,
):
    width = layer_in.shape[-1]
    item, projected, meta_columns, meta_rows, table_rows = projected_item(
        layer_in, (segment, key_mask, position, layout_x, layout_y),
        qkv_weight, query_bias, value_bias, (text_table, horiz_table, vert_table),
    )
    mixed, logs, *wide_arrays = attention_forward(meta_columns, meta_rows, table_rows, projected, width)
    layer_out, d_hidden, d_mixed, grad_out, grad_down, grad_up, small = fed_forward_and_back(
        item, mixed, cotangent, out_weight, up_weight, down_weight,
        (out_bias, attn_gain, attn_shift, up_bias, down_bias, ffn_gain, ffn_shift),
    )
    main, tail, small, diagonals, grad_input = summed_with_attention_back(
        meta_columns, meta_rows, projected, mixed, d_mixed, logs, wide_arrays, item, qkv_weight,
        d_hidden, small, grad_down, grad_up, grad_out,
    )
    done = finished(
        main, tail, grad_input, small, diagonals, up_weight.shape[1], text_table.shape[0]
    )
    sum_down, sum_up, sum_out, sum_qkv, grad_input = done[:5]
    singles, tables = done[5:14], [t.T for t in done[14:]]
    return (
        layer_out, grad_input, sum_qkv, singles[0], singles[1], sum_out, singles[2], singles[3],
        singles[4], sum_up, singles[8], sum_down, singles[5], singles[6], singles[7],
        tables[0], tables[1], tables[2],
    )


def solution(mesh):
    rows = P("dp", "seq", None)
    marks_spec = P("dp", "seq")
    return jax.shard_map(
        per_device,
        mesh=mesh,
        in_specs=(rows,) + (marks_spec,) * 5 + (P(),) * 16 + (rows,),
        out_specs=(rows, rows) + (P(),) * 16,
        check_vma=False,
    )
```

```python
import functools

import jax
import jax.numpy as jnp
from jax import lax
from jax.experimental import pallas as pl
from jax.experimental.pallas import tpu as pltpu
from jax.sharding import PartitionSpec as P

BF = jnp.bfloat16
F32 = jnp.float32
BIG = 1e30
LANES = 128
HEAD = 64
TEXT = 512
POS = 64
COORD = 48
Y0 = 64
GROUP0 = 112
MEMBER0 = 116
FLAG = 124
X_TABLE = 33
Y_TABLE = 66
NOTHING = 127


def dot_nt(a, b):
    return lax.dot_general(a, b, (((1,), (1,)), ((), ())), preferred_element_type=F32)


def dot_nn(a, b):
    return lax.dot_general(a, b, (((1,), (0,)), ((), ())), preferred_element_type=F32)


def looked_up(table_row, index):
    rows = index.shape[0]
    return jnp.take_along_axis(
        jnp.broadcast_to(table_row, (rows, LANES)), index, axis=1, mode="promise_in_bounds"
    )


def bucket(distance):
    return jnp.clip(distance, -16, 16) + 16


def between(lane, low, high):
    return (lane >= low) & (lane < high)


def columns_of(meta_ref):
    return tuple(meta_ref[:, field : field + 1] for field in range(5))


def marks(meta_ref):
    segment, key_mask, position, across, down = columns_of(meta_ref)
    rows = segment.shape[0]
    lane = lax.broadcasted_iota(jnp.int32, (rows, LANES), 1)
    row = lax.broadcasted_iota(jnp.int32, (rows, LANES), 0)
    even = between(lane, HEAD, HEAD + COORD) & (lane - HEAD == across)
    odd = (lane < COORD) & (lane == across)
    group = (segment - 1) >> 3
    member = (segment - 1) & 7
    named = segment > 0
    shared = (
        ((row < TEXT) & (lane < POS) & (lane == position))
        | (between(lane, Y0, Y0 + COORD) & (lane - Y0 == down))
        | (named & between(lane, GROUP0, MEMBER0) & (lane - GROUP0 == group))
        | (named & between(lane, MEMBER0, FLAG) & (lane - MEMBER0 == member))
        | ((lane == FLAG) & (key_mask <= 0))
    )
    return tuple(jnp.where(m, 1.0, 0.0).astype(BF) for m in (even, odd, shared))


def barred(meta_ref):
    segment = meta_ref[:, 0:1]
    rows = segment.shape[0]
    lane = lax.broadcasted_iota(jnp.int32, (rows, LANES), 1)
    group = (segment - 1) >> 3
    member = (segment - 1) & 7
    shut = (
        ((segment > 0) & between(lane, GROUP0, MEMBER0) & (lane - GROUP0 != group))
        | ((segment < 0) & between(lane, GROUP0, MEMBER0))
        | ((segment > 0) & between(lane, MEMBER0, FLAG) & (lane - MEMBER0 != member))
        | (lane == FLAG)
    )
    return jnp.where(shut, -BIG, 0.0).astype(F32)


def query_index(meta_ref):
    segment, key_mask, position, across, down = columns_of(meta_ref)
    rows = segment.shape[0]
    lane = lax.broadcasted_iota(jnp.int32, (rows, LANES), 1)
    x_even = bucket(across - (lane - HEAD)) + X_TABLE
    x_odd = bucket(across - lane) + X_TABLE
    even = jnp.where(between(lane, HEAD, HEAD + COORD), x_even, NOTHING)
    odd = jnp.where(lane < COORD, x_odd, NOTHING)
    shared = jnp.where(
        lane < POS,
        bucket(position - lane),
        jnp.where(between(lane, Y0, Y0 + COORD), bucket(down - (lane - Y0)) + Y_TABLE, NOTHING),
    )
    return even, odd, shared


def image_key_index(meta_ref):
    position = meta_ref[TEXT:, 2:3]
    lane = lax.broadcasted_iota(jnp.int32, (position.shape[0], LANES), 1)
    return jnp.where(lane < POS, bucket(lane - position), NOTHING)


def prepare(meta_ref, mark_refs, bar_ref, index_refs, key_index_ref):
    for ref, value in zip(mark_refs, marks(meta_ref)):
        ref[...] = value
    bar_ref[...] = barred(meta_ref)
    for ref, value in zip(index_refs, query_index(meta_ref)):
        ref[...] = value
    key_index_ref[...] = image_key_index(meta_ref)


def image_offsets(row_positions, column_positions):
    return bucket(column_positions - row_positions)


def own_lanes(parity, rows):
    lane = lax.broadcasted_iota(jnp.int32, (rows, LANES), 1)
    return (lane < HEAD) if parity == 0 else (lane >= HEAD)


def widened(parity, q, table_row, bar_ref, index_refs, key_index_ref, shared_ref):
    rows = q.shape[0]
    images = key_index_ref.shape[0]
    first = jnp.where(
        own_lanes(parity, rows),
        q.astype(F32) * 0.125,
        looked_up(table_row, index_refs[parity][...]),
    )
    second = (looked_up(table_row, index_refs[2][...]) + bar_ref[...]).astype(BF)
    image_lane = lax.broadcasted_iota(jnp.int32, (images, LANES), 1)
    key_image = jnp.where(
        image_lane < POS, looked_up(table_row, key_index_ref[...]).astype(BF), shared_ref[TEXT:]
    )
    return first.astype(BF), second, key_image


def joined(parity, first, second, key_image, k, marks_own, shared):
    rows = k.shape[0]
    lane = lax.broadcasted_iota(jnp.int32, (rows, LANES), 1)
    to_image = jnp.where(lane < POS, shared, second)
    key_first = jnp.where(own_lanes(parity, rows), k, marks_own)
    q_text = jnp.concatenate([first, second], axis=1)
    q_image = jnp.concatenate([first, to_image], axis=1)
    k_text = jnp.concatenate([key_first[:TEXT], shared[:TEXT]], axis=1)
    k_image = jnp.concatenate([key_first[TEXT:], key_image], axis=1)
    return q_text, q_image, k_text, k_image


def image_bias(table_row, offsets):
    return jnp.concatenate(
        [looked_up(table_row, offsets[:, :LANES]), looked_up(table_row, offsets[:, LANES:])], axis=1
    )


def forward_kernel(
    meta_ref, rows_ref, table_ref, q_ref, k_ref, v_ref,
    mixed_ref, log_ref, first_ref, second_ref, key_image_ref, bias_ref,
    even_ref, odd_ref, shared_ref, bar_ref, index_even, index_odd, index_shared, key_index_ref,
):
    mark_refs = (even_ref, odd_ref, shared_ref)
    index_refs = (index_even, index_odd, index_shared)

    @pl.when(pl.program_id(0) == 0)
    def _():
        prepare(meta_ref, mark_refs, bar_ref, index_refs, key_index_ref)

    rows = q_ref.shape[0]
    images = rows - TEXT
    q, k, v = q_ref[...], k_ref[...], v_ref[...]
    offsets = bucket(rows_ref[2:3, TEXT:] - meta_ref[TEXT:, 2:3])
    tile = 256
    v_turned = transposed(v)
    heads = [None, None]

    def prepared(parity):
        table_row = table_ref[pl.ds(2 * pl.program_id(0) + parity, 1), :]
        first, second, key_image = widened(
            parity, q, table_row, bar_ref, index_refs, key_index_ref, shared_ref
        )
        bias = image_bias(table_row, offsets)
        first_ref[parity] = first
        second_ref[parity] = second
        key_image_ref[parity] = key_image
        bias_ref[parity] = bias.astype(BF)
        wide = joined(
            parity, first, second, key_image, k, mark_refs[parity][...], shared_ref[...]
        )
        heads[parity] = wide + (bias,)

    def scored(parity, start):
        q_text, q_image, k_text, k_image, bias = heads[parity]
        here = slice(start, start + tile)
        on_image = dot_nt(k_image, q_image[here])
        if start >= TEXT:
            on_image = on_image + bias[:, start - TEXT : start - TEXT + tile]
        return dot_nt(k_text, q_text[here]), on_image

    spots = [(parity, start) for parity in range(2) for start in range(0, rows, tile)]
    outs = ([], [])
    prepared(0)
    following = scored(*spots[0])
    for index, (parity, start) in enumerate(spots):
        on_text, on_image = following
        if index == 1:
            prepared(1)
        if index + 1 < len(spots):
            following = scored(*spots[index + 1])
        top = jnp.maximum(
            jnp.max(on_text, axis=0, keepdims=True), jnp.max(on_image, axis=0, keepdims=True)
        )
        on_text = jnp.exp(on_text - top)
        on_image = jnp.exp(on_image - top)
        total = jnp.sum(on_text, axis=0, keepdims=True) + jnp.sum(on_image, axis=0, keepdims=True)
        own = slice(parity * HEAD, parity * HEAD + HEAD)
        out = dot_nn(v_turned[own, :TEXT], on_text.astype(BF)) + dot_nn(
            v_turned[own, TEXT:], on_image.astype(BF)
        )
        outs[parity].append(out * (1.0 / total))
        log_ref[0, parity : parity + 1, start : start + tile] = top + jnp.log(total)
    mixed_ref[...] = jnp.transpose(
        jnp.concatenate([jnp.concatenate(outs[parity], axis=1) for parity in range(2)], axis=0)
    )


def static_scratch(rows):
    return [
        pltpu.VMEM((rows, LANES), BF),
        pltpu.VMEM((rows, LANES), BF),
        pltpu.VMEM((rows, LANES), BF),
        pltpu.VMEM((rows, LANES), F32),
        pltpu.VMEM((rows, LANES), jnp.int32),
        pltpu.VMEM((rows, LANES), jnp.int32),
        pltpu.VMEM((rows, LANES), jnp.int32),
        pltpu.VMEM((rows - TEXT, LANES), jnp.int32),
    ]


def attention_forward(meta_columns, meta_rows, table_rows, projected, width):
    rows = projected.shape[0]
    images = rows - TEXT
    pairs = width // LANES

    def block(part):
        return pl.BlockSpec((rows, LANES), lambda p: (0, part * pairs + p))

    whole = lambda shape: pl.BlockSpec(shape, lambda p: (0,) * len(shape))
    return pl.pallas_call(
        forward_kernel,
        grid=(pairs,),
        in_specs=[
            whole(meta_columns.shape),
            whole(meta_rows.shape),
            whole(table_rows.shape),
            block(0), block(1), block(2),
        ],
        out_specs=[
            pl.BlockSpec((rows, LANES), lambda p: (0, p)),
            pl.BlockSpec((1, 2, rows), lambda p: (p, 0, 0)),
            pl.BlockSpec((2, rows, LANES), lambda p: (p, 0, 0)),
            pl.BlockSpec((2, rows, LANES), lambda p: (p, 0, 0)),
            pl.BlockSpec((2, images, LANES), lambda p: (p, 0, 0)),
            pl.BlockSpec((2, images, images), lambda p: (p, 0, 0)),
        ],
        out_shape=[
            jax.ShapeDtypeStruct((rows, width), F32),
            jax.ShapeDtypeStruct((pairs, 2, rows), F32),
            jax.ShapeDtypeStruct((2 * pairs, rows, LANES), BF),
            jax.ShapeDtypeStruct((2 * pairs, rows, LANES), BF),
            jax.ShapeDtypeStruct((2 * pairs, images, LANES), BF),
            jax.ShapeDtypeStruct((2 * pairs, images, images), BF),
        ],
        scratch_shapes=static_scratch(rows),
        compiler_params=pltpu.CompilerParams(vmem_limit_bytes=60 * 1024 * 1024),
        name="attention_forward",
    )(meta_columns, meta_rows, table_rows, projected, projected, projected)


def skewed(block):
    size = block.shape[0]
    lane = lax.broadcasted_iota(jnp.int32, (size, LANES), 1)
    row = lax.broadcasted_iota(jnp.int32, (size, LANES), 0)
    turned = jnp.take_along_axis(
        block, (lane + row) & (LANES - 1), axis=1, mode="promise_in_bounds"
    )
    straight = lane + row < LANES
    above = jnp.sum(jnp.where(straight, turned, 0.0), axis=0, keepdims=True)
    below = jnp.sum(jnp.where(straight, 0.0, turned), axis=0, keepdims=True)
    return above, below


def transposed(array):
    return jnp.transpose(array.astype(F32)).astype(array.dtype)


def static_prepare(meta_ref, static):
    for ref, turned, value in zip(static[:3], static[3:], marks(meta_ref)):
        ref[...] = value
        turned[...] = transposed(value)


def head_back(
    parity, pair, rows_ref, wide_refs, k_ref, v_ref, mixed_ref, grad_ref, log_ref, static, diag_ref,
):
    mark_refs, turned_refs = static[:3], static[3:]
    first_ref, second_ref, key_image_ref, bias_ref = wide_refs
    head = 2 * pair + parity
    shared_t = turned_refs[2]
    rows = k_ref.shape[1]
    images = rows - TEXT
    tile = 256
    k, v, grad = k_ref[pair], v_ref[pair], grad_ref[pair]
    products = grad.astype(F32) * mixed_ref[pair]
    k_turned = transposed(k)
    is_image = rows_ref[1:2, TEXT:] > 0
    own = own_lanes(parity, rows)
    log_row = log_ref[pair, parity : parity + 1, :]
    first, shared = first_ref[head], mark_refs[2][...]
    q_text, q_image, k_text, k_image = joined(
        parity, first, second_ref[head], key_image_ref[head], k, mark_refs[parity][...], shared
    )
    bias = bias_ref[head].astype(F32)
    ones = jnp.where(own_lanes(parity, 8), 1.0, 0.0).astype(BF)
    delta = jnp.zeros((8, rows), F32)
    rest = products
    for _ in range(3):
        piece = rest.astype(BF)
        delta = delta + dot_nt(ones, piece)
        rest = rest - piece.astype(F32)
    delta = delta[0:1]
    v_own = jnp.where(own, v, jnp.zeros_like(v))
    q_marked = jnp.concatenate(
        [jnp.where(own, first, mark_refs[parity][...]), shared], axis=1
    )
    dq = jnp.zeros((HEAD, rows), F32)
    dks = []
    dvs = []
    first_sum = jnp.zeros((LANES, LANES), F32)
    second_sum = jnp.zeros((LANES, LANES), F32)
    text_image = jnp.zeros((LANES, images), F32)
    def scored(start):
        here = slice(start, start + tile)
        if start < TEXT:
            scores = dot_nt(k_text[here], q_text)
        else:
            scores = dot_nt(k_image[start - TEXT : start - TEXT + tile], q_image)
            scores = jnp.concatenate([scores[:, :TEXT], scores[:, TEXT:] + bias], axis=1)
        return scores, dot_nt(v_own[here], grad)

    following = scored(0)
    for start in range(0, rows, tile):
        here = slice(start, start + tile)
        scores, prob_grad = following
        if start + tile < rows:
            following = scored(start + tile)
        soft = jnp.exp(scores - log_row)
        score_grad = soft * (prob_grad - delta)
        low = score_grad.astype(BF)
        dvs.append(dot_nn(soft.astype(BF), grad))
        wide = dot_nn(low, q_marked)
        dks.append(wide[:, :LANES])
        dq = dq + dot_nn(k_turned[parity * HEAD : parity * HEAD + HEAD, here], low)
        rounded = wide.astype(BF)
        first_sum = first_sum + dot_nn(turned_refs[parity][:, here], rounded[:, :LANES])
        second_sum = second_sum + dot_nn(shared_t[:, here], rounded[:, LANES:])
        if start < TEXT:
            text_image = text_image + dot_nn(shared_t[:, here], low[:, TEXT:])
        else:
            by_position = wide[:, LANES:]
            on_image = score_grad[:, TEXT:]
    small = lax.broadcasted_iota(jnp.int32, (LANES, LANES), 1)
    small_row = lax.broadcasted_iota(jnp.int32, (LANES, LANES), 0)
    x0 = HEAD if parity == 0 else 0
    x_block = jnp.where(
        between(small, x0, x0 + COORD) & between(small_row, x0, x0 + COORD), first_sum, 0.0
    )
    y_block = jnp.where(
        between(small, Y0, Y0 + COORD) & between(small_row, Y0, Y0 + COORD), second_sum, 0.0
    )
    p_block = jnp.where((small < POS) & (small_row < POS), second_sum, 0.0)
    wide_lane = lax.broadcasted_iota(jnp.int32, (images, images), 1)
    outside = jnp.sum(jnp.where(is_image, 0.0, on_image), axis=1, keepdims=True)
    pairs = jnp.where(is_image, on_image, 0.0) + jnp.where(wide_lane == 0, outside, 0.0)
    outside_text = jnp.sum(jnp.where(is_image, 0.0, text_image), axis=1, keepdims=True)
    text_lane = lax.broadcasted_iota(jnp.int32, (LANES, images), 1)
    text_row = lax.broadcasted_iota(jnp.int32, (LANES, images), 0)
    text_image = jnp.where(is_image, text_image, 0.0) + jnp.where(
        text_lane == 0, outside_text, 0.0
    )
    text_image = jnp.where(text_row < POS, text_image, 0.0)
    first_lane = lax.broadcasted_iota(jnp.int32, (images, LANES), 1)
    left = pairs[:, :LANES] + jnp.where(first_lane < POS, by_position, 0.0)
    right = pairs[:, LANES:]
    a00, b00 = skewed(left[:LANES] + text_image[:, :LANES] + p_block)
    a01, b01 = skewed(right[:LANES] + text_image[:, LANES:])
    a10, b10 = skewed(left[LANES:])
    a11, b11 = skewed(right[LANES:])
    ax, bx = skewed(x_block)
    ay, by = skewed(y_block)
    diag_ref[head] = jnp.concatenate(
        [b10, b00 + b11 + a10, a00 + a11 + b01, a01, bx, ax, by, ay], axis=0
    )
    return dq * 0.125, jnp.concatenate(dks, axis=0), jnp.concatenate(dvs, axis=0)


MESH = pl.DeviceIdType.MESH
VMEM = pl.BlockSpec(memory_space=pltpu.VMEM)
HBM = pl.BlockSpec(memory_space=pltpu.HBM)
MIB = 1024 * 1024


def remote(src, dst, send, receive, device):
    return pltpu.make_async_remote_copy(
        src_ref=src, dst_ref=dst, send_sem=send, recv_sem=receive, device_id=device,
        device_id_type=MESH,
    )


def project_kernel(
    layer_ref, weight_hbm, *refs,
):
    small_hbm, refs = refs[:10], refs[10:]
    (item_ref, projected_out, columns_ref, rows_ref, table_ref,
     projected_ref, weight_ref, meta_send, bias_ref, sems, load_sems, store_sems), small = (
        refs[:12], refs[12:],
    )
    (segment_ref, mask_ref, position_ref, across_ref, down_ref, query_bias_ref, value_bias_ref,
     text_ref, horiz_ref, vert_ref) = small
    mine = lax.axis_index("seq")
    partner = (1 - mine, lax.axis_index("dp"))
    count, width = layer_ref.shape[1:]
    own = pl.ds(pl.multiple_of(mine * count, LANES), count)
    loads = [
        pltpu.make_async_copy(source, target, load_sems.at[index])
        for index, (source, target) in enumerate(
            list(zip(small_hbm, small))
            + [(layer_ref.at[mine], item_ref.at[own]), (weight_hbm, weight_ref)]
        )
    ]
    for load in loads:
        load.start()
    barrier = pltpu.get_barrier_semaphore()
    pl.semaphore_signal(barrier, inc=1, device_id=partner, device_id_type=MESH)
    pl.semaphore_wait(barrier, 1)
    pieces = count // LANES
    rows_out = [
        remote(
            layer_ref.at[1 - mine, pl.ds(piece * LANES, LANES)],
            item_ref.at[pl.ds(pl.multiple_of(mine * count + piece * LANES, LANES), LANES)],
            sems.at[0, piece], sems.at[1, piece], partner,
        )
        for piece in range(pieces)
    ]
    for copy in rows_out:
        copy.start()
    for load in loads[:-2]:
        load.wait()

    fields = (segment_ref, mask_ref, position_ref, across_ref, down_ref)
    blocks = [
        jnp.concatenate(
            [field[item : item + 1, :] for field in fields] + [jnp.zeros((3, count), jnp.int32)],
            axis=0,
        )
        for item in range(2)
    ]
    meta_send[...] = jnp.where(mine == 0, blocks[1], blocks[0])
    meta_out = remote(
        meta_send, rows_ref.at[:, own], sems.at[0, pieces], sems.at[1, pieces], partner
    )
    meta_out.start()
    rows_ref[:, own] = jnp.where(mine == 0, blocks[0], blocks[1])
    bias_ref[:, :width] = query_bias_ref[...].astype(F32).reshape(1, width)
    bias_ref[:, width : 2 * width] = jnp.zeros((1, width), F32)
    bias_ref[:, 2 * width :] = value_bias_ref[...].astype(F32).reshape(1, width)
    heads, levels = text_ref.shape
    spot = lax.broadcasted_iota(jnp.int32, (levels, LANES), 1)
    level = lax.broadcasted_iota(jnp.int32, (levels, LANES), 0)
    table = jnp.zeros((heads, LANES), F32)
    for source, begin in ((text_ref, 0), (horiz_ref, X_TABLE), (vert_ref, Y_TABLE)):
        table = table + dot_nn(source[...], (spot == level + begin).astype(BF))
    table_ref[...] = jnp.concatenate([table, jnp.zeros((16 - heads, LANES), F32)], axis=0)

    def project(there):
        step = 256

        def body(index, carry):
            columns = pl.ds(pl.multiple_of(index * step, step), step)
            product = dot_nn(item_ref[there], weight_ref[:, columns])
            projected_ref[there, columns] = (product + bias_ref[:, columns]).astype(BF)
            return carry

        lax.fori_loop(0, 3 * width // step, body, 0)

    def stored(index, there):
        return pltpu.make_async_copy(
            projected_ref.at[there], projected_out.at[there], store_sems.at[index]
        )

    for load in loads[-2:]:
        load.wait()
    project(own)
    stored(0, own).start()
    for piece in range(pieces):
        rows_out[piece].wait()
        there = pl.ds(pl.multiple_of((1 - mine) * count + piece * LANES, LANES), LANES)
        project(there)
        stored(1 + piece, there).start()
    meta_out.wait()
    meta = rows_ref[...].astype(F32)
    tall = jnp.concatenate([meta, jnp.zeros((LANES - 8, meta.shape[1]), F32)], axis=0)
    columns_ref[...] = jnp.transpose(tall).astype(jnp.int32)
    stored(0, own).wait()
    for piece in range(pieces):
        there = pl.ds(pl.multiple_of((1 - mine) * count + piece * LANES, LANES), LANES)
        stored(1 + piece, there).wait()


def projected_item(layer_in, fields, qkv_weight, query_bias, value_bias, tables):
    rows = 2 * layer_in.shape[1]
    width = layer_in.shape[2]
    pieces = rows // 2 // LANES
    small = list(fields) + [query_bias, value_bias] + [t.T for t in tables]
    return pl.pallas_call(
        project_kernel,
        in_specs=[HBM] * (2 + len(small)),
        out_specs=[VMEM, HBM, VMEM, VMEM, VMEM],
        out_shape=[
            jax.ShapeDtypeStruct((rows, width), BF),
            jax.ShapeDtypeStruct((rows, 3 * width), BF),
            jax.ShapeDtypeStruct((rows, LANES), jnp.int32),
            jax.ShapeDtypeStruct((8, rows), jnp.int32),
            jax.ShapeDtypeStruct((16, LANES), F32),
        ],
        scratch_shapes=[
            pltpu.VMEM((rows, 3 * width), BF),
            pltpu.VMEM((width, 3 * width), BF),
            pltpu.VMEM((8, rows // 2), jnp.int32),
            pltpu.VMEM((1, 3 * width), F32),
            pltpu.SemaphoreType.DMA((2, pieces + 1)),
            pltpu.SemaphoreType.DMA((len(small) + 2,)),
            pltpu.SemaphoreType.DMA((pieces + 1,)),
        ]
        + [pltpu.VMEM(array.shape, array.dtype) for array in small],
        compiler_params=pltpu.CompilerParams(
            collective_id=1, has_side_effects=True, vmem_limit_bytes=60 * MIB
        ),
        name="projected_item",
    )(layer_in, qkv_weight, *small)


EPSILON = 1e-05
TILE = 256


def vector(ref):
    return ref[...].astype(F32).reshape(1, ref.shape[0])


def gelu_and_slope(x):
    bell = jnp.exp2(-0.7213475204444817 * (x * x))
    rough = 1.0 + 0.23164188826 * jnp.abs(x)
    t = pl.reciprocal(rough, approx=True)
    t = t * (2.0 - rough * t)
    series = t * (
        0.127414796
        + t * (-0.142248368 + t * (0.7107068705 + t * (-0.7265760135 + t * 0.5307027145)))
    )
    tail = bell * series
    below = jnp.where(x >= 0.0, 1.0 - tail, tail)
    return x * below, below + x * (0.3989422804014327 * bell)


def row_mean(block):
    return jnp.mean(block, axis=1, keepdims=True)


def normalized(hidden):
    center = hidden - row_mean(hidden)
    scale = lax.rsqrt(row_mean(center * center) + EPSILON)
    return center * scale, scale


def norm_pulled(grad, unit, scale):
    return scale * (grad - row_mean(grad) - unit * row_mean(grad * unit))


def column_sum(block):
    return jnp.sum(block, axis=0, keepdims=True)


def feed_kernel(
    depth, count_each, item_ref, mixed_ref, cotangent_ref, out_weight_ref, up_ref, down_ref, *refs,
):
    vectors_hbm, refs = refs[:7], refs[7:]
    (layer_out, d_hidden_ref, d_mixed_ref, grad_out_ref, down_out, up_out, small_ref,
     grad_down, grad_up, layer_ref, cotangent_all, active, slope, unit, scale_ref, normed, normed_t, total, d_branch, d_branch_t,
     sems, load_sems, store_sems) = refs[:23]
    vectors, scratch = refs[23:30], refs[30:]
    (out_bias_ref, attn_gain_ref, attn_shift_ref, up_bias_ref, down_bias_ref, ffn_gain_ref,
     ffn_shift_ref) = vectors
    step = pl.program_id(0)
    blocks = pl.num_programs(0) // 2
    rows, width = item_ref.shape
    count = rows // 2
    mine = lax.axis_index("seq")
    partner = (1 - mine, lax.axis_index("dp"))
    own = pl.ds(pl.multiple_of(mine * count, LANES), count)
    place = Place(depth)
    down_sum, up_sum = [
        Chunk(place, depth, source, None, 0, opening(*source.shape), pieces)
        for source, pieces in ((grad_down, scratch[:count_each]), (grad_up, scratch[count_each:]))
    ]

    def stores():
        copies = [pltpu.make_async_copy(up_sum.work, up_out, store_sems.at[0])]
        for part in range(2):
            size = down_sum.size(part, 0)
            begin = down_sum.aligned(down_sum.spot(part, 0))
            copies.append(
                pltpu.make_async_copy(
                    down_sum.work.at[pl.ds(begin, size)],
                    down_out.at[pl.ds(part * size, size)], store_sems.at[1 + part],
                )
            )
        return copies

    def sent():
        return remote(
            cotangent_ref.at[1 - mine], cotangent_all.at[own], sems.at[0], sems.at[1], partner
        )

    def returned():
        theirs = pl.ds(pl.multiple_of((1 - mine) * count, LANES), count)
        return [
            pltpu.make_async_copy(layer_ref.at[own], layer_out.at[mine], load_sems.at[8]),
            remote(
                layer_ref.at[theirs], layer_out.at[mine], sems.at[2], sems.at[3], partner
            ),
        ]

    def loads():
        copies = list(zip(vectors_hbm, vectors)) + [(cotangent_ref.at[mine], cotangent_all.at[own])]
        return [
            pltpu.make_async_copy(source, target, load_sems.at[index])
            for index, (source, target) in enumerate(copies)
        ]

    def over_tiles(size, body, carry, unroll=1):
        def run(index, state):
            return body(pl.ds(pl.multiple_of(index * size, size), size), state)

        return lax.fori_loop(0, rows // size, run, carry, unroll=unroll)

    @pl.when(step == 0)
    def _():
        for load in loads():
            load.start()
        place.greet("cxy")
        sent().start()
        small_ref[...] = jnp.zeros_like(small_ref)
        for load in loads():
            load.wait()
        out_bias, gain, shift = vector(out_bias_ref), vector(attn_gain_ref), vector(attn_shift_ref)

        def tile(there, carry):
            attn = dot_nn(mixed_ref[there].astype(BF), out_weight_ref[...]) + out_bias
            standard, scale = normalized(item_ref[there].astype(F32) + attn)
            unit[there] = standard
            scale_ref[there] = jnp.broadcast_to(scale, (scale.shape[0], LANES))
            result = standard * gain + shift
            normed[there] = result.astype(BF)
            normed_t[:, there] = jnp.transpose(result).astype(BF)
            return carry

        over_tiles(TILE, tile, 0, 3)
        total[...] = jnp.zeros_like(total)

    @pl.when(step < blocks)
    def _():
        columns = [slice(begin, begin + TILE) for begin in range(0, width, TILE)]
        low = normed[...]
        following = dot_nn(low, up_ref[:, columns[0]])
        values = []
        for index, here in enumerate(columns):
            product = following
            if index + 1 < len(columns):
                following = dot_nn(low, up_ref[:, columns[index + 1]])
            bias = up_bias_ref[pl.ds(pl.multiple_of(step * width + here.start, LANES), TILE)]
            value, grade = gelu_and_slope(product + bias.astype(F32).reshape(1, TILE))
            values.append(value.astype(BF))
            active[step, :, here] = values[-1]
            slope[step, :, here] = grade.astype(BF)
        values = jnp.concatenate(values, axis=1)
        for here in columns:
            total[:, here] += dot_nn(values, down_ref[:, here])

    @pl.when(step == blocks)
    def _():
        sent().wait()
        gain, shift, bias = vector(ffn_gain_ref), vector(ffn_shift_ref), vector(down_bias_ref)
        first_gain, first_shift = vector(attn_gain_ref), vector(attn_shift_ref)

        def tile(there, sums):
            hidden = unit[there] * first_gain + first_shift + (total[there] + bias)
            standard, scale = normalized(hidden)
            layer_ref[there] = (standard * gain + shift).astype(BF)
            cotangent = cotangent_all[there].astype(F32)
            pulled = norm_pulled(cotangent * gain, standard, scale)
            total[there] = pulled
            low = pulled.astype(BF)
            d_branch[there] = low
            return (
                sums[0] + column_sum(low.astype(F32)),
                sums[1] + column_sum(cotangent * standard),
                sums[2] + column_sum(cotangent),
            )

        zero = jnp.zeros((1, width), F32)
        sums = over_tiles(64, tile, (zero, zero, zero), 4)
        for row, value in zip((5, 6, 7), sums):
            small_ref[row : row + 1] = value

        for copy in returned():
            copy.start()

        def turn(there, carry):
            d_branch_t[:, there] = jnp.transpose(d_branch[there].astype(F32)).astype(BF)
            return carry

        over_tiles(TILE, turn, 0, 3)

        def whole_block(block, carry):
            base = pl.multiple_of(block * width, width)
            for begin in range(0, width, TILE):
                here = slice(begin, begin + TILE)
                product = dot_nn(d_branch_t[...], active[block, :, here])
                grad_down[pl.ds(base, width), here] = product.astype(BF)
            return carry

        lax.fori_loop(0, blocks, whole_block, 0)
        down_sum.stage(0)

    @pl.when(step >= blocks)
    def _():
        block = step - blocks

        columns = [slice(begin, begin + TILE) for begin in range(0, width, TILE)]
        branch = d_branch[...]
        following = dot_nt(branch, down_ref[columns[0]])
        values = []
        for index, here in enumerate(columns):
            product = following
            if index + 1 < len(columns):
                following = dot_nt(branch, down_ref[columns[index + 1]])
            d_up = (product * slope[block, :, here].astype(F32)).astype(BF)
            small_ref[pl.ds(8 + block, 1), here] = column_sum(d_up.astype(F32))
            values.append(d_up)
        values = jnp.concatenate(values, axis=1)
        turned = normed_t[...]
        for here in columns:
            product = dot_nn(turned, values[:, here])
            grad_up[pl.ds(pl.multiple_of(block * width, width), width), here] = product.astype(BF)
            total[:, here] += dot_nt(values, up_ref[here])

    @pl.when(step == blocks + 1)
    def _():
        down_sum.stage(1)

    @pl.when(step == 2 * blocks - 1)
    def _():
        up_sum.stage(0)
        gain = vector(attn_gain_ref)

        def tile(there, sums):
            d_normed = total[there]
            standard = unit[there]
            d_hidden = norm_pulled(d_normed * gain, standard, scale_ref[there, :1])
            d_hidden_ref[there] = d_hidden
            low = d_hidden.astype(BF)
            d_branch[there] = low
            return (
                sums[0] + column_sum(low.astype(F32)),
                sums[1] + column_sum(d_normed * standard),
                sums[2] + column_sum(d_normed),
            )

        zero = jnp.zeros((1, width), F32)
        sums = over_tiles(64, tile, (zero, zero, zero), 4)
        for row, value in zip((2, 3, 4), sums):
            small_ref[row : row + 1] = value

        def turn(there, carry):
            normed_t[:, there] = jnp.transpose(mixed_ref[there]).astype(BF)
            return carry

        over_tiles(TILE, turn, 0, 3)

        for begin in range(0, width, TILE):
            here = slice(begin, begin + TILE)
            d_mixed_ref[:, here] = dot_nt(d_branch[...], out_weight_ref[here]).astype(BF)
            grad_out_ref[:, here] = dot_nn(normed_t[...], d_branch[:, here]).astype(BF)

        for copy in up_sum.pair_down():
            copy.wait()
        up_sum.add(0, [up_sum.fresh], up_sum.half)
        for copy in down_sum.down(0):
            copy.wait()
        down_sum.add_hop(0)
        for copy in stores():
            copy.start()
        for copy in returned() + stores():
            copy.wait()


def opening(hidden, width):
    return (0, 0, hidden, 0, width, 0, "x y", 0, -1)


def fed_forward_and_back(
    item, mixed, cotangent, out_weight, up_weight, down_weight, vectors,
):
    rows, width = item.shape
    blocks = up_weight.shape[1] // width
    whole = pl.BlockSpec(memory_space=pltpu.VMEM)
    square = lambda kind: jax.ShapeDtypeStruct((rows, width), kind)
    depth = line_depth()
    hidden = up_weight.shape[1]
    sums = [chunk_scratch(opening(hidden, width), depth) for _ in range(2)]
    return pl.pallas_call(
        functools.partial(feed_kernel, depth, len(sums[0])),
        grid=(2 * blocks,),
        in_specs=[whole, whole, HBM, whole]
        + [
            pl.BlockSpec((width, width), lambda i: (0, lax.rem(i, blocks))),
            pl.BlockSpec((width, width), lambda i: (lax.rem(i, blocks), 0)),
        ]
        + [HBM] * 7,
        out_specs=[HBM] + [whole] * 3
        + [HBM, HBM, whole],
        out_shape=[
            jax.ShapeDtypeStruct((2, rows // 2, width), BF), square(F32), square(BF),
            jax.ShapeDtypeStruct((width, width), BF),
            jax.ShapeDtypeStruct((hidden // 4, width), BF),
            jax.ShapeDtypeStruct((hidden // 2, width), BF),
            jax.ShapeDtypeStruct((16, width), F32),
        ],
        scratch_shapes=[
            pltpu.VMEM((hidden, width), BF),
            pltpu.VMEM((hidden, width), BF),
            pltpu.VMEM((rows, width), BF),
            pltpu.VMEM((rows, width), BF),
            pltpu.VMEM((blocks, rows, width), BF),
            pltpu.VMEM((blocks, rows, width), BF),
            pltpu.VMEM((rows, width), F32),
            pltpu.VMEM((rows, LANES), F32),
            pltpu.VMEM((rows, width), BF),
            pltpu.VMEM((width, rows), BF),
            pltpu.VMEM((rows, width), F32),
            pltpu.VMEM((rows, width), BF),
            pltpu.VMEM((width, rows), BF),
            pltpu.SemaphoreType.DMA((4,)),
            pltpu.SemaphoreType.DMA((9,)),
            pltpu.SemaphoreType.DMA((3,)),
        ]
        + [pltpu.VMEM(vector.shape, vector.dtype) for vector in vectors]
        + [piece for pieces in sums for piece in pieces],
        compiler_params=pltpu.CompilerParams(
            collective_id=2, has_side_effects=True, vmem_limit_bytes=62 * MIB
        ),
        name="feed_forward",
    )(item, mixed, cotangent, out_weight, up_weight, down_weight, *vectors)


SLOTS = 4


def finish_kernel(
    main_ref, tail_ref, input_hbm, small_ref, diagonal_ref,
    down_ref, up_ref, out_ref, qkv_ref, input_ref, *refs,
):
    singles, (main_in, tail_in, slots, input_in, input_slot, in_sems, out_sems, item_sems) = (
        refs[:12], refs[12:],
    )
    mains, width = main_in.shape[0], main_in.shape[2]
    pairs, across = tail_in.shape[0], tail_in.shape[2]
    hidden = mains // 2
    blocks = mains + pairs

    def load(block):
        if block < mains:
            source, target = main_ref.at[pl.ds(block * width, width)], main_in.at[block]
        else:
            pair = block - mains
            source, target = tail_ref.at[pl.ds(pair * TAIL_ROWS, TAIL_ROWS)], tail_in.at[pair]
        return pltpu.make_async_copy(source, target, in_sems.at[block])

    def stores(block):
        slot, sem = slots.at[block % SLOTS], out_sems.at[block % SLOTS]
        if block < hidden:
            targets = [(slot, down_ref.at[pl.ds(block * width, width)])]
        elif block < mains:
            targets = [(slot, up_ref.at[:, pl.ds((block - hidden) * width, width)])]
        else:
            pair = block - mains
            targets = [
                (
                    slot.at[:, pl.ds(part * LANES, LANES)],
                    qkv_ref.at[:, pl.ds(part * width + pair * LANES, LANES)],
                )
                for part in range(3)
            ]
            down = pl.ds(0, TAIL_ROWS - width)
            targets.append(
                (slot.at[down, pl.ds(across, across)], out_ref.at[out_spot(pair, pairs, width)])
            )
        return [
            pltpu.make_async_copy(source, target, sem.at[index])
            for index, (source, target) in enumerate(targets)
        ]

    load_input = pltpu.make_async_copy(input_hbm, input_in, item_sems.at[0])
    store_input = pltpu.make_async_copy(input_slot, input_ref, item_sems.at[1])
    for block in range(blocks):
        load(block).start()
    load_input.start()
    for block in range(blocks):
        load(block).wait()
        if block >= SLOTS:
            for copy in stores(block - SLOTS):
                copy.wait()
        slot = block % SLOTS
        if block < hidden:
            slots[slot] = jnp.transpose(main_in[block].astype(F32))
        elif block < mains:
            slots[slot] = main_in[block].astype(F32)
        else:
            slots[slot, :, :across] = tail_in[block - mains, :width].astype(F32)
            slots[slot, : TAIL_ROWS - width, across:] = tail_in[block - mains, width:].astype(F32)
        for copy in stores(block):
            copy.start()
    load_input.wait()
    input_slot[...] = input_in[...].astype(F32)
    store_input.start()
    for row in range(8):
        singles[row][...] = small_ref[row]
    for row in range(hidden):
        singles[8][row * width : row * width + width] = small_ref[8 + row]
    heads, levels = singles[9].shape
    diagonals = diagonal_ref[...]
    level = lax.broadcasted_iota(jnp.int32, (LANES, LANES), 1)
    lane = lax.broadcasted_iota(jnp.int32, (LANES, LANES), 0)
    for table, (first, size, skip) in enumerate(((0, 4, 0), (4, 2, 1), (6, 2, 1))):
        total = jnp.zeros((heads, LANES), F32)
        for row in range(size):
            distance = lane + LANES * (row + skip - 2)
            chosen = (bucket(distance) == level).astype(F32)
            total = total + jnp.dot(
                diagonals[:, first + row, :], chosen, preferred_element_type=F32,
                precision=lax.Precision.HIGHEST,
            )
        singles[9 + table][...] = total[:, :levels]
    for block in range(blocks - SLOTS, blocks):
        for copy in stores(block):
            copy.wait()
    store_input.wait()


def finished(main, tail, grad_input, small, diagonals, hidden, levels):
    width = main.shape[1]
    heads = diagonals.shape[0]
    mains = main.shape[0] // width
    pairs = tail.shape[0] // TAIL_ROWS
    single = jax.ShapeDtypeStruct((width,), F32)
    table = jax.ShapeDtypeStruct((heads, levels), F32)
    dma = pltpu.SemaphoreType.DMA
    return pl.pallas_call(
        finish_kernel,
        in_specs=[HBM, HBM, HBM, VMEM, VMEM],
        out_specs=[HBM] * 5 + [VMEM] * 12,
        out_shape=[
            jax.ShapeDtypeStruct((hidden, width), F32),
            jax.ShapeDtypeStruct((width, hidden), F32),
            jax.ShapeDtypeStruct((width, width), F32),
            jax.ShapeDtypeStruct((width, 3 * width), F32),
            jax.ShapeDtypeStruct(grad_input.shape, F32),
        ]
        + [single] * 8
        + [jax.ShapeDtypeStruct((hidden,), F32)]
        + [table] * 3,
        scratch_shapes=[
            pltpu.VMEM((mains, width, width), BF),
            pltpu.VMEM((pairs, TAIL_ROWS, tail.shape[1]), BF),
            pltpu.VMEM((SLOTS, width, width), F32),
            pltpu.VMEM(grad_input.shape, BF),
            pltpu.VMEM(grad_input.shape, F32),
            dma((mains + pairs,)),
            dma((SLOTS, 4)),
            dma((2,)),
        ],
        compiler_params=pltpu.CompilerParams(vmem_limit_bytes=56 * MIB),
        name="finished",
    )(main, tail, grad_input, small, diagonals)


PIECE = 16


class Place:
    def __init__(self, depth):
        place = lax.axis_index("dp")
        self.depth = depth
        self.group = lax.div(place, 4 * depth)
        self.z = lax.rem(lax.div(place, 4), depth)
        self.bits = {
            "x": lax.axis_index("seq"),
            "c": lax.rem(place, 2),
            "y": lax.rem(lax.div(place, 2), 2),
            "a": lax.rem(self.z, 2),
            "b": lax.div(self.z, 2),
        }

    def partner(self, letters):
        bit = {
            letter: 1 - value if letter in letters else value
            for letter, value in self.bits.items()
        }
        z = self.z
        for letter, reach in (("a", 1), ("b", 2)):
            if letter in letters:
                z = z + reach - 2 * reach * self.bits[letter]
        return (bit["x"], (self.group * self.depth + z) * 4 + bit["y"] * 2 + bit["c"])

    def greet(self, met):
        barrier = pltpu.get_barrier_semaphore()
        for letters in met:
            pl.semaphore_signal(
                barrier, inc=1, device_id=self.partner(letters), device_id_type=MESH
            )
        pl.semaphore_wait(barrier, len(met))


def line_depth():
    size = lax.axis_size("dp")
    return 4 if size % 16 == 0 else size // 4


def letters_of(depth):
    return "xy" + "ab"[: (depth - 1).bit_length()]


def parsed(routes, depth):
    kept = letters_of(depth)
    parts = []
    for route in routes.split():
        hops = ["".join(letter for letter in hop if letter in kept) for hop in route.split(".")]
        parts.append([hop for hop in hops if hop])
    return parts


def subsets(hop):
    return [
        "".join(letter for index, letter in enumerate(hop) if mask >> index & 1)
        for mask in range(1, 2 ** len(hop))
    ]


class Chunk:
    def __init__(self, place, depth, source, out_ref, offset, spot, scratch):
        _, self.begin, rows, first, columns, _, routes, _, self.done = spot
        self.place, self.source, self.columns = place, source, pl.ds(first, columns)
        self.out_ref, self.out_begin = out_ref, offset + self.begin
        self.parts = parsed(routes, depth)
        self.half = rows // 2
        self.share = self.half // len(self.parts)
        self.hops = max(len(part) for part in self.parts)
        *landing, self.sends, self.receives, self.locals = scratch
        if self.done < 0:
            self.work = source.at[
                pl.ds(self.aligned(self.begin + place.bits["c"] * self.half), self.half)
            ]
        else:
            self.work = landing.pop(0)
        if self.done <= 0:
            self.fresh = landing.pop(0)
        self.numbers = list(range(2 * self.hops + 3))
        if self.done == 2:
            self.numbers.remove(1)
        self.landing = {}
        self.sems = {}
        count = 2
        for part, hops in enumerate(self.parts):
            for hop, letters in enumerate(hops):
                if hop > 0 or self.done < 2:
                    self.landing[part, hop] = landing.pop(0)
                for way in range(2):
                    for index in range(2 ** len(letters) - 1):
                        self.sems[way, part, hop, index] = count
                        count += 1

    def aligned(self, value):
        return pl.multiple_of(value, PIECE)

    def size(self, part, hop):
        return self.share >> sum(len(letters) for letters in self.parts[part][: hop + 1])

    def spot(self, part, hop, other=""):
        start = part * self.share
        for level in range(hop + 1):
            for index, letter in enumerate(self.parts[part][level]):
                bit = self.place.bits[letter]
                if level == hop and letter in other:
                    bit = 1 - bit
                start = start + bit * (self.size(part, level) << index)
        return start

    def out(self, begin, size, core=None):
        core = self.place.bits["c"] if core is None else core
        return self.out_ref.at[
            pl.ds(self.aligned(self.out_begin + core * self.half + begin), size), self.columns
        ]

    def copy(self, index, source, target, letters):
        return remote(
            source, target, self.sends.at[index], self.receives.at[index],
            self.place.partner(letters),
        )

    def pair_down(self):
        core = self.place.bits["c"]
        at = lambda c: self.source.at[
            pl.ds(self.aligned(self.begin + c * self.half), self.half), self.columns
        ]
        copies = [self.copy(0, at(1 - core), self.fresh, "c")]
        if self.done == 0:
            copies.append(pltpu.make_async_copy(at(core), self.work, self.locals.at[0]))
        return copies

    def loaded(self):
        if self.done == 1:
            pieces = [(0, 0, self.half)]
        else:
            pieces = [
                (part * self.size(part, 0), self.spot(part, 0), self.size(part, 0))
                for part in range(len(self.parts))
            ]
        return [
            pltpu.make_async_copy(
                self.source.at[pl.ds(begin, size), self.columns],
                self.work.at[pl.ds(target if self.done == 1 else self.aligned(target), size)],
                self.locals.at[index],
            )
            for index, (begin, target, size) in enumerate(pieces)
        ]

    def pair_up(self, arriving):
        core = self.place.bits["c"]
        target = self.out(0, self.half, 1 - core if arriving else core)
        return [self.copy(1, self.out(0, self.half), target, "c")]

    def at_hop(self, hop):
        return [
            (part, hops[hop]) for part, hops in enumerate(self.parts) if hop < len(hops)
        ]

    def down(self, hop):
        copies = []
        for part, letters in self.at_hop(hop):
            size = self.size(part, hop)
            for index, other in enumerate(subsets(letters)):
                begin = self.aligned(self.spot(part, hop, other))
                copies.append(
                    self.copy(
                        self.sems[0, part, hop, index], self.work.at[pl.ds(begin, size)],
                        self.landing[part, hop].at[index], other,
                    )
                )
        return copies

    def kept(self):
        copies = []
        for part, hops in enumerate(self.parts):
            last = len(hops) - 1
            size = self.size(part, last)
            begin = self.aligned(self.spot(part, last))
            copies.append(
                pltpu.make_async_copy(
                    self.work.at[pl.ds(begin, size)], self.out(begin, size),
                    self.locals.at[2 + part],
                )
            )
        return copies

    def up(self, hop, arriving):
        copies = []
        for part, letters in self.at_hop(hop):
            mine = self.spot(part, hop)
            size = self.size(part, hop)
            if hop == len(self.parts[part]) - 1:
                source = self.work.at[pl.ds(self.aligned(mine), size)]
            else:
                source = self.out(mine, size)
            for index, other in enumerate(subsets(letters)):
                target = self.out(self.spot(part, hop, other) if arriving else mine, size)
                copies.append(self.copy(self.sems[1, part, hop, index], source, target, other))
        return copies

    def add(self, begin, sources, size):
        step = 64 if size % 64 == 0 else 32 if size % 32 == 0 else PIECE

        def body(index, carry):
            offset = self.aligned(index * step)
            there = pl.ds(self.aligned(begin + offset), step)
            total = self.work[there]
            if len(sources) == 1:
                total = total + sources[0][pl.ds(offset, step)]
            else:
                total = total.astype(F32)
                for source in sources:
                    total = total + source[pl.ds(offset, step)].astype(F32)
            self.work[there] = total.astype(BF)
            return carry

        lax.fori_loop(0, size // step, body, 0)

    def stage(self, index):
        hops = self.hops
        number = self.numbers[index]
        opened = index == 1
        ended, started = [], []
        if number == 0:
            started = self.loaded() if self.done > 0 else self.pair_down()
        elif opened:
            ended = self.loaded() if self.done > 0 else self.pair_down()
            started = self.down(number - 1)
        elif number <= hops:
            ended = self.down(number - 2)
            started = self.down(number - 1)
        elif number == hops + 1:
            ended = self.down(hops - 1)
            started = self.up(hops - 1, False) + self.kept()
        elif number <= 2 * hops:
            level = 2 * hops + 1 - number
            ended = self.up(level, True) + (self.kept() if level == hops - 1 else [])
            started = self.up(level - 1, False)
        elif number == 2 * hops + 1:
            ended = self.up(0, True)
            started = self.pair_up(False)
        else:
            ended = self.pair_up(True)
        for copy in ended:
            copy.wait()
        if opened and self.done <= 0:
            self.add(0, [self.fresh], self.half)
        elif not opened and 2 <= number <= hops + 1:
            self.add_hop(number - 2)
        for copy in started:
            copy.start()

    def add_hop(self, hop):
        for part, letters in self.at_hop(hop):
            landing = self.landing[part, hop]
            sources = [landing.at[index] for index in range(2 ** len(letters) - 1)]
            self.add(self.spot(part, hop), sources, self.size(part, hop))


def chunk_scratch(spot, depth):
    _, _, rows, _, columns, _, routes, _, done = spot
    parts = parsed(routes, depth)
    half = pltpu.VMEM((rows // 2, columns), BF)
    buffers = {-1: [half], 0: [half, half], 1: [half], 2: [half]}[done]
    copies = 2
    for hops in parts:
        size = rows // 2 // len(parts)
        for hop, letters in enumerate(hops):
            size >>= len(letters)
            others = 2 ** len(letters) - 1
            copies += 2 * others
            if hop > 0 or done < 2:
                buffers.append(pltpu.VMEM((others, size, columns), BF))
    dma = pltpu.SemaphoreType.DMA
    return buffers + [dma((copies,)), dma((copies,)), dma((2 + len(parts),))]


def loads_of(hop, size):
    if "x" in hop and "y" in hop:
        return [("x", 2 * size), ("y", 2 * size)]
    if hop in ("x", "y"):
        return [(hop, size)]
    if "a" in hop and "b" in hop:
        return [("end", 3 * size), ("middle", 4 * size)]
    return [("end", size), ("middle", 2 * size)] if hop == "b" else [("end", size)]


def planned(chunks, work, depth, hop_count):
    latency, issue, link, pair = 3.5, 0.08, 100e3, 600e3
    free = {}
    now = 3.0
    chains = []
    for rows, columns, need, routes, _, ahead in chunks:
        parts = parsed(routes, depth)
        sizes = [rows // 2 // len(parts)] * len(parts)
        down = []
        for hop in range(max(len(part) for part in parts)):
            loads, copies, added = [], 0, 0
            for index, part in enumerate(parts):
                if hop < len(part):
                    sizes[index] >>= len(part[hop])
                    others = 2 ** len(part[hop]) - 1
                    loads += loads_of(part[hop], sizes[index])
                    copies += others
                    added += sizes[index] * others
            down.append((loads, copies, added, columns))
        first = [([("core", rows // 2)], 1.5, rows // 2, columns)]
        if ahead:
            first = [([("core", 0)], 0.5, 0, columns)]
        last = [([("core", rows // 2)], 1, 0, columns)]
        back = [(loads, copies, 0, columns) for loads, copies, _, _ in down[::-1]]
        chains.append((need, first + down[1 if ahead == 2 else 0 :] + back + last))
    chains.append((len(work), [([("core", 16)], 2, 0, 768)] * hop_count))
    ranks = [chunk[4] for chunk in chunks] + [0]
    position = [0] * len(chains)
    ready = [0.0] * len(chains)
    order = [[] for _ in range(len(work) + 1)]
    done = 0
    while True:
        open_ones = [
            (ranks[i], ready[i], i) for i, (need, chain) in enumerate(chains)
            if position[i] <= len(chain) and need <= done
        ]
        due = [entry for entry in open_ones if entry[1] <= now]
        if not due and done < len(work):
            now += work[done]
            done += 1
            continue
        if not open_ones:
            return order
        _, when, index = min(due) if due else min(open_ones, key=lambda entry: entry[1])
        now = max(now, when)
        chain = chains[index][1]
        stage = position[index]
        order[done].append((index, stage))
        if stage > 0:
            now += 1e-6 * chain[stage - 1][2] * chain[stage - 1][3]
        if stage < len(chain):
            loads, copies, _, columns = chain[stage]
            now += issue * copies
            end = now
            for lane, rows in loads:
                rate = pair if lane == "core" else link / 2
                free[lane] = max(now, free.get(lane, 0.0)) + 2 * rows * columns / rate
                end = max(end, free[lane])
            ready[index] = end + latency
        position[index] += 1


def last_kernel(
    depth, plan, orders, counts, *refs,
):
    (meta_ref, rows_ref, projected_hbm, mixed_hbm, grad_hbm, log_ref, first_hbm, second_hbm,
     key_image_hbm, bias_hbm, small_ref, item_hbm, weight_hbm, d_hidden_hbm, grad_down_ref, grad_up_ref,
     grad_out_ref,
     main_out, tail_out, small_out, diagonal_out, input_out,
     *scratch) = refs
    static, scratch = scratch[:6], scratch[6:]
    (k_ref, v_ref, mixed_ref, grad_ref, first_ref, second_ref, key_image_ref, bias_ref, pair_sems,
     item_ref, weight_ref, d_hidden_ref, load_sems, d_project, item_t, tail, input_grad,
     small_in, diagonal_in, small_sems, item_sems, *scratch) = scratch
    place = Place(depth)
    step = pl.program_id(0)
    pairs = k_ref.shape[0]
    rows, width = item_hbm.shape
    count = rows // 2
    x = place.bits["x"]
    hidden = 2 * grad_up_ref.shape[0]
    sources = ((grad_down_ref, main_out, 0), (grad_up_ref, main_out, hidden), (tail, tail_out, 0))
    chunks = []
    for spot, pieces in zip(plan, counts):
        chunks.append(Chunk(place, depth, *sources[spot[0]], spot, scratch[:pieces]))
        scratch = scratch[pieces:]
    hop_letters = "c" + letters_of(depth)
    wide_hbm = (first_hbm, second_hbm, key_image_hbm, bias_hbm)
    wide_refs = (first_ref, second_ref, key_image_ref, bias_ref)

    def pair_loads(pair):
        copies = []
        held = (
            (projected_hbm, k_ref, width), (projected_hbm, v_ref, 2 * width),
            (mixed_hbm, mixed_ref, 0), (grad_hbm, grad_ref, 0),
        )
        for source, target, first in held:
            columns = pl.ds(pl.multiple_of(first + pair * LANES, LANES), LANES)
            copies.append((source.at[:, columns], target.at[pair]))
        heads = pl.ds(2 * pair, 2)
        for source, target in zip(wide_hbm, wide_refs):
            copies.append((source.at[heads], target.at[heads]))
        return [
            pltpu.make_async_copy(source, target, pair_sems.at[pair, index])
            for index, (source, target) in enumerate(copies)
        ]

    def loads():
        copies = [(item_hbm, item_ref), (weight_hbm, weight_ref), (d_hidden_hbm, d_hidden_ref)]
        for pair in range(pairs):
            down, across = out_spot(pair, pairs, width)
            copies.append(
                (
                    grad_out_ref.at[down, across],
                    tail.at[pl.ds(pair * TAIL_ROWS + width, TAIL_ROWS - width)],
                )
            )
        return [
            pltpu.make_async_copy(source, target, load_sems.at[index])
            for index, (source, target) in enumerate(copies)
        ]

    def input_copies():
        return [
            pltpu.make_async_copy(
                input_grad.at[pl.ds(pl.multiple_of(x * count, LANES), count)], input_out.at[x],
                item_sems.at[0],
            ),
            remote(
                input_grad.at[pl.ds(pl.multiple_of((1 - x) * count, LANES), count)],
                input_out.at[x], item_sems.at[1], item_sems.at[2], place.partner("x"),
            ),
        ]

    def small_copies(hop):
        return [
            remote(source, landing.at[hop], small_sems.at[0, kind, hop],
                   small_sems.at[1, kind, hop], place.partner(hop_letters[hop]))
            for kind, (source, landing) in enumerate(
                ((small_out, small_in), (diagonal_out, diagonal_in))
            )
        ]

    def small_stage(hop):
        if hop > 0:
            for copy in small_copies(hop - 1):
                copy.wait()
            small_out[...] = small_out[...] + small_in[hop - 1]
            diagonal_out[...] = diagonal_out[...] + diagonal_in[hop - 1]
        if hop < len(hop_letters):
            for copy in small_copies(hop):
                copy.start()

    def perform(slot):
        for index, stage in orders[slot]:
            if index == len(chunks):
                small_stage(stage)
            else:
                chunks[index].stage(stage)

    @pl.when(step == 0)
    def _():
        for pair in range(pairs):
            for copy in pair_loads(pair):
                copy.start()
        for copy in loads():
            copy.start()
        met = set(hop_letters)
        for chunk in chunks:
            for hops in chunk.parts:
                for letters in hops:
                    met.update(subsets(letters))
        place.greet(sorted(met))
        small_out[...] = small_ref[...]

    for pair in range(pairs):
        @pl.when(step == pair)
        def _(pair=pair):
            perform(pair)

    @pl.when(step == 0)
    def _():
        static_prepare(meta_ref, static)
        for copy in loads():
            copy.wait()
        for tile in range(rows // TILE):
            there = slice(tile * TILE, tile * TILE + TILE)
            item_t[:, there] = jnp.transpose(item_ref[there].astype(F32)).astype(BF)

    for copy in pair_loads(step):
        copy.wait()
    (dq_even, dk_even, dv_even), (dq_odd, dk_odd, dv_odd) = [
        head_back(
            parity, step, rows_ref, wide_refs, k_ref, v_ref, mixed_ref, grad_ref, log_ref,
            static, diagonal_out,
        )
        for parity in range(2)
    ]
    even = own_lanes(0, rows)
    pieces = [
        jnp.transpose(jnp.concatenate([dq_even, dq_odd], axis=0)).astype(BF),
        jnp.where(even, dk_even, dk_odd).astype(BF),
        jnp.where(even, dv_even, dv_odd).astype(BF),
    ]
    for part, piece in enumerate(pieces):
        d_project[:, pl.ds(pl.multiple_of(part * width + step * LANES, LANES), LANES)] = piece
    slab = pl.ds(pl.multiple_of(step * TAIL_ROWS, TAIL_ROWS), width)
    tail[slab] = dot_nn(item_t[...], jnp.concatenate(pieces, axis=1)).astype(BF)

    @pl.when(step == pairs - 1)
    def _():
        perform(pairs)
        for begin in range(0, width, TILE):
            here = slice(begin, begin + TILE)
            total = d_hidden_ref[:, here] + dot_nt(d_project[...], weight_ref[here])
            input_grad[:, here] = total.astype(BF)
        for copy in input_copies():
            copy.start()
        for begin in range(0, width, TILE):
            here = slice(begin, begin + TILE)
            there = slice(2 * width + begin, 2 * width + begin + TILE)
            small_out[0:1, here] = column_sum(d_project[:, here].astype(F32))
            small_out[1:2, here] = column_sum(d_project[:, there].astype(F32))
        perform(pairs + 1)
        for copy in input_copies():
            copy.wait()


TAIL_ROWS = 1024


def out_spot(pair, pairs, width):
    down = TAIL_ROWS - width
    across = width * width // (pairs * down)
    per_row = width // across
    return (
        pl.ds(pair // per_row * down, down),
        pl.ds(pair % per_row * across, across),
    )


def summed_with_attention_back(
    meta_columns, meta_rows, projected, mixed, d_mixed, logs, wide_arrays, item, qkv_weight,
    d_hidden, small, grad_down, grad_up, grad_out,
):
    depth = line_depth()
    size = lax.axis_size("dp")
    rows, width = item.shape
    pairs = width // LANES
    hidden = 2 * grad_up.shape[0]
    hops = len(letters_of(depth)) + 1
    work = [6.8] * pairs + [4.0]
    tall = 1024
    plan = [
        (0, 0, hidden, 0, 256, 0, "x.a.b.y y.x.a.b", 4, 2),
        (0, 0, hidden, 256, 256, 0, "x.y.a.b y.a.x.b", 3, 2),
        (0, 0, hidden, 512, 256, 0, "x.a.y.b y.a.b.x", 1, 2),
        (1, 0, hidden, 0, 256, 0, "a.x.b.y y.a.x.b", 3, 1),
        (1, 0, hidden, 256, 256, 0, "xy.ab", 2, 1),
        (1, 0, hidden, 512, 256, 0, "x.y.a.b a.x.b.y", 3, 1),
        (2, 0 * tall, tall, 0, 384, 1, "xy.ab", 4, 0),
        (2, 1 * tall, tall, 0, 384, 2, "x.y.a.b a.b.y.x", 2, 0),
        (2, 2 * tall, tall, 0, 384, 3, "y.a.b.x x.y.a.b", 1, 0),
        (2, 3 * tall, tall, 0, 384, 4, "x.y.a.b y.x.a.b", 2, 0),
        (2, 4 * tall, tall, 0, 384, 5, "y.ab.x x.y.ab", 4, 0),
        (2, 5 * tall, tall, 0, 384, 6, "ab.y.x y.ab.x", 1, 0),
    ]
    orders = planned([(spot[2],) + spot[4:] for spot in plan], work, depth, hops)

    whole = pl.BlockSpec(memory_space=pltpu.VMEM)
    diagonals = jax.ShapeDtypeStruct((2 * pairs, 8, LANES), F32)
    dma = pltpu.SemaphoreType.DMA
    scratch = []
    for spot in plan:
        scratch.append(chunk_scratch(spot, depth))
    main, tail, small, diagonals, grad_input = pl.pallas_call(
        functools.partial(last_kernel, depth, plan, orders, [len(pieces) for pieces in scratch]),
        grid=(pairs,),
        in_specs=[whole] * 2 + [HBM] * 3 + [whole] + [HBM] * 4 + [whole] + [HBM] * 6,
        out_specs=[HBM, HBM, whole, whole, HBM],
        out_shape=[
            jax.ShapeDtypeStruct((2 * hidden, width), BF),
            jax.ShapeDtypeStruct((pairs * TAIL_ROWS, 3 * LANES), BF),
            jax.ShapeDtypeStruct(small.shape, F32),
            diagonals,
            jax.ShapeDtypeStruct((2, rows // 2, width), BF),
        ],
        scratch_shapes=[pltpu.VMEM((rows, LANES), BF)] * 3
        + [pltpu.VMEM((LANES, rows), BF)] * 3
        + [pltpu.VMEM((pairs, rows, LANES), kind) for kind in (BF, BF, F32, BF)]
        + [pltpu.VMEM(array.shape, BF) for array in wide_arrays]
        + [
            dma((pairs, 8)),
            pltpu.VMEM((rows, width), BF),
            pltpu.VMEM((width, 3 * width), BF),
            pltpu.VMEM((rows, width), F32),
            dma((3 + pairs,)),
            pltpu.VMEM((rows, 3 * width), BF),
            pltpu.VMEM((width, rows), BF),
            pltpu.VMEM((pairs * TAIL_ROWS, 3 * LANES), BF),
            pltpu.VMEM((rows, width), BF),
            pltpu.VMEM((hops,) + small.shape, F32),
            pltpu.VMEM((hops,) + diagonals.shape, F32),
            dma((2, 2, hops)),
            dma((3,)),
        ]
        + [piece for pieces in scratch for piece in pieces],
        compiler_params=pltpu.CompilerParams(
            collective_id=0, has_side_effects=True, vmem_limit_bytes=62 * MIB
        ),
        name="summed_with_attention_back",
    )(meta_columns, meta_rows, projected, mixed, d_mixed, logs, *wide_arrays,
      small, item, qkv_weight, d_hidden, grad_down, grad_up, grad_out)
    span = 4 * depth
    if size > span:
        groups = [list(range(first, size, span)) for first in range(span)]
        main, tail, small, diagonals = lax.psum(
            (main.astype(F32), tail.astype(F32), small, diagonals), "dp",
            axis_index_groups=groups,
        )
        main, tail = main.astype(BF), tail.astype(BF)
    return main, tail, small, diagonals, grad_input


def per_device(
    layer_in, segment, key_mask, position, layout_x, layout_y,
    qkv_weight, query_bias, value_bias, out_weight, out_bias, attn_gain, attn_shift,
    up_weight, up_bias, down_weight, down_bias, ffn_gain, ffn_shift,
    text_table, horiz_table, vert_table, cotangent,
):
    width = layer_in.shape[-1]
    item, projected, meta_columns, meta_rows, table_rows = projected_item(
        layer_in, (segment, key_mask, position, layout_x, layout_y),
        qkv_weight, query_bias, value_bias, (text_table, horiz_table, vert_table),
    )
    mixed, logs, *wide_arrays = attention_forward(meta_columns, meta_rows, table_rows, projected, width)
    layer_out, d_hidden, d_mixed, grad_out, grad_down, grad_up, small = fed_forward_and_back(
        item, mixed, cotangent, out_weight, up_weight, down_weight,
        (out_bias, attn_gain, attn_shift, up_bias, down_bias, ffn_gain, ffn_shift),
    )
    main, tail, small, diagonals, grad_input = summed_with_attention_back(
        meta_columns, meta_rows, projected, mixed, d_mixed, logs, wide_arrays, item, qkv_weight,
        d_hidden, small, grad_down, grad_up, grad_out,
    )
    done = finished(
        main, tail, grad_input, small, diagonals, up_weight.shape[1], text_table.shape[0]
    )
    sum_down, sum_up, sum_out, sum_qkv, grad_input = done[:5]
    singles, tables = done[5:14], [t.T for t in done[14:]]
    return (
        layer_out, grad_input, sum_qkv, singles[0], singles[1], sum_out, singles[2], singles[3],
        singles[4], sum_up, singles[8], sum_down, singles[5], singles[6], singles[7],
        tables[0], tables[1], tables[2],
    )


def solution(mesh):
    rows = P("dp", "seq", None)
    marks_spec = P("dp", "seq")
    return jax.shard_map(
        per_device,
        mesh=mesh,
        in_specs=(rows,) + (marks_spec,) * 5 + (P(),) * 16 + (rows,),
        out_specs=(rows, rows) + (P(),) * 16,
        check_vma=False,
    )
```

```python
import functools

import jax
import jax.numpy as jnp
from jax import lax
from jax.experimental import pallas as pl
from jax.experimental.pallas import tpu as pltpu
from jax.sharding import PartitionSpec as P

BF = jnp.bfloat16
F32 = jnp.float32
BIG = 1e30
LANES = 128
HEAD = 64
TEXT = 512
POS = 64
COORD = 48
Y0 = 64
GROUP0 = 112
MEMBER0 = 116
FLAG = 124
X_TABLE = 33
Y_TABLE = 66
NOTHING = 127


def dot_nt(a, b):
    return lax.dot_general(a, b, (((1,), (1,)), ((), ())), preferred_element_type=F32)


def dot_nn(a, b):
    return lax.dot_general(a, b, (((1,), (0,)), ((), ())), preferred_element_type=F32)


def looked_up(table_row, index):
    rows = index.shape[0]
    return jnp.take_along_axis(
        jnp.broadcast_to(table_row, (rows, LANES)), index, axis=1, mode="promise_in_bounds"
    )


def bucket(distance):
    return jnp.clip(distance, -16, 16) + 16


def between(lane, low, high):
    return (lane >= low) & (lane < high)


def columns_of(meta_ref):
    return tuple(meta_ref[:, field : field + 1] for field in range(5))


def marks(meta_ref):
    segment, key_mask, position, across, down = columns_of(meta_ref)
    rows = segment.shape[0]
    lane = lax.broadcasted_iota(jnp.int32, (rows, LANES), 1)
    row = lax.broadcasted_iota(jnp.int32, (rows, LANES), 0)
    even = between(lane, HEAD, HEAD + COORD) & (lane - HEAD == across)
    odd = (lane < COORD) & (lane == across)
    group = (segment - 1) >> 3
    member = (segment - 1) & 7
    named = segment > 0
    shared = (
        ((row < TEXT) & (lane < POS) & (lane == position))
        | (between(lane, Y0, Y0 + COORD) & (lane - Y0 == down))
        | (named & between(lane, GROUP0, MEMBER0) & (lane - GROUP0 == group))
        | (named & between(lane, MEMBER0, FLAG) & (lane - MEMBER0 == member))
        | ((lane == FLAG) & (key_mask <= 0))
    )
    return tuple(jnp.where(m, 1.0, 0.0).astype(BF) for m in (even, odd, shared))


def barred(meta_ref):
    segment = meta_ref[:, 0:1]
    rows = segment.shape[0]
    lane = lax.broadcasted_iota(jnp.int32, (rows, LANES), 1)
    group = (segment - 1) >> 3
    member = (segment - 1) & 7
    shut = (
        ((segment > 0) & between(lane, GROUP0, MEMBER0) & (lane - GROUP0 != group))
        | ((segment < 0) & between(lane, GROUP0, MEMBER0))
        | ((segment > 0) & between(lane, MEMBER0, FLAG) & (lane - MEMBER0 != member))
        | (lane == FLAG)
    )
    return jnp.where(shut, -BIG, 0.0).astype(F32)


def query_index(meta_ref):
    segment, key_mask, position, across, down = columns_of(meta_ref)
    rows = segment.shape[0]
    lane = lax.broadcasted_iota(jnp.int32, (rows, LANES), 1)
    x_even = bucket(across - (lane - HEAD)) + X_TABLE
    x_odd = bucket(across - lane) + X_TABLE
    even = jnp.where(between(lane, HEAD, HEAD + COORD), x_even, NOTHING)
    odd = jnp.where(lane < COORD, x_odd, NOTHING)
    shared = jnp.where(
        lane < POS,
        bucket(position - lane),
        jnp.where(between(lane, Y0, Y0 + COORD), bucket(down - (lane - Y0)) + Y_TABLE, NOTHING),
    )
    return even, odd, shared


def image_key_index(meta_ref):
    position = meta_ref[TEXT:, 2:3]
    lane = lax.broadcasted_iota(jnp.int32, (position.shape[0], LANES), 1)
    return jnp.where(lane < POS, bucket(lane - position), NOTHING)


def prepare(meta_ref, mark_refs, bar_ref, index_refs, key_index_ref):
    for ref, value in zip(mark_refs, marks(meta_ref)):
        ref[...] = value
    bar_ref[...] = barred(meta_ref)
    for ref, value in zip(index_refs, query_index(meta_ref)):
        ref[...] = value
    key_index_ref[...] = image_key_index(meta_ref)


def image_offsets(row_positions, column_positions):
    return bucket(column_positions - row_positions)


def own_lanes(parity, rows):
    lane = lax.broadcasted_iota(jnp.int32, (rows, LANES), 1)
    return (lane < HEAD) if parity == 0 else (lane >= HEAD)


def widened(parity, q, table_row, bar_ref, index_refs, key_index_ref, shared_ref):
    rows = q.shape[0]
    images = key_index_ref.shape[0]
    first = jnp.where(
        own_lanes(parity, rows),
        q.astype(F32) * 0.125,
        looked_up(table_row, index_refs[parity][...]),
    )
    second = (looked_up(table_row, index_refs[2][...]) + bar_ref[...]).astype(BF)
    image_lane = lax.broadcasted_iota(jnp.int32, (images, LANES), 1)
    key_image = jnp.where(
        image_lane < POS, looked_up(table_row, key_index_ref[...]).astype(BF), shared_ref[TEXT:]
    )
    return first.astype(BF), second, key_image


def joined(parity, first, second, key_image, k, marks_own, shared):
    rows = k.shape[0]
    lane = lax.broadcasted_iota(jnp.int32, (rows, LANES), 1)
    to_image = jnp.where(lane < POS, shared, second)
    key_first = jnp.where(own_lanes(parity, rows), k, marks_own)
    q_text = jnp.concatenate([first, second], axis=1)
    q_image = jnp.concatenate([first, to_image], axis=1)
    k_text = jnp.concatenate([key_first[:TEXT], shared[:TEXT]], axis=1)
    k_image = jnp.concatenate([key_first[TEXT:], key_image], axis=1)
    return q_text, q_image, k_text, k_image


def near(start, size):
    if start >= TEXT:
        return slice(0, TEXT)
    return slice(max(0, start - LANES), min(TEXT, start + size + LANES))


def image_bias(table_row, offsets):
    return jnp.concatenate(
        [looked_up(table_row, offsets[:, :LANES]), looked_up(table_row, offsets[:, LANES:])], axis=1
    )


def forward_kernel(
    meta_ref, rows_ref, table_ref, q_ref, k_ref, v_ref,
    mixed_ref, log_ref, first_ref, second_ref, key_image_ref, bias_ref,
    even_ref, odd_ref, shared_ref, bar_ref, index_even, index_odd, index_shared, key_index_ref,
):
    mark_refs = (even_ref, odd_ref, shared_ref)
    index_refs = (index_even, index_odd, index_shared)

    @pl.when(pl.program_id(0) == 0)
    def _():
        prepare(meta_ref, mark_refs, bar_ref, index_refs, key_index_ref)

    rows = q_ref.shape[0]
    images = rows - TEXT
    q, k, v = q_ref[...], k_ref[...], v_ref[...]
    offsets = bucket(rows_ref[2:3, TEXT:] - meta_ref[TEXT:, 2:3])
    tile = 256
    v_turned = transposed(v)
    heads = [None, None]

    def prepared(parity):
        table_row = table_ref[pl.ds(2 * pl.program_id(0) + parity, 1), :]
        first, second, key_image = widened(
            parity, q, table_row, bar_ref, index_refs, key_index_ref, shared_ref
        )
        bias = image_bias(table_row, offsets)
        first_ref[parity] = first
        second_ref[parity] = second
        key_image_ref[parity] = key_image
        bias_ref[parity] = bias.astype(BF)
        wide = joined(
            parity, first, second, key_image, k, mark_refs[parity][...], shared_ref[...]
        )
        heads[parity] = wide + (bias,)

    def scored(parity, start):
        q_text, q_image, k_text, k_image, bias = heads[parity]
        here = slice(start, start + tile)
        on_image = dot_nt(k_image, q_image[here])
        if start >= TEXT:
            on_image = on_image + bias[:, start - TEXT : start - TEXT + tile]
        return dot_nt(k_text[near(start, tile)], q_text[here]), on_image

    spots = [(parity, start) for parity in range(2) for start in range(0, rows, tile)]
    outs = ([], [])
    prepared(0)
    following = scored(*spots[0])
    for index, (parity, start) in enumerate(spots):
        on_text, on_image = following
        if index == 1:
            prepared(1)
        if index + 1 < len(spots):
            following = scored(*spots[index + 1])
        top = jnp.maximum(
            jnp.max(on_text, axis=0, keepdims=True), jnp.max(on_image, axis=0, keepdims=True)
        )
        on_text = jnp.exp(on_text - top)
        on_image = jnp.exp(on_image - top)
        total = jnp.sum(on_text, axis=0, keepdims=True) + jnp.sum(on_image, axis=0, keepdims=True)
        own = slice(parity * HEAD, parity * HEAD + HEAD)
        out = dot_nn(v_turned[own, near(start, tile)], on_text.astype(BF)) + dot_nn(
            v_turned[own, TEXT:], on_image.astype(BF)
        )
        outs[parity].append(out * (1.0 / total))
        log_ref[0, parity : parity + 1, start : start + tile] = top + jnp.log(total)
    mixed_ref[...] = jnp.transpose(
        jnp.concatenate([jnp.concatenate(outs[parity], axis=1) for parity in range(2)], axis=0)
    )


def static_scratch(rows):
    return [
        pltpu.VMEM((rows, LANES), BF),
        pltpu.VMEM((rows, LANES), BF),
        pltpu.VMEM((rows, LANES), BF),
        pltpu.VMEM((rows, LANES), F32),
        pltpu.VMEM((rows, LANES), jnp.int32),
        pltpu.VMEM((rows, LANES), jnp.int32),
        pltpu.VMEM((rows, LANES), jnp.int32),
        pltpu.VMEM((rows - TEXT, LANES), jnp.int32),
    ]


def attention_forward(meta_columns, meta_rows, table_rows, projected, width):
    rows = projected.shape[0]
    images = rows - TEXT
    pairs = width // LANES

    def block(part):
        return pl.BlockSpec((rows, LANES), lambda p: (0, part * pairs + p))

    whole = lambda shape: pl.BlockSpec(shape, lambda p: (0,) * len(shape))
    return pl.pallas_call(
        forward_kernel,
        grid=(pairs,),
        in_specs=[
            whole(meta_columns.shape),
            whole(meta_rows.shape),
            whole(table_rows.shape),
            block(0), block(1), block(2),
        ],
        out_specs=[
            pl.BlockSpec((rows, LANES), lambda p: (0, p)),
            pl.BlockSpec((1, 2, rows), lambda p: (p, 0, 0)),
            pl.BlockSpec((2, rows, LANES), lambda p: (p, 0, 0)),
            pl.BlockSpec((2, rows, LANES), lambda p: (p, 0, 0)),
            pl.BlockSpec((2, images, LANES), lambda p: (p, 0, 0)),
            pl.BlockSpec((2, images, images), lambda p: (p, 0, 0)),
        ],
        out_shape=[
            jax.ShapeDtypeStruct((rows, width), F32),
            jax.ShapeDtypeStruct((pairs, 2, rows), F32),
            jax.ShapeDtypeStruct((2 * pairs, rows, LANES), BF),
            jax.ShapeDtypeStruct((2 * pairs, rows, LANES), BF),
            jax.ShapeDtypeStruct((2 * pairs, images, LANES), BF),
            jax.ShapeDtypeStruct((2 * pairs, images, images), BF),
        ],
        scratch_shapes=static_scratch(rows),
        compiler_params=pltpu.CompilerParams(vmem_limit_bytes=60 * 1024 * 1024),
        name="attention_forward",
    )(meta_columns, meta_rows, table_rows, projected, projected, projected)


def skewed(block):
    size = block.shape[0]
    lane = lax.broadcasted_iota(jnp.int32, (size, LANES), 1)
    row = lax.broadcasted_iota(jnp.int32, (size, LANES), 0)
    turned = jnp.take_along_axis(
        block, (lane + row) & (LANES - 1), axis=1, mode="promise_in_bounds"
    )
    straight = lane + row < LANES
    above = jnp.sum(jnp.where(straight, turned, 0.0), axis=0, keepdims=True)
    below = jnp.sum(jnp.where(straight, 0.0, turned), axis=0, keepdims=True)
    return above, below


def transposed(array):
    return jnp.transpose(array.astype(F32)).astype(array.dtype)


def static_prepare(meta_ref, static):
    for ref, turned, value in zip(static[:3], static[3:], marks(meta_ref)):
        ref[...] = value
        turned[...] = transposed(value)


def head_back(
    parity, pair, rows_ref, wide_refs, k_ref, v_ref, mixed_ref, grad_ref, log_ref, static, diag_ref,
):
    mark_refs, turned_refs = static[:3], static[3:]
    first_ref, second_ref, key_image_ref, bias_ref = wide_refs
    head = 2 * pair + parity
    shared_t = turned_refs[2]
    rows = k_ref.shape[1]
    images = rows - TEXT
    tile = 256
    k, v, grad = k_ref[pair], v_ref[pair], grad_ref[pair]
    products = grad.astype(F32) * mixed_ref[pair]
    k_turned = transposed(k)
    is_image = rows_ref[1:2, TEXT:] > 0
    own = own_lanes(parity, rows)
    log_row = log_ref[pair, parity : parity + 1, :]
    first, shared = first_ref[head], mark_refs[2][...]
    q_text, q_image, k_text, k_image = joined(
        parity, first, second_ref[head], key_image_ref[head], k, mark_refs[parity][...], shared
    )
    bias = bias_ref[head].astype(F32)
    ones = jnp.where(own_lanes(parity, 8), 1.0, 0.0).astype(BF)
    delta = jnp.zeros((8, rows), F32)
    rest = products
    for _ in range(3):
        piece = rest.astype(BF)
        delta = delta + dot_nt(ones, piece)
        rest = rest - piece.astype(F32)
    delta = delta[0:1]
    v_own = jnp.where(own, v, jnp.zeros_like(v))
    q_marked = jnp.concatenate(
        [jnp.where(own, first, mark_refs[parity][...]), shared], axis=1
    )
    dq_text = jnp.zeros((HEAD, TEXT), F32)
    dq_image = jnp.zeros((HEAD, images), F32)
    dks = []
    dvs = []
    first_sum = jnp.zeros((LANES, LANES), F32)
    second_sum = jnp.zeros((LANES, LANES), F32)
    text_image = jnp.zeros((LANES, images), F32)

    def met(start, array, axis=0):
        text = near(start, tile)
        if axis == 0:
            return jnp.concatenate([array[text], array[TEXT:]], axis=0)
        return jnp.concatenate([array[:, text], array[:, TEXT:]], axis=1)

    def scored(start):
        here = slice(start, start + tile)
        if start < TEXT:
            scores = dot_nt(k_text[here], met(start, q_text))
        else:
            scores = dot_nt(k_image[start - TEXT : start - TEXT + tile], q_image)
            scores = jnp.concatenate([scores[:, :TEXT], scores[:, TEXT:] + bias], axis=1)
        return scores, dot_nt(v_own[here], met(start, grad))

    following = scored(0)
    for start in range(0, rows, tile):
        here = slice(start, start + tile)
        scores, prob_grad = following
        if start + tile < rows:
            following = scored(start + tile)
        soft = jnp.exp(scores - met(start, log_row, 1))
        score_grad = soft * (prob_grad - met(start, delta, 1))
        low = score_grad.astype(BF)
        dvs.append(dot_nn(soft.astype(BF), met(start, grad)))
        wide = dot_nn(low, met(start, q_marked))
        dks.append(wide[:, :LANES])
        part = dot_nn(k_turned[parity * HEAD : parity * HEAD + HEAD, here], low)
        text = near(start, tile)
        count = text.stop - text.start
        before = [jnp.zeros((HEAD, text.start), F32)] if text.start > 0 else []
        after = [jnp.zeros((HEAD, TEXT - text.stop), F32)] if text.stop < TEXT else []
        dq_text = dq_text + jnp.concatenate(before + [part[:, :count]] + after, axis=1)
        dq_image = dq_image + part[:, count:]
        rounded = wide.astype(BF)
        first_sum = first_sum + dot_nn(turned_refs[parity][:, here], rounded[:, :LANES])
        second_sum = second_sum + dot_nn(shared_t[:, here], rounded[:, LANES:])
        if start < TEXT:
            text_image = text_image + dot_nn(shared_t[:, here], low[:, count:])
        else:
            by_position = wide[:, LANES:]
            on_image = score_grad[:, TEXT:]
    dq = jnp.concatenate([dq_text, dq_image], axis=1)
    small = lax.broadcasted_iota(jnp.int32, (LANES, LANES), 1)
    small_row = lax.broadcasted_iota(jnp.int32, (LANES, LANES), 0)
    x0 = HEAD if parity == 0 else 0
    x_block = jnp.where(
        between(small, x0, x0 + COORD) & between(small_row, x0, x0 + COORD), first_sum, 0.0
    )
    y_block = jnp.where(
        between(small, Y0, Y0 + COORD) & between(small_row, Y0, Y0 + COORD), second_sum, 0.0
    )
    p_block = jnp.where((small < POS) & (small_row < POS), second_sum, 0.0)
    wide_lane = lax.broadcasted_iota(jnp.int32, (images, images), 1)
    outside = jnp.sum(jnp.where(is_image, 0.0, on_image), axis=1, keepdims=True)
    pairs = jnp.where(is_image, on_image, 0.0) + jnp.where(wide_lane == 0, outside, 0.0)
    outside_text = jnp.sum(jnp.where(is_image, 0.0, text_image), axis=1, keepdims=True)
    text_lane = lax.broadcasted_iota(jnp.int32, (LANES, images), 1)
    text_row = lax.broadcasted_iota(jnp.int32, (LANES, images), 0)
    text_image = jnp.where(is_image, text_image, 0.0) + jnp.where(
        text_lane == 0, outside_text, 0.0
    )
    text_image = jnp.where(text_row < POS, text_image, 0.0)
    first_lane = lax.broadcasted_iota(jnp.int32, (images, LANES), 1)
    left = pairs[:, :LANES] + jnp.where(first_lane < POS, by_position, 0.0)
    right = pairs[:, LANES:]
    a00, b00 = skewed(left[:LANES] + text_image[:, :LANES] + p_block)
    a01, b01 = skewed(right[:LANES] + text_image[:, LANES:])
    a10, b10 = skewed(left[LANES:])
    a11, b11 = skewed(right[LANES:])
    ax, bx = skewed(x_block)
    ay, by = skewed(y_block)
    diag_ref[head] = jnp.concatenate(
        [b10, b00 + b11 + a10, a00 + a11 + b01, a01, bx, ax, by, ay], axis=0
    )
    return dq * 0.125, jnp.concatenate(dks, axis=0), jnp.concatenate(dvs, axis=0)


MESH = pl.DeviceIdType.MESH
VMEM = pl.BlockSpec(memory_space=pltpu.VMEM)
HBM = pl.BlockSpec(memory_space=pltpu.HBM)
MIB = 1024 * 1024


def remote(src, dst, send, receive, device):
    return pltpu.make_async_remote_copy(
        src_ref=src, dst_ref=dst, send_sem=send, recv_sem=receive, device_id=device,
        device_id_type=MESH,
    )


def project_kernel(
    layer_ref, weight_hbm, *refs,
):
    small_hbm, refs = refs[:10], refs[10:]
    (item_ref, projected_out, columns_ref, rows_ref, table_ref,
     projected_ref, weight_ref, meta_send, bias_ref, sems, load_sems, store_sems), small = (
        refs[:12], refs[12:],
    )
    (segment_ref, mask_ref, position_ref, across_ref, down_ref, query_bias_ref, value_bias_ref,
     text_ref, horiz_ref, vert_ref) = small
    mine = lax.axis_index("seq")
    partner = (1 - mine, lax.axis_index("dp"))
    count, width = layer_ref.shape[1:]
    own = pl.ds(pl.multiple_of(mine * count, LANES), count)
    loads = [
        pltpu.make_async_copy(source, target, load_sems.at[index])
        for index, (source, target) in enumerate(
            list(zip(small_hbm, small))
            + [(layer_ref.at[mine], item_ref.at[own]), (weight_hbm, weight_ref)]
        )
    ]
    for load in loads:
        load.start()
    barrier = pltpu.get_barrier_semaphore()
    pl.semaphore_signal(barrier, inc=1, device_id=partner, device_id_type=MESH)
    pl.semaphore_wait(barrier, 1)
    pieces = count // LANES
    rows_out = [
        remote(
            layer_ref.at[1 - mine, pl.ds(piece * LANES, LANES)],
            item_ref.at[pl.ds(pl.multiple_of(mine * count + piece * LANES, LANES), LANES)],
            sems.at[0, piece], sems.at[1, piece], partner,
        )
        for piece in range(pieces)
    ]
    for copy in rows_out:
        copy.start()
    for load in loads[:-2]:
        load.wait()

    fields = (segment_ref, mask_ref, position_ref, across_ref, down_ref)
    blocks = [
        jnp.concatenate(
            [field[item : item + 1, :] for field in fields] + [jnp.zeros((3, count), jnp.int32)],
            axis=0,
        )
        for item in range(2)
    ]
    meta_send[...] = jnp.where(mine == 0, blocks[1], blocks[0])
    meta_out = remote(
        meta_send, rows_ref.at[:, own], sems.at[0, pieces], sems.at[1, pieces], partner
    )
    meta_out.start()
    rows_ref[:, own] = jnp.where(mine == 0, blocks[0], blocks[1])
    bias_ref[:, :width] = query_bias_ref[...].astype(F32).reshape(1, width)
    bias_ref[:, width : 2 * width] = jnp.zeros((1, width), F32)
    bias_ref[:, 2 * width :] = value_bias_ref[...].astype(F32).reshape(1, width)
    heads, levels = text_ref.shape
    spot = lax.broadcasted_iota(jnp.int32, (levels, LANES), 1)
    level = lax.broadcasted_iota(jnp.int32, (levels, LANES), 0)
    table = jnp.zeros((heads, LANES), F32)
    for source, begin in ((text_ref, 0), (horiz_ref, X_TABLE), (vert_ref, Y_TABLE)):
        table = table + dot_nn(source[...], (spot == level + begin).astype(BF))
    table_ref[...] = jnp.concatenate([table, jnp.zeros((16 - heads, LANES), F32)], axis=0)

    def project(there):
        step = 256

        def body(index, carry):
            columns = pl.ds(pl.multiple_of(index * step, step), step)
            product = dot_nn(item_ref[there], weight_ref[:, columns])
            projected_ref[there, columns] = (product + bias_ref[:, columns]).astype(BF)
            return carry

        lax.fori_loop(0, 3 * width // step, body, 0)

    def stored(index, there):
        return pltpu.make_async_copy(
            projected_ref.at[there], projected_out.at[there], store_sems.at[index]
        )

    for load in loads[-2:]:
        load.wait()
    project(own)
    stored(0, own).start()
    for piece in range(pieces):
        rows_out[piece].wait()
        there = pl.ds(pl.multiple_of((1 - mine) * count + piece * LANES, LANES), LANES)
        project(there)
        stored(1 + piece, there).start()
    meta_out.wait()
    meta = rows_ref[...].astype(F32)
    tall = jnp.concatenate([meta, jnp.zeros((LANES - 8, meta.shape[1]), F32)], axis=0)
    columns_ref[...] = jnp.transpose(tall).astype(jnp.int32)
    stored(0, own).wait()
    for piece in range(pieces):
        there = pl.ds(pl.multiple_of((1 - mine) * count + piece * LANES, LANES), LANES)
        stored(1 + piece, there).wait()


def projected_item(layer_in, fields, qkv_weight, query_bias, value_bias, tables):
    rows = 2 * layer_in.shape[1]
    width = layer_in.shape[2]
    pieces = rows // 2 // LANES
    small = list(fields) + [query_bias, value_bias] + [t.T for t in tables]
    return pl.pallas_call(
        project_kernel,
        in_specs=[HBM] * (2 + len(small)),
        out_specs=[VMEM, HBM, VMEM, VMEM, VMEM],
        out_shape=[
            jax.ShapeDtypeStruct((rows, width), BF),
            jax.ShapeDtypeStruct((rows, 3 * width), BF),
            jax.ShapeDtypeStruct((rows, LANES), jnp.int32),
            jax.ShapeDtypeStruct((8, rows), jnp.int32),
            jax.ShapeDtypeStruct((16, LANES), F32),
        ],
        scratch_shapes=[
            pltpu.VMEM((rows, 3 * width), BF),
            pltpu.VMEM((width, 3 * width), BF),
            pltpu.VMEM((8, rows // 2), jnp.int32),
            pltpu.VMEM((1, 3 * width), F32),
            pltpu.SemaphoreType.DMA((2, pieces + 1)),
            pltpu.SemaphoreType.DMA((len(small) + 2,)),
            pltpu.SemaphoreType.DMA((pieces + 1,)),
        ]
        + [pltpu.VMEM(array.shape, array.dtype) for array in small],
        compiler_params=pltpu.CompilerParams(
            collective_id=1, has_side_effects=True, vmem_limit_bytes=60 * MIB
        ),
        name="projected_item",
    )(layer_in, qkv_weight, *small)


EPSILON = 1e-05
TILE = 256


def vector(ref):
    return ref[...].astype(F32).reshape(1, ref.shape[0])


def gelu_and_slope(x):
    bell = jnp.exp2(-0.7213475204444817 * (x * x))
    rough = 1.0 + 0.23164188826 * jnp.abs(x)
    t = pl.reciprocal(rough, approx=True)
    t = t * (2.0 - rough * t)
    series = t * (
        0.127414796
        + t * (-0.142248368 + t * (0.7107068705 + t * (-0.7265760135 + t * 0.5307027145)))
    )
    tail = bell * series
    below = jnp.where(x >= 0.0, 1.0 - tail, tail)
    return x * below, below + x * (0.3989422804014327 * bell)


def row_mean(block):
    return jnp.mean(block, axis=1, keepdims=True)


def normalized(hidden):
    center = hidden - row_mean(hidden)
    scale = lax.rsqrt(row_mean(center * center) + EPSILON)
    return center * scale, scale


def norm_pulled(grad, unit, scale):
    return scale * (grad - row_mean(grad) - unit * row_mean(grad * unit))


def column_sum(block):
    return jnp.sum(block, axis=0, keepdims=True)


def feed_kernel(
    item_ref, mixed_ref, cotangent_ref, out_weight_ref, up_ref, down_ref, *refs,
):
    vectors_hbm, refs = refs[:7], refs[7:]
    (layer_out, d_hidden_ref, d_mixed_ref, grad_out_ref, grad_down_ref, grad_up_ref, small_ref,
     layer_ref, cotangent_all, active, slope, unit, scale_ref, normed, normed_t, total, d_branch, d_branch_t,
     sems, load_sems) = refs[:20]
    vectors = refs[20:]
    (out_bias_ref, attn_gain_ref, attn_shift_ref, up_bias_ref, down_bias_ref, ffn_gain_ref,
     ffn_shift_ref) = vectors
    step = pl.program_id(0)
    blocks = pl.num_programs(0) // 2
    rows, width = item_ref.shape
    count = rows // 2
    mine = lax.axis_index("seq")
    partner = (1 - mine, lax.axis_index("dp"))
    own = pl.ds(pl.multiple_of(mine * count, LANES), count)
    tiles = rows // TILE

    def sent():
        return remote(
            cotangent_ref.at[1 - mine], cotangent_all.at[own], sems.at[0], sems.at[1], partner
        )

    def returned():
        theirs = pl.ds(pl.multiple_of((1 - mine) * count, LANES), count)
        return [
            pltpu.make_async_copy(layer_ref.at[own], layer_out.at[mine], load_sems.at[8]),
            remote(
                layer_ref.at[theirs], layer_out.at[mine], sems.at[2], sems.at[3], partner
            ),
        ]

    def loads():
        copies = list(zip(vectors_hbm, vectors)) + [(cotangent_ref.at[mine], cotangent_all.at[own])]
        return [
            pltpu.make_async_copy(source, target, load_sems.at[index])
            for index, (source, target) in enumerate(copies)
        ]

    def over_tiles(size, body, carry, unroll=1):
        def run(index, state):
            return body(pl.ds(pl.multiple_of(index * size, size), size), state)

        return lax.fori_loop(0, rows // size, run, carry, unroll=unroll)

    @pl.when(step == 0)
    def _():
        for load in loads():
            load.start()
        barrier = pltpu.get_barrier_semaphore()
        pl.semaphore_signal(barrier, inc=1, device_id=partner, device_id_type=MESH)
        pl.semaphore_wait(barrier, 1)
        sent().start()
        small_ref[...] = jnp.zeros_like(small_ref)
        for load in loads():
            load.wait()
        out_bias, gain, shift = vector(out_bias_ref), vector(attn_gain_ref), vector(attn_shift_ref)

        def tile(there, carry):
            attn = dot_nn(mixed_ref[there].astype(BF), out_weight_ref[...]) + out_bias
            standard, scale = normalized(item_ref[there].astype(F32) + attn)
            unit[there] = standard
            scale_ref[there] = jnp.broadcast_to(scale, (scale.shape[0], LANES))
            result = standard * gain + shift
            normed[there] = result.astype(BF)
            normed_t[:, there] = jnp.transpose(result).astype(BF)
            return carry

        over_tiles(TILE, tile, 0, 3)
        total[...] = jnp.zeros_like(total)

    @pl.when(step < blocks)
    def _():
        columns = [slice(begin, begin + TILE) for begin in range(0, width, TILE)]
        low = normed[...]
        following = dot_nn(low, up_ref[:, columns[0]])
        values = []
        for index, here in enumerate(columns):
            product = following
            if index + 1 < len(columns):
                following = dot_nn(low, up_ref[:, columns[index + 1]])
            bias = up_bias_ref[pl.ds(pl.multiple_of(step * width + here.start, LANES), TILE)]
            value, grade = gelu_and_slope(product + bias.astype(F32).reshape(1, TILE))
            values.append(value.astype(BF))
            active[step, :, here] = values[-1]
            slope[step, :, here] = grade.astype(BF)
        values = jnp.concatenate(values, axis=1)
        for here in columns:
            total[:, here] += dot_nn(values, down_ref[:, here])

    @pl.when(step == blocks)
    def _():
        sent().wait()
        gain, shift, bias = vector(ffn_gain_ref), vector(ffn_shift_ref), vector(down_bias_ref)
        first_gain, first_shift = vector(attn_gain_ref), vector(attn_shift_ref)

        def tile(there, sums):
            hidden = unit[there] * first_gain + first_shift + (total[there] + bias)
            standard, scale = normalized(hidden)
            layer_ref[there] = (standard * gain + shift).astype(BF)
            cotangent = cotangent_all[there].astype(F32)
            pulled = norm_pulled(cotangent * gain, standard, scale)
            total[there] = pulled
            low = pulled.astype(BF)
            d_branch[there] = low
            return (
                sums[0] + column_sum(low.astype(F32)),
                sums[1] + column_sum(cotangent * standard),
                sums[2] + column_sum(cotangent),
            )

        zero = jnp.zeros((1, width), F32)
        sums = over_tiles(64, tile, (zero, zero, zero), 4)
        for row, value in zip((5, 6, 7), sums):
            small_ref[row : row + 1] = value

        for copy in returned():
            copy.start()

        def turn(there, carry):
            d_branch_t[:, there] = jnp.transpose(d_branch[there].astype(F32)).astype(BF)
            return carry

        over_tiles(TILE, turn, 0, 3)

    @pl.when(step >= blocks)
    def _():
        block = step - blocks

        columns = [slice(begin, begin + TILE) for begin in range(0, width, TILE)]
        branch = d_branch[...]
        turned = d_branch_t[...]
        following = dot_nt(branch, down_ref[columns[0]])
        values = []
        for index, here in enumerate(columns):
            product = following
            if index + 1 < len(columns):
                following = dot_nt(branch, down_ref[columns[index + 1]])
            grad_down_ref[:, here] = dot_nn(turned, active[block, :, here]).astype(BF)
            d_up = (product * slope[block, :, here].astype(F32)).astype(BF)
            small_ref[pl.ds(8 + block, 1), here] = column_sum(d_up.astype(F32))
            values.append(d_up)
        values = jnp.concatenate(values, axis=1)
        turned = normed_t[...]
        for here in columns:
            grad_up_ref[:, here] = dot_nn(turned, values[:, here]).astype(BF)
            total[:, here] += dot_nt(values, up_ref[here])

    @pl.when(step == 2 * blocks - 1)
    def _():
        gain = vector(attn_gain_ref)

        def tile(there, sums):
            d_normed = total[there]
            standard = unit[there]
            d_hidden = norm_pulled(d_normed * gain, standard, scale_ref[there, :1])
            d_hidden_ref[there] = d_hidden
            low = d_hidden.astype(BF)
            d_branch[there] = low
            return (
                sums[0] + column_sum(low.astype(F32)),
                sums[1] + column_sum(d_normed * standard),
                sums[2] + column_sum(d_normed),
            )

        zero = jnp.zeros((1, width), F32)
        sums = over_tiles(64, tile, (zero, zero, zero), 4)
        for row, value in zip((2, 3, 4), sums):
            small_ref[row : row + 1] = value

        def turn(there, carry):
            normed_t[:, there] = jnp.transpose(mixed_ref[there]).astype(BF)
            return carry

        over_tiles(TILE, turn, 0, 3)

        for begin in range(0, width, TILE):
            here = slice(begin, begin + TILE)
            d_mixed_ref[:, here] = dot_nt(d_branch[...], out_weight_ref[here]).astype(BF)
            grad_out_ref[:, here] = dot_nn(normed_t[...], d_branch[:, here]).astype(BF)

        for copy in returned():
            copy.wait()


def fed_forward_and_back(
    item, mixed, cotangent, out_weight, up_weight, down_weight, vectors,
):
    rows, width = item.shape
    blocks = up_weight.shape[1] // width
    whole = pl.BlockSpec(memory_space=pltpu.VMEM)
    square = lambda kind: jax.ShapeDtypeStruct((rows, width), kind)
    later = lambda i: jnp.maximum(i - blocks, 0)
    return pl.pallas_call(
        feed_kernel,
        grid=(2 * blocks,),
        in_specs=[whole, whole, HBM, whole]
        + [
            pl.BlockSpec((width, width), lambda i: (0, lax.rem(i, blocks))),
            pl.BlockSpec((width, width), lambda i: (lax.rem(i, blocks), 0)),
        ]
        + [HBM] * 7,
        out_specs=[HBM] + [whole] * 3
        + [
            pl.BlockSpec((width, width), lambda i: (later(i), 0)),
            pl.BlockSpec((width, width), lambda i: (later(i), 0)),
            whole,
        ],
        out_shape=[
            jax.ShapeDtypeStruct((2, rows // 2, width), BF), square(F32), square(BF),
            jax.ShapeDtypeStruct((width, width), BF),
            jax.ShapeDtypeStruct((blocks * width, width), BF),
            jax.ShapeDtypeStruct((blocks * width, width), BF),
            jax.ShapeDtypeStruct((16, width), F32),
        ],
        scratch_shapes=[
            pltpu.VMEM((rows, width), BF),
            pltpu.VMEM((rows, width), BF),
            pltpu.VMEM((blocks, rows, width), BF),
            pltpu.VMEM((blocks, rows, width), BF),
            pltpu.VMEM((rows, width), F32),
            pltpu.VMEM((rows, LANES), F32),
            pltpu.VMEM((rows, width), BF),
            pltpu.VMEM((width, rows), BF),
            pltpu.VMEM((rows, width), F32),
            pltpu.VMEM((rows, width), BF),
            pltpu.VMEM((width, rows), BF),
            pltpu.SemaphoreType.DMA((4,)),
            pltpu.SemaphoreType.DMA((9,)),
        ]
        + [pltpu.VMEM(vector.shape, vector.dtype) for vector in vectors],
        compiler_params=pltpu.CompilerParams(
            collective_id=2, has_side_effects=True, vmem_limit_bytes=60 * MIB
        ),
        name="feed_forward",
    )(item, mixed, cotangent, out_weight, up_weight, down_weight, *vectors)


SLOTS = 4


def finish_kernel(
    main_ref, tail_ref, input_hbm, small_ref, diagonal_ref,
    down_ref, up_ref, out_ref, qkv_ref, input_ref, *refs,
):
    singles, (main_in, tail_in, slots, input_in, input_slot, in_sems, out_sems, item_sems) = (
        refs[:12], refs[12:],
    )
    mains, width = main_in.shape[0], main_in.shape[2]
    pairs, across = tail_in.shape[0], tail_in.shape[2]
    hidden = mains // 2
    blocks = mains + pairs

    def load(block):
        if block < mains:
            source, target = main_ref.at[pl.ds(block * width, width)], main_in.at[block]
        else:
            pair = block - mains
            source, target = tail_ref.at[pl.ds(pair * TAIL_ROWS, TAIL_ROWS)], tail_in.at[pair]
        return pltpu.make_async_copy(source, target, in_sems.at[block])

    def stores(block):
        slot, sem = slots.at[block % SLOTS], out_sems.at[block % SLOTS]
        if block < hidden:
            targets = [(slot, down_ref.at[pl.ds(block * width, width)])]
        elif block < mains:
            targets = [(slot, up_ref.at[:, pl.ds((block - hidden) * width, width)])]
        else:
            pair = block - mains
            targets = [
                (
                    slot.at[:, pl.ds(part * LANES, LANES)],
                    qkv_ref.at[:, pl.ds(part * width + pair * LANES, LANES)],
                )
                for part in range(3)
            ]
            down = pl.ds(0, TAIL_ROWS - width)
            targets.append(
                (slot.at[down, pl.ds(across, across)], out_ref.at[out_spot(pair, pairs, width)])
            )
        return [
            pltpu.make_async_copy(source, target, sem.at[index])
            for index, (source, target) in enumerate(targets)
        ]

    load_input = pltpu.make_async_copy(input_hbm, input_in, item_sems.at[0])
    store_input = pltpu.make_async_copy(input_slot, input_ref, item_sems.at[1])
    for block in range(blocks):
        load(block).start()
    load_input.start()
    for block in range(blocks):
        load(block).wait()
        if block >= SLOTS:
            for copy in stores(block - SLOTS):
                copy.wait()
        slot = block % SLOTS
        if block < hidden:
            slots[slot] = jnp.transpose(main_in[block].astype(F32))
        elif block < mains:
            slots[slot] = main_in[block].astype(F32)
        else:
            slots[slot, :, :across] = tail_in[block - mains, :width].astype(F32)
            slots[slot, : TAIL_ROWS - width, across:] = tail_in[block - mains, width:].astype(F32)
        for copy in stores(block):
            copy.start()
    load_input.wait()
    input_slot[...] = input_in[...].astype(F32)
    store_input.start()
    for row in range(8):
        singles[row][...] = small_ref[row]
    for row in range(hidden):
        singles[8][row * width : row * width + width] = small_ref[8 + row]
    heads, levels = singles[9].shape
    diagonals = diagonal_ref[...]
    level = lax.broadcasted_iota(jnp.int32, (LANES, LANES), 1)
    lane = lax.broadcasted_iota(jnp.int32, (LANES, LANES), 0)
    for table, (first, size, skip) in enumerate(((0, 4, 0), (4, 2, 1), (6, 2, 1))):
        total = jnp.zeros((heads, LANES), F32)
        for row in range(size):
            distance = lane + LANES * (row + skip - 2)
            chosen = (bucket(distance) == level).astype(F32)
            total = total + jnp.dot(
                diagonals[:, first + row, :], chosen, preferred_element_type=F32,
                precision=lax.Precision.HIGHEST,
            )
        singles[9 + table][...] = total[:, :levels]
    for block in range(blocks - SLOTS, blocks):
        for copy in stores(block):
            copy.wait()
    store_input.wait()


def finished(main, tail, grad_input, small, diagonals, hidden, levels):
    width = main.shape[1]
    heads = diagonals.shape[0]
    mains = main.shape[0] // width
    pairs = tail.shape[0] // TAIL_ROWS
    single = jax.ShapeDtypeStruct((width,), F32)
    table = jax.ShapeDtypeStruct((heads, levels), F32)
    dma = pltpu.SemaphoreType.DMA
    return pl.pallas_call(
        finish_kernel,
        in_specs=[HBM, HBM, HBM, VMEM, VMEM],
        out_specs=[HBM] * 5 + [VMEM] * 12,
        out_shape=[
            jax.ShapeDtypeStruct((hidden, width), F32),
            jax.ShapeDtypeStruct((width, hidden), F32),
            jax.ShapeDtypeStruct((width, width), F32),
            jax.ShapeDtypeStruct((width, 3 * width), F32),
            jax.ShapeDtypeStruct(grad_input.shape, F32),
        ]
        + [single] * 8
        + [jax.ShapeDtypeStruct((hidden,), F32)]
        + [table] * 3,
        scratch_shapes=[
            pltpu.VMEM((mains, width, width), BF),
            pltpu.VMEM((pairs, TAIL_ROWS, tail.shape[1]), BF),
            pltpu.VMEM((SLOTS, width, width), F32),
            pltpu.VMEM(grad_input.shape, BF),
            pltpu.VMEM(grad_input.shape, F32),
            dma((mains + pairs,)),
            dma((SLOTS, 4)),
            dma((2,)),
        ],
        compiler_params=pltpu.CompilerParams(vmem_limit_bytes=56 * MIB),
        name="finished",
    )(main, tail, grad_input, small, diagonals)


PIECE = 16


class Place:
    def __init__(self, depth):
        place = lax.axis_index("dp")
        self.depth = depth
        self.group = lax.div(place, 4 * depth)
        self.z = lax.rem(lax.div(place, 4), depth)
        self.bits = {
            "x": lax.axis_index("seq"),
            "c": lax.rem(place, 2),
            "y": lax.rem(lax.div(place, 2), 2),
            "a": lax.rem(self.z, 2),
            "b": lax.div(self.z, 2),
        }

    def partner(self, letters):
        bit = {
            letter: 1 - value if letter in letters else value
            for letter, value in self.bits.items()
        }
        z = self.z
        for letter, reach in (("a", 1), ("b", 2)):
            if letter in letters:
                z = z + reach - 2 * reach * self.bits[letter]
        return (bit["x"], (self.group * self.depth + z) * 4 + bit["y"] * 2 + bit["c"])

    def greet(self, met):
        barrier = pltpu.get_barrier_semaphore()
        for letters in met:
            pl.semaphore_signal(
                barrier, inc=1, device_id=self.partner(letters), device_id_type=MESH
            )
        pl.semaphore_wait(barrier, len(met))


def letters_of(depth):
    return "xy" + "ab"[: (depth - 1).bit_length()]


def parsed(routes, depth):
    kept = letters_of(depth)
    parts = []
    for route in routes.split():
        hops = ["".join(letter for letter in hop if letter in kept) for hop in route.split(".")]
        parts.append([hop for hop in hops if hop])
    return parts


def subsets(hop):
    return [
        "".join(letter for index, letter in enumerate(hop) if mask >> index & 1)
        for mask in range(1, 2 ** len(hop))
    ]


class Chunk:
    def __init__(self, place, depth, source, out_ref, offset, spot, scratch):
        _, self.begin, rows, first, columns, _, routes, _ = spot
        self.place, self.source, self.columns = place, source, pl.ds(first, columns)
        self.out_ref, self.out_begin = out_ref, offset + self.begin
        self.parts = parsed(routes, depth)
        self.half = rows // 2
        self.share = self.half // len(self.parts)
        self.hops = max(len(part) for part in self.parts)
        self.work, self.fresh, *landing, self.sends, self.receives, self.locals = scratch
        self.landing = {}
        self.sems = {}
        count = 2
        for part, hops in enumerate(self.parts):
            for hop, letters in enumerate(hops):
                self.landing[part, hop] = landing.pop(0)
                for way in range(2):
                    for index in range(2 ** len(letters) - 1):
                        self.sems[way, part, hop, index] = count
                        count += 1

    def aligned(self, value):
        return pl.multiple_of(value, PIECE)

    def size(self, part, hop):
        return self.share >> sum(len(letters) for letters in self.parts[part][: hop + 1])

    def spot(self, part, hop, other=""):
        start = part * self.share
        for level in range(hop + 1):
            for index, letter in enumerate(self.parts[part][level]):
                bit = self.place.bits[letter]
                if level == hop and letter in other:
                    bit = 1 - bit
                start = start + bit * (self.size(part, level) << index)
        return start

    def out(self, core):
        begin = self.aligned(self.out_begin + core * self.half)
        return self.out_ref.at[pl.ds(begin, self.half), self.columns]

    def held(self, buffer, begin, size):
        return buffer.at[pl.ds(self.aligned(begin), size)]

    def copy(self, index, source, target, letters):
        return remote(
            source, target, self.sends.at[index], self.receives.at[index],
            self.place.partner(letters),
        )

    def pair_down(self):
        core = self.place.bits["c"]
        at = lambda c: self.source.at[
            pl.ds(self.aligned(self.begin + c * self.half), self.half), self.columns
        ]
        return [
            self.copy(0, at(1 - core), self.fresh, "c"),
            pltpu.make_async_copy(at(core), self.work, self.locals.at[0]),
        ]

    def pair_up(self, arriving):
        core = self.place.bits["c"]
        return [
            self.copy(1, self.fresh, self.out(1 - core if arriving else core), "c"),
            pltpu.make_async_copy(self.fresh, self.out(core), self.locals.at[1]),
        ]

    def at_hop(self, hop):
        return [
            (part, hops[hop]) for part, hops in enumerate(self.parts) if hop < len(hops)
        ]

    def down(self, hop):
        copies = []
        for part, letters in self.at_hop(hop):
            size = self.size(part, hop)
            for index, other in enumerate(subsets(letters)):
                copies.append(
                    self.copy(
                        self.sems[0, part, hop, index],
                        self.held(self.work, self.spot(part, hop, other), size),
                        self.landing[part, hop].at[index], other,
                    )
                )
        return copies

    def up(self, hop, arriving):
        copies = []
        for part, letters in self.at_hop(hop):
            mine = self.spot(part, hop)
            size = self.size(part, hop)
            for index, other in enumerate(subsets(letters)):
                target = self.spot(part, hop, other) if arriving else mine
                copies.append(
                    self.copy(
                        self.sems[1, part, hop, index], self.held(self.fresh, mine, size),
                        self.held(self.fresh, target, size), other,
                    )
                )
        return copies

    def add(self, begin, sources, size):
        step = 64 if size % 64 == 0 else 32 if size % 32 == 0 else PIECE

        def body(index, carry):
            offset = self.aligned(index * step)
            there = pl.ds(self.aligned(begin + offset), step)
            total = self.work[there]
            if len(sources) == 1:
                total = total + sources[0][pl.ds(offset, step)]
            else:
                total = total.astype(F32)
                for source in sources:
                    total = total + source[pl.ds(offset, step)].astype(F32)
            self.work[there] = total.astype(BF)
            return carry

        lax.fori_loop(0, size // step, body, 0)

    def stage(self, number):
        hops = self.hops
        ended, started = [], []
        if number == 0:
            started = self.pair_down()
        elif number == 1:
            ended = self.pair_down()
            started = self.down(0)
        elif number <= hops:
            ended = self.down(number - 2)
            started = self.down(number - 1)
        elif number == hops + 1:
            ended = self.down(hops - 1)
            started = self.up(hops - 1, False)
        elif number <= 2 * hops:
            level = 2 * hops + 1 - number
            ended = self.up(level, True)
            started = self.up(level - 1, False)
        elif number == 2 * hops + 1:
            ended = self.up(0, True)
            started = self.pair_up(False)
        else:
            ended = self.pair_up(True)
        for copy in ended:
            copy.wait()
        if number == 1:
            self.add(0, [self.fresh], self.half)
        elif 2 <= number <= hops + 1:
            hop = number - 2
            for part, letters in self.at_hop(hop):
                landing = self.landing[part, hop]
                sources = [landing.at[index] for index in range(2 ** len(letters) - 1)]
                self.add(self.spot(part, hop), sources, self.size(part, hop))
        if number == hops + 1:
            for part, route in enumerate(self.parts):
                last = len(route) - 1
                there = pl.ds(self.aligned(self.spot(part, last)), self.size(part, last))
                self.fresh[there] = self.work[there]
        for copy in started:
            copy.start()


def chunk_scratch(spot, depth):
    _, _, rows, _, columns, _, routes, _ = spot
    parts = parsed(routes, depth)
    landing = []
    copies = 2
    for hops in parts:
        size = rows // 2 // len(parts)
        for letters in hops:
            size >>= len(letters)
            others = 2 ** len(letters) - 1
            copies += 2 * others
            landing.append(pltpu.VMEM((others, size, columns), BF))
    dma = pltpu.SemaphoreType.DMA
    return (
        [pltpu.VMEM((rows // 2, columns), BF)] * 2
        + landing
        + [dma((copies,)), dma((copies,)), dma((2,))]
    )


def loads_of(hop, size):
    if "x" in hop and "y" in hop:
        return [("x", 2 * size), ("y", 2 * size)]
    if hop in ("x", "y"):
        return [(hop, size)]
    if "a" in hop and "b" in hop:
        return [("end", 3 * size), ("middle", 4 * size)]
    return [("end", size), ("middle", 2 * size)] if hop == "b" else [("end", size)]


def planned(chunks, work, depth, hop_count):
    latency, issue, link, pair = 3.5, 0.08, 100e3, 600e3
    free = {}
    now = 3.0
    chains = []
    for rows, columns, need, routes, _ in chunks:
        parts = parsed(routes, depth)
        sizes = [rows // 2 // len(parts)] * len(parts)
        down = []
        for hop in range(max(len(part) for part in parts)):
            loads, copies, added = [], 0, 0
            for index, part in enumerate(parts):
                if hop < len(part):
                    sizes[index] >>= len(part[hop])
                    others = 2 ** len(part[hop]) - 1
                    loads += loads_of(part[hop], sizes[index])
                    copies += others
                    added += sizes[index] * others
            down.append((loads, copies, added, columns))
        first = [([("core", rows // 2)], 1.5, rows // 2, columns)]
        last = [([("core", rows // 2)], 1, 0, columns)]
        chains.append((need, first + down + down[::-1] + last))
    chains.append((len(work), [([("core", 16)], 2, 0, 768)] * hop_count))
    ranks = [chunk[4] for chunk in chunks] + [0]
    position = [0] * len(chains)
    ready = [0.0] * len(chains)
    order = [[] for _ in range(len(work) + 1)]
    done = 0
    while True:
        open_ones = [
            (ranks[i], ready[i], i) for i, (need, chain) in enumerate(chains)
            if position[i] <= len(chain) and need <= done
        ]
        due = [entry for entry in open_ones if entry[1] <= now]
        if not due and done < len(work):
            now += work[done]
            done += 1
            continue
        if not open_ones:
            return order
        _, when, index = min(due) if due else min(open_ones, key=lambda entry: entry[1])
        now = max(now, when)
        chain = chains[index][1]
        stage = position[index]
        order[done].append((index, stage))
        if 0 < stage <= len(chain) // 2:
            now += 1e-6 * chain[stage - 1][2] * chain[stage - 1][3]
        if stage < len(chain):
            loads, copies, _, columns = chain[stage]
            now += issue * copies
            end = now
            for lane, rows in loads:
                rate = pair if lane == "core" else link / 2
                free[lane] = max(now, free.get(lane, 0.0)) + 2 * rows * columns / rate
                end = max(end, free[lane])
            ready[index] = end + latency
        position[index] += 1


def last_kernel(
    depth, plan, orders, counts, *refs,
):
    (meta_ref, rows_ref, projected_hbm, mixed_hbm, grad_hbm, log_ref, first_hbm, second_hbm,
     key_image_hbm, bias_hbm, small_ref, item_hbm, weight_hbm, d_hidden_hbm, grad_down_ref, grad_up_ref,
     grad_out_ref,
     main_out, tail_out, small_out, diagonal_out, input_out,
     *scratch) = refs
    static, scratch = scratch[:6], scratch[6:]
    (k_ref, v_ref, mixed_ref, grad_ref, first_ref, second_ref, key_image_ref, bias_ref, pair_sems,
     item_ref, weight_ref, d_hidden_ref, load_sems, d_project, item_t, tail, input_grad,
     small_in, diagonal_in, small_sems, item_sems, *scratch) = scratch
    place = Place(depth)
    step = pl.program_id(0)
    pairs = k_ref.shape[0]
    rows, width = item_hbm.shape
    count = rows // 2
    x = place.bits["x"]
    hidden = grad_down_ref.shape[0]
    sources = ((grad_down_ref, main_out, 0), (grad_up_ref, main_out, hidden), (tail, tail_out, 0))
    chunks = []
    for spot, pieces in zip(plan, counts):
        chunks.append(Chunk(place, depth, *sources[spot[0]], spot, scratch[:pieces]))
        scratch = scratch[pieces:]
    hop_letters = "c" + letters_of(depth)
    wide_hbm = (first_hbm, second_hbm, key_image_hbm, bias_hbm)
    wide_refs = (first_ref, second_ref, key_image_ref, bias_ref)

    def pair_loads(pair):
        copies = []
        held = (
            (projected_hbm, k_ref, width), (projected_hbm, v_ref, 2 * width),
            (mixed_hbm, mixed_ref, 0), (grad_hbm, grad_ref, 0),
        )
        for source, target, first in held:
            columns = pl.ds(pl.multiple_of(first + pair * LANES, LANES), LANES)
            copies.append((source.at[:, columns], target.at[pair]))
        heads = pl.ds(2 * pair, 2)
        for source, target in zip(wide_hbm, wide_refs):
            copies.append((source.at[heads], target.at[heads]))
        return [
            pltpu.make_async_copy(source, target, pair_sems.at[pair, index])
            for index, (source, target) in enumerate(copies)
        ]

    def loads():
        copies = [(item_hbm, item_ref), (weight_hbm, weight_ref), (d_hidden_hbm, d_hidden_ref)]
        for pair in range(pairs):
            down, across = out_spot(pair, pairs, width)
            copies.append(
                (
                    grad_out_ref.at[down, across],
                    tail.at[pl.ds(pair * TAIL_ROWS + width, TAIL_ROWS - width)],
                )
            )
        return [
            pltpu.make_async_copy(source, target, load_sems.at[index])
            for index, (source, target) in enumerate(copies)
        ]

    def input_copies():
        return [
            pltpu.make_async_copy(
                input_grad.at[pl.ds(pl.multiple_of(x * count, LANES), count)], input_out.at[x],
                item_sems.at[0],
            ),
            remote(
                input_grad.at[pl.ds(pl.multiple_of((1 - x) * count, LANES), count)],
                input_out.at[x], item_sems.at[1], item_sems.at[2], place.partner("x"),
            ),
        ]

    def small_copies(hop):
        return [
            remote(source, landing.at[hop], small_sems.at[0, kind, hop],
                   small_sems.at[1, kind, hop], place.partner(hop_letters[hop]))
            for kind, (source, landing) in enumerate(
                ((small_out, small_in), (diagonal_out, diagonal_in))
            )
        ]

    def small_stage(hop):
        if hop > 0:
            for copy in small_copies(hop - 1):
                copy.wait()
            small_out[...] = small_out[...] + small_in[hop - 1]
            diagonal_out[...] = diagonal_out[...] + diagonal_in[hop - 1]
        if hop < len(hop_letters):
            for copy in small_copies(hop):
                copy.start()

    def perform(slot):
        for index, stage in orders[slot]:
            if index == len(chunks):
                small_stage(stage)
            else:
                chunks[index].stage(stage)

    @pl.when(step == 0)
    def _():
        for pair in range(pairs):
            for copy in pair_loads(pair):
                copy.start()
        for copy in loads():
            copy.start()
        met = set(hop_letters)
        for chunk in chunks:
            for hops in chunk.parts:
                for letters in hops:
                    met.update(subsets(letters))
        place.greet(sorted(met))
        small_out[...] = small_ref[...]

    for pair in range(pairs):
        @pl.when(step == pair)
        def _(pair=pair):
            perform(pair)

    @pl.when(step == 0)
    def _():
        static_prepare(meta_ref, static)
        for copy in loads():
            copy.wait()
        for tile in range(rows // TILE):
            there = slice(tile * TILE, tile * TILE + TILE)
            item_t[:, there] = jnp.transpose(item_ref[there].astype(F32)).astype(BF)

    for copy in pair_loads(step):
        copy.wait()
    (dq_even, dk_even, dv_even), (dq_odd, dk_odd, dv_odd) = [
        head_back(
            parity, step, rows_ref, wide_refs, k_ref, v_ref, mixed_ref, grad_ref, log_ref,
            static, diagonal_out,
        )
        for parity in range(2)
    ]
    even = own_lanes(0, rows)
    pieces = [
        jnp.transpose(jnp.concatenate([dq_even, dq_odd], axis=0)).astype(BF),
        jnp.where(even, dk_even, dk_odd).astype(BF),
        jnp.where(even, dv_even, dv_odd).astype(BF),
    ]
    for part, piece in enumerate(pieces):
        d_project[:, pl.ds(pl.multiple_of(part * width + step * LANES, LANES), LANES)] = piece
    slab = pl.ds(pl.multiple_of(step * TAIL_ROWS, TAIL_ROWS), width)
    tail[slab] = dot_nn(item_t[...], jnp.concatenate(pieces, axis=1)).astype(BF)

    @pl.when(step == pairs - 1)
    def _():
        perform(pairs)
        for begin in range(0, width, TILE):
            here = slice(begin, begin + TILE)
            total = d_hidden_ref[:, here] + dot_nt(d_project[...], weight_ref[here])
            input_grad[:, here] = total.astype(BF)
        for copy in input_copies():
            copy.start()
        for begin in range(0, width, TILE):
            here = slice(begin, begin + TILE)
            there = slice(2 * width + begin, 2 * width + begin + TILE)
            small_out[0:1, here] = column_sum(d_project[:, here].astype(F32))
            small_out[1:2, here] = column_sum(d_project[:, there].astype(F32))
        perform(pairs + 1)
        for copy in input_copies():
            copy.wait()


TAIL_ROWS = 1024


def out_spot(pair, pairs, width):
    down = TAIL_ROWS - width
    across = width * width // (pairs * down)
    per_row = width // across
    return (
        pl.ds(pair // per_row * down, down),
        pl.ds(pair % per_row * across, across),
    )


def summed_with_attention_back(
    meta_columns, meta_rows, projected, mixed, d_mixed, logs, wide_arrays, item, qkv_weight,
    d_hidden, small, grad_down, grad_up, grad_out,
):
    size = lax.axis_size("dp")
    depth = 4 if size % 16 == 0 else size // 4
    rows, width = item.shape
    pairs = width // LANES
    hidden = grad_down.shape[0]
    hops = len(letters_of(depth)) + 1
    work = [6.8] * pairs + [4.0]
    tall, wide, slim = 1024, 3 * LANES, 2 * LANES
    plan = [
        (0, 0, 2 * tall, 0, width, 0, "a.b.x.y x.y.a.b", 1),
        (0, 2 * tall, tall, 0, width, 0, "x.a.y.b y.a.b.x", 2),
        (1, 0, 3 * tall, 0, slim, 0, "a.b.x.y y.x.a.b", 4),
        (1, 0, 3 * tall, slim, slim, 0, "y.a.x.b x.y.a.b", 0),
        (1, 0, 3 * tall, 2 * slim, slim, 0, "x.y.a.b y.x.a.b", 2),
        (2, 0, tall, 0, wide, 1, "y.x.a.b a.b.x.y", 3),
        (2, tall, tall, 0, wide, 2, "xy.a.b", 2),
        (2, 2 * tall, tall, 0, wide, 3, "x.y.ab y.ab.x", 3),
        (2, 3 * tall, tall, 0, wide, 4, "xy.a.b", 1),
        (2, 4 * tall, tall, 0, wide, 5, "xy.a.b", 1),
        (2, 5 * tall, tall, 0, wide, 6, "ab.y.x y.ab.x", 2),
    ]
    orders = planned([(spot[2],) + spot[4:] for spot in plan], work, depth, hops)

    whole = pl.BlockSpec(memory_space=pltpu.VMEM)
    diagonals = jax.ShapeDtypeStruct((2 * pairs, 8, LANES), F32)
    dma = pltpu.SemaphoreType.DMA
    scratch = []
    for spot in plan:
        scratch.append(chunk_scratch(spot, depth))
    main, tail, small, diagonals, grad_input = pl.pallas_call(
        functools.partial(last_kernel, depth, plan, orders, [len(pieces) for pieces in scratch]),
        grid=(pairs,),
        in_specs=[whole] * 2 + [HBM] * 3 + [whole] + [HBM] * 4 + [whole] + [HBM] * 6,
        out_specs=[HBM, HBM, whole, whole, HBM],
        out_shape=[
            jax.ShapeDtypeStruct((2 * hidden, width), BF),
            jax.ShapeDtypeStruct((pairs * TAIL_ROWS, 3 * LANES), BF),
            jax.ShapeDtypeStruct(small.shape, F32),
            diagonals,
            jax.ShapeDtypeStruct((2, rows // 2, width), BF),
        ],
        scratch_shapes=[pltpu.VMEM((rows, LANES), BF)] * 3
        + [pltpu.VMEM((LANES, rows), BF)] * 3
        + [pltpu.VMEM((pairs, rows, LANES), kind) for kind in (BF, BF, F32, BF)]
        + [pltpu.VMEM(array.shape, BF) for array in wide_arrays]
        + [
            dma((pairs, 8)),
            pltpu.VMEM((rows, width), BF),
            pltpu.VMEM((width, 3 * width), BF),
            pltpu.VMEM((rows, width), F32),
            dma((3 + pairs,)),
            pltpu.VMEM((rows, 3 * width), BF),
            pltpu.VMEM((width, rows), BF),
            pltpu.VMEM((pairs * TAIL_ROWS, 3 * LANES), BF),
            pltpu.VMEM((rows, width), BF),
            pltpu.VMEM((hops,) + small.shape, F32),
            pltpu.VMEM((hops,) + diagonals.shape, F32),
            dma((2, 2, hops)),
            dma((3,)),
        ]
        + [piece for pieces in scratch for piece in pieces],
        compiler_params=pltpu.CompilerParams(
            collective_id=0, has_side_effects=True, vmem_limit_bytes=62 * MIB
        ),
        name="summed_with_attention_back",
    )(meta_columns, meta_rows, projected, mixed, d_mixed, logs, *wide_arrays,
      small, item, qkv_weight, d_hidden, grad_down, grad_up, grad_out)
    span = 4 * depth
    if size > span:
        groups = [list(range(first, size, span)) for first in range(span)]
        main, tail, small, diagonals = lax.psum(
            (main.astype(F32), tail.astype(F32), small, diagonals), "dp",
            axis_index_groups=groups,
        )
        main, tail = main.astype(BF), tail.astype(BF)
    return main, tail, small, diagonals, grad_input


def per_device(
    layer_in, segment, key_mask, position, layout_x, layout_y,
    qkv_weight, query_bias, value_bias, out_weight, out_bias, attn_gain, attn_shift,
    up_weight, up_bias, down_weight, down_bias, ffn_gain, ffn_shift,
    text_table, horiz_table, vert_table, cotangent,
):
    width = layer_in.shape[-1]
    item, projected, meta_columns, meta_rows, table_rows = projected_item(
        layer_in, (segment, key_mask, position, layout_x, layout_y),
        qkv_weight, query_bias, value_bias, (text_table, horiz_table, vert_table),
    )
    mixed, logs, *wide_arrays = attention_forward(meta_columns, meta_rows, table_rows, projected, width)
    layer_out, d_hidden, d_mixed, grad_out, grad_down, grad_up, small = fed_forward_and_back(
        item, mixed, cotangent, out_weight, up_weight, down_weight,
        (out_bias, attn_gain, attn_shift, up_bias, down_bias, ffn_gain, ffn_shift),
    )
    main, tail, small, diagonals, grad_input = summed_with_attention_back(
        meta_columns, meta_rows, projected, mixed, d_mixed, logs, wide_arrays, item, qkv_weight,
        d_hidden, small, grad_down, grad_up, grad_out,
    )
    done = finished(
        main, tail, grad_input, small, diagonals, up_weight.shape[1], text_table.shape[0]
    )
    sum_down, sum_up, sum_out, sum_qkv, grad_input = done[:5]
    singles, tables = done[5:14], [t.T for t in done[14:]]
    return (
        layer_out, grad_input, sum_qkv, singles[0], singles[1], sum_out, singles[2], singles[3],
        singles[4], sum_up, singles[8], sum_down, singles[5], singles[6], singles[7],
        tables[0], tables[1], tables[2],
    )


def solution(mesh):
    rows = P("dp", "seq", None)
    marks_spec = P("dp", "seq")
    return jax.shard_map(
        per_device,
        mesh=mesh,
        in_specs=(rows,) + (marks_spec,) * 5 + (P(),) * 16 + (rows,),
        out_specs=(rows, rows) + (P(),) * 16,
        check_vma=False,
    )
```

```python
import functools

import jax
import jax.numpy as jnp
from jax import lax
from jax.experimental import pallas as pl
from jax.experimental.pallas import tpu as pltpu
from jax.sharding import PartitionSpec as P

BF = jnp.bfloat16
F32 = jnp.float32
BIG = 1e30
LANES = 128
HEAD = 64
TEXT = 512
POS = 64
COORD = 48
Y0 = 64
GROUP0 = 112
MEMBER0 = 116
FLAG = 124
EVERY = 125
STRAY = 126
X_TABLE = 33
Y_TABLE = 66
NOTHING = 127


def dot_nt(a, b):
    return lax.dot_general(a, b, (((1,), (1,)), ((), ())), preferred_element_type=F32)


def dot_nn(a, b):
    return lax.dot_general(a, b, (((1,), (0,)), ((), ())), preferred_element_type=F32)


def looked_up(table_row, index):
    rows = index.shape[0]
    return jnp.take_along_axis(
        jnp.broadcast_to(table_row, (rows, LANES)), index, axis=1, mode="promise_in_bounds"
    )


def bucket(distance):
    return jnp.clip(distance, -16, 16) + 16


def between(lane, low, high):
    return (lane >= low) & (lane < high)


def columns_of(meta_ref):
    return tuple(meta_ref[:, field : field + 1] for field in range(5))


def marks(meta_ref):
    segment, key_mask, position, across, down = columns_of(meta_ref)
    rows = segment.shape[0]
    lane = lax.broadcasted_iota(jnp.int32, (rows, LANES), 1)
    row = lax.broadcasted_iota(jnp.int32, (rows, LANES), 0)
    even = between(lane, HEAD, HEAD + COORD) & (lane - HEAD == across)
    odd = (lane < COORD) & (lane == across)
    group = (segment - 1) >> 3
    member = (segment - 1) & 7
    named = segment > 0
    shared = (
        ((row < TEXT) & (lane < POS) & (lane == position))
        | (between(lane, Y0, Y0 + COORD) & (lane - Y0 == down))
        | (named & between(lane, GROUP0, MEMBER0) & (lane - GROUP0 == group))
        | (named & between(lane, MEMBER0, FLAG) & (lane - MEMBER0 == member))
        | ((lane == FLAG) & (key_mask <= 0))
        | (lane == EVERY)
        | ((lane == STRAY) & (segment < 0))
    )
    return tuple(jnp.where(m, 1.0, 0.0).astype(BF) for m in (even, odd, shared))


def square_lanes():
    shape = (LANES, LANES)
    return lax.broadcasted_iota(jnp.int32, shape, 0), lax.broadcasted_iota(jnp.int32, shape, 1)


def barred():
    row, lane = square_lanes()
    in_groups = between(lane, GROUP0, MEMBER0)
    shut = (
        (between(row, GROUP0, MEMBER0) & in_groups & (lane != row))
        | (between(row, MEMBER0, FLAG) & between(lane, MEMBER0, FLAG) & (lane != row))
        | ((row == EVERY) & (lane == FLAG))
        | ((row == STRAY) & in_groups)
    )
    return jnp.where(shut, -BIG, 0.0).astype(F32)


def table_index():
    row, lane = square_lanes()
    distance = bucket(row - lane)
    inside = lambda low, high: between(row, low, high) & between(lane, low, high)
    even = jnp.where(inside(HEAD, HEAD + COORD), distance + X_TABLE, NOTHING)
    odd = jnp.where(inside(0, COORD), distance + X_TABLE, NOTHING)
    shared = jnp.where(
        inside(0, POS), distance, jnp.where(inside(Y0, Y0 + COORD), distance + Y_TABLE, NOTHING)
    )
    return even, odd, shared


def image_query_index(meta_ref):
    position = meta_ref[TEXT:, 2:3]
    lane = lax.broadcasted_iota(jnp.int32, (position.shape[0], LANES), 1)
    return jnp.where(lane < POS, bucket(position - lane), NOTHING)


def prepare(meta_ref, mark_refs, bar_ref, index_refs, image_index_ref):
    for ref, value in zip(mark_refs, marks(meta_ref)):
        ref[...] = value
    bar_ref[...] = barred()
    for ref, value in zip(index_refs, table_index()):
        ref[...] = value
    image_index_ref[...] = image_query_index(meta_ref)


def own_lanes(parity, rows):
    lane = lax.broadcasted_iota(jnp.int32, (rows, LANES), 1)
    return (lane < HEAD) if parity == 0 else (lane >= HEAD)


def widened(parity, q, table_row, bias, bar_ref, index_refs, image_index_ref, mark_refs):
    rows = q.shape[0]
    shared = mark_refs[2][...]
    across = looked_up(table_row, index_refs[parity][...]).astype(BF)
    first = jnp.where(
        own_lanes(parity, rows), q.astype(F32) * 0.125, dot_nn(mark_refs[parity][...], across)
    )
    others = (looked_up(table_row, index_refs[2][...]) + bar_ref[...]).astype(BF)
    second = dot_nn(shared, others)
    on_images = looked_up(table_row, image_index_ref[...])
    second = jnp.concatenate([second[:TEXT], second[TEXT:] + on_images], axis=0)
    image_lane = lax.broadcasted_iota(jnp.int32, on_images.shape, 1)
    key_image = jnp.where(image_lane < POS, bias[:, :LANES].astype(BF), shared[TEXT:])
    return first.astype(BF), second.astype(BF), key_image


def joined(parity, first, second, key_image, k, marks_own, shared):
    rows = k.shape[0]
    lane = lax.broadcasted_iota(jnp.int32, (rows, LANES), 1)
    to_image = jnp.where(lane < POS, shared, second)
    key_first = jnp.where(own_lanes(parity, rows), k, marks_own)
    q_text = jnp.concatenate([first, second], axis=1)
    q_image = jnp.concatenate([first, to_image], axis=1)
    k_text = jnp.concatenate([key_first[:TEXT], shared[:TEXT]], axis=1)
    k_image = jnp.concatenate([key_first[TEXT:], key_image], axis=1)
    return q_text, q_image, k_text, k_image


def near(start, size):
    if start >= TEXT:
        return slice(0, TEXT)
    return slice(max(0, start - LANES), min(TEXT, start + size + LANES))


def image_bias(table_row, offsets):
    return jnp.concatenate(
        [looked_up(table_row, offsets[:, :LANES]), looked_up(table_row, offsets[:, LANES:])], axis=1
    )


def forward_kernel(
    meta_ref, rows_ref, table_ref, q_ref, k_ref, v_ref,
    mixed_ref, log_ref, first_ref, second_ref, key_image_ref, bias_ref,
    even_ref, odd_ref, shared_ref, bar_ref, index_even, index_odd, index_shared, image_index_ref,
):
    mark_refs = (even_ref, odd_ref, shared_ref)
    index_refs = (index_even, index_odd, index_shared)

    @pl.when(pl.program_id(0) == 0)
    def _():
        prepare(meta_ref, mark_refs, bar_ref, index_refs, image_index_ref)

    rows = q_ref.shape[0]
    images = rows - TEXT
    q, k, v = q_ref[...], k_ref[...], v_ref[...]
    offsets = bucket(rows_ref[2:3, TEXT:] - meta_ref[TEXT:, 2:3])
    tile = 256
    v_turned = transposed(v)
    heads = [None, None]

    def prepared(parity):
        table_row = table_ref[pl.ds(2 * pl.program_id(0) + parity, 1), :]
        bias = image_bias(table_row, offsets)
        first, second, key_image = widened(
            parity, q, table_row, bias, bar_ref, index_refs, image_index_ref, mark_refs
        )
        first_ref[parity] = first
        second_ref[parity] = second
        key_image_ref[parity] = key_image
        bias_ref[parity] = bias.astype(BF)
        wide = joined(
            parity, first, second, key_image, k, mark_refs[parity][...], shared_ref[...]
        )
        heads[parity] = wide + (bias,)

    def scored(parity, start):
        q_text, q_image, k_text, k_image, bias = heads[parity]
        here = slice(start, start + tile)
        on_image = dot_nt(k_image, q_image[here])
        if start >= TEXT:
            on_image = on_image + bias[:, start - TEXT : start - TEXT + tile]
        return dot_nt(k_text[near(start, tile)], q_text[here]), on_image

    spots = [(parity, start) for parity in range(2) for start in range(0, rows, tile)]
    outs = ([], [])
    prepared(0)
    following = scored(*spots[0])
    for index, (parity, start) in enumerate(spots):
        on_text, on_image = following
        if index == 1:
            prepared(1)
        if index + 1 < len(spots):
            following = scored(*spots[index + 1])
        top = jnp.maximum(
            jnp.max(on_text, axis=0, keepdims=True), jnp.max(on_image, axis=0, keepdims=True)
        )
        on_text = jnp.exp(on_text - top)
        on_image = jnp.exp(on_image - top)
        total = jnp.sum(on_text, axis=0, keepdims=True) + jnp.sum(on_image, axis=0, keepdims=True)
        own = slice(parity * HEAD, parity * HEAD + HEAD)
        out = dot_nn(v_turned[own, near(start, tile)], on_text.astype(BF)) + dot_nn(
            v_turned[own, TEXT:], on_image.astype(BF)
        )
        outs[parity].append(out * (1.0 / total))
        log_ref[0, parity : parity + 1, start : start + tile] = top + jnp.log(total)
    mixed_ref[...] = jnp.transpose(
        jnp.concatenate([jnp.concatenate(outs[parity], axis=1) for parity in range(2)], axis=0)
    )


def static_scratch(rows):
    square = (LANES, LANES)
    return [
        pltpu.VMEM((rows, LANES), BF),
        pltpu.VMEM((rows, LANES), BF),
        pltpu.VMEM((rows, LANES), BF),
        pltpu.VMEM(square, F32),
        pltpu.VMEM(square, jnp.int32),
        pltpu.VMEM(square, jnp.int32),
        pltpu.VMEM(square, jnp.int32),
        pltpu.VMEM((rows - TEXT, LANES), jnp.int32),
    ]


def attention_forward(meta_columns, meta_rows, table_rows, projected, width):
    rows = projected.shape[0]
    images = rows - TEXT
    pairs = width // LANES

    def block(part):
        return pl.BlockSpec((rows, LANES), lambda p: (0, part * pairs + p))

    whole = lambda shape: pl.BlockSpec(shape, lambda p: (0,) * len(shape))
    return pl.pallas_call(
        forward_kernel,
        grid=(pairs,),
        in_specs=[
            whole(meta_columns.shape),
            whole(meta_rows.shape),
            whole(table_rows.shape),
            block(0), block(1), block(2),
        ],
        out_specs=[
            pl.BlockSpec((rows, LANES), lambda p: (0, p)),
            pl.BlockSpec((1, 2, rows), lambda p: (p, 0, 0)),
            pl.BlockSpec((2, rows, LANES), lambda p: (p, 0, 0)),
            pl.BlockSpec((2, rows, LANES), lambda p: (p, 0, 0)),
            pl.BlockSpec((2, images, LANES), lambda p: (p, 0, 0)),
            pl.BlockSpec((2, images, images), lambda p: (p, 0, 0)),
        ],
        out_shape=[
            jax.ShapeDtypeStruct((rows, width), F32),
            jax.ShapeDtypeStruct((pairs, 2, rows), F32),
            jax.ShapeDtypeStruct((2 * pairs, rows, LANES), BF),
            jax.ShapeDtypeStruct((2 * pairs, rows, LANES), BF),
            jax.ShapeDtypeStruct((2 * pairs, images, LANES), BF),
            jax.ShapeDtypeStruct((2 * pairs, images, images), BF),
        ],
        scratch_shapes=static_scratch(rows),
        compiler_params=pltpu.CompilerParams(vmem_limit_bytes=60 * 1024 * 1024),
        name="attention_forward",
    )(meta_columns, meta_rows, table_rows, projected, projected, projected)


def skewed(block):
    size = block.shape[0]
    lane = lax.broadcasted_iota(jnp.int32, (size, LANES), 1)
    row = lax.broadcasted_iota(jnp.int32, (size, LANES), 0)
    turned = jnp.take_along_axis(
        block, (lane + row) & (LANES - 1), axis=1, mode="promise_in_bounds"
    )
    straight = lane + row < LANES
    above = jnp.sum(jnp.where(straight, turned, 0.0), axis=0, keepdims=True)
    below = jnp.sum(jnp.where(straight, 0.0, turned), axis=0, keepdims=True)
    return above, below


def transposed(array):
    return jnp.transpose(array.astype(F32)).astype(array.dtype)


def static_prepare(meta_ref, static):
    for ref, turned, value in zip(static[:3], static[3:], marks(meta_ref)):
        ref[...] = value
        turned[...] = transposed(value)


def head_back(
    parity, pair, rows_ref, wide_refs, k_ref, v_ref, mixed_ref, grad_ref, log_ref, static, diag_ref,
):
    mark_refs, turned_refs = static[:3], static[3:]
    first_ref, second_ref, key_image_ref, bias_ref = wide_refs
    head = 2 * pair + parity
    shared_t = turned_refs[2]
    rows = k_ref.shape[1]
    images = rows - TEXT
    tile = 256
    k, v, grad = k_ref[pair], v_ref[pair], grad_ref[pair]
    products = grad.astype(F32) * mixed_ref[pair]
    k_turned = transposed(k)
    is_image = rows_ref[1:2, TEXT:] > 0
    own = own_lanes(parity, rows)
    log_row = log_ref[pair, parity : parity + 1, :]
    first, shared = first_ref[head], mark_refs[2][...]
    q_text, q_image, k_text, k_image = joined(
        parity, first, second_ref[head], key_image_ref[head], k, mark_refs[parity][...], shared
    )
    bias = bias_ref[head].astype(F32)
    ones = jnp.where(own_lanes(parity, 8), 1.0, 0.0).astype(BF)
    delta = jnp.zeros((8, rows), F32)
    rest = products
    for _ in range(3):
        piece = rest.astype(BF)
        delta = delta + dot_nt(ones, piece)
        rest = rest - piece.astype(F32)
    delta = delta[0:1]
    v_own = jnp.where(own, v, jnp.zeros_like(v))
    q_marked = jnp.concatenate(
        [jnp.where(own, first, mark_refs[parity][...]), shared], axis=1
    )
    dq_text = jnp.zeros((HEAD, TEXT), F32)
    dq_image = jnp.zeros((HEAD, images), F32)
    dks = []
    dvs = []
    first_sum = jnp.zeros((LANES, LANES), F32)
    second_sum = jnp.zeros((LANES, LANES), F32)
    text_image = jnp.zeros((LANES, images), F32)

    def met(start, array, axis=0):
        text = near(start, tile)
        if axis == 0:
            return jnp.concatenate([array[text], array[TEXT:]], axis=0)
        return jnp.concatenate([array[:, text], array[:, TEXT:]], axis=1)

    def scored(start):
        here = slice(start, start + tile)
        if start < TEXT:
            scores = dot_nt(k_text[here], met(start, q_text))
        else:
            scores = dot_nt(k_image[start - TEXT : start - TEXT + tile], q_image)
            scores = jnp.concatenate([scores[:, :TEXT], scores[:, TEXT:] + bias], axis=1)
        return scores, dot_nt(v_own[here], met(start, grad))

    following = scored(0)
    for start in range(0, rows, tile):
        here = slice(start, start + tile)
        scores, prob_grad = following
        if start + tile < rows:
            following = scored(start + tile)
        soft = jnp.exp(scores - met(start, log_row, 1))
        score_grad = soft * (prob_grad - met(start, delta, 1))
        low = score_grad.astype(BF)
        dvs.append(dot_nn(soft.astype(BF), met(start, grad)))
        wide = dot_nn(low, met(start, q_marked))
        dks.append(wide[:, :LANES])
        part = dot_nn(k_turned[parity * HEAD : parity * HEAD + HEAD, here], low)
        text = near(start, tile)
        count = text.stop - text.start
        before = [jnp.zeros((HEAD, text.start), F32)] if text.start > 0 else []
        after = [jnp.zeros((HEAD, TEXT - text.stop), F32)] if text.stop < TEXT else []
        dq_text = dq_text + jnp.concatenate(before + [part[:, :count]] + after, axis=1)
        dq_image = dq_image + part[:, count:]
        rounded = wide.astype(BF)
        first_sum = first_sum + dot_nn(turned_refs[parity][:, here], rounded[:, :LANES])
        second_sum = second_sum + dot_nn(shared_t[:, here], rounded[:, LANES:])
        if start < TEXT:
            text_image = text_image + dot_nn(shared_t[:, here], low[:, count:])
        else:
            by_position = wide[:, LANES:]
            on_image = score_grad[:, TEXT:]
    dq = jnp.concatenate([dq_text, dq_image], axis=1)
    small = lax.broadcasted_iota(jnp.int32, (LANES, LANES), 1)
    small_row = lax.broadcasted_iota(jnp.int32, (LANES, LANES), 0)
    x0 = HEAD if parity == 0 else 0
    x_block = jnp.where(
        between(small, x0, x0 + COORD) & between(small_row, x0, x0 + COORD), first_sum, 0.0
    )
    y_block = jnp.where(
        between(small, Y0, Y0 + COORD) & between(small_row, Y0, Y0 + COORD), second_sum, 0.0
    )
    p_block = jnp.where((small < POS) & (small_row < POS), second_sum, 0.0)
    wide_lane = lax.broadcasted_iota(jnp.int32, (images, images), 1)
    outside = jnp.sum(jnp.where(is_image, 0.0, on_image), axis=1, keepdims=True)
    pairs = jnp.where(is_image, on_image, 0.0) + jnp.where(wide_lane == 0, outside, 0.0)
    outside_text = jnp.sum(jnp.where(is_image, 0.0, text_image), axis=1, keepdims=True)
    text_lane = lax.broadcasted_iota(jnp.int32, (LANES, images), 1)
    text_row = lax.broadcasted_iota(jnp.int32, (LANES, images), 0)
    text_image = jnp.where(is_image, text_image, 0.0) + jnp.where(
        text_lane == 0, outside_text, 0.0
    )
    text_image = jnp.where(text_row < POS, text_image, 0.0)
    first_lane = lax.broadcasted_iota(jnp.int32, (images, LANES), 1)
    left = pairs[:, :LANES] + jnp.where(first_lane < POS, by_position, 0.0)
    right = pairs[:, LANES:]
    a00, b00 = skewed(left[:LANES] + text_image[:, :LANES] + p_block)
    a01, b01 = skewed(right[:LANES] + text_image[:, LANES:])
    a10, b10 = skewed(left[LANES:])
    a11, b11 = skewed(right[LANES:])
    ax, bx = skewed(x_block)
    ay, by = skewed(y_block)
    diag_ref[head] = jnp.concatenate(
        [b10, b00 + b11 + a10, a00 + a11 + b01, a01, bx, ax, by, ay], axis=0
    )
    return dq * 0.125, jnp.concatenate(dks, axis=0), jnp.concatenate(dvs, axis=0)


MESH = pl.DeviceIdType.MESH
VMEM = pl.BlockSpec(memory_space=pltpu.VMEM)
HBM = pl.BlockSpec(memory_space=pltpu.HBM)
MIB = 1024 * 1024


def remote(src, dst, send, receive, device):
    return pltpu.make_async_remote_copy(
        src_ref=src, dst_ref=dst, send_sem=send, recv_sem=receive, device_id=device,
        device_id_type=MESH,
    )


def project_kernel(
    layer_ref, weight_hbm, *refs,
):
    small_hbm, refs = refs[:10], refs[10:]
    (item_ref, projected_out, columns_ref, rows_ref, table_ref,
     projected_ref, weight_ref, meta_send, bias_ref, sems, load_sems, store_sems), small = (
        refs[:12], refs[12:],
    )
    (segment_ref, mask_ref, position_ref, across_ref, down_ref, query_bias_ref, value_bias_ref,
     text_ref, horiz_ref, vert_ref) = small
    mine = lax.axis_index("seq")
    partner = (1 - mine, lax.axis_index("dp"))
    count, width = layer_ref.shape[1:]
    own = pl.ds(pl.multiple_of(mine * count, LANES), count)
    loads = [
        pltpu.make_async_copy(source, target, load_sems.at[index])
        for index, (source, target) in enumerate(
            list(zip(small_hbm, small))
            + [(layer_ref.at[mine], item_ref.at[own]), (weight_hbm, weight_ref)]
        )
    ]
    for load in loads:
        load.start()
    barrier = pltpu.get_barrier_semaphore()
    pl.semaphore_signal(barrier, inc=1, device_id=partner, device_id_type=MESH)
    pl.semaphore_wait(barrier, 1)
    pieces = count // LANES
    rows_out = [
        remote(
            layer_ref.at[1 - mine, pl.ds(piece * LANES, LANES)],
            item_ref.at[pl.ds(pl.multiple_of(mine * count + piece * LANES, LANES), LANES)],
            sems.at[0, piece], sems.at[1, piece], partner,
        )
        for piece in range(pieces)
    ]
    for copy in rows_out:
        copy.start()
    for load in loads[:-2]:
        load.wait()

    fields = (segment_ref, mask_ref, position_ref, across_ref, down_ref)
    blocks = [
        jnp.concatenate(
            [field[item : item + 1, :] for field in fields] + [jnp.zeros((3, count), jnp.int32)],
            axis=0,
        )
        for item in range(2)
    ]
    meta_send[...] = jnp.where(mine == 0, blocks[1], blocks[0])
    meta_out = remote(
        meta_send, rows_ref.at[:, own], sems.at[0, pieces], sems.at[1, pieces], partner
    )
    meta_out.start()
    rows_ref[:, own] = jnp.where(mine == 0, blocks[0], blocks[1])
    bias_ref[:, :width] = query_bias_ref[...].astype(F32).reshape(1, width)
    bias_ref[:, width : 2 * width] = jnp.zeros((1, width), F32)
    bias_ref[:, 2 * width :] = value_bias_ref[...].astype(F32).reshape(1, width)
    heads, levels = text_ref.shape
    spot = lax.broadcasted_iota(jnp.int32, (levels, LANES), 1)
    level = lax.broadcasted_iota(jnp.int32, (levels, LANES), 0)
    table = jnp.zeros((heads, LANES), F32)
    for source, begin in ((text_ref, 0), (horiz_ref, X_TABLE), (vert_ref, Y_TABLE)):
        table = table + dot_nn(source[...], (spot == level + begin).astype(BF))
    table_ref[...] = jnp.concatenate([table, jnp.zeros((16 - heads, LANES), F32)], axis=0)

    def project(there):
        step = 256

        def body(index, carry):
            columns = pl.ds(pl.multiple_of(index * step, step), step)
            product = dot_nn(item_ref[there], weight_ref[:, columns])
            projected_ref[there, columns] = (product + bias_ref[:, columns]).astype(BF)
            return carry

        lax.fori_loop(0, 3 * width // step, body, 0)

    def stored(index, there):
        return pltpu.make_async_copy(
            projected_ref.at[there], projected_out.at[there], store_sems.at[index]
        )

    for load in loads[-2:]:
        load.wait()
    project(own)
    stored(0, own).start()
    for piece in range(pieces):
        rows_out[piece].wait()
        there = pl.ds(pl.multiple_of((1 - mine) * count + piece * LANES, LANES), LANES)
        project(there)
        stored(1 + piece, there).start()
    meta_out.wait()
    meta = rows_ref[...].astype(F32)
    tall = jnp.concatenate([meta, jnp.zeros((LANES - 8, meta.shape[1]), F32)], axis=0)
    columns_ref[...] = jnp.transpose(tall).astype(jnp.int32)
    stored(0, own).wait()
    for piece in range(pieces):
        there = pl.ds(pl.multiple_of((1 - mine) * count + piece * LANES, LANES), LANES)
        stored(1 + piece, there).wait()


def projected_item(layer_in, fields, qkv_weight, query_bias, value_bias, tables):
    rows = 2 * layer_in.shape[1]
    width = layer_in.shape[2]
    pieces = rows // 2 // LANES
    small = list(fields) + [query_bias, value_bias] + [t.T for t in tables]
    return pl.pallas_call(
        project_kernel,
        in_specs=[HBM] * (2 + len(small)),
        out_specs=[VMEM, HBM, VMEM, VMEM, VMEM],
        out_shape=[
            jax.ShapeDtypeStruct((rows, width), BF),
            jax.ShapeDtypeStruct((rows, 3 * width), BF),
            jax.ShapeDtypeStruct((rows, LANES), jnp.int32),
            jax.ShapeDtypeStruct((8, rows), jnp.int32),
            jax.ShapeDtypeStruct((16, LANES), F32),
        ],
        scratch_shapes=[
            pltpu.VMEM((rows, 3 * width), BF),
            pltpu.VMEM((width, 3 * width), BF),
            pltpu.VMEM((8, rows // 2), jnp.int32),
            pltpu.VMEM((1, 3 * width), F32),
            pltpu.SemaphoreType.DMA((2, pieces + 1)),
            pltpu.SemaphoreType.DMA((len(small) + 2,)),
            pltpu.SemaphoreType.DMA((pieces + 1,)),
        ]
        + [pltpu.VMEM(array.shape, array.dtype) for array in small],
        compiler_params=pltpu.CompilerParams(
            collective_id=1, has_side_effects=True, vmem_limit_bytes=60 * MIB
        ),
        name="projected_item",
    )(layer_in, qkv_weight, *small)


EPSILON = 1e-05
TILE = 256


def vector(ref):
    return ref[...].astype(F32).reshape(1, ref.shape[0])


def gelu_and_slope(x):
    bell = jnp.exp2(-0.7213475204444817 * (x * x))
    rough = 1.0 + 0.23164188826 * jnp.abs(x)
    t = pl.reciprocal(rough, approx=True)
    t = t * (2.0 - rough * t)
    series = t * (
        0.127414796
        + t * (-0.142248368 + t * (0.7107068705 + t * (-0.7265760135 + t * 0.5307027145)))
    )
    tail = bell * series
    below = jnp.where(x >= 0.0, 1.0 - tail, tail)
    return x * below, below + x * (0.3989422804014327 * bell)


def row_mean(block):
    return jnp.mean(block, axis=1, keepdims=True)


def normalized(hidden):
    center = hidden - row_mean(hidden)
    scale = lax.rsqrt(row_mean(center * center) + EPSILON)
    return center * scale, scale


def norm_pulled(grad, unit, scale):
    return scale * (grad - row_mean(grad) - unit * row_mean(grad * unit))


def column_sum(block):
    return jnp.sum(block, axis=0, keepdims=True)


def feed_kernel(
    item_hbm, mixed_hbm, cotangent_ref, out_weight_ref, up_ref, down_ref, *refs,
):
    vectors_hbm, refs = refs[:7], refs[7:]
    (layer_out, d_hidden_out, d_mixed_out, grad_out_out, grad_down_ref, grad_up_ref, small_ref,
     item_ref, mixed_ref, d_hidden_ref, d_mixed_ref, grad_out_ref, layer_ref, cotangent_all, active, slope, unit, scale_ref, normed, normed_t, total, d_branch, d_branch_t,
     sems, load_sems, tile_sems, store_sems) = refs[:27]
    vectors = refs[27:]
    (out_bias_ref, attn_gain_ref, attn_shift_ref, up_bias_ref, down_bias_ref, ffn_gain_ref,
     ffn_shift_ref) = vectors
    step = pl.program_id(0)
    blocks = pl.num_programs(0) // 2
    rows, width = item_hbm.shape
    count = rows // 2
    mine = lax.axis_index("seq")
    partner = (1 - mine, lax.axis_index("dp"))
    own = pl.ds(pl.multiple_of(mine * count, LANES), count)
    tiles = rows // TILE

    def sent():
        return remote(
            cotangent_ref.at[1 - mine], cotangent_all.at[own], sems.at[0], sems.at[1], partner
        )

    def returned():
        theirs = pl.ds(pl.multiple_of((1 - mine) * count, LANES), count)
        return [
            pltpu.make_async_copy(layer_ref.at[own], layer_out.at[mine], load_sems.at[8]),
            remote(
                layer_ref.at[theirs], layer_out.at[mine], sems.at[2], sems.at[3], partner
            ),
        ]

    def tile_loads(tile):
        there = pl.ds(tile * TILE, TILE)
        return [
            pltpu.make_async_copy(source.at[there], target.at[there], tile_sems.at[index, tile])
            for index, (source, target) in enumerate(
                ((mixed_hbm, mixed_ref), (item_hbm, item_ref))
            )
        ]

    def store(index):
        source, target = (
            (d_hidden_ref, d_hidden_out), (d_mixed_ref, d_mixed_out), (grad_out_ref, grad_out_out),
        )[index]
        return pltpu.make_async_copy(source, target, store_sems.at[index])

    def loads():
        copies = list(zip(vectors_hbm, vectors)) + [(cotangent_ref.at[mine], cotangent_all.at[own])]
        return [
            pltpu.make_async_copy(source, target, load_sems.at[index])
            for index, (source, target) in enumerate(copies)
        ]

    def over_tiles(size, body, carry, unroll=1):
        def run(index, state):
            return body(pl.ds(pl.multiple_of(index * size, size), size), state)

        return lax.fori_loop(0, rows // size, run, carry, unroll=unroll)

    @pl.when(step == 0)
    def _():
        for index in range(rows // TILE):
            for load in tile_loads(index):
                load.start()
        for load in loads():
            load.start()
        barrier = pltpu.get_barrier_semaphore()
        pl.semaphore_signal(barrier, inc=1, device_id=partner, device_id_type=MESH)
        pl.semaphore_wait(barrier, 1)
        sent().start()
        small_ref[...] = jnp.zeros_like(small_ref)
        for load in loads():
            load.wait()
        out_bias, gain, shift = vector(out_bias_ref), vector(attn_gain_ref), vector(attn_shift_ref)

        for index in range(rows // TILE):
            for load in tile_loads(index):
                load.wait()
            there = slice(index * TILE, index * TILE + TILE)
            attn = dot_nn(mixed_ref[there].astype(BF), out_weight_ref[...]) + out_bias
            standard, scale = normalized(item_ref[there].astype(F32) + attn)
            unit[there] = standard
            scale_ref[there] = jnp.broadcast_to(scale, (TILE, LANES))
            result = standard * gain + shift
            normed[there] = result.astype(BF)
            normed_t[:, there] = jnp.transpose(result).astype(BF)
        total[...] = jnp.zeros_like(total)

    @pl.when(step < blocks)
    def _():
        columns = [slice(begin, begin + TILE) for begin in range(0, width, TILE)]
        low = normed[...]
        following = dot_nn(low, up_ref[:, columns[0]])
        values = []
        for index, here in enumerate(columns):
            product = following
            if index + 1 < len(columns):
                following = dot_nn(low, up_ref[:, columns[index + 1]])
            bias = up_bias_ref[pl.ds(pl.multiple_of(step * width + here.start, LANES), TILE)]
            value, grade = gelu_and_slope(product + bias.astype(F32).reshape(1, TILE))
            values.append(value.astype(BF))
            active[step, :, here] = values[-1]
            slope[step, :, here] = grade.astype(BF)
        values = jnp.concatenate(values, axis=1)
        for here in columns:
            total[:, here] += dot_nn(values, down_ref[:, here])

    @pl.when(step == blocks)
    def _():
        sent().wait()
        gain, shift, bias = vector(ffn_gain_ref), vector(ffn_shift_ref), vector(down_bias_ref)
        first_gain, first_shift = vector(attn_gain_ref), vector(attn_shift_ref)

        def tile(there, sums):
            hidden = unit[there] * first_gain + first_shift + (total[there] + bias)
            standard, scale = normalized(hidden)
            layer_ref[there] = (standard * gain + shift).astype(BF)
            cotangent = cotangent_all[there].astype(F32)
            pulled = norm_pulled(cotangent * gain, standard, scale)
            total[there] = pulled
            low = pulled.astype(BF)
            d_branch[there] = low
            return (
                sums[0] + column_sum(low.astype(F32)),
                sums[1] + column_sum(cotangent * standard),
                sums[2] + column_sum(cotangent),
            )

        zero = jnp.zeros((1, width), F32)
        sums = over_tiles(64, tile, (zero, zero, zero), 4)
        for row, value in zip((5, 6, 7), sums):
            small_ref[row : row + 1] = value

        for copy in returned():
            copy.start()

        def turn(there, carry):
            d_branch_t[:, there] = jnp.transpose(d_branch[there].astype(F32)).astype(BF)
            return carry

        over_tiles(TILE, turn, 0, 3)

    @pl.when(step >= blocks)
    def _():
        block = step - blocks

        columns = [slice(begin, begin + TILE) for begin in range(0, width, TILE)]
        branch = d_branch[...]
        turned = d_branch_t[...]
        following = dot_nt(branch, down_ref[columns[0]])
        values = []
        for index, here in enumerate(columns):
            product = following
            if index + 1 < len(columns):
                following = dot_nt(branch, down_ref[columns[index + 1]])
            grad_down_ref[:, here] = dot_nn(turned, active[block, :, here]).astype(BF)
            d_up = (product * slope[block, :, here].astype(F32)).astype(BF)
            small_ref[pl.ds(8 + block, 1), here] = column_sum(d_up.astype(F32))
            values.append(d_up)
        values = jnp.concatenate(values, axis=1)
        turned = normed_t[...]
        for here in columns:
            grad_up_ref[:, here] = dot_nn(turned, values[:, here]).astype(BF)
            total[:, here] += dot_nt(values, up_ref[here])

    @pl.when(step == 2 * blocks - 1)
    def _():
        gain = vector(attn_gain_ref)

        def tile(there, sums):
            d_normed = total[there]
            standard = unit[there]
            d_hidden = norm_pulled(d_normed * gain, standard, scale_ref[there, :1])
            d_hidden_ref[there] = d_hidden
            low = d_hidden.astype(BF)
            d_branch[there] = low
            return (
                sums[0] + column_sum(low.astype(F32)),
                sums[1] + column_sum(d_normed * standard),
                sums[2] + column_sum(d_normed),
            )

        zero = jnp.zeros((1, width), F32)
        sums = over_tiles(64, tile, (zero, zero, zero), 4)
        for row, value in zip((2, 3, 4), sums):
            small_ref[row : row + 1] = value
        store(0).start()

        def turn(there, carry):
            normed_t[:, there] = jnp.transpose(mixed_ref[there]).astype(BF)
            return carry

        over_tiles(TILE, turn, 0, 3)

        for begin in range(0, width, TILE):
            here = slice(begin, begin + TILE)
            d_mixed_ref[:, here] = dot_nt(d_branch[...], out_weight_ref[here]).astype(BF)
        store(1).start()
        for begin in range(0, width, TILE):
            here = slice(begin, begin + TILE)
            grad_out_ref[:, here] = dot_nn(normed_t[...], d_branch[:, here]).astype(BF)
        store(2).start()

        for copy in returned() + [store(0), store(1), store(2)]:
            copy.wait()


def fed_forward_and_back(
    item, mixed, cotangent, out_weight, up_weight, down_weight, vectors,
):
    rows, width = item.shape
    blocks = up_weight.shape[1] // width
    whole = pl.BlockSpec(memory_space=pltpu.VMEM)
    square = lambda kind: jax.ShapeDtypeStruct((rows, width), kind)
    later = lambda i: jnp.maximum(i - blocks, 0)
    return pl.pallas_call(
        feed_kernel,
        grid=(2 * blocks,),
        in_specs=[HBM, HBM, HBM, whole]
        + [
            pl.BlockSpec((width, width), lambda i: (0, lax.rem(i, blocks))),
            pl.BlockSpec((width, width), lambda i: (lax.rem(i, blocks), 0)),
        ]
        + [HBM] * 7,
        out_specs=[HBM] * 4
        + [
            pl.BlockSpec((width, width), lambda i: (later(i), 0)),
            pl.BlockSpec((width, width), lambda i: (later(i), 0)),
            whole,
        ],
        out_shape=[
            jax.ShapeDtypeStruct((2, rows // 2, width), BF), square(F32), square(BF),
            jax.ShapeDtypeStruct((width, width), BF),
            jax.ShapeDtypeStruct((blocks * width, width), BF),
            jax.ShapeDtypeStruct((blocks * width, width), BF),
            jax.ShapeDtypeStruct((16, width), F32),
        ],
        scratch_shapes=[
            pltpu.VMEM((rows, width), BF),
            pltpu.VMEM((rows, width), F32),
            pltpu.VMEM((rows, width), F32),
            pltpu.VMEM((rows, width), BF),
            pltpu.VMEM((width, width), BF),
            pltpu.VMEM((rows, width), BF),
            pltpu.VMEM((rows, width), BF),
            pltpu.VMEM((blocks, rows, width), BF),
            pltpu.VMEM((blocks, rows, width), BF),
            pltpu.VMEM((rows, width), F32),
            pltpu.VMEM((rows, LANES), F32),
            pltpu.VMEM((rows, width), BF),
            pltpu.VMEM((width, rows), BF),
            pltpu.VMEM((rows, width), F32),
            pltpu.VMEM((rows, width), BF),
            pltpu.VMEM((width, rows), BF),
            pltpu.SemaphoreType.DMA((4,)),
            pltpu.SemaphoreType.DMA((9,)),
            pltpu.SemaphoreType.DMA((2, rows // TILE)),
            pltpu.SemaphoreType.DMA((3,)),
        ]
        + [pltpu.VMEM(vector.shape, vector.dtype) for vector in vectors],
        compiler_params=pltpu.CompilerParams(
            collective_id=2, has_side_effects=True, vmem_limit_bytes=60 * MIB
        ),
        name="feed_forward",
    )(item, mixed, cotangent, out_weight, up_weight, down_weight, *vectors)


SLOTS = 4


def finish_kernel(
    main_ref, tail_ref, input_hbm, small_ref, diagonal_ref,
    down_ref, up_ref, out_ref, qkv_ref, input_ref, *refs,
):
    singles, (main_in, tail_in, slots, input_in, input_slot, in_sems, out_sems, item_sems) = (
        refs[:12], refs[12:],
    )
    mains, width = main_in.shape[0], main_in.shape[2]
    pairs, across = tail_in.shape[0], tail_in.shape[2]
    hidden = mains // 2
    blocks = mains + pairs

    def load(block):
        if block < mains:
            source, target = main_ref.at[pl.ds(block * width, width)], main_in.at[block]
        else:
            pair = block - mains
            source, target = tail_ref.at[pl.ds(pair * TAIL_ROWS, TAIL_ROWS)], tail_in.at[pair]
        return pltpu.make_async_copy(source, target, in_sems.at[block])

    def stores(block):
        slot, sem = slots.at[block % SLOTS], out_sems.at[block % SLOTS]
        if block < hidden:
            targets = [(slot, down_ref.at[pl.ds(block * width, width)])]
        elif block < mains:
            targets = [(slot, up_ref.at[:, pl.ds((block - hidden) * width, width)])]
        else:
            pair = block - mains
            targets = [
                (
                    slot.at[:, pl.ds(part * LANES, LANES)],
                    qkv_ref.at[:, pl.ds(part * width + pair * LANES, LANES)],
                )
                for part in range(3)
            ]
            down = pl.ds(0, TAIL_ROWS - width)
            targets.append(
                (slot.at[down, pl.ds(across, across)], out_ref.at[out_spot(pair, pairs, width)])
            )
        return [
            pltpu.make_async_copy(source, target, sem.at[index])
            for index, (source, target) in enumerate(targets)
        ]

    load_input = pltpu.make_async_copy(input_hbm, input_in, item_sems.at[0])
    store_input = pltpu.make_async_copy(input_slot, input_ref, item_sems.at[1])
    for block in range(blocks):
        load(block).start()
    load_input.start()
    for block in range(blocks):
        load(block).wait()
        if block >= SLOTS:
            for copy in stores(block - SLOTS):
                copy.wait()
        slot = block % SLOTS
        if block < hidden:
            slots[slot] = jnp.transpose(main_in[block].astype(F32))
        elif block < mains:
            slots[slot] = main_in[block].astype(F32)
        else:
            slots[slot, :, :across] = tail_in[block - mains, :width].astype(F32)
            slots[slot, : TAIL_ROWS - width, across:] = tail_in[block - mains, width:].astype(F32)
        for copy in stores(block):
            copy.start()
    load_input.wait()
    input_slot[...] = input_in[...].astype(F32)
    store_input.start()
    for row in range(8):
        singles[row][...] = small_ref[row]
    for row in range(hidden):
        singles[8][row * width : row * width + width] = small_ref[8 + row]
    heads, levels = singles[9].shape
    diagonals = diagonal_ref[...]
    level = lax.broadcasted_iota(jnp.int32, (LANES, LANES), 1)
    lane = lax.broadcasted_iota(jnp.int32, (LANES, LANES), 0)
    for table, (first, size, skip) in enumerate(((0, 4, 0), (4, 2, 1), (6, 2, 1))):
        total = jnp.zeros((heads, LANES), F32)
        for row in range(size):
            distance = lane + LANES * (row + skip - 2)
            chosen = (bucket(distance) == level).astype(F32)
            total = total + jnp.dot(
                diagonals[:, first + row, :], chosen, preferred_element_type=F32,
                precision=lax.Precision.HIGHEST,
            )
        singles[9 + table][...] = total[:, :levels]
    for block in range(blocks - SLOTS, blocks):
        for copy in stores(block):
            copy.wait()
    store_input.wait()


def finished(main, tail, grad_input, small, diagonals, hidden, levels):
    width = main.shape[1]
    heads = diagonals.shape[0]
    mains = main.shape[0] // width
    pairs = tail.shape[0] // TAIL_ROWS
    single = jax.ShapeDtypeStruct((width,), F32)
    table = jax.ShapeDtypeStruct((heads, levels), F32)
    dma = pltpu.SemaphoreType.DMA
    return pl.pallas_call(
        finish_kernel,
        in_specs=[HBM, HBM, HBM, VMEM, VMEM],
        out_specs=[HBM] * 5 + [VMEM] * 12,
        out_shape=[
            jax.ShapeDtypeStruct((hidden, width), F32),
            jax.ShapeDtypeStruct((width, hidden), F32),
            jax.ShapeDtypeStruct((width, width), F32),
            jax.ShapeDtypeStruct((width, 3 * width), F32),
            jax.ShapeDtypeStruct(grad_input.shape, F32),
        ]
        + [single] * 8
        + [jax.ShapeDtypeStruct((hidden,), F32)]
        + [table] * 3,
        scratch_shapes=[
            pltpu.VMEM((mains, width, width), BF),
            pltpu.VMEM((pairs, TAIL_ROWS, tail.shape[1]), BF),
            pltpu.VMEM((SLOTS, width, width), F32),
            pltpu.VMEM(grad_input.shape, BF),
            pltpu.VMEM(grad_input.shape, F32),
            dma((mains + pairs,)),
            dma((SLOTS, 4)),
            dma((2,)),
        ],
        compiler_params=pltpu.CompilerParams(vmem_limit_bytes=56 * MIB),
        name="finished",
    )(main, tail, grad_input, small, diagonals)


PIECE = 16


class Place:
    def __init__(self, depth):
        place = lax.axis_index("dp")
        self.depth = depth
        self.group = lax.div(place, 4 * depth)
        self.z = lax.rem(lax.div(place, 4), depth)
        self.bits = {
            "x": lax.axis_index("seq"),
            "c": lax.rem(place, 2),
            "y": lax.rem(lax.div(place, 2), 2),
            "a": lax.rem(self.z, 2),
            "b": lax.div(self.z, 2),
        }

    def partner(self, letters):
        bit = {
            letter: 1 - value if letter in letters else value
            for letter, value in self.bits.items()
        }
        z = self.z
        for letter, reach in (("a", 1), ("b", 2)):
            if letter in letters:
                z = z + reach - 2 * reach * self.bits[letter]
        return (bit["x"], (self.group * self.depth + z) * 4 + bit["y"] * 2 + bit["c"])

    def greet(self, met):
        barrier = pltpu.get_barrier_semaphore()
        for letters in met:
            pl.semaphore_signal(
                barrier, inc=1, device_id=self.partner(letters), device_id_type=MESH
            )
        pl.semaphore_wait(barrier, len(met))


def letters_of(depth):
    return "xy" + "ab"[: (depth - 1).bit_length()]


def parsed(routes, depth):
    kept = letters_of(depth)
    parts = []
    for route in routes.split():
        hops = ["".join(letter for letter in hop if letter in kept) for hop in route.split(".")]
        parts.append([hop for hop in hops if hop])
    return parts


def subsets(hop):
    return [
        "".join(letter for index, letter in enumerate(hop) if mask >> index & 1)
        for mask in range(1, 2 ** len(hop))
    ]


class Chunk:
    def __init__(self, place, depth, source, out_ref, offset, spot, scratch):
        _, self.begin, rows, first, columns, _, routes, _ = spot
        self.place, self.source, self.columns = place, source, pl.ds(first, columns)
        self.out_ref, self.out_begin = out_ref, offset + self.begin
        self.parts = parsed(routes, depth)
        self.half = rows // 2
        self.share = self.half // len(self.parts)
        self.hops = max(len(part) for part in self.parts)
        self.work, self.fresh, *landing, self.sends, self.receives, self.locals = scratch
        self.landing = {}
        self.sems = {}
        count = 2
        for part, hops in enumerate(self.parts):
            for hop, letters in enumerate(hops):
                self.landing[part, hop] = landing.pop(0)
                for way in range(2):
                    for index in range(2 ** len(letters) - 1):
                        self.sems[way, part, hop, index] = count
                        count += 1

    def aligned(self, value):
        return pl.multiple_of(value, PIECE)

    def size(self, part, hop):
        return self.share >> sum(len(letters) for letters in self.parts[part][: hop + 1])

    def spot(self, part, hop, other=""):
        start = part * self.share
        for level in range(hop + 1):
            for index, letter in enumerate(self.parts[part][level]):
                bit = self.place.bits[letter]
                if level == hop and letter in other:
                    bit = 1 - bit
                start = start + bit * (self.size(part, level) << index)
        return start

    def out(self, core):
        begin = self.aligned(self.out_begin + core * self.half)
        return self.out_ref.at[pl.ds(begin, self.half), self.columns]

    def held(self, buffer, begin, size):
        return buffer.at[pl.ds(self.aligned(begin), size)]

    def copy(self, index, source, target, letters):
        return remote(
            source, target, self.sends.at[index], self.receives.at[index],
            self.place.partner(letters),
        )

    def pair_down(self):
        core = self.place.bits["c"]
        at = lambda c: self.source.at[
            pl.ds(self.aligned(self.begin + c * self.half), self.half), self.columns
        ]
        return [
            self.copy(0, at(1 - core), self.fresh, "c"),
            pltpu.make_async_copy(at(core), self.work, self.locals.at[0]),
        ]

    def pair_up(self, arriving):
        core = self.place.bits["c"]
        return [
            self.copy(1, self.fresh, self.out(1 - core if arriving else core), "c"),
            pltpu.make_async_copy(self.fresh, self.out(core), self.locals.at[1]),
        ]

    def at_hop(self, hop):
        return [
            (part, hops[hop]) for part, hops in enumerate(self.parts) if hop < len(hops)
        ]

    def down(self, hop):
        copies = []
        for part, letters in self.at_hop(hop):
            size = self.size(part, hop)
            for index, other in enumerate(subsets(letters)):
                copies.append(
                    self.copy(
                        self.sems[0, part, hop, index],
                        self.held(self.work, self.spot(part, hop, other), size),
                        self.landing[part, hop].at[index], other,
                    )
                )
        return copies

    def up(self, hop, arriving):
        copies = []
        for part, letters in self.at_hop(hop):
            mine = self.spot(part, hop)
            size = self.size(part, hop)
            for index, other in enumerate(subsets(letters)):
                target = self.spot(part, hop, other) if arriving else mine
                copies.append(
                    self.copy(
                        self.sems[1, part, hop, index], self.held(self.fresh, mine, size),
                        self.held(self.fresh, target, size), other,
                    )
                )
        return copies

    def add(self, begin, sources, size):
        step = 64 if size % 64 == 0 else 32 if size % 32 == 0 else PIECE

        def body(index, carry):
            offset = self.aligned(index * step)
            there = pl.ds(self.aligned(begin + offset), step)
            total = self.work[there]
            if len(sources) == 1:
                total = total + sources[0][pl.ds(offset, step)]
            else:
                total = total.astype(F32)
                for source in sources:
                    total = total + source[pl.ds(offset, step)].astype(F32)
            self.work[there] = total.astype(BF)
            return carry

        lax.fori_loop(0, size // step, body, 0)

    def stage(self, number):
        hops = self.hops
        ended, started = [], []
        if number == 0:
            started = self.pair_down()
        elif number == 1:
            ended = self.pair_down()
            started = self.down(0)
        elif number <= hops:
            ended = self.down(number - 2)
            started = self.down(number - 1)
        elif number == hops + 1:
            ended = self.down(hops - 1)
            started = self.up(hops - 1, False)
        elif number <= 2 * hops:
            level = 2 * hops + 1 - number
            ended = self.up(level, True)
            started = self.up(level - 1, False)
        elif number == 2 * hops + 1:
            ended = self.up(0, True)
            started = self.pair_up(False)
        else:
            ended = self.pair_up(True)
        for copy in ended:
            copy.wait()
        if number == 1:
            self.add(0, [self.fresh], self.half)
        elif 2 <= number <= hops + 1:
            hop = number - 2
            for part, letters in self.at_hop(hop):
                landing = self.landing[part, hop]
                sources = [landing.at[index] for index in range(2 ** len(letters) - 1)]
                self.add(self.spot(part, hop), sources, self.size(part, hop))
        if number == hops + 1:
            for part, route in enumerate(self.parts):
                last = len(route) - 1
                there = pl.ds(self.aligned(self.spot(part, last)), self.size(part, last))
                self.fresh[there] = self.work[there]
        for copy in started:
            copy.start()


def chunk_scratch(spot, depth):
    _, _, rows, _, columns, _, routes, _ = spot
    parts = parsed(routes, depth)
    landing = []
    copies = 2
    for hops in parts:
        size = rows // 2 // len(parts)
        for letters in hops:
            size >>= len(letters)
            others = 2 ** len(letters) - 1
            copies += 2 * others
            landing.append(pltpu.VMEM((others, size, columns), BF))
    dma = pltpu.SemaphoreType.DMA
    return (
        [pltpu.VMEM((rows // 2, columns), BF)] * 2
        + landing
        + [dma((copies,)), dma((copies,)), dma((2,))]
    )


def loads_of(hop, size):
    if "x" in hop and "y" in hop:
        return [("x", 2 * size), ("y", 2 * size)]
    if hop in ("x", "y"):
        return [(hop, size)]
    if "a" in hop and "b" in hop:
        return [("end", 3 * size), ("middle", 4 * size)]
    return [("end", size), ("middle", 2 * size)] if hop == "b" else [("end", size)]


def planned(chunks, work, depth, hop_count):
    latency, issue, link, pair = 3.0, 0.08, 85e3, 600e3
    free = {}
    now = 3.0
    chains = []
    for rows, columns, need, routes, _ in chunks:
        parts = parsed(routes, depth)
        sizes = [rows // 2 // len(parts)] * len(parts)
        down = []
        for hop in range(max(len(part) for part in parts)):
            loads, copies, added = [], 0, 0
            for index, part in enumerate(parts):
                if hop < len(part):
                    sizes[index] >>= len(part[hop])
                    others = 2 ** len(part[hop]) - 1
                    loads += loads_of(part[hop], sizes[index])
                    copies += others
                    added += sizes[index] * others
            down.append((loads, copies, added, columns))
        first = [([("core", rows // 2)], 1.5, rows // 2, columns)]
        last = [([("core", rows // 2)], 1, 0, columns)]
        chains.append((need, first + down + down[::-1] + last))
    chains.append((len(work), [([("core", 16)], 2, 0, 768)] * hop_count))
    ranks = [chunk[4] for chunk in chunks] + [0]
    position = [0] * len(chains)
    ready = [0.0] * len(chains)
    order = [[] for _ in range(len(work) + 1)]
    done = 0
    while True:
        open_ones = [
            (ranks[i], ready[i], i) for i, (need, chain) in enumerate(chains)
            if position[i] <= len(chain) and need <= done
        ]
        due = [entry for entry in open_ones if entry[1] <= now]
        if not due and done < len(work):
            now += work[done]
            done += 1
            continue
        if not open_ones:
            return order
        _, when, index = min(due) if due else min(open_ones, key=lambda entry: entry[1])
        now = max(now, when)
        chain = chains[index][1]
        stage = position[index]
        order[done].append((index, stage))
        if 0 < stage <= len(chain) // 2:
            now += 1e-6 * chain[stage - 1][2] * chain[stage - 1][3]
        if stage < len(chain):
            loads, copies, _, columns = chain[stage]
            now += issue * copies
            end = now
            for lane, rows in loads:
                rate = pair if lane == "core" else link / 2
                free[lane] = max(now, free.get(lane, 0.0)) + 2 * rows * columns / rate
                end = max(end, free[lane])
            ready[index] = end + latency
        position[index] += 1


def last_kernel(
    depth, plan, orders, counts, *refs,
):
    (meta_ref, rows_ref, projected_hbm, mixed_hbm, grad_hbm, log_ref, first_hbm, second_hbm,
     key_image_hbm, bias_hbm, small_ref, item_hbm, weight_hbm, d_hidden_hbm, grad_down_ref, grad_up_ref,
     grad_out_ref,
     main_out, tail_out, small_out, diagonal_out, input_out,
     *scratch) = refs
    static, scratch = scratch[:6], scratch[6:]
    (k_ref, v_ref, mixed_ref, grad_ref, first_ref, second_ref, key_image_ref, bias_ref, pair_sems,
     item_ref, weight_ref, d_hidden_ref, load_sems, d_project, item_t, tail, input_grad,
     small_in, diagonal_in, small_sems, item_sems, *scratch) = scratch
    place = Place(depth)
    step = pl.program_id(0)
    pairs = k_ref.shape[0]
    rows, width = item_hbm.shape
    count = rows // 2
    x = place.bits["x"]
    hidden = grad_down_ref.shape[0]
    sources = ((grad_down_ref, main_out, 0), (grad_up_ref, main_out, hidden), (tail, tail_out, 0))
    chunks = []
    for spot, pieces in zip(plan, counts):
        chunks.append(Chunk(place, depth, *sources[spot[0]], spot, scratch[:pieces]))
        scratch = scratch[pieces:]
    hop_letters = "c" + letters_of(depth)
    wide_hbm = (first_hbm, second_hbm, key_image_hbm, bias_hbm)
    wide_refs = (first_ref, second_ref, key_image_ref, bias_ref)

    def pair_loads(pair):
        copies = []
        held = (
            (projected_hbm, k_ref, width), (projected_hbm, v_ref, 2 * width),
            (mixed_hbm, mixed_ref, 0), (grad_hbm, grad_ref, 0),
        )
        for source, target, first in held:
            columns = pl.ds(pl.multiple_of(first + pair * LANES, LANES), LANES)
            copies.append((source.at[:, columns], target.at[pair]))
        heads = pl.ds(2 * pair, 2)
        for source, target in zip(wide_hbm, wide_refs):
            copies.append((source.at[heads], target.at[heads]))
        return [
            pltpu.make_async_copy(source, target, pair_sems.at[pair, index])
            for index, (source, target) in enumerate(copies)
        ]

    def loads(first):
        copies = [(item_hbm, item_ref), (weight_hbm, weight_ref), (d_hidden_hbm, d_hidden_ref)]
        for pair in range(pairs):
            down, across = out_spot(pair, pairs, width)
            copies.append(
                (
                    grad_out_ref.at[down, across],
                    tail.at[pl.ds(pair * TAIL_ROWS + width, TAIL_ROWS - width)],
                )
            )
        return [
            pltpu.make_async_copy(source, target, load_sems.at[index])
            for index, (source, target) in enumerate(copies)
            if (index == 0) == first
        ]

    def input_copies():
        return [
            pltpu.make_async_copy(
                input_grad.at[pl.ds(pl.multiple_of(x * count, LANES), count)], input_out.at[x],
                item_sems.at[0],
            ),
            remote(
                input_grad.at[pl.ds(pl.multiple_of((1 - x) * count, LANES), count)],
                input_out.at[x], item_sems.at[1], item_sems.at[2], place.partner("x"),
            ),
        ]

    def small_copies(hop):
        return [
            remote(source, landing.at[hop], small_sems.at[0, kind, hop],
                   small_sems.at[1, kind, hop], place.partner(hop_letters[hop]))
            for kind, (source, landing) in enumerate(
                ((small_out, small_in), (diagonal_out, diagonal_in))
            )
        ]

    def small_stage(hop):
        if hop > 0:
            for copy in small_copies(hop - 1):
                copy.wait()
            small_out[...] = small_out[...] + small_in[hop - 1]
            diagonal_out[...] = diagonal_out[...] + diagonal_in[hop - 1]
        if hop < len(hop_letters):
            for copy in small_copies(hop):
                copy.start()

    def perform(slot):
        for index, stage in orders[slot]:
            if index == len(chunks):
                small_stage(stage)
            else:
                chunks[index].stage(stage)

    @pl.when(step == 0)
    def _():
        for copy in pair_loads(0) + loads(True):
            copy.start()
        met = set(hop_letters)
        for chunk in chunks:
            for hops in chunk.parts:
                for letters in hops:
                    met.update(subsets(letters))
        place.greet(sorted(met))
        small_out[...] = small_ref[...]

    for pair in range(pairs):
        @pl.when(step == pair)
        def _(pair=pair):
            perform(pair)

    @pl.when(step == 0)
    def _():
        for pair in range(1, pairs):
            for copy in pair_loads(pair):
                copy.start()
        for copy in loads(False):
            copy.start()
        static_prepare(meta_ref, static)
        for copy in loads(True):
            copy.wait()
        for tile in range(rows // TILE):
            there = slice(tile * TILE, tile * TILE + TILE)
            item_t[:, there] = jnp.transpose(item_ref[there].astype(F32)).astype(BF)

    for copy in pair_loads(step):
        copy.wait()
    (dq_even, dk_even, dv_even), (dq_odd, dk_odd, dv_odd) = [
        head_back(
            parity, step, rows_ref, wide_refs, k_ref, v_ref, mixed_ref, grad_ref, log_ref,
            static, diagonal_out,
        )
        for parity in range(2)
    ]
    even = own_lanes(0, rows)
    pieces = [
        jnp.transpose(jnp.concatenate([dq_even, dq_odd], axis=0)).astype(BF),
        jnp.where(even, dk_even, dk_odd).astype(BF),
        jnp.where(even, dv_even, dv_odd).astype(BF),
    ]
    for part, piece in enumerate(pieces):
        d_project[:, pl.ds(pl.multiple_of(part * width + step * LANES, LANES), LANES)] = piece
    slab = pl.ds(pl.multiple_of(step * TAIL_ROWS, TAIL_ROWS), width)
    tail[slab] = dot_nn(item_t[...], jnp.concatenate(pieces, axis=1)).astype(BF)

    @pl.when(step == 0)
    def _():
        for copy in loads(False):
            copy.wait()

    @pl.when(step == pairs - 1)
    def _():
        perform(pairs)
        for begin in range(0, width, TILE):
            here = slice(begin, begin + TILE)
            total = d_hidden_ref[:, here] + dot_nt(d_project[...], weight_ref[here])
            input_grad[:, here] = total.astype(BF)
        for copy in input_copies():
            copy.start()
        for begin in range(0, width, TILE):
            here = slice(begin, begin + TILE)
            there = slice(2 * width + begin, 2 * width + begin + TILE)
            small_out[0:1, here] = column_sum(d_project[:, here].astype(F32))
            small_out[1:2, here] = column_sum(d_project[:, there].astype(F32))
        perform(pairs + 1)
        for copy in input_copies():
            copy.wait()


TAIL_ROWS = 1024


def out_spot(pair, pairs, width):
    down = TAIL_ROWS - width
    across = width * width // (pairs * down)
    per_row = width // across
    return (
        pl.ds(pair // per_row * down, down),
        pl.ds(pair % per_row * across, across),
    )


def summed_with_attention_back(
    meta_columns, meta_rows, projected, mixed, d_mixed, logs, wide_arrays, item, qkv_weight,
    d_hidden, small, grad_down, grad_up, grad_out,
):
    size = lax.axis_size("dp")
    depth = 4 if size % 16 == 0 else size // 4
    rows, width = item.shape
    pairs = width // LANES
    hidden = grad_down.shape[0]
    hops = len(letters_of(depth)) + 1
    work = [6.0] * pairs + [4.0]
    tall = 1024
    plan = [
        (0, 0, 3072, 0, 256, 0, "a.b.x.y x.a.y.b", 3),
        (0, 0, 3072, 256, 256, 0, "y.ab.x x.y.ab", 2),
        (0, 0, 3072, 512, 256, 0, "a.b.x.y x.y.a.b", 2),
        (1, 0, 2048, 0, 384, 0, "y.x.a.b a.b.x.y", 2),
        (1, 0, 2048, 384, 384, 0, "y.x.a.b y.x.a.b", 0),
        (1, 2048, 1024, 0, 384, 0, "y.x.a.b x.y.a.b", 3),
        (1, 2048, 1024, 384, 384, 0, "a.b.y.x x.a.b.y", 2),
        (2, 0 * tall, tall, 0, 384, 1, "y.a.x.b x.y.a.b", 3),
        (2, 1 * tall, tall, 0, 384, 2, "a.b.y.x x.a.y.b", 4),
        (2, 2 * tall, tall, 0, 384, 3, "x.y.a.b y.x.a.b", 3),
        (2, 3 * tall, tall, 0, 384, 4, "xy.ab", 4),
        (2, 4 * tall, tall, 0, 384, 5, "y.x.ab y.x.ab", 1),
        (2, 5 * tall, tall, 0, 384, 6, "y.x.ab y.x.ab", 4),
    ]
    orders = planned([(spot[2],) + spot[4:] for spot in plan], work, depth, hops)

    whole = pl.BlockSpec(memory_space=pltpu.VMEM)
    diagonals = jax.ShapeDtypeStruct((2 * pairs, 8, LANES), F32)
    dma = pltpu.SemaphoreType.DMA
    scratch = []
    for spot in plan:
        scratch.append(chunk_scratch(spot, depth))
    main, tail, small, diagonals, grad_input = pl.pallas_call(
        functools.partial(last_kernel, depth, plan, orders, [len(pieces) for pieces in scratch]),
        grid=(pairs,),
        in_specs=[whole] * 2 + [HBM] * 3 + [whole] + [HBM] * 4 + [whole] + [HBM] * 6,
        out_specs=[HBM, HBM, whole, whole, HBM],
        out_shape=[
            jax.ShapeDtypeStruct((2 * hidden, width), BF),
            jax.ShapeDtypeStruct((pairs * TAIL_ROWS, 3 * LANES), BF),
            jax.ShapeDtypeStruct(small.shape, F32),
            diagonals,
            jax.ShapeDtypeStruct((2, rows // 2, width), BF),
        ],
        scratch_shapes=[pltpu.VMEM((rows, LANES), BF)] * 3
        + [pltpu.VMEM((LANES, rows), BF)] * 3
        + [pltpu.VMEM((pairs, rows, LANES), kind) for kind in (BF, BF, F32, BF)]
        + [pltpu.VMEM(array.shape, BF) for array in wide_arrays]
        + [
            dma((pairs, 8)),
            pltpu.VMEM((rows, width), BF),
            pltpu.VMEM((width, 3 * width), BF),
            pltpu.VMEM((rows, width), F32),
            dma((3 + pairs,)),
            pltpu.VMEM((rows, 3 * width), BF),
            pltpu.VMEM((width, rows), BF),
            pltpu.VMEM((pairs * TAIL_ROWS, 3 * LANES), BF),
            pltpu.VMEM((rows, width), BF),
            pltpu.VMEM((hops,) + small.shape, F32),
            pltpu.VMEM((hops,) + diagonals.shape, F32),
            dma((2, 2, hops)),
            dma((3,)),
        ]
        + [piece for pieces in scratch for piece in pieces],
        compiler_params=pltpu.CompilerParams(
            collective_id=0, has_side_effects=True, vmem_limit_bytes=62 * MIB
        ),
        name="summed_with_attention_back",
    )(meta_columns, meta_rows, projected, mixed, d_mixed, logs, *wide_arrays,
      small, item, qkv_weight, d_hidden, grad_down, grad_up, grad_out)
    span = 4 * depth
    if size > span:
        groups = [list(range(first, size, span)) for first in range(span)]
        main, tail, small, diagonals = lax.psum(
            (main.astype(F32), tail.astype(F32), small, diagonals), "dp",
            axis_index_groups=groups,
        )
        main, tail = main.astype(BF), tail.astype(BF)
    return main, tail, small, diagonals, grad_input


def per_device(
    layer_in, segment, key_mask, position, layout_x, layout_y,
    qkv_weight, query_bias, value_bias, out_weight, out_bias, attn_gain, attn_shift,
    up_weight, up_bias, down_weight, down_bias, ffn_gain, ffn_shift,
    text_table, horiz_table, vert_table, cotangent,
):
    width = layer_in.shape[-1]
    item, projected, meta_columns, meta_rows, table_rows = projected_item(
        layer_in, (segment, key_mask, position, layout_x, layout_y),
        qkv_weight, query_bias, value_bias, (text_table, horiz_table, vert_table),
    )
    mixed, logs, *wide_arrays = attention_forward(meta_columns, meta_rows, table_rows, projected, width)
    layer_out, d_hidden, d_mixed, grad_out, grad_down, grad_up, small = fed_forward_and_back(
        item, mixed, cotangent, out_weight, up_weight, down_weight,
        (out_bias, attn_gain, attn_shift, up_bias, down_bias, ffn_gain, ffn_shift),
    )
    main, tail, small, diagonals, grad_input = summed_with_attention_back(
        meta_columns, meta_rows, projected, mixed, d_mixed, logs, wide_arrays, item, qkv_weight,
        d_hidden, small, grad_down, grad_up, grad_out,
    )
    done = finished(
        main, tail, grad_input, small, diagonals, up_weight.shape[1], text_table.shape[0]
    )
    sum_down, sum_up, sum_out, sum_qkv, grad_input = done[:5]
    singles, tables = done[5:14], [t.T for t in done[14:]]
    return (
        layer_out, grad_input, sum_qkv, singles[0], singles[1], sum_out, singles[2], singles[3],
        singles[4], sum_up, singles[8], sum_down, singles[5], singles[6], singles[7],
        tables[0], tables[1], tables[2],
    )


def solution(mesh):
    rows = P("dp", "seq", None)
    marks_spec = P("dp", "seq")
    return jax.shard_map(
        per_device,
        mesh=mesh,
        in_specs=(rows,) + (marks_spec,) * 5 + (P(),) * 16 + (rows,),
        out_specs=(rows, rows) + (P(),) * 16,
        check_vma=False,
    )
```

```python
import functools

import jax
import jax.numpy as jnp
from jax import lax
from jax.experimental import pallas as pl
from jax.experimental.pallas import tpu as pltpu
from jax.sharding import PartitionSpec as P

BF = jnp.bfloat16
F32 = jnp.float32
BIG = 1e30
LANES = 128
HEAD = 64
TEXT = 512
POS = 64
COORD = 48
Y0 = 64
GROUP0 = 112
MEMBER0 = 116
FLAG = 124
EVERY = 125
STRAY = 126
X_TABLE = 33
Y_TABLE = 66
NOTHING = 127


def dot_nt(a, b):
    return lax.dot_general(a, b, (((1,), (1,)), ((), ())), preferred_element_type=F32)


def dot_nn(a, b):
    return lax.dot_general(a, b, (((1,), (0,)), ((), ())), preferred_element_type=F32)


def looked_up(table_row, index):
    rows = index.shape[0]
    return jnp.take_along_axis(
        jnp.broadcast_to(table_row, (rows, LANES)), index, axis=1, mode="promise_in_bounds"
    )


def bucket(distance):
    return jnp.clip(distance, -16, 16) + 16


def between(lane, low, high):
    return (lane >= low) & (lane < high)


def columns_of(meta_ref):
    return tuple(meta_ref[:, field : field + 1] for field in range(5))


def marks(meta_ref):
    segment, key_mask, position, across, down = columns_of(meta_ref)
    rows = segment.shape[0]
    lane = lax.broadcasted_iota(jnp.int32, (rows, LANES), 1)
    row = lax.broadcasted_iota(jnp.int32, (rows, LANES), 0)
    even = between(lane, HEAD, HEAD + COORD) & (lane - HEAD == across)
    odd = (lane < COORD) & (lane == across)
    group = (segment - 1) >> 3
    member = (segment - 1) & 7
    named = segment > 0
    shared = (
        ((row < TEXT) & (lane < POS) & (lane == position))
        | (between(lane, Y0, Y0 + COORD) & (lane - Y0 == down))
        | (named & between(lane, GROUP0, MEMBER0) & (lane - GROUP0 == group))
        | (named & between(lane, MEMBER0, FLAG) & (lane - MEMBER0 == member))
        | ((lane == FLAG) & (key_mask <= 0))
        | (lane == EVERY)
        | ((lane == STRAY) & (segment < 0))
    )
    return tuple(jnp.where(m, 1.0, 0.0).astype(BF) for m in (even, odd, shared))


def square_lanes():
    shape = (LANES, LANES)
    return lax.broadcasted_iota(jnp.int32, shape, 0), lax.broadcasted_iota(jnp.int32, shape, 1)


def barred():
    row, lane = square_lanes()
    in_groups = between(lane, GROUP0, MEMBER0)
    shut = (
        (between(row, GROUP0, MEMBER0) & in_groups & (lane != row))
        | (between(row, MEMBER0, FLAG) & between(lane, MEMBER0, FLAG) & (lane != row))
        | ((row == EVERY) & (lane == FLAG))
        | ((row == STRAY) & in_groups)
    )
    return jnp.where(shut, -BIG, 0.0).astype(F32)


def table_index():
    row, lane = square_lanes()
    distance = bucket(row - lane)
    inside = lambda low, high: between(row, low, high) & between(lane, low, high)
    even = jnp.where(inside(HEAD, HEAD + COORD), distance + X_TABLE, NOTHING)
    odd = jnp.where(inside(0, COORD), distance + X_TABLE, NOTHING)
    shared = jnp.where(
        inside(0, POS), distance, jnp.where(inside(Y0, Y0 + COORD), distance + Y_TABLE, NOTHING)
    )
    return even, odd, shared


def image_query_index(meta_ref):
    position = meta_ref[TEXT:, 2:3]
    lane = lax.broadcasted_iota(jnp.int32, (position.shape[0], LANES), 1)
    return jnp.where(lane < POS, bucket(position - lane), NOTHING)


def prepare(meta_ref, mark_refs, bar_ref, index_refs, image_index_ref):
    for ref, value in zip(mark_refs, marks(meta_ref)):
        ref[...] = value
    bar_ref[...] = barred()
    for ref, value in zip(index_refs, table_index()):
        ref[...] = value
    image_index_ref[...] = image_query_index(meta_ref)


def own_lanes(parity, rows):
    lane = lax.broadcasted_iota(jnp.int32, (rows, LANES), 1)
    return (lane < HEAD) if parity == 0 else (lane >= HEAD)


def widened(parity, q, table_row, bias, bar_ref, index_refs, image_index_ref, mark_refs):
    rows = q.shape[0]
    shared = mark_refs[2][...]
    across = looked_up(table_row, index_refs[parity][...]).astype(BF)
    first = jnp.where(
        own_lanes(parity, rows), q.astype(F32) * 0.125, dot_nn(mark_refs[parity][...], across)
    )
    others = (looked_up(table_row, index_refs[2][...]) + bar_ref[...]).astype(BF)
    second = dot_nn(shared, others)
    on_images = looked_up(table_row, image_index_ref[...])
    second = jnp.concatenate([second[:TEXT], second[TEXT:] + on_images], axis=0)
    image_lane = lax.broadcasted_iota(jnp.int32, on_images.shape, 1)
    key_image = jnp.where(image_lane < POS, bias[:, :LANES].astype(BF), shared[TEXT:])
    return first.astype(BF), second.astype(BF), key_image


def joined(parity, first, second, key_image, k, marks_own, shared):
    rows = k.shape[0]
    lane = lax.broadcasted_iota(jnp.int32, (rows, LANES), 1)
    to_image = jnp.where(lane < POS, shared, second)
    key_first = jnp.where(own_lanes(parity, rows), k, marks_own)
    q_text = jnp.concatenate([first, second], axis=1)
    q_image = jnp.concatenate([first, to_image], axis=1)
    k_text = jnp.concatenate([key_first[:TEXT], shared[:TEXT]], axis=1)
    k_image = jnp.concatenate([key_first[TEXT:], key_image], axis=1)
    return q_text, q_image, k_text, k_image


def near(start, size):
    if start >= TEXT:
        return slice(0, TEXT)
    return slice(max(0, start - LANES), min(TEXT, start + size + LANES))


def image_bias(table_row, offsets):
    return jnp.concatenate(
        [looked_up(table_row, offsets[:, :LANES]), looked_up(table_row, offsets[:, LANES:])], axis=1
    )


def forward_kernel(
    meta_ref, rows_ref, table_ref, q_ref, k_ref, v_ref,
    mixed_ref, log_ref, first_ref, second_ref, key_image_ref, bias_ref,
    even_ref, odd_ref, shared_ref, bar_ref, index_even, index_odd, index_shared, image_index_ref,
):
    mark_refs = (even_ref, odd_ref, shared_ref)
    index_refs = (index_even, index_odd, index_shared)

    @pl.when(pl.program_id(0) == 0)
    def _():
        prepare(meta_ref, mark_refs, bar_ref, index_refs, image_index_ref)

    rows = q_ref.shape[0]
    images = rows - TEXT
    q, k, v = q_ref[...], k_ref[...], v_ref[...]
    offsets = bucket(rows_ref[2:3, TEXT:] - meta_ref[TEXT:, 2:3])
    tile = 256
    v_turned = transposed(v)
    heads = [None, None]

    def prepared(parity):
        table_row = table_ref[pl.ds(2 * pl.program_id(0) + parity, 1), :]
        bias = image_bias(table_row, offsets)
        first, second, key_image = widened(
            parity, q, table_row, bias, bar_ref, index_refs, image_index_ref, mark_refs
        )
        first_ref[parity] = first
        second_ref[parity] = second
        key_image_ref[parity] = key_image
        bias_ref[parity] = bias.astype(BF)
        wide = joined(
            parity, first, second, key_image, k, mark_refs[parity][...], shared_ref[...]
        )
        heads[parity] = wide + (bias,)

    def scored(parity, start):
        q_text, q_image, k_text, k_image, bias = heads[parity]
        here = slice(start, start + tile)
        on_image = dot_nt(k_image, q_image[here])
        if start >= TEXT:
            on_image = on_image + bias[:, start - TEXT : start - TEXT + tile]
        return dot_nt(k_text[near(start, tile)], q_text[here]), on_image

    spots = [(parity, start) for parity in range(2) for start in range(0, rows, tile)]
    outs = ([], [])
    prepared(0)
    following = scored(*spots[0])
    for index, (parity, start) in enumerate(spots):
        on_text, on_image = following
        if index == 1:
            prepared(1)
        if index + 1 < len(spots):
            following = scored(*spots[index + 1])
        top = jnp.maximum(
            jnp.max(on_text, axis=0, keepdims=True), jnp.max(on_image, axis=0, keepdims=True)
        )
        on_text = jnp.exp(on_text - top)
        on_image = jnp.exp(on_image - top)
        total = jnp.sum(on_text, axis=0, keepdims=True) + jnp.sum(on_image, axis=0, keepdims=True)
        own = slice(parity * HEAD, parity * HEAD + HEAD)
        out = dot_nn(v_turned[own, near(start, tile)], on_text.astype(BF)) + dot_nn(
            v_turned[own, TEXT:], on_image.astype(BF)
        )
        outs[parity].append(out * (1.0 / total))
        log_ref[0, parity : parity + 1, start : start + tile] = top + jnp.log(total)
    mixed_ref[...] = jnp.transpose(
        jnp.concatenate([jnp.concatenate(outs[parity], axis=1) for parity in range(2)], axis=0)
    )


def static_scratch(rows):
    square = (LANES, LANES)
    return [
        pltpu.VMEM((rows, LANES), BF),
        pltpu.VMEM((rows, LANES), BF),
        pltpu.VMEM((rows, LANES), BF),
        pltpu.VMEM(square, F32),
        pltpu.VMEM(square, jnp.int32),
        pltpu.VMEM(square, jnp.int32),
        pltpu.VMEM(square, jnp.int32),
        pltpu.VMEM((rows - TEXT, LANES), jnp.int32),
    ]


def attention_forward(meta_columns, meta_rows, table_rows, projected, width):
    rows = projected.shape[0]
    images = rows - TEXT
    pairs = width // LANES

    def block(part):
        return pl.BlockSpec((rows, LANES), lambda p: (0, part * pairs + p))

    whole = lambda shape: pl.BlockSpec(shape, lambda p: (0,) * len(shape))
    return pl.pallas_call(
        forward_kernel,
        grid=(pairs,),
        in_specs=[
            whole(meta_columns.shape),
            whole(meta_rows.shape),
            whole(table_rows.shape),
            block(0), block(1), block(2),
        ],
        out_specs=[
            pl.BlockSpec((rows, LANES), lambda p: (0, p)),
            pl.BlockSpec((1, 2, rows), lambda p: (p, 0, 0)),
            pl.BlockSpec((2, rows, LANES), lambda p: (p, 0, 0)),
            pl.BlockSpec((2, rows, LANES), lambda p: (p, 0, 0)),
            pl.BlockSpec((2, images, LANES), lambda p: (p, 0, 0)),
            pl.BlockSpec((2, images, images), lambda p: (p, 0, 0)),
        ],
        out_shape=[
            jax.ShapeDtypeStruct((rows, width), F32),
            jax.ShapeDtypeStruct((pairs, 2, rows), F32),
            jax.ShapeDtypeStruct((2 * pairs, rows, LANES), BF),
            jax.ShapeDtypeStruct((2 * pairs, rows, LANES), BF),
            jax.ShapeDtypeStruct((2 * pairs, images, LANES), BF),
            jax.ShapeDtypeStruct((2 * pairs, images, images), BF),
        ],
        scratch_shapes=static_scratch(rows),
        compiler_params=pltpu.CompilerParams(vmem_limit_bytes=60 * 1024 * 1024),
        name="attention_forward",
    )(meta_columns, meta_rows, table_rows, projected, projected, projected)


def skewed(block):
    size = block.shape[0]
    lane = lax.broadcasted_iota(jnp.int32, (size, LANES), 1)
    row = lax.broadcasted_iota(jnp.int32, (size, LANES), 0)
    turned = jnp.take_along_axis(
        block, (lane + row) & (LANES - 1), axis=1, mode="promise_in_bounds"
    )
    straight = lane + row < LANES
    above = jnp.sum(jnp.where(straight, turned, 0.0), axis=0, keepdims=True)
    below = jnp.sum(jnp.where(straight, 0.0, turned), axis=0, keepdims=True)
    return above, below


def transposed(array):
    return jnp.transpose(array.astype(F32)).astype(array.dtype)


def static_prepare(meta_ref, static):
    for ref, turned, value in zip(static[:3], static[3:], marks(meta_ref)):
        ref[...] = value
        turned[...] = transposed(value)


def head_back(
    parity, pair, rows_ref, wide_refs, k_ref, v_ref, mixed_ref, grad_ref, log_ref, static, diag_ref,
):
    mark_refs, turned_refs = static[:3], static[3:]
    first_ref, second_ref, key_image_ref, bias_ref = wide_refs
    head = 2 * pair + parity
    shared_t = turned_refs[2]
    rows = k_ref.shape[1]
    images = rows - TEXT
    tile = 256
    k, v, grad = k_ref[pair], v_ref[pair], grad_ref[pair]
    products = grad.astype(F32) * mixed_ref[pair]
    k_turned = transposed(k)
    is_image = rows_ref[1:2, TEXT:] > 0
    own = own_lanes(parity, rows)
    log_row = log_ref[pair, parity : parity + 1, :]
    first, shared = first_ref[head], mark_refs[2][...]
    q_text, q_image, k_text, k_image = joined(
        parity, first, second_ref[head], key_image_ref[head], k, mark_refs[parity][...], shared
    )
    bias = bias_ref[head].astype(F32)
    ones = jnp.where(own_lanes(parity, 8), 1.0, 0.0).astype(BF)
    delta = jnp.zeros((8, rows), F32)
    rest = products
    for _ in range(3):
        piece = rest.astype(BF)
        delta = delta + dot_nt(ones, piece)
        rest = rest - piece.astype(F32)
    delta = delta[0:1]
    v_own = jnp.where(own, v, jnp.zeros_like(v))
    q_marked = jnp.concatenate(
        [jnp.where(own, first, mark_refs[parity][...]), shared], axis=1
    )
    dq_text = jnp.zeros((HEAD, TEXT), F32)
    dq_image = jnp.zeros((HEAD, images), F32)
    dks = []
    dvs = []
    first_sum = jnp.zeros((LANES, LANES), F32)
    second_sum = jnp.zeros((LANES, LANES), F32)
    text_image = jnp.zeros((LANES, images), F32)

    def met(start, array, axis=0):
        text = near(start, tile)
        if axis == 0:
            return jnp.concatenate([array[text], array[TEXT:]], axis=0)
        return jnp.concatenate([array[:, text], array[:, TEXT:]], axis=1)

    def scored(start):
        here = slice(start, start + tile)
        if start < TEXT:
            scores = dot_nt(k_text[here], met(start, q_text))
        else:
            scores = dot_nt(k_image[start - TEXT : start - TEXT + tile], q_image)
            scores = jnp.concatenate([scores[:, :TEXT], scores[:, TEXT:] + bias], axis=1)
        return scores, dot_nt(v_own[here], met(start, grad))

    following = scored(0)
    for start in range(0, rows, tile):
        here = slice(start, start + tile)
        scores, prob_grad = following
        if start + tile < rows:
            following = scored(start + tile)
        soft = jnp.exp(scores - met(start, log_row, 1))
        score_grad = soft * (prob_grad - met(start, delta, 1))
        low = score_grad.astype(BF)
        dvs.append(dot_nn(soft.astype(BF), met(start, grad)))
        wide = dot_nn(low, met(start, q_marked))
        dks.append(wide[:, :LANES])
        part = dot_nn(k_turned[parity * HEAD : parity * HEAD + HEAD, here], low)
        text = near(start, tile)
        count = text.stop - text.start
        before = [jnp.zeros((HEAD, text.start), F32)] if text.start > 0 else []
        after = [jnp.zeros((HEAD, TEXT - text.stop), F32)] if text.stop < TEXT else []
        dq_text = dq_text + jnp.concatenate(before + [part[:, :count]] + after, axis=1)
        dq_image = dq_image + part[:, count:]
        rounded = wide.astype(BF)
        first_sum = first_sum + dot_nn(turned_refs[parity][:, here], rounded[:, :LANES])
        second_sum = second_sum + dot_nn(shared_t[:, here], rounded[:, LANES:])
        if start < TEXT:
            text_image = text_image + dot_nn(shared_t[:, here], low[:, count:])
        else:
            by_position = wide[:, LANES:]
            on_image = score_grad[:, TEXT:]
    dq = jnp.concatenate([dq_text, dq_image], axis=1)
    small = lax.broadcasted_iota(jnp.int32, (LANES, LANES), 1)
    small_row = lax.broadcasted_iota(jnp.int32, (LANES, LANES), 0)
    x0 = HEAD if parity == 0 else 0
    x_block = jnp.where(
        between(small, x0, x0 + COORD) & between(small_row, x0, x0 + COORD), first_sum, 0.0
    )
    y_block = jnp.where(
        between(small, Y0, Y0 + COORD) & between(small_row, Y0, Y0 + COORD), second_sum, 0.0
    )
    p_block = jnp.where((small < POS) & (small_row < POS), second_sum, 0.0)
    wide_lane = lax.broadcasted_iota(jnp.int32, (images, images), 1)
    outside = jnp.sum(jnp.where(is_image, 0.0, on_image), axis=1, keepdims=True)
    pairs = jnp.where(is_image, on_image, 0.0) + jnp.where(wide_lane == 0, outside, 0.0)
    outside_text = jnp.sum(jnp.where(is_image, 0.0, text_image), axis=1, keepdims=True)
    text_lane = lax.broadcasted_iota(jnp.int32, (LANES, images), 1)
    text_row = lax.broadcasted_iota(jnp.int32, (LANES, images), 0)
    text_image = jnp.where(is_image, text_image, 0.0) + jnp.where(
        text_lane == 0, outside_text, 0.0
    )
    text_image = jnp.where(text_row < POS, text_image, 0.0)
    first_lane = lax.broadcasted_iota(jnp.int32, (images, LANES), 1)
    left = pairs[:, :LANES] + jnp.where(first_lane < POS, by_position, 0.0)
    right = pairs[:, LANES:]
    a00, b00 = skewed(left[:LANES] + text_image[:, :LANES] + p_block)
    a01, b01 = skewed(right[:LANES] + text_image[:, LANES:])
    a10, b10 = skewed(left[LANES:])
    a11, b11 = skewed(right[LANES:])
    ax, bx = skewed(x_block)
    ay, by = skewed(y_block)
    diag_ref[head] = jnp.concatenate(
        [b10, b00 + b11 + a10, a00 + a11 + b01, a01, bx, ax, by, ay], axis=0
    )
    return dq * 0.125, jnp.concatenate(dks, axis=0), jnp.concatenate(dvs, axis=0)


MESH = pl.DeviceIdType.MESH
VMEM = pl.BlockSpec(memory_space=pltpu.VMEM)
HBM = pl.BlockSpec(memory_space=pltpu.HBM)
MIB = 1024 * 1024


def remote(src, dst, send, receive, device):
    return pltpu.make_async_remote_copy(
        src_ref=src, dst_ref=dst, send_sem=send, recv_sem=receive, device_id=device,
        device_id_type=MESH,
    )


def project_kernel(
    layer_ref, weight_hbm, *refs,
):
    small_hbm, refs = refs[:10], refs[10:]
    (item_ref, projected_out, columns_ref, rows_ref, table_ref,
     projected_ref, weight_ref, meta_send, bias_ref, sems, load_sems, store_sems), small = (
        refs[:12], refs[12:],
    )
    (segment_ref, mask_ref, position_ref, across_ref, down_ref, query_bias_ref, value_bias_ref,
     text_ref, horiz_ref, vert_ref) = small
    mine = lax.axis_index("seq")
    partner = (1 - mine, lax.axis_index("dp"))
    count, width = layer_ref.shape[1:]
    own = pl.ds(pl.multiple_of(mine * count, LANES), count)
    loads = [
        pltpu.make_async_copy(source, target, load_sems.at[index])
        for index, (source, target) in enumerate(
            list(zip(small_hbm, small))
            + [(layer_ref.at[mine], item_ref.at[own]), (weight_hbm, weight_ref)]
        )
    ]
    for load in loads:
        load.start()
    barrier = pltpu.get_barrier_semaphore()
    pl.semaphore_signal(barrier, inc=1, device_id=partner, device_id_type=MESH)
    pl.semaphore_wait(barrier, 1)
    pieces = count // LANES
    rows_out = [
        remote(
            layer_ref.at[1 - mine, pl.ds(piece * LANES, LANES)],
            item_ref.at[pl.ds(pl.multiple_of(mine * count + piece * LANES, LANES), LANES)],
            sems.at[0, piece], sems.at[1, piece], partner,
        )
        for piece in range(pieces)
    ]
    for copy in rows_out:
        copy.start()
    for load in loads[:-2]:
        load.wait()

    fields = (segment_ref, mask_ref, position_ref, across_ref, down_ref)
    blocks = [
        jnp.concatenate(
            [field[item : item + 1, :] for field in fields] + [jnp.zeros((3, count), jnp.int32)],
            axis=0,
        )
        for item in range(2)
    ]
    meta_send[...] = jnp.where(mine == 0, blocks[1], blocks[0])
    meta_out = remote(
        meta_send, rows_ref.at[:, own], sems.at[0, pieces], sems.at[1, pieces], partner
    )
    meta_out.start()
    rows_ref[:, own] = jnp.where(mine == 0, blocks[0], blocks[1])
    bias_ref[:, :width] = query_bias_ref[...].astype(F32).reshape(1, width)
    bias_ref[:, width : 2 * width] = jnp.zeros((1, width), F32)
    bias_ref[:, 2 * width :] = value_bias_ref[...].astype(F32).reshape(1, width)
    heads, levels = text_ref.shape
    spot = lax.broadcasted_iota(jnp.int32, (levels, LANES), 1)
    level = lax.broadcasted_iota(jnp.int32, (levels, LANES), 0)
    table = jnp.zeros((heads, LANES), F32)
    for source, begin in ((text_ref, 0), (horiz_ref, X_TABLE), (vert_ref, Y_TABLE)):
        table = table + dot_nn(source[...], (spot == level + begin).astype(BF))
    table_ref[...] = jnp.concatenate([table, jnp.zeros((16 - heads, LANES), F32)], axis=0)

    def project(there):
        step = 256

        def body(index, carry):
            columns = pl.ds(pl.multiple_of(index * step, step), step)
            product = dot_nn(item_ref[there], weight_ref[:, columns])
            projected_ref[there, columns] = (product + bias_ref[:, columns]).astype(BF)
            return carry

        lax.fori_loop(0, 3 * width // step, body, 0)

    def stored(index, there):
        return pltpu.make_async_copy(
            projected_ref.at[there], projected_out.at[there], store_sems.at[index]
        )

    for load in loads[-2:]:
        load.wait()
    project(own)
    stored(0, own).start()
    for piece in range(pieces):
        rows_out[piece].wait()
        there = pl.ds(pl.multiple_of((1 - mine) * count + piece * LANES, LANES), LANES)
        project(there)
        stored(1 + piece, there).start()
    meta_out.wait()
    meta = rows_ref[...].astype(F32)
    tall = jnp.concatenate([meta, jnp.zeros((LANES - 8, meta.shape[1]), F32)], axis=0)
    columns_ref[...] = jnp.transpose(tall).astype(jnp.int32)
    stored(0, own).wait()
    for piece in range(pieces):
        there = pl.ds(pl.multiple_of((1 - mine) * count + piece * LANES, LANES), LANES)
        stored(1 + piece, there).wait()


def projected_item(layer_in, fields, qkv_weight, query_bias, value_bias, tables):
    rows = 2 * layer_in.shape[1]
    width = layer_in.shape[2]
    pieces = rows // 2 // LANES
    small = list(fields) + [query_bias, value_bias] + [t.T for t in tables]
    return pl.pallas_call(
        project_kernel,
        in_specs=[HBM] * (2 + len(small)),
        out_specs=[VMEM, HBM, VMEM, VMEM, VMEM],
        out_shape=[
            jax.ShapeDtypeStruct((rows, width), BF),
            jax.ShapeDtypeStruct((rows, 3 * width), BF),
            jax.ShapeDtypeStruct((rows, LANES), jnp.int32),
            jax.ShapeDtypeStruct((8, rows), jnp.int32),
            jax.ShapeDtypeStruct((16, LANES), F32),
        ],
        scratch_shapes=[
            pltpu.VMEM((rows, 3 * width), BF),
            pltpu.VMEM((width, 3 * width), BF),
            pltpu.VMEM((8, rows // 2), jnp.int32),
            pltpu.VMEM((1, 3 * width), F32),
            pltpu.SemaphoreType.DMA((2, pieces + 1)),
            pltpu.SemaphoreType.DMA((len(small) + 2,)),
            pltpu.SemaphoreType.DMA((pieces + 1,)),
        ]
        + [pltpu.VMEM(array.shape, array.dtype) for array in small],
        compiler_params=pltpu.CompilerParams(
            collective_id=1, has_side_effects=True, vmem_limit_bytes=60 * MIB
        ),
        name="projected_item",
    )(layer_in, qkv_weight, *small)


EPSILON = 1e-05
TILE = 256


def vector(ref):
    return ref[...].astype(F32).reshape(1, ref.shape[0])


def gelu_and_slope(x):
    bell = jnp.exp2(-0.7213475204444817 * (x * x))
    rough = 1.0 + 0.23164188826 * jnp.abs(x)
    t = pl.reciprocal(rough, approx=True)
    t = t * (2.0 - rough * t)
    series = t * (
        0.127414796
        + t * (-0.142248368 + t * (0.7107068705 + t * (-0.7265760135 + t * 0.5307027145)))
    )
    tail = bell * series
    below = jnp.where(x >= 0.0, 1.0 - tail, tail)
    return x * below, below + x * (0.3989422804014327 * bell)


def row_mean(block):
    return jnp.mean(block, axis=1, keepdims=True)


def normalized(hidden):
    center = hidden - row_mean(hidden)
    scale = lax.rsqrt(row_mean(center * center) + EPSILON)
    return center * scale, scale


def norm_pulled(grad, unit, scale):
    return scale * (grad - row_mean(grad) - unit * row_mean(grad * unit))


def column_sum(block):
    return jnp.sum(block, axis=0, keepdims=True)


def feed_kernel(
    item_hbm, mixed_hbm, cotangent_ref, out_weight_ref, up_ref, down_ref, *refs,
):
    vectors_hbm, refs = refs[:7], refs[7:]
    (layer_out, total_out, unit_out, scale_out, grad_down_ref, grad_up_ref, small_ref,
     item_ref, mixed_ref, layer_ref, cotangent_all, active, slope, unit, scale_ref, normed, normed_t, total, d_branch, d_branch_t,
     sems, load_sems, tile_sems, store_sems) = refs[:24]
    vectors = refs[24:]
    (out_bias_ref, attn_gain_ref, attn_shift_ref, up_bias_ref, down_bias_ref, ffn_gain_ref,
     ffn_shift_ref) = vectors
    step = pl.program_id(0)
    blocks = pl.num_programs(0) // 2
    rows, width = item_hbm.shape
    count = rows // 2
    mine = lax.axis_index("seq")
    partner = (1 - mine, lax.axis_index("dp"))
    own = pl.ds(pl.multiple_of(mine * count, LANES), count)
    tiles = rows // TILE

    def sent():
        return remote(
            cotangent_ref.at[1 - mine], cotangent_all.at[own], sems.at[0], sems.at[1], partner
        )

    def returned():
        theirs = pl.ds(pl.multiple_of((1 - mine) * count, LANES), count)
        return [
            pltpu.make_async_copy(layer_ref.at[own], layer_out.at[mine], load_sems.at[8]),
            remote(
                layer_ref.at[theirs], layer_out.at[mine], sems.at[2], sems.at[3], partner
            ),
        ]

    def tile_loads(tile):
        there = pl.ds(tile * TILE, TILE)
        return [
            pltpu.make_async_copy(source.at[there], target.at[there], tile_sems.at[index, tile])
            for index, (source, target) in enumerate(
                ((mixed_hbm, mixed_ref), (item_hbm, item_ref))
            )
        ]

    def store(index):
        source, target = (
            (total, total_out), (unit, unit_out), (scale_ref, scale_out),
        )[index]
        return pltpu.make_async_copy(source, target, store_sems.at[index])

    def loads():
        copies = list(zip(vectors_hbm, vectors)) + [(cotangent_ref.at[mine], cotangent_all.at[own])]
        return [
            pltpu.make_async_copy(source, target, load_sems.at[index])
            for index, (source, target) in enumerate(copies)
        ]

    def over_tiles(size, body, carry, unroll=1):
        def run(index, state):
            return body(pl.ds(pl.multiple_of(index * size, size), size), state)

        return lax.fori_loop(0, rows // size, run, carry, unroll=unroll)

    @pl.when(step == 0)
    def _():
        for index in range(rows // TILE):
            for load in tile_loads(index):
                load.start()
        for load in loads():
            load.start()
        barrier = pltpu.get_barrier_semaphore()
        pl.semaphore_signal(barrier, inc=1, device_id=partner, device_id_type=MESH)
        pl.semaphore_wait(barrier, 1)
        sent().start()
        small_ref[...] = jnp.zeros_like(small_ref)
        for load in loads():
            load.wait()
        out_bias, gain, shift = vector(out_bias_ref), vector(attn_gain_ref), vector(attn_shift_ref)

        for index in range(rows // TILE):
            for load in tile_loads(index):
                load.wait()
            there = slice(index * TILE, index * TILE + TILE)
            attn = dot_nn(mixed_ref[there].astype(BF), out_weight_ref[...]) + out_bias
            standard, scale = normalized(item_ref[there].astype(F32) + attn)
            unit[there] = standard
            scale_ref[there] = jnp.broadcast_to(scale, (TILE, LANES))
            result = standard * gain + shift
            normed[there] = result.astype(BF)
            normed_t[:, there] = jnp.transpose(result).astype(BF)
        store(1).start()
        store(2).start()
        total[...] = jnp.zeros_like(total)

    @pl.when(step < blocks)
    def _():
        columns = [slice(begin, begin + TILE) for begin in range(0, width, TILE)]
        low = normed[...]
        following = dot_nn(low, up_ref[:, columns[0]])
        values = []
        for index, here in enumerate(columns):
            product = following
            if index + 1 < len(columns):
                following = dot_nn(low, up_ref[:, columns[index + 1]])
            bias = up_bias_ref[pl.ds(pl.multiple_of(step * width + here.start, LANES), TILE)]
            value, grade = gelu_and_slope(product + bias.astype(F32).reshape(1, TILE))
            values.append(value.astype(BF))
            active[step, :, here] = values[-1]
            slope[step, :, here] = grade.astype(BF)
        values = jnp.concatenate(values, axis=1)
        for here in columns:
            total[:, here] += dot_nn(values, down_ref[:, here])

    @pl.when(step == blocks)
    def _():
        sent().wait()
        gain, shift, bias = vector(ffn_gain_ref), vector(ffn_shift_ref), vector(down_bias_ref)
        first_gain, first_shift = vector(attn_gain_ref), vector(attn_shift_ref)

        def tile(there, sums):
            hidden = unit[there] * first_gain + first_shift + (total[there] + bias)
            standard, scale = normalized(hidden)
            layer_ref[there] = (standard * gain + shift).astype(BF)
            cotangent = cotangent_all[there].astype(F32)
            pulled = norm_pulled(cotangent * gain, standard, scale)
            total[there] = pulled
            low = pulled.astype(BF)
            d_branch[there] = low
            return (
                sums[0] + column_sum(low.astype(F32)),
                sums[1] + column_sum(cotangent * standard),
                sums[2] + column_sum(cotangent),
            )

        zero = jnp.zeros((1, width), F32)
        sums = over_tiles(64, tile, (zero, zero, zero), 4)
        for row, value in zip((5, 6, 7), sums):
            small_ref[row : row + 1] = value

        for copy in returned():
            copy.start()

        def turn(there, carry):
            d_branch_t[:, there] = jnp.transpose(d_branch[there].astype(F32)).astype(BF)
            return carry

        over_tiles(TILE, turn, 0, 3)

    @pl.when(step >= blocks)
    def _():
        block = step - blocks

        columns = [slice(begin, begin + TILE) for begin in range(0, width, TILE)]
        branch = d_branch[...]
        turned = d_branch_t[...]
        following = dot_nt(branch, down_ref[columns[0]])
        values = []
        for index, here in enumerate(columns):
            product = following
            if index + 1 < len(columns):
                following = dot_nt(branch, down_ref[columns[index + 1]])
            grad_down_ref[:, here] = dot_nn(turned, active[block, :, here]).astype(BF)
            d_up = (product * slope[block, :, here].astype(F32)).astype(BF)
            small_ref[pl.ds(8 + block, 1), here] = column_sum(d_up.astype(F32))
            values.append(d_up)
        values = jnp.concatenate(values, axis=1)
        turned = normed_t[...]
        for here in columns:
            grad_up_ref[:, here] = dot_nn(turned, values[:, here]).astype(BF)
            total[:, here] += dot_nt(values, up_ref[here])

    @pl.when(step == 2 * blocks - 1)
    def _():
        store(0).start()
        for copy in returned() + [store(0), store(1), store(2)]:
            copy.wait()


def fed_forward_and_back(
    item, mixed, cotangent, out_weight, up_weight, down_weight, vectors,
):
    rows, width = item.shape
    blocks = up_weight.shape[1] // width
    whole = pl.BlockSpec(memory_space=pltpu.VMEM)
    square = lambda kind: jax.ShapeDtypeStruct((rows, width), kind)
    later = lambda i: jnp.maximum(i - blocks, 0)
    return pl.pallas_call(
        feed_kernel,
        grid=(2 * blocks,),
        in_specs=[HBM, HBM, HBM, whole]
        + [
            pl.BlockSpec((width, width), lambda i: (0, lax.rem(i, blocks))),
            pl.BlockSpec((width, width), lambda i: (lax.rem(i, blocks), 0)),
        ]
        + [HBM] * 7,
        out_specs=[HBM] * 4
        + [
            pl.BlockSpec((width, width), lambda i: (later(i), 0)),
            pl.BlockSpec((width, width), lambda i: (later(i), 0)),
            whole,
        ],
        out_shape=[
            jax.ShapeDtypeStruct((2, rows // 2, width), BF), square(F32), square(F32),
            jax.ShapeDtypeStruct((rows, LANES), F32),
            jax.ShapeDtypeStruct((blocks * width, width), BF),
            jax.ShapeDtypeStruct((blocks * width, width), BF),
            jax.ShapeDtypeStruct((16, width), F32),
        ],
        scratch_shapes=[
            pltpu.VMEM((rows, width), BF),
            pltpu.VMEM((rows, width), F32),
            pltpu.VMEM((rows, width), BF),
            pltpu.VMEM((rows, width), BF),
            pltpu.VMEM((blocks, rows, width), BF),
            pltpu.VMEM((blocks, rows, width), BF),
            pltpu.VMEM((rows, width), F32),
            pltpu.VMEM((rows, LANES), F32),
            pltpu.VMEM((rows, width), BF),
            pltpu.VMEM((width, rows), BF),
            pltpu.VMEM((rows, width), F32),
            pltpu.VMEM((rows, width), BF),
            pltpu.VMEM((width, rows), BF),
            pltpu.SemaphoreType.DMA((4,)),
            pltpu.SemaphoreType.DMA((9,)),
            pltpu.SemaphoreType.DMA((2, rows // TILE)),
            pltpu.SemaphoreType.DMA((3,)),
        ]
        + [pltpu.VMEM(vector.shape, vector.dtype) for vector in vectors],
        compiler_params=pltpu.CompilerParams(
            collective_id=2, has_side_effects=True, vmem_limit_bytes=60 * MIB
        ),
        name="feed_forward",
    )(item, mixed, cotangent, out_weight, up_weight, down_weight, *vectors)


SLOTS = 4


def finish_kernel(
    main_ref, tail_ref, input_hbm, small_ref, diagonal_ref,
    down_ref, up_ref, out_ref, qkv_ref, input_ref, *refs,
):
    singles, (main_in, tail_in, slots, input_in, input_slot, in_sems, out_sems, item_sems) = (
        refs[:12], refs[12:],
    )
    mains, width = main_in.shape[0], main_in.shape[2]
    pairs, across = tail_in.shape[0], tail_in.shape[2]
    hidden = mains // 2
    blocks = mains + pairs

    def load(block):
        if block < mains:
            source, target = main_ref.at[pl.ds(block * width, width)], main_in.at[block]
        else:
            pair = block - mains
            source, target = tail_ref.at[pl.ds(pair * TAIL_ROWS, TAIL_ROWS)], tail_in.at[pair]
        return pltpu.make_async_copy(source, target, in_sems.at[block])

    def stores(block):
        slot, sem = slots.at[block % SLOTS], out_sems.at[block % SLOTS]
        if block < hidden:
            targets = [(slot, down_ref.at[pl.ds(block * width, width)])]
        elif block < mains:
            targets = [(slot, up_ref.at[:, pl.ds((block - hidden) * width, width)])]
        else:
            pair = block - mains
            targets = [
                (
                    slot.at[:, pl.ds(part * LANES, LANES)],
                    qkv_ref.at[:, pl.ds(part * width + pair * LANES, LANES)],
                )
                for part in range(3)
            ]
            down = pl.ds(0, TAIL_ROWS - width)
            targets.append(
                (slot.at[down, pl.ds(across, across)], out_ref.at[out_spot(pair, pairs, width)])
            )
        return [
            pltpu.make_async_copy(source, target, sem.at[index])
            for index, (source, target) in enumerate(targets)
        ]

    load_input = pltpu.make_async_copy(input_hbm, input_in, item_sems.at[0])
    store_input = pltpu.make_async_copy(input_slot, input_ref, item_sems.at[1])
    for block in range(blocks):
        load(block).start()
    load_input.start()
    for block in range(blocks):
        load(block).wait()
        if block >= SLOTS:
            for copy in stores(block - SLOTS):
                copy.wait()
        slot = block % SLOTS
        if block < hidden:
            slots[slot] = jnp.transpose(main_in[block].astype(F32))
        elif block < mains:
            slots[slot] = main_in[block].astype(F32)
        else:
            slots[slot, :, :across] = tail_in[block - mains, :width].astype(F32)
            slots[slot, : TAIL_ROWS - width, across:] = tail_in[block - mains, width:].astype(F32)
        for copy in stores(block):
            copy.start()
    load_input.wait()
    input_slot[...] = input_in[...].astype(F32)
    store_input.start()
    for row in range(8):
        singles[row][...] = small_ref[row]
    for row in range(hidden):
        singles[8][row * width : row * width + width] = small_ref[8 + row]
    heads, levels = singles[9].shape
    diagonals = diagonal_ref[...]
    level = lax.broadcasted_iota(jnp.int32, (LANES, LANES), 1)
    lane = lax.broadcasted_iota(jnp.int32, (LANES, LANES), 0)
    for table, (first, size, skip) in enumerate(((0, 4, 0), (4, 2, 1), (6, 2, 1))):
        total = jnp.zeros((heads, LANES), F32)
        for row in range(size):
            distance = lane + LANES * (row + skip - 2)
            chosen = (bucket(distance) == level).astype(F32)
            total = total + jnp.dot(
                diagonals[:, first + row, :], chosen, preferred_element_type=F32,
                precision=lax.Precision.HIGHEST,
            )
        singles[9 + table][...] = total[:, :levels]
    for block in range(blocks - SLOTS, blocks):
        for copy in stores(block):
            copy.wait()
    store_input.wait()


def finished(main, tail, grad_input, small, diagonals, hidden, levels):
    width = main.shape[1]
    heads = diagonals.shape[0]
    mains = main.shape[0] // width
    pairs = tail.shape[0] // TAIL_ROWS
    single = jax.ShapeDtypeStruct((width,), F32)
    table = jax.ShapeDtypeStruct((heads, levels), F32)
    dma = pltpu.SemaphoreType.DMA
    return pl.pallas_call(
        finish_kernel,
        in_specs=[HBM, HBM, HBM, VMEM, VMEM],
        out_specs=[HBM] * 5 + [VMEM] * 12,
        out_shape=[
            jax.ShapeDtypeStruct((hidden, width), F32),
            jax.ShapeDtypeStruct((width, hidden), F32),
            jax.ShapeDtypeStruct((width, width), F32),
            jax.ShapeDtypeStruct((width, 3 * width), F32),
            jax.ShapeDtypeStruct(grad_input.shape, F32),
        ]
        + [single] * 8
        + [jax.ShapeDtypeStruct((hidden,), F32)]
        + [table] * 3,
        scratch_shapes=[
            pltpu.VMEM((mains, width, width), BF),
            pltpu.VMEM((pairs, TAIL_ROWS, tail.shape[1]), BF),
            pltpu.VMEM((SLOTS, width, width), F32),
            pltpu.VMEM(grad_input.shape, BF),
            pltpu.VMEM(grad_input.shape, F32),
            dma((mains + pairs,)),
            dma((SLOTS, 4)),
            dma((2,)),
        ],
        compiler_params=pltpu.CompilerParams(vmem_limit_bytes=56 * MIB),
        name="finished",
    )(main, tail, grad_input, small, diagonals)


PIECE = 16


class Place:
    def __init__(self, depth):
        place = lax.axis_index("dp")
        self.depth = depth
        self.group = lax.div(place, 4 * depth)
        self.z = lax.rem(lax.div(place, 4), depth)
        self.bits = {
            "x": lax.axis_index("seq"),
            "c": lax.rem(place, 2),
            "y": lax.rem(lax.div(place, 2), 2),
            "a": lax.rem(self.z, 2),
            "b": lax.div(self.z, 2),
        }

    def partner(self, letters):
        bit = {
            letter: 1 - value if letter in letters else value
            for letter, value in self.bits.items()
        }
        z = self.z
        for letter, reach in (("a", 1), ("b", 2)):
            if letter in letters:
                z = z + reach - 2 * reach * self.bits[letter]
        return (bit["x"], (self.group * self.depth + z) * 4 + bit["y"] * 2 + bit["c"])

    def greet(self, met):
        barrier = pltpu.get_barrier_semaphore()
        for letters in met:
            pl.semaphore_signal(
                barrier, inc=1, device_id=self.partner(letters), device_id_type=MESH
            )
        pl.semaphore_wait(barrier, len(met))


def letters_of(depth):
    return "xy" + "ab"[: (depth - 1).bit_length()]


def parsed(routes, depth):
    kept = letters_of(depth)
    parts = []
    for route in routes.split():
        hops = ["".join(letter for letter in hop if letter in kept) for hop in route.split(".")]
        parts.append([hop for hop in hops if hop])
    return parts


def subsets(hop):
    return [
        "".join(letter for index, letter in enumerate(hop) if mask >> index & 1)
        for mask in range(1, 2 ** len(hop))
    ]


class Chunk:
    def __init__(self, place, depth, source, out_ref, offset, spot, scratch):
        _, self.begin, rows, first, columns, _, routes, _ = spot
        self.place, self.source, self.columns = place, source, pl.ds(first, columns)
        self.out_ref, self.out_begin = out_ref, offset + self.begin
        self.parts = parsed(routes, depth)
        self.half = rows // 2
        self.share = self.half // len(self.parts)
        self.hops = max(len(part) for part in self.parts)
        self.work, self.fresh, *landing, self.sends, self.receives, self.locals = scratch
        self.landing = {}
        self.sems = {}
        count = 2
        for part, hops in enumerate(self.parts):
            for hop, letters in enumerate(hops):
                self.landing[part, hop] = landing.pop(0)
                for way in range(2):
                    for index in range(2 ** len(letters) - 1):
                        self.sems[way, part, hop, index] = count
                        count += 1

    def aligned(self, value):
        return pl.multiple_of(value, PIECE)

    def size(self, part, hop):
        return self.share >> sum(len(letters) for letters in self.parts[part][: hop + 1])

    def spot(self, part, hop, other=""):
        start = part * self.share
        for level in range(hop + 1):
            for index, letter in enumerate(self.parts[part][level]):
                bit = self.place.bits[letter]
                if level == hop and letter in other:
                    bit = 1 - bit
                start = start + bit * (self.size(part, level) << index)
        return start

    def out(self, core):
        begin = self.aligned(self.out_begin + core * self.half)
        return self.out_ref.at[pl.ds(begin, self.half), self.columns]

    def held(self, buffer, begin, size):
        return buffer.at[pl.ds(self.aligned(begin), size)]

    def copy(self, index, source, target, letters):
        return remote(
            source, target, self.sends.at[index], self.receives.at[index],
            self.place.partner(letters),
        )

    def pair_down(self):
        core = self.place.bits["c"]
        at = lambda c: self.source.at[
            pl.ds(self.aligned(self.begin + c * self.half), self.half), self.columns
        ]
        return [
            self.copy(0, at(1 - core), self.fresh, "c"),
            pltpu.make_async_copy(at(core), self.work, self.locals.at[0]),
        ]

    def pair_up(self, arriving):
        core = self.place.bits["c"]
        return [
            self.copy(1, self.fresh, self.out(1 - core if arriving else core), "c"),
            pltpu.make_async_copy(self.fresh, self.out(core), self.locals.at[1]),
        ]

    def at_hop(self, hop):
        return [
            (part, hops[hop]) for part, hops in enumerate(self.parts) if hop < len(hops)
        ]

    def down(self, hop):
        copies = []
        for part, letters in self.at_hop(hop):
            size = self.size(part, hop)
            for index, other in enumerate(subsets(letters)):
                copies.append(
                    self.copy(
                        self.sems[0, part, hop, index],
                        self.held(self.work, self.spot(part, hop, other), size),
                        self.landing[part, hop].at[index], other,
                    )
                )
        return copies

    def up(self, hop, arriving):
        copies = []
        for part, letters in self.at_hop(hop):
            mine = self.spot(part, hop)
            size = self.size(part, hop)
            for index, other in enumerate(subsets(letters)):
                target = self.spot(part, hop, other) if arriving else mine
                copies.append(
                    self.copy(
                        self.sems[1, part, hop, index], self.held(self.fresh, mine, size),
                        self.held(self.fresh, target, size), other,
                    )
                )
        return copies

    def add(self, begin, sources, size):
        step = 64 if size % 64 == 0 else 32 if size % 32 == 0 else PIECE

        def body(index, carry):
            offset = self.aligned(index * step)
            there = pl.ds(self.aligned(begin + offset), step)
            total = self.work[there]
            if len(sources) == 1:
                total = total + sources[0][pl.ds(offset, step)]
            else:
                total = total.astype(F32)
                for source in sources:
                    total = total + source[pl.ds(offset, step)].astype(F32)
            self.work[there] = total.astype(BF)
            return carry

        lax.fori_loop(0, size // step, body, 0)

    def stage(self, number):
        hops = self.hops
        ended, started = [], []
        if number == 0:
            started = self.pair_down()
        elif number == 1:
            ended = self.pair_down()
            started = self.down(0)
        elif number <= hops:
            ended = self.down(number - 2)
            started = self.down(number - 1)
        elif number == hops + 1:
            ended = self.down(hops - 1)
            started = self.up(hops - 1, False)
        elif number <= 2 * hops:
            level = 2 * hops + 1 - number
            ended = self.up(level, True)
            started = self.up(level - 1, False)
        elif number == 2 * hops + 1:
            ended = self.up(0, True)
            started = self.pair_up(False)
        else:
            ended = self.pair_up(True)
        for copy in ended:
            copy.wait()
        if number == 1:
            self.add(0, [self.fresh], self.half)
        elif 2 <= number <= hops + 1:
            hop = number - 2
            for part, letters in self.at_hop(hop):
                landing = self.landing[part, hop]
                sources = [landing.at[index] for index in range(2 ** len(letters) - 1)]
                self.add(self.spot(part, hop), sources, self.size(part, hop))
        if number == hops + 1:
            for part, route in enumerate(self.parts):
                last = len(route) - 1
                there = pl.ds(self.aligned(self.spot(part, last)), self.size(part, last))
                self.fresh[there] = self.work[there]
        for copy in started:
            copy.start()


def chunk_scratch(spot, depth):
    _, _, rows, _, columns, _, routes, _ = spot
    parts = parsed(routes, depth)
    landing = []
    copies = 2
    for hops in parts:
        size = rows // 2 // len(parts)
        for letters in hops:
            size >>= len(letters)
            others = 2 ** len(letters) - 1
            copies += 2 * others
            landing.append(pltpu.VMEM((others, size, columns), BF))
    dma = pltpu.SemaphoreType.DMA
    return (
        [pltpu.VMEM((rows // 2, columns), BF)] * 2
        + landing
        + [dma((copies,)), dma((copies,)), dma((2,))]
    )


def loads_of(hop, size):
    if "x" in hop and "y" in hop:
        return [("x", 2 * size), ("y", 2 * size)]
    if hop in ("x", "y"):
        return [(hop, size)]
    if "a" in hop and "b" in hop:
        return [("end", 3 * size), ("middle", 4 * size)]
    return [("end", size), ("middle", 2 * size)] if hop == "b" else [("end", size)]


def planned(chunks, work, depth, hop_count):
    latency, issue, link, pair = 3.5, 0.08, 100e3, 600e3
    free = {}
    now = 3.0
    chains = []
    for rows, columns, need, routes, _ in chunks:
        parts = parsed(routes, depth)
        sizes = [rows // 2 // len(parts)] * len(parts)
        down = []
        for hop in range(max(len(part) for part in parts)):
            loads, copies, added = [], 0, 0
            for index, part in enumerate(parts):
                if hop < len(part):
                    sizes[index] >>= len(part[hop])
                    others = 2 ** len(part[hop]) - 1
                    loads += loads_of(part[hop], sizes[index])
                    copies += others
                    added += sizes[index] * others
            down.append((loads, copies, added, columns))
        first = [([("core", rows // 2)], 1.5, rows // 2, columns)]
        last = [([("core", rows // 2)], 1, 0, columns)]
        chains.append((need, first + down + down[::-1] + last))
    chains.append((len(work), [([("core", 16)], 2, 0, 768)] * hop_count))
    ranks = [chunk[4] for chunk in chunks] + [0]
    position = [0] * len(chains)
    ready = [0.0] * len(chains)
    order = [[] for _ in range(len(work) + 1)]
    done = 0
    while True:
        open_ones = [
            (ranks[i], ready[i], i) for i, (need, chain) in enumerate(chains)
            if position[i] <= len(chain) and need <= done
        ]
        due = [entry for entry in open_ones if entry[1] <= now]
        if not due and done < len(work):
            now += work[done]
            done += 1
            continue
        if not open_ones:
            return order
        _, when, index = min(due) if due else min(open_ones, key=lambda entry: entry[1])
        now = max(now, when)
        chain = chains[index][1]
        stage = position[index]
        order[done].append((index, stage))
        if 0 < stage <= len(chain) // 2:
            now += 1e-6 * chain[stage - 1][2] * chain[stage - 1][3]
        if stage < len(chain):
            loads, copies, _, columns = chain[stage]
            now += issue * copies
            end = now
            for lane, rows in loads:
                rate = pair if lane == "core" else link / 2
                free[lane] = max(now, free.get(lane, 0.0)) + 2 * rows * columns / rate
                end = max(end, free[lane])
            ready[index] = end + latency
        position[index] += 1


def last_kernel(
    depth, plan, orders, counts, *refs,
):
    (meta_ref, rows_ref, projected_hbm, mixed_hbm, log_ref, first_hbm, second_hbm,
     key_image_hbm, bias_hbm, small_ref, gain_ref, item_hbm, weight_hbm, total_hbm, unit_hbm, scale_hbm,
     out_weight_hbm, grad_down_ref, grad_up_ref,
     main_out, tail_out, small_out, diagonal_out, input_out,
     *scratch) = refs
    static, scratch = scratch[:6], scratch[6:]
    (k_ref, v_ref, mixed_ref, grad_ref, first_ref, second_ref, key_image_ref, bias_ref, pair_sems,
     item_ref, weight_ref, d_hidden_ref, unit_ref, scale_ref, load_sems, d_project, item_t, tail, input_grad,
     small_in, diagonal_in, small_sems, item_sems, *scratch) = scratch
    out_weight_ref = item_t
    place = Place(depth)
    step = pl.program_id(0)
    pairs = k_ref.shape[0]
    rows, width = item_hbm.shape
    count = rows // 2
    x = place.bits["x"]
    hidden = grad_down_ref.shape[0]
    sources = ((grad_down_ref, main_out, 0), (grad_up_ref, main_out, hidden), (tail, tail_out, 0))
    chunks = []
    for spot, pieces in zip(plan, counts):
        chunks.append(Chunk(place, depth, *sources[spot[0]], spot, scratch[:pieces]))
        scratch = scratch[pieces:]
    hop_letters = "c" + letters_of(depth)
    wide_hbm = (first_hbm, second_hbm, key_image_hbm, bias_hbm)
    wide_refs = (first_ref, second_ref, key_image_ref, bias_ref)

    def pair_loads(pair):
        copies = []
        held = ((projected_hbm, k_ref, width), (projected_hbm, v_ref, 2 * width))
        for source, target, first in held:
            columns = pl.ds(pl.multiple_of(first + pair * LANES, LANES), LANES)
            copies.append((source.at[:, columns], target.at[pair]))
        heads = pl.ds(2 * pair, 2)
        for source, target in zip(wide_hbm, wide_refs):
            copies.append((source.at[heads], target.at[heads]))
        return [
            pltpu.make_async_copy(source, target, pair_sems.at[pair, index])
            for index, (source, target) in enumerate(copies)
        ]

    def loads(first):
        if first:
            copies = [
                (total_hbm, d_hidden_ref), (unit_hbm, unit_ref), (scale_hbm, scale_ref),
                (out_weight_hbm, out_weight_ref), (item_hbm, item_ref),
            ]
            copies += [
                (mixed_hbm.at[:, pl.ds(pair * LANES, LANES)], mixed_ref.at[pair])
                for pair in range(pairs)
            ]
        else:
            copies = [(weight_hbm, weight_ref)]
        return [
            pltpu.make_async_copy(source, target, load_sems.at[0 if first else 1, index])
            for index, (source, target) in enumerate(copies)
        ]

    def back_to_attention():
        gain = vector(gain_ref)

        def tile(index, sums):
            there = pl.ds(pl.multiple_of(index * 64, 64), 64)
            d_normed = d_hidden_ref[there]
            standard = unit_ref[there]
            d_hidden = norm_pulled(d_normed * gain, standard, scale_ref[there, :1])
            d_hidden_ref[there] = d_hidden
            low = d_hidden.astype(BF)
            input_grad[there] = low
            return (
                sums[0] + column_sum(low.astype(F32)),
                sums[1] + column_sum(d_normed * standard),
                sums[2] + column_sum(d_normed),
            )

        zero = jnp.zeros((1, width), F32)
        sums = lax.fori_loop(0, rows // 64, tile, (zero, zero, zero), unroll=4)
        for row, value in zip((2, 3, 4), sums):
            small_out[row : row + 1] = value
        low = input_grad[...]
        down = TAIL_ROWS - width
        for begin in range(0, width, down):
            first = begin // LANES
            several = range(first, first + down // LANES)
            d_mixed = dot_nt(low, out_weight_ref[begin : begin + down]).astype(BF)
            for index, pair in enumerate(several):
                grad_ref[pair] = d_mixed[:, index * LANES : index * LANES + LANES]
            turned = jnp.concatenate(
                [jnp.transpose(mixed_ref[pair]).astype(BF) for pair in several], axis=0
            )
            for pair in range(pairs):
                rows_of, across = out_spot(pair, pairs, width)
                if rows_of.start == begin:
                    product = dot_nn(turned, low[:, across.start : across.start + across.size])
                    base = pair * TAIL_ROWS + width
                    tail[base : base + down] = product.astype(BF)

    def input_copies():
        return [
            pltpu.make_async_copy(
                input_grad.at[pl.ds(pl.multiple_of(x * count, LANES), count)], input_out.at[x],
                item_sems.at[0],
            ),
            remote(
                input_grad.at[pl.ds(pl.multiple_of((1 - x) * count, LANES), count)],
                input_out.at[x], item_sems.at[1], item_sems.at[2], place.partner("x"),
            ),
        ]

    def small_copies(hop):
        return [
            remote(source, landing.at[hop], small_sems.at[0, kind, hop],
                   small_sems.at[1, kind, hop], place.partner(hop_letters[hop]))
            for kind, (source, landing) in enumerate(
                ((small_out, small_in), (diagonal_out, diagonal_in))
            )
        ]

    def small_stage(hop):
        if hop > 0:
            for copy in small_copies(hop - 1):
                copy.wait()
            small_out[...] = small_out[...] + small_in[hop - 1]
            diagonal_out[...] = diagonal_out[...] + diagonal_in[hop - 1]
        if hop < len(hop_letters):
            for copy in small_copies(hop):
                copy.start()

    def perform(slot):
        for index, stage in orders[slot]:
            if index == len(chunks):
                small_stage(stage)
            else:
                chunks[index].stage(stage)

    @pl.when(step == 0)
    def _():
        for copy in pair_loads(0) + loads(True):
            copy.start()
        met = set(hop_letters)
        for chunk in chunks:
            for hops in chunk.parts:
                for letters in hops:
                    met.update(subsets(letters))
        place.greet(sorted(met))
        small_out[...] = small_ref[...]

    for pair in range(pairs):
        @pl.when(step == pair)
        def _(pair=pair):
            perform(pair)

    @pl.when(step == 0)
    def _():
        for pair in range(1, pairs):
            for copy in pair_loads(pair):
                copy.start()
        for copy in loads(False):
            copy.start()
        static_prepare(meta_ref, static)
        for copy in loads(True):
            copy.wait()
        back_to_attention()
        for tile in range(rows // TILE):
            there = slice(tile * TILE, tile * TILE + TILE)
            item_t[:, there] = jnp.transpose(item_ref[there].astype(F32)).astype(BF)

    for copy in pair_loads(step):
        copy.wait()
    (dq_even, dk_even, dv_even), (dq_odd, dk_odd, dv_odd) = [
        head_back(
            parity, step, rows_ref, wide_refs, k_ref, v_ref, mixed_ref, grad_ref, log_ref,
            static, diagonal_out,
        )
        for parity in range(2)
    ]
    even = own_lanes(0, rows)
    pieces = [
        jnp.transpose(jnp.concatenate([dq_even, dq_odd], axis=0)).astype(BF),
        jnp.where(even, dk_even, dk_odd).astype(BF),
        jnp.where(even, dv_even, dv_odd).astype(BF),
    ]
    for part, piece in enumerate(pieces):
        d_project[:, pl.ds(pl.multiple_of(part * width + step * LANES, LANES), LANES)] = piece
    slab = pl.ds(pl.multiple_of(step * TAIL_ROWS, TAIL_ROWS), width)
    tail[slab] = dot_nn(item_t[...], jnp.concatenate(pieces, axis=1)).astype(BF)

    @pl.when(step == 0)
    def _():
        for copy in loads(False):
            copy.wait()

    @pl.when(step == pairs - 1)
    def _():
        perform(pairs)
        for begin in range(0, width, TILE):
            here = slice(begin, begin + TILE)
            total = d_hidden_ref[:, here] + dot_nt(d_project[...], weight_ref[here])
            input_grad[:, here] = total.astype(BF)
        for copy in input_copies():
            copy.start()
        for begin in range(0, width, TILE):
            here = slice(begin, begin + TILE)
            there = slice(2 * width + begin, 2 * width + begin + TILE)
            small_out[0:1, here] = column_sum(d_project[:, here].astype(F32))
            small_out[1:2, here] = column_sum(d_project[:, there].astype(F32))
        perform(pairs + 1)
        for copy in input_copies():
            copy.wait()


TAIL_ROWS = 1024


def out_spot(pair, pairs, width):
    down = TAIL_ROWS - width
    across = width * width // (pairs * down)
    per_row = width // across
    return (
        pl.ds(pair // per_row * down, down),
        pl.ds(pair % per_row * across, across),
    )


def summed_with_attention_back(
    meta_columns, meta_rows, projected, mixed, logs, wide_arrays, item, qkv_weight,
    total, unit, scale, out_weight, attn_gain, small, grad_down, grad_up,
):
    size = lax.axis_size("dp")
    depth = 4 if size % 16 == 0 else size // 4
    rows, width = item.shape
    pairs = width // LANES
    hidden = grad_down.shape[0]
    hops = len(letters_of(depth)) + 1
    work = [6.8] * pairs + [4.0]
    tall, wide, slim = 1024, 3 * LANES, 2 * LANES
    plan = [
        (0, 0, 2 * tall, 0, width, 0, "a.b.x.y x.y.a.b", 1),
        (0, 2 * tall, tall, 0, width, 0, "x.a.y.b y.a.b.x", 2),
        (1, 0, 3 * tall, 0, slim, 0, "a.b.x.y y.x.a.b", 4),
        (1, 0, 3 * tall, slim, slim, 0, "y.a.x.b x.y.a.b", 0),
        (1, 0, 3 * tall, 2 * slim, slim, 0, "x.y.a.b y.x.a.b", 2),
        (2, 0, tall, 0, wide, 1, "y.x.a.b a.b.x.y", 3),
        (2, tall, tall, 0, wide, 2, "xy.a.b", 2),
        (2, 2 * tall, tall, 0, wide, 3, "x.y.ab y.ab.x", 3),
        (2, 3 * tall, tall, 0, wide, 4, "xy.a.b", 1),
        (2, 4 * tall, tall, 0, wide, 5, "xy.a.b", 1),
        (2, 5 * tall, tall, 0, wide, 6, "ab.y.x y.ab.x", 2),
    ]
    orders = planned([(spot[2],) + spot[4:] for spot in plan], work, depth, hops)

    whole = pl.BlockSpec(memory_space=pltpu.VMEM)
    diagonals = jax.ShapeDtypeStruct((2 * pairs, 8, LANES), F32)
    dma = pltpu.SemaphoreType.DMA
    scratch = []
    for spot in plan:
        scratch.append(chunk_scratch(spot, depth))
    main, tail, small, diagonals, grad_input = pl.pallas_call(
        functools.partial(last_kernel, depth, plan, orders, [len(pieces) for pieces in scratch]),
        grid=(pairs,),
        in_specs=[whole] * 2 + [HBM] * 2 + [whole] + [HBM] * 4 + [whole] * 2 + [HBM] * 8,
        out_specs=[HBM, HBM, whole, whole, HBM],
        out_shape=[
            jax.ShapeDtypeStruct((2 * hidden, width), BF),
            jax.ShapeDtypeStruct((pairs * TAIL_ROWS, 3 * LANES), BF),
            jax.ShapeDtypeStruct(small.shape, F32),
            diagonals,
            jax.ShapeDtypeStruct((2, rows // 2, width), BF),
        ],
        scratch_shapes=[pltpu.VMEM((rows, LANES), BF)] * 3
        + [pltpu.VMEM((LANES, rows), BF)] * 3
        + [pltpu.VMEM((pairs, rows, LANES), kind) for kind in (BF, BF, F32, BF)]
        + [pltpu.VMEM(array.shape, BF) for array in wide_arrays]
        + [
            dma((pairs, 6)),
            pltpu.VMEM((rows, width), BF),
            pltpu.VMEM((width, 3 * width), BF),
            pltpu.VMEM((rows, width), F32),
            pltpu.VMEM((rows, width), F32),
            pltpu.VMEM((rows, LANES), F32),
            dma((2, 5 + pairs)),
            pltpu.VMEM((rows, 3 * width), BF),
            pltpu.VMEM((width, rows), BF),
            pltpu.VMEM((pairs * TAIL_ROWS, 3 * LANES), BF),
            pltpu.VMEM((rows, width), BF),
            pltpu.VMEM((hops,) + small.shape, F32),
            pltpu.VMEM((hops,) + diagonals.shape, F32),
            dma((2, 2, hops)),
            dma((3,)),
        ]
        + [piece for pieces in scratch for piece in pieces],
        compiler_params=pltpu.CompilerParams(
            collective_id=0, has_side_effects=True, vmem_limit_bytes=62 * MIB
        ),
        name="summed_with_attention_back",
    )(meta_columns, meta_rows, projected, mixed, logs, *wide_arrays,
      small, attn_gain, item, qkv_weight, total, unit, scale, out_weight, grad_down, grad_up)
    span = 4 * depth
    if size > span:
        groups = [list(range(first, size, span)) for first in range(span)]
        main, tail, small, diagonals = lax.psum(
            (main.astype(F32), tail.astype(F32), small, diagonals), "dp",
            axis_index_groups=groups,
        )
        main, tail = main.astype(BF), tail.astype(BF)
    return main, tail, small, diagonals, grad_input


def per_device(
    layer_in, segment, key_mask, position, layout_x, layout_y,
    qkv_weight, query_bias, value_bias, out_weight, out_bias, attn_gain, attn_shift,
    up_weight, up_bias, down_weight, down_bias, ffn_gain, ffn_shift,
    text_table, horiz_table, vert_table, cotangent,
):
    width = layer_in.shape[-1]
    item, projected, meta_columns, meta_rows, table_rows = projected_item(
        layer_in, (segment, key_mask, position, layout_x, layout_y),
        qkv_weight, query_bias, value_bias, (text_table, horiz_table, vert_table),
    )
    mixed, logs, *wide_arrays = attention_forward(meta_columns, meta_rows, table_rows, projected, width)
    layer_out, total, unit, scale, grad_down, grad_up, small = fed_forward_and_back(
        item, mixed, cotangent, out_weight, up_weight, down_weight,
        (out_bias, attn_gain, attn_shift, up_bias, down_bias, ffn_gain, ffn_shift),
    )
    main, tail, small, diagonals, grad_input = summed_with_attention_back(
        meta_columns, meta_rows, projected, mixed, logs, wide_arrays, item, qkv_weight,
        total, unit, scale, out_weight, attn_gain, small, grad_down, grad_up,
    )
    done = finished(
        main, tail, grad_input, small, diagonals, up_weight.shape[1], text_table.shape[0]
    )
    sum_down, sum_up, sum_out, sum_qkv, grad_input = done[:5]
    singles, tables = done[5:14], [t.T for t in done[14:]]
    return (
        layer_out, grad_input, sum_qkv, singles[0], singles[1], sum_out, singles[2], singles[3],
        singles[4], sum_up, singles[8], sum_down, singles[5], singles[6], singles[7],
        tables[0], tables[1], tables[2],
    )


def solution(mesh):
    rows = P("dp", "seq", None)
    marks_spec = P("dp", "seq")
    return jax.shard_map(
        per_device,
        mesh=mesh,
        in_specs=(rows,) + (marks_spec,) * 5 + (P(),) * 16 + (rows,),
        out_specs=(rows, rows) + (P(),) * 16,
        check_vma=False,
    )
```

```python
import functools

import jax
import jax.numpy as jnp
from jax import lax
from jax.experimental import pallas as pl
from jax.experimental.pallas import tpu as pltpu
from jax.sharding import PartitionSpec as P

BF = jnp.bfloat16
F32 = jnp.float32
BIG = 1e30
LANES = 128
HEAD = 64
TEXT = 512
POS = 64
COORD = 48
Y0 = 64
GROUP0 = 112
MEMBER0 = 116
FLAG = 124
EVERY = 125
STRAY = 126
X_TABLE = 33
Y_TABLE = 66
NOTHING = 127


def dot_nt(a, b):
    return lax.dot_general(a, b, (((1,), (1,)), ((), ())), preferred_element_type=F32)


def dot_nn(a, b):
    return lax.dot_general(a, b, (((1,), (0,)), ((), ())), preferred_element_type=F32)


def looked_up(table_row, index):
    rows = index.shape[0]
    return jnp.take_along_axis(
        jnp.broadcast_to(table_row, (rows, LANES)), index, axis=1, mode="promise_in_bounds"
    )


def bucket(distance):
    return jnp.clip(distance, -16, 16) + 16


def between(lane, low, high):
    return (lane >= low) & (lane < high)


def columns_of(meta_ref):
    return tuple(meta_ref[:, field : field + 1] for field in range(5))


def marks(meta_ref):
    segment, key_mask, position, across, down = columns_of(meta_ref)
    rows = segment.shape[0]
    lane = lax.broadcasted_iota(jnp.int32, (rows, LANES), 1)
    row = lax.broadcasted_iota(jnp.int32, (rows, LANES), 0)
    even = between(lane, HEAD, HEAD + COORD) & (lane - HEAD == across)
    odd = (lane < COORD) & (lane == across)
    group = (segment - 1) >> 3
    member = (segment - 1) & 7
    named = segment > 0
    shared = (
        ((row < TEXT) & (lane < POS) & (lane == position))
        | (between(lane, Y0, Y0 + COORD) & (lane - Y0 == down))
        | (named & between(lane, GROUP0, MEMBER0) & (lane - GROUP0 == group))
        | (named & between(lane, MEMBER0, FLAG) & (lane - MEMBER0 == member))
        | ((lane == FLAG) & (key_mask <= 0))
        | (lane == EVERY)
        | ((lane == STRAY) & (segment < 0))
    )
    return tuple(jnp.where(m, 1.0, 0.0).astype(BF) for m in (even, odd, shared))


def square_lanes():
    shape = (LANES, LANES)
    return lax.broadcasted_iota(jnp.int32, shape, 0), lax.broadcasted_iota(jnp.int32, shape, 1)


def barred():
    row, lane = square_lanes()
    in_groups = between(lane, GROUP0, MEMBER0)
    shut = (
        (between(row, GROUP0, MEMBER0) & in_groups & (lane != row))
        | (between(row, MEMBER0, FLAG) & between(lane, MEMBER0, FLAG) & (lane != row))
        | ((row == EVERY) & (lane == FLAG))
        | ((row == STRAY) & in_groups)
    )
    return jnp.where(shut, -BIG, 0.0).astype(F32)


def table_index():
    row, lane = square_lanes()
    distance = bucket(row - lane)
    inside = lambda low, high: between(row, low, high) & between(lane, low, high)
    even = jnp.where(inside(HEAD, HEAD + COORD), distance + X_TABLE, NOTHING)
    odd = jnp.where(inside(0, COORD), distance + X_TABLE, NOTHING)
    shared = jnp.where(
        inside(0, POS), distance, jnp.where(inside(Y0, Y0 + COORD), distance + Y_TABLE, NOTHING)
    )
    return even, odd, shared


def image_query_index(meta_ref):
    position = meta_ref[TEXT:, 2:3]
    lane = lax.broadcasted_iota(jnp.int32, (position.shape[0], LANES), 1)
    return jnp.where(lane < POS, bucket(position - lane), NOTHING)


def prepare(meta_ref, mark_refs, bar_ref, index_refs, image_index_ref):
    for ref, value in zip(mark_refs, marks(meta_ref)):
        ref[...] = value
    bar_ref[...] = barred()
    for ref, value in zip(index_refs, table_index()):
        ref[...] = value
    image_index_ref[...] = image_query_index(meta_ref)


def own_lanes(parity, rows):
    lane = lax.broadcasted_iota(jnp.int32, (rows, LANES), 1)
    return (lane < HEAD) if parity == 0 else (lane >= HEAD)


def widened(parity, q, table_row, bias, bar_ref, index_refs, image_index_ref, mark_refs):
    rows = q.shape[0]
    shared = mark_refs[2][...]
    across = looked_up(table_row, index_refs[parity][...]).astype(BF)
    first = jnp.where(
        own_lanes(parity, rows), q.astype(F32) * 0.125, dot_nn(mark_refs[parity][...], across)
    )
    others = (looked_up(table_row, index_refs[2][...]) + bar_ref[...]).astype(BF)
    second = dot_nn(shared, others)
    on_images = looked_up(table_row, image_index_ref[...])
    second = jnp.concatenate([second[:TEXT], second[TEXT:] + on_images], axis=0)
    image_lane = lax.broadcasted_iota(jnp.int32, on_images.shape, 1)
    key_image = jnp.where(image_lane < POS, bias[:, :LANES].astype(BF), shared[TEXT:])
    return first.astype(BF), second.astype(BF), key_image


def joined(parity, first, second, key_image, k, marks_own, shared):
    rows = k.shape[0]
    lane = lax.broadcasted_iota(jnp.int32, (rows, LANES), 1)
    to_image = jnp.where(lane < POS, shared, second)
    key_first = jnp.where(own_lanes(parity, rows), k, marks_own)
    q_text = jnp.concatenate([first, second], axis=1)
    q_image = jnp.concatenate([first, to_image], axis=1)
    k_text = jnp.concatenate([key_first[:TEXT], shared[:TEXT]], axis=1)
    k_image = jnp.concatenate([key_first[TEXT:], key_image], axis=1)
    return q_text, q_image, k_text, k_image


def near(start, size):
    if start >= TEXT:
        return slice(0, TEXT)
    return slice(max(0, start - LANES), min(TEXT, start + size + LANES))


def image_bias(table_row, offsets):
    return jnp.concatenate(
        [looked_up(table_row, offsets[:, :LANES]), looked_up(table_row, offsets[:, LANES:])], axis=1
    )


def forward_kernel(
    meta_ref, rows_ref, table_ref, q_ref, k_ref, v_ref,
    mixed_ref, log_ref, first_ref, second_ref, key_image_ref, bias_ref,
    even_ref, odd_ref, shared_ref, bar_ref, index_even, index_odd, index_shared, image_index_ref,
):
    mark_refs = (even_ref, odd_ref, shared_ref)
    index_refs = (index_even, index_odd, index_shared)

    @pl.when(pl.program_id(0) == 0)
    def _():
        prepare(meta_ref, mark_refs, bar_ref, index_refs, image_index_ref)

    rows = q_ref.shape[0]
    images = rows - TEXT
    q, k, v = q_ref[...], k_ref[...], v_ref[...]
    offsets = bucket(rows_ref[2:3, TEXT:] - meta_ref[TEXT:, 2:3])
    tile = 256
    v_turned = transposed(v)
    heads = [None, None]

    def prepared(parity):
        table_row = table_ref[pl.ds(2 * pl.program_id(0) + parity, 1), :]
        bias = image_bias(table_row, offsets)
        first, second, key_image = widened(
            parity, q, table_row, bias, bar_ref, index_refs, image_index_ref, mark_refs
        )
        first_ref[parity] = first
        second_ref[parity] = second
        key_image_ref[parity] = key_image
        bias_ref[parity] = bias.astype(BF)
        wide = joined(
            parity, first, second, key_image, k, mark_refs[parity][...], shared_ref[...]
        )
        heads[parity] = wide + (bias,)

    def scored(parity, start):
        q_text, q_image, k_text, k_image, bias = heads[parity]
        here = slice(start, start + tile)
        on_image = dot_nt(k_image, q_image[here])
        if start >= TEXT:
            on_image = on_image + bias[:, start - TEXT : start - TEXT + tile]
        return dot_nt(k_text[near(start, tile)], q_text[here]), on_image

    spots = [(parity, start) for parity in range(2) for start in range(0, rows, tile)]
    outs = ([], [])
    prepared(0)
    following = scored(*spots[0])
    for index, (parity, start) in enumerate(spots):
        on_text, on_image = following
        if index == 1:
            prepared(1)
        if index + 1 < len(spots):
            following = scored(*spots[index + 1])
        top = jnp.maximum(
            jnp.max(on_text, axis=0, keepdims=True), jnp.max(on_image, axis=0, keepdims=True)
        )
        on_text = jnp.exp(on_text - top)
        on_image = jnp.exp(on_image - top)
        total = jnp.sum(on_text, axis=0, keepdims=True) + jnp.sum(on_image, axis=0, keepdims=True)
        own = slice(parity * HEAD, parity * HEAD + HEAD)
        out = dot_nn(v_turned[own, near(start, tile)], on_text.astype(BF)) + dot_nn(
            v_turned[own, TEXT:], on_image.astype(BF)
        )
        outs[parity].append(out * (1.0 / total))
        log_ref[0, parity : parity + 1, start : start + tile] = top + jnp.log(total)
    mixed_ref[...] = jnp.transpose(
        jnp.concatenate([jnp.concatenate(outs[parity], axis=1) for parity in range(2)], axis=0)
    )


def static_scratch(rows):
    square = (LANES, LANES)
    return [
        pltpu.VMEM((rows, LANES), BF),
        pltpu.VMEM((rows, LANES), BF),
        pltpu.VMEM((rows, LANES), BF),
        pltpu.VMEM(square, F32),
        pltpu.VMEM(square, jnp.int32),
        pltpu.VMEM(square, jnp.int32),
        pltpu.VMEM(square, jnp.int32),
        pltpu.VMEM((rows - TEXT, LANES), jnp.int32),
    ]


def attention_forward(meta_columns, meta_rows, table_rows, projected, width):
    rows = projected.shape[0]
    images = rows - TEXT
    pairs = width // LANES

    def block(part):
        return pl.BlockSpec((rows, LANES), lambda p: (0, part * pairs + p))

    whole = lambda shape: pl.BlockSpec(shape, lambda p: (0,) * len(shape))
    return pl.pallas_call(
        forward_kernel,
        grid=(pairs,),
        in_specs=[
            whole(meta_columns.shape),
            whole(meta_rows.shape),
            whole(table_rows.shape),
            block(0), block(1), block(2),
        ],
        out_specs=[
            pl.BlockSpec((rows, LANES), lambda p: (0, p)),
            pl.BlockSpec((1, 2, rows), lambda p: (p, 0, 0)),
            pl.BlockSpec((2, rows, LANES), lambda p: (p, 0, 0)),
            pl.BlockSpec((2, rows, LANES), lambda p: (p, 0, 0)),
            pl.BlockSpec((2, images, LANES), lambda p: (p, 0, 0)),
            pl.BlockSpec((2, images, images), lambda p: (p, 0, 0)),
        ],
        out_shape=[
            jax.ShapeDtypeStruct((rows, width), F32),
            jax.ShapeDtypeStruct((pairs, 2, rows), F32),
            jax.ShapeDtypeStruct((2 * pairs, rows, LANES), BF),
            jax.ShapeDtypeStruct((2 * pairs, rows, LANES), BF),
            jax.ShapeDtypeStruct((2 * pairs, images, LANES), BF),
            jax.ShapeDtypeStruct((2 * pairs, images, images), BF),
        ],
        scratch_shapes=static_scratch(rows),
        compiler_params=pltpu.CompilerParams(vmem_limit_bytes=60 * 1024 * 1024),
        name="attention_forward",
    )(meta_columns, meta_rows, table_rows, projected, projected, projected)


def skewed(block):
    size = block.shape[0]
    lane = lax.broadcasted_iota(jnp.int32, (size, LANES), 1)
    row = lax.broadcasted_iota(jnp.int32, (size, LANES), 0)
    turned = jnp.take_along_axis(
        block, (lane + row) & (LANES - 1), axis=1, mode="promise_in_bounds"
    )
    straight = lane + row < LANES
    above = jnp.sum(jnp.where(straight, turned, 0.0), axis=0, keepdims=True)
    below = jnp.sum(jnp.where(straight, 0.0, turned), axis=0, keepdims=True)
    return above, below


def transposed(array):
    return jnp.transpose(array.astype(F32)).astype(array.dtype)


def static_prepare(meta_ref, static):
    for ref, turned, value in zip(static[:3], static[3:], marks(meta_ref)):
        ref[...] = value
        turned[...] = transposed(value)


def head_back(
    parity, pair, rows_ref, wide_refs, k_ref, v_ref, mixed_ref, grad_ref, log_ref, static, diag_ref,
):
    mark_refs, turned_refs = static[:3], static[3:]
    first_ref, second_ref, key_image_ref, bias_ref = wide_refs
    head = 2 * pair + parity
    shared_t = turned_refs[2]
    rows = k_ref.shape[1]
    images = rows - TEXT
    tile = 256
    k, v, grad = k_ref[pair], v_ref[pair], grad_ref[pair]
    products = grad.astype(F32) * mixed_ref[pair]
    k_turned = transposed(k)
    is_image = rows_ref[1:2, TEXT:] > 0
    own = own_lanes(parity, rows)
    log_row = log_ref[pair, parity : parity + 1, :]
    first, shared = first_ref[head], mark_refs[2][...]
    q_text, q_image, k_text, k_image = joined(
        parity, first, second_ref[head], key_image_ref[head], k, mark_refs[parity][...], shared
    )
    bias = bias_ref[head].astype(F32)
    ones = jnp.where(own_lanes(parity, 8), 1.0, 0.0).astype(BF)
    delta = jnp.zeros((8, rows), F32)
    rest = products
    for _ in range(3):
        piece = rest.astype(BF)
        delta = delta + dot_nt(ones, piece)
        rest = rest - piece.astype(F32)
    delta = delta[0:1]
    v_own = jnp.where(own, v, jnp.zeros_like(v))
    q_marked = jnp.concatenate(
        [jnp.where(own, first, mark_refs[parity][...]), shared], axis=1
    )
    dq_text = jnp.zeros((HEAD, TEXT), F32)
    dq_image = jnp.zeros((HEAD, images), F32)
    dks = []
    dvs = []
    first_sum = jnp.zeros((LANES, LANES), F32)
    second_sum = jnp.zeros((LANES, LANES), F32)
    text_image = jnp.zeros((LANES, images), F32)

    def met(start, array, axis=0):
        text = near(start, tile)
        if axis == 0:
            return jnp.concatenate([array[text], array[TEXT:]], axis=0)
        return jnp.concatenate([array[:, text], array[:, TEXT:]], axis=1)

    def scored(start):
        here = slice(start, start + tile)
        if start < TEXT:
            scores = dot_nt(k_text[here], met(start, q_text))
        else:
            scores = dot_nt(k_image[start - TEXT : start - TEXT + tile], q_image)
            scores = jnp.concatenate([scores[:, :TEXT], scores[:, TEXT:] + bias], axis=1)
        return scores, dot_nt(v_own[here], met(start, grad))

    following = scored(0)
    for start in range(0, rows, tile):
        here = slice(start, start + tile)
        scores, prob_grad = following
        if start + tile < rows:
            following = scored(start + tile)
        soft = jnp.exp(scores - met(start, log_row, 1))
        score_grad = soft * (prob_grad - met(start, delta, 1))
        low = score_grad.astype(BF)
        dvs.append(dot_nn(soft.astype(BF), met(start, grad)))
        wide = dot_nn(low, met(start, q_marked))
        dks.append(wide[:, :LANES])
        part = dot_nn(k_turned[parity * HEAD : parity * HEAD + HEAD, here], low)
        text = near(start, tile)
        count = text.stop - text.start
        before = [jnp.zeros((HEAD, text.start), F32)] if text.start > 0 else []
        after = [jnp.zeros((HEAD, TEXT - text.stop), F32)] if text.stop < TEXT else []
        dq_text = dq_text + jnp.concatenate(before + [part[:, :count]] + after, axis=1)
        dq_image = dq_image + part[:, count:]
        rounded = wide.astype(BF)
        first_sum = first_sum + dot_nn(turned_refs[parity][:, here], rounded[:, :LANES])
        second_sum = second_sum + dot_nn(shared_t[:, here], rounded[:, LANES:])
        if start < TEXT:
            text_image = text_image + dot_nn(shared_t[:, here], low[:, count:])
        else:
            by_position = wide[:, LANES:]
            on_image = score_grad[:, TEXT:]
    dq = jnp.concatenate([dq_text, dq_image], axis=1)
    small = lax.broadcasted_iota(jnp.int32, (LANES, LANES), 1)
    small_row = lax.broadcasted_iota(jnp.int32, (LANES, LANES), 0)
    x0 = HEAD if parity == 0 else 0
    x_block = jnp.where(
        between(small, x0, x0 + COORD) & between(small_row, x0, x0 + COORD), first_sum, 0.0
    )
    y_block = jnp.where(
        between(small, Y0, Y0 + COORD) & between(small_row, Y0, Y0 + COORD), second_sum, 0.0
    )
    p_block = jnp.where((small < POS) & (small_row < POS), second_sum, 0.0)
    wide_lane = lax.broadcasted_iota(jnp.int32, (images, images), 1)
    outside = jnp.sum(jnp.where(is_image, 0.0, on_image), axis=1, keepdims=True)
    pairs = jnp.where(is_image, on_image, 0.0) + jnp.where(wide_lane == 0, outside, 0.0)
    outside_text = jnp.sum(jnp.where(is_image, 0.0, text_image), axis=1, keepdims=True)
    text_lane = lax.broadcasted_iota(jnp.int32, (LANES, images), 1)
    text_row = lax.broadcasted_iota(jnp.int32, (LANES, images), 0)
    text_image = jnp.where(is_image, text_image, 0.0) + jnp.where(
        text_lane == 0, outside_text, 0.0
    )
    text_image = jnp.where(text_row < POS, text_image, 0.0)
    first_lane = lax.broadcasted_iota(jnp.int32, (images, LANES), 1)
    left = pairs[:, :LANES] + jnp.where(first_lane < POS, by_position, 0.0)
    right = pairs[:, LANES:]
    a00, b00 = skewed(left[:LANES] + text_image[:, :LANES] + p_block)
    a01, b01 = skewed(right[:LANES] + text_image[:, LANES:])
    a10, b10 = skewed(left[LANES:])
    a11, b11 = skewed(right[LANES:])
    ax, bx = skewed(x_block)
    ay, by = skewed(y_block)
    diag_ref[head] = jnp.concatenate(
        [b10, b00 + b11 + a10, a00 + a11 + b01, a01, bx, ax, by, ay], axis=0
    )
    return dq * 0.125, jnp.concatenate(dks, axis=0), jnp.concatenate(dvs, axis=0)


MESH = pl.DeviceIdType.MESH
VMEM = pl.BlockSpec(memory_space=pltpu.VMEM)
HBM = pl.BlockSpec(memory_space=pltpu.HBM)
MIB = 1024 * 1024


def remote(src, dst, send, receive, device):
    return pltpu.make_async_remote_copy(
        src_ref=src, dst_ref=dst, send_sem=send, recv_sem=receive, device_id=device,
        device_id_type=MESH,
    )


def project_kernel(
    layer_ref, weight_hbm, *refs,
):
    small_hbm, refs = refs[:10], refs[10:]
    (item_ref, projected_out, columns_ref, rows_ref, table_ref,
     projected_ref, weight_ref, meta_send, bias_ref, sems, load_sems, store_sems), small = (
        refs[:12], refs[12:],
    )
    (segment_ref, mask_ref, position_ref, across_ref, down_ref, query_bias_ref, value_bias_ref,
     text_ref, horiz_ref, vert_ref) = small
    mine = lax.axis_index("seq")
    partner = (1 - mine, lax.axis_index("dp"))
    count, width = layer_ref.shape[1:]
    own = pl.ds(pl.multiple_of(mine * count, LANES), count)
    loads = [
        pltpu.make_async_copy(source, target, load_sems.at[index])
        for index, (source, target) in enumerate(
            list(zip(small_hbm, small))
            + [(layer_ref.at[mine], item_ref.at[own]), (weight_hbm, weight_ref)]
        )
    ]
    for load in loads:
        load.start()
    barrier = pltpu.get_barrier_semaphore()
    pl.semaphore_signal(barrier, inc=1, device_id=partner, device_id_type=MESH)
    pl.semaphore_wait(barrier, 1)
    pieces = count // LANES
    rows_out = [
        remote(
            layer_ref.at[1 - mine, pl.ds(piece * LANES, LANES)],
            item_ref.at[pl.ds(pl.multiple_of(mine * count + piece * LANES, LANES), LANES)],
            sems.at[0, piece], sems.at[1, piece], partner,
        )
        for piece in range(pieces)
    ]
    for copy in rows_out:
        copy.start()
    for load in loads[:-2]:
        load.wait()

    fields = (segment_ref, mask_ref, position_ref, across_ref, down_ref)
    blocks = [
        jnp.concatenate(
            [field[item : item + 1, :] for field in fields] + [jnp.zeros((3, count), jnp.int32)],
            axis=0,
        )
        for item in range(2)
    ]
    meta_send[...] = jnp.where(mine == 0, blocks[1], blocks[0])
    meta_out = remote(
        meta_send, rows_ref.at[:, own], sems.at[0, pieces], sems.at[1, pieces], partner
    )
    meta_out.start()
    rows_ref[:, own] = jnp.where(mine == 0, blocks[0], blocks[1])
    bias_ref[:, :width] = query_bias_ref[...].astype(F32).reshape(1, width)
    bias_ref[:, width : 2 * width] = jnp.zeros((1, width), F32)
    bias_ref[:, 2 * width :] = value_bias_ref[...].astype(F32).reshape(1, width)
    heads, levels = text_ref.shape
    spot = lax.broadcasted_iota(jnp.int32, (levels, LANES), 1)
    level = lax.broadcasted_iota(jnp.int32, (levels, LANES), 0)
    table = jnp.zeros((heads, LANES), F32)
    for source, begin in ((text_ref, 0), (horiz_ref, X_TABLE), (vert_ref, Y_TABLE)):
        table = table + dot_nn(source[...], (spot == level + begin).astype(BF))
    table_ref[...] = jnp.concatenate([table, jnp.zeros((16 - heads, LANES), F32)], axis=0)

    def project(there):
        step = 256

        def body(index, carry):
            columns = pl.ds(pl.multiple_of(index * step, step), step)
            product = dot_nn(item_ref[there], weight_ref[:, columns])
            projected_ref[there, columns] = (product + bias_ref[:, columns]).astype(BF)
            return carry

        lax.fori_loop(0, 3 * width // step, body, 0)

    def stored(index, there):
        return pltpu.make_async_copy(
            projected_ref.at[there], projected_out.at[there], store_sems.at[index]
        )

    for load in loads[-2:]:
        load.wait()
    project(own)
    stored(0, own).start()
    for piece in range(pieces):
        rows_out[piece].wait()
        there = pl.ds(pl.multiple_of((1 - mine) * count + piece * LANES, LANES), LANES)
        project(there)
        stored(1 + piece, there).start()
    meta_out.wait()
    meta = rows_ref[...].astype(F32)
    tall = jnp.concatenate([meta, jnp.zeros((LANES - 8, meta.shape[1]), F32)], axis=0)
    columns_ref[...] = jnp.transpose(tall).astype(jnp.int32)
    stored(0, own).wait()
    for piece in range(pieces):
        there = pl.ds(pl.multiple_of((1 - mine) * count + piece * LANES, LANES), LANES)
        stored(1 + piece, there).wait()


def projected_item(layer_in, fields, qkv_weight, query_bias, value_bias, tables):
    rows = 2 * layer_in.shape[1]
    width = layer_in.shape[2]
    pieces = rows // 2 // LANES
    small = list(fields) + [query_bias, value_bias] + [t.T for t in tables]
    return pl.pallas_call(
        project_kernel,
        in_specs=[HBM] * (2 + len(small)),
        out_specs=[VMEM, HBM, VMEM, VMEM, VMEM],
        out_shape=[
            jax.ShapeDtypeStruct((rows, width), BF),
            jax.ShapeDtypeStruct((rows, 3 * width), BF),
            jax.ShapeDtypeStruct((rows, LANES), jnp.int32),
            jax.ShapeDtypeStruct((8, rows), jnp.int32),
            jax.ShapeDtypeStruct((16, LANES), F32),
        ],
        scratch_shapes=[
            pltpu.VMEM((rows, 3 * width), BF),
            pltpu.VMEM((width, 3 * width), BF),
            pltpu.VMEM((8, rows // 2), jnp.int32),
            pltpu.VMEM((1, 3 * width), F32),
            pltpu.SemaphoreType.DMA((2, pieces + 1)),
            pltpu.SemaphoreType.DMA((len(small) + 2,)),
            pltpu.SemaphoreType.DMA((pieces + 1,)),
        ]
        + [pltpu.VMEM(array.shape, array.dtype) for array in small],
        compiler_params=pltpu.CompilerParams(
            collective_id=1, has_side_effects=True, vmem_limit_bytes=60 * MIB
        ),
        name="projected_item",
    )(layer_in, qkv_weight, *small)


EPSILON = 1e-05
TILE = 256


def vector(ref):
    return ref[...].astype(F32).reshape(1, ref.shape[0])


def gelu_and_slope(x):
    bell = jnp.exp2(-0.7213475204444817 * (x * x))
    rough = 1.0 + 0.23164188826 * jnp.abs(x)
    t = pl.reciprocal(rough, approx=True)
    t = t * (2.0 - rough * t)
    series = t * (
        0.127414796
        + t * (-0.142248368 + t * (0.7107068705 + t * (-0.7265760135 + t * 0.5307027145)))
    )
    tail = bell * series
    below = jnp.where(x >= 0.0, 1.0 - tail, tail)
    return x * below, below + x * (0.3989422804014327 * bell)


def row_mean(block):
    return jnp.mean(block, axis=1, keepdims=True)


def normalized(hidden):
    center = hidden - row_mean(hidden)
    scale = lax.rsqrt(row_mean(center * center) + EPSILON)
    return center * scale, scale


def norm_pulled(grad, unit, scale):
    return scale * (grad - row_mean(grad) - unit * row_mean(grad * unit))


def column_sum(block):
    return jnp.sum(block, axis=0, keepdims=True)


def feed_kernel(
    item_hbm, mixed_hbm, cotangent_ref, out_weight_ref, up_ref, down_ref, *refs,
):
    vectors_hbm, refs = refs[:7], refs[7:]
    (layer_out, total_out, unit_out, scale_out, grad_down_ref, grad_up_ref, small_ref,
     item_ref, mixed_ref, layer_ref, cotangent_all, active, slope, unit, scale_ref, normed, normed_t, total, d_branch, d_branch_t,
     sems, load_sems, tile_sems, store_sems) = refs[:24]
    vectors = refs[24:]
    (out_bias_ref, attn_gain_ref, attn_shift_ref, up_bias_ref, down_bias_ref, ffn_gain_ref,
     ffn_shift_ref) = vectors
    step = pl.program_id(0)
    blocks = pl.num_programs(0) // 2
    rows, width = item_hbm.shape
    count = rows // 2
    mine = lax.axis_index("seq")
    partner = (1 - mine, lax.axis_index("dp"))
    own = pl.ds(pl.multiple_of(mine * count, LANES), count)
    tiles = rows // TILE

    def sent():
        return remote(
            cotangent_ref.at[1 - mine], cotangent_all.at[own], sems.at[0], sems.at[1], partner
        )

    def returned():
        theirs = pl.ds(pl.multiple_of((1 - mine) * count, LANES), count)
        return [
            pltpu.make_async_copy(layer_ref.at[own], layer_out.at[mine], load_sems.at[8]),
            remote(
                layer_ref.at[theirs], layer_out.at[mine], sems.at[2], sems.at[3], partner
            ),
        ]

    def tile_loads(tile):
        there = pl.ds(tile * TILE, TILE)
        return [
            pltpu.make_async_copy(source.at[there], target.at[there], tile_sems.at[index, tile])
            for index, (source, target) in enumerate(
                ((mixed_hbm, mixed_ref), (item_hbm, item_ref))
            )
        ]

    def store(index):
        source, target = (
            (total, total_out), (unit, unit_out), (scale_ref, scale_out),
        )[index]
        return pltpu.make_async_copy(source, target, store_sems.at[index])

    def loads():
        copies = list(zip(vectors_hbm, vectors)) + [(cotangent_ref.at[mine], cotangent_all.at[own])]
        return [
            pltpu.make_async_copy(source, target, load_sems.at[index])
            for index, (source, target) in enumerate(copies)
        ]

    def over_tiles(size, body, carry, unroll=1):
        def run(index, state):
            return body(pl.ds(pl.multiple_of(index * size, size), size), state)

        return lax.fori_loop(0, rows // size, run, carry, unroll=unroll)

    @pl.when(step == 0)
    def _():
        for index in range(rows // TILE):
            for load in tile_loads(index):
                load.start()
        for load in loads():
            load.start()
        barrier = pltpu.get_barrier_semaphore()
        pl.semaphore_signal(barrier, inc=1, device_id=partner, device_id_type=MESH)
        pl.semaphore_wait(barrier, 1)
        sent().start()
        small_ref[...] = jnp.zeros_like(small_ref)
        for load in loads():
            load.wait()
        out_bias, gain, shift = vector(out_bias_ref), vector(attn_gain_ref), vector(attn_shift_ref)

        for index in range(rows // TILE):
            for load in tile_loads(index):
                load.wait()
            there = slice(index * TILE, index * TILE + TILE)
            attn = dot_nn(mixed_ref[there].astype(BF), out_weight_ref[...]) + out_bias
            standard, scale = normalized(item_ref[there].astype(F32) + attn)
            unit[there] = standard
            scale_ref[there] = jnp.broadcast_to(scale, (TILE, LANES))
            result = standard * gain + shift
            normed[there] = result.astype(BF)
            normed_t[:, there] = jnp.transpose(result).astype(BF)
        store(1).start()
        store(2).start()
        total[...] = jnp.zeros_like(total)

    @pl.when(step < blocks)
    def _():
        columns = [slice(begin, begin + TILE) for begin in range(0, width, TILE)]
        low = normed[...]
        following = dot_nn(low, up_ref[:, columns[0]])
        values = []
        for index, here in enumerate(columns):
            product = following
            if index + 1 < len(columns):
                following = dot_nn(low, up_ref[:, columns[index + 1]])
            bias = up_bias_ref[pl.ds(pl.multiple_of(step * width + here.start, LANES), TILE)]
            value, grade = gelu_and_slope(product + bias.astype(F32).reshape(1, TILE))
            values.append(value.astype(BF))
            active[step, :, here] = values[-1]
            slope[step, :, here] = grade.astype(BF)
        values = jnp.concatenate(values, axis=1)
        for here in columns:
            total[:, here] += dot_nn(values, down_ref[:, here])

    @pl.when(step == blocks)
    def _():
        sent().wait()
        gain, shift, bias = vector(ffn_gain_ref), vector(ffn_shift_ref), vector(down_bias_ref)
        first_gain, first_shift = vector(attn_gain_ref), vector(attn_shift_ref)

        def tile(there, sums):
            hidden = unit[there] * first_gain + first_shift + (total[there] + bias)
            standard, scale = normalized(hidden)
            layer_ref[there] = (standard * gain + shift).astype(BF)
            cotangent = cotangent_all[there].astype(F32)
            pulled = norm_pulled(cotangent * gain, standard, scale)
            total[there] = pulled
            low = pulled.astype(BF)
            d_branch[there] = low
            return (
                sums[0] + column_sum(low.astype(F32)),
                sums[1] + column_sum(cotangent * standard),
                sums[2] + column_sum(cotangent),
            )

        zero = jnp.zeros((1, width), F32)
        sums = over_tiles(64, tile, (zero, zero, zero), 4)
        for row, value in zip((5, 6, 7), sums):
            small_ref[row : row + 1] = value

        for copy in returned():
            copy.start()

        def turn(there, carry):
            d_branch_t[:, there] = jnp.transpose(d_branch[there].astype(F32)).astype(BF)
            return carry

        over_tiles(TILE, turn, 0, 3)

    @pl.when(step >= blocks)
    def _():
        block = step - blocks

        columns = [slice(begin, begin + TILE) for begin in range(0, width, TILE)]
        branch = d_branch[...]
        turned = d_branch_t[...]
        following = dot_nt(branch, down_ref[columns[0]])
        values = []
        for index, here in enumerate(columns):
            product = following
            if index + 1 < len(columns):
                following = dot_nt(branch, down_ref[columns[index + 1]])
            grad_down_ref[:, here] = dot_nn(turned, active[block, :, here]).astype(BF)
            d_up = (product * slope[block, :, here].astype(F32)).astype(BF)
            small_ref[pl.ds(8 + block, 1), here] = column_sum(d_up.astype(F32))
            values.append(d_up)
        values = jnp.concatenate(values, axis=1)
        turned = normed_t[...]
        for here in columns:
            grad_up_ref[:, here] = dot_nn(turned, values[:, here]).astype(BF)
            total[:, here] += dot_nt(values, up_ref[here])

    @pl.when(step == 2 * blocks - 1)
    def _():
        store(0).start()
        for copy in returned() + [store(0), store(1), store(2)]:
            copy.wait()


def fed_forward_and_back(
    item, mixed, cotangent, out_weight, up_weight, down_weight, vectors,
):
    rows, width = item.shape
    blocks = up_weight.shape[1] // width
    whole = pl.BlockSpec(memory_space=pltpu.VMEM)
    square = lambda kind: jax.ShapeDtypeStruct((rows, width), kind)
    later = lambda i: jnp.maximum(i - blocks, 0)
    return pl.pallas_call(
        feed_kernel,
        grid=(2 * blocks,),
        in_specs=[HBM, HBM, HBM, whole]
        + [
            pl.BlockSpec((width, width), lambda i: (0, lax.rem(i, blocks))),
            pl.BlockSpec((width, width), lambda i: (lax.rem(i, blocks), 0)),
        ]
        + [HBM] * 7,
        out_specs=[HBM] * 4
        + [
            pl.BlockSpec((width, width), lambda i: (later(i), 0)),
            pl.BlockSpec((width, width), lambda i: (later(i), 0)),
            whole,
        ],
        out_shape=[
            jax.ShapeDtypeStruct((2, rows // 2, width), BF), square(F32), square(F32),
            jax.ShapeDtypeStruct((rows, LANES), F32),
            jax.ShapeDtypeStruct((blocks * width, width), BF),
            jax.ShapeDtypeStruct((blocks * width, width), BF),
            jax.ShapeDtypeStruct((16, width), F32),
        ],
        scratch_shapes=[
            pltpu.VMEM((rows, width), BF),
            pltpu.VMEM((rows, width), F32),
            pltpu.VMEM((rows, width), BF),
            pltpu.VMEM((rows, width), BF),
            pltpu.VMEM((blocks, rows, width), BF),
            pltpu.VMEM((blocks, rows, width), BF),
            pltpu.VMEM((rows, width), F32),
            pltpu.VMEM((rows, LANES), F32),
            pltpu.VMEM((rows, width), BF),
            pltpu.VMEM((width, rows), BF),
            pltpu.VMEM((rows, width), F32),
            pltpu.VMEM((rows, width), BF),
            pltpu.VMEM((width, rows), BF),
            pltpu.SemaphoreType.DMA((4,)),
            pltpu.SemaphoreType.DMA((9,)),
            pltpu.SemaphoreType.DMA((2, rows // TILE)),
            pltpu.SemaphoreType.DMA((3,)),
        ]
        + [pltpu.VMEM(vector.shape, vector.dtype) for vector in vectors],
        compiler_params=pltpu.CompilerParams(
            collective_id=2, has_side_effects=True, vmem_limit_bytes=60 * MIB
        ),
        name="feed_forward",
    )(item, mixed, cotangent, out_weight, up_weight, down_weight, *vectors)


SLOTS = 4


def finish_kernel(
    main_ref, tail_ref, input_hbm, small_ref, diagonal_ref,
    down_ref, up_ref, out_ref, qkv_ref, input_ref, *refs,
):
    singles, (main_in, tail_in, slots, input_in, input_slot, in_sems, out_sems, item_sems) = (
        refs[:12], refs[12:],
    )
    mains, width = main_in.shape[0], main_in.shape[2]
    pairs, across = tail_in.shape[0], tail_in.shape[2]
    hidden = mains // 2
    blocks = mains + pairs

    def load(block):
        if block < mains:
            source, target = main_ref.at[pl.ds(block * width, width)], main_in.at[block]
        else:
            pair = block - mains
            source, target = tail_ref.at[pl.ds(pair * TAIL_ROWS, TAIL_ROWS)], tail_in.at[pair]
        return pltpu.make_async_copy(source, target, in_sems.at[block])

    def stores(block):
        slot, sem = slots.at[block % SLOTS], out_sems.at[block % SLOTS]
        if block < hidden:
            targets = [(slot, down_ref.at[pl.ds(block * width, width)])]
        elif block < mains:
            targets = [(slot, up_ref.at[:, pl.ds((block - hidden) * width, width)])]
        else:
            pair = block - mains
            targets = [
                (
                    slot.at[:, pl.ds(part * LANES, LANES)],
                    qkv_ref.at[:, pl.ds(part * width + pair * LANES, LANES)],
                )
                for part in range(3)
            ]
            down = pl.ds(0, TAIL_ROWS - width)
            targets.append(
                (slot.at[down, pl.ds(across, across)], out_ref.at[out_spot(pair, pairs, width)])
            )
        return [
            pltpu.make_async_copy(source, target, sem.at[index])
            for index, (source, target) in enumerate(targets)
        ]

    load_input = pltpu.make_async_copy(input_hbm, input_in, item_sems.at[0])
    store_input = pltpu.make_async_copy(input_slot, input_ref, item_sems.at[1])
    for block in range(blocks):
        load(block).start()
    load_input.start()
    for block in range(blocks):
        load(block).wait()
        if block >= SLOTS:
            for copy in stores(block - SLOTS):
                copy.wait()
        slot = block % SLOTS
        if block < hidden:
            slots[slot] = jnp.transpose(main_in[block].astype(F32))
        elif block < mains:
            slots[slot] = main_in[block].astype(F32)
        else:
            slots[slot, :, :across] = tail_in[block - mains, :width].astype(F32)
            slots[slot, : TAIL_ROWS - width, across:] = tail_in[block - mains, width:].astype(F32)
        for copy in stores(block):
            copy.start()
    load_input.wait()
    input_slot[...] = input_in[...].astype(F32)
    store_input.start()
    for row in range(8):
        singles[row][...] = small_ref[row]
    for row in range(hidden):
        singles[8][row * width : row * width + width] = small_ref[8 + row]
    heads, levels = singles[9].shape
    diagonals = diagonal_ref[...]
    level = lax.broadcasted_iota(jnp.int32, (LANES, LANES), 1)
    lane = lax.broadcasted_iota(jnp.int32, (LANES, LANES), 0)
    for table, (first, size, skip) in enumerate(((0, 4, 0), (4, 2, 1), (6, 2, 1))):
        total = jnp.zeros((heads, LANES), F32)
        for row in range(size):
            distance = lane + LANES * (row + skip - 2)
            chosen = (bucket(distance) == level).astype(F32)
            total = total + jnp.dot(
                diagonals[:, first + row, :], chosen, preferred_element_type=F32,
                precision=lax.Precision.HIGHEST,
            )
        singles[9 + table][...] = total[:, :levels]
    for block in range(blocks - SLOTS, blocks):
        for copy in stores(block):
            copy.wait()
    store_input.wait()


def finished(main, tail, grad_input, small, diagonals, hidden, levels):
    width = main.shape[1]
    heads = diagonals.shape[0]
    mains = main.shape[0] // width
    pairs = tail.shape[0] // TAIL_ROWS
    single = jax.ShapeDtypeStruct((width,), F32)
    table = jax.ShapeDtypeStruct((heads, levels), F32)
    dma = pltpu.SemaphoreType.DMA
    return pl.pallas_call(
        finish_kernel,
        in_specs=[HBM, HBM, HBM, VMEM, VMEM],
        out_specs=[HBM] * 5 + [VMEM] * 12,
        out_shape=[
            jax.ShapeDtypeStruct((hidden, width), F32),
            jax.ShapeDtypeStruct((width, hidden), F32),
            jax.ShapeDtypeStruct((width, width), F32),
            jax.ShapeDtypeStruct((width, 3 * width), F32),
            jax.ShapeDtypeStruct(grad_input.shape, F32),
        ]
        + [single] * 8
        + [jax.ShapeDtypeStruct((hidden,), F32)]
        + [table] * 3,
        scratch_shapes=[
            pltpu.VMEM((mains, width, width), BF),
            pltpu.VMEM((pairs, TAIL_ROWS, tail.shape[1]), BF),
            pltpu.VMEM((SLOTS, width, width), F32),
            pltpu.VMEM(grad_input.shape, BF),
            pltpu.VMEM(grad_input.shape, F32),
            dma((mains + pairs,)),
            dma((SLOTS, 4)),
            dma((2,)),
        ],
        compiler_params=pltpu.CompilerParams(vmem_limit_bytes=56 * MIB),
        name="finished",
    )(main, tail, grad_input, small, diagonals)


PIECE = 16


class Place:
    def __init__(self, depth):
        place = lax.axis_index("dp")
        self.depth = depth
        self.group = lax.div(place, 4 * depth)
        self.z = lax.rem(lax.div(place, 4), depth)
        self.bits = {
            "x": lax.axis_index("seq"),
            "c": lax.rem(place, 2),
            "y": lax.rem(lax.div(place, 2), 2),
            "a": lax.rem(self.z, 2),
            "b": lax.div(self.z, 2),
        }

    def partner(self, letters):
        bit = {
            letter: 1 - value if letter in letters else value
            for letter, value in self.bits.items()
        }
        z = self.z
        for letter, reach in (("a", 1), ("b", 2)):
            if letter in letters:
                z = z + reach - 2 * reach * self.bits[letter]
        return (bit["x"], (self.group * self.depth + z) * 4 + bit["y"] * 2 + bit["c"])

    def greet(self, met):
        barrier = pltpu.get_barrier_semaphore()
        for letters in met:
            pl.semaphore_signal(
                barrier, inc=1, device_id=self.partner(letters), device_id_type=MESH
            )
        pl.semaphore_wait(barrier, len(met))


def letters_of(depth):
    return "xy" + "ab"[: (depth - 1).bit_length()]


def parsed(routes, depth):
    kept = letters_of(depth)
    parts = []
    for route in routes.split():
        hops = ["".join(letter for letter in hop if letter in kept) for hop in route.split(".")]
        parts.append([hop for hop in hops if hop])
    return parts


def subsets(hop):
    return [
        "".join(letter for index, letter in enumerate(hop) if mask >> index & 1)
        for mask in range(1, 2 ** len(hop))
    ]


class Chunk:
    def __init__(self, place, depth, source, out_ref, offset, spot, scratch):
        _, self.begin, rows, first, columns, _, routes, _ = spot
        self.place, self.source, self.columns = place, source, pl.ds(first, columns)
        self.out_ref, self.out_begin = out_ref, offset + self.begin
        self.parts = parsed(routes, depth)
        self.half = rows // 2
        self.share = self.half // len(self.parts)
        self.hops = max(len(part) for part in self.parts)
        self.work, self.fresh, *landing, self.sends, self.receives, self.locals = scratch
        self.landing = {}
        self.sems = {}
        count = 2
        for part, hops in enumerate(self.parts):
            for hop, letters in enumerate(hops):
                self.landing[part, hop] = landing.pop(0)
                for way in range(2):
                    for index in range(2 ** len(letters) - 1):
                        self.sems[way, part, hop, index] = count
                        count += 1

    def aligned(self, value):
        return pl.multiple_of(value, PIECE)

    def size(self, part, hop):
        return self.share >> sum(len(letters) for letters in self.parts[part][: hop + 1])

    def spot(self, part, hop, other=""):
        start = part * self.share
        for level in range(hop + 1):
            for index, letter in enumerate(self.parts[part][level]):
                bit = self.place.bits[letter]
                if level == hop and letter in other:
                    bit = 1 - bit
                start = start + bit * (self.size(part, level) << index)
        return start

    def out(self, core):
        begin = self.aligned(self.out_begin + core * self.half)
        return self.out_ref.at[pl.ds(begin, self.half), self.columns]

    def held(self, buffer, begin, size):
        return buffer.at[pl.ds(self.aligned(begin), size)]

    def copy(self, index, source, target, letters):
        return remote(
            source, target, self.sends.at[index], self.receives.at[index],
            self.place.partner(letters),
        )

    def pair_down(self):
        core = self.place.bits["c"]
        at = lambda c: self.source.at[
            pl.ds(self.aligned(self.begin + c * self.half), self.half), self.columns
        ]
        return [
            self.copy(0, at(1 - core), self.fresh, "c"),
            pltpu.make_async_copy(at(core), self.work, self.locals.at[0]),
        ]

    def pair_up(self, arriving):
        core = self.place.bits["c"]
        return [
            self.copy(1, self.fresh, self.out(1 - core if arriving else core), "c"),
            pltpu.make_async_copy(self.fresh, self.out(core), self.locals.at[1]),
        ]

    def at_hop(self, hop):
        return [
            (part, hops[hop]) for part, hops in enumerate(self.parts) if hop < len(hops)
        ]

    def down(self, hop):
        copies = []
        for part, letters in self.at_hop(hop):
            size = self.size(part, hop)
            for index, other in enumerate(subsets(letters)):
                copies.append(
                    self.copy(
                        self.sems[0, part, hop, index],
                        self.held(self.work, self.spot(part, hop, other), size),
                        self.landing[part, hop].at[index], other,
                    )
                )
        return copies

    def up(self, hop, arriving):
        copies = []
        for part, letters in self.at_hop(hop):
            mine = self.spot(part, hop)
            size = self.size(part, hop)
            for index, other in enumerate(subsets(letters)):
                target = self.spot(part, hop, other) if arriving else mine
                copies.append(
                    self.copy(
                        self.sems[1, part, hop, index], self.held(self.fresh, mine, size),
                        self.held(self.fresh, target, size), other,
                    )
                )
        return copies

    def add(self, begin, sources, size):
        step = 64 if size % 64 == 0 else 32 if size % 32 == 0 else PIECE

        def body(index, carry):
            offset = self.aligned(index * step)
            there = pl.ds(self.aligned(begin + offset), step)
            total = self.work[there]
            if len(sources) == 1:
                total = total + sources[0][pl.ds(offset, step)]
            else:
                total = total.astype(F32)
                for source in sources:
                    total = total + source[pl.ds(offset, step)].astype(F32)
            self.work[there] = total.astype(BF)
            return carry

        lax.fori_loop(0, size // step, body, 0)

    def stage(self, number):
        hops = self.hops
        ended, started = [], []
        if number == 0:
            started = self.pair_down()
        elif number == 1:
            ended = self.pair_down()
            started = self.down(0)
        elif number <= hops:
            ended = self.down(number - 2)
            started = self.down(number - 1)
        elif number == hops + 1:
            ended = self.down(hops - 1)
            started = self.up(hops - 1, False)
        elif number <= 2 * hops:
            level = 2 * hops + 1 - number
            ended = self.up(level, True)
            started = self.up(level - 1, False)
        elif number == 2 * hops + 1:
            ended = self.up(0, True)
            started = self.pair_up(False)
        else:
            ended = self.pair_up(True)
        for copy in ended:
            copy.wait()
        if number == 1:
            self.add(0, [self.fresh], self.half)
        elif 2 <= number <= hops + 1:
            hop = number - 2
            for part, letters in self.at_hop(hop):
                landing = self.landing[part, hop]
                sources = [landing.at[index] for index in range(2 ** len(letters) - 1)]
                self.add(self.spot(part, hop), sources, self.size(part, hop))
        if number == hops + 1:
            for part, route in enumerate(self.parts):
                last = len(route) - 1
                there = pl.ds(self.aligned(self.spot(part, last)), self.size(part, last))
                self.fresh[there] = self.work[there]
        for copy in started:
            copy.start()


def chunk_scratch(spot, depth):
    _, _, rows, _, columns, _, routes, _ = spot
    parts = parsed(routes, depth)
    landing = []
    copies = 2
    for hops in parts:
        size = rows // 2 // len(parts)
        for letters in hops:
            size >>= len(letters)
            others = 2 ** len(letters) - 1
            copies += 2 * others
            landing.append(pltpu.VMEM((others, size, columns), BF))
    dma = pltpu.SemaphoreType.DMA
    return (
        [pltpu.VMEM((rows // 2, columns), BF)] * 2
        + landing
        + [dma((copies,)), dma((copies,)), dma((2,))]
    )


def loads_of(hop, size):
    if "x" in hop and "y" in hop:
        return [("x", 2 * size), ("y", 2 * size)]
    if hop in ("x", "y"):
        return [(hop, size)]
    if "a" in hop and "b" in hop:
        return [("end", 3 * size), ("middle", 4 * size)]
    return [("end", size), ("middle", 2 * size)] if hop == "b" else [("end", size)]


def planned(chunks, work, depth, hop_count):
    latency, issue, link, pair = 3.5, 0.08, 100e3, 600e3
    free = {}
    now = 3.0
    chains = []
    for rows, columns, need, routes, _ in chunks:
        parts = parsed(routes, depth)
        sizes = [rows // 2 // len(parts)] * len(parts)
        down = []
        for hop in range(max(len(part) for part in parts)):
            loads, copies, added = [], 0, 0
            for index, part in enumerate(parts):
                if hop < len(part):
                    sizes[index] >>= len(part[hop])
                    others = 2 ** len(part[hop]) - 1
                    loads += loads_of(part[hop], sizes[index])
                    copies += others
                    added += sizes[index] * others
            down.append((loads, copies, added, columns))
        first = [([("core", rows // 2)], 1.5, rows // 2, columns)]
        last = [([("core", rows // 2)], 1, 0, columns)]
        chains.append((need, first + down + down[::-1] + last))
    chains.append((len(work), [([("core", 16)], 2, 0, 768)] * hop_count))
    ranks = [chunk[4] for chunk in chunks] + [0]
    position = [0] * len(chains)
    ready = [0.0] * len(chains)
    order = [[] for _ in range(len(work) + 1)]
    done = 0
    while True:
        open_ones = [
            (ranks[i], ready[i], i) for i, (need, chain) in enumerate(chains)
            if position[i] <= len(chain) and need <= done
        ]
        due = [entry for entry in open_ones if entry[1] <= now]
        if not due and done < len(work):
            now += work[done]
            done += 1
            continue
        if not open_ones:
            return order
        _, when, index = min(due) if due else min(open_ones, key=lambda entry: entry[1])
        now = max(now, when)
        chain = chains[index][1]
        stage = position[index]
        order[done].append((index, stage))
        if 0 < stage <= len(chain) // 2:
            now += 1e-6 * chain[stage - 1][2] * chain[stage - 1][3]
        if stage < len(chain):
            loads, copies, _, columns = chain[stage]
            now += issue * copies
            end = now
            for lane, rows in loads:
                rate = pair if lane == "core" else link / 2
                free[lane] = max(now, free.get(lane, 0.0)) + 2 * rows * columns / rate
                end = max(end, free[lane])
            ready[index] = end + latency
        position[index] += 1


def last_kernel(
    depth, plan, orders, counts, *refs,
):
    (meta_ref, rows_ref, projected_hbm, mixed_hbm, log_ref, first_hbm, second_hbm,
     key_image_hbm, bias_hbm, small_ref, gain_ref, item_hbm, weight_hbm, total_hbm, unit_hbm, scale_hbm,
     out_weight_hbm, grad_down_ref, grad_up_ref,
     main_out, tail_out, small_out, diagonal_out, input_out,
     *scratch) = refs
    static, scratch = scratch[:6], scratch[6:]
    (k_ref, v_ref, mixed_ref, grad_ref, first_ref, second_ref, key_image_ref, bias_ref, pair_sems,
     item_ref, weight_ref, d_hidden_ref, unit_ref, scale_ref, load_sems, d_project, item_t, tail, input_grad,
     small_in, diagonal_in, small_sems, item_sems, *scratch) = scratch
    out_weight_ref = item_t
    place = Place(depth)
    step = pl.program_id(0)
    pairs = k_ref.shape[0]
    rows, width = item_hbm.shape
    count = rows // 2
    x = place.bits["x"]
    hidden = grad_down_ref.shape[0]
    sources = ((grad_down_ref, main_out, 0), (grad_up_ref, main_out, hidden), (tail, tail_out, 0))
    chunks = []
    for spot, pieces in zip(plan, counts):
        chunks.append(Chunk(place, depth, *sources[spot[0]], spot, scratch[:pieces]))
        scratch = scratch[pieces:]
    hop_letters = "c" + letters_of(depth)
    wide_hbm = (first_hbm, second_hbm, key_image_hbm, bias_hbm)
    wide_refs = (first_ref, second_ref, key_image_ref, bias_ref)

    def pair_loads(pair):
        copies = []
        held = ((projected_hbm, k_ref, width), (projected_hbm, v_ref, 2 * width))
        for source, target, first in held:
            columns = pl.ds(pl.multiple_of(first + pair * LANES, LANES), LANES)
            copies.append((source.at[:, columns], target.at[pair]))
        heads = pl.ds(2 * pair, 2)
        for source, target in zip(wide_hbm, wide_refs):
            copies.append((source.at[heads], target.at[heads]))
        return [
            pltpu.make_async_copy(source, target, pair_sems.at[pair, index])
            for index, (source, target) in enumerate(copies)
        ]

    def loads(first):
        if first:
            copies = [
                (total_hbm, d_hidden_ref), (unit_hbm, unit_ref), (scale_hbm, scale_ref),
                (out_weight_hbm, out_weight_ref), (item_hbm, item_ref),
            ]
            copies += [
                (mixed_hbm.at[:, pl.ds(pair * LANES, LANES)], mixed_ref.at[pair])
                for pair in range(pairs)
            ]
        else:
            copies = [(weight_hbm, weight_ref)]
        return [
            pltpu.make_async_copy(source, target, load_sems.at[0 if first else 1, index])
            for index, (source, target) in enumerate(copies)
        ]

    def back_to_attention():
        gain = vector(gain_ref)

        def tile(index, sums):
            there = pl.ds(pl.multiple_of(index * 64, 64), 64)
            d_normed = d_hidden_ref[there]
            standard = unit_ref[there]
            d_hidden = norm_pulled(d_normed * gain, standard, scale_ref[there, :1])
            d_hidden_ref[there] = d_hidden
            low = d_hidden.astype(BF)
            input_grad[there] = low
            return (
                sums[0] + column_sum(low.astype(F32)),
                sums[1] + column_sum(d_normed * standard),
                sums[2] + column_sum(d_normed),
            )

        zero = jnp.zeros((1, width), F32)
        sums = lax.fori_loop(0, rows // 64, tile, (zero, zero, zero), unroll=4)
        for row, value in zip((2, 3, 4), sums):
            small_out[row : row + 1] = value
        low = input_grad[...]
        down = TAIL_ROWS - width
        for begin in range(0, width, down):
            first = begin // LANES
            several = range(first, first + down // LANES)
            d_mixed = dot_nt(low, out_weight_ref[begin : begin + down]).astype(BF)
            for index, pair in enumerate(several):
                grad_ref[pair] = d_mixed[:, index * LANES : index * LANES + LANES]
            turned = jnp.concatenate(
                [jnp.transpose(mixed_ref[pair]).astype(BF) for pair in several], axis=0
            )
            for pair in range(pairs):
                rows_of, across = out_spot(pair, pairs, width)
                if rows_of.start == begin:
                    product = dot_nn(turned, low[:, across.start : across.start + across.size])
                    base = pair * TAIL_ROWS + width
                    tail[base : base + down] = product.astype(BF)

    def input_copies():
        return [
            pltpu.make_async_copy(
                input_grad.at[pl.ds(pl.multiple_of(x * count, LANES), count)], input_out.at[x],
                item_sems.at[0],
            ),
            remote(
                input_grad.at[pl.ds(pl.multiple_of((1 - x) * count, LANES), count)],
                input_out.at[x], item_sems.at[1], item_sems.at[2], place.partner("x"),
            ),
        ]

    def small_copies(hop):
        return [
            remote(source, landing.at[hop], small_sems.at[0, kind, hop],
                   small_sems.at[1, kind, hop], place.partner(hop_letters[hop]))
            for kind, (source, landing) in enumerate(
                ((small_out, small_in), (diagonal_out, diagonal_in))
            )
        ]

    def small_stage(hop):
        if hop > 0:
            for copy in small_copies(hop - 1):
                copy.wait()
            small_out[...] = small_out[...] + small_in[hop - 1]
            diagonal_out[...] = diagonal_out[...] + diagonal_in[hop - 1]
        if hop < len(hop_letters):
            for copy in small_copies(hop):
                copy.start()

    def perform(slot):
        for index, stage in orders[slot]:
            if index == len(chunks):
                small_stage(stage)
            else:
                chunks[index].stage(stage)

    @pl.when(step == 0)
    def _():
        for copy in pair_loads(0) + loads(True):
            copy.start()
        met = set(hop_letters)
        for chunk in chunks:
            for hops in chunk.parts:
                for letters in hops:
                    met.update(subsets(letters))
        place.greet(sorted(met))
        small_out[...] = small_ref[...]

    @pl.when(step == 0)
    def _():
        perform(0)
        for pair in range(1, pairs):
            for copy in pair_loads(pair):
                copy.start()
        for copy in loads(False):
            copy.start()
        static_prepare(meta_ref, static)
        for copy in loads(True):
            copy.wait()
        back_to_attention()
        for tile in range(rows // TILE):
            there = slice(tile * TILE, tile * TILE + TILE)
            item_t[:, there] = jnp.transpose(item_ref[there].astype(F32)).astype(BF)

    for copy in pair_loads(step):
        copy.wait()
    for parity in range(2):
        for pair in range(pairs):
            @pl.when(step == pair)
            def _(pair=pair, parity=parity):
                perform(1 + 2 * pair + parity)

        dq, dk, dv = head_back(
            parity, step, rows_ref, wide_refs, k_ref, v_ref, mixed_ref, grad_ref, log_ref,
            static, diagonal_out,
        )
        empty = jnp.zeros_like(dq)
        both = [dq, empty] if parity == 0 else [empty, dq]
        pieces = [jnp.transpose(jnp.concatenate(both, axis=0)), dk, dv]
        own = own_lanes(parity, rows)
        for part, piece in enumerate(pieces):
            columns = pl.ds(pl.multiple_of(part * width + step * LANES, LANES), LANES)
            piece = piece.astype(BF)
            if parity == 1:
                piece = jnp.where(own, piece, d_project[:, columns])
            d_project[:, columns] = piece
    pieces = [
        d_project[:, pl.ds(pl.multiple_of(part * width + step * LANES, LANES), LANES)]
        for part in range(3)
    ]
    slab = pl.ds(pl.multiple_of(step * TAIL_ROWS, TAIL_ROWS), width)
    tail[slab] = dot_nn(item_t[...], jnp.concatenate(pieces, axis=1)).astype(BF)

    @pl.when(step == 0)
    def _():
        for copy in loads(False):
            copy.wait()

    @pl.when(step == pairs - 1)
    def _():
        perform(2 * pairs + 1)
        for begin in range(0, width, TILE):
            here = slice(begin, begin + TILE)
            total = d_hidden_ref[:, here] + dot_nt(d_project[...], weight_ref[here])
            input_grad[:, here] = total.astype(BF)
        for copy in input_copies():
            copy.start()
        for begin in range(0, width, TILE):
            here = slice(begin, begin + TILE)
            there = slice(2 * width + begin, 2 * width + begin + TILE)
            small_out[0:1, here] = column_sum(d_project[:, here].astype(F32))
            small_out[1:2, here] = column_sum(d_project[:, there].astype(F32))
        perform(2 * pairs + 2)
        for copy in input_copies():
            copy.wait()


TAIL_ROWS = 1024


def out_spot(pair, pairs, width):
    down = TAIL_ROWS - width
    across = width * width // (pairs * down)
    per_row = width // across
    return (
        pl.ds(pair // per_row * down, down),
        pl.ds(pair % per_row * across, across),
    )


def summed_with_attention_back(
    meta_columns, meta_rows, projected, mixed, logs, wide_arrays, item, qkv_weight,
    total, unit, scale, out_weight, attn_gain, small, grad_down, grad_up,
):
    size = lax.axis_size("dp")
    depth = 4 if size % 16 == 0 else size // 4
    rows, width = item.shape
    pairs = width // LANES
    hidden = grad_down.shape[0]
    hops = len(letters_of(depth)) + 1
    work = [9.0] + [3.2, 4.0] * pairs + [4.0]
    tall, wide, slim = 1024, 3 * LANES, 2 * LANES
    plan = [
        (0, 0, 2 * tall, 0, width, 0, "a.b.x.y x.y.a.b", 1),
        (0, 2 * tall, tall, 0, width, 0, "x.a.y.b y.a.b.x", 2),
        (1, 0, 3 * tall, 0, slim, 0, "a.b.x.y y.x.a.b", 4),
        (1, 0, 3 * tall, slim, slim, 0, "y.a.x.b x.y.a.b", 0),
        (1, 0, 3 * tall, 2 * slim, slim, 0, "x.y.a.b y.x.a.b", 2),
        (2, 0, tall, 0, wide, 3, "y.x.a.b a.b.x.y", 3),
        (2, tall, tall, 0, wide, 5, "xy.a.b", 2),
        (2, 2 * tall, tall, 0, wide, 7, "x.y.ab y.ab.x", 3),
        (2, 3 * tall, tall, 0, wide, 9, "xy.a.b", 1),
        (2, 4 * tall, tall, 0, wide, 11, "xy.a.b", 1),
        (2, 5 * tall, tall, 0, wide, 13, "ab.y.x y.ab.x", 2),
    ]
    orders = planned([(spot[2],) + spot[4:] for spot in plan], work, depth, hops)

    whole = pl.BlockSpec(memory_space=pltpu.VMEM)
    diagonals = jax.ShapeDtypeStruct((2 * pairs, 8, LANES), F32)
    dma = pltpu.SemaphoreType.DMA
    scratch = []
    for spot in plan:
        scratch.append(chunk_scratch(spot, depth))
    main, tail, small, diagonals, grad_input = pl.pallas_call(
        functools.partial(last_kernel, depth, plan, orders, [len(pieces) for pieces in scratch]),
        grid=(pairs,),
        in_specs=[whole] * 2 + [HBM] * 2 + [whole] + [HBM] * 4 + [whole] * 2 + [HBM] * 8,
        out_specs=[HBM, HBM, whole, whole, HBM],
        out_shape=[
            jax.ShapeDtypeStruct((2 * hidden, width), BF),
            jax.ShapeDtypeStruct((pairs * TAIL_ROWS, 3 * LANES), BF),
            jax.ShapeDtypeStruct(small.shape, F32),
            diagonals,
            jax.ShapeDtypeStruct((2, rows // 2, width), BF),
        ],
        scratch_shapes=[pltpu.VMEM((rows, LANES), BF)] * 3
        + [pltpu.VMEM((LANES, rows), BF)] * 3
        + [pltpu.VMEM((pairs, rows, LANES), kind) for kind in (BF, BF, F32, BF)]
        + [pltpu.VMEM(array.shape, BF) for array in wide_arrays]
        + [
            dma((pairs, 6)),
            pltpu.VMEM((rows, width), BF),
            pltpu.VMEM((width, 3 * width), BF),
            pltpu.VMEM((rows, width), F32),
            pltpu.VMEM((rows, width), F32),
            pltpu.VMEM((rows, LANES), F32),
            dma((2, 5 + pairs)),
            pltpu.VMEM((rows, 3 * width), BF),
            pltpu.VMEM((width, rows), BF),
            pltpu.VMEM((pairs * TAIL_ROWS, 3 * LANES), BF),
            pltpu.VMEM((rows, width), BF),
            pltpu.VMEM((hops,) + small.shape, F32),
            pltpu.VMEM((hops,) + diagonals.shape, F32),
            dma((2, 2, hops)),
            dma((3,)),
        ]
        + [piece for pieces in scratch for piece in pieces],
        compiler_params=pltpu.CompilerParams(
            collective_id=0, has_side_effects=True, vmem_limit_bytes=62 * MIB
        ),
        name="summed_with_attention_back",
    )(meta_columns, meta_rows, projected, mixed, logs, *wide_arrays,
      small, attn_gain, item, qkv_weight, total, unit, scale, out_weight, grad_down, grad_up)
    span = 4 * depth
    if size > span:
        groups = [list(range(first, size, span)) for first in range(span)]
        main, tail, small, diagonals = lax.psum(
            (main.astype(F32), tail.astype(F32), small, diagonals), "dp",
            axis_index_groups=groups,
        )
        main, tail = main.astype(BF), tail.astype(BF)
    return main, tail, small, diagonals, grad_input


def per_device(
    layer_in, segment, key_mask, position, layout_x, layout_y,
    qkv_weight, query_bias, value_bias, out_weight, out_bias, attn_gain, attn_shift,
    up_weight, up_bias, down_weight, down_bias, ffn_gain, ffn_shift,
    text_table, horiz_table, vert_table, cotangent,
):
    width = layer_in.shape[-1]
    item, projected, meta_columns, meta_rows, table_rows = projected_item(
        layer_in, (segment, key_mask, position, layout_x, layout_y),
        qkv_weight, query_bias, value_bias, (text_table, horiz_table, vert_table),
    )
    mixed, logs, *wide_arrays = attention_forward(meta_columns, meta_rows, table_rows, projected, width)
    layer_out, total, unit, scale, grad_down, grad_up, small = fed_forward_and_back(
        item, mixed, cotangent, out_weight, up_weight, down_weight,
        (out_bias, attn_gain, attn_shift, up_bias, down_bias, ffn_gain, ffn_shift),
    )
    main, tail, small, diagonals, grad_input = summed_with_attention_back(
        meta_columns, meta_rows, projected, mixed, logs, wide_arrays, item, qkv_weight,
        total, unit, scale, out_weight, attn_gain, small, grad_down, grad_up,
    )
    done = finished(
        main, tail, grad_input, small, diagonals, up_weight.shape[1], text_table.shape[0]
    )
    sum_down, sum_up, sum_out, sum_qkv, grad_input = done[:5]
    singles, tables = done[5:14], [t.T for t in done[14:]]
    return (
        layer_out, grad_input, sum_qkv, singles[0], singles[1], sum_out, singles[2], singles[3],
        singles[4], sum_up, singles[8], sum_down, singles[5], singles[6], singles[7],
        tables[0], tables[1], tables[2],
    )


def solution(mesh):
    rows = P("dp", "seq", None)
    marks_spec = P("dp", "seq")
    return jax.shard_map(
        per_device,
        mesh=mesh,
        in_specs=(rows,) + (marks_spec,) * 5 + (P(),) * 16 + (rows,),
        out_specs=(rows, rows) + (P(),) * 16,
        check_vma=False,
    )
```

```python
import functools

import jax
import jax.numpy as jnp
from jax import lax
from jax.experimental import pallas as pl
from jax.experimental.pallas import tpu as pltpu
from jax.sharding import PartitionSpec as P

BF = jnp.bfloat16
F32 = jnp.float32
BIG = 1e30
LANES = 128
HEAD = 64
TEXT = 512
POS = 64
COORD = 48
Y0 = 64
GROUP0 = 112
MEMBER0 = 116
FLAG = 124
EVERY = 125
STRAY = 126
X_TABLE = 33
Y_TABLE = 66
NOTHING = 127


def dot_nt(a, b):
    return lax.dot_general(a, b, (((1,), (1,)), ((), ())), preferred_element_type=F32)


def dot_nn(a, b):
    return lax.dot_general(a, b, (((1,), (0,)), ((), ())), preferred_element_type=F32)


def looked_up(table_row, index):
    rows = index.shape[0]
    return jnp.take_along_axis(
        jnp.broadcast_to(table_row, (rows, LANES)), index, axis=1, mode="promise_in_bounds"
    )


def bucket(distance):
    return jnp.clip(distance, -16, 16) + 16


def between(lane, low, high):
    return (lane >= low) & (lane < high)


def columns_of(meta_ref):
    return tuple(meta_ref[:, field : field + 1] for field in range(5))


def marks(meta_ref):
    segment, key_mask, position, across, down = columns_of(meta_ref)
    rows = segment.shape[0]
    lane = lax.broadcasted_iota(jnp.int32, (rows, LANES), 1)
    row = lax.broadcasted_iota(jnp.int32, (rows, LANES), 0)
    even = between(lane, HEAD, HEAD + COORD) & (lane - HEAD == across)
    odd = (lane < COORD) & (lane == across)
    group = (segment - 1) >> 3
    member = (segment - 1) & 7
    named = segment > 0
    shared = (
        ((row < TEXT) & (lane < POS) & (lane == position))
        | (between(lane, Y0, Y0 + COORD) & (lane - Y0 == down))
        | (named & between(lane, GROUP0, MEMBER0) & (lane - GROUP0 == group))
        | (named & between(lane, MEMBER0, FLAG) & (lane - MEMBER0 == member))
        | ((lane == FLAG) & (key_mask <= 0))
        | (lane == EVERY)
        | ((lane == STRAY) & (segment < 0))
    )
    return tuple(jnp.where(m, 1.0, 0.0).astype(BF) for m in (even, odd, shared))


def square_lanes():
    shape = (LANES, LANES)
    return lax.broadcasted_iota(jnp.int32, shape, 0), lax.broadcasted_iota(jnp.int32, shape, 1)


def barred():
    row, lane = square_lanes()
    in_groups = between(lane, GROUP0, MEMBER0)
    shut = (
        (between(row, GROUP0, MEMBER0) & in_groups & (lane != row))
        | (between(row, MEMBER0, FLAG) & between(lane, MEMBER0, FLAG) & (lane != row))
        | ((row == EVERY) & (lane == FLAG))
        | ((row == STRAY) & in_groups)
    )
    return jnp.where(shut, -BIG, 0.0).astype(F32)


def table_index():
    row, lane = square_lanes()
    distance = bucket(row - lane)
    inside = lambda low, high: between(row, low, high) & between(lane, low, high)
    even = jnp.where(inside(HEAD, HEAD + COORD), distance + X_TABLE, NOTHING)
    odd = jnp.where(inside(0, COORD), distance + X_TABLE, NOTHING)
    shared = jnp.where(
        inside(0, POS), distance, jnp.where(inside(Y0, Y0 + COORD), distance + Y_TABLE, NOTHING)
    )
    return even, odd, shared


def image_query_index(meta_ref):
    position = meta_ref[TEXT:, 2:3]
    lane = lax.broadcasted_iota(jnp.int32, (position.shape[0], LANES), 1)
    return jnp.where(lane < POS, bucket(position - lane), NOTHING)


def prepare(meta_ref, mark_refs, bar_ref, index_refs, image_index_ref):
    for ref, value in zip(mark_refs, marks(meta_ref)):
        ref[...] = value
    bar_ref[...] = barred()
    for ref, value in zip(index_refs, table_index()):
        ref[...] = value
    image_index_ref[...] = image_query_index(meta_ref)


def own_lanes(parity, rows):
    lane = lax.broadcasted_iota(jnp.int32, (rows, LANES), 1)
    return (lane < HEAD) if parity == 0 else (lane >= HEAD)


def widened(parity, q, table_row, bias, bar_ref, index_refs, image_index_ref, mark_refs):
    rows = q.shape[0]
    shared = mark_refs[2][...]
    across = looked_up(table_row, index_refs[parity][...]).astype(BF)
    first = jnp.where(
        own_lanes(parity, rows), q.astype(F32) * 0.125, dot_nn(mark_refs[parity][...], across)
    )
    others = (looked_up(table_row, index_refs[2][...]) + bar_ref[...]).astype(BF)
    second = dot_nn(shared, others)
    on_images = looked_up(table_row, image_index_ref[...])
    second = jnp.concatenate([second[:TEXT], second[TEXT:] + on_images], axis=0)
    image_lane = lax.broadcasted_iota(jnp.int32, on_images.shape, 1)
    key_image = jnp.where(image_lane < POS, bias[:, :LANES].astype(BF), shared[TEXT:])
    return first.astype(BF), second.astype(BF), key_image


def joined(parity, first, second, key_image, k, marks_own, shared):
    rows = k.shape[0]
    lane = lax.broadcasted_iota(jnp.int32, (rows, LANES), 1)
    to_image = jnp.where(lane < POS, shared, second)
    key_first = jnp.where(own_lanes(parity, rows), k, marks_own)
    q_text = jnp.concatenate([first, second], axis=1)
    q_image = jnp.concatenate([first, to_image], axis=1)
    k_text = jnp.concatenate([key_first[:TEXT], shared[:TEXT]], axis=1)
    k_image = jnp.concatenate([key_first[TEXT:], key_image], axis=1)
    return q_text, q_image, k_text, k_image


def near(start, size):
    if start >= TEXT:
        return slice(0, TEXT)
    return slice(max(0, start - LANES), min(TEXT, start + size + LANES))


def image_bias(table_row, offsets):
    return jnp.concatenate(
        [looked_up(table_row, offsets[:, :LANES]), looked_up(table_row, offsets[:, LANES:])], axis=1
    )


def forward_kernel(
    meta_ref, rows_ref, table_ref, q_ref, k_ref, v_ref,
    mixed_ref, log_ref, first_ref, second_ref, key_image_ref, bias_ref,
    even_ref, odd_ref, shared_ref, bar_ref, index_even, index_odd, index_shared, image_index_ref,
):
    mark_refs = (even_ref, odd_ref, shared_ref)
    index_refs = (index_even, index_odd, index_shared)

    @pl.when(pl.program_id(0) == 0)
    def _():
        prepare(meta_ref, mark_refs, bar_ref, index_refs, image_index_ref)

    rows = q_ref.shape[0]
    images = rows - TEXT
    q, k, v = q_ref[...], k_ref[...], v_ref[...]
    offsets = bucket(rows_ref[2:3, TEXT:] - meta_ref[TEXT:, 2:3])
    tile = 256
    v_turned = transposed(v)
    heads = [None, None]

    def prepared(parity):
        table_row = table_ref[pl.ds(2 * pl.program_id(0) + parity, 1), :]
        bias = image_bias(table_row, offsets)
        first, second, key_image = widened(
            parity, q, table_row, bias, bar_ref, index_refs, image_index_ref, mark_refs
        )
        first_ref[parity] = first
        second_ref[parity] = second
        key_image_ref[parity] = key_image
        bias_ref[parity] = bias.astype(BF)
        wide = joined(
            parity, first, second, key_image, k, mark_refs[parity][...], shared_ref[...]
        )
        heads[parity] = wide + (bias,)

    def scored(parity, start):
        q_text, q_image, k_text, k_image, bias = heads[parity]
        here = slice(start, start + tile)
        on_image = dot_nt(k_image, q_image[here])
        if start >= TEXT:
            on_image = on_image + bias[:, start - TEXT : start - TEXT + tile]
        return dot_nt(k_text[near(start, tile)], q_text[here]), on_image

    spots = [(parity, start) for parity in range(2) for start in range(0, rows, tile)]
    outs = ([], [])
    prepared(0)
    following = scored(*spots[0])
    for index, (parity, start) in enumerate(spots):
        on_text, on_image = following
        if index == 1:
            prepared(1)
        if index + 1 < len(spots):
            following = scored(*spots[index + 1])
        top = jnp.maximum(
            jnp.max(on_text, axis=0, keepdims=True), jnp.max(on_image, axis=0, keepdims=True)
        )
        on_text = jnp.exp(on_text - top)
        on_image = jnp.exp(on_image - top)
        total = jnp.sum(on_text, axis=0, keepdims=True) + jnp.sum(on_image, axis=0, keepdims=True)
        own = slice(parity * HEAD, parity * HEAD + HEAD)
        out = dot_nn(v_turned[own, near(start, tile)], on_text.astype(BF)) + dot_nn(
            v_turned[own, TEXT:], on_image.astype(BF)
        )
        outs[parity].append(out * (1.0 / total))
        log_ref[0, parity : parity + 1, start : start + tile] = top + jnp.log(total)
    mixed_ref[...] = jnp.transpose(
        jnp.concatenate([jnp.concatenate(outs[parity], axis=1) for parity in range(2)], axis=0)
    )


def static_scratch(rows):
    square = (LANES, LANES)
    return [
        pltpu.VMEM((rows, LANES), BF),
        pltpu.VMEM((rows, LANES), BF),
        pltpu.VMEM((rows, LANES), BF),
        pltpu.VMEM(square, F32),
        pltpu.VMEM(square, jnp.int32),
        pltpu.VMEM(square, jnp.int32),
        pltpu.VMEM(square, jnp.int32),
        pltpu.VMEM((rows - TEXT, LANES), jnp.int32),
    ]


def attention_forward(meta_columns, meta_rows, table_rows, projected, width):
    rows = projected.shape[0]
    images = rows - TEXT
    pairs = width // LANES

    def block(part):
        return pl.BlockSpec((rows, LANES), lambda p: (0, part * pairs + p))

    whole = lambda shape: pl.BlockSpec(shape, lambda p: (0,) * len(shape))
    return pl.pallas_call(
        forward_kernel,
        grid=(pairs,),
        in_specs=[
            whole(meta_columns.shape),
            whole(meta_rows.shape),
            whole(table_rows.shape),
            block(0), block(1), block(2),
        ],
        out_specs=[
            pl.BlockSpec((rows, LANES), lambda p: (0, p)),
            pl.BlockSpec((1, 2, rows), lambda p: (p, 0, 0)),
            pl.BlockSpec((2, rows, LANES), lambda p: (p, 0, 0)),
            pl.BlockSpec((2, rows, LANES), lambda p: (p, 0, 0)),
            pl.BlockSpec((2, images, LANES), lambda p: (p, 0, 0)),
            pl.BlockSpec((2, images, images), lambda p: (p, 0, 0)),
        ],
        out_shape=[
            jax.ShapeDtypeStruct((rows, width), F32),
            jax.ShapeDtypeStruct((pairs, 2, rows), F32),
            jax.ShapeDtypeStruct((2 * pairs, rows, LANES), BF),
            jax.ShapeDtypeStruct((2 * pairs, rows, LANES), BF),
            jax.ShapeDtypeStruct((2 * pairs, images, LANES), BF),
            jax.ShapeDtypeStruct((2 * pairs, images, images), BF),
        ],
        scratch_shapes=static_scratch(rows),
        compiler_params=pltpu.CompilerParams(vmem_limit_bytes=60 * 1024 * 1024),
        name="attention_forward",
    )(meta_columns, meta_rows, table_rows, projected, projected, projected)


def skewed(block):
    size = block.shape[0]
    lane = lax.broadcasted_iota(jnp.int32, (size, LANES), 1)
    row = lax.broadcasted_iota(jnp.int32, (size, LANES), 0)
    turned = jnp.take_along_axis(
        block, (lane + row) & (LANES - 1), axis=1, mode="promise_in_bounds"
    )
    straight = lane + row < LANES
    above = jnp.sum(jnp.where(straight, turned, 0.0), axis=0, keepdims=True)
    below = jnp.sum(jnp.where(straight, 0.0, turned), axis=0, keepdims=True)
    return above, below


def transposed(array):
    return jnp.transpose(array.astype(F32)).astype(array.dtype)


def static_prepare(meta_ref, static):
    for ref, turned, value in zip(static[:3], static[3:], marks(meta_ref)):
        ref[...] = value
        turned[...] = transposed(value)


def head_back(
    parity, pair, rows_ref, wide_refs, k_ref, v_ref, mixed_ref, grad_ref, log_ref, static, diag_ref,
):
    mark_refs, turned_refs = static[:3], static[3:]
    first_ref, second_ref, key_image_ref, bias_ref = wide_refs
    head = 2 * pair + parity
    shared_t = turned_refs[2]
    rows = k_ref.shape[1]
    images = rows - TEXT
    tile = 256
    k, v, grad = k_ref[pair], v_ref[pair], grad_ref[pair]
    products = grad.astype(F32) * mixed_ref[pair]
    k_turned = transposed(k)
    is_image = rows_ref[1:2, TEXT:] > 0
    own = own_lanes(parity, rows)
    log_row = log_ref[pair, parity : parity + 1, :]
    first, shared = first_ref[head], mark_refs[2][...]
    q_text, q_image, k_text, k_image = joined(
        parity, first, second_ref[head], key_image_ref[head], k, mark_refs[parity][...], shared
    )
    bias = bias_ref[head].astype(F32)
    ones = jnp.where(own_lanes(parity, 8), 1.0, 0.0).astype(BF)
    delta = jnp.zeros((8, rows), F32)
    rest = products
    for _ in range(3):
        piece = rest.astype(BF)
        delta = delta + dot_nt(ones, piece)
        rest = rest - piece.astype(F32)
    delta = delta[0:1]
    v_own = jnp.where(own, v, jnp.zeros_like(v))
    q_marked = jnp.concatenate(
        [jnp.where(own, first, mark_refs[parity][...]), shared], axis=1
    )
    dq_text = jnp.zeros((HEAD, TEXT), F32)
    dq_image = jnp.zeros((HEAD, images), F32)
    dks = []
    dvs = []
    first_sum = jnp.zeros((LANES, LANES), F32)
    second_sum = jnp.zeros((LANES, LANES), F32)
    text_image = jnp.zeros((LANES, images), F32)

    def met(start, array, axis=0):
        text = near(start, tile)
        if axis == 0:
            return jnp.concatenate([array[text], array[TEXT:]], axis=0)
        return jnp.concatenate([array[:, text], array[:, TEXT:]], axis=1)

    def scored(start):
        here = slice(start, start + tile)
        if start < TEXT:
            scores = dot_nt(k_text[here], met(start, q_text))
        else:
            scores = dot_nt(k_image[start - TEXT : start - TEXT + tile], q_image)
            scores = jnp.concatenate([scores[:, :TEXT], scores[:, TEXT:] + bias], axis=1)
        return scores, dot_nt(v_own[here], met(start, grad))

    following = scored(0)
    for start in range(0, rows, tile):
        here = slice(start, start + tile)
        scores, prob_grad = following
        if start + tile < rows:
            following = scored(start + tile)
        soft = jnp.exp(scores - met(start, log_row, 1))
        score_grad = soft * (prob_grad - met(start, delta, 1))
        low = score_grad.astype(BF)
        dvs.append(dot_nn(soft.astype(BF), met(start, grad)))
        wide = dot_nn(low, met(start, q_marked))
        dks.append(wide[:, :LANES])
        part = dot_nn(k_turned[parity * HEAD : parity * HEAD + HEAD, here], low)
        text = near(start, tile)
        count = text.stop - text.start
        before = [jnp.zeros((HEAD, text.start), F32)] if text.start > 0 else []
        after = [jnp.zeros((HEAD, TEXT - text.stop), F32)] if text.stop < TEXT else []
        dq_text = dq_text + jnp.concatenate(before + [part[:, :count]] + after, axis=1)
        dq_image = dq_image + part[:, count:]
        rounded = wide.astype(BF)
        first_sum = first_sum + dot_nn(turned_refs[parity][:, here], rounded[:, :LANES])
        second_sum = second_sum + dot_nn(shared_t[:, here], rounded[:, LANES:])
        if start < TEXT:
            text_image = text_image + dot_nn(shared_t[:, here], low[:, count:])
        else:
            by_position = wide[:, LANES:]
            on_image = score_grad[:, TEXT:]
    dq = jnp.concatenate([dq_text, dq_image], axis=1)
    small = lax.broadcasted_iota(jnp.int32, (LANES, LANES), 1)
    small_row = lax.broadcasted_iota(jnp.int32, (LANES, LANES), 0)
    x0 = HEAD if parity == 0 else 0
    x_block = jnp.where(
        between(small, x0, x0 + COORD) & between(small_row, x0, x0 + COORD), first_sum, 0.0
    )
    y_block = jnp.where(
        between(small, Y0, Y0 + COORD) & between(small_row, Y0, Y0 + COORD), second_sum, 0.0
    )
    p_block = jnp.where((small < POS) & (small_row < POS), second_sum, 0.0)
    wide_lane = lax.broadcasted_iota(jnp.int32, (images, images), 1)
    outside = jnp.sum(jnp.where(is_image, 0.0, on_image), axis=1, keepdims=True)
    pairs = jnp.where(is_image, on_image, 0.0) + jnp.where(wide_lane == 0, outside, 0.0)
    outside_text = jnp.sum(jnp.where(is_image, 0.0, text_image), axis=1, keepdims=True)
    text_lane = lax.broadcasted_iota(jnp.int32, (LANES, images), 1)
    text_row = lax.broadcasted_iota(jnp.int32, (LANES, images), 0)
    text_image = jnp.where(is_image, text_image, 0.0) + jnp.where(
        text_lane == 0, outside_text, 0.0
    )
    text_image = jnp.where(text_row < POS, text_image, 0.0)
    first_lane = lax.broadcasted_iota(jnp.int32, (images, LANES), 1)
    left = pairs[:, :LANES] + jnp.where(first_lane < POS, by_position, 0.0)
    right = pairs[:, LANES:]
    a00, b00 = skewed(left[:LANES] + text_image[:, :LANES] + p_block)
    a01, b01 = skewed(right[:LANES] + text_image[:, LANES:])
    a10, b10 = skewed(left[LANES:])
    a11, b11 = skewed(right[LANES:])
    ax, bx = skewed(x_block)
    ay, by = skewed(y_block)
    diag_ref[head] = jnp.concatenate(
        [b10, b00 + b11 + a10, a00 + a11 + b01, a01, bx, ax, by, ay], axis=0
    )
    return dq * 0.125, jnp.concatenate(dks, axis=0), jnp.concatenate(dvs, axis=0)


MESH = pl.DeviceIdType.MESH
VMEM = pl.BlockSpec(memory_space=pltpu.VMEM)
HBM = pl.BlockSpec(memory_space=pltpu.HBM)
MIB = 1024 * 1024


def remote(src, dst, send, receive, device):
    return pltpu.make_async_remote_copy(
        src_ref=src, dst_ref=dst, send_sem=send, recv_sem=receive, device_id=device,
        device_id_type=MESH,
    )


def project_kernel(
    layer_ref, weight_hbm, *refs,
):
    small_hbm, refs = refs[:10], refs[10:]
    (item_ref, projected_out, columns_ref, rows_ref, table_ref,
     projected_ref, weight_ref, meta_send, bias_ref, sems, load_sems, store_sems), small = (
        refs[:12], refs[12:],
    )
    (segment_ref, mask_ref, position_ref, across_ref, down_ref, query_bias_ref, value_bias_ref,
     text_ref, horiz_ref, vert_ref) = small
    mine = lax.axis_index("seq")
    partner = (1 - mine, lax.axis_index("dp"))
    count, width = layer_ref.shape[1:]
    own = pl.ds(pl.multiple_of(mine * count, LANES), count)
    loads = [
        pltpu.make_async_copy(source, target, load_sems.at[index])
        for index, (source, target) in enumerate(
            list(zip(small_hbm, small))
            + [(layer_ref.at[mine], item_ref.at[own]), (weight_hbm, weight_ref)]
        )
    ]
    for load in loads:
        load.start()
    barrier = pltpu.get_barrier_semaphore()
    pl.semaphore_signal(barrier, inc=1, device_id=partner, device_id_type=MESH)
    pl.semaphore_wait(barrier, 1)
    pieces = count // LANES
    rows_out = [
        remote(
            layer_ref.at[1 - mine, pl.ds(piece * LANES, LANES)],
            item_ref.at[pl.ds(pl.multiple_of(mine * count + piece * LANES, LANES), LANES)],
            sems.at[0, piece], sems.at[1, piece], partner,
        )
        for piece in range(pieces)
    ]
    for copy in rows_out:
        copy.start()
    for load in loads[:-2]:
        load.wait()

    fields = (segment_ref, mask_ref, position_ref, across_ref, down_ref)
    blocks = [
        jnp.concatenate(
            [field[item : item + 1, :] for field in fields] + [jnp.zeros((3, count), jnp.int32)],
            axis=0,
        )
        for item in range(2)
    ]
    meta_send[...] = jnp.where(mine == 0, blocks[1], blocks[0])
    meta_out = remote(
        meta_send, rows_ref.at[:, own], sems.at[0, pieces], sems.at[1, pieces], partner
    )
    meta_out.start()
    rows_ref[:, own] = jnp.where(mine == 0, blocks[0], blocks[1])
    bias_ref[:, :width] = query_bias_ref[...].astype(F32).reshape(1, width)
    bias_ref[:, width : 2 * width] = jnp.zeros((1, width), F32)
    bias_ref[:, 2 * width :] = value_bias_ref[...].astype(F32).reshape(1, width)
    heads, levels = text_ref.shape
    spot = lax.broadcasted_iota(jnp.int32, (levels, LANES), 1)
    level = lax.broadcasted_iota(jnp.int32, (levels, LANES), 0)
    table = jnp.zeros((heads, LANES), F32)
    for source, begin in ((text_ref, 0), (horiz_ref, X_TABLE), (vert_ref, Y_TABLE)):
        table = table + dot_nn(source[...], (spot == level + begin).astype(BF))
    table_ref[...] = jnp.concatenate([table, jnp.zeros((16 - heads, LANES), F32)], axis=0)

    def project(there):
        step = 256

        def body(index, carry):
            columns = pl.ds(pl.multiple_of(index * step, step), step)
            product = dot_nn(item_ref[there], weight_ref[:, columns])
            projected_ref[there, columns] = (product + bias_ref[:, columns]).astype(BF)
            return carry

        lax.fori_loop(0, 3 * width // step, body, 0)

    def stored(index, there):
        return pltpu.make_async_copy(
            projected_ref.at[there], projected_out.at[there], store_sems.at[index]
        )

    for load in loads[-2:]:
        load.wait()
    project(own)
    stored(0, own).start()
    for piece in range(pieces):
        rows_out[piece].wait()
        there = pl.ds(pl.multiple_of((1 - mine) * count + piece * LANES, LANES), LANES)
        project(there)
        stored(1 + piece, there).start()
    meta_out.wait()
    meta = rows_ref[...].astype(F32)
    tall = jnp.concatenate([meta, jnp.zeros((LANES - 8, meta.shape[1]), F32)], axis=0)
    columns_ref[...] = jnp.transpose(tall).astype(jnp.int32)
    stored(0, own).wait()
    for piece in range(pieces):
        there = pl.ds(pl.multiple_of((1 - mine) * count + piece * LANES, LANES), LANES)
        stored(1 + piece, there).wait()


def projected_item(layer_in, fields, qkv_weight, query_bias, value_bias, tables):
    rows = 2 * layer_in.shape[1]
    width = layer_in.shape[2]
    pieces = rows // 2 // LANES
    small = list(fields) + [query_bias, value_bias] + [t.T for t in tables]
    return pl.pallas_call(
        project_kernel,
        in_specs=[HBM] * (2 + len(small)),
        out_specs=[VMEM, HBM, VMEM, VMEM, VMEM],
        out_shape=[
            jax.ShapeDtypeStruct((rows, width), BF),
            jax.ShapeDtypeStruct((rows, 3 * width), BF),
            jax.ShapeDtypeStruct((rows, LANES), jnp.int32),
            jax.ShapeDtypeStruct((8, rows), jnp.int32),
            jax.ShapeDtypeStruct((16, LANES), F32),
        ],
        scratch_shapes=[
            pltpu.VMEM((rows, 3 * width), BF),
            pltpu.VMEM((width, 3 * width), BF),
            pltpu.VMEM((8, rows // 2), jnp.int32),
            pltpu.VMEM((1, 3 * width), F32),
            pltpu.SemaphoreType.DMA((2, pieces + 1)),
            pltpu.SemaphoreType.DMA((len(small) + 2,)),
            pltpu.SemaphoreType.DMA((pieces + 1,)),
        ]
        + [pltpu.VMEM(array.shape, array.dtype) for array in small],
        compiler_params=pltpu.CompilerParams(
            collective_id=1, has_side_effects=True, vmem_limit_bytes=60 * MIB
        ),
        name="projected_item",
    )(layer_in, qkv_weight, *small)


EPSILON = 1e-05
TILE = 256


def vector(ref):
    return ref[...].astype(F32).reshape(1, ref.shape[0])


def gelu_and_slope(x):
    bell = jnp.exp2(-0.7213475204444817 * (x * x))
    rough = 1.0 + 0.23164188826 * jnp.abs(x)
    t = pl.reciprocal(rough, approx=True)
    t = t * (2.0 - rough * t)
    series = t * (
        0.127414796
        + t * (-0.142248368 + t * (0.7107068705 + t * (-0.7265760135 + t * 0.5307027145)))
    )
    tail = bell * series
    below = jnp.where(x >= 0.0, 1.0 - tail, tail)
    return x * below, below + x * (0.3989422804014327 * bell)


def row_mean(block):
    return jnp.mean(block, axis=1, keepdims=True)


def normalized(hidden):
    center = hidden - row_mean(hidden)
    scale = lax.rsqrt(row_mean(center * center) + EPSILON)
    return center * scale, scale


def norm_pulled(grad, unit, scale):
    return scale * (grad - row_mean(grad) - unit * row_mean(grad * unit))


def column_sum(block):
    return jnp.sum(block, axis=0, keepdims=True)


def feed_kernel(
    item_hbm, mixed_hbm, cotangent_ref, out_weight_ref, up_ref, down_ref, *refs,
):
    vectors_hbm, refs = refs[:7], refs[7:]
    (layer_out, total_out, unit_out, scale_out, grad_down_ref, grad_up_ref, small_ref,
     item_ref, mixed_ref, layer_ref, cotangent_all, active, slope, unit, scale_ref, normed, normed_t, total, d_branch, d_branch_t,
     sems, load_sems, tile_sems, store_sems) = refs[:24]
    vectors = refs[24:]
    (out_bias_ref, attn_gain_ref, attn_shift_ref, up_bias_ref, down_bias_ref, ffn_gain_ref,
     ffn_shift_ref) = vectors
    step = pl.program_id(0)
    blocks = pl.num_programs(0) // 2
    rows, width = item_hbm.shape
    count = rows // 2
    mine = lax.axis_index("seq")
    partner = (1 - mine, lax.axis_index("dp"))
    own = pl.ds(pl.multiple_of(mine * count, LANES), count)
    tiles = rows // TILE

    def sent():
        return remote(
            cotangent_ref.at[1 - mine], cotangent_all.at[own], sems.at[0], sems.at[1], partner
        )

    def returned():
        theirs = pl.ds(pl.multiple_of((1 - mine) * count, LANES), count)
        return [
            pltpu.make_async_copy(layer_ref.at[own], layer_out.at[mine], load_sems.at[8]),
            remote(
                layer_ref.at[theirs], layer_out.at[mine], sems.at[2], sems.at[3], partner
            ),
        ]

    def tile_loads(tile):
        there = pl.ds(tile * TILE, TILE)
        return [
            pltpu.make_async_copy(source.at[there], target.at[there], tile_sems.at[index, tile])
            for index, (source, target) in enumerate(
                ((mixed_hbm, mixed_ref), (item_hbm, item_ref))
            )
        ]

    def store(index):
        source, target = (
            (total, total_out), (unit, unit_out), (scale_ref, scale_out),
        )[index]
        return pltpu.make_async_copy(source, target, store_sems.at[index])

    def loads():
        copies = list(zip(vectors_hbm, vectors)) + [(cotangent_ref.at[mine], cotangent_all.at[own])]
        return [
            pltpu.make_async_copy(source, target, load_sems.at[index])
            for index, (source, target) in enumerate(copies)
        ]

    def over_tiles(size, body, carry, unroll=1):
        def run(index, state):
            return body(pl.ds(pl.multiple_of(index * size, size), size), state)

        return lax.fori_loop(0, rows // size, run, carry, unroll=unroll)

    @pl.when(step == 0)
    def _():
        for index in range(rows // TILE):
            for load in tile_loads(index):
                load.start()
        for load in loads():
            load.start()
        barrier = pltpu.get_barrier_semaphore()
        pl.semaphore_signal(barrier, inc=1, device_id=partner, device_id_type=MESH)
        pl.semaphore_wait(barrier, 1)
        sent().start()
        small_ref[...] = jnp.zeros_like(small_ref)
        for load in loads():
            load.wait()
        out_bias, gain, shift = vector(out_bias_ref), vector(attn_gain_ref), vector(attn_shift_ref)

        for index in range(rows // TILE):
            for load in tile_loads(index):
                load.wait()
            there = slice(index * TILE, index * TILE + TILE)
            attn = dot_nn(mixed_ref[there].astype(BF), out_weight_ref[...]) + out_bias
            standard, scale = normalized(item_ref[there].astype(F32) + attn)
            unit[there] = standard
            scale_ref[there] = jnp.broadcast_to(scale, (TILE, LANES))
            result = standard * gain + shift
            normed[there] = result.astype(BF)
            normed_t[:, there] = jnp.transpose(result).astype(BF)
        store(1).start()
        store(2).start()
        total[...] = jnp.zeros_like(total)

    @pl.when(step < blocks)
    def _():
        columns = [slice(begin, begin + TILE) for begin in range(0, width, TILE)]
        low = normed[...]
        following = dot_nn(low, up_ref[:, columns[0]])
        values = []
        for index, here in enumerate(columns):
            product = following
            if index + 1 < len(columns):
                following = dot_nn(low, up_ref[:, columns[index + 1]])
            bias = up_bias_ref[pl.ds(pl.multiple_of(step * width + here.start, LANES), TILE)]
            value, grade = gelu_and_slope(product + bias.astype(F32).reshape(1, TILE))
            values.append(value.astype(BF))
            active[step, :, here] = values[-1]
            slope[step, :, here] = grade.astype(BF)
        values = jnp.concatenate(values, axis=1)
        for here in columns:
            total[:, here] += dot_nn(values, down_ref[:, here])

    @pl.when(step == blocks)
    def _():
        sent().wait()
        gain, shift, bias = vector(ffn_gain_ref), vector(ffn_shift_ref), vector(down_bias_ref)
        first_gain, first_shift = vector(attn_gain_ref), vector(attn_shift_ref)

        def tile(there, sums):
            hidden = unit[there] * first_gain + first_shift + (total[there] + bias)
            standard, scale = normalized(hidden)
            layer_ref[there] = (standard * gain + shift).astype(BF)
            cotangent = cotangent_all[there].astype(F32)
            pulled = norm_pulled(cotangent * gain, standard, scale)
            total[there] = pulled
            low = pulled.astype(BF)
            d_branch[there] = low
            return (
                sums[0] + column_sum(low.astype(F32)),
                sums[1] + column_sum(cotangent * standard),
                sums[2] + column_sum(cotangent),
            )

        zero = jnp.zeros((1, width), F32)
        sums = over_tiles(64, tile, (zero, zero, zero), 4)
        for row, value in zip((5, 6, 7), sums):
            small_ref[row : row + 1] = value

        for copy in returned():
            copy.start()

        def turn(there, carry):
            d_branch_t[:, there] = jnp.transpose(d_branch[there].astype(F32)).astype(BF)
            return carry

        over_tiles(TILE, turn, 0, 3)

    @pl.when(step >= blocks)
    def _():
        block = step - blocks

        columns = [slice(begin, begin + TILE) for begin in range(0, width, TILE)]
        branch = d_branch[...]
        turned = d_branch_t[...]
        following = dot_nt(branch, down_ref[columns[0]])
        values = []
        for index, here in enumerate(columns):
            product = following
            if index + 1 < len(columns):
                following = dot_nt(branch, down_ref[columns[index + 1]])
            grad_down_ref[:, here] = dot_nn(turned, active[block, :, here]).astype(BF)
            d_up = (product * slope[block, :, here].astype(F32)).astype(BF)
            small_ref[pl.ds(8 + block, 1), here] = column_sum(d_up.astype(F32))
            values.append(d_up)
        values = jnp.concatenate(values, axis=1)
        turned = normed_t[...]
        for here in columns:
            grad_up_ref[:, here] = dot_nn(turned, values[:, here]).astype(BF)
            total[:, here] += dot_nt(values, up_ref[here])

    @pl.when(step == 2 * blocks - 1)
    def _():
        store(0).start()
        for copy in returned() + [store(0), store(1), store(2)]:
            copy.wait()


def fed_forward_and_back(
    item, mixed, cotangent, out_weight, up_weight, down_weight, vectors,
):
    rows, width = item.shape
    blocks = up_weight.shape[1] // width
    whole = pl.BlockSpec(memory_space=pltpu.VMEM)
    square = lambda kind: jax.ShapeDtypeStruct((rows, width), kind)
    later = lambda i: jnp.maximum(i - blocks, 0)
    return pl.pallas_call(
        feed_kernel,
        grid=(2 * blocks,),
        in_specs=[HBM, HBM, HBM, whole]
        + [
            pl.BlockSpec((width, width), lambda i: (0, lax.rem(i, blocks))),
            pl.BlockSpec((width, width), lambda i: (lax.rem(i, blocks), 0)),
        ]
        + [HBM] * 7,
        out_specs=[HBM] * 4
        + [
            pl.BlockSpec((width, width), lambda i: (later(i), 0)),
            pl.BlockSpec((width, width), lambda i: (later(i), 0)),
            whole,
        ],
        out_shape=[
            jax.ShapeDtypeStruct((2, rows // 2, width), BF), square(F32), square(F32),
            jax.ShapeDtypeStruct((rows, LANES), F32),
            jax.ShapeDtypeStruct((blocks * width, width), BF),
            jax.ShapeDtypeStruct((blocks * width, width), BF),
            jax.ShapeDtypeStruct((16, width), F32),
        ],
        scratch_shapes=[
            pltpu.VMEM((rows, width), BF),
            pltpu.VMEM((rows, width), F32),
            pltpu.VMEM((rows, width), BF),
            pltpu.VMEM((rows, width), BF),
            pltpu.VMEM((blocks, rows, width), BF),
            pltpu.VMEM((blocks, rows, width), BF),
            pltpu.VMEM((rows, width), F32),
            pltpu.VMEM((rows, LANES), F32),
            pltpu.VMEM((rows, width), BF),
            pltpu.VMEM((width, rows), BF),
            pltpu.VMEM((rows, width), F32),
            pltpu.VMEM((rows, width), BF),
            pltpu.VMEM((width, rows), BF),
            pltpu.SemaphoreType.DMA((4,)),
            pltpu.SemaphoreType.DMA((9,)),
            pltpu.SemaphoreType.DMA((2, rows // TILE)),
            pltpu.SemaphoreType.DMA((3,)),
        ]
        + [pltpu.VMEM(vector.shape, vector.dtype) for vector in vectors],
        compiler_params=pltpu.CompilerParams(
            collective_id=2, has_side_effects=True, vmem_limit_bytes=60 * MIB
        ),
        name="feed_forward",
    )(item, mixed, cotangent, out_weight, up_weight, down_weight, *vectors)


SLOTS = 4


def finish_kernel(
    main_ref, tail_ref, input_hbm, small_ref, diagonal_ref,
    down_ref, up_ref, out_ref, qkv_ref, input_ref, *refs,
):
    singles, (main_in, tail_in, slots, input_in, input_slot, in_sems, out_sems, item_sems) = (
        refs[:12], refs[12:],
    )
    mains, width = main_in.shape[0], main_in.shape[2]
    pairs, across = tail_in.shape[0], tail_in.shape[2]
    hidden = mains // 2
    blocks = mains + pairs

    def load(block):
        if block < mains:
            source, target = main_ref.at[pl.ds(block * width, width)], main_in.at[block]
        else:
            pair = block - mains
            source, target = tail_ref.at[pl.ds(pair * TAIL_ROWS, TAIL_ROWS)], tail_in.at[pair]
        return pltpu.make_async_copy(source, target, in_sems.at[block])

    def stores(block):
        slot, sem = slots.at[block % SLOTS], out_sems.at[block % SLOTS]
        if block < hidden:
            targets = [(slot, down_ref.at[pl.ds(block * width, width)])]
        elif block < mains:
            targets = [(slot, up_ref.at[:, pl.ds((block - hidden) * width, width)])]
        else:
            pair = block - mains
            targets = [
                (
                    slot.at[:, pl.ds(part * LANES, LANES)],
                    qkv_ref.at[:, pl.ds(part * width + pair * LANES, LANES)],
                )
                for part in range(3)
            ]
            down = pl.ds(0, TAIL_ROWS - width)
            targets.append(
                (slot.at[down, pl.ds(across, across)], out_ref.at[out_spot(pair, pairs, width)])
            )
        return [
            pltpu.make_async_copy(source, target, sem.at[index])
            for index, (source, target) in enumerate(targets)
        ]

    load_input = pltpu.make_async_copy(input_hbm, input_in, item_sems.at[0])
    store_input = pltpu.make_async_copy(input_slot, input_ref, item_sems.at[1])
    for block in range(blocks):
        load(block).start()
    load_input.start()
    for block in range(blocks):
        load(block).wait()
        if block >= SLOTS:
            for copy in stores(block - SLOTS):
                copy.wait()
        slot = block % SLOTS
        if block < hidden:
            slots[slot] = jnp.transpose(main_in[block].astype(F32))
        elif block < mains:
            slots[slot] = main_in[block].astype(F32)
        else:
            slots[slot, :, :across] = tail_in[block - mains, :width].astype(F32)
            slots[slot, : TAIL_ROWS - width, across:] = tail_in[block - mains, width:].astype(F32)
        for copy in stores(block):
            copy.start()
    load_input.wait()
    input_slot[...] = input_in[...].astype(F32)
    store_input.start()
    for row in range(8):
        singles[row][...] = small_ref[row]
    for row in range(hidden):
        singles[8][row * width : row * width + width] = small_ref[8 + row]
    heads, levels = singles[9].shape
    diagonals = diagonal_ref[...]
    level = lax.broadcasted_iota(jnp.int32, (LANES, LANES), 1)
    lane = lax.broadcasted_iota(jnp.int32, (LANES, LANES), 0)
    for table, (first, size, skip) in enumerate(((0, 4, 0), (4, 2, 1), (6, 2, 1))):
        total = jnp.zeros((heads, LANES), F32)
        for row in range(size):
            distance = lane + LANES * (row + skip - 2)
            chosen = (bucket(distance) == level).astype(F32)
            total = total + jnp.dot(
                diagonals[:, first + row, :], chosen, preferred_element_type=F32,
                precision=lax.Precision.HIGHEST,
            )
        singles[9 + table][...] = total[:, :levels]
    for block in range(blocks - SLOTS, blocks):
        for copy in stores(block):
            copy.wait()
    store_input.wait()


def finished(main, tail, grad_input, small, diagonals, hidden, levels):
    width = main.shape[1]
    heads = diagonals.shape[0]
    mains = main.shape[0] // width
    pairs = tail.shape[0] // TAIL_ROWS
    single = jax.ShapeDtypeStruct((width,), F32)
    table = jax.ShapeDtypeStruct((heads, levels), F32)
    dma = pltpu.SemaphoreType.DMA
    return pl.pallas_call(
        finish_kernel,
        in_specs=[HBM, HBM, HBM, VMEM, VMEM],
        out_specs=[HBM] * 5 + [VMEM] * 12,
        out_shape=[
            jax.ShapeDtypeStruct((hidden, width), F32),
            jax.ShapeDtypeStruct((width, hidden), F32),
            jax.ShapeDtypeStruct((width, width), F32),
            jax.ShapeDtypeStruct((width, 3 * width), F32),
            jax.ShapeDtypeStruct(grad_input.shape, F32),
        ]
        + [single] * 8
        + [jax.ShapeDtypeStruct((hidden,), F32)]
        + [table] * 3,
        scratch_shapes=[
            pltpu.VMEM((mains, width, width), BF),
            pltpu.VMEM((pairs, TAIL_ROWS, tail.shape[1]), BF),
            pltpu.VMEM((SLOTS, width, width), F32),
            pltpu.VMEM(grad_input.shape, BF),
            pltpu.VMEM(grad_input.shape, F32),
            dma((mains + pairs,)),
            dma((SLOTS, 4)),
            dma((2,)),
        ],
        compiler_params=pltpu.CompilerParams(vmem_limit_bytes=56 * MIB),
        name="finished",
    )(main, tail, grad_input, small, diagonals)


PIECE = 16


class Place:
    def __init__(self, depth):
        place = lax.axis_index("dp")
        self.depth = depth
        self.group = lax.div(place, 4 * depth)
        self.z = lax.rem(lax.div(place, 4), depth)
        self.bits = {
            "x": lax.axis_index("seq"),
            "c": lax.rem(place, 2),
            "y": lax.rem(lax.div(place, 2), 2),
            "a": lax.rem(self.z, 2),
            "b": lax.div(self.z, 2),
        }

    def partner(self, letters):
        bit = {
            letter: 1 - value if letter in letters else value
            for letter, value in self.bits.items()
        }
        z = self.z
        for letter, reach in (("a", 1), ("b", 2)):
            if letter in letters:
                z = z + reach - 2 * reach * self.bits[letter]
        return (bit["x"], (self.group * self.depth + z) * 4 + bit["y"] * 2 + bit["c"])

    def greet(self, met):
        barrier = pltpu.get_barrier_semaphore()
        for letters in met:
            pl.semaphore_signal(
                barrier, inc=1, device_id=self.partner(letters), device_id_type=MESH
            )
        pl.semaphore_wait(barrier, len(met))


def letters_of(depth):
    return "xy" + "ab"[: (depth - 1).bit_length()]


def parsed(routes, depth):
    kept = letters_of(depth)
    parts = []
    for route in routes.split():
        hops = ["".join(letter for letter in hop if letter in kept) for hop in route.split(".")]
        parts.append([hop for hop in hops if hop])
    return parts


def subsets(hop):
    return [
        "".join(letter for index, letter in enumerate(hop) if mask >> index & 1)
        for mask in range(1, 2 ** len(hop))
    ]


class Chunk:
    def __init__(self, place, depth, source, out_ref, offset, spot, scratch):
        _, self.begin, rows, first, columns, _, routes, _ = spot
        self.place, self.source, self.columns = place, source, pl.ds(first, columns)
        self.out_ref, self.out_begin = out_ref, offset + self.begin
        self.parts = parsed(routes, depth)
        self.half = rows // 2
        self.share = self.half // len(self.parts)
        self.hops = max(len(part) for part in self.parts)
        self.work, self.fresh, *landing, self.sends, self.receives, self.locals = scratch
        self.landing = {}
        self.sems = {}
        count = 2
        for part, hops in enumerate(self.parts):
            for hop, letters in enumerate(hops):
                self.landing[part, hop] = landing.pop(0)
                for way in range(2):
                    for index in range(2 ** len(letters) - 1):
                        self.sems[way, part, hop, index] = count
                        count += 1

    def aligned(self, value):
        return pl.multiple_of(value, PIECE)

    def size(self, part, hop):
        return self.share >> sum(len(letters) for letters in self.parts[part][: hop + 1])

    def spot(self, part, hop, other=""):
        start = part * self.share
        for level in range(hop + 1):
            for index, letter in enumerate(self.parts[part][level]):
                bit = self.place.bits[letter]
                if level == hop and letter in other:
                    bit = 1 - bit
                start = start + bit * (self.size(part, level) << index)
        return start

    def out(self, core):
        begin = self.aligned(self.out_begin + core * self.half)
        return self.out_ref.at[pl.ds(begin, self.half), self.columns]

    def held(self, buffer, begin, size):
        return buffer.at[pl.ds(self.aligned(begin), size)]

    def copy(self, index, source, target, letters):
        return remote(
            source, target, self.sends.at[index], self.receives.at[index],
            self.place.partner(letters),
        )

    def pair_down(self):
        core = self.place.bits["c"]
        at = lambda c: self.source.at[
            pl.ds(self.aligned(self.begin + c * self.half), self.half), self.columns
        ]
        return [
            self.copy(0, at(1 - core), self.fresh, "c"),
            pltpu.make_async_copy(at(core), self.work, self.locals.at[0]),
        ]

    def pair_up(self, arriving):
        core = self.place.bits["c"]
        return [
            self.copy(1, self.fresh, self.out(1 - core if arriving else core), "c"),
            pltpu.make_async_copy(self.fresh, self.out(core), self.locals.at[1]),
        ]

    def at_hop(self, hop):
        return [
            (part, hops[hop]) for part, hops in enumerate(self.parts) if hop < len(hops)
        ]

    def down(self, hop):
        copies = []
        for part, letters in self.at_hop(hop):
            size = self.size(part, hop)
            for index, other in enumerate(subsets(letters)):
                copies.append(
                    self.copy(
                        self.sems[0, part, hop, index],
                        self.held(self.work, self.spot(part, hop, other), size),
                        self.landing[part, hop].at[index], other,
                    )
                )
        return copies

    def up(self, hop, arriving):
        copies = []
        for part, letters in self.at_hop(hop):
            mine = self.spot(part, hop)
            size = self.size(part, hop)
            for index, other in enumerate(subsets(letters)):
                target = self.spot(part, hop, other) if arriving else mine
                copies.append(
                    self.copy(
                        self.sems[1, part, hop, index], self.held(self.fresh, mine, size),
                        self.held(self.fresh, target, size), other,
                    )
                )
        return copies

    def add(self, begin, sources, size):
        step = 64 if size % 64 == 0 else 32 if size % 32 == 0 else PIECE

        def body(index, carry):
            offset = self.aligned(index * step)
            there = pl.ds(self.aligned(begin + offset), step)
            total = self.work[there]
            if len(sources) == 1:
                total = total + sources[0][pl.ds(offset, step)]
            else:
                total = total.astype(F32)
                for source in sources:
                    total = total + source[pl.ds(offset, step)].astype(F32)
            self.work[there] = total.astype(BF)
            return carry

        lax.fori_loop(0, size // step, body, 0)

    def stage(self, number):
        hops = self.hops
        ended, started = [], []
        if number == 0:
            started = self.pair_down()
        elif number == 1:
            ended = self.pair_down()
            started = self.down(0)
        elif number <= hops:
            ended = self.down(number - 2)
            started = self.down(number - 1)
        elif number == hops + 1:
            ended = self.down(hops - 1)
            started = self.up(hops - 1, False)
        elif number <= 2 * hops:
            level = 2 * hops + 1 - number
            ended = self.up(level, True)
            started = self.up(level - 1, False)
        elif number == 2 * hops + 1:
            ended = self.up(0, True)
            started = self.pair_up(False)
        else:
            ended = self.pair_up(True)
        for copy in ended:
            copy.wait()
        if number == 1:
            self.add(0, [self.fresh], self.half)
        elif 2 <= number <= hops + 1:
            hop = number - 2
            for part, letters in self.at_hop(hop):
                landing = self.landing[part, hop]
                sources = [landing.at[index] for index in range(2 ** len(letters) - 1)]
                self.add(self.spot(part, hop), sources, self.size(part, hop))
        if number == hops + 1:
            for part, route in enumerate(self.parts):
                last = len(route) - 1
                there = pl.ds(self.aligned(self.spot(part, last)), self.size(part, last))
                self.fresh[there] = self.work[there]
        for copy in started:
            copy.start()


def chunk_scratch(spot, depth):
    _, _, rows, _, columns, _, routes, _ = spot
    parts = parsed(routes, depth)
    landing = []
    copies = 2
    for hops in parts:
        size = rows // 2 // len(parts)
        for letters in hops:
            size >>= len(letters)
            others = 2 ** len(letters) - 1
            copies += 2 * others
            landing.append(pltpu.VMEM((others, size, columns), BF))
    dma = pltpu.SemaphoreType.DMA
    return (
        [pltpu.VMEM((rows // 2, columns), BF)] * 2
        + landing
        + [dma((copies,)), dma((copies,)), dma((2,))]
    )


def loads_of(hop, size):
    if "x" in hop and "y" in hop:
        return [("x", 2 * size), ("y", 2 * size)]
    if hop in ("x", "y"):
        return [(hop, size)]
    if "a" in hop and "b" in hop:
        return [("end", 3 * size), ("middle", 4 * size)]
    return [("end", size), ("middle", 2 * size)] if hop == "b" else [("end", size)]


def planned(chunks, work, depth, hop_count):
    latency, issue, link, pair = 5.0, 0.08, 75e3, 300e3
    free = {}
    now = 3.0
    chains = []
    for rows, columns, need, routes, _ in chunks:
        parts = parsed(routes, depth)
        sizes = [rows // 2 // len(parts)] * len(parts)
        down = []
        for hop in range(max(len(part) for part in parts)):
            loads, copies, added = [], 0, 0
            for index, part in enumerate(parts):
                if hop < len(part):
                    sizes[index] >>= len(part[hop])
                    others = 2 ** len(part[hop]) - 1
                    loads += loads_of(part[hop], sizes[index])
                    copies += others
                    added += sizes[index] * others
            down.append((loads, copies, added, columns))
        first = [([("core", rows // 2)], 1.5, rows // 2, columns)]
        last = [([("core", rows // 2)], 1, 0, columns)]
        chains.append((need, first + down + down[::-1] + last))
    chains.append((len(work), [([("core", 16)], 2, 0, 768)] * hop_count))
    ranks = [chunk[4] for chunk in chunks] + [0]
    position = [0] * len(chains)
    ready = [0.0] * len(chains)
    order = [[] for _ in range(len(work) + 1)]
    done = 0
    while True:
        open_ones = [
            (ranks[i], ready[i], i) for i, (need, chain) in enumerate(chains)
            if position[i] <= len(chain) and need <= done
        ]
        due = [entry for entry in open_ones if entry[1] <= now]
        if not due and done < len(work):
            now += work[done]
            done += 1
            continue
        if not open_ones:
            return order
        fresh = [entry for entry in due if position[entry[2]] == 0]
        if due:
            _, when, index = min(fresh or due)
        else:
            _, when, index = min(open_ones, key=lambda entry: entry[1])
        now = max(now, when)
        chain = chains[index][1]
        stage = position[index]
        order[done].append((index, stage))
        if 0 < stage <= len(chain) // 2:
            now += 1e-6 * chain[stage - 1][2] * chain[stage - 1][3]
        if stage < len(chain):
            loads, copies, _, columns = chain[stage]
            now += issue * copies
            end = now
            for lane, rows in loads:
                rate = pair if lane == "core" else link / 2
                free[lane] = max(now, free.get(lane, 0.0)) + 2 * rows * columns / rate
                end = max(end, free[lane])
            ready[index] = end + latency
        position[index] += 1


def last_kernel(
    depth, plan, orders, counts, *refs,
):
    (meta_ref, rows_ref, projected_hbm, mixed_hbm, log_ref, first_hbm, second_hbm,
     key_image_hbm, bias_hbm, small_ref, gain_ref, item_hbm, weight_hbm, total_hbm, unit_hbm, scale_hbm,
     out_weight_hbm, grad_down_ref, grad_up_ref,
     main_out, tail_out, small_out, diagonal_out, input_out,
     *scratch) = refs
    static, scratch = scratch[:6], scratch[6:]
    (k_ref, v_ref, mixed_ref, grad_ref, first_ref, second_ref, key_image_ref, bias_ref, pair_sems,
     item_ref, weight_ref, d_hidden_ref, unit_ref, scale_ref, load_sems, d_project, item_t, tail, input_grad,
     small_in, diagonal_in, small_sems, item_sems, *scratch) = scratch
    out_weight_ref = item_t
    place = Place(depth)
    step = pl.program_id(0)
    pairs = k_ref.shape[0]
    rows, width = item_hbm.shape
    count = rows // 2
    x = place.bits["x"]
    hidden = grad_down_ref.shape[0]
    sources = ((grad_down_ref, main_out, 0), (grad_up_ref, main_out, hidden), (tail, tail_out, 0))
    chunks = []
    for spot, pieces in zip(plan, counts):
        chunks.append(Chunk(place, depth, *sources[spot[0]], spot, scratch[:pieces]))
        scratch = scratch[pieces:]
    hop_letters = "c" + letters_of(depth)
    wide_hbm = (first_hbm, second_hbm, key_image_hbm, bias_hbm)
    wide_refs = (first_ref, second_ref, key_image_ref, bias_ref)

    def pair_loads(pair):
        copies = []
        held = ((projected_hbm, k_ref, width), (projected_hbm, v_ref, 2 * width))
        for source, target, first in held:
            columns = pl.ds(pl.multiple_of(first + pair * LANES, LANES), LANES)
            copies.append((source.at[:, columns], target.at[pair]))
        heads = pl.ds(2 * pair, 2)
        for source, target in zip(wide_hbm, wide_refs):
            copies.append((source.at[heads], target.at[heads]))
        return [
            pltpu.make_async_copy(source, target, pair_sems.at[pair, index])
            for index, (source, target) in enumerate(copies)
        ]

    def loads(first):
        if first:
            copies = [
                (total_hbm, d_hidden_ref), (unit_hbm, unit_ref), (scale_hbm, scale_ref),
                (out_weight_hbm, out_weight_ref), (item_hbm, item_ref),
            ]
            copies += [
                (mixed_hbm.at[:, pl.ds(pair * LANES, LANES)], mixed_ref.at[pair])
                for pair in range(pairs)
            ]
        else:
            copies = [(weight_hbm, weight_ref)]
        return [
            pltpu.make_async_copy(source, target, load_sems.at[0 if first else 1, index])
            for index, (source, target) in enumerate(copies)
        ]

    def back_to_attention():
        gain = vector(gain_ref)

        def tile(index, sums):
            there = pl.ds(pl.multiple_of(index * 64, 64), 64)
            d_normed = d_hidden_ref[there]
            standard = unit_ref[there]
            d_hidden = norm_pulled(d_normed * gain, standard, scale_ref[there, :1])
            d_hidden_ref[there] = d_hidden
            low = d_hidden.astype(BF)
            input_grad[there] = low
            return (
                sums[0] + column_sum(low.astype(F32)),
                sums[1] + column_sum(d_normed * standard),
                sums[2] + column_sum(d_normed),
            )

        zero = jnp.zeros((1, width), F32)
        sums = lax.fori_loop(0, rows // 64, tile, (zero, zero, zero), unroll=4)
        for row, value in zip((2, 3, 4), sums):
            small_out[row : row + 1] = value
        low = input_grad[...]
        down = TAIL_ROWS - width
        for begin in range(0, width, down):
            first = begin // LANES
            several = range(first, first + down // LANES)
            d_mixed = dot_nt(low, out_weight_ref[begin : begin + down]).astype(BF)
            for index, pair in enumerate(several):
                grad_ref[pair] = d_mixed[:, index * LANES : index * LANES + LANES]
            turned = jnp.concatenate(
                [jnp.transpose(mixed_ref[pair]).astype(BF) for pair in several], axis=0
            )
            for pair in range(pairs):
                rows_of, across = out_spot(pair, pairs, width)
                if rows_of.start == begin:
                    product = dot_nn(turned, low[:, across.start : across.start + across.size])
                    base = pair * TAIL_ROWS + width
                    tail[base : base + down] = product.astype(BF)

    def input_copies():
        return [
            pltpu.make_async_copy(
                input_grad.at[pl.ds(pl.multiple_of(x * count, LANES), count)], input_out.at[x],
                item_sems.at[0],
            ),
            remote(
                input_grad.at[pl.ds(pl.multiple_of((1 - x) * count, LANES), count)],
                input_out.at[x], item_sems.at[1], item_sems.at[2], place.partner("x"),
            ),
        ]

    def small_copies(hop):
        return [
            remote(source, landing.at[hop], small_sems.at[0, kind, hop],
                   small_sems.at[1, kind, hop], place.partner(hop_letters[hop]))
            for kind, (source, landing) in enumerate(
                ((small_out, small_in), (diagonal_out, diagonal_in))
            )
        ]

    def small_stage(hop):
        if hop > 0:
            for copy in small_copies(hop - 1):
                copy.wait()
            small_out[...] = small_out[...] + small_in[hop - 1]
            diagonal_out[...] = diagonal_out[...] + diagonal_in[hop - 1]
        if hop < len(hop_letters):
            for copy in small_copies(hop):
                copy.start()

    def perform(slot):
        for index, stage in orders[slot]:
            if index == len(chunks):
                small_stage(stage)
            else:
                chunks[index].stage(stage)

    @pl.when(step == 0)
    def _():
        for copy in pair_loads(0) + loads(True):
            copy.start()
        met = set(hop_letters)
        for chunk in chunks:
            for hops in chunk.parts:
                for letters in hops:
                    met.update(subsets(letters))
        place.greet(sorted(met))
        small_out[...] = small_ref[...]

    for pair in range(pairs):
        @pl.when(step == pair)
        def _(pair=pair):
            perform(pair)

    @pl.when(step == 0)
    def _():
        for pair in range(1, pairs):
            for copy in pair_loads(pair):
                copy.start()
        for copy in loads(False):
            copy.start()
        static_prepare(meta_ref, static)
        for copy in loads(True):
            copy.wait()
        back_to_attention()
        for tile in range(rows // TILE):
            there = slice(tile * TILE, tile * TILE + TILE)
            item_t[:, there] = jnp.transpose(item_ref[there].astype(F32)).astype(BF)

    for copy in pair_loads(step):
        copy.wait()
    (dq_even, dk_even, dv_even), (dq_odd, dk_odd, dv_odd) = [
        head_back(
            parity, step, rows_ref, wide_refs, k_ref, v_ref, mixed_ref, grad_ref, log_ref,
            static, diagonal_out,
        )
        for parity in range(2)
    ]
    even = own_lanes(0, rows)
    pieces = [
        jnp.transpose(jnp.concatenate([dq_even, dq_odd], axis=0)).astype(BF),
        jnp.where(even, dk_even, dk_odd).astype(BF),
        jnp.where(even, dv_even, dv_odd).astype(BF),
    ]
    for part, piece in enumerate(pieces):
        d_project[:, pl.ds(pl.multiple_of(part * width + step * LANES, LANES), LANES)] = piece
    slab = pl.ds(pl.multiple_of(step * TAIL_ROWS, TAIL_ROWS), width)
    tail[slab] = dot_nn(item_t[...], jnp.concatenate(pieces, axis=1)).astype(BF)

    @pl.when(step == 0)
    def _():
        for copy in loads(False):
            copy.wait()

    @pl.when(step == pairs - 1)
    def _():
        perform(pairs)
        for begin in range(0, width, TILE):
            here = slice(begin, begin + TILE)
            total = d_hidden_ref[:, here] + dot_nt(d_project[...], weight_ref[here])
            input_grad[:, here] = total.astype(BF)
        for copy in input_copies():
            copy.start()
        for begin in range(0, width, TILE):
            here = slice(begin, begin + TILE)
            there = slice(2 * width + begin, 2 * width + begin + TILE)
            small_out[0:1, here] = column_sum(d_project[:, here].astype(F32))
            small_out[1:2, here] = column_sum(d_project[:, there].astype(F32))
        perform(pairs + 1)
        for copy in input_copies():
            copy.wait()


TAIL_ROWS = 1024


def out_spot(pair, pairs, width):
    down = TAIL_ROWS - width
    across = width * width // (pairs * down)
    per_row = width // across
    return (
        pl.ds(pair // per_row * down, down),
        pl.ds(pair % per_row * across, across),
    )


def summed_with_attention_back(
    meta_columns, meta_rows, projected, mixed, logs, wide_arrays, item, qkv_weight,
    total, unit, scale, out_weight, attn_gain, small, grad_down, grad_up,
):
    size = lax.axis_size("dp")
    depth = 4 if size % 16 == 0 else size // 4
    rows, width = item.shape
    pairs = width // LANES
    hidden = grad_down.shape[0]
    hops = len(letters_of(depth)) + 1
    work = [14.0] + [5.5] * (pairs - 1) + [4.0]
    tall, wide, slim = 1024, 3 * LANES, 2 * LANES
    plan = [
        (0, 0, 2 * tall, 0, width, 0, "a.b.x.y x.y.a.b", 1),
        (0, 2 * tall, tall, 0, width, 0, "x.a.y.b y.a.b.x", 2),
        (1, 0, 3 * tall, 0, slim, 0, "a.b.x.y y.x.a.b", 4),
        (1, 0, 3 * tall, slim, slim, 0, "y.a.x.b x.y.a.b", 0),
        (1, 0, 3 * tall, 2 * slim, slim, 0, "x.y.a.b y.x.a.b", 2),
        (2, 0, tall, 0, wide, 1, "y.x.a.b a.b.x.y", 3),
        (2, tall, tall, 0, wide, 2, "xy.a.b", 2),
        (2, 2 * tall, tall, 0, wide, 3, "x.y.ab y.ab.x", 3),
        (2, 3 * tall, tall, 0, wide, 4, "xy.a.b", 1),
        (2, 4 * tall, tall, 0, wide, 5, "xy.a.b", 1),
        (2, 5 * tall, tall, 0, wide, 6, "ab.y.x y.ab.x", 2),
    ]
    orders = planned([(spot[2],) + spot[4:] for spot in plan], work, depth, hops)

    whole = pl.BlockSpec(memory_space=pltpu.VMEM)
    diagonals = jax.ShapeDtypeStruct((2 * pairs, 8, LANES), F32)
    dma = pltpu.SemaphoreType.DMA
    scratch = []
    for spot in plan:
        scratch.append(chunk_scratch(spot, depth))
    main, tail, small, diagonals, grad_input = pl.pallas_call(
        functools.partial(last_kernel, depth, plan, orders, [len(pieces) for pieces in scratch]),
        grid=(pairs,),
        in_specs=[whole] * 2 + [HBM] * 2 + [whole] + [HBM] * 4 + [whole] * 2 + [HBM] * 8,
        out_specs=[HBM, HBM, whole, whole, HBM],
        out_shape=[
            jax.ShapeDtypeStruct((2 * hidden, width), BF),
            jax.ShapeDtypeStruct((pairs * TAIL_ROWS, 3 * LANES), BF),
            jax.ShapeDtypeStruct(small.shape, F32),
            diagonals,
            jax.ShapeDtypeStruct((2, rows // 2, width), BF),
        ],
        scratch_shapes=[pltpu.VMEM((rows, LANES), BF)] * 3
        + [pltpu.VMEM((LANES, rows), BF)] * 3
        + [pltpu.VMEM((pairs, rows, LANES), kind) for kind in (BF, BF, F32, BF)]
        + [pltpu.VMEM(array.shape, BF) for array in wide_arrays]
        + [
            dma((pairs, 6)),
            pltpu.VMEM((rows, width), BF),
            pltpu.VMEM((width, 3 * width), BF),
            pltpu.VMEM((rows, width), F32),
            pltpu.VMEM((rows, width), F32),
            pltpu.VMEM((rows, LANES), F32),
            dma((2, 5 + pairs)),
            pltpu.VMEM((rows, 3 * width), BF),
            pltpu.VMEM((width, rows), BF),
            pltpu.VMEM((pairs * TAIL_ROWS, 3 * LANES), BF),
            pltpu.VMEM((rows, width), BF),
            pltpu.VMEM((hops,) + small.shape, F32),
            pltpu.VMEM((hops,) + diagonals.shape, F32),
            dma((2, 2, hops)),
            dma((3,)),
        ]
        + [piece for pieces in scratch for piece in pieces],
        compiler_params=pltpu.CompilerParams(
            collective_id=0, has_side_effects=True, vmem_limit_bytes=62 * MIB
        ),
        name="summed_with_attention_back",
    )(meta_columns, meta_rows, projected, mixed, logs, *wide_arrays,
      small, attn_gain, item, qkv_weight, total, unit, scale, out_weight, grad_down, grad_up)
    span = 4 * depth
    if size > span:
        groups = [list(range(first, size, span)) for first in range(span)]
        main, tail, small, diagonals = lax.psum(
            (main.astype(F32), tail.astype(F32), small, diagonals), "dp",
            axis_index_groups=groups,
        )
        main, tail = main.astype(BF), tail.astype(BF)
    return main, tail, small, diagonals, grad_input


def per_device(
    layer_in, segment, key_mask, position, layout_x, layout_y,
    qkv_weight, query_bias, value_bias, out_weight, out_bias, attn_gain, attn_shift,
    up_weight, up_bias, down_weight, down_bias, ffn_gain, ffn_shift,
    text_table, horiz_table, vert_table, cotangent,
):
    width = layer_in.shape[-1]
    item, projected, meta_columns, meta_rows, table_rows = projected_item(
        layer_in, (segment, key_mask, position, layout_x, layout_y),
        qkv_weight, query_bias, value_bias, (text_table, horiz_table, vert_table),
    )
    mixed, logs, *wide_arrays = attention_forward(meta_columns, meta_rows, table_rows, projected, width)
    layer_out, total, unit, scale, grad_down, grad_up, small = fed_forward_and_back(
        item, mixed, cotangent, out_weight, up_weight, down_weight,
        (out_bias, attn_gain, attn_shift, up_bias, down_bias, ffn_gain, ffn_shift),
    )
    main, tail, small, diagonals, grad_input = summed_with_attention_back(
        meta_columns, meta_rows, projected, mixed, logs, wide_arrays, item, qkv_weight,
        total, unit, scale, out_weight, attn_gain, small, grad_down, grad_up,
    )
    done = finished(
        main, tail, grad_input, small, diagonals, up_weight.shape[1], text_table.shape[0]
    )
    sum_down, sum_up, sum_out, sum_qkv, grad_input = done[:5]
    singles, tables = done[5:14], [t.T for t in done[14:]]
    return (
        layer_out, grad_input, sum_qkv, singles[0], singles[1], sum_out, singles[2], singles[3],
        singles[4], sum_up, singles[8], sum_down, singles[5], singles[6], singles[7],
        tables[0], tables[1], tables[2],
    )


def solution(mesh):
    rows = P("dp", "seq", None)
    marks_spec = P("dp", "seq")
    return jax.shard_map(
        per_device,
        mesh=mesh,
        in_specs=(rows,) + (marks_spec,) * 5 + (P(),) * 16 + (rows,),
        out_specs=(rows, rows) + (P(),) * 16,
        check_vma=False,
    )
```

```python
import functools

import jax
import jax.numpy as jnp
from jax import lax
from jax.experimental import pallas as pl
from jax.experimental.pallas import tpu as pltpu
from jax.sharding import PartitionSpec as P

BF = jnp.bfloat16
F32 = jnp.float32
BIG = 1e30
LANES = 128
HEAD = 64
TEXT = 512
POS = 64
COORD = 48
Y0 = 64
GROUP0 = 112
MEMBER0 = 116
FLAG = 124
EVERY = 125
STRAY = 126
X_TABLE = 33
Y_TABLE = 66
NOTHING = 127


def dot_nt(a, b):
    return lax.dot_general(a, b, (((1,), (1,)), ((), ())), preferred_element_type=F32)


def dot_nn(a, b):
    return lax.dot_general(a, b, (((1,), (0,)), ((), ())), preferred_element_type=F32)


def looked_up(table_row, index):
    rows = index.shape[0]
    return jnp.take_along_axis(
        jnp.broadcast_to(table_row, (rows, LANES)), index, axis=1, mode="promise_in_bounds"
    )


def bucket(distance):
    return jnp.clip(distance, -16, 16) + 16


def between(lane, low, high):
    return (lane >= low) & (lane < high)


def columns_of(meta_ref):
    return tuple(meta_ref[:, field : field + 1] for field in range(5))


def marks(meta_ref):
    segment, key_mask, position, across, down = columns_of(meta_ref)
    rows = segment.shape[0]
    lane = lax.broadcasted_iota(jnp.int32, (rows, LANES), 1)
    row = lax.broadcasted_iota(jnp.int32, (rows, LANES), 0)
    even = between(lane, HEAD, HEAD + COORD) & (lane - HEAD == across)
    odd = (lane < COORD) & (lane == across)
    group = (segment - 1) >> 3
    member = (segment - 1) & 7
    named = segment > 0
    shared = (
        ((row < TEXT) & (lane < POS) & (lane == position))
        | (between(lane, Y0, Y0 + COORD) & (lane - Y0 == down))
        | (named & between(lane, GROUP0, MEMBER0) & (lane - GROUP0 == group))
        | (named & between(lane, MEMBER0, FLAG) & (lane - MEMBER0 == member))
        | ((lane == FLAG) & (key_mask <= 0))
        | (lane == EVERY)
        | ((lane == STRAY) & (segment < 0))
    )
    return tuple(jnp.where(m, 1.0, 0.0).astype(BF) for m in (even, odd, shared))


def square_lanes():
    shape = (LANES, LANES)
    return lax.broadcasted_iota(jnp.int32, shape, 0), lax.broadcasted_iota(jnp.int32, shape, 1)


def barred():
    row, lane = square_lanes()
    in_groups = between(lane, GROUP0, MEMBER0)
    shut = (
        (between(row, GROUP0, MEMBER0) & in_groups & (lane != row))
        | (between(row, MEMBER0, FLAG) & between(lane, MEMBER0, FLAG) & (lane != row))
        | ((row == EVERY) & (lane == FLAG))
        | ((row == STRAY) & in_groups)
    )
    return jnp.where(shut, -BIG, 0.0).astype(F32)


def table_index():
    row, lane = square_lanes()
    distance = bucket(row - lane)
    inside = lambda low, high: between(row, low, high) & between(lane, low, high)
    even = jnp.where(inside(HEAD, HEAD + COORD), distance + X_TABLE, NOTHING)
    odd = jnp.where(inside(0, COORD), distance + X_TABLE, NOTHING)
    shared = jnp.where(
        inside(0, POS), distance, jnp.where(inside(Y0, Y0 + COORD), distance + Y_TABLE, NOTHING)
    )
    return even, odd, shared


def image_query_index(meta_ref):
    position = meta_ref[TEXT:, 2:3]
    lane = lax.broadcasted_iota(jnp.int32, (position.shape[0], LANES), 1)
    return jnp.where(lane < POS, bucket(position - lane), NOTHING)


def prepare(meta_ref, mark_refs, bar_ref, index_refs, image_index_ref):
    for ref, value in zip(mark_refs, marks(meta_ref)):
        ref[...] = value
    bar_ref[...] = barred()
    for ref, value in zip(index_refs, table_index()):
        ref[...] = value
    image_index_ref[...] = image_query_index(meta_ref)


def own_lanes(parity, rows):
    lane = lax.broadcasted_iota(jnp.int32, (rows, LANES), 1)
    return (lane < HEAD) if parity == 0 else (lane >= HEAD)


def widened(parity, q, table_row, bias, bar_ref, index_refs, image_index_ref, mark_refs):
    rows = q.shape[0]
    shared = mark_refs[2][...]
    across = looked_up(table_row, index_refs[parity][...]).astype(BF)
    first = jnp.where(
        own_lanes(parity, rows), q.astype(F32) * 0.125, dot_nn(mark_refs[parity][...], across)
    )
    others = (looked_up(table_row, index_refs[2][...]) + bar_ref[...]).astype(BF)
    second = dot_nn(shared, others)
    on_images = looked_up(table_row, image_index_ref[...])
    second = jnp.concatenate([second[:TEXT], second[TEXT:] + on_images], axis=0)
    image_lane = lax.broadcasted_iota(jnp.int32, on_images.shape, 1)
    key_image = jnp.where(image_lane < POS, bias[:, :LANES].astype(BF), shared[TEXT:])
    return first.astype(BF), second.astype(BF), key_image


def joined(parity, first, second, key_image, k, marks_own, shared):
    rows = k.shape[0]
    lane = lax.broadcasted_iota(jnp.int32, (rows, LANES), 1)
    to_image = jnp.where(lane < POS, shared, second)
    key_first = jnp.where(own_lanes(parity, rows), k, marks_own)
    q_text = jnp.concatenate([first, second], axis=1)
    q_image = jnp.concatenate([first, to_image], axis=1)
    k_text = jnp.concatenate([key_first[:TEXT], shared[:TEXT]], axis=1)
    k_image = jnp.concatenate([key_first[TEXT:], key_image], axis=1)
    return q_text, q_image, k_text, k_image


def near(start, size):
    if start >= TEXT:
        return slice(0, TEXT)
    return slice(max(0, start - LANES), min(TEXT, start + size + LANES))


def image_bias(table_row, offsets):
    return jnp.concatenate(
        [looked_up(table_row, offsets[:, :LANES]), looked_up(table_row, offsets[:, LANES:])], axis=1
    )


def forward_kernel(
    meta_ref, rows_ref, table_ref, q_ref, k_ref, v_ref,
    mixed_ref, log_ref, first_ref, second_ref, key_image_ref, bias_ref,
    even_ref, odd_ref, shared_ref, bar_ref, index_even, index_odd, index_shared, image_index_ref,
):
    mark_refs = (even_ref, odd_ref, shared_ref)
    index_refs = (index_even, index_odd, index_shared)

    @pl.when(pl.program_id(0) == 0)
    def _():
        prepare(meta_ref, mark_refs, bar_ref, index_refs, image_index_ref)

    rows = q_ref.shape[0]
    images = rows - TEXT
    q, k, v = q_ref[...], k_ref[...], v_ref[...]
    offsets = bucket(rows_ref[2:3, TEXT:] - meta_ref[TEXT:, 2:3])
    tile = 256
    v_turned = transposed(v)
    heads = [None, None]

    def prepared(parity):
        table_row = table_ref[pl.ds(2 * pl.program_id(0) + parity, 1), :]
        bias = image_bias(table_row, offsets)
        first, second, key_image = widened(
            parity, q, table_row, bias, bar_ref, index_refs, image_index_ref, mark_refs
        )
        first_ref[parity] = first
        second_ref[parity] = second
        key_image_ref[parity] = key_image
        bias_ref[parity] = bias.astype(BF)
        wide = joined(
            parity, first, second, key_image, k, mark_refs[parity][...], shared_ref[...]
        )
        heads[parity] = wide + (bias,)

    def scored(parity, start):
        q_text, q_image, k_text, k_image, bias = heads[parity]
        here = slice(start, start + tile)
        on_image = dot_nt(k_image, q_image[here])
        if start >= TEXT:
            on_image = on_image + bias[:, start - TEXT : start - TEXT + tile]
        return dot_nt(k_text[near(start, tile)], q_text[here]), on_image

    spots = [(parity, start) for parity in range(2) for start in range(0, rows, tile)]
    outs = ([], [])
    prepared(0)
    following = scored(*spots[0])
    for index, (parity, start) in enumerate(spots):
        on_text, on_image = following
        if index == 1:
            prepared(1)
        if index + 1 < len(spots):
            following = scored(*spots[index + 1])
        top = jnp.maximum(
            jnp.max(on_text, axis=0, keepdims=True), jnp.max(on_image, axis=0, keepdims=True)
        )
        on_text = jnp.exp(on_text - top)
        on_image = jnp.exp(on_image - top)
        total = jnp.sum(on_text, axis=0, keepdims=True) + jnp.sum(on_image, axis=0, keepdims=True)
        own = slice(parity * HEAD, parity * HEAD + HEAD)
        out = dot_nn(v_turned[own, near(start, tile)], on_text.astype(BF)) + dot_nn(
            v_turned[own, TEXT:], on_image.astype(BF)
        )
        outs[parity].append(out * (1.0 / total))
        log_ref[0, parity : parity + 1, start : start + tile] = top + jnp.log(total)
    mixed_ref[...] = jnp.transpose(
        jnp.concatenate([jnp.concatenate(outs[parity], axis=1) for parity in range(2)], axis=0)
    )


def static_scratch(rows):
    square = (LANES, LANES)
    return [
        pltpu.VMEM((rows, LANES), BF),
        pltpu.VMEM((rows, LANES), BF),
        pltpu.VMEM((rows, LANES), BF),
        pltpu.VMEM(square, F32),
        pltpu.VMEM(square, jnp.int32),
        pltpu.VMEM(square, jnp.int32),
        pltpu.VMEM(square, jnp.int32),
        pltpu.VMEM((rows - TEXT, LANES), jnp.int32),
    ]


def attention_forward(meta_columns, meta_rows, table_rows, projected, width):
    rows = projected.shape[0]
    images = rows - TEXT
    pairs = width // LANES

    def block(part):
        return pl.BlockSpec((rows, LANES), lambda p: (0, part * pairs + p))

    whole = lambda shape: pl.BlockSpec(shape, lambda p: (0,) * len(shape))
    return pl.pallas_call(
        forward_kernel,
        grid=(pairs,),
        in_specs=[
            whole(meta_columns.shape),
            whole(meta_rows.shape),
            whole(table_rows.shape),
            block(0), block(1), block(2),
        ],
        out_specs=[
            pl.BlockSpec((rows, LANES), lambda p: (0, p)),
            pl.BlockSpec((1, 2, rows), lambda p: (p, 0, 0)),
            pl.BlockSpec((2, rows, LANES), lambda p: (p, 0, 0)),
            pl.BlockSpec((2, rows, LANES), lambda p: (p, 0, 0)),
            pl.BlockSpec((2, images, LANES), lambda p: (p, 0, 0)),
            pl.BlockSpec((2, images, images), lambda p: (p, 0, 0)),
        ],
        out_shape=[
            jax.ShapeDtypeStruct((rows, width), F32),
            jax.ShapeDtypeStruct((pairs, 2, rows), F32),
            jax.ShapeDtypeStruct((2 * pairs, rows, LANES), BF),
            jax.ShapeDtypeStruct((2 * pairs, rows, LANES), BF),
            jax.ShapeDtypeStruct((2 * pairs, images, LANES), BF),
            jax.ShapeDtypeStruct((2 * pairs, images, images), BF),
        ],
        scratch_shapes=static_scratch(rows),
        compiler_params=pltpu.CompilerParams(vmem_limit_bytes=60 * 1024 * 1024),
        name="attention_forward",
    )(meta_columns, meta_rows, table_rows, projected, projected, projected)


def skewed(block):
    size = block.shape[0]
    lane = lax.broadcasted_iota(jnp.int32, (size, LANES), 1)
    row = lax.broadcasted_iota(jnp.int32, (size, LANES), 0)
    turned = jnp.take_along_axis(
        block, (lane + row) & (LANES - 1), axis=1, mode="promise_in_bounds"
    )
    straight = lane + row < LANES
    above = jnp.sum(jnp.where(straight, turned, 0.0), axis=0, keepdims=True)
    below = jnp.sum(jnp.where(straight, 0.0, turned), axis=0, keepdims=True)
    return above, below


def transposed(array):
    return jnp.transpose(array.astype(F32)).astype(array.dtype)


def static_prepare(meta_ref, static):
    for ref, turned, value in zip(static[:3], static[3:], marks(meta_ref)):
        ref[...] = value
        turned[...] = transposed(value)


def head_back(
    parity, pair, rows_ref, wide_refs, k_ref, v_ref, mixed_ref, grad_ref, log_ref, static, diag_ref,
):
    mark_refs, turned_refs = static[:3], static[3:]
    first_ref, second_ref, key_image_ref, bias_ref = wide_refs
    head = 2 * pair + parity
    shared_t = turned_refs[2]
    rows = k_ref.shape[1]
    images = rows - TEXT
    tile = 256
    k, v, grad = k_ref[pair], v_ref[pair], grad_ref[pair]
    products = grad.astype(F32) * mixed_ref[pair]
    k_turned = transposed(k)
    is_image = rows_ref[1:2, TEXT:] > 0
    own = own_lanes(parity, rows)
    log_row = log_ref[pair, parity : parity + 1, :]
    first, shared = first_ref[head], mark_refs[2][...]
    q_text, q_image, k_text, k_image = joined(
        parity, first, second_ref[head], key_image_ref[head], k, mark_refs[parity][...], shared
    )
    bias = bias_ref[head].astype(F32)
    ones = jnp.where(own_lanes(parity, 8), 1.0, 0.0).astype(BF)
    delta = jnp.zeros((8, rows), F32)
    rest = products
    for _ in range(3):
        piece = rest.astype(BF)
        delta = delta + dot_nt(ones, piece)
        rest = rest - piece.astype(F32)
    delta = delta[0:1]
    v_own = jnp.where(own, v, jnp.zeros_like(v))
    q_marked = jnp.concatenate(
        [jnp.where(own, first, mark_refs[parity][...]), shared], axis=1
    )
    dq_text = jnp.zeros((HEAD, TEXT), F32)
    dq_image = jnp.zeros((HEAD, images), F32)
    dks = []
    dvs = []
    first_sum = jnp.zeros((LANES, LANES), F32)
    second_sum = jnp.zeros((LANES, LANES), F32)
    text_image = jnp.zeros((LANES, images), F32)

    def met(start, array, axis=0):
        text = near(start, tile)
        if axis == 0:
            return jnp.concatenate([array[text], array[TEXT:]], axis=0)
        return jnp.concatenate([array[:, text], array[:, TEXT:]], axis=1)

    def scored(start):
        here = slice(start, start + tile)
        if start < TEXT:
            scores = dot_nt(k_text[here], met(start, q_text))
        else:
            scores = dot_nt(k_image[start - TEXT : start - TEXT + tile], q_image)
            scores = jnp.concatenate([scores[:, :TEXT], scores[:, TEXT:] + bias], axis=1)
        return scores, dot_nt(v_own[here], met(start, grad))

    following = scored(0)
    for start in range(0, rows, tile):
        here = slice(start, start + tile)
        scores, prob_grad = following
        if start + tile < rows:
            following = scored(start + tile)
        soft = jnp.exp(scores - met(start, log_row, 1))
        score_grad = soft * (prob_grad - met(start, delta, 1))
        low = score_grad.astype(BF)
        dvs.append(dot_nn(soft.astype(BF), met(start, grad)))
        wide = dot_nn(low, met(start, q_marked))
        dks.append(wide[:, :LANES])
        part = dot_nn(k_turned[parity * HEAD : parity * HEAD + HEAD, here], low)
        text = near(start, tile)
        count = text.stop - text.start
        before = [jnp.zeros((HEAD, text.start), F32)] if text.start > 0 else []
        after = [jnp.zeros((HEAD, TEXT - text.stop), F32)] if text.stop < TEXT else []
        dq_text = dq_text + jnp.concatenate(before + [part[:, :count]] + after, axis=1)
        dq_image = dq_image + part[:, count:]
        rounded = wide.astype(BF)
        first_sum = first_sum + dot_nn(turned_refs[parity][:, here], rounded[:, :LANES])
        second_sum = second_sum + dot_nn(shared_t[:, here], rounded[:, LANES:])
        if start < TEXT:
            text_image = text_image + dot_nn(shared_t[:, here], low[:, count:])
        else:
            by_position = wide[:, LANES:]
            on_image = score_grad[:, TEXT:]
    dq = jnp.concatenate([dq_text, dq_image], axis=1)
    small = lax.broadcasted_iota(jnp.int32, (LANES, LANES), 1)
    small_row = lax.broadcasted_iota(jnp.int32, (LANES, LANES), 0)
    x0 = HEAD if parity == 0 else 0
    x_block = jnp.where(
        between(small, x0, x0 + COORD) & between(small_row, x0, x0 + COORD), first_sum, 0.0
    )
    y_block = jnp.where(
        between(small, Y0, Y0 + COORD) & between(small_row, Y0, Y0 + COORD), second_sum, 0.0
    )
    p_block = jnp.where((small < POS) & (small_row < POS), second_sum, 0.0)
    wide_lane = lax.broadcasted_iota(jnp.int32, (images, images), 1)
    outside = jnp.sum(jnp.where(is_image, 0.0, on_image), axis=1, keepdims=True)
    pairs = jnp.where(is_image, on_image, 0.0) + jnp.where(wide_lane == 0, outside, 0.0)
    outside_text = jnp.sum(jnp.where(is_image, 0.0, text_image), axis=1, keepdims=True)
    text_lane = lax.broadcasted_iota(jnp.int32, (LANES, images), 1)
    text_row = lax.broadcasted_iota(jnp.int32, (LANES, images), 0)
    text_image = jnp.where(is_image, text_image, 0.0) + jnp.where(
        text_lane == 0, outside_text, 0.0
    )
    text_image = jnp.where(text_row < POS, text_image, 0.0)
    first_lane = lax.broadcasted_iota(jnp.int32, (images, LANES), 1)
    left = pairs[:, :LANES] + jnp.where(first_lane < POS, by_position, 0.0)
    right = pairs[:, LANES:]
    a00, b00 = skewed(left[:LANES] + text_image[:, :LANES] + p_block)
    a01, b01 = skewed(right[:LANES] + text_image[:, LANES:])
    a10, b10 = skewed(left[LANES:])
    a11, b11 = skewed(right[LANES:])
    ax, bx = skewed(x_block)
    ay, by = skewed(y_block)
    diag_ref[head] = jnp.concatenate(
        [b10, b00 + b11 + a10, a00 + a11 + b01, a01, bx, ax, by, ay], axis=0
    )
    return dq * 0.125, jnp.concatenate(dks, axis=0), jnp.concatenate(dvs, axis=0)


MESH = pl.DeviceIdType.MESH
VMEM = pl.BlockSpec(memory_space=pltpu.VMEM)
HBM = pl.BlockSpec(memory_space=pltpu.HBM)
MIB = 1024 * 1024


def remote(src, dst, send, receive, device):
    return pltpu.make_async_remote_copy(
        src_ref=src, dst_ref=dst, send_sem=send, recv_sem=receive, device_id=device,
        device_id_type=MESH,
    )


def project_kernel(
    layer_ref, weight_hbm, *refs,
):
    small_hbm, refs = refs[:10], refs[10:]
    (item_ref, projected_out, columns_ref, rows_ref, table_ref,
     projected_ref, weight_ref, meta_send, bias_ref, sems, load_sems, store_sems), small = (
        refs[:12], refs[12:],
    )
    (segment_ref, mask_ref, position_ref, across_ref, down_ref, query_bias_ref, value_bias_ref,
     text_ref, horiz_ref, vert_ref) = small
    mine = lax.axis_index("seq")
    partner = (1 - mine, lax.axis_index("dp"))
    count, width = layer_ref.shape[1:]
    own = pl.ds(pl.multiple_of(mine * count, LANES), count)
    loads = [
        pltpu.make_async_copy(source, target, load_sems.at[index])
        for index, (source, target) in enumerate(
            list(zip(small_hbm, small))
            + [(layer_ref.at[mine], item_ref.at[own]), (weight_hbm, weight_ref)]
        )
    ]
    for load in loads:
        load.start()
    barrier = pltpu.get_barrier_semaphore()
    pl.semaphore_signal(barrier, inc=1, device_id=partner, device_id_type=MESH)
    pl.semaphore_wait(barrier, 1)
    pieces = count // LANES
    rows_out = [
        remote(
            layer_ref.at[1 - mine, pl.ds(piece * LANES, LANES)],
            item_ref.at[pl.ds(pl.multiple_of(mine * count + piece * LANES, LANES), LANES)],
            sems.at[0, piece], sems.at[1, piece], partner,
        )
        for piece in range(pieces)
    ]
    for copy in rows_out:
        copy.start()
    for load in loads[:-2]:
        load.wait()

    fields = (segment_ref, mask_ref, position_ref, across_ref, down_ref)
    blocks = [
        jnp.concatenate(
            [field[item : item + 1, :] for field in fields] + [jnp.zeros((3, count), jnp.int32)],
            axis=0,
        )
        for item in range(2)
    ]
    meta_send[...] = jnp.where(mine == 0, blocks[1], blocks[0])
    meta_out = remote(
        meta_send, rows_ref.at[:, own], sems.at[0, pieces], sems.at[1, pieces], partner
    )
    meta_out.start()
    rows_ref[:, own] = jnp.where(mine == 0, blocks[0], blocks[1])
    bias_ref[:, :width] = query_bias_ref[...].astype(F32).reshape(1, width)
    bias_ref[:, width : 2 * width] = jnp.zeros((1, width), F32)
    bias_ref[:, 2 * width :] = value_bias_ref[...].astype(F32).reshape(1, width)
    heads, levels = text_ref.shape
    spot = lax.broadcasted_iota(jnp.int32, (levels, LANES), 1)
    level = lax.broadcasted_iota(jnp.int32, (levels, LANES), 0)
    table = jnp.zeros((heads, LANES), F32)
    for source, begin in ((text_ref, 0), (horiz_ref, X_TABLE), (vert_ref, Y_TABLE)):
        table = table + dot_nn(source[...], (spot == level + begin).astype(BF))
    table_ref[...] = jnp.concatenate([table, jnp.zeros((16 - heads, LANES), F32)], axis=0)

    def project(there):
        step = 256

        def body(index, carry):
            columns = pl.ds(pl.multiple_of(index * step, step), step)
            product = dot_nn(item_ref[there], weight_ref[:, columns])
            projected_ref[there, columns] = (product + bias_ref[:, columns]).astype(BF)
            return carry

        lax.fori_loop(0, 3 * width // step, body, 0)

    def stored(index, there):
        return pltpu.make_async_copy(
            projected_ref.at[there], projected_out.at[there], store_sems.at[index]
        )

    for load in loads[-2:]:
        load.wait()
    project(own)
    stored(0, own).start()
    for piece in range(pieces):
        rows_out[piece].wait()
        there = pl.ds(pl.multiple_of((1 - mine) * count + piece * LANES, LANES), LANES)
        project(there)
        stored(1 + piece, there).start()
    meta_out.wait()
    meta = rows_ref[...].astype(F32)
    tall = jnp.concatenate([meta, jnp.zeros((LANES - 8, meta.shape[1]), F32)], axis=0)
    columns_ref[...] = jnp.transpose(tall).astype(jnp.int32)
    stored(0, own).wait()
    for piece in range(pieces):
        there = pl.ds(pl.multiple_of((1 - mine) * count + piece * LANES, LANES), LANES)
        stored(1 + piece, there).wait()


def projected_item(layer_in, fields, qkv_weight, query_bias, value_bias, tables):
    rows = 2 * layer_in.shape[1]
    width = layer_in.shape[2]
    pieces = rows // 2 // LANES
    small = list(fields) + [query_bias, value_bias] + [t.T for t in tables]
    return pl.pallas_call(
        project_kernel,
        in_specs=[HBM] * (2 + len(small)),
        out_specs=[VMEM, HBM, VMEM, VMEM, VMEM],
        out_shape=[
            jax.ShapeDtypeStruct((rows, width), BF),
            jax.ShapeDtypeStruct((rows, 3 * width), BF),
            jax.ShapeDtypeStruct((rows, LANES), jnp.int32),
            jax.ShapeDtypeStruct((8, rows), jnp.int32),
            jax.ShapeDtypeStruct((16, LANES), F32),
        ],
        scratch_shapes=[
            pltpu.VMEM((rows, 3 * width), BF),
            pltpu.VMEM((width, 3 * width), BF),
            pltpu.VMEM((8, rows // 2), jnp.int32),
            pltpu.VMEM((1, 3 * width), F32),
            pltpu.SemaphoreType.DMA((2, pieces + 1)),
            pltpu.SemaphoreType.DMA((len(small) + 2,)),
            pltpu.SemaphoreType.DMA((pieces + 1,)),
        ]
        + [pltpu.VMEM(array.shape, array.dtype) for array in small],
        compiler_params=pltpu.CompilerParams(
            collective_id=1, has_side_effects=True, vmem_limit_bytes=60 * MIB
        ),
        name="projected_item",
    )(layer_in, qkv_weight, *small)


EPSILON = 1e-05
TILE = 256


def vector(ref):
    return ref[...].astype(F32).reshape(1, ref.shape[0])


def gelu_and_slope(x):
    bell = jnp.exp2(-0.7213475204444817 * (x * x))
    rough = 1.0 + 0.23164188826 * jnp.abs(x)
    t = pl.reciprocal(rough, approx=True)
    t = t * (2.0 - rough * t)
    series = t * (
        0.127414796
        + t * (-0.142248368 + t * (0.7107068705 + t * (-0.7265760135 + t * 0.5307027145)))
    )
    tail = bell * series
    below = jnp.where(x >= 0.0, 1.0 - tail, tail)
    return x * below, below + x * (0.3989422804014327 * bell)


def row_mean(block):
    return jnp.mean(block, axis=1, keepdims=True)


def normalized(hidden):
    center = hidden - row_mean(hidden)
    scale = lax.rsqrt(row_mean(center * center) + EPSILON)
    return center * scale, scale


def norm_pulled(grad, unit, scale):
    return scale * (grad - row_mean(grad) - unit * row_mean(grad * unit))


def column_sum(block):
    return jnp.sum(block, axis=0, keepdims=True)


def feed_kernel(
    item_hbm, mixed_hbm, cotangent_ref, out_weight_ref, up_ref, down_ref, *refs,
):
    vectors_hbm, refs = refs[:7], refs[7:]
    (layer_out, total_out, unit_out, scale_out, grad_down_ref, grad_up_ref, small_ref,
     item_ref, mixed_ref, layer_ref, cotangent_all, active, slope, unit, scale_ref, normed, normed_t, total, d_branch, d_branch_t,
     sems, load_sems, tile_sems, store_sems) = refs[:24]
    vectors = refs[24:]
    (out_bias_ref, attn_gain_ref, attn_shift_ref, up_bias_ref, down_bias_ref, ffn_gain_ref,
     ffn_shift_ref) = vectors
    step = pl.program_id(0)
    blocks = pl.num_programs(0) // 2
    rows, width = item_hbm.shape
    count = rows // 2
    mine = lax.axis_index("seq")
    partner = (1 - mine, lax.axis_index("dp"))
    own = pl.ds(pl.multiple_of(mine * count, LANES), count)
    tiles = rows // TILE

    def sent():
        return remote(
            cotangent_ref.at[1 - mine], cotangent_all.at[own], sems.at[0], sems.at[1], partner
        )

    def returned():
        theirs = pl.ds(pl.multiple_of((1 - mine) * count, LANES), count)
        return [
            pltpu.make_async_copy(layer_ref.at[own], layer_out.at[mine], load_sems.at[8]),
            remote(
                layer_ref.at[theirs], layer_out.at[mine], sems.at[2], sems.at[3], partner
            ),
        ]

    def tile_loads(tile):
        there = pl.ds(tile * TILE, TILE)
        return [
            pltpu.make_async_copy(source.at[there], target.at[there], tile_sems.at[index, tile])
            for index, (source, target) in enumerate(
                ((mixed_hbm, mixed_ref), (item_hbm, item_ref))
            )
        ]

    def store(index):
        source, target = (
            (total, total_out), (unit, unit_out), (scale_ref, scale_out),
        )[index]
        return pltpu.make_async_copy(source, target, store_sems.at[index])

    def loads():
        copies = list(zip(vectors_hbm, vectors)) + [(cotangent_ref.at[mine], cotangent_all.at[own])]
        return [
            pltpu.make_async_copy(source, target, load_sems.at[index])
            for index, (source, target) in enumerate(copies)
        ]

    def over_tiles(size, body, carry, unroll=1):
        def run(index, state):
            return body(pl.ds(pl.multiple_of(index * size, size), size), state)

        return lax.fori_loop(0, rows // size, run, carry, unroll=unroll)

    @pl.when(step == 0)
    def _():
        for index in range(rows // TILE):
            for load in tile_loads(index):
                load.start()
        for load in loads():
            load.start()
        barrier = pltpu.get_barrier_semaphore()
        pl.semaphore_signal(barrier, inc=1, device_id=partner, device_id_type=MESH)
        pl.semaphore_wait(barrier, 1)
        sent().start()
        small_ref[...] = jnp.zeros_like(small_ref)
        for load in loads():
            load.wait()
        out_bias, gain, shift = vector(out_bias_ref), vector(attn_gain_ref), vector(attn_shift_ref)

        for index in range(rows // TILE):
            for load in tile_loads(index):
                load.wait()
            there = slice(index * TILE, index * TILE + TILE)
            attn = dot_nn(mixed_ref[there].astype(BF), out_weight_ref[...]) + out_bias
            standard, scale = normalized(item_ref[there].astype(F32) + attn)
            unit[there] = standard
            scale_ref[there] = jnp.broadcast_to(scale, (TILE, LANES))
            result = standard * gain + shift
            normed[there] = result.astype(BF)
            normed_t[:, there] = jnp.transpose(result).astype(BF)
        store(1).start()
        store(2).start()
        total[...] = jnp.zeros_like(total)

    @pl.when(step < blocks)
    def _():
        columns = [slice(begin, begin + TILE) for begin in range(0, width, TILE)]
        low = normed[...]
        following = dot_nn(low, up_ref[:, columns[0]])
        values = []
        for index, here in enumerate(columns):
            product = following
            if index + 1 < len(columns):
                following = dot_nn(low, up_ref[:, columns[index + 1]])
            bias = up_bias_ref[pl.ds(pl.multiple_of(step * width + here.start, LANES), TILE)]
            value, grade = gelu_and_slope(product + bias.astype(F32).reshape(1, TILE))
            values.append(value.astype(BF))
            active[step, :, here] = values[-1]
            slope[step, :, here] = grade.astype(BF)
        values = jnp.concatenate(values, axis=1)
        for here in columns:
            total[:, here] += dot_nn(values, down_ref[:, here])

    @pl.when(step == blocks)
    def _():
        sent().wait()
        gain, shift, bias = vector(ffn_gain_ref), vector(ffn_shift_ref), vector(down_bias_ref)
        first_gain, first_shift = vector(attn_gain_ref), vector(attn_shift_ref)

        def tile(there, sums):
            hidden = unit[there] * first_gain + first_shift + (total[there] + bias)
            standard, scale = normalized(hidden)
            layer_ref[there] = (standard * gain + shift).astype(BF)
            cotangent = cotangent_all[there].astype(F32)
            pulled = norm_pulled(cotangent * gain, standard, scale)
            total[there] = pulled
            low = pulled.astype(BF)
            d_branch[there] = low
            return (
                sums[0] + column_sum(low.astype(F32)),
                sums[1] + column_sum(cotangent * standard),
                sums[2] + column_sum(cotangent),
            )

        zero = jnp.zeros((1, width), F32)
        sums = over_tiles(64, tile, (zero, zero, zero), 4)
        for row, value in zip((5, 6, 7), sums):
            small_ref[row : row + 1] = value

        for copy in returned():
            copy.start()

        def turn(there, carry):
            d_branch_t[:, there] = jnp.transpose(d_branch[there].astype(F32)).astype(BF)
            return carry

        over_tiles(TILE, turn, 0, 3)

    @pl.when(step >= blocks)
    def _():
        block = step - blocks

        columns = [slice(begin, begin + TILE) for begin in range(0, width, TILE)]
        branch = d_branch[...]
        turned = d_branch_t[...]
        following = dot_nt(branch, down_ref[columns[0]])
        values = []
        for index, here in enumerate(columns):
            product = following
            if index + 1 < len(columns):
                following = dot_nt(branch, down_ref[columns[index + 1]])
            grad_down_ref[:, here] = dot_nn(turned, active[block, :, here]).astype(BF)
            d_up = (product * slope[block, :, here].astype(F32)).astype(BF)
            small_ref[pl.ds(8 + block, 1), here] = column_sum(d_up.astype(F32))
            values.append(d_up)
        values = jnp.concatenate(values, axis=1)
        turned = normed_t[...]
        for here in columns:
            grad_up_ref[:, here] = dot_nn(turned, values[:, here]).astype(BF)
            total[:, here] += dot_nt(values, up_ref[here])

    @pl.when(step == 2 * blocks - 1)
    def _():
        store(0).start()
        for copy in returned() + [store(0), store(1), store(2)]:
            copy.wait()


def fed_forward_and_back(
    item, mixed, cotangent, out_weight, up_weight, down_weight, vectors,
):
    rows, width = item.shape
    blocks = up_weight.shape[1] // width
    whole = pl.BlockSpec(memory_space=pltpu.VMEM)
    square = lambda kind: jax.ShapeDtypeStruct((rows, width), kind)
    later = lambda i: jnp.maximum(i - blocks, 0)
    return pl.pallas_call(
        feed_kernel,
        grid=(2 * blocks,),
        in_specs=[HBM, HBM, HBM, whole]
        + [
            pl.BlockSpec((width, width), lambda i: (0, lax.rem(i, blocks))),
            pl.BlockSpec((width, width), lambda i: (lax.rem(i, blocks), 0)),
        ]
        + [HBM] * 7,
        out_specs=[HBM] * 4
        + [
            pl.BlockSpec((width, width), lambda i: (later(i), 0)),
            pl.BlockSpec((width, width), lambda i: (later(i), 0)),
            whole,
        ],
        out_shape=[
            jax.ShapeDtypeStruct((2, rows // 2, width), BF), square(F32), square(F32),
            jax.ShapeDtypeStruct((rows, LANES), F32),
            jax.ShapeDtypeStruct((blocks * width, width), BF),
            jax.ShapeDtypeStruct((blocks * width, width), BF),
            jax.ShapeDtypeStruct((16, width), F32),
        ],
        scratch_shapes=[
            pltpu.VMEM((rows, width), BF),
            pltpu.VMEM((rows, width), F32),
            pltpu.VMEM((rows, width), BF),
            pltpu.VMEM((rows, width), BF),
            pltpu.VMEM((blocks, rows, width), BF),
            pltpu.VMEM((blocks, rows, width), BF),
            pltpu.VMEM((rows, width), F32),
            pltpu.VMEM((rows, LANES), F32),
            pltpu.VMEM((rows, width), BF),
            pltpu.VMEM((width, rows), BF),
            pltpu.VMEM((rows, width), F32),
            pltpu.VMEM((rows, width), BF),
            pltpu.VMEM((width, rows), BF),
            pltpu.SemaphoreType.DMA((4,)),
            pltpu.SemaphoreType.DMA((9,)),
            pltpu.SemaphoreType.DMA((2, rows // TILE)),
            pltpu.SemaphoreType.DMA((3,)),
        ]
        + [pltpu.VMEM(vector.shape, vector.dtype) for vector in vectors],
        compiler_params=pltpu.CompilerParams(
            collective_id=2, has_side_effects=True, vmem_limit_bytes=60 * MIB
        ),
        name="feed_forward",
    )(item, mixed, cotangent, out_weight, up_weight, down_weight, *vectors)


SLOTS = 4


def finish_kernel(
    main_ref, tail_ref, input_hbm, small_ref, diagonal_ref,
    down_ref, up_ref, out_ref, qkv_ref, input_ref, *refs,
):
    singles, (main_in, tail_in, slots, input_in, input_slot, in_sems, out_sems, item_sems) = (
        refs[:12], refs[12:],
    )
    mains, width = main_in.shape[0], main_in.shape[2]
    pairs, across = tail_in.shape[0], tail_in.shape[2]
    hidden = mains // 2
    blocks = mains + pairs

    def load(block):
        if block < mains:
            source, target = main_ref.at[pl.ds(block * width, width)], main_in.at[block]
        else:
            pair = block - mains
            source, target = tail_ref.at[pl.ds(pair * TAIL_ROWS, TAIL_ROWS)], tail_in.at[pair]
        return pltpu.make_async_copy(source, target, in_sems.at[block])

    def stores(block):
        slot, sem = slots.at[block % SLOTS], out_sems.at[block % SLOTS]
        if block < hidden:
            targets = [(slot, down_ref.at[pl.ds(block * width, width)])]
        elif block < mains:
            targets = [(slot, up_ref.at[:, pl.ds((block - hidden) * width, width)])]
        else:
            pair = block - mains
            targets = [
                (
                    slot.at[:, pl.ds(part * LANES, LANES)],
                    qkv_ref.at[:, pl.ds(part * width + pair * LANES, LANES)],
                )
                for part in range(3)
            ]
            down = pl.ds(0, TAIL_ROWS - width)
            targets.append(
                (slot.at[down, pl.ds(across, across)], out_ref.at[out_spot(pair, pairs, width)])
            )
        return [
            pltpu.make_async_copy(source, target, sem.at[index])
            for index, (source, target) in enumerate(targets)
        ]

    load_input = pltpu.make_async_copy(input_hbm, input_in, item_sems.at[0])
    store_input = pltpu.make_async_copy(input_slot, input_ref, item_sems.at[1])
    for block in range(blocks):
        load(block).start()
    load_input.start()
    for block in range(blocks):
        load(block).wait()
        if block >= SLOTS:
            for copy in stores(block - SLOTS):
                copy.wait()
        slot = block % SLOTS
        if block < hidden:
            slots[slot] = jnp.transpose(main_in[block].astype(F32))
        elif block < mains:
            slots[slot] = main_in[block].astype(F32)
        else:
            slots[slot, :, :across] = tail_in[block - mains, :width].astype(F32)
            slots[slot, : TAIL_ROWS - width, across:] = tail_in[block - mains, width:].astype(F32)
        for copy in stores(block):
            copy.start()
    load_input.wait()
    input_slot[...] = input_in[...].astype(F32)
    store_input.start()
    for row in range(8):
        singles[row][...] = small_ref[row]
    for row in range(hidden):
        singles[8][row * width : row * width + width] = small_ref[8 + row]
    heads, levels = singles[9].shape
    diagonals = diagonal_ref[...]
    level = lax.broadcasted_iota(jnp.int32, (LANES, LANES), 1)
    lane = lax.broadcasted_iota(jnp.int32, (LANES, LANES), 0)
    for table, (first, size, skip) in enumerate(((0, 4, 0), (4, 2, 1), (6, 2, 1))):
        total = jnp.zeros((heads, LANES), F32)
        for row in range(size):
            distance = lane + LANES * (row + skip - 2)
            chosen = (bucket(distance) == level).astype(F32)
            total = total + jnp.dot(
                diagonals[:, first + row, :], chosen, preferred_element_type=F32,
                precision=lax.Precision.HIGHEST,
            )
        singles[9 + table][...] = total[:, :levels]
    for block in range(blocks - SLOTS, blocks):
        for copy in stores(block):
            copy.wait()
    store_input.wait()


def finished(main, tail, grad_input, small, diagonals, hidden, levels):
    width = main.shape[1]
    heads = diagonals.shape[0]
    mains = main.shape[0] // width
    pairs = tail.shape[0] // TAIL_ROWS
    single = jax.ShapeDtypeStruct((width,), F32)
    table = jax.ShapeDtypeStruct((heads, levels), F32)
    dma = pltpu.SemaphoreType.DMA
    return pl.pallas_call(
        finish_kernel,
        in_specs=[HBM, HBM, HBM, VMEM, VMEM],
        out_specs=[HBM] * 5 + [VMEM] * 12,
        out_shape=[
            jax.ShapeDtypeStruct((hidden, width), F32),
            jax.ShapeDtypeStruct((width, hidden), F32),
            jax.ShapeDtypeStruct((width, width), F32),
            jax.ShapeDtypeStruct((width, 3 * width), F32),
            jax.ShapeDtypeStruct(grad_input.shape, F32),
        ]
        + [single] * 8
        + [jax.ShapeDtypeStruct((hidden,), F32)]
        + [table] * 3,
        scratch_shapes=[
            pltpu.VMEM((mains, width, width), BF),
            pltpu.VMEM((pairs, TAIL_ROWS, tail.shape[1]), BF),
            pltpu.VMEM((SLOTS, width, width), F32),
            pltpu.VMEM(grad_input.shape, BF),
            pltpu.VMEM(grad_input.shape, F32),
            dma((mains + pairs,)),
            dma((SLOTS, 4)),
            dma((2,)),
        ],
        compiler_params=pltpu.CompilerParams(vmem_limit_bytes=56 * MIB),
        name="finished",
    )(main, tail, grad_input, small, diagonals)


PIECE = 16


class Place:
    def __init__(self, depth):
        place = lax.axis_index("dp")
        self.depth = depth
        self.group = lax.div(place, 4 * depth)
        self.z = lax.rem(lax.div(place, 4), depth)
        self.bits = {
            "x": lax.axis_index("seq"),
            "c": lax.rem(place, 2),
            "y": lax.rem(lax.div(place, 2), 2),
            "a": lax.rem(self.z, 2),
            "b": lax.div(self.z, 2),
        }

    def partner(self, letters):
        bit = {
            letter: 1 - value if letter in letters else value
            for letter, value in self.bits.items()
        }
        z = self.z
        for letter, reach in (("a", 1), ("b", 2)):
            if letter in letters:
                z = z + reach - 2 * reach * self.bits[letter]
        return (bit["x"], (self.group * self.depth + z) * 4 + bit["y"] * 2 + bit["c"])

    def greet(self, met):
        barrier = pltpu.get_barrier_semaphore()
        for letters in met:
            pl.semaphore_signal(
                barrier, inc=1, device_id=self.partner(letters), device_id_type=MESH
            )
        pl.semaphore_wait(barrier, len(met))


def letters_of(depth):
    return "xy" + "ab"[: (depth - 1).bit_length()]


def parsed(routes, depth):
    kept = letters_of(depth)
    parts = []
    for route in routes.split():
        hops = ["".join(letter for letter in hop if letter in kept) for hop in route.split(".")]
        parts.append([hop for hop in hops if hop])
    return parts


def subsets(hop):
    return [
        "".join(letter for index, letter in enumerate(hop) if mask >> index & 1)
        for mask in range(1, 2 ** len(hop))
    ]


class Chunk:
    def __init__(self, place, depth, source, out_ref, offset, spot, scratch):
        _, self.begin, rows, first, columns, _, routes, _ = spot
        self.place, self.source, self.columns = place, source, pl.ds(first, columns)
        self.out_ref, self.out_begin = out_ref, offset + self.begin
        self.parts = parsed(routes, depth)
        self.half = rows // 2
        self.share = self.half // len(self.parts)
        self.hops = max(len(part) for part in self.parts)
        self.work, self.fresh, *landing, self.sends, self.receives, self.locals = scratch
        self.landing = {}
        self.sems = {}
        count = 2
        for part, hops in enumerate(self.parts):
            for hop, letters in enumerate(hops):
                self.landing[part, hop] = landing.pop(0)
                for way in range(2):
                    for index in range(2 ** len(letters) - 1):
                        self.sems[way, part, hop, index] = count
                        count += 1

    def aligned(self, value):
        return pl.multiple_of(value, PIECE)

    def size(self, part, hop):
        return self.share >> sum(len(letters) for letters in self.parts[part][: hop + 1])

    def spot(self, part, hop, other=""):
        start = part * self.share
        for level in range(hop + 1):
            for index, letter in enumerate(self.parts[part][level]):
                bit = self.place.bits[letter]
                if level == hop and letter in other:
                    bit = 1 - bit
                start = start + bit * (self.size(part, level) << index)
        return start

    def out(self, core):
        begin = self.aligned(self.out_begin + core * self.half)
        return self.out_ref.at[pl.ds(begin, self.half), self.columns]

    def held(self, buffer, begin, size):
        return buffer.at[pl.ds(self.aligned(begin), size)]

    def copy(self, index, source, target, letters):
        return remote(
            source, target, self.sends.at[index], self.receives.at[index],
            self.place.partner(letters),
        )

    def pair_down(self):
        core = self.place.bits["c"]
        at = lambda c: self.source.at[
            pl.ds(self.aligned(self.begin + c * self.half), self.half), self.columns
        ]
        return [
            self.copy(0, at(1 - core), self.fresh, "c"),
            pltpu.make_async_copy(at(core), self.work, self.locals.at[0]),
        ]

    def pair_up(self, arriving):
        core = self.place.bits["c"]
        return [
            self.copy(1, self.fresh, self.out(1 - core if arriving else core), "c"),
            pltpu.make_async_copy(self.fresh, self.out(core), self.locals.at[1]),
        ]

    def at_hop(self, hop):
        return [
            (part, hops[hop]) for part, hops in enumerate(self.parts) if hop < len(hops)
        ]

    def down(self, hop):
        copies = []
        for part, letters in self.at_hop(hop):
            size = self.size(part, hop)
            for index, other in enumerate(subsets(letters)):
                copies.append(
                    self.copy(
                        self.sems[0, part, hop, index],
                        self.held(self.work, self.spot(part, hop, other), size),
                        self.landing[part, hop].at[index], other,
                    )
                )
        return copies

    def up(self, hop, arriving):
        copies = []
        for part, letters in self.at_hop(hop):
            mine = self.spot(part, hop)
            size = self.size(part, hop)
            for index, other in enumerate(subsets(letters)):
                target = self.spot(part, hop, other) if arriving else mine
                copies.append(
                    self.copy(
                        self.sems[1, part, hop, index], self.held(self.fresh, mine, size),
                        self.held(self.fresh, target, size), other,
                    )
                )
        return copies

    def add(self, begin, sources, size):
        step = 64 if size % 64 == 0 else 32 if size % 32 == 0 else PIECE

        def body(index, carry):
            offset = self.aligned(index * step)
            there = pl.ds(self.aligned(begin + offset), step)
            total = self.work[there]
            if len(sources) == 1:
                total = total + sources[0][pl.ds(offset, step)]
            else:
                total = total.astype(F32)
                for source in sources:
                    total = total + source[pl.ds(offset, step)].astype(F32)
            self.work[there] = total.astype(BF)
            return carry

        lax.fori_loop(0, size // step, body, 0)

    def stage(self, number):
        hops = self.hops
        ended, started = [], []
        if number == 0:
            started = self.pair_down()
        elif number == 1:
            ended = self.pair_down()
            started = self.down(0)
        elif number <= hops:
            ended = self.down(number - 2)
            started = self.down(number - 1)
        elif number == hops + 1:
            ended = self.down(hops - 1)
            started = self.up(hops - 1, False)
        elif number <= 2 * hops:
            level = 2 * hops + 1 - number
            ended = self.up(level, True)
            started = self.up(level - 1, False)
        elif number == 2 * hops + 1:
            ended = self.up(0, True)
            started = self.pair_up(False)
        else:
            ended = self.pair_up(True)
        for copy in ended:
            copy.wait()
        if number == 1:
            self.add(0, [self.fresh], self.half)
        elif 2 <= number <= hops + 1:
            hop = number - 2
            for part, letters in self.at_hop(hop):
                landing = self.landing[part, hop]
                sources = [landing.at[index] for index in range(2 ** len(letters) - 1)]
                self.add(self.spot(part, hop), sources, self.size(part, hop))
        if number == hops + 1:
            for part, route in enumerate(self.parts):
                last = len(route) - 1
                there = pl.ds(self.aligned(self.spot(part, last)), self.size(part, last))
                self.fresh[there] = self.work[there]
        for copy in started:
            copy.start()


def chunk_scratch(spot, depth):
    _, _, rows, _, columns, _, routes, _ = spot
    parts = parsed(routes, depth)
    landing = []
    copies = 2
    for hops in parts:
        size = rows // 2 // len(parts)
        for letters in hops:
            size >>= len(letters)
            others = 2 ** len(letters) - 1
            copies += 2 * others
            landing.append(pltpu.VMEM((others, size, columns), BF))
    dma = pltpu.SemaphoreType.DMA
    return (
        [pltpu.VMEM((rows // 2, columns), BF)] * 2
        + landing
        + [dma((copies,)), dma((copies,)), dma((2,))]
    )


def loads_of(hop, size):
    if "x" in hop and "y" in hop:
        return [("x", 2 * size), ("y", 2 * size)]
    if hop in ("x", "y"):
        return [(hop, size)]
    if "a" in hop and "b" in hop:
        return [("end", 3 * size), ("middle", 4 * size)]
    return [("end", size), ("middle", 2 * size)] if hop == "b" else [("end", size)]


def planned(chunks, work, depth, hop_count):
    latency, issue, link, pair = 3.5, 0.08, 100e3, 600e3
    free = {}
    now = 3.0
    chains = []
    for rows, columns, need, routes, _ in chunks:
        parts = parsed(routes, depth)
        sizes = [rows // 2 // len(parts)] * len(parts)
        down = []
        for hop in range(max(len(part) for part in parts)):
            loads, copies, added = [], 0, 0
            for index, part in enumerate(parts):
                if hop < len(part):
                    sizes[index] >>= len(part[hop])
                    others = 2 ** len(part[hop]) - 1
                    loads += loads_of(part[hop], sizes[index])
                    copies += others
                    added += sizes[index] * others
            down.append((loads, copies, added, columns))
        first = [([("core", rows // 2)], 1.5, rows // 2, columns)]
        last = [([("core", rows // 2)], 1, 0, columns)]
        chains.append((need, first + down + down[::-1] + last))
    chains.append((len(work), [([("core", 16)], 2, 0, 768)] * hop_count))
    ranks = [chunk[4] for chunk in chunks] + [0]
    position = [0] * len(chains)
    ready = [0.0] * len(chains)
    order = [[] for _ in range(len(work) + 1)]
    done = 0
    while True:
        open_ones = [
            (ranks[i], ready[i], i) for i, (need, chain) in enumerate(chains)
            if position[i] <= len(chain) and need <= done
        ]
        due = [entry for entry in open_ones if entry[1] <= now]
        if not due and done < len(work):
            now += work[done]
            done += 1
            continue
        if not open_ones:
            return order
        _, when, index = min(due) if due else min(open_ones, key=lambda entry: entry[1])
        now = max(now, when)
        chain = chains[index][1]
        stage = position[index]
        order[done].append((index, stage))
        if 0 < stage <= len(chain) // 2:
            now += 1e-6 * chain[stage - 1][2] * chain[stage - 1][3]
        if stage < len(chain):
            loads, copies, _, columns = chain[stage]
            now += issue * copies
            end = now
            for lane, rows in loads:
                rate = pair if lane == "core" else link / 2
                free[lane] = max(now, free.get(lane, 0.0)) + 2 * rows * columns / rate
                end = max(end, free[lane])
            ready[index] = end + latency
        position[index] += 1


def last_kernel(
    depth, plan, orders, counts, *refs,
):
    (meta_ref, rows_ref, projected_hbm, mixed_hbm, log_ref, first_hbm, second_hbm,
     key_image_hbm, bias_hbm, small_ref, gain_ref, item_hbm, weight_hbm, total_hbm, unit_hbm, scale_hbm,
     out_weight_hbm, grad_down_ref, grad_up_ref,
     main_out, tail_out, small_out, diagonal_out, input_out,
     *scratch) = refs
    static, scratch = scratch[:6], scratch[6:]
    (k_ref, v_ref, mixed_ref, grad_ref, first_ref, second_ref, key_image_ref, bias_ref, pair_sems,
     item_ref, weight_ref, d_hidden_ref, unit_ref, scale_ref, load_sems, d_project, item_t, tail, input_grad,
     small_in, diagonal_in, small_sems, item_sems, *scratch) = scratch
    out_weight_ref = item_t
    place = Place(depth)
    step = pl.program_id(0)
    pairs = k_ref.shape[0]
    rows, width = item_hbm.shape
    count = rows // 2
    x = place.bits["x"]
    hidden = grad_down_ref.shape[0]
    sources = ((grad_down_ref, main_out, 0), (grad_up_ref, main_out, hidden), (tail, tail_out, 0))
    chunks = []
    for spot, pieces in zip(plan, counts):
        chunks.append(Chunk(place, depth, *sources[spot[0]], spot, scratch[:pieces]))
        scratch = scratch[pieces:]
    hop_letters = "c" + letters_of(depth)
    wide_hbm = (first_hbm, second_hbm, key_image_hbm, bias_hbm)
    wide_refs = (first_ref, second_ref, key_image_ref, bias_ref)

    def pair_loads(pair):
        copies = []
        held = ((projected_hbm, k_ref, width), (projected_hbm, v_ref, 2 * width))
        for source, target, first in held:
            columns = pl.ds(pl.multiple_of(first + pair * LANES, LANES), LANES)
            copies.append((source.at[:, columns], target.at[pair]))
        heads = pl.ds(2 * pair, 2)
        for source, target in zip(wide_hbm, wide_refs):
            copies.append((source.at[heads], target.at[heads]))
        return [
            pltpu.make_async_copy(source, target, pair_sems.at[pair, index])
            for index, (source, target) in enumerate(copies)
        ]

    def loads(first):
        if first:
            copies = [
                (total_hbm, d_hidden_ref), (unit_hbm, unit_ref), (scale_hbm, scale_ref),
                (out_weight_hbm, out_weight_ref), (item_hbm, item_ref),
            ]
            copies += [
                (mixed_hbm.at[:, pl.ds(pair * LANES, LANES)], mixed_ref.at[pair])
                for pair in range(pairs)
            ]
        else:
            copies = [(weight_hbm, weight_ref)]
        return [
            pltpu.make_async_copy(source, target, load_sems.at[0 if first else 1, index])
            for index, (source, target) in enumerate(copies)
        ]

    def back_to_attention():
        gain = vector(gain_ref)

        def tile(index, sums):
            there = pl.ds(pl.multiple_of(index * 64, 64), 64)
            d_normed = d_hidden_ref[there]
            standard = unit_ref[there]
            d_hidden = norm_pulled(d_normed * gain, standard, scale_ref[there, :1])
            d_hidden_ref[there] = d_hidden
            low = d_hidden.astype(BF)
            input_grad[there] = low
            return (
                sums[0] + column_sum(low.astype(F32)),
                sums[1] + column_sum(d_normed * standard),
                sums[2] + column_sum(d_normed),
            )

        zero = jnp.zeros((1, width), F32)
        sums = lax.fori_loop(0, rows // 64, tile, (zero, zero, zero), unroll=4)
        for row, value in zip((2, 3, 4), sums):
            small_out[row : row + 1] = value

    def back_to_heads():
        low = input_grad[...]
        down = TAIL_ROWS - width
        for begin in range(0, width, down):
            first = begin // LANES
            several = range(first, first + down // LANES)
            d_mixed = dot_nt(low, out_weight_ref[begin : begin + down]).astype(BF)
            for index, pair in enumerate(several):
                grad_ref[pair] = d_mixed[:, index * LANES : index * LANES + LANES]
            turned = jnp.concatenate(
                [jnp.transpose(mixed_ref[pair]).astype(BF) for pair in several], axis=0
            )
            for pair in range(pairs):
                rows_of, across = out_spot(pair, pairs, width)
                if rows_of.start == begin:
                    product = dot_nn(turned, low[:, across.start : across.start + across.size])
                    base = pair * TAIL_ROWS + width
                    tail[base : base + down] = product.astype(BF)

    def input_copies():
        return [
            pltpu.make_async_copy(
                input_grad.at[pl.ds(pl.multiple_of(x * count, LANES), count)], input_out.at[x],
                item_sems.at[0],
            ),
            remote(
                input_grad.at[pl.ds(pl.multiple_of((1 - x) * count, LANES), count)],
                input_out.at[x], item_sems.at[1], item_sems.at[2], place.partner("x"),
            ),
        ]

    def small_copies(hop):
        return [
            remote(source, landing.at[hop], small_sems.at[0, kind, hop],
                   small_sems.at[1, kind, hop], place.partner(hop_letters[hop]))
            for kind, (source, landing) in enumerate(
                ((small_out, small_in), (diagonal_out, diagonal_in))
            )
        ]

    def small_stage(hop):
        if hop > 0:
            for copy in small_copies(hop - 1):
                copy.wait()
            small_out[...] = small_out[...] + small_in[hop - 1]
            diagonal_out[...] = diagonal_out[...] + diagonal_in[hop - 1]
        if hop < len(hop_letters):
            for copy in small_copies(hop):
                copy.start()

    def perform(slot):
        for index, stage in orders[slot]:
            if index == len(chunks):
                small_stage(stage)
            else:
                chunks[index].stage(stage)

    @pl.when(step == 0)
    def _():
        for copy in pair_loads(0) + loads(True):
            copy.start()
        met = set(hop_letters)
        for chunk in chunks:
            for hops in chunk.parts:
                for letters in hops:
                    met.update(subsets(letters))
        place.greet(sorted(met))
        small_out[...] = small_ref[...]

    @pl.when(step == 0)
    def _():
        perform(0)
        for pair in range(1, pairs):
            for copy in pair_loads(pair):
                copy.start()
        for copy in loads(False):
            copy.start()
        static_prepare(meta_ref, static)
        for copy in loads(True):
            copy.wait()
        back_to_attention()
        perform(1)
        back_to_heads()
        for tile in range(rows // TILE):
            there = slice(tile * TILE, tile * TILE + TILE)
            item_t[:, there] = jnp.transpose(item_ref[there].astype(F32)).astype(BF)

    for pair in range(pairs):
        @pl.when(step == pair)
        def _(pair=pair):
            perform(2 + pair)

    for copy in pair_loads(step):
        copy.wait()
    (dq_even, dk_even, dv_even), (dq_odd, dk_odd, dv_odd) = [
        head_back(
            parity, step, rows_ref, wide_refs, k_ref, v_ref, mixed_ref, grad_ref, log_ref,
            static, diagonal_out,
        )
        for parity in range(2)
    ]
    even = own_lanes(0, rows)
    pieces = [
        jnp.transpose(jnp.concatenate([dq_even, dq_odd], axis=0)).astype(BF),
        jnp.where(even, dk_even, dk_odd).astype(BF),
        jnp.where(even, dv_even, dv_odd).astype(BF),
    ]
    for part, piece in enumerate(pieces):
        d_project[:, pl.ds(pl.multiple_of(part * width + step * LANES, LANES), LANES)] = piece
    slab = pl.ds(pl.multiple_of(step * TAIL_ROWS, TAIL_ROWS), width)
    tail[slab] = dot_nn(item_t[...], jnp.concatenate(pieces, axis=1)).astype(BF)

    @pl.when(step == 0)
    def _():
        for copy in loads(False):
            copy.wait()

    @pl.when(step == pairs - 1)
    def _():
        perform(pairs + 2)
        for begin in range(0, width, TILE):
            here = slice(begin, begin + TILE)
            total = d_hidden_ref[:, here] + dot_nt(d_project[...], weight_ref[here])
            input_grad[:, here] = total.astype(BF)
        for copy in input_copies():
            copy.start()
        for begin in range(0, width, TILE):
            here = slice(begin, begin + TILE)
            there = slice(2 * width + begin, 2 * width + begin + TILE)
            small_out[0:1, here] = column_sum(d_project[:, here].astype(F32))
            small_out[1:2, here] = column_sum(d_project[:, there].astype(F32))
        perform(pairs + 3)
        for copy in input_copies():
            copy.wait()


TAIL_ROWS = 1024


def out_spot(pair, pairs, width):
    down = TAIL_ROWS - width
    across = width * width // (pairs * down)
    per_row = width // across
    return (
        pl.ds(pair // per_row * down, down),
        pl.ds(pair % per_row * across, across),
    )


def summed_with_attention_back(
    meta_columns, meta_rows, projected, mixed, logs, wide_arrays, item, qkv_weight,
    total, unit, scale, out_weight, attn_gain, small, grad_down, grad_up,
):
    size = lax.axis_size("dp")
    depth = 4 if size % 16 == 0 else size // 4
    rows, width = item.shape
    pairs = width // LANES
    hidden = grad_down.shape[0]
    hops = len(letters_of(depth)) + 1
    work = [5.0, 4.0] + [6.5] * pairs + [4.0]
    tall, wide, slim = 1024, 3 * LANES, 2 * LANES
    plan = [
        (0, 0, 2 * tall, 0, width, 0, "a.b.x.y x.y.a.b", 1),
        (0, 2 * tall, tall, 0, width, 0, "x.a.y.b y.a.b.x", 2),
        (1, 0, 3 * tall, 0, slim, 0, "a.b.x.y y.x.a.b", 4),
        (1, 0, 3 * tall, slim, slim, 0, "y.a.x.b x.y.a.b", 0),
        (1, 0, 3 * tall, 2 * slim, slim, 0, "x.y.a.b y.x.a.b", 2),
        (2, 0, tall, 0, wide, 3, "y.x.a.b a.b.x.y", 3),
        (2, tall, tall, 0, wide, 4, "xy.a.b", 2),
        (2, 2 * tall, tall, 0, wide, 5, "x.y.ab y.ab.x", 3),
        (2, 3 * tall, tall, 0, wide, 6, "xy.a.b", 1),
        (2, 4 * tall, tall, 0, wide, 7, "xy.a.b", 1),
        (2, 5 * tall, tall, 0, wide, 8, "ab.y.x y.ab.x", 2),
    ]
    orders = planned([(spot[2],) + spot[4:] for spot in plan], work, depth, hops)

    whole = pl.BlockSpec(memory_space=pltpu.VMEM)
    diagonals = jax.ShapeDtypeStruct((2 * pairs, 8, LANES), F32)
    dma = pltpu.SemaphoreType.DMA
    scratch = []
    for spot in plan:
        scratch.append(chunk_scratch(spot, depth))
    main, tail, small, diagonals, grad_input = pl.pallas_call(
        functools.partial(last_kernel, depth, plan, orders, [len(pieces) for pieces in scratch]),
        grid=(pairs,),
        in_specs=[whole] * 2 + [HBM] * 2 + [whole] + [HBM] * 4 + [whole] * 2 + [HBM] * 8,
        out_specs=[HBM, HBM, whole, whole, HBM],
        out_shape=[
            jax.ShapeDtypeStruct((2 * hidden, width), BF),
            jax.ShapeDtypeStruct((pairs * TAIL_ROWS, 3 * LANES), BF),
            jax.ShapeDtypeStruct(small.shape, F32),
            diagonals,
            jax.ShapeDtypeStruct((2, rows // 2, width), BF),
        ],
        scratch_shapes=[pltpu.VMEM((rows, LANES), BF)] * 3
        + [pltpu.VMEM((LANES, rows), BF)] * 3
        + [pltpu.VMEM((pairs, rows, LANES), kind) for kind in (BF, BF, F32, BF)]
        + [pltpu.VMEM(array.shape, BF) for array in wide_arrays]
        + [
            dma((pairs, 6)),
            pltpu.VMEM((rows, width), BF),
            pltpu.VMEM((width, 3 * width), BF),
            pltpu.VMEM((rows, width), F32),
            pltpu.VMEM((rows, width), F32),
            pltpu.VMEM((rows, LANES), F32),
            dma((2, 5 + pairs)),
            pltpu.VMEM((rows, 3 * width), BF),
            pltpu.VMEM((width, rows), BF),
            pltpu.VMEM((pairs * TAIL_ROWS, 3 * LANES), BF),
            pltpu.VMEM((rows, width), BF),
            pltpu.VMEM((hops,) + small.shape, F32),
            pltpu.VMEM((hops,) + diagonals.shape, F32),
            dma((2, 2, hops)),
            dma((3,)),
        ]
        + [piece for pieces in scratch for piece in pieces],
        compiler_params=pltpu.CompilerParams(
            collective_id=0, has_side_effects=True, vmem_limit_bytes=62 * MIB
        ),
        name="summed_with_attention_back",
    )(meta_columns, meta_rows, projected, mixed, logs, *wide_arrays,
      small, attn_gain, item, qkv_weight, total, unit, scale, out_weight, grad_down, grad_up)
    span = 4 * depth
    if size > span:
        groups = [list(range(first, size, span)) for first in range(span)]
        main, tail, small, diagonals = lax.psum(
            (main.astype(F32), tail.astype(F32), small, diagonals), "dp",
            axis_index_groups=groups,
        )
        main, tail = main.astype(BF), tail.astype(BF)
    return main, tail, small, diagonals, grad_input


def per_device(
    layer_in, segment, key_mask, position, layout_x, layout_y,
    qkv_weight, query_bias, value_bias, out_weight, out_bias, attn_gain, attn_shift,
    up_weight, up_bias, down_weight, down_bias, ffn_gain, ffn_shift,
    text_table, horiz_table, vert_table, cotangent,
):
    width = layer_in.shape[-1]
    item, projected, meta_columns, meta_rows, table_rows = projected_item(
        layer_in, (segment, key_mask, position, layout_x, layout_y),
        qkv_weight, query_bias, value_bias, (text_table, horiz_table, vert_table),
    )
    mixed, logs, *wide_arrays = attention_forward(meta_columns, meta_rows, table_rows, projected, width)
    layer_out, total, unit, scale, grad_down, grad_up, small = fed_forward_and_back(
        item, mixed, cotangent, out_weight, up_weight, down_weight,
        (out_bias, attn_gain, attn_shift, up_bias, down_bias, ffn_gain, ffn_shift),
    )
    main, tail, small, diagonals, grad_input = summed_with_attention_back(
        meta_columns, meta_rows, projected, mixed, logs, wide_arrays, item, qkv_weight,
        total, unit, scale, out_weight, attn_gain, small, grad_down, grad_up,
    )
    done = finished(
        main, tail, grad_input, small, diagonals, up_weight.shape[1], text_table.shape[0]
    )
    sum_down, sum_up, sum_out, sum_qkv, grad_input = done[:5]
    singles, tables = done[5:14], [t.T for t in done[14:]]
    return (
        layer_out, grad_input, sum_qkv, singles[0], singles[1], sum_out, singles[2], singles[3],
        singles[4], sum_up, singles[8], sum_down, singles[5], singles[6], singles[7],
        tables[0], tables[1], tables[2],
    )


def solution(mesh):
    rows = P("dp", "seq", None)
    marks_spec = P("dp", "seq")
    return jax.shard_map(
        per_device,
        mesh=mesh,
        in_specs=(rows,) + (marks_spec,) * 5 + (P(),) * 16 + (rows,),
        out_specs=(rows, rows) + (P(),) * 16,
        check_vma=False,
    )
```

```python
import functools

import jax
import jax.numpy as jnp
from jax import lax
from jax.experimental import pallas as pl
from jax.experimental.pallas import tpu as pltpu
from jax.sharding import PartitionSpec as P

BF = jnp.bfloat16
F32 = jnp.float32
BIG = 1e30
LANES = 128
HEAD = 64
TEXT = 512
POS = 64
COORD = 48
Y0 = 64
GROUP0 = 112
MEMBER0 = 116
FLAG = 124
EVERY = 125
STRAY = 126
X_TABLE = 33
Y_TABLE = 66
NOTHING = 127


def dot_nt(a, b):
    return lax.dot_general(a, b, (((1,), (1,)), ((), ())), preferred_element_type=F32)


def dot_nn(a, b):
    return lax.dot_general(a, b, (((1,), (0,)), ((), ())), preferred_element_type=F32)


def looked_up(table_row, index):
    rows = index.shape[0]
    return jnp.take_along_axis(
        jnp.broadcast_to(table_row, (rows, LANES)), index, axis=1, mode="promise_in_bounds"
    )


def bucket(distance):
    return jnp.clip(distance, -16, 16) + 16


def between(lane, low, high):
    return (lane >= low) & (lane < high)


def columns_of(meta_ref):
    return tuple(meta_ref[:, field : field + 1] for field in range(5))


def marks(meta_ref):
    segment, key_mask, position, across, down = columns_of(meta_ref)
    rows = segment.shape[0]
    lane = lax.broadcasted_iota(jnp.int32, (rows, LANES), 1)
    row = lax.broadcasted_iota(jnp.int32, (rows, LANES), 0)
    even = between(lane, HEAD, HEAD + COORD) & (lane - HEAD == across)
    odd = (lane < COORD) & (lane == across)
    group = (segment - 1) >> 3
    member = (segment - 1) & 7
    named = segment > 0
    shared = (
        ((row < TEXT) & (lane < POS) & (lane == position))
        | (between(lane, Y0, Y0 + COORD) & (lane - Y0 == down))
        | (named & between(lane, GROUP0, MEMBER0) & (lane - GROUP0 == group))
        | (named & between(lane, MEMBER0, FLAG) & (lane - MEMBER0 == member))
        | ((lane == FLAG) & (key_mask <= 0))
        | (lane == EVERY)
        | ((lane == STRAY) & (segment < 0))
    )
    return tuple(jnp.where(m, 1.0, 0.0).astype(BF) for m in (even, odd, shared))


def square_lanes():
    shape = (LANES, LANES)
    return lax.broadcasted_iota(jnp.int32, shape, 0), lax.broadcasted_iota(jnp.int32, shape, 1)


def barred():
    row, lane = square_lanes()
    in_groups = between(lane, GROUP0, MEMBER0)
    shut = (
        (between(row, GROUP0, MEMBER0) & in_groups & (lane != row))
        | (between(row, MEMBER0, FLAG) & between(lane, MEMBER0, FLAG) & (lane != row))
        | ((row == EVERY) & (lane == FLAG))
        | ((row == STRAY) & in_groups)
    )
    return jnp.where(shut, -BIG, 0.0).astype(F32)


def table_index():
    row, lane = square_lanes()
    distance = bucket(row - lane)
    inside = lambda low, high: between(row, low, high) & between(lane, low, high)
    even = jnp.where(inside(HEAD, HEAD + COORD), distance + X_TABLE, NOTHING)
    odd = jnp.where(inside(0, COORD), distance + X_TABLE, NOTHING)
    shared = jnp.where(
        inside(0, POS), distance, jnp.where(inside(Y0, Y0 + COORD), distance + Y_TABLE, NOTHING)
    )
    return even, odd, shared


def image_query_index(meta_ref):
    position = meta_ref[TEXT:, 2:3]
    lane = lax.broadcasted_iota(jnp.int32, (position.shape[0], LANES), 1)
    return jnp.where(lane < POS, bucket(position - lane), NOTHING)


def prepare(meta_ref, mark_refs, bar_ref, index_refs, image_index_ref):
    for ref, value in zip(mark_refs, marks(meta_ref)):
        ref[...] = value
    bar_ref[...] = barred()
    for ref, value in zip(index_refs, table_index()):
        ref[...] = value
    image_index_ref[...] = image_query_index(meta_ref)


def own_lanes(parity, rows):
    lane = lax.broadcasted_iota(jnp.int32, (rows, LANES), 1)
    return (lane < HEAD) if parity == 0 else (lane >= HEAD)


def widened(parity, q, table_row, bias, bar_ref, index_refs, image_index_ref, mark_refs):
    rows = q.shape[0]
    shared = mark_refs[2][...]
    across = looked_up(table_row, index_refs[parity][...]).astype(BF)
    first = jnp.where(
        own_lanes(parity, rows), q.astype(F32) * 0.125, dot_nn(mark_refs[parity][...], across)
    )
    others = (looked_up(table_row, index_refs[2][...]) + bar_ref[...]).astype(BF)
    second = dot_nn(shared, others)
    on_images = looked_up(table_row, image_index_ref[...])
    second = jnp.concatenate([second[:TEXT], second[TEXT:] + on_images], axis=0)
    image_lane = lax.broadcasted_iota(jnp.int32, on_images.shape, 1)
    key_image = jnp.where(image_lane < POS, bias[:, :LANES].astype(BF), shared[TEXT:])
    return first.astype(BF), second.astype(BF), key_image


def joined(parity, first, second, key_image, k, marks_own, shared):
    rows = k.shape[0]
    lane = lax.broadcasted_iota(jnp.int32, (rows, LANES), 1)
    to_image = jnp.where(lane < POS, shared, second)
    key_first = jnp.where(own_lanes(parity, rows), k, marks_own)
    q_text = jnp.concatenate([first, second], axis=1)
    q_image = jnp.concatenate([first, to_image], axis=1)
    k_text = jnp.concatenate([key_first[:TEXT], shared[:TEXT]], axis=1)
    k_image = jnp.concatenate([key_first[TEXT:], key_image], axis=1)
    return q_text, q_image, k_text, k_image


def near(start, size):
    if start >= TEXT:
        return slice(0, TEXT)
    return slice(max(0, start - LANES), min(TEXT, start + size + LANES))


def image_bias(table_row, offsets):
    return jnp.concatenate(
        [looked_up(table_row, offsets[:, :LANES]), looked_up(table_row, offsets[:, LANES:])], axis=1
    )


def forward_kernel(
    meta_ref, rows_ref, table_ref, q_ref, k_ref, v_ref,
    mixed_ref, log_ref, first_ref, second_ref, key_image_ref, bias_ref,
    even_ref, odd_ref, shared_ref, bar_ref, index_even, index_odd, index_shared, image_index_ref,
):
    mark_refs = (even_ref, odd_ref, shared_ref)
    index_refs = (index_even, index_odd, index_shared)

    @pl.when(pl.program_id(0) == 0)
    def _():
        prepare(meta_ref, mark_refs, bar_ref, index_refs, image_index_ref)

    rows = q_ref.shape[0]
    images = rows - TEXT
    q, k, v = q_ref[...], k_ref[...], v_ref[...]
    offsets = bucket(rows_ref[2:3, TEXT:] - meta_ref[TEXT:, 2:3])
    tile = 256
    v_turned = transposed(v)
    heads = [None, None]

    def prepared(parity):
        table_row = table_ref[pl.ds(2 * pl.program_id(0) + parity, 1), :]
        bias = image_bias(table_row, offsets)
        first, second, key_image = widened(
            parity, q, table_row, bias, bar_ref, index_refs, image_index_ref, mark_refs
        )
        first_ref[parity] = first
        second_ref[parity] = second
        key_image_ref[parity] = key_image
        bias_ref[parity] = bias.astype(BF)
        wide = joined(
            parity, first, second, key_image, k, mark_refs[parity][...], shared_ref[...]
        )
        heads[parity] = wide + (bias,)

    def scored(parity, start):
        q_text, q_image, k_text, k_image, bias = heads[parity]
        here = slice(start, start + tile)
        on_image = dot_nt(k_image, q_image[here])
        if start >= TEXT:
            on_image = on_image + bias[:, start - TEXT : start - TEXT + tile]
        return dot_nt(k_text[near(start, tile)], q_text[here]), on_image

    spots = [(parity, start) for parity in range(2) for start in range(0, rows, tile)]
    outs = ([], [])
    prepared(0)
    following = scored(*spots[0])
    for index, (parity, start) in enumerate(spots):
        on_text, on_image = following
        if index == 1:
            prepared(1)
        if index + 1 < len(spots):
            following = scored(*spots[index + 1])
        top = jnp.maximum(
            jnp.max(on_text, axis=0, keepdims=True), jnp.max(on_image, axis=0, keepdims=True)
        )
        on_text = jnp.exp(on_text - top)
        on_image = jnp.exp(on_image - top)
        total = jnp.sum(on_text, axis=0, keepdims=True) + jnp.sum(on_image, axis=0, keepdims=True)
        own = slice(parity * HEAD, parity * HEAD + HEAD)
        out = dot_nn(v_turned[own, near(start, tile)], on_text.astype(BF)) + dot_nn(
            v_turned[own, TEXT:], on_image.astype(BF)
        )
        outs[parity].append(out * (1.0 / total))
        log_ref[0, parity : parity + 1, start : start + tile] = top + jnp.log(total)
    mixed_ref[...] = jnp.transpose(
        jnp.concatenate([jnp.concatenate(outs[parity], axis=1) for parity in range(2)], axis=0)
    )


def static_scratch(rows):
    square = (LANES, LANES)
    return [
        pltpu.VMEM((rows, LANES), BF),
        pltpu.VMEM((rows, LANES), BF),
        pltpu.VMEM((rows, LANES), BF),
        pltpu.VMEM(square, F32),
        pltpu.VMEM(square, jnp.int32),
        pltpu.VMEM(square, jnp.int32),
        pltpu.VMEM(square, jnp.int32),
        pltpu.VMEM((rows - TEXT, LANES), jnp.int32),
    ]


def attention_forward(meta_columns, meta_rows, table_rows, projected, width):
    rows = projected.shape[0]
    images = rows - TEXT
    pairs = width // LANES

    def block(part):
        return pl.BlockSpec((rows, LANES), lambda p: (0, part * pairs + p))

    whole = lambda shape: pl.BlockSpec(shape, lambda p: (0,) * len(shape))
    return pl.pallas_call(
        forward_kernel,
        grid=(pairs,),
        in_specs=[
            whole(meta_columns.shape),
            whole(meta_rows.shape),
            whole(table_rows.shape),
            block(0), block(1), block(2),
        ],
        out_specs=[
            pl.BlockSpec((rows, LANES), lambda p: (0, p)),
            pl.BlockSpec((1, 2, rows), lambda p: (p, 0, 0)),
            pl.BlockSpec((2, rows, LANES), lambda p: (p, 0, 0)),
            pl.BlockSpec((2, rows, LANES), lambda p: (p, 0, 0)),
            pl.BlockSpec((2, images, LANES), lambda p: (p, 0, 0)),
            pl.BlockSpec((2, images, images), lambda p: (p, 0, 0)),
        ],
        out_shape=[
            jax.ShapeDtypeStruct((rows, width), F32),
            jax.ShapeDtypeStruct((pairs, 2, rows), F32),
            jax.ShapeDtypeStruct((2 * pairs, rows, LANES), BF),
            jax.ShapeDtypeStruct((2 * pairs, rows, LANES), BF),
            jax.ShapeDtypeStruct((2 * pairs, images, LANES), BF),
            jax.ShapeDtypeStruct((2 * pairs, images, images), BF),
        ],
        scratch_shapes=static_scratch(rows),
        compiler_params=pltpu.CompilerParams(vmem_limit_bytes=60 * 1024 * 1024),
        name="attention_forward",
    )(meta_columns, meta_rows, table_rows, projected, projected, projected)


def skewed(block):
    size = block.shape[0]
    lane = lax.broadcasted_iota(jnp.int32, (size, LANES), 1)
    row = lax.broadcasted_iota(jnp.int32, (size, LANES), 0)
    turned = jnp.take_along_axis(
        block, (lane + row) & (LANES - 1), axis=1, mode="promise_in_bounds"
    )
    straight = lane + row < LANES
    above = jnp.sum(jnp.where(straight, turned, 0.0), axis=0, keepdims=True)
    below = jnp.sum(jnp.where(straight, 0.0, turned), axis=0, keepdims=True)
    return above, below


def transposed(array):
    return jnp.transpose(array.astype(F32)).astype(array.dtype)


def static_prepare(meta_ref, static):
    for ref, turned, value in zip(static[:3], static[3:], marks(meta_ref)):
        ref[...] = value
        turned[...] = transposed(value)


def head_back(
    parity, pair, rows_ref, wide_refs, k_ref, v_ref, mixed_ref, grad_ref, log_ref, static, diag_ref,
):
    mark_refs, turned_refs = static[:3], static[3:]
    first_ref, second_ref, key_image_ref, bias_ref = wide_refs
    head = 2 * pair + parity
    shared_t = turned_refs[2]
    rows = k_ref.shape[1]
    images = rows - TEXT
    tile = 256
    k, v, grad = k_ref[pair], v_ref[pair], grad_ref[pair]
    products = grad.astype(F32) * mixed_ref[pair]
    k_turned = transposed(k)
    is_image = rows_ref[1:2, TEXT:] > 0
    own = own_lanes(parity, rows)
    log_row = log_ref[pair, parity : parity + 1, :]
    first, shared = first_ref[head], mark_refs[2][...]
    q_text, q_image, k_text, k_image = joined(
        parity, first, second_ref[head], key_image_ref[head], k, mark_refs[parity][...], shared
    )
    bias = bias_ref[head].astype(F32)
    ones = jnp.where(own_lanes(parity, 8), 1.0, 0.0).astype(BF)
    delta = jnp.zeros((8, rows), F32)
    rest = products
    for _ in range(3):
        piece = rest.astype(BF)
        delta = delta + dot_nt(ones, piece)
        rest = rest - piece.astype(F32)
    delta = delta[0:1]
    v_own = jnp.where(own, v, jnp.zeros_like(v))
    q_marked = jnp.concatenate(
        [jnp.where(own, first, mark_refs[parity][...]), shared], axis=1
    )
    dq_text = jnp.zeros((HEAD, TEXT), F32)
    dq_image = jnp.zeros((HEAD, images), F32)
    dks = []
    dvs = []
    first_sum = jnp.zeros((LANES, LANES), F32)
    second_sum = jnp.zeros((LANES, LANES), F32)
    text_image = jnp.zeros((LANES, images), F32)

    def met(start, array, axis=0):
        text = near(start, tile)
        if axis == 0:
            return jnp.concatenate([array[text], array[TEXT:]], axis=0)
        return jnp.concatenate([array[:, text], array[:, TEXT:]], axis=1)

    def scored(start):
        here = slice(start, start + tile)
        if start < TEXT:
            scores = dot_nt(k_text[here], met(start, q_text))
        else:
            scores = dot_nt(k_image[start - TEXT : start - TEXT + tile], q_image)
            scores = jnp.concatenate([scores[:, :TEXT], scores[:, TEXT:] + bias], axis=1)
        return scores, dot_nt(v_own[here], met(start, grad))

    following = scored(0)
    for start in range(0, rows, tile):
        here = slice(start, start + tile)
        scores, prob_grad = following
        if start + tile < rows:
            following = scored(start + tile)
        soft = jnp.exp(scores - met(start, log_row, 1))
        score_grad = soft * (prob_grad - met(start, delta, 1))
        low = score_grad.astype(BF)
        dvs.append(dot_nn(soft.astype(BF), met(start, grad)))
        wide = dot_nn(low, met(start, q_marked))
        dks.append(wide[:, :LANES])
        part = dot_nn(k_turned[parity * HEAD : parity * HEAD + HEAD, here], low)
        text = near(start, tile)
        count = text.stop - text.start
        before = [jnp.zeros((HEAD, text.start), F32)] if text.start > 0 else []
        after = [jnp.zeros((HEAD, TEXT - text.stop), F32)] if text.stop < TEXT else []
        dq_text = dq_text + jnp.concatenate(before + [part[:, :count]] + after, axis=1)
        dq_image = dq_image + part[:, count:]
        rounded = wide.astype(BF)
        first_sum = first_sum + dot_nn(turned_refs[parity][:, here], rounded[:, :LANES])
        second_sum = second_sum + dot_nn(shared_t[:, here], rounded[:, LANES:])
        if start < TEXT:
            text_image = text_image + dot_nn(shared_t[:, here], low[:, count:])
        else:
            by_position = wide[:, LANES:]
            on_image = score_grad[:, TEXT:]
    dq = jnp.concatenate([dq_text, dq_image], axis=1)
    small = lax.broadcasted_iota(jnp.int32, (LANES, LANES), 1)
    small_row = lax.broadcasted_iota(jnp.int32, (LANES, LANES), 0)
    x0 = HEAD if parity == 0 else 0
    x_block = jnp.where(
        between(small, x0, x0 + COORD) & between(small_row, x0, x0 + COORD), first_sum, 0.0
    )
    y_block = jnp.where(
        between(small, Y0, Y0 + COORD) & between(small_row, Y0, Y0 + COORD), second_sum, 0.0
    )
    p_block = jnp.where((small < POS) & (small_row < POS), second_sum, 0.0)
    wide_lane = lax.broadcasted_iota(jnp.int32, (images, images), 1)
    outside = jnp.sum(jnp.where(is_image, 0.0, on_image), axis=1, keepdims=True)
    pairs = jnp.where(is_image, on_image, 0.0) + jnp.where(wide_lane == 0, outside, 0.0)
    outside_text = jnp.sum(jnp.where(is_image, 0.0, text_image), axis=1, keepdims=True)
    text_lane = lax.broadcasted_iota(jnp.int32, (LANES, images), 1)
    text_row = lax.broadcasted_iota(jnp.int32, (LANES, images), 0)
    text_image = jnp.where(is_image, text_image, 0.0) + jnp.where(
        text_lane == 0, outside_text, 0.0
    )
    text_image = jnp.where(text_row < POS, text_image, 0.0)
    first_lane = lax.broadcasted_iota(jnp.int32, (images, LANES), 1)
    left = pairs[:, :LANES] + jnp.where(first_lane < POS, by_position, 0.0)
    right = pairs[:, LANES:]
    a00, b00 = skewed(left[:LANES] + text_image[:, :LANES] + p_block)
    a01, b01 = skewed(right[:LANES] + text_image[:, LANES:])
    a10, b10 = skewed(left[LANES:])
    a11, b11 = skewed(right[LANES:])
    ax, bx = skewed(x_block)
    ay, by = skewed(y_block)
    diag_ref[head] = jnp.concatenate(
        [b10, b00 + b11 + a10, a00 + a11 + b01, a01, bx, ax, by, ay], axis=0
    )
    return dq * 0.125, jnp.concatenate(dks, axis=0), jnp.concatenate(dvs, axis=0)


MESH = pl.DeviceIdType.MESH
VMEM = pl.BlockSpec(memory_space=pltpu.VMEM)
HBM = pl.BlockSpec(memory_space=pltpu.HBM)
MIB = 1024 * 1024


def remote(src, dst, send, receive, device):
    return pltpu.make_async_remote_copy(
        src_ref=src, dst_ref=dst, send_sem=send, recv_sem=receive, device_id=device,
        device_id_type=MESH,
    )


def project_kernel(
    layer_ref, weight_hbm, *refs,
):
    small_hbm, refs = refs[:10], refs[10:]
    (item_ref, projected_out, columns_ref, rows_ref, table_ref,
     projected_ref, weight_ref, meta_send, bias_ref, sems, load_sems, store_sems), small = (
        refs[:12], refs[12:],
    )
    (segment_ref, mask_ref, position_ref, across_ref, down_ref, query_bias_ref, value_bias_ref,
     text_ref, horiz_ref, vert_ref) = small
    mine = lax.axis_index("seq")
    partner = (1 - mine, lax.axis_index("dp"))
    count, width = layer_ref.shape[1:]
    own = pl.ds(pl.multiple_of(mine * count, LANES), count)
    loads = [
        pltpu.make_async_copy(source, target, load_sems.at[index])
        for index, (source, target) in enumerate(
            list(zip(small_hbm, small))
            + [(layer_ref.at[mine], item_ref.at[own]), (weight_hbm, weight_ref)]
        )
    ]
    for load in loads:
        load.start()
    barrier = pltpu.get_barrier_semaphore()
    pl.semaphore_signal(barrier, inc=1, device_id=partner, device_id_type=MESH)
    pl.semaphore_wait(barrier, 1)
    pieces = count // LANES
    rows_out = [
        remote(
            layer_ref.at[1 - mine, pl.ds(piece * LANES, LANES)],
            item_ref.at[pl.ds(pl.multiple_of(mine * count + piece * LANES, LANES), LANES)],
            sems.at[0, piece], sems.at[1, piece], partner,
        )
        for piece in range(pieces)
    ]
    for copy in rows_out:
        copy.start()
    for load in loads[:-2]:
        load.wait()

    fields = (segment_ref, mask_ref, position_ref, across_ref, down_ref)
    blocks = [
        jnp.concatenate(
            [field[item : item + 1, :] for field in fields] + [jnp.zeros((3, count), jnp.int32)],
            axis=0,
        )
        for item in range(2)
    ]
    meta_send[...] = jnp.where(mine == 0, blocks[1], blocks[0])
    meta_out = remote(
        meta_send, rows_ref.at[:, own], sems.at[0, pieces], sems.at[1, pieces], partner
    )
    meta_out.start()
    rows_ref[:, own] = jnp.where(mine == 0, blocks[0], blocks[1])
    bias_ref[:, :width] = query_bias_ref[...].astype(F32).reshape(1, width)
    bias_ref[:, width : 2 * width] = jnp.zeros((1, width), F32)
    bias_ref[:, 2 * width :] = value_bias_ref[...].astype(F32).reshape(1, width)
    heads, levels = text_ref.shape
    spot = lax.broadcasted_iota(jnp.int32, (levels, LANES), 1)
    level = lax.broadcasted_iota(jnp.int32, (levels, LANES), 0)
    table = jnp.zeros((heads, LANES), F32)
    for source, begin in ((text_ref, 0), (horiz_ref, X_TABLE), (vert_ref, Y_TABLE)):
        table = table + dot_nn(source[...], (spot == level + begin).astype(BF))
    table_ref[...] = jnp.concatenate([table, jnp.zeros((16 - heads, LANES), F32)], axis=0)

    def project(there):
        step = 256

        def body(index, carry):
            columns = pl.ds(pl.multiple_of(index * step, step), step)
            product = dot_nn(item_ref[there], weight_ref[:, columns])
            projected_ref[there, columns] = (product + bias_ref[:, columns]).astype(BF)
            return carry

        lax.fori_loop(0, 3 * width // step, body, 0)

    def stored(index, there):
        return pltpu.make_async_copy(
            projected_ref.at[there], projected_out.at[there], store_sems.at[index]
        )

    for load in loads[-2:]:
        load.wait()
    project(own)
    stored(0, own).start()
    for piece in range(pieces):
        rows_out[piece].wait()
        there = pl.ds(pl.multiple_of((1 - mine) * count + piece * LANES, LANES), LANES)
        project(there)
        stored(1 + piece, there).start()
    meta_out.wait()
    meta = rows_ref[...].astype(F32)
    tall = jnp.concatenate([meta, jnp.zeros((LANES - 8, meta.shape[1]), F32)], axis=0)
    columns_ref[...] = jnp.transpose(tall).astype(jnp.int32)
    stored(0, own).wait()
    for piece in range(pieces):
        there = pl.ds(pl.multiple_of((1 - mine) * count + piece * LANES, LANES), LANES)
        stored(1 + piece, there).wait()


def projected_item(layer_in, fields, qkv_weight, query_bias, value_bias, tables):
    rows = 2 * layer_in.shape[1]
    width = layer_in.shape[2]
    pieces = rows // 2 // LANES
    small = list(fields) + [query_bias, value_bias] + [t.T for t in tables]
    return pl.pallas_call(
        project_kernel,
        in_specs=[HBM] * (2 + len(small)),
        out_specs=[VMEM, HBM, VMEM, VMEM, VMEM],
        out_shape=[
            jax.ShapeDtypeStruct((rows, width), BF),
            jax.ShapeDtypeStruct((rows, 3 * width), BF),
            jax.ShapeDtypeStruct((rows, LANES), jnp.int32),
            jax.ShapeDtypeStruct((8, rows), jnp.int32),
            jax.ShapeDtypeStruct((16, LANES), F32),
        ],
        scratch_shapes=[
            pltpu.VMEM((rows, 3 * width), BF),
            pltpu.VMEM((width, 3 * width), BF),
            pltpu.VMEM((8, rows // 2), jnp.int32),
            pltpu.VMEM((1, 3 * width), F32),
            pltpu.SemaphoreType.DMA((2, pieces + 1)),
            pltpu.SemaphoreType.DMA((len(small) + 2,)),
            pltpu.SemaphoreType.DMA((pieces + 1,)),
        ]
        + [pltpu.VMEM(array.shape, array.dtype) for array in small],
        compiler_params=pltpu.CompilerParams(
            collective_id=1, has_side_effects=True, vmem_limit_bytes=60 * MIB
        ),
        name="projected_item",
    )(layer_in, qkv_weight, *small)


EPSILON = 1e-05
TILE = 256


def vector(ref):
    return ref[...].astype(F32).reshape(1, ref.shape[0])


def gelu_and_slope(x):
    bell = jnp.exp2(-0.7213475204444817 * (x * x))
    rough = 1.0 + 0.23164188826 * jnp.abs(x)
    t = pl.reciprocal(rough, approx=True)
    t = t * (2.0 - rough * t)
    series = t * (
        0.127414796
        + t * (-0.142248368 + t * (0.7107068705 + t * (-0.7265760135 + t * 0.5307027145)))
    )
    tail = bell * series
    below = jnp.where(x >= 0.0, 1.0 - tail, tail)
    return x * below, below + x * (0.3989422804014327 * bell)


def row_mean(block):
    return jnp.mean(block, axis=1, keepdims=True)


def normalized(hidden):
    center = hidden - row_mean(hidden)
    scale = lax.rsqrt(row_mean(center * center) + EPSILON)
    return center * scale, scale


def norm_pulled(grad, unit, scale):
    return scale * (grad - row_mean(grad) - unit * row_mean(grad * unit))


def column_sum(block):
    return jnp.sum(block, axis=0, keepdims=True)


def feed_kernel(
    item_hbm, mixed_hbm, cotangent_ref, out_weight_ref, up_ref, down_ref, *refs,
):
    vectors_hbm, refs = refs[:7], refs[7:]
    (layer_out, total_out, unit_out, scale_out, grad_down_ref, grad_up_ref, small_ref,
     item_ref, mixed_ref, layer_ref, cotangent_all, active, slope, unit, scale_ref, normed, normed_t, total, d_branch, d_branch_t,
     sems, load_sems, tile_sems, store_sems) = refs[:24]
    vectors = refs[24:]
    (out_bias_ref, attn_gain_ref, attn_shift_ref, up_bias_ref, down_bias_ref, ffn_gain_ref,
     ffn_shift_ref) = vectors
    step = pl.program_id(0)
    blocks = pl.num_programs(0) // 2
    rows, width = item_hbm.shape
    count = rows // 2
    mine = lax.axis_index("seq")
    partner = (1 - mine, lax.axis_index("dp"))
    own = pl.ds(pl.multiple_of(mine * count, LANES), count)
    tiles = rows // TILE

    def sent():
        return remote(
            cotangent_ref.at[1 - mine], cotangent_all.at[own], sems.at[0], sems.at[1], partner
        )

    def returned():
        theirs = pl.ds(pl.multiple_of((1 - mine) * count, LANES), count)
        return [
            pltpu.make_async_copy(layer_ref.at[own], layer_out.at[mine], load_sems.at[8]),
            remote(
                layer_ref.at[theirs], layer_out.at[mine], sems.at[2], sems.at[3], partner
            ),
        ]

    def tile_loads(tile):
        there = pl.ds(tile * TILE, TILE)
        return [
            pltpu.make_async_copy(source.at[there], target.at[there], tile_sems.at[index, tile])
            for index, (source, target) in enumerate(
                ((mixed_hbm, mixed_ref), (item_hbm, item_ref))
            )
        ]

    def store(index):
        source, target = (
            (total, total_out), (unit, unit_out), (scale_ref, scale_out),
        )[index]
        return pltpu.make_async_copy(source, target, store_sems.at[index])

    def loads():
        copies = list(zip(vectors_hbm, vectors)) + [(cotangent_ref.at[mine], cotangent_all.at[own])]
        return [
            pltpu.make_async_copy(source, target, load_sems.at[index])
            for index, (source, target) in enumerate(copies)
        ]

    def over_tiles(size, body, carry, unroll=1):
        def run(index, state):
            return body(pl.ds(pl.multiple_of(index * size, size), size), state)

        return lax.fori_loop(0, rows // size, run, carry, unroll=unroll)

    @pl.when(step == 0)
    def _():
        for index in range(rows // TILE):
            for load in tile_loads(index):
                load.start()
        for load in loads():
            load.start()
        barrier = pltpu.get_barrier_semaphore()
        pl.semaphore_signal(barrier, inc=1, device_id=partner, device_id_type=MESH)
        pl.semaphore_wait(barrier, 1)
        sent().start()
        small_ref[...] = jnp.zeros_like(small_ref)
        for load in loads():
            load.wait()
        out_bias, gain, shift = vector(out_bias_ref), vector(attn_gain_ref), vector(attn_shift_ref)

        for index in range(rows // TILE):
            for load in tile_loads(index):
                load.wait()
            there = slice(index * TILE, index * TILE + TILE)
            attn = dot_nn(mixed_ref[there].astype(BF), out_weight_ref[...]) + out_bias
            standard, scale = normalized(item_ref[there].astype(F32) + attn)
            unit[there] = standard
            scale_ref[there] = jnp.broadcast_to(scale, (TILE, LANES))
            result = standard * gain + shift
            normed[there] = result.astype(BF)
            normed_t[:, there] = jnp.transpose(result).astype(BF)
        store(1).start()
        store(2).start()
        total[...] = jnp.zeros_like(total)

    @pl.when(step < blocks)
    def _():
        columns = [slice(begin, begin + TILE) for begin in range(0, width, TILE)]
        low = normed[...]
        following = dot_nn(low, up_ref[:, columns[0]])
        values = []
        early = None
        for index, here in enumerate(columns):
            product = following
            if index + 1 < len(columns):
                following = dot_nn(low, up_ref[:, columns[index + 1]])
            else:
                ahead = jnp.concatenate(values, axis=1)
                early = [dot_nn(ahead, down_ref[: here.start, there]) for there in columns]
            bias = up_bias_ref[pl.ds(pl.multiple_of(step * width + here.start, LANES), TILE)]
            value, grade = gelu_and_slope(product + bias.astype(F32).reshape(1, TILE))
            values.append(value.astype(BF))
            active[step, :, here] = values[-1]
            slope[step, :, here] = grade.astype(BF)
        for part, there in zip(early, columns):
            total[:, there] += part + dot_nn(values[-1], down_ref[columns[-1], there])

    @pl.when(step == blocks)
    def _():
        sent().wait()
        gain, shift, bias = vector(ffn_gain_ref), vector(ffn_shift_ref), vector(down_bias_ref)
        first_gain, first_shift = vector(attn_gain_ref), vector(attn_shift_ref)

        def tile(there, sums):
            hidden = unit[there] * first_gain + first_shift + (total[there] + bias)
            standard, scale = normalized(hidden)
            layer_ref[there] = (standard * gain + shift).astype(BF)
            cotangent = cotangent_all[there].astype(F32)
            pulled = norm_pulled(cotangent * gain, standard, scale)
            total[there] = pulled
            low = pulled.astype(BF)
            d_branch[there] = low
            return (
                sums[0] + column_sum(low.astype(F32)),
                sums[1] + column_sum(cotangent * standard),
                sums[2] + column_sum(cotangent),
            )

        zero = jnp.zeros((1, width), F32)
        sums = over_tiles(64, tile, (zero, zero, zero), 4)
        for row, value in zip((5, 6, 7), sums):
            small_ref[row : row + 1] = value

        for copy in returned():
            copy.start()

        def turn(there, carry):
            d_branch_t[:, there] = jnp.transpose(d_branch[there].astype(F32)).astype(BF)
            return carry

        over_tiles(TILE, turn, 0, 3)

    @pl.when(step >= blocks)
    def _():
        block = step - blocks

        columns = [slice(begin, begin + TILE) for begin in range(0, width, TILE)]
        branch = d_branch[...]
        turned = d_branch_t[...]
        following = dot_nt(branch, down_ref[columns[0]])
        values = []
        for index, here in enumerate(columns):
            product = following
            if index + 1 < len(columns):
                following = dot_nt(branch, down_ref[columns[index + 1]])
            grad_down_ref[:, here] = dot_nn(turned, active[block, :, here]).astype(BF)
            d_up = (product * slope[block, :, here].astype(F32)).astype(BF)
            small_ref[pl.ds(8 + block, 1), here] = column_sum(d_up.astype(F32))
            values.append(d_up)
        values = jnp.concatenate(values, axis=1)
        turned = normed_t[...]
        for here in columns:
            grad_up_ref[:, here] = dot_nn(turned, values[:, here]).astype(BF)
            total[:, here] += dot_nt(values, up_ref[here])

    @pl.when(step == 2 * blocks - 1)
    def _():
        store(0).start()
        for copy in returned() + [store(0), store(1), store(2)]:
            copy.wait()


def fed_forward_and_back(
    item, mixed, cotangent, out_weight, up_weight, down_weight, vectors,
):
    rows, width = item.shape
    blocks = up_weight.shape[1] // width
    whole = pl.BlockSpec(memory_space=pltpu.VMEM)
    square = lambda kind: jax.ShapeDtypeStruct((rows, width), kind)
    later = lambda i: jnp.maximum(i - blocks, 0)
    return pl.pallas_call(
        feed_kernel,
        grid=(2 * blocks,),
        in_specs=[HBM, HBM, HBM, whole]
        + [
            pl.BlockSpec((width, width), lambda i: (0, lax.rem(i, blocks))),
            pl.BlockSpec((width, width), lambda i: (lax.rem(i, blocks), 0)),
        ]
        + [HBM] * 7,
        out_specs=[HBM] * 4
        + [
            pl.BlockSpec((width, width), lambda i: (later(i), 0)),
            pl.BlockSpec((width, width), lambda i: (later(i), 0)),
            whole,
        ],
        out_shape=[
            jax.ShapeDtypeStruct((2, rows // 2, width), BF), square(F32), square(F32),
            jax.ShapeDtypeStruct((rows, LANES), F32),
            jax.ShapeDtypeStruct((blocks * width, width), BF),
            jax.ShapeDtypeStruct((blocks * width, width), BF),
            jax.ShapeDtypeStruct((16, width), F32),
        ],
        scratch_shapes=[
            pltpu.VMEM((rows, width), BF),
            pltpu.VMEM((rows, width), F32),
            pltpu.VMEM((rows, width), BF),
            pltpu.VMEM((rows, width), BF),
            pltpu.VMEM((blocks, rows, width), BF),
            pltpu.VMEM((blocks, rows, width), BF),
            pltpu.VMEM((rows, width), F32),
            pltpu.VMEM((rows, LANES), F32),
            pltpu.VMEM((rows, width), BF),
            pltpu.VMEM((width, rows), BF),
            pltpu.VMEM((rows, width), F32),
            pltpu.VMEM((rows, width), BF),
            pltpu.VMEM((width, rows), BF),
            pltpu.SemaphoreType.DMA((4,)),
            pltpu.SemaphoreType.DMA((9,)),
            pltpu.SemaphoreType.DMA((2, rows // TILE)),
            pltpu.SemaphoreType.DMA((3,)),
        ]
        + [pltpu.VMEM(vector.shape, vector.dtype) for vector in vectors],
        compiler_params=pltpu.CompilerParams(
            collective_id=2, has_side_effects=True, vmem_limit_bytes=60 * MIB
        ),
        name="feed_forward",
    )(item, mixed, cotangent, out_weight, up_weight, down_weight, *vectors)


SLOTS = 4


def finish_kernel(
    main_ref, tail_ref, input_hbm, small_ref, diagonal_ref,
    down_ref, up_ref, out_ref, qkv_ref, input_ref, *refs,
):
    singles, (main_in, tail_in, slots, input_in, input_slot, in_sems, out_sems, item_sems) = (
        refs[:12], refs[12:],
    )
    mains, width = main_in.shape[0], main_in.shape[2]
    pairs, across = tail_in.shape[0], tail_in.shape[2]
    hidden = mains // 2
    blocks = mains + pairs

    def load(block):
        if block < mains:
            source, target = main_ref.at[pl.ds(block * width, width)], main_in.at[block]
        else:
            pair = block - mains
            source, target = tail_ref.at[pl.ds(pair * TAIL_ROWS, TAIL_ROWS)], tail_in.at[pair]
        return pltpu.make_async_copy(source, target, in_sems.at[block])

    def stores(block):
        slot, sem = slots.at[block % SLOTS], out_sems.at[block % SLOTS]
        if block < hidden:
            targets = [(slot, down_ref.at[pl.ds(block * width, width)])]
        elif block < mains:
            targets = [(slot, up_ref.at[:, pl.ds((block - hidden) * width, width)])]
        else:
            pair = block - mains
            targets = [
                (
                    slot.at[:, pl.ds(part * LANES, LANES)],
                    qkv_ref.at[:, pl.ds(part * width + pair * LANES, LANES)],
                )
                for part in range(3)
            ]
            down = pl.ds(0, TAIL_ROWS - width)
            targets.append(
                (slot.at[down, pl.ds(across, across)], out_ref.at[out_spot(pair, pairs, width)])
            )
        return [
            pltpu.make_async_copy(source, target, sem.at[index])
            for index, (source, target) in enumerate(targets)
        ]

    load_input = pltpu.make_async_copy(input_hbm, input_in, item_sems.at[0])
    store_input = pltpu.make_async_copy(input_slot, input_ref, item_sems.at[1])
    for block in range(blocks):
        load(block).start()
    load_input.start()
    for block in range(blocks):
        load(block).wait()
        if block >= SLOTS:
            for copy in stores(block - SLOTS):
                copy.wait()
        slot = block % SLOTS
        if block < hidden:
            slots[slot] = jnp.transpose(main_in[block].astype(F32))
        elif block < mains:
            slots[slot] = main_in[block].astype(F32)
        else:
            slots[slot, :, :across] = tail_in[block - mains, :width].astype(F32)
            slots[slot, : TAIL_ROWS - width, across:] = tail_in[block - mains, width:].astype(F32)
        for copy in stores(block):
            copy.start()
    load_input.wait()
    input_slot[...] = input_in[...].astype(F32)
    store_input.start()
    for row in range(8):
        singles[row][...] = small_ref[row]
    for row in range(hidden):
        singles[8][row * width : row * width + width] = small_ref[8 + row]
    heads, levels = singles[9].shape
    diagonals = diagonal_ref[...]
    level = lax.broadcasted_iota(jnp.int32, (LANES, LANES), 1)
    lane = lax.broadcasted_iota(jnp.int32, (LANES, LANES), 0)
    for table, (first, size, skip) in enumerate(((0, 4, 0), (4, 2, 1), (6, 2, 1))):
        total = jnp.zeros((heads, LANES), F32)
        for row in range(size):
            distance = lane + LANES * (row + skip - 2)
            chosen = (bucket(distance) == level).astype(F32)
            total = total + jnp.dot(
                diagonals[:, first + row, :], chosen, preferred_element_type=F32,
                precision=lax.Precision.HIGHEST,
            )
        singles[9 + table][...] = total[:, :levels]
    for block in range(blocks - SLOTS, blocks):
        for copy in stores(block):
            copy.wait()
    store_input.wait()


def finished(main, tail, grad_input, small, diagonals, hidden, levels):
    width = main.shape[1]
    heads = diagonals.shape[0]
    mains = main.shape[0] // width
    pairs = tail.shape[0] // TAIL_ROWS
    single = jax.ShapeDtypeStruct((width,), F32)
    table = jax.ShapeDtypeStruct((heads, levels), F32)
    dma = pltpu.SemaphoreType.DMA
    return pl.pallas_call(
        finish_kernel,
        in_specs=[HBM, HBM, HBM, VMEM, VMEM],
        out_specs=[HBM] * 5 + [VMEM] * 12,
        out_shape=[
            jax.ShapeDtypeStruct((hidden, width), F32),
            jax.ShapeDtypeStruct((width, hidden), F32),
            jax.ShapeDtypeStruct((width, width), F32),
            jax.ShapeDtypeStruct((width, 3 * width), F32),
            jax.ShapeDtypeStruct(grad_input.shape, F32),
        ]
        + [single] * 8
        + [jax.ShapeDtypeStruct((hidden,), F32)]
        + [table] * 3,
        scratch_shapes=[
            pltpu.VMEM((mains, width, width), BF),
            pltpu.VMEM((pairs, TAIL_ROWS, tail.shape[1]), BF),
            pltpu.VMEM((SLOTS, width, width), F32),
            pltpu.VMEM(grad_input.shape, BF),
            pltpu.VMEM(grad_input.shape, F32),
            dma((mains + pairs,)),
            dma((SLOTS, 4)),
            dma((2,)),
        ],
        compiler_params=pltpu.CompilerParams(vmem_limit_bytes=56 * MIB),
        name="finished",
    )(main, tail, grad_input, small, diagonals)


PIECE = 16


class Place:
    def __init__(self, depth):
        place = lax.axis_index("dp")
        self.depth = depth
        self.group = lax.div(place, 4 * depth)
        self.z = lax.rem(lax.div(place, 4), depth)
        self.bits = {
            "x": lax.axis_index("seq"),
            "c": lax.rem(place, 2),
            "y": lax.rem(lax.div(place, 2), 2),
            "a": lax.rem(self.z, 2),
            "b": lax.div(self.z, 2),
        }

    def partner(self, letters):
        bit = {
            letter: 1 - value if letter in letters else value
            for letter, value in self.bits.items()
        }
        z = self.z
        for letter, reach in (("a", 1), ("b", 2)):
            if letter in letters:
                z = z + reach - 2 * reach * self.bits[letter]
        return (bit["x"], (self.group * self.depth + z) * 4 + bit["y"] * 2 + bit["c"])

    def greet(self, met):
        barrier = pltpu.get_barrier_semaphore()
        for letters in met:
            pl.semaphore_signal(
                barrier, inc=1, device_id=self.partner(letters), device_id_type=MESH
            )
        pl.semaphore_wait(barrier, len(met))


def letters_of(depth):
    return "xy" + "ab"[: (depth - 1).bit_length()]


def parsed(routes, depth):
    kept = letters_of(depth)
    parts = []
    for route in routes.split():
        hops = ["".join(letter for letter in hop if letter in kept) for hop in route.split(".")]
        parts.append([hop for hop in hops if hop])
    return parts


def subsets(hop):
    return [
        "".join(letter for index, letter in enumerate(hop) if mask >> index & 1)
        for mask in range(1, 2 ** len(hop))
    ]


class Chunk:
    def __init__(self, place, depth, source, out_ref, offset, spot, scratch):
        _, self.begin, rows, first, columns, _, routes, _ = spot
        self.place, self.source, self.columns = place, source, pl.ds(first, columns)
        self.out_ref, self.out_begin = out_ref, offset + self.begin
        self.parts = parsed(routes, depth)
        self.half = rows // 2
        self.share = self.half // len(self.parts)
        self.hops = max(len(part) for part in self.parts)
        self.work, self.fresh, *landing, self.sends, self.receives, self.locals = scratch
        self.landing = {}
        self.sems = {}
        count = 2
        for part, hops in enumerate(self.parts):
            for hop, letters in enumerate(hops):
                self.landing[part, hop] = landing.pop(0)
                for way in range(2):
                    for index in range(2 ** len(letters) - 1):
                        self.sems[way, part, hop, index] = count
                        count += 1

    def aligned(self, value):
        return pl.multiple_of(value, PIECE)

    def size(self, part, hop):
        return self.share >> sum(len(letters) for letters in self.parts[part][: hop + 1])

    def spot(self, part, hop, other=""):
        start = part * self.share
        for level in range(hop + 1):
            for index, letter in enumerate(self.parts[part][level]):
                bit = self.place.bits[letter]
                if level == hop and letter in other:
                    bit = 1 - bit
                start = start + bit * (self.size(part, level) << index)
        return start

    def out(self, core):
        begin = self.aligned(self.out_begin + core * self.half)
        return self.out_ref.at[pl.ds(begin, self.half), self.columns]

    def held(self, buffer, begin, size):
        return buffer.at[pl.ds(self.aligned(begin), size)]

    def copy(self, index, source, target, letters):
        return remote(
            source, target, self.sends.at[index], self.receives.at[index],
            self.place.partner(letters),
        )

    def pair_down(self):
        core = self.place.bits["c"]
        at = lambda c: self.source.at[
            pl.ds(self.aligned(self.begin + c * self.half), self.half), self.columns
        ]
        return [
            self.copy(0, at(1 - core), self.fresh, "c"),
            pltpu.make_async_copy(at(core), self.work, self.locals.at[0]),
        ]

    def pair_up(self, arriving):
        core = self.place.bits["c"]
        return [
            self.copy(1, self.fresh, self.out(1 - core if arriving else core), "c"),
            pltpu.make_async_copy(self.fresh, self.out(core), self.locals.at[1]),
        ]

    def at_hop(self, hop):
        return [
            (part, hops[hop]) for part, hops in enumerate(self.parts) if hop < len(hops)
        ]

    def down(self, hop):
        copies = []
        for part, letters in self.at_hop(hop):
            size = self.size(part, hop)
            for index, other in enumerate(subsets(letters)):
                copies.append(
                    self.copy(
                        self.sems[0, part, hop, index],
                        self.held(self.work, self.spot(part, hop, other), size),
                        self.landing[part, hop].at[index], other,
                    )
                )
        return copies

    def up(self, hop, arriving):
        copies = []
        for part, letters in self.at_hop(hop):
            mine = self.spot(part, hop)
            size = self.size(part, hop)
            for index, other in enumerate(subsets(letters)):
                target = self.spot(part, hop, other) if arriving else mine
                copies.append(
                    self.copy(
                        self.sems[1, part, hop, index], self.held(self.fresh, mine, size),
                        self.held(self.fresh, target, size), other,
                    )
                )
        return copies

    def add(self, begin, sources, size):
        step = 64 if size % 64 == 0 else 32 if size % 32 == 0 else PIECE

        def body(index, carry):
            offset = self.aligned(index * step)
            there = pl.ds(self.aligned(begin + offset), step)
            total = self.work[there]
            if len(sources) == 1:
                total = total + sources[0][pl.ds(offset, step)]
            else:
                total = total.astype(F32)
                for source in sources:
                    total = total + source[pl.ds(offset, step)].astype(F32)
            self.work[there] = total.astype(BF)
            return carry

        lax.fori_loop(0, size // step, body, 0)

    def stage(self, number):
        hops = self.hops
        ended, started = [], []
        if number == 0:
            started = self.pair_down()
        elif number == 1:
            ended = self.pair_down()
            started = self.down(0)
        elif number <= hops:
            ended = self.down(number - 2)
            started = self.down(number - 1)
        elif number == hops + 1:
            ended = self.down(hops - 1)
            started = self.up(hops - 1, False)
        elif number <= 2 * hops:
            level = 2 * hops + 1 - number
            ended = self.up(level, True)
            started = self.up(level - 1, False)
        elif number == 2 * hops + 1:
            ended = self.up(0, True)
            started = self.pair_up(False)
        else:
            ended = self.pair_up(True)
        for copy in ended:
            copy.wait()
        if number == 1:
            self.add(0, [self.fresh], self.half)
        elif 2 <= number <= hops + 1:
            hop = number - 2
            for part, letters in self.at_hop(hop):
                landing = self.landing[part, hop]
                sources = [landing.at[index] for index in range(2 ** len(letters) - 1)]
                self.add(self.spot(part, hop), sources, self.size(part, hop))
        if number == hops + 1:
            for part, route in enumerate(self.parts):
                last = len(route) - 1
                there = pl.ds(self.aligned(self.spot(part, last)), self.size(part, last))
                self.fresh[there] = self.work[there]
        for copy in started:
            copy.start()


def chunk_scratch(spot, depth):
    _, _, rows, _, columns, _, routes, _ = spot
    parts = parsed(routes, depth)
    landing = []
    copies = 2
    for hops in parts:
        size = rows // 2 // len(parts)
        for letters in hops:
            size >>= len(letters)
            others = 2 ** len(letters) - 1
            copies += 2 * others
            landing.append(pltpu.VMEM((others, size, columns), BF))
    dma = pltpu.SemaphoreType.DMA
    return (
        [pltpu.VMEM((rows // 2, columns), BF)] * 2
        + landing
        + [dma((copies,)), dma((copies,)), dma((2,))]
    )


def loads_of(hop, size):
    if "x" in hop and "y" in hop:
        return [("x", 2 * size), ("y", 2 * size)]
    if hop in ("x", "y"):
        return [(hop, size)]
    if "a" in hop and "b" in hop:
        return [("end", 3 * size), ("middle", 4 * size)]
    return [("end", size), ("middle", 2 * size)] if hop == "b" else [("end", size)]


def planned(chunks, work, depth, hop_count):
    latency, issue, link, pair = 3.0, 0.08, 92e3, 600e3
    free = {}
    now = 3.0
    chains = []
    for rows, columns, need, routes, _ in chunks:
        parts = parsed(routes, depth)
        sizes = [rows // 2 // len(parts)] * len(parts)
        down = []
        for hop in range(max(len(part) for part in parts)):
            loads, copies, added = [], 0, 0
            for index, part in enumerate(parts):
                if hop < len(part):
                    sizes[index] >>= len(part[hop])
                    others = 2 ** len(part[hop]) - 1
                    loads += loads_of(part[hop], sizes[index])
                    copies += others
                    added += sizes[index] * others
            down.append((loads, copies, added, columns))
        first = [([("core", rows // 2)], 1.5, rows // 2, columns)]
        last = [([("core", rows // 2)], 1, 0, columns)]
        chains.append((need, first + down + down[::-1] + last))
    chains.append((len(work), [([("core", 16)], 2, 0, 768)] * hop_count))
    ranks = [chunk[4] for chunk in chunks] + [0]
    position = [0] * len(chains)
    ready = [0.0] * len(chains)
    order = [[] for _ in range(len(work) + 1)]
    done = 0
    while True:
        open_ones = [
            (ranks[i], ready[i], i) for i, (need, chain) in enumerate(chains)
            if position[i] <= len(chain) and need <= done
        ]
        due = [entry for entry in open_ones if entry[1] <= now]
        if not due and done < len(work):
            now += work[done]
            done += 1
            continue
        if not open_ones:
            return order
        _, when, index = min(due) if due else min(open_ones, key=lambda entry: entry[1])
        now = max(now, when)
        chain = chains[index][1]
        stage = position[index]
        order[done].append((index, stage))
        if 0 < stage <= len(chain) // 2:
            now += 1e-6 * chain[stage - 1][2] * chain[stage - 1][3]
        if stage < len(chain):
            loads, copies, _, columns = chain[stage]
            now += issue * copies
            end = now
            for lane, rows in loads:
                rate = pair if lane == "core" else link / 2
                free[lane] = max(now, free.get(lane, 0.0)) + 2 * rows * columns / rate
                end = max(end, free[lane])
            ready[index] = end + latency
        position[index] += 1


def last_kernel(
    depth, plan, orders, counts, *refs,
):
    (meta_ref, rows_ref, projected_hbm, mixed_hbm, log_ref, first_hbm, second_hbm,
     key_image_hbm, bias_hbm, small_ref, gain_ref, item_hbm, weight_hbm, total_hbm, unit_hbm, scale_hbm,
     out_weight_hbm, grad_down_ref, grad_up_ref,
     main_out, tail_out, small_out, diagonal_out, input_out,
     *scratch) = refs
    static, scratch = scratch[:6], scratch[6:]
    (k_ref, v_ref, mixed_ref, grad_ref, first_ref, second_ref, key_image_ref, bias_ref, pair_sems,
     item_ref, weight_ref, d_hidden_ref, unit_ref, scale_ref, load_sems, d_project, item_t, tail, input_grad,
     small_in, diagonal_in, small_sems, item_sems, *scratch) = scratch
    out_weight_ref = item_t
    place = Place(depth)
    step = pl.program_id(0)
    pairs = k_ref.shape[0]
    rows, width = item_hbm.shape
    count = rows // 2
    x = place.bits["x"]
    hidden = grad_down_ref.shape[0]
    sources = ((grad_down_ref, main_out, 0), (grad_up_ref, main_out, hidden), (tail, tail_out, 0))
    chunks = []
    for spot, pieces in zip(plan, counts):
        chunks.append(Chunk(place, depth, *sources[spot[0]], spot, scratch[:pieces]))
        scratch = scratch[pieces:]
    hop_letters = "c" + letters_of(depth)
    wide_hbm = (first_hbm, second_hbm, key_image_hbm, bias_hbm)
    wide_refs = (first_ref, second_ref, key_image_ref, bias_ref)

    def pair_loads(pair):
        copies = []
        held = ((projected_hbm, k_ref, width), (projected_hbm, v_ref, 2 * width))
        for source, target, first in held:
            columns = pl.ds(pl.multiple_of(first + pair * LANES, LANES), LANES)
            copies.append((source.at[:, columns], target.at[pair]))
        heads = pl.ds(2 * pair, 2)
        for source, target in zip(wide_hbm, wide_refs):
            copies.append((source.at[heads], target.at[heads]))
        return [
            pltpu.make_async_copy(source, target, pair_sems.at[pair, index])
            for index, (source, target) in enumerate(copies)
        ]

    def loads(first):
        if first:
            copies = [
                (total_hbm, d_hidden_ref), (unit_hbm, unit_ref), (scale_hbm, scale_ref),
                (out_weight_hbm, out_weight_ref), (item_hbm, item_ref),
            ]
            copies += [
                (mixed_hbm.at[:, pl.ds(pair * LANES, LANES)], mixed_ref.at[pair])
                for pair in range(pairs)
            ]
        else:
            copies = [(weight_hbm, weight_ref)]
        return [
            pltpu.make_async_copy(source, target, load_sems.at[0 if first else 1, index])
            for index, (source, target) in enumerate(copies)
        ]

    def back_to_attention():
        gain = vector(gain_ref)

        def tile(index, sums):
            there = pl.ds(pl.multiple_of(index * 64, 64), 64)
            d_normed = d_hidden_ref[there]
            standard = unit_ref[there]
            d_hidden = norm_pulled(d_normed * gain, standard, scale_ref[there, :1])
            d_hidden_ref[there] = d_hidden
            low = d_hidden.astype(BF)
            input_grad[there] = low
            return (
                sums[0] + column_sum(low.astype(F32)),
                sums[1] + column_sum(d_normed * standard),
                sums[2] + column_sum(d_normed),
            )

        zero = jnp.zeros((1, width), F32)
        sums = lax.fori_loop(0, rows // 64, tile, (zero, zero, zero), unroll=4)
        for row, value in zip((2, 3, 4), sums):
            small_out[row : row + 1] = value
        low = input_grad[...]
        down = TAIL_ROWS - width
        for begin in range(0, width, down):
            first = begin // LANES
            several = range(first, first + down // LANES)
            d_mixed = dot_nt(low, out_weight_ref[begin : begin + down]).astype(BF)
            for index, pair in enumerate(several):
                grad_ref[pair] = d_mixed[:, index * LANES : index * LANES + LANES]
            turned = jnp.concatenate(
                [jnp.transpose(mixed_ref[pair]).astype(BF) for pair in several], axis=0
            )
            for pair in range(pairs):
                rows_of, across = out_spot(pair, pairs, width)
                if rows_of.start == begin:
                    product = dot_nn(turned, low[:, across.start : across.start + across.size])
                    base = pair * TAIL_ROWS + width
                    tail[base : base + down] = product.astype(BF)

    def input_copies():
        return [
            pltpu.make_async_copy(
                input_grad.at[pl.ds(pl.multiple_of(x * count, LANES), count)], input_out.at[x],
                item_sems.at[0],
            ),
            remote(
                input_grad.at[pl.ds(pl.multiple_of((1 - x) * count, LANES), count)],
                input_out.at[x], item_sems.at[1], item_sems.at[2], place.partner("x"),
            ),
        ]

    def small_copies(hop):
        return [
            remote(source, landing.at[hop], small_sems.at[0, kind, hop],
                   small_sems.at[1, kind, hop], place.partner(hop_letters[hop]))
            for kind, (source, landing) in enumerate(
                ((small_out, small_in), (diagonal_out, diagonal_in))
            )
        ]

    def small_stage(hop):
        if hop > 0:
            for copy in small_copies(hop - 1):
                copy.wait()
            small_out[...] = small_out[...] + small_in[hop - 1]
            diagonal_out[...] = diagonal_out[...] + diagonal_in[hop - 1]
        if hop < len(hop_letters):
            for copy in small_copies(hop):
                copy.start()

    def perform(slot):
        for index, stage in orders[slot]:
            if index == len(chunks):
                small_stage(stage)
            else:
                chunks[index].stage(stage)

    @pl.when(step == 0)
    def _():
        for copy in pair_loads(0) + loads(True):
            copy.start()
        met = set(hop_letters)
        for chunk in chunks:
            for hops in chunk.parts:
                for letters in hops:
                    met.update(subsets(letters))
        place.greet(sorted(met))
        small_out[...] = small_ref[...]

    for pair in range(pairs):
        @pl.when(step == pair)
        def _(pair=pair):
            perform(pair)

    @pl.when(step == 0)
    def _():
        for pair in range(1, pairs):
            for copy in pair_loads(pair):
                copy.start()
        for copy in loads(False):
            copy.start()
        static_prepare(meta_ref, static)
        for copy in loads(True):
            copy.wait()
        back_to_attention()
        for tile in range(rows // TILE):
            there = slice(tile * TILE, tile * TILE + TILE)
            item_t[:, there] = jnp.transpose(item_ref[there].astype(F32)).astype(BF)

    for copy in pair_loads(step):
        copy.wait()
    (dq_even, dk_even, dv_even), (dq_odd, dk_odd, dv_odd) = [
        head_back(
            parity, step, rows_ref, wide_refs, k_ref, v_ref, mixed_ref, grad_ref, log_ref,
            static, diagonal_out,
        )
        for parity in range(2)
    ]
    even = own_lanes(0, rows)
    pieces = [
        jnp.transpose(jnp.concatenate([dq_even, dq_odd], axis=0)).astype(BF),
        jnp.where(even, dk_even, dk_odd).astype(BF),
        jnp.where(even, dv_even, dv_odd).astype(BF),
    ]
    for part, piece in enumerate(pieces):
        d_project[:, pl.ds(pl.multiple_of(part * width + step * LANES, LANES), LANES)] = piece
    slab = pl.ds(pl.multiple_of(step * TAIL_ROWS, TAIL_ROWS), width)
    tail[slab] = dot_nn(item_t[...], jnp.concatenate(pieces, axis=1)).astype(BF)

    @pl.when(step == 0)
    def _():
        for copy in loads(False):
            copy.wait()

    @pl.when(step == pairs - 1)
    def _():
        perform(pairs)
        for begin in range(0, width, TILE):
            here = slice(begin, begin + TILE)
            total = d_hidden_ref[:, here] + dot_nt(d_project[...], weight_ref[here])
            input_grad[:, here] = total.astype(BF)
        for copy in input_copies():
            copy.start()
        for begin in range(0, width, TILE):
            here = slice(begin, begin + TILE)
            there = slice(2 * width + begin, 2 * width + begin + TILE)
            small_out[0:1, here] = column_sum(d_project[:, here].astype(F32))
            small_out[1:2, here] = column_sum(d_project[:, there].astype(F32))
        perform(pairs + 1)
        for copy in input_copies():
            copy.wait()


TAIL_ROWS = 1024


def out_spot(pair, pairs, width):
    down = TAIL_ROWS - width
    across = width * width // (pairs * down)
    per_row = width // across
    return (
        pl.ds(pair // per_row * down, down),
        pl.ds(pair % per_row * across, across),
    )


def summed_with_attention_back(
    meta_columns, meta_rows, projected, mixed, logs, wide_arrays, item, qkv_weight,
    total, unit, scale, out_weight, attn_gain, small, grad_down, grad_up,
):
    size = lax.axis_size("dp")
    depth = 4 if size % 16 == 0 else size // 4
    rows, width = item.shape
    pairs = width // LANES
    hidden = grad_down.shape[0]
    hops = len(letters_of(depth)) + 1
    work = [15.0] + [6.0] * (pairs - 1) + [4.0]
    tall, wide = 1024, 3 * LANES
    plan = [
        (0, 0 * tall, 3 * tall, 0 * wide, wide, 0, "x.a.y.b y.x.a.b", 0),
        (0, 0 * tall, 3 * tall, 1 * wide, wide, 0, "a.x.b.y y.x.a.b", 4),
        (1, 0 * tall, 3 * tall, 0 * wide, wide, 0, "a.b.y.x x.y.a.b", 4),
        (1, 0 * tall, 3 * tall, 1 * wide, wide, 0, "x.a.y.b y.x.a.b", 4),
        (2, 0 * tall, 2 * tall, 0 * wide, wide, 2, "y.a.b.x a.b.y.x", 2),
        (2, 2 * tall, 2 * tall, 0 * wide, wide, 4, "y.x.ab x.y.ab", 4),
        (2, 4 * tall, 1 * tall, 0 * wide, wide, 5, "xy.ab", 1),
        (2, 5 * tall, 1 * tall, 0 * wide, wide, 6, "x.y.ab y.x.ab", 3),
    ]
    orders = planned([(spot[2],) + spot[4:] for spot in plan], work, depth, hops)

    whole = pl.BlockSpec(memory_space=pltpu.VMEM)
    diagonals = jax.ShapeDtypeStruct((2 * pairs, 8, LANES), F32)
    dma = pltpu.SemaphoreType.DMA
    scratch = []
    for spot in plan:
        scratch.append(chunk_scratch(spot, depth))
    main, tail, small, diagonals, grad_input = pl.pallas_call(
        functools.partial(last_kernel, depth, plan, orders, [len(pieces) for pieces in scratch]),
        grid=(pairs,),
        in_specs=[whole] * 2 + [HBM] * 2 + [whole] + [HBM] * 4 + [whole] * 2 + [HBM] * 8,
        out_specs=[HBM, HBM, whole, whole, HBM],
        out_shape=[
            jax.ShapeDtypeStruct((2 * hidden, width), BF),
            jax.ShapeDtypeStruct((pairs * TAIL_ROWS, 3 * LANES), BF),
            jax.ShapeDtypeStruct(small.shape, F32),
            diagonals,
            jax.ShapeDtypeStruct((2, rows // 2, width), BF),
        ],
        scratch_shapes=[pltpu.VMEM((rows, LANES), BF)] * 3
        + [pltpu.VMEM((LANES, rows), BF)] * 3
        + [pltpu.VMEM((pairs, rows, LANES), kind) for kind in (BF, BF, F32, BF)]
        + [pltpu.VMEM(array.shape, BF) for array in wide_arrays]
        + [
            dma((pairs, 6)),
            pltpu.VMEM((rows, width), BF),
            pltpu.VMEM((width, 3 * width), BF),
            pltpu.VMEM((rows, width), F32),
            pltpu.VMEM((rows, width), F32),
            pltpu.VMEM((rows, LANES), F32),
            dma((2, 5 + pairs)),
            pltpu.VMEM((rows, 3 * width), BF),
            pltpu.VMEM((width, rows), BF),
            pltpu.VMEM((pairs * TAIL_ROWS, 3 * LANES), BF),
            pltpu.VMEM((rows, width), BF),
            pltpu.VMEM((hops,) + small.shape, F32),
            pltpu.VMEM((hops,) + diagonals.shape, F32),
            dma((2, 2, hops)),
            dma((3,)),
        ]
        + [piece for pieces in scratch for piece in pieces],
        compiler_params=pltpu.CompilerParams(
            collective_id=0, has_side_effects=True, vmem_limit_bytes=62 * MIB
        ),
        name="summed_with_attention_back",
    )(meta_columns, meta_rows, projected, mixed, logs, *wide_arrays,
      small, attn_gain, item, qkv_weight, total, unit, scale, out_weight, grad_down, grad_up)
    span = 4 * depth
    if size > span:
        groups = [list(range(first, size, span)) for first in range(span)]
        main, tail, small, diagonals = lax.psum(
            (main.astype(F32), tail.astype(F32), small, diagonals), "dp",
            axis_index_groups=groups,
        )
        main, tail = main.astype(BF), tail.astype(BF)
    return main, tail, small, diagonals, grad_input


def per_device(
    layer_in, segment, key_mask, position, layout_x, layout_y,
    qkv_weight, query_bias, value_bias, out_weight, out_bias, attn_gain, attn_shift,
    up_weight, up_bias, down_weight, down_bias, ffn_gain, ffn_shift,
    text_table, horiz_table, vert_table, cotangent,
):
    width = layer_in.shape[-1]
    item, projected, meta_columns, meta_rows, table_rows = projected_item(
        layer_in, (segment, key_mask, position, layout_x, layout_y),
        qkv_weight, query_bias, value_bias, (text_table, horiz_table, vert_table),
    )
    mixed, logs, *wide_arrays = attention_forward(meta_columns, meta_rows, table_rows, projected, width)
    layer_out, total, unit, scale, grad_down, grad_up, small = fed_forward_and_back(
        item, mixed, cotangent, out_weight, up_weight, down_weight,
        (out_bias, attn_gain, attn_shift, up_bias, down_bias, ffn_gain, ffn_shift),
    )
    main, tail, small, diagonals, grad_input = summed_with_attention_back(
        meta_columns, meta_rows, projected, mixed, logs, wide_arrays, item, qkv_weight,
        total, unit, scale, out_weight, attn_gain, small, grad_down, grad_up,
    )
    done = finished(
        main, tail, grad_input, small, diagonals, up_weight.shape[1], text_table.shape[0]
    )
    sum_down, sum_up, sum_out, sum_qkv, grad_input = done[:5]
    singles, tables = done[5:14], [t.T for t in done[14:]]
    return (
        layer_out, grad_input, sum_qkv, singles[0], singles[1], sum_out, singles[2], singles[3],
        singles[4], sum_up, singles[8], sum_down, singles[5], singles[6], singles[7],
        tables[0], tables[1], tables[2],
    )


def solution(mesh):
    rows = P("dp", "seq", None)
    marks_spec = P("dp", "seq")
    return jax.shard_map(
        per_device,
        mesh=mesh,
        in_specs=(rows,) + (marks_spec,) * 5 + (P(),) * 16 + (rows,),
        out_specs=(rows, rows) + (P(),) * 16,
        check_vma=False,
    )
```

```python
import functools

import jax
import jax.numpy as jnp
from jax import lax
from jax.experimental import pallas as pl
from jax.experimental.pallas import tpu as pltpu
from jax.sharding import PartitionSpec as P

BF = jnp.bfloat16
F32 = jnp.float32
BIG = 1e30
LANES = 128
HEAD = 64
TEXT = 512
POS = 64
COORD = 48
Y0 = 64
GROUP0 = 112
MEMBER0 = 116
FLAG = 124
EVERY = 125
STRAY = 126
X_TABLE = 33
Y_TABLE = 66
NOTHING = 127


def dot_nt(a, b):
    return lax.dot_general(a, b, (((1,), (1,)), ((), ())), preferred_element_type=F32)


def dot_nn(a, b):
    return lax.dot_general(a, b, (((1,), (0,)), ((), ())), preferred_element_type=F32)


def looked_up(table_row, index):
    rows = index.shape[0]
    return jnp.take_along_axis(
        jnp.broadcast_to(table_row, (rows, LANES)), index, axis=1, mode="promise_in_bounds"
    )


def bucket(distance):
    return jnp.clip(distance, -16, 16) + 16


def between(lane, low, high):
    return (lane >= low) & (lane < high)


def columns_of(meta_ref):
    return tuple(meta_ref[:, field : field + 1] for field in range(5))


def marks(meta_ref):
    segment, key_mask, position, across, down = columns_of(meta_ref)
    rows = segment.shape[0]
    lane = lax.broadcasted_iota(jnp.int32, (rows, LANES), 1)
    row = lax.broadcasted_iota(jnp.int32, (rows, LANES), 0)
    even = between(lane, HEAD, HEAD + COORD) & (lane - HEAD == across)
    odd = (lane < COORD) & (lane == across)
    group = (segment - 1) >> 3
    member = (segment - 1) & 7
    named = segment > 0
    shared = (
        ((row < TEXT) & (lane < POS) & (lane == position))
        | (between(lane, Y0, Y0 + COORD) & (lane - Y0 == down))
        | (named & between(lane, GROUP0, MEMBER0) & (lane - GROUP0 == group))
        | (named & between(lane, MEMBER0, FLAG) & (lane - MEMBER0 == member))
        | ((lane == FLAG) & (key_mask <= 0))
        | (lane == EVERY)
        | ((lane == STRAY) & (segment < 0))
    )
    return tuple(jnp.where(m, 1.0, 0.0).astype(BF) for m in (even, odd, shared))


def square_lanes():
    shape = (LANES, LANES)
    return lax.broadcasted_iota(jnp.int32, shape, 0), lax.broadcasted_iota(jnp.int32, shape, 1)


def barred():
    row, lane = square_lanes()
    in_groups = between(lane, GROUP0, MEMBER0)
    shut = (
        (between(row, GROUP0, MEMBER0) & in_groups & (lane != row))
        | (between(row, MEMBER0, FLAG) & between(lane, MEMBER0, FLAG) & (lane != row))
        | ((row == EVERY) & (lane == FLAG))
        | ((row == STRAY) & in_groups)
    )
    return jnp.where(shut, -BIG, 0.0).astype(F32)


def table_index():
    row, lane = square_lanes()
    distance = bucket(row - lane)
    inside = lambda low, high: between(row, low, high) & between(lane, low, high)
    even = jnp.where(inside(HEAD, HEAD + COORD), distance + X_TABLE, NOTHING)
    odd = jnp.where(inside(0, COORD), distance + X_TABLE, NOTHING)
    shared = jnp.where(
        inside(0, POS), distance, jnp.where(inside(Y0, Y0 + COORD), distance + Y_TABLE, NOTHING)
    )
    return even, odd, shared


def image_query_index(meta_ref):
    position = meta_ref[TEXT:, 2:3]
    lane = lax.broadcasted_iota(jnp.int32, (position.shape[0], LANES), 1)
    return jnp.where(lane < POS, bucket(position - lane), NOTHING)


def prepare(meta_ref, mark_refs, bar_ref, index_refs, image_index_ref):
    for ref, value in zip(mark_refs, marks(meta_ref)):
        ref[...] = value
    bar_ref[...] = barred()
    for ref, value in zip(index_refs, table_index()):
        ref[...] = value
    image_index_ref[...] = image_query_index(meta_ref)


def own_lanes(parity, rows):
    lane = lax.broadcasted_iota(jnp.int32, (rows, LANES), 1)
    return (lane < HEAD) if parity == 0 else (lane >= HEAD)


def widened(parity, q, table_row, bias, bar_ref, index_refs, image_index_ref, mark_refs):
    rows = q.shape[0]
    shared = mark_refs[2][...]
    across = looked_up(table_row, index_refs[parity][...]).astype(BF)
    first = jnp.where(
        own_lanes(parity, rows), q.astype(F32) * 0.125, dot_nn(mark_refs[parity][...], across)
    )
    others = (looked_up(table_row, index_refs[2][...]) + bar_ref[...]).astype(BF)
    second = dot_nn(shared, others)
    on_images = looked_up(table_row, image_index_ref[...])
    second = jnp.concatenate([second[:TEXT], second[TEXT:] + on_images], axis=0)
    image_lane = lax.broadcasted_iota(jnp.int32, on_images.shape, 1)
    key_image = jnp.where(image_lane < POS, bias[:, :LANES].astype(BF), shared[TEXT:])
    return first.astype(BF), second.astype(BF), key_image


def joined(parity, first, second, key_image, k, marks_own, shared):
    rows = k.shape[0]
    lane = lax.broadcasted_iota(jnp.int32, (rows, LANES), 1)
    to_image = jnp.where(lane < POS, shared, second)
    key_first = jnp.where(own_lanes(parity, rows), k, marks_own)
    q_text = jnp.concatenate([first, second], axis=1)
    q_image = jnp.concatenate([first, to_image], axis=1)
    k_text = jnp.concatenate([key_first[:TEXT], shared[:TEXT]], axis=1)
    k_image = jnp.concatenate([key_first[TEXT:], key_image], axis=1)
    return q_text, q_image, k_text, k_image


def near(start, size):
    if start >= TEXT:
        return slice(0, TEXT)
    return slice(max(0, start - LANES), min(TEXT, start + size + LANES))


def image_bias(table_row, offsets):
    return jnp.concatenate(
        [looked_up(table_row, offsets[:, :LANES]), looked_up(table_row, offsets[:, LANES:])], axis=1
    )


def forward_kernel(
    meta_ref, rows_ref, table_ref, q_ref, k_ref, v_ref,
    mixed_ref, log_ref, first_ref, second_ref, key_image_ref, bias_ref,
    even_ref, odd_ref, shared_ref, bar_ref, index_even, index_odd, index_shared, image_index_ref,
):
    mark_refs = (even_ref, odd_ref, shared_ref)
    index_refs = (index_even, index_odd, index_shared)

    @pl.when(pl.program_id(0) == 0)
    def _():
        prepare(meta_ref, mark_refs, bar_ref, index_refs, image_index_ref)

    rows = q_ref.shape[0]
    images = rows - TEXT
    q, k, v = q_ref[...], k_ref[...], v_ref[...]
    offsets = bucket(rows_ref[2:3, TEXT:] - meta_ref[TEXT:, 2:3])
    tile = 256
    v_turned = transposed(v)
    heads = [None, None]

    def prepared(parity):
        table_row = table_ref[pl.ds(2 * pl.program_id(0) + parity, 1), :]
        bias = image_bias(table_row, offsets)
        first, second, key_image = widened(
            parity, q, table_row, bias, bar_ref, index_refs, image_index_ref, mark_refs
        )
        first_ref[parity] = first
        second_ref[parity] = second
        key_image_ref[parity] = key_image
        bias_ref[parity] = bias.astype(BF)
        wide = joined(
            parity, first, second, key_image, k, mark_refs[parity][...], shared_ref[...]
        )
        heads[parity] = wide + (bias,)

    def scored(parity, start):
        q_text, q_image, k_text, k_image, bias = heads[parity]
        here = slice(start, start + tile)
        on_image = dot_nt(k_image, q_image[here])
        if start >= TEXT:
            on_image = on_image + bias[:, start - TEXT : start - TEXT + tile]
        return dot_nt(k_text[near(start, tile)], q_text[here]), on_image

    spots = [(parity, start) for parity in range(2) for start in range(0, rows, tile)]
    outs = ([], [])
    prepared(0)
    following = scored(*spots[0])
    for index, (parity, start) in enumerate(spots):
        on_text, on_image = following
        if index == 1:
            prepared(1)
        if index + 1 < len(spots):
            following = scored(*spots[index + 1])
        top = jnp.maximum(
            jnp.max(on_text, axis=0, keepdims=True), jnp.max(on_image, axis=0, keepdims=True)
        )
        on_text = jnp.exp(on_text - top)
        on_image = jnp.exp(on_image - top)
        total = jnp.sum(on_text, axis=0, keepdims=True) + jnp.sum(on_image, axis=0, keepdims=True)
        own = slice(parity * HEAD, parity * HEAD + HEAD)
        out = dot_nn(v_turned[own, near(start, tile)], on_text.astype(BF)) + dot_nn(
            v_turned[own, TEXT:], on_image.astype(BF)
        )
        outs[parity].append(out * (1.0 / total))
        log_ref[0, parity : parity + 1, start : start + tile] = top + jnp.log(total)
    mixed_ref[...] = jnp.transpose(
        jnp.concatenate([jnp.concatenate(outs[parity], axis=1) for parity in range(2)], axis=0)
    )


def static_scratch(rows):
    square = (LANES, LANES)
    return [
        pltpu.VMEM((rows, LANES), BF),
        pltpu.VMEM((rows, LANES), BF),
        pltpu.VMEM((rows, LANES), BF),
        pltpu.VMEM(square, F32),
        pltpu.VMEM(square, jnp.int32),
        pltpu.VMEM(square, jnp.int32),
        pltpu.VMEM(square, jnp.int32),
        pltpu.VMEM((rows - TEXT, LANES), jnp.int32),
    ]


def attention_forward(meta_columns, meta_rows, table_rows, projected, width):
    rows = projected.shape[0]
    images = rows - TEXT
    pairs = width // LANES

    def block(part):
        return pl.BlockSpec((rows, LANES), lambda p: (0, part * pairs + p))

    whole = lambda shape: pl.BlockSpec(shape, lambda p: (0,) * len(shape))
    return pl.pallas_call(
        forward_kernel,
        grid=(pairs,),
        in_specs=[
            whole(meta_columns.shape),
            whole(meta_rows.shape),
            whole(table_rows.shape),
            block(0), block(1), block(2),
        ],
        out_specs=[
            pl.BlockSpec((rows, LANES), lambda p: (0, p)),
            pl.BlockSpec((1, 2, rows), lambda p: (p, 0, 0)),
            pl.BlockSpec((2, rows, LANES), lambda p: (p, 0, 0)),
            pl.BlockSpec((2, rows, LANES), lambda p: (p, 0, 0)),
            pl.BlockSpec((2, images, LANES), lambda p: (p, 0, 0)),
            pl.BlockSpec((2, images, images), lambda p: (p, 0, 0)),
        ],
        out_shape=[
            jax.ShapeDtypeStruct((rows, width), F32),
            jax.ShapeDtypeStruct((pairs, 2, rows), F32),
            jax.ShapeDtypeStruct((2 * pairs, rows, LANES), BF),
            jax.ShapeDtypeStruct((2 * pairs, rows, LANES), BF),
            jax.ShapeDtypeStruct((2 * pairs, images, LANES), BF),
            jax.ShapeDtypeStruct((2 * pairs, images, images), BF),
        ],
        scratch_shapes=static_scratch(rows),
        compiler_params=pltpu.CompilerParams(vmem_limit_bytes=60 * 1024 * 1024),
        name="attention_forward",
    )(meta_columns, meta_rows, table_rows, projected, projected, projected)


def skewed(block):
    size = block.shape[0]
    lane = lax.broadcasted_iota(jnp.int32, (size, LANES), 1)
    row = lax.broadcasted_iota(jnp.int32, (size, LANES), 0)
    turned = jnp.take_along_axis(
        block, (lane + row) & (LANES - 1), axis=1, mode="promise_in_bounds"
    )
    straight = lane + row < LANES
    above = jnp.sum(jnp.where(straight, turned, 0.0), axis=0, keepdims=True)
    below = jnp.sum(jnp.where(straight, 0.0, turned), axis=0, keepdims=True)
    return above, below


def transposed(array):
    return jnp.transpose(array.astype(F32)).astype(array.dtype)


def static_prepare(meta_ref, static):
    for ref, turned, value in zip(static[:3], static[3:], marks(meta_ref)):
        ref[...] = value
        turned[...] = transposed(value)


def head_back(
    parity, pair, rows_ref, wide_refs, k_ref, v_ref, mixed_ref, grad_ref, log_ref, static, diag_ref,
):
    mark_refs, turned_refs = static[:3], static[3:]
    first_ref, second_ref, key_image_ref, bias_ref = wide_refs
    head = 2 * pair + parity
    shared_t = turned_refs[2]
    rows = k_ref.shape[1]
    images = rows - TEXT
    tile = 256
    k, v, grad = k_ref[pair], v_ref[pair], grad_ref[pair]
    products = grad.astype(F32) * mixed_ref[pair]
    k_turned = transposed(k)
    is_image = rows_ref[1:2, TEXT:] > 0
    own = own_lanes(parity, rows)
    log_row = log_ref[pair, parity : parity + 1, :]
    first, shared = first_ref[head], mark_refs[2][...]
    q_text, q_image, k_text, k_image = joined(
        parity, first, second_ref[head], key_image_ref[head], k, mark_refs[parity][...], shared
    )
    bias = bias_ref[head].astype(F32)
    ones = jnp.where(own_lanes(parity, 8), 1.0, 0.0).astype(BF)
    delta = jnp.zeros((8, rows), F32)
    rest = products
    for _ in range(3):
        piece = rest.astype(BF)
        delta = delta + dot_nt(ones, piece)
        rest = rest - piece.astype(F32)
    delta = delta[0:1]
    v_own = jnp.where(own, v, jnp.zeros_like(v))
    q_marked = jnp.concatenate(
        [jnp.where(own, first, mark_refs[parity][...]), shared], axis=1
    )
    dq_text = jnp.zeros((HEAD, TEXT), F32)
    dq_image = jnp.zeros((HEAD, images), F32)
    dks = []
    dvs = []
    first_sum = jnp.zeros((LANES, LANES), F32)
    second_sum = jnp.zeros((LANES, LANES), F32)
    text_image = jnp.zeros((LANES, images), F32)

    def met(start, array, axis=0):
        text = near(start, tile)
        if axis == 0:
            return jnp.concatenate([array[text], array[TEXT:]], axis=0)
        return jnp.concatenate([array[:, text], array[:, TEXT:]], axis=1)

    def scored(start):
        here = slice(start, start + tile)
        if start < TEXT:
            scores = dot_nt(k_text[here], met(start, q_text))
        else:
            scores = dot_nt(k_image[start - TEXT : start - TEXT + tile], q_image)
            scores = jnp.concatenate([scores[:, :TEXT], scores[:, TEXT:] + bias], axis=1)
        return scores, dot_nt(v_own[here], met(start, grad))

    following = scored(0)
    for start in range(0, rows, tile):
        here = slice(start, start + tile)
        scores, prob_grad = following
        if start + tile < rows:
            following = scored(start + tile)
        soft = jnp.exp(scores - met(start, log_row, 1))
        score_grad = soft * (prob_grad - met(start, delta, 1))
        low = score_grad.astype(BF)
        dvs.append(dot_nn(soft.astype(BF), met(start, grad)))
        wide = dot_nn(low, met(start, q_marked))
        dks.append(wide[:, :LANES])
        part = dot_nn(k_turned[parity * HEAD : parity * HEAD + HEAD, here], low)
        text = near(start, tile)
        count = text.stop - text.start
        before = [jnp.zeros((HEAD, text.start), F32)] if text.start > 0 else []
        after = [jnp.zeros((HEAD, TEXT - text.stop), F32)] if text.stop < TEXT else []
        dq_text = dq_text + jnp.concatenate(before + [part[:, :count]] + after, axis=1)
        dq_image = dq_image + part[:, count:]
        rounded = wide.astype(BF)
        first_sum = first_sum + dot_nn(turned_refs[parity][:, here], rounded[:, :LANES])
        second_sum = second_sum + dot_nn(shared_t[:, here], rounded[:, LANES:])
        if start < TEXT:
            text_image = text_image + dot_nn(shared_t[:, here], low[:, count:])
        else:
            by_position = wide[:, LANES:]
            on_image = score_grad[:, TEXT:]
    dq = jnp.concatenate([dq_text, dq_image], axis=1)
    small = lax.broadcasted_iota(jnp.int32, (LANES, LANES), 1)
    small_row = lax.broadcasted_iota(jnp.int32, (LANES, LANES), 0)
    x0 = HEAD if parity == 0 else 0
    x_block = jnp.where(
        between(small, x0, x0 + COORD) & between(small_row, x0, x0 + COORD), first_sum, 0.0
    )
    y_block = jnp.where(
        between(small, Y0, Y0 + COORD) & between(small_row, Y0, Y0 + COORD), second_sum, 0.0
    )
    p_block = jnp.where((small < POS) & (small_row < POS), second_sum, 0.0)
    wide_lane = lax.broadcasted_iota(jnp.int32, (images, images), 1)
    outside = jnp.sum(jnp.where(is_image, 0.0, on_image), axis=1, keepdims=True)
    pairs = jnp.where(is_image, on_image, 0.0) + jnp.where(wide_lane == 0, outside, 0.0)
    outside_text = jnp.sum(jnp.where(is_image, 0.0, text_image), axis=1, keepdims=True)
    text_lane = lax.broadcasted_iota(jnp.int32, (LANES, images), 1)
    text_row = lax.broadcasted_iota(jnp.int32, (LANES, images), 0)
    text_image = jnp.where(is_image, text_image, 0.0) + jnp.where(
        text_lane == 0, outside_text, 0.0
    )
    text_image = jnp.where(text_row < POS, text_image, 0.0)
    first_lane = lax.broadcasted_iota(jnp.int32, (images, LANES), 1)
    left = pairs[:, :LANES] + jnp.where(first_lane < POS, by_position, 0.0)
    right = pairs[:, LANES:]
    a00, b00 = skewed(left[:LANES] + text_image[:, :LANES] + p_block)
    a01, b01 = skewed(right[:LANES] + text_image[:, LANES:])
    a10, b10 = skewed(left[LANES:])
    a11, b11 = skewed(right[LANES:])
    ax, bx = skewed(x_block)
    ay, by = skewed(y_block)
    diag_ref[head] = jnp.concatenate(
        [b10, b00 + b11 + a10, a00 + a11 + b01, a01, bx, ax, by, ay], axis=0
    )
    return dq * 0.125, jnp.concatenate(dks, axis=0), jnp.concatenate(dvs, axis=0)


MESH = pl.DeviceIdType.MESH
VMEM = pl.BlockSpec(memory_space=pltpu.VMEM)
HBM = pl.BlockSpec(memory_space=pltpu.HBM)
MIB = 1024 * 1024


def remote(src, dst, send, receive, device):
    return pltpu.make_async_remote_copy(
        src_ref=src, dst_ref=dst, send_sem=send, recv_sem=receive, device_id=device,
        device_id_type=MESH,
    )


def project_kernel(
    layer_ref, weight_hbm, *refs,
):
    small_hbm, refs = refs[:10], refs[10:]
    (item_ref, projected_out, columns_ref, rows_ref, table_ref,
     projected_ref, weight_ref, meta_send, bias_ref, sems, load_sems, store_sems), small = (
        refs[:12], refs[12:],
    )
    (segment_ref, mask_ref, position_ref, across_ref, down_ref, query_bias_ref, value_bias_ref,
     text_ref, horiz_ref, vert_ref) = small
    mine = lax.axis_index("seq")
    partner = (1 - mine, lax.axis_index("dp"))
    count, width = layer_ref.shape[1:]
    own = pl.ds(pl.multiple_of(mine * count, LANES), count)
    loads = [
        pltpu.make_async_copy(source, target, load_sems.at[index])
        for index, (source, target) in enumerate(
            list(zip(small_hbm, small))
            + [(layer_ref.at[mine], item_ref.at[own]), (weight_hbm, weight_ref)]
        )
    ]
    barrier = pltpu.get_barrier_semaphore()
    pl.semaphore_signal(barrier, inc=1, device_id=partner, device_id_type=MESH)
    pl.semaphore_wait(barrier, 1)
    pieces = count // LANES
    rows_out = [
        remote(
            layer_ref.at[1 - mine, pl.ds(piece * LANES, LANES)],
            item_ref.at[pl.ds(pl.multiple_of(mine * count + piece * LANES, LANES), LANES)],
            sems.at[0, piece], sems.at[1, piece], partner,
        )
        for piece in range(pieces)
    ]
    for copy in rows_out:
        copy.start()
    for load in loads:
        load.start()
    for load in loads[:-2]:
        load.wait()

    fields = (segment_ref, mask_ref, position_ref, across_ref, down_ref)
    blocks = [
        jnp.concatenate(
            [field[item : item + 1, :] for field in fields] + [jnp.zeros((3, count), jnp.int32)],
            axis=0,
        )
        for item in range(2)
    ]
    meta_send[...] = jnp.where(mine == 0, blocks[1], blocks[0])
    meta_out = remote(
        meta_send, rows_ref.at[:, own], sems.at[0, pieces], sems.at[1, pieces], partner
    )
    meta_out.start()
    rows_ref[:, own] = jnp.where(mine == 0, blocks[0], blocks[1])
    bias_ref[:, :width] = query_bias_ref[...].astype(F32).reshape(1, width)
    bias_ref[:, width : 2 * width] = jnp.zeros((1, width), F32)
    bias_ref[:, 2 * width :] = value_bias_ref[...].astype(F32).reshape(1, width)
    heads, levels = text_ref.shape
    spot = lax.broadcasted_iota(jnp.int32, (levels, LANES), 1)
    level = lax.broadcasted_iota(jnp.int32, (levels, LANES), 0)
    table = jnp.zeros((heads, LANES), F32)
    for source, begin in ((text_ref, 0), (horiz_ref, X_TABLE), (vert_ref, Y_TABLE)):
        table = table + dot_nn(source[...], (spot == level + begin).astype(BF))
    table_ref[...] = jnp.concatenate([table, jnp.zeros((16 - heads, LANES), F32)], axis=0)

    def project(there):
        step = 256

        def body(index, carry):
            columns = pl.ds(pl.multiple_of(index * step, step), step)
            product = dot_nn(item_ref[there], weight_ref[:, columns])
            projected_ref[there, columns] = (product + bias_ref[:, columns]).astype(BF)
            return carry

        lax.fori_loop(0, 3 * width // step, body, 0)

    def stored(index, there):
        return pltpu.make_async_copy(
            projected_ref.at[there], projected_out.at[there], store_sems.at[index]
        )

    for load in loads[-2:]:
        load.wait()
    project(own)
    stored(0, own).start()
    for piece in range(pieces):
        rows_out[piece].wait()
        there = pl.ds(pl.multiple_of((1 - mine) * count + piece * LANES, LANES), LANES)
        project(there)
        stored(1 + piece, there).start()
    meta_out.wait()
    meta = rows_ref[...].astype(F32)
    tall = jnp.concatenate([meta, jnp.zeros((LANES - 8, meta.shape[1]), F32)], axis=0)
    columns_ref[...] = jnp.transpose(tall).astype(jnp.int32)
    stored(0, own).wait()
    for piece in range(pieces):
        there = pl.ds(pl.multiple_of((1 - mine) * count + piece * LANES, LANES), LANES)
        stored(1 + piece, there).wait()


def projected_item(layer_in, fields, qkv_weight, query_bias, value_bias, tables):
    rows = 2 * layer_in.shape[1]
    width = layer_in.shape[2]
    pieces = rows // 2 // LANES
    small = list(fields) + [query_bias, value_bias] + [t.T for t in tables]
    return pl.pallas_call(
        project_kernel,
        in_specs=[HBM] * (2 + len(small)),
        out_specs=[VMEM, HBM, VMEM, VMEM, VMEM],
        out_shape=[
            jax.ShapeDtypeStruct((rows, width), BF),
            jax.ShapeDtypeStruct((rows, 3 * width), BF),
            jax.ShapeDtypeStruct((rows, LANES), jnp.int32),
            jax.ShapeDtypeStruct((8, rows), jnp.int32),
            jax.ShapeDtypeStruct((16, LANES), F32),
        ],
        scratch_shapes=[
            pltpu.VMEM((rows, 3 * width), BF),
            pltpu.VMEM((width, 3 * width), BF),
            pltpu.VMEM((8, rows // 2), jnp.int32),
            pltpu.VMEM((1, 3 * width), F32),
            pltpu.SemaphoreType.DMA((2, pieces + 1)),
            pltpu.SemaphoreType.DMA((len(small) + 2,)),
            pltpu.SemaphoreType.DMA((pieces + 1,)),
        ]
        + [pltpu.VMEM(array.shape, array.dtype) for array in small],
        compiler_params=pltpu.CompilerParams(
            collective_id=1, has_side_effects=True, vmem_limit_bytes=60 * MIB
        ),
        name="projected_item",
    )(layer_in, qkv_weight, *small)


EPSILON = 1e-05
TILE = 256


def vector(ref):
    return ref[...].astype(F32).reshape(1, ref.shape[0])


def gelu_and_slope(x):
    bell = jnp.exp2(-0.7213475204444817 * (x * x))
    rough = 1.0 + 0.23164188826 * jnp.abs(x)
    t = pl.reciprocal(rough, approx=True)
    t = t * (2.0 - rough * t)
    series = t * (
        0.127414796
        + t * (-0.142248368 + t * (0.7107068705 + t * (-0.7265760135 + t * 0.5307027145)))
    )
    tail = bell * series
    below = jnp.where(x >= 0.0, 1.0 - tail, tail)
    return x * below, below + x * (0.3989422804014327 * bell)


def row_mean(block):
    return jnp.mean(block, axis=1, keepdims=True)


def normalized(hidden):
    center = hidden - row_mean(hidden)
    scale = lax.rsqrt(row_mean(center * center) + EPSILON)
    return center * scale, scale


def norm_pulled(grad, unit, scale):
    return scale * (grad - row_mean(grad) - unit * row_mean(grad * unit))


def column_sum(block):
    return jnp.sum(block, axis=0, keepdims=True)


def feed_kernel(
    item_hbm, mixed_hbm, cotangent_ref, out_weight_ref, up_ref, down_ref, *refs,
):
    vectors_hbm, refs = refs[:7], refs[7:]
    (layer_out, total_out, unit_out, scale_out, grad_down_ref, grad_up_ref, small_ref,
     item_ref, mixed_ref, layer_ref, cotangent_all, active, slope, unit, scale_ref, normed, normed_t, total, d_branch, d_branch_t,
     sems, load_sems, tile_sems, store_sems) = refs[:24]
    vectors = refs[24:]
    (out_bias_ref, attn_gain_ref, attn_shift_ref, up_bias_ref, down_bias_ref, ffn_gain_ref,
     ffn_shift_ref) = vectors
    step = pl.program_id(0)
    blocks = pl.num_programs(0) // 2
    rows, width = item_hbm.shape
    count = rows // 2
    mine = lax.axis_index("seq")
    partner = (1 - mine, lax.axis_index("dp"))
    own = pl.ds(pl.multiple_of(mine * count, LANES), count)
    tiles = rows // TILE

    def sent():
        return remote(
            cotangent_ref.at[1 - mine], cotangent_all.at[own], sems.at[0], sems.at[1], partner
        )

    def returned():
        theirs = pl.ds(pl.multiple_of((1 - mine) * count, LANES), count)
        return [
            pltpu.make_async_copy(layer_ref.at[own], layer_out.at[mine], load_sems.at[8]),
            remote(
                layer_ref.at[theirs], layer_out.at[mine], sems.at[2], sems.at[3], partner
            ),
        ]

    def tile_loads(tile):
        there = pl.ds(tile * TILE, TILE)
        return [
            pltpu.make_async_copy(source.at[there], target.at[there], tile_sems.at[index, tile])
            for index, (source, target) in enumerate(
                ((mixed_hbm, mixed_ref), (item_hbm, item_ref))
            )
        ]

    def store(index):
        source, target = (
            (total, total_out), (unit, unit_out), (scale_ref, scale_out),
        )[index]
        return pltpu.make_async_copy(source, target, store_sems.at[index])

    def loads():
        copies = list(zip(vectors_hbm, vectors)) + [(cotangent_ref.at[mine], cotangent_all.at[own])]
        return [
            pltpu.make_async_copy(source, target, load_sems.at[index])
            for index, (source, target) in enumerate(copies)
        ]

    def over_tiles(size, body, carry, unroll=1):
        def run(index, state):
            return body(pl.ds(pl.multiple_of(index * size, size), size), state)

        return lax.fori_loop(0, rows // size, run, carry, unroll=unroll)

    @pl.when(step == 0)
    def _():
        for index in range(rows // TILE):
            for load in tile_loads(index):
                load.start()
        for load in loads():
            load.start()
        barrier = pltpu.get_barrier_semaphore()
        pl.semaphore_signal(barrier, inc=1, device_id=partner, device_id_type=MESH)
        pl.semaphore_wait(barrier, 1)
        sent().start()
        small_ref[...] = jnp.zeros_like(small_ref)
        for load in loads():
            load.wait()
        out_bias, gain, shift = vector(out_bias_ref), vector(attn_gain_ref), vector(attn_shift_ref)

        for index in range(rows // TILE):
            for load in tile_loads(index):
                load.wait()
            there = slice(index * TILE, index * TILE + TILE)
            attn = dot_nn(mixed_ref[there].astype(BF), out_weight_ref[...]) + out_bias
            standard, scale = normalized(item_ref[there].astype(F32) + attn)
            unit[there] = standard
            scale_ref[there] = jnp.broadcast_to(scale, (TILE, LANES))
            result = standard * gain + shift
            normed[there] = result.astype(BF)
            normed_t[:, there] = jnp.transpose(result).astype(BF)
        store(1).start()
        store(2).start()
        total[...] = jnp.zeros_like(total)

    @pl.when(step < blocks)
    def _():
        columns = [slice(begin, begin + TILE) for begin in range(0, width, TILE)]
        low = normed[...]
        following = dot_nn(low, up_ref[:, columns[0]])
        values = []
        for index, here in enumerate(columns):
            product = following
            if index + 1 < len(columns):
                following = dot_nn(low, up_ref[:, columns[index + 1]])
            bias = up_bias_ref[pl.ds(pl.multiple_of(step * width + here.start, LANES), TILE)]
            value, grade = gelu_and_slope(product + bias.astype(F32).reshape(1, TILE))
            values.append(value.astype(BF))
            active[step, :, here] = values[-1]
            slope[step, :, here] = grade.astype(BF)
        values = jnp.concatenate(values, axis=1)
        for here in columns:
            total[:, here] += dot_nn(values, down_ref[:, here])

    @pl.when(step == blocks)
    def _():
        sent().wait()
        gain, shift, bias = vector(ffn_gain_ref), vector(ffn_shift_ref), vector(down_bias_ref)
        first_gain, first_shift = vector(attn_gain_ref), vector(attn_shift_ref)

        def tile(there, sums):
            hidden = unit[there] * first_gain + first_shift + (total[there] + bias)
            standard, scale = normalized(hidden)
            layer_ref[there] = (standard * gain + shift).astype(BF)
            cotangent = cotangent_all[there].astype(F32)
            pulled = norm_pulled(cotangent * gain, standard, scale)
            total[there] = pulled
            low = pulled.astype(BF)
            d_branch[there] = low
            return (
                sums[0] + column_sum(low.astype(F32)),
                sums[1] + column_sum(cotangent * standard),
                sums[2] + column_sum(cotangent),
            )

        zero = jnp.zeros((1, width), F32)
        sums = over_tiles(64, tile, (zero, zero, zero), 4)
        for row, value in zip((5, 6, 7), sums):
            small_ref[row : row + 1] = value

        for copy in returned():
            copy.start()

        def turn(there, carry):
            d_branch_t[:, there] = jnp.transpose(d_branch[there].astype(F32)).astype(BF)
            return carry

        over_tiles(TILE, turn, 0, 3)

    @pl.when(step >= blocks)
    def _():
        block = step - blocks

        columns = [slice(begin, begin + TILE) for begin in range(0, width, TILE)]
        branch = d_branch[...]
        turned = d_branch_t[...]
        following = dot_nt(branch, down_ref[columns[0]])
        values = []
        for index, here in enumerate(columns):
            product = following
            if index + 1 < len(columns):
                following = dot_nt(branch, down_ref[columns[index + 1]])
            grad_down_ref[:, here] = dot_nn(turned, active[block, :, here]).astype(BF)
            d_up = (product * slope[block, :, here].astype(F32)).astype(BF)
            small_ref[pl.ds(8 + block, 1), here] = column_sum(d_up.astype(F32))
            values.append(d_up)
        values = jnp.concatenate(values, axis=1)
        turned = normed_t[...]
        for here in columns:
            grad_up_ref[:, here] = dot_nn(turned, values[:, here]).astype(BF)
            total[:, here] += dot_nt(values, up_ref[here])

    @pl.when(step == 2 * blocks - 1)
    def _():
        store(0).start()
        for copy in returned() + [store(0), store(1), store(2)]:
            copy.wait()


def fed_forward_and_back(
    item, mixed, cotangent, out_weight, up_weight, down_weight, vectors,
):
    rows, width = item.shape
    blocks = up_weight.shape[1] // width
    whole = pl.BlockSpec(memory_space=pltpu.VMEM)
    square = lambda kind: jax.ShapeDtypeStruct((rows, width), kind)
    later = lambda i: jnp.maximum(i - blocks, 0)
    return pl.pallas_call(
        feed_kernel,
        grid=(2 * blocks,),
        in_specs=[HBM, HBM, HBM, whole]
        + [
            pl.BlockSpec((width, width), lambda i: (0, lax.rem(i, blocks))),
            pl.BlockSpec((width, width), lambda i: (lax.rem(i, blocks), 0)),
        ]
        + [HBM] * 7,
        out_specs=[HBM] * 4
        + [
            pl.BlockSpec((width, width), lambda i: (later(i), 0)),
            pl.BlockSpec((width, width), lambda i: (later(i), 0)),
            whole,
        ],
        out_shape=[
            jax.ShapeDtypeStruct((2, rows // 2, width), BF), square(F32), square(F32),
            jax.ShapeDtypeStruct((rows, LANES), F32),
            jax.ShapeDtypeStruct((blocks * width, width), BF),
            jax.ShapeDtypeStruct((blocks * width, width), BF),
            jax.ShapeDtypeStruct((16, width), F32),
        ],
        scratch_shapes=[
            pltpu.VMEM((rows, width), BF),
            pltpu.VMEM((rows, width), F32),
            pltpu.VMEM((rows, width), BF),
            pltpu.VMEM((rows, width), BF),
            pltpu.VMEM((blocks, rows, width), BF),
            pltpu.VMEM((blocks, rows, width), BF),
            pltpu.VMEM((rows, width), F32),
            pltpu.VMEM((rows, LANES), F32),
            pltpu.VMEM((rows, width), BF),
            pltpu.VMEM((width, rows), BF),
            pltpu.VMEM((rows, width), F32),
            pltpu.VMEM((rows, width), BF),
            pltpu.VMEM((width, rows), BF),
            pltpu.SemaphoreType.DMA((4,)),
            pltpu.SemaphoreType.DMA((9,)),
            pltpu.SemaphoreType.DMA((2, rows // TILE)),
            pltpu.SemaphoreType.DMA((3,)),
        ]
        + [pltpu.VMEM(vector.shape, vector.dtype) for vector in vectors],
        compiler_params=pltpu.CompilerParams(
            collective_id=2, has_side_effects=True, vmem_limit_bytes=60 * MIB
        ),
        name="feed_forward",
    )(item, mixed, cotangent, out_weight, up_weight, down_weight, *vectors)


SLOTS = 4


def finish_kernel(
    main_ref, tail_ref, input_hbm, small_ref, diagonal_ref,
    down_ref, up_ref, out_ref, qkv_ref, input_ref, *refs,
):
    singles, (main_in, tail_in, slots, input_in, input_slot, in_sems, out_sems, item_sems) = (
        refs[:12], refs[12:],
    )
    mains, width = main_in.shape[0], main_in.shape[2]
    pairs, across = tail_in.shape[0], tail_in.shape[2]
    hidden = mains // 2
    blocks = mains + pairs

    def load(block):
        if block < mains:
            source, target = main_ref.at[pl.ds(block * width, width)], main_in.at[block]
        else:
            pair = block - mains
            source, target = tail_ref.at[pl.ds(pair * TAIL_ROWS, TAIL_ROWS)], tail_in.at[pair]
        return pltpu.make_async_copy(source, target, in_sems.at[block])

    def stores(block):
        slot, sem = slots.at[block % SLOTS], out_sems.at[block % SLOTS]
        if block < hidden:
            targets = [(slot, down_ref.at[pl.ds(block * width, width)])]
        elif block < mains:
            targets = [(slot, up_ref.at[:, pl.ds((block - hidden) * width, width)])]
        else:
            pair = block - mains
            targets = [
                (
                    slot.at[:, pl.ds(part * LANES, LANES)],
                    qkv_ref.at[:, pl.ds(part * width + pair * LANES, LANES)],
                )
                for part in range(3)
            ]
            down = pl.ds(0, TAIL_ROWS - width)
            targets.append(
                (slot.at[down, pl.ds(across, across)], out_ref.at[out_spot(pair, pairs, width)])
            )
        return [
            pltpu.make_async_copy(source, target, sem.at[index])
            for index, (source, target) in enumerate(targets)
        ]

    load_input = pltpu.make_async_copy(input_hbm, input_in, item_sems.at[0])
    store_input = pltpu.make_async_copy(input_slot, input_ref, item_sems.at[1])
    for block in range(SLOTS):
        load(block).start()
    for block in range(blocks):
        load(block).wait()
        if block >= SLOTS:
            for copy in stores(block - SLOTS):
                copy.wait()
        slot = block % SLOTS
        if block < hidden:
            slots[slot] = jnp.transpose(main_in[block].astype(F32))
        elif block < mains:
            slots[slot] = main_in[block].astype(F32)
        else:
            slots[slot, :, :across] = tail_in[block - mains, :width].astype(F32)
            slots[slot, : TAIL_ROWS - width, across:] = tail_in[block - mains, width:].astype(F32)
        for copy in stores(block):
            copy.start()
        if block + SLOTS < blocks:
            load(block + SLOTS).start()
        elif block + SLOTS == blocks:
            load_input.start()
    load_input.wait()
    input_slot[...] = input_in[...].astype(F32)
    store_input.start()
    for row in range(8):
        singles[row][...] = small_ref[row]
    for row in range(hidden):
        singles[8][row * width : row * width + width] = small_ref[8 + row]
    heads, levels = singles[9].shape
    diagonals = diagonal_ref[...]
    level = lax.broadcasted_iota(jnp.int32, (LANES, LANES), 1)
    lane = lax.broadcasted_iota(jnp.int32, (LANES, LANES), 0)
    for table, (first, size, skip) in enumerate(((0, 4, 0), (4, 2, 1), (6, 2, 1))):
        total = jnp.zeros((heads, LANES), F32)
        for row in range(size):
            distance = lane + LANES * (row + skip - 2)
            chosen = (bucket(distance) == level).astype(F32)
            total = total + jnp.dot(
                diagonals[:, first + row, :], chosen, preferred_element_type=F32,
                precision=lax.Precision.HIGHEST,
            )
        singles[9 + table][...] = total[:, :levels]
    for block in range(blocks - SLOTS, blocks):
        for copy in stores(block):
            copy.wait()
    store_input.wait()


def finished(main, tail, grad_input, small, diagonals, hidden, levels):
    width = main.shape[1]
    heads = diagonals.shape[0]
    mains = main.shape[0] // width
    pairs = tail.shape[0] // TAIL_ROWS
    single = jax.ShapeDtypeStruct((width,), F32)
    table = jax.ShapeDtypeStruct((heads, levels), F32)
    dma = pltpu.SemaphoreType.DMA
    return pl.pallas_call(
        finish_kernel,
        in_specs=[HBM, HBM, HBM, VMEM, VMEM],
        out_specs=[HBM] * 5 + [VMEM] * 12,
        out_shape=[
            jax.ShapeDtypeStruct((hidden, width), F32),
            jax.ShapeDtypeStruct((width, hidden), F32),
            jax.ShapeDtypeStruct((width, width), F32),
            jax.ShapeDtypeStruct((width, 3 * width), F32),
            jax.ShapeDtypeStruct(grad_input.shape, F32),
        ]
        + [single] * 8
        + [jax.ShapeDtypeStruct((hidden,), F32)]
        + [table] * 3,
        scratch_shapes=[
            pltpu.VMEM((mains, width, width), BF),
            pltpu.VMEM((pairs, TAIL_ROWS, tail.shape[1]), BF),
            pltpu.VMEM((SLOTS, width, width), F32),
            pltpu.VMEM(grad_input.shape, BF),
            pltpu.VMEM(grad_input.shape, F32),
            dma((mains + pairs,)),
            dma((SLOTS, 4)),
            dma((2,)),
        ],
        compiler_params=pltpu.CompilerParams(vmem_limit_bytes=56 * MIB),
        name="finished",
    )(main, tail, grad_input, small, diagonals)


PIECE = 16


class Place:
    def __init__(self, depth):
        place = lax.axis_index("dp")
        self.depth = depth
        self.group = lax.div(place, 4 * depth)
        self.z = lax.rem(lax.div(place, 4), depth)
        self.bits = {
            "x": lax.axis_index("seq"),
            "c": lax.rem(place, 2),
            "y": lax.rem(lax.div(place, 2), 2),
            "a": lax.rem(self.z, 2),
            "b": lax.div(self.z, 2),
        }

    def partner(self, letters):
        bit = {
            letter: 1 - value if letter in letters else value
            for letter, value in self.bits.items()
        }
        z = self.z
        for letter, reach in (("a", 1), ("b", 2)):
            if letter in letters:
                z = z + reach - 2 * reach * self.bits[letter]
        return (bit["x"], (self.group * self.depth + z) * 4 + bit["y"] * 2 + bit["c"])

    def greet(self, met):
        barrier = pltpu.get_barrier_semaphore()
        for letters in met:
            pl.semaphore_signal(
                barrier, inc=1, device_id=self.partner(letters), device_id_type=MESH
            )
        pl.semaphore_wait(barrier, len(met))


def letters_of(depth):
    return "xy" + "ab"[: (depth - 1).bit_length()]


def parsed(routes, depth):
    kept = letters_of(depth)
    parts = []
    for route in routes.split():
        hops = ["".join(letter for letter in hop if letter in kept) for hop in route.split(".")]
        parts.append([hop for hop in hops if hop])
    return parts


def subsets(hop):
    return [
        "".join(letter for index, letter in enumerate(hop) if mask >> index & 1)
        for mask in range(1, 2 ** len(hop))
    ]


class Chunk:
    def __init__(self, place, depth, source, out_ref, offset, spot, scratch):
        _, self.begin, rows, first, columns, _, routes, _ = spot
        self.place, self.source, self.columns = place, source, pl.ds(first, columns)
        self.out_ref, self.out_begin = out_ref, offset + self.begin
        self.parts = parsed(routes, depth)
        self.half = rows // 2
        self.share = self.half // len(self.parts)
        self.hops = max(len(part) for part in self.parts)
        self.work, self.fresh, *landing, self.sends, self.receives, self.locals = scratch
        self.landing = {}
        self.sems = {}
        count = 2
        for part, hops in enumerate(self.parts):
            for hop, letters in enumerate(hops):
                self.landing[part, hop] = landing.pop(0)
                for way in range(2):
                    for index in range(2 ** len(letters) - 1):
                        self.sems[way, part, hop, index] = count
                        count += 1

    def aligned(self, value):
        return pl.multiple_of(value, PIECE)

    def size(self, part, hop):
        return self.share >> sum(len(letters) for letters in self.parts[part][: hop + 1])

    def spot(self, part, hop, other=""):
        start = part * self.share
        for level in range(hop + 1):
            for index, letter in enumerate(self.parts[part][level]):
                bit = self.place.bits[letter]
                if level == hop and letter in other:
                    bit = 1 - bit
                start = start + bit * (self.size(part, level) << index)
        return start

    def out(self, core):
        begin = self.aligned(self.out_begin + core * self.half)
        return self.out_ref.at[pl.ds(begin, self.half), self.columns]

    def held(self, buffer, begin, size):
        return buffer.at[pl.ds(self.aligned(begin), size)]

    def copy(self, index, source, target, letters):
        return remote(
            source, target, self.sends.at[index], self.receives.at[index],
            self.place.partner(letters),
        )

    def pair_down(self):
        core = self.place.bits["c"]
        at = lambda c: self.source.at[
            pl.ds(self.aligned(self.begin + c * self.half), self.half), self.columns
        ]
        return [
            self.copy(0, at(1 - core), self.fresh, "c"),
            pltpu.make_async_copy(at(core), self.work, self.locals.at[0]),
        ]

    def pair_up(self, arriving):
        core = self.place.bits["c"]
        return [
            self.copy(1, self.fresh, self.out(1 - core if arriving else core), "c"),
            pltpu.make_async_copy(self.fresh, self.out(core), self.locals.at[1]),
        ]

    def at_hop(self, hop):
        return [
            (part, hops[hop]) for part, hops in enumerate(self.parts) if hop < len(hops)
        ]

    def down(self, hop):
        copies = []
        for part, letters in self.at_hop(hop):
            size = self.size(part, hop)
            for index, other in enumerate(subsets(letters)):
                copies.append(
                    self.copy(
                        self.sems[0, part, hop, index],
                        self.held(self.work, self.spot(part, hop, other), size),
                        self.landing[part, hop].at[index], other,
                    )
                )
        return copies

    def up(self, hop, arriving):
        copies = []
        for part, letters in self.at_hop(hop):
            mine = self.spot(part, hop)
            size = self.size(part, hop)
            for index, other in enumerate(subsets(letters)):
                target = self.spot(part, hop, other) if arriving else mine
                copies.append(
                    self.copy(
                        self.sems[1, part, hop, index], self.held(self.fresh, mine, size),
                        self.held(self.fresh, target, size), other,
                    )
                )
        return copies

    def add(self, begin, sources, size):
        step = 64 if size % 64 == 0 else 32 if size % 32 == 0 else PIECE

        def body(index, carry):
            offset = self.aligned(index * step)
            there = pl.ds(self.aligned(begin + offset), step)
            total = self.work[there]
            if len(sources) == 1:
                total = total + sources[0][pl.ds(offset, step)]
            else:
                total = total.astype(F32)
                for source in sources:
                    total = total + source[pl.ds(offset, step)].astype(F32)
            self.work[there] = total.astype(BF)
            return carry

        lax.fori_loop(0, size // step, body, 0)

    def stage(self, number):
        hops = self.hops
        ended, started = [], []
        if number == 0:
            started = self.pair_down()
        elif number == 1:
            ended = self.pair_down()
            started = self.down(0)
        elif number <= hops:
            ended = self.down(number - 2)
            started = self.down(number - 1)
        elif number == hops + 1:
            ended = self.down(hops - 1)
            started = self.up(hops - 1, False)
        elif number <= 2 * hops:
            level = 2 * hops + 1 - number
            ended = self.up(level, True)
            started = self.up(level - 1, False)
        elif number == 2 * hops + 1:
            ended = self.up(0, True)
            started = self.pair_up(False)
        else:
            ended = self.pair_up(True)
        for copy in ended:
            copy.wait()
        if number == 1:
            self.add(0, [self.fresh], self.half)
        elif 2 <= number <= hops + 1:
            hop = number - 2
            for part, letters in self.at_hop(hop):
                landing = self.landing[part, hop]
                sources = [landing.at[index] for index in range(2 ** len(letters) - 1)]
                self.add(self.spot(part, hop), sources, self.size(part, hop))
        if number == hops + 1:
            for part, route in enumerate(self.parts):
                last = len(route) - 1
                there = pl.ds(self.aligned(self.spot(part, last)), self.size(part, last))
                self.fresh[there] = self.work[there]
        for copy in started:
            copy.start()


def chunk_scratch(spot, depth):
    _, _, rows, _, columns, _, routes, _ = spot
    parts = parsed(routes, depth)
    landing = []
    copies = 2
    for hops in parts:
        size = rows // 2 // len(parts)
        for letters in hops:
            size >>= len(letters)
            others = 2 ** len(letters) - 1
            copies += 2 * others
            landing.append(pltpu.VMEM((others, size, columns), BF))
    dma = pltpu.SemaphoreType.DMA
    return (
        [pltpu.VMEM((rows // 2, columns), BF)] * 2
        + landing
        + [dma((copies,)), dma((copies,)), dma((2,))]
    )


def loads_of(hop, size):
    if "x" in hop and "y" in hop:
        return [("x", 2 * size), ("y", 2 * size)]
    if hop in ("x", "y"):
        return [(hop, size)]
    if "a" in hop and "b" in hop:
        return [("end", 3 * size), ("middle", 4 * size)]
    return [("end", size), ("middle", 2 * size)] if hop == "b" else [("end", size)]


def planned(chunks, work, depth, hop_count):
    latency, issue, link, pair = 3.5, 0.08, 100e3, 600e3
    free = {}
    now = 3.0
    chains = []
    for rows, columns, need, routes, _ in chunks:
        parts = parsed(routes, depth)
        sizes = [rows // 2 // len(parts)] * len(parts)
        down = []
        for hop in range(max(len(part) for part in parts)):
            loads, copies, added = [], 0, 0
            for index, part in enumerate(parts):
                if hop < len(part):
                    sizes[index] >>= len(part[hop])
                    others = 2 ** len(part[hop]) - 1
                    loads += loads_of(part[hop], sizes[index])
                    copies += others
                    added += sizes[index] * others
            down.append((loads, copies, added, columns))
        first = [([("core", rows // 2)], 1.5, rows // 2, columns)]
        last = [([("core", rows // 2)], 1, 0, columns)]
        chains.append((need, first + down + down[::-1] + last))
    chains.append((len(work), [([("core", 16)], 2, 0, 768)] * hop_count))
    ranks = [chunk[4] for chunk in chunks] + [0]
    position = [0] * len(chains)
    ready = [0.0] * len(chains)
    order = [[] for _ in range(len(work) + 1)]
    done = 0
    while True:
        open_ones = [
            (ranks[i], ready[i], i) for i, (need, chain) in enumerate(chains)
            if position[i] <= len(chain) and need <= done
        ]
        due = [entry for entry in open_ones if entry[1] <= now]
        if not due and done < len(work):
            now += work[done]
            done += 1
            continue
        if not open_ones:
            return order
        _, when, index = min(due) if due else min(open_ones, key=lambda entry: entry[1])
        now = max(now, when)
        chain = chains[index][1]
        stage = position[index]
        order[done].append((index, stage))
        if 0 < stage <= len(chain) // 2:
            now += 1e-6 * chain[stage - 1][2] * chain[stage - 1][3]
        if stage < len(chain):
            loads, copies, _, columns = chain[stage]
            now += issue * copies
            end = now
            for lane, rows in loads:
                rate = pair if lane == "core" else link / 2
                free[lane] = max(now, free.get(lane, 0.0)) + 2 * rows * columns / rate
                end = max(end, free[lane])
            ready[index] = end + latency
        position[index] += 1


def last_kernel(
    depth, plan, orders, counts, *refs,
):
    (meta_ref, rows_ref, projected_hbm, mixed_hbm, log_ref, first_hbm, second_hbm,
     key_image_hbm, bias_hbm, small_ref, gain_ref, item_hbm, weight_hbm, total_hbm, unit_hbm, scale_hbm,
     out_weight_hbm, grad_down_ref, grad_up_ref,
     main_out, tail_out, small_out, diagonal_out, input_out,
     *scratch) = refs
    static, scratch = scratch[:6], scratch[6:]
    (k_ref, v_ref, mixed_ref, grad_ref, first_ref, second_ref, key_image_ref, bias_ref, pair_sems,
     item_ref, weight_ref, d_hidden_ref, unit_ref, scale_ref, load_sems, d_project, item_t, tail, input_grad,
     small_in, diagonal_in, small_sems, item_sems, *scratch) = scratch
    out_weight_ref = item_t
    place = Place(depth)
    step = pl.program_id(0)
    pairs = k_ref.shape[0]
    rows, width = item_hbm.shape
    count = rows // 2
    x = place.bits["x"]
    hidden = grad_down_ref.shape[0]
    sources = ((grad_down_ref, main_out, 0), (grad_up_ref, main_out, hidden), (tail, tail_out, 0))
    chunks = []
    for spot, pieces in zip(plan, counts):
        chunks.append(Chunk(place, depth, *sources[spot[0]], spot, scratch[:pieces]))
        scratch = scratch[pieces:]
    hop_letters = "c" + letters_of(depth)
    wide_hbm = (first_hbm, second_hbm, key_image_hbm, bias_hbm)
    wide_refs = (first_ref, second_ref, key_image_ref, bias_ref)

    def pair_loads(pair):
        copies = []
        held = ((projected_hbm, k_ref, width), (projected_hbm, v_ref, 2 * width))
        for source, target, first in held:
            columns = pl.ds(pl.multiple_of(first + pair * LANES, LANES), LANES)
            copies.append((source.at[:, columns], target.at[pair]))
        heads = pl.ds(2 * pair, 2)
        for source, target in zip(wide_hbm, wide_refs):
            copies.append((source.at[heads], target.at[heads]))
        return [
            pltpu.make_async_copy(source, target, pair_sems.at[pair, index])
            for index, (source, target) in enumerate(copies)
        ]

    def loads(first):
        if first:
            copies = [
                (total_hbm, d_hidden_ref), (unit_hbm, unit_ref), (scale_hbm, scale_ref),
                (out_weight_hbm, out_weight_ref), (item_hbm, item_ref),
            ]
            copies += [
                (mixed_hbm.at[:, pl.ds(pair * LANES, LANES)], mixed_ref.at[pair])
                for pair in range(pairs)
            ]
        else:
            copies = [(weight_hbm, weight_ref)]
        return [
            pltpu.make_async_copy(source, target, load_sems.at[0 if first else 1, index])
            for index, (source, target) in enumerate(copies)
        ]

    def back_to_attention():
        gain = vector(gain_ref)

        def tile(index, sums):
            there = pl.ds(pl.multiple_of(index * 64, 64), 64)
            d_normed = d_hidden_ref[there]
            standard = unit_ref[there]
            d_hidden = norm_pulled(d_normed * gain, standard, scale_ref[there, :1])
            d_hidden_ref[there] = d_hidden
            low = d_hidden.astype(BF)
            input_grad[there] = low
            return (
                sums[0] + column_sum(low.astype(F32)),
                sums[1] + column_sum(d_normed * standard),
                sums[2] + column_sum(d_normed),
            )

        zero = jnp.zeros((1, width), F32)
        sums = lax.fori_loop(0, rows // 64, tile, (zero, zero, zero), unroll=4)
        for row, value in zip((2, 3, 4), sums):
            small_out[row : row + 1] = value
        low = input_grad[...]
        down = TAIL_ROWS - width
        for begin in range(0, width, down):
            first = begin // LANES
            several = range(first, first + down // LANES)
            d_mixed = dot_nt(low, out_weight_ref[begin : begin + down]).astype(BF)
            for index, pair in enumerate(several):
                grad_ref[pair] = d_mixed[:, index * LANES : index * LANES + LANES]
            turned = jnp.concatenate(
                [jnp.transpose(mixed_ref[pair]).astype(BF) for pair in several], axis=0
            )
            for pair in range(pairs):
                rows_of, across = out_spot(pair, pairs, width)
                if rows_of.start == begin:
                    product = dot_nn(turned, low[:, across.start : across.start + across.size])
                    base = pair * TAIL_ROWS + width
                    tail[base : base + down] = product.astype(BF)

    def input_copies():
        return [
            pltpu.make_async_copy(
                input_grad.at[pl.ds(pl.multiple_of(x * count, LANES), count)], input_out.at[x],
                item_sems.at[0],
            ),
            remote(
                input_grad.at[pl.ds(pl.multiple_of((1 - x) * count, LANES), count)],
                input_out.at[x], item_sems.at[1], item_sems.at[2], place.partner("x"),
            ),
        ]

    def small_copies(hop):
        return [
            remote(source, landing.at[hop], small_sems.at[0, kind, hop],
                   small_sems.at[1, kind, hop], place.partner(hop_letters[hop]))
            for kind, (source, landing) in enumerate(
                ((small_out, small_in), (diagonal_out, diagonal_in))
            )
        ]

    def small_stage(hop):
        if hop > 0:
            for copy in small_copies(hop - 1):
                copy.wait()
            small_out[...] = small_out[...] + small_in[hop - 1]
            diagonal_out[...] = diagonal_out[...] + diagonal_in[hop - 1]
        if hop < len(hop_letters):
            for copy in small_copies(hop):
                copy.start()

    def perform(slot):
        for index, stage in orders[slot]:
            if index == len(chunks):
                small_stage(stage)
            else:
                chunks[index].stage(stage)

    @pl.when(step == 0)
    def _():
        met = set(hop_letters)
        for chunk in chunks:
            for hops in chunk.parts:
                for letters in hops:
                    met.update(subsets(letters))
        place.greet(sorted(met))
        small_out[...] = small_ref[...]

    for pair in range(pairs):
        @pl.when(step == pair)
        def _(pair=pair):
            perform(pair)

    @pl.when(step == 0)
    def _():
        for copy in loads(True):
            copy.start()
        for pair in range(pairs):
            for copy in pair_loads(pair):
                copy.start()
        for copy in loads(False):
            copy.start()
        static_prepare(meta_ref, static)
        for copy in loads(True):
            copy.wait()
        back_to_attention()
        for tile in range(rows // TILE):
            there = slice(tile * TILE, tile * TILE + TILE)
            item_t[:, there] = jnp.transpose(item_ref[there].astype(F32)).astype(BF)

    for copy in pair_loads(step):
        copy.wait()
    (dq_even, dk_even, dv_even), (dq_odd, dk_odd, dv_odd) = [
        head_back(
            parity, step, rows_ref, wide_refs, k_ref, v_ref, mixed_ref, grad_ref, log_ref,
            static, diagonal_out,
        )
        for parity in range(2)
    ]
    even = own_lanes(0, rows)
    pieces = [
        jnp.transpose(jnp.concatenate([dq_even, dq_odd], axis=0)).astype(BF),
        jnp.where(even, dk_even, dk_odd).astype(BF),
        jnp.where(even, dv_even, dv_odd).astype(BF),
    ]
    for part, piece in enumerate(pieces):
        d_project[:, pl.ds(pl.multiple_of(part * width + step * LANES, LANES), LANES)] = piece
    slab = pl.ds(pl.multiple_of(step * TAIL_ROWS, TAIL_ROWS), width)
    tail[slab] = dot_nn(item_t[...], jnp.concatenate(pieces, axis=1)).astype(BF)

    @pl.when(step == 0)
    def _():
        for copy in loads(False):
            copy.wait()

    @pl.when(step == pairs - 1)
    def _():
        perform(pairs)
        for begin in range(0, width, TILE):
            here = slice(begin, begin + TILE)
            total = d_hidden_ref[:, here] + dot_nt(d_project[...], weight_ref[here])
            input_grad[:, here] = total.astype(BF)
        for copy in input_copies():
            copy.start()
        for begin in range(0, width, TILE):
            here = slice(begin, begin + TILE)
            there = slice(2 * width + begin, 2 * width + begin + TILE)
            small_out[0:1, here] = column_sum(d_project[:, here].astype(F32))
            small_out[1:2, here] = column_sum(d_project[:, there].astype(F32))
        perform(pairs + 1)
        for copy in input_copies():
            copy.wait()


TAIL_ROWS = 1024


def out_spot(pair, pairs, width):
    down = TAIL_ROWS - width
    across = width * width // (pairs * down)
    per_row = width // across
    return (
        pl.ds(pair // per_row * down, down),
        pl.ds(pair % per_row * across, across),
    )


def summed_with_attention_back(
    meta_columns, meta_rows, projected, mixed, logs, wide_arrays, item, qkv_weight,
    total, unit, scale, out_weight, attn_gain, small, grad_down, grad_up,
):
    size = lax.axis_size("dp")
    depth = 4 if size % 16 == 0 else size // 4
    rows, width = item.shape
    pairs = width // LANES
    hidden = grad_down.shape[0]
    hops = len(letters_of(depth)) + 1
    work = [6.8] * pairs + [4.0]
    tall, wide, slim = 1024, 3 * LANES, 2 * LANES
    plan = [
        (0, 0, 2 * tall, 0, width, 0, "a.b.x.y x.y.a.b", 1),
        (0, 2 * tall, tall, 0, width, 0, "x.a.y.b y.a.b.x", 2),
        (1, 0, 3 * tall, 0, slim, 0, "a.b.x.y y.x.a.b", 4),
        (1, 0, 3 * tall, slim, slim, 0, "y.a.x.b x.y.a.b", 0),
        (1, 0, 3 * tall, 2 * slim, slim, 0, "x.y.a.b y.x.a.b", 2),
        (2, 0, tall, 0, wide, 1, "y.x.a.b a.b.x.y", 3),
        (2, tall, tall, 0, wide, 2, "xy.a.b", 2),
        (2, 2 * tall, tall, 0, wide, 3, "x.y.ab y.ab.x", 3),
        (2, 3 * tall, tall, 0, wide, 4, "xy.a.b", 1),
        (2, 4 * tall, tall, 0, wide, 5, "xy.a.b", 1),
        (2, 5 * tall, tall, 0, wide, 6, "ab.y.x y.ab.x", 2),
    ]
    orders = planned([(spot[2],) + spot[4:] for spot in plan], work, depth, hops)

    whole = pl.BlockSpec(memory_space=pltpu.VMEM)
    diagonals = jax.ShapeDtypeStruct((2 * pairs, 8, LANES), F32)
    dma = pltpu.SemaphoreType.DMA
    scratch = []
    for spot in plan:
        scratch.append(chunk_scratch(spot, depth))
    main, tail, small, diagonals, grad_input = pl.pallas_call(
        functools.partial(last_kernel, depth, plan, orders, [len(pieces) for pieces in scratch]),
        grid=(pairs,),
        in_specs=[whole] * 2 + [HBM] * 2 + [whole] + [HBM] * 4 + [whole] * 2 + [HBM] * 8,
        out_specs=[HBM, HBM, whole, whole, HBM],
        out_shape=[
            jax.ShapeDtypeStruct((2 * hidden, width), BF),
            jax.ShapeDtypeStruct((pairs * TAIL_ROWS, 3 * LANES), BF),
            jax.ShapeDtypeStruct(small.shape, F32),
            diagonals,
            jax.ShapeDtypeStruct((2, rows // 2, width), BF),
        ],
        scratch_shapes=[pltpu.VMEM((rows, LANES), BF)] * 3
        + [pltpu.VMEM((LANES, rows), BF)] * 3
        + [pltpu.VMEM((pairs, rows, LANES), kind) for kind in (BF, BF, F32, BF)]
        + [pltpu.VMEM(array.shape, BF) for array in wide_arrays]
        + [
            dma((pairs, 6)),
            pltpu.VMEM((rows, width), BF),
            pltpu.VMEM((width, 3 * width), BF),
            pltpu.VMEM((rows, width), F32),
            pltpu.VMEM((rows, width), F32),
            pltpu.VMEM((rows, LANES), F32),
            dma((2, 5 + pairs)),
            pltpu.VMEM((rows, 3 * width), BF),
            pltpu.VMEM((width, rows), BF),
            pltpu.VMEM((pairs * TAIL_ROWS, 3 * LANES), BF),
            pltpu.VMEM((rows, width), BF),
            pltpu.VMEM((hops,) + small.shape, F32),
            pltpu.VMEM((hops,) + diagonals.shape, F32),
            dma((2, 2, hops)),
            dma((3,)),
        ]
        + [piece for pieces in scratch for piece in pieces],
        compiler_params=pltpu.CompilerParams(
            collective_id=0, has_side_effects=True, vmem_limit_bytes=62 * MIB
        ),
        name="summed_with_attention_back",
    )(meta_columns, meta_rows, projected, mixed, logs, *wide_arrays,
      small, attn_gain, item, qkv_weight, total, unit, scale, out_weight, grad_down, grad_up)
    span = 4 * depth
    if size > span:
        groups = [list(range(first, size, span)) for first in range(span)]
        main, tail, small, diagonals = lax.psum(
            (main.astype(F32), tail.astype(F32), small, diagonals), "dp",
            axis_index_groups=groups,
        )
        main, tail = main.astype(BF), tail.astype(BF)
    return main, tail, small, diagonals, grad_input


def per_device(
    layer_in, segment, key_mask, position, layout_x, layout_y,
    qkv_weight, query_bias, value_bias, out_weight, out_bias, attn_gain, attn_shift,
    up_weight, up_bias, down_weight, down_bias, ffn_gain, ffn_shift,
    text_table, horiz_table, vert_table, cotangent,
):
    width = layer_in.shape[-1]
    item, projected, meta_columns, meta_rows, table_rows = projected_item(
        layer_in, (segment, key_mask, position, layout_x, layout_y),
        qkv_weight, query_bias, value_bias, (text_table, horiz_table, vert_table),
    )
    mixed, logs, *wide_arrays = attention_forward(meta_columns, meta_rows, table_rows, projected, width)
    layer_out, total, unit, scale, grad_down, grad_up, small = fed_forward_and_back(
        item, mixed, cotangent, out_weight, up_weight, down_weight,
        (out_bias, attn_gain, attn_shift, up_bias, down_bias, ffn_gain, ffn_shift),
    )
    main, tail, small, diagonals, grad_input = summed_with_attention_back(
        meta_columns, meta_rows, projected, mixed, logs, wide_arrays, item, qkv_weight,
        total, unit, scale, out_weight, attn_gain, small, grad_down, grad_up,
    )
    done = finished(
        main, tail, grad_input, small, diagonals, up_weight.shape[1], text_table.shape[0]
    )
    sum_down, sum_up, sum_out, sum_qkv, grad_input = done[:5]
    singles, tables = done[5:14], [t.T for t in done[14:]]
    return (
        layer_out, grad_input, sum_qkv, singles[0], singles[1], sum_out, singles[2], singles[3],
        singles[4], sum_up, singles[8], sum_down, singles[5], singles[6], singles[7],
        tables[0], tables[1], tables[2],
    )


def solution(mesh):
    rows = P("dp", "seq", None)
    marks_spec = P("dp", "seq")
    return jax.shard_map(
        per_device,
        mesh=mesh,
        in_specs=(rows,) + (marks_spec,) * 5 + (P(),) * 16 + (rows,),
        out_specs=(rows, rows) + (P(),) * 16,
        check_vma=False,
    )
```

```python
import functools

import jax
import jax.numpy as jnp
from jax import lax
from jax.experimental import pallas as pl
from jax.experimental.pallas import tpu as pltpu
from jax.sharding import PartitionSpec as P

BF = jnp.bfloat16
F32 = jnp.float32
BIG = 1e30
LANES = 128
HEAD = 64
TEXT = 512
POS = 64
COORD = 48
Y0 = 64
GROUP0 = 112
MEMBER0 = 116
FLAG = 124
EVERY = 125
STRAY = 126
X_TABLE = 33
Y_TABLE = 66
NOTHING = 127


def dot_nt(a, b):
    return lax.dot_general(a, b, (((1,), (1,)), ((), ())), preferred_element_type=F32)


def dot_nn(a, b):
    return lax.dot_general(a, b, (((1,), (0,)), ((), ())), preferred_element_type=F32)


def looked_up(table_row, index):
    rows = index.shape[0]
    return jnp.take_along_axis(
        jnp.broadcast_to(table_row, (rows, LANES)), index, axis=1, mode="promise_in_bounds"
    )


def bucket(distance):
    return jnp.clip(distance, -16, 16) + 16


def between(lane, low, high):
    return (lane >= low) & (lane < high)


def columns_of(meta_ref):
    return tuple(meta_ref[:, field : field + 1] for field in range(5))


def marks(meta_ref):
    segment, key_mask, position, across, down = columns_of(meta_ref)
    rows = segment.shape[0]
    lane = lax.broadcasted_iota(jnp.int32, (rows, LANES), 1)
    row = lax.broadcasted_iota(jnp.int32, (rows, LANES), 0)
    even = between(lane, HEAD, HEAD + COORD) & (lane - HEAD == across)
    odd = (lane < COORD) & (lane == across)
    group = (segment - 1) >> 3
    member = (segment - 1) & 7
    named = segment > 0
    shared = (
        ((row < TEXT) & (lane < POS) & (lane == position))
        | (between(lane, Y0, Y0 + COORD) & (lane - Y0 == down))
        | (named & between(lane, GROUP0, MEMBER0) & (lane - GROUP0 == group))
        | (named & between(lane, MEMBER0, FLAG) & (lane - MEMBER0 == member))
        | ((lane == FLAG) & (key_mask <= 0))
        | (lane == EVERY)
        | ((lane == STRAY) & (segment < 0))
    )
    return tuple(jnp.where(m, 1.0, 0.0).astype(BF) for m in (even, odd, shared))


def square_lanes():
    shape = (LANES, LANES)
    return lax.broadcasted_iota(jnp.int32, shape, 0), lax.broadcasted_iota(jnp.int32, shape, 1)


def barred():
    row, lane = square_lanes()
    in_groups = between(lane, GROUP0, MEMBER0)
    shut = (
        (between(row, GROUP0, MEMBER0) & in_groups & (lane != row))
        | (between(row, MEMBER0, FLAG) & between(lane, MEMBER0, FLAG) & (lane != row))
        | ((row == EVERY) & (lane == FLAG))
        | ((row == STRAY) & in_groups)
    )
    return jnp.where(shut, -BIG, 0.0).astype(F32)


def table_index():
    row, lane = square_lanes()
    distance = bucket(row - lane)
    inside = lambda low, high: between(row, low, high) & between(lane, low, high)
    even = jnp.where(inside(HEAD, HEAD + COORD), distance + X_TABLE, NOTHING)
    odd = jnp.where(inside(0, COORD), distance + X_TABLE, NOTHING)
    shared = jnp.where(
        inside(0, POS), distance, jnp.where(inside(Y0, Y0 + COORD), distance + Y_TABLE, NOTHING)
    )
    return even, odd, shared


def image_query_index(meta_ref):
    position = meta_ref[TEXT:, 2:3]
    lane = lax.broadcasted_iota(jnp.int32, (position.shape[0], LANES), 1)
    return jnp.where(lane < POS, bucket(position - lane), NOTHING)


def prepare(meta_ref, mark_refs, bar_ref, index_refs, image_index_ref):
    for ref, value in zip(mark_refs, marks(meta_ref)):
        ref[...] = value
    bar_ref[...] = barred()
    for ref, value in zip(index_refs, table_index()):
        ref[...] = value
    image_index_ref[...] = image_query_index(meta_ref)


def own_lanes(parity, rows):
    lane = lax.broadcasted_iota(jnp.int32, (rows, LANES), 1)
    return (lane < HEAD) if parity == 0 else (lane >= HEAD)


def widened(parity, q, table_row, bias, bar_ref, index_refs, image_index_ref, mark_refs):
    rows = q.shape[0]
    shared = mark_refs[2][...]
    across = looked_up(table_row, index_refs[parity][...]).astype(BF)
    first = jnp.where(
        own_lanes(parity, rows), q.astype(F32) * 0.125, dot_nn(mark_refs[parity][...], across)
    )
    others = (looked_up(table_row, index_refs[2][...]) + bar_ref[...]).astype(BF)
    second = dot_nn(shared, others)
    on_images = looked_up(table_row, image_index_ref[...])
    second = jnp.concatenate([second[:TEXT], second[TEXT:] + on_images], axis=0)
    image_lane = lax.broadcasted_iota(jnp.int32, on_images.shape, 1)
    key_image = jnp.where(image_lane < POS, bias[:, :LANES].astype(BF), shared[TEXT:])
    return first.astype(BF), second.astype(BF), key_image


def joined(parity, first, second, key_image, k, marks_own, shared):
    rows = k.shape[0]
    lane = lax.broadcasted_iota(jnp.int32, (rows, LANES), 1)
    to_image = jnp.where(lane < POS, shared, second)
    key_first = jnp.where(own_lanes(parity, rows), k, marks_own)
    q_text = jnp.concatenate([first, second], axis=1)
    q_image = jnp.concatenate([first, to_image], axis=1)
    k_text = jnp.concatenate([key_first[:TEXT], shared[:TEXT]], axis=1)
    k_image = jnp.concatenate([key_first[TEXT:], key_image], axis=1)
    return q_text, q_image, k_text, k_image


def near(start, size):
    if start >= TEXT:
        return slice(0, TEXT)
    return slice(max(0, start - LANES), min(TEXT, start + size + LANES))


def image_bias(table_row, offsets):
    return jnp.concatenate(
        [looked_up(table_row, offsets[:, :LANES]), looked_up(table_row, offsets[:, LANES:])], axis=1
    )


def forward_kernel(
    meta_ref, rows_ref, table_ref, q_ref, k_ref, v_ref,
    mixed_ref, log_ref, first_ref, second_ref, key_image_ref, bias_ref,
    even_ref, odd_ref, shared_ref, bar_ref, index_even, index_odd, index_shared, image_index_ref,
):
    mark_refs = (even_ref, odd_ref, shared_ref)
    index_refs = (index_even, index_odd, index_shared)

    @pl.when(pl.program_id(0) == 0)
    def _():
        prepare(meta_ref, mark_refs, bar_ref, index_refs, image_index_ref)

    rows = q_ref.shape[0]
    images = rows - TEXT
    q, k, v = q_ref[...], k_ref[...], v_ref[...]
    offsets = bucket(rows_ref[2:3, TEXT:] - meta_ref[TEXT:, 2:3])
    tile = 256
    v_turned = transposed(v)
    heads = [None, None]

    def prepared(parity):
        table_row = table_ref[pl.ds(2 * pl.program_id(0) + parity, 1), :]
        bias = image_bias(table_row, offsets)
        first, second, key_image = widened(
            parity, q, table_row, bias, bar_ref, index_refs, image_index_ref, mark_refs
        )
        first_ref[parity] = first
        second_ref[parity] = second
        key_image_ref[parity] = key_image
        bias_ref[parity] = bias.astype(BF)
        wide = joined(
            parity, first, second, key_image, k, mark_refs[parity][...], shared_ref[...]
        )
        heads[parity] = wide + (bias,)

    def scored(parity, start):
        q_text, q_image, k_text, k_image, bias = heads[parity]
        here = slice(start, start + tile)
        on_image = dot_nt(k_image, q_image[here])
        if start >= TEXT:
            on_image = on_image + bias[:, start - TEXT : start - TEXT + tile]
        return dot_nt(k_text[near(start, tile)], q_text[here]), on_image

    spots = [(parity, start) for parity in range(2) for start in range(0, rows, tile)]
    outs = ([], [])
    prepared(0)
    following = scored(*spots[0])
    for index, (parity, start) in enumerate(spots):
        on_text, on_image = following
        if index == 1:
            prepared(1)
        if index + 1 < len(spots):
            following = scored(*spots[index + 1])
        top = jnp.maximum(
            jnp.max(on_text, axis=0, keepdims=True), jnp.max(on_image, axis=0, keepdims=True)
        )
        on_text = jnp.exp(on_text - top)
        on_image = jnp.exp(on_image - top)
        total = jnp.sum(on_text, axis=0, keepdims=True) + jnp.sum(on_image, axis=0, keepdims=True)
        own = slice(parity * HEAD, parity * HEAD + HEAD)
        out = dot_nn(v_turned[own, near(start, tile)], on_text.astype(BF)) + dot_nn(
            v_turned[own, TEXT:], on_image.astype(BF)
        )
        outs[parity].append(out * (1.0 / total))
        log_ref[0, parity : parity + 1, start : start + tile] = top + jnp.log(total)
    mixed_ref[...] = jnp.transpose(
        jnp.concatenate([jnp.concatenate(outs[parity], axis=1) for parity in range(2)], axis=0)
    )


def static_scratch(rows):
    square = (LANES, LANES)
    return [
        pltpu.VMEM((rows, LANES), BF),
        pltpu.VMEM((rows, LANES), BF),
        pltpu.VMEM((rows, LANES), BF),
        pltpu.VMEM(square, F32),
        pltpu.VMEM(square, jnp.int32),
        pltpu.VMEM(square, jnp.int32),
        pltpu.VMEM(square, jnp.int32),
        pltpu.VMEM((rows - TEXT, LANES), jnp.int32),
    ]


def attention_forward(meta_columns, meta_rows, table_rows, projected, width):
    rows = projected.shape[0]
    images = rows - TEXT
    pairs = width // LANES

    def block(part):
        return pl.BlockSpec((rows, LANES), lambda p: (0, part * pairs + p))

    whole = lambda shape: pl.BlockSpec(shape, lambda p: (0,) * len(shape))
    return pl.pallas_call(
        forward_kernel,
        grid=(pairs,),
        in_specs=[
            whole(meta_columns.shape),
            whole(meta_rows.shape),
            whole(table_rows.shape),
            block(0), block(1), block(2),
        ],
        out_specs=[
            pl.BlockSpec((rows, LANES), lambda p: (0, p)),
            pl.BlockSpec((1, 2, rows), lambda p: (p, 0, 0)),
            pl.BlockSpec((2, rows, LANES), lambda p: (p, 0, 0)),
            pl.BlockSpec((2, rows, LANES), lambda p: (p, 0, 0)),
            pl.BlockSpec((2, images, LANES), lambda p: (p, 0, 0)),
            pl.BlockSpec((2, images, images), lambda p: (p, 0, 0)),
        ],
        out_shape=[
            jax.ShapeDtypeStruct((rows, width), F32),
            jax.ShapeDtypeStruct((pairs, 2, rows), F32),
            jax.ShapeDtypeStruct((2 * pairs, rows, LANES), BF),
            jax.ShapeDtypeStruct((2 * pairs, rows, LANES), BF),
            jax.ShapeDtypeStruct((2 * pairs, images, LANES), BF),
            jax.ShapeDtypeStruct((2 * pairs, images, images), BF),
        ],
        scratch_shapes=static_scratch(rows),
        compiler_params=pltpu.CompilerParams(vmem_limit_bytes=60 * 1024 * 1024),
        name="attention_forward",
    )(meta_columns, meta_rows, table_rows, projected, projected, projected)


def skewed(block):
    size = block.shape[0]
    lane = lax.broadcasted_iota(jnp.int32, (size, LANES), 1)
    row = lax.broadcasted_iota(jnp.int32, (size, LANES), 0)
    turned = jnp.take_along_axis(
        block, (lane + row) & (LANES - 1), axis=1, mode="promise_in_bounds"
    )
    straight = lane + row < LANES
    above = jnp.sum(jnp.where(straight, turned, 0.0), axis=0, keepdims=True)
    below = jnp.sum(jnp.where(straight, 0.0, turned), axis=0, keepdims=True)
    return above, below


def transposed(array):
    return jnp.transpose(array.astype(F32)).astype(array.dtype)


def static_prepare(meta_ref, static):
    for ref, turned, value in zip(static[:3], static[3:], marks(meta_ref)):
        ref[...] = value
        turned[...] = transposed(value)


def head_back(
    parity, pair, rows_ref, wide_refs, k_ref, v_ref, mixed_ref, grad_ref, log_ref, static, diag_ref,
):
    mark_refs, turned_refs = static[:3], static[3:]
    first_ref, second_ref, key_image_ref, bias_ref = wide_refs
    head = 2 * pair + parity
    shared_t = turned_refs[2]
    rows = k_ref.shape[1]
    images = rows - TEXT
    tile = 256
    k, v, grad = k_ref[pair], v_ref[pair], grad_ref[pair]
    products = grad.astype(F32) * mixed_ref[pair]
    k_turned = transposed(k)
    is_image = rows_ref[1:2, TEXT:] > 0
    own = own_lanes(parity, rows)
    log_row = log_ref[pair, parity : parity + 1, :]
    first, shared = first_ref[head], mark_refs[2][...]
    q_text, q_image, k_text, k_image = joined(
        parity, first, second_ref[head], key_image_ref[head], k, mark_refs[parity][...], shared
    )
    bias = bias_ref[head].astype(F32)
    ones = jnp.where(own_lanes(parity, 8), 1.0, 0.0).astype(BF)
    delta = jnp.zeros((8, rows), F32)
    rest = products
    for _ in range(3):
        piece = rest.astype(BF)
        delta = delta + dot_nt(ones, piece)
        rest = rest - piece.astype(F32)
    delta = delta[0:1]
    v_own = jnp.where(own, v, jnp.zeros_like(v))
    q_marked = jnp.concatenate(
        [jnp.where(own, first, mark_refs[parity][...]), shared], axis=1
    )
    dq_text = jnp.zeros((HEAD, TEXT), F32)
    dq_image = jnp.zeros((HEAD, images), F32)
    dks = []
    dvs = []
    first_sum = jnp.zeros((LANES, LANES), F32)
    second_sum = jnp.zeros((LANES, LANES), F32)
    text_image = jnp.zeros((LANES, images), F32)

    def met(start, array, axis=0):
        text = near(start, tile)
        if axis == 0:
            return jnp.concatenate([array[text], array[TEXT:]], axis=0)
        return jnp.concatenate([array[:, text], array[:, TEXT:]], axis=1)

    def scored(start):
        here = slice(start, start + tile)
        if start < TEXT:
            scores = dot_nt(k_text[here], met(start, q_text))
        else:
            scores = dot_nt(k_image[start - TEXT : start - TEXT + tile], q_image)
            scores = jnp.concatenate([scores[:, :TEXT], scores[:, TEXT:] + bias], axis=1)
        return scores, dot_nt(v_own[here], met(start, grad))

    following = scored(0)
    for start in range(0, rows, tile):
        here = slice(start, start + tile)
        scores, prob_grad = following
        if start + tile < rows:
            following = scored(start + tile)
        soft = jnp.exp(scores - met(start, log_row, 1))
        score_grad = soft * (prob_grad - met(start, delta, 1))
        low = score_grad.astype(BF)
        dvs.append(dot_nn(soft.astype(BF), met(start, grad)))
        wide = dot_nn(low, met(start, q_marked))
        dks.append(wide[:, :LANES])
        part = dot_nn(k_turned[parity * HEAD : parity * HEAD + HEAD, here], low)
        text = near(start, tile)
        count = text.stop - text.start
        before = [jnp.zeros((HEAD, text.start), F32)] if text.start > 0 else []
        after = [jnp.zeros((HEAD, TEXT - text.stop), F32)] if text.stop < TEXT else []
        dq_text = dq_text + jnp.concatenate(before + [part[:, :count]] + after, axis=1)
        dq_image = dq_image + part[:, count:]
        rounded = wide.astype(BF)
        first_sum = first_sum + dot_nn(turned_refs[parity][:, here], rounded[:, :LANES])
        second_sum = second_sum + dot_nn(shared_t[:, here], rounded[:, LANES:])
        if start < TEXT:
            text_image = text_image + dot_nn(shared_t[:, here], low[:, count:])
        else:
            by_position = wide[:, LANES:]
            on_image = score_grad[:, TEXT:]
    dq = jnp.concatenate([dq_text, dq_image], axis=1)
    small = lax.broadcasted_iota(jnp.int32, (LANES, LANES), 1)
    small_row = lax.broadcasted_iota(jnp.int32, (LANES, LANES), 0)
    x0 = HEAD if parity == 0 else 0
    x_block = jnp.where(
        between(small, x0, x0 + COORD) & between(small_row, x0, x0 + COORD), first_sum, 0.0
    )
    y_block = jnp.where(
        between(small, Y0, Y0 + COORD) & between(small_row, Y0, Y0 + COORD), second_sum, 0.0
    )
    p_block = jnp.where((small < POS) & (small_row < POS), second_sum, 0.0)
    wide_lane = lax.broadcasted_iota(jnp.int32, (images, images), 1)
    outside = jnp.sum(jnp.where(is_image, 0.0, on_image), axis=1, keepdims=True)
    pairs = jnp.where(is_image, on_image, 0.0) + jnp.where(wide_lane == 0, outside, 0.0)
    outside_text = jnp.sum(jnp.where(is_image, 0.0, text_image), axis=1, keepdims=True)
    text_lane = lax.broadcasted_iota(jnp.int32, (LANES, images), 1)
    text_row = lax.broadcasted_iota(jnp.int32, (LANES, images), 0)
    text_image = jnp.where(is_image, text_image, 0.0) + jnp.where(
        text_lane == 0, outside_text, 0.0
    )
    text_image = jnp.where(text_row < POS, text_image, 0.0)
    first_lane = lax.broadcasted_iota(jnp.int32, (images, LANES), 1)
    left = pairs[:, :LANES] + jnp.where(first_lane < POS, by_position, 0.0)
    right = pairs[:, LANES:]
    a00, b00 = skewed(left[:LANES] + text_image[:, :LANES] + p_block)
    a01, b01 = skewed(right[:LANES] + text_image[:, LANES:])
    a10, b10 = skewed(left[LANES:])
    a11, b11 = skewed(right[LANES:])
    ax, bx = skewed(x_block)
    ay, by = skewed(y_block)
    diag_ref[head] = jnp.concatenate(
        [b10, b00 + b11 + a10, a00 + a11 + b01, a01, bx, ax, by, ay], axis=0
    )
    return dq * 0.125, jnp.concatenate(dks, axis=0), jnp.concatenate(dvs, axis=0)


MESH = pl.DeviceIdType.MESH
VMEM = pl.BlockSpec(memory_space=pltpu.VMEM)
HBM = pl.BlockSpec(memory_space=pltpu.HBM)
MIB = 1024 * 1024


def remote(src, dst, send, receive, device):
    return pltpu.make_async_remote_copy(
        src_ref=src, dst_ref=dst, send_sem=send, recv_sem=receive, device_id=device,
        device_id_type=MESH,
    )


def project_kernel(
    layer_ref, weight_hbm, *refs,
):
    small_hbm, refs = refs[:10], refs[10:]
    (item_ref, projected_out, columns_ref, rows_ref, table_ref,
     projected_ref, weight_ref, meta_send, bias_ref, sems, load_sems, store_sems), small = (
        refs[:12], refs[12:],
    )
    (segment_ref, mask_ref, position_ref, across_ref, down_ref, query_bias_ref, value_bias_ref,
     text_ref, horiz_ref, vert_ref) = small
    mine = lax.axis_index("seq")
    partner = (1 - mine, lax.axis_index("dp"))
    count, width = layer_ref.shape[1:]
    own = pl.ds(pl.multiple_of(mine * count, LANES), count)
    loads = [
        pltpu.make_async_copy(source, target, load_sems.at[index])
        for index, (source, target) in enumerate(
            list(zip(small_hbm, small))
            + [(layer_ref.at[mine], item_ref.at[own]), (weight_hbm, weight_ref)]
        )
    ]
    for load in loads:
        load.start()
    barrier = pltpu.get_barrier_semaphore()
    pl.semaphore_signal(barrier, inc=1, device_id=partner, device_id_type=MESH)
    pl.semaphore_wait(barrier, 1)
    pieces = count // LANES
    rows_out = [
        remote(
            layer_ref.at[1 - mine, pl.ds(piece * LANES, LANES)],
            item_ref.at[pl.ds(pl.multiple_of(mine * count + piece * LANES, LANES), LANES)],
            sems.at[0, piece], sems.at[1, piece], partner,
        )
        for piece in range(pieces)
    ]
    for copy in rows_out:
        copy.start()
    for load in loads[:-2]:
        load.wait()

    fields = (segment_ref, mask_ref, position_ref, across_ref, down_ref)
    blocks = [
        jnp.concatenate(
            [field[item : item + 1, :] for field in fields] + [jnp.zeros((3, count), jnp.int32)],
            axis=0,
        )
        for item in range(2)
    ]
    meta_send[...] = jnp.where(mine == 0, blocks[1], blocks[0])
    meta_out = remote(
        meta_send, rows_ref.at[:, own], sems.at[0, pieces], sems.at[1, pieces], partner
    )
    meta_out.start()
    rows_ref[:, own] = jnp.where(mine == 0, blocks[0], blocks[1])
    bias_ref[:, :width] = query_bias_ref[...].astype(F32).reshape(1, width)
    bias_ref[:, width : 2 * width] = jnp.zeros((1, width), F32)
    bias_ref[:, 2 * width :] = value_bias_ref[...].astype(F32).reshape(1, width)
    heads, levels = text_ref.shape
    spot = lax.broadcasted_iota(jnp.int32, (levels, LANES), 1)
    level = lax.broadcasted_iota(jnp.int32, (levels, LANES), 0)
    table = jnp.zeros((heads, LANES), F32)
    for source, begin in ((text_ref, 0), (horiz_ref, X_TABLE), (vert_ref, Y_TABLE)):
        table = table + dot_nn(source[...], (spot == level + begin).astype(BF))
    table_ref[...] = jnp.concatenate([table, jnp.zeros((16 - heads, LANES), F32)], axis=0)

    def project(there):
        step = 256

        def body(index, carry):
            columns = pl.ds(pl.multiple_of(index * step, step), step)
            product = dot_nn(item_ref[there], weight_ref[:, columns])
            projected_ref[there, columns] = (product + bias_ref[:, columns]).astype(BF)
            return carry

        lax.fori_loop(0, 3 * width // step, body, 0)

    def stored(index, there):
        return pltpu.make_async_copy(
            projected_ref.at[there], projected_out.at[there], store_sems.at[index]
        )

    for load in loads[-2:]:
        load.wait()
    project(own)
    stored(0, own).start()
    for piece in range(pieces):
        rows_out[piece].wait()
        there = pl.ds(pl.multiple_of((1 - mine) * count + piece * LANES, LANES), LANES)
        project(there)
        stored(1 + piece, there).start()
    meta_out.wait()
    meta = rows_ref[...].astype(F32)
    tall = jnp.concatenate([meta, jnp.zeros((LANES - 8, meta.shape[1]), F32)], axis=0)
    columns_ref[...] = jnp.transpose(tall).astype(jnp.int32)
    stored(0, own).wait()
    for piece in range(pieces):
        there = pl.ds(pl.multiple_of((1 - mine) * count + piece * LANES, LANES), LANES)
        stored(1 + piece, there).wait()


def projected_item(layer_in, fields, qkv_weight, query_bias, value_bias, tables):
    rows = 2 * layer_in.shape[1]
    width = layer_in.shape[2]
    pieces = rows // 2 // LANES
    small = list(fields) + [query_bias, value_bias] + [t.T for t in tables]
    return pl.pallas_call(
        project_kernel,
        in_specs=[HBM] * (2 + len(small)),
        out_specs=[VMEM, HBM, VMEM, VMEM, VMEM],
        out_shape=[
            jax.ShapeDtypeStruct((rows, width), BF),
            jax.ShapeDtypeStruct((rows, 3 * width), BF),
            jax.ShapeDtypeStruct((rows, LANES), jnp.int32),
            jax.ShapeDtypeStruct((8, rows), jnp.int32),
            jax.ShapeDtypeStruct((16, LANES), F32),
        ],
        scratch_shapes=[
            pltpu.VMEM((rows, 3 * width), BF),
            pltpu.VMEM((width, 3 * width), BF),
            pltpu.VMEM((8, rows // 2), jnp.int32),
            pltpu.VMEM((1, 3 * width), F32),
            pltpu.SemaphoreType.DMA((2, pieces + 1)),
            pltpu.SemaphoreType.DMA((len(small) + 2,)),
            pltpu.SemaphoreType.DMA((pieces + 1,)),
        ]
        + [pltpu.VMEM(array.shape, array.dtype) for array in small],
        compiler_params=pltpu.CompilerParams(
            collective_id=1, has_side_effects=True, vmem_limit_bytes=60 * MIB
        ),
        name="projected_item",
    )(layer_in, qkv_weight, *small)


EPSILON = 1e-05
TILE = 256


def vector(ref):
    return ref[...].astype(F32).reshape(1, ref.shape[0])


def gelu_and_slope(x):
    bell = jnp.exp2(-0.7213475204444817 * (x * x))
    rough = 1.0 + 0.23164188826 * jnp.abs(x)
    t = pl.reciprocal(rough, approx=True)
    t = t * (2.0 - rough * t)
    series = t * (
        0.127414796
        + t * (-0.142248368 + t * (0.7107068705 + t * (-0.7265760135 + t * 0.5307027145)))
    )
    tail = bell * series
    below = jnp.where(x >= 0.0, 1.0 - tail, tail)
    return x * below, below + x * (0.3989422804014327 * bell)


def row_mean(block):
    return jnp.mean(block, axis=1, keepdims=True)


def normalized(hidden):
    center = hidden - row_mean(hidden)
    scale = lax.rsqrt(row_mean(center * center) + EPSILON)
    return center * scale, scale


def norm_pulled(grad, unit, scale):
    return scale * (grad - row_mean(grad) - unit * row_mean(grad * unit))


def column_sum(block):
    return jnp.sum(block, axis=0, keepdims=True)


def feed_kernel(
    item_hbm, mixed_hbm, cotangent_ref, out_weight_ref, up_ref, down_ref, *refs,
):
    vectors_hbm, refs = refs[:7], refs[7:]
    (layer_out, total_out, unit_out, scale_out, grad_down_ref, grad_up_ref, small_ref,
     item_ref, mixed_ref, layer_ref, cotangent_all, active, slope, unit, scale_ref, normed, normed_t, total, d_branch, d_branch_t,
     sems, load_sems, tile_sems, store_sems) = refs[:24]
    vectors = refs[24:]
    (out_bias_ref, attn_gain_ref, attn_shift_ref, up_bias_ref, down_bias_ref, ffn_gain_ref,
     ffn_shift_ref) = vectors
    step = pl.program_id(0)
    blocks = pl.num_programs(0) // 2
    rows, width = item_hbm.shape
    count = rows // 2
    mine = lax.axis_index("seq")
    partner = (1 - mine, lax.axis_index("dp"))
    own = pl.ds(pl.multiple_of(mine * count, LANES), count)
    tiles = rows // TILE

    def sent():
        return remote(
            cotangent_ref.at[1 - mine], cotangent_all.at[own], sems.at[0], sems.at[1], partner
        )

    def returned():
        theirs = pl.ds(pl.multiple_of((1 - mine) * count, LANES), count)
        return [
            pltpu.make_async_copy(layer_ref.at[own], layer_out.at[mine], load_sems.at[8]),
            remote(
                layer_ref.at[theirs], layer_out.at[mine], sems.at[2], sems.at[3], partner
            ),
        ]

    def tile_loads(tile):
        there = pl.ds(tile * TILE, TILE)
        return [
            pltpu.make_async_copy(source.at[there], target.at[there], tile_sems.at[index, tile])
            for index, (source, target) in enumerate(
                ((mixed_hbm, mixed_ref), (item_hbm, item_ref))
            )
        ]

    def store(index):
        source, target = (
            (total, total_out), (unit, unit_out), (scale_ref, scale_out),
        )[index]
        return pltpu.make_async_copy(source, target, store_sems.at[index])

    def loads():
        copies = list(zip(vectors_hbm, vectors)) + [(cotangent_ref.at[mine], cotangent_all.at[own])]
        return [
            pltpu.make_async_copy(source, target, load_sems.at[index])
            for index, (source, target) in enumerate(copies)
        ]

    def over_tiles(size, body, carry, unroll=1):
        def run(index, state):
            return body(pl.ds(pl.multiple_of(index * size, size), size), state)

        return lax.fori_loop(0, rows // size, run, carry, unroll=unroll)

    @pl.when(step == 0)
    def _():
        for index in range(rows // TILE):
            for load in tile_loads(index):
                load.start()
        for load in loads():
            load.start()
        barrier = pltpu.get_barrier_semaphore()
        pl.semaphore_signal(barrier, inc=1, device_id=partner, device_id_type=MESH)
        pl.semaphore_wait(barrier, 1)
        sent().start()
        small_ref[...] = jnp.zeros_like(small_ref)
        for load in loads():
            load.wait()
        out_bias, gain, shift = vector(out_bias_ref), vector(attn_gain_ref), vector(attn_shift_ref)

        for index in range(rows // TILE):
            for load in tile_loads(index):
                load.wait()
            there = slice(index * TILE, index * TILE + TILE)
            attn = dot_nn(mixed_ref[there].astype(BF), out_weight_ref[...]) + out_bias
            standard, scale = normalized(item_ref[there].astype(F32) + attn)
            unit[there] = standard
            scale_ref[there] = jnp.broadcast_to(scale, (TILE, LANES))
            result = standard * gain + shift
            normed[there] = result.astype(BF)
            normed_t[:, there] = jnp.transpose(result).astype(BF)
        store(1).start()
        store(2).start()
        total[...] = jnp.zeros_like(total)

    @pl.when(step < blocks)
    def _():
        columns = [slice(begin, begin + TILE) for begin in range(0, width, TILE)]
        low = normed[...]
        following = dot_nn(low, up_ref[:, columns[0]])
        values = []
        for index, here in enumerate(columns):
            product = following
            if index + 1 < len(columns):
                following = dot_nn(low, up_ref[:, columns[index + 1]])
            bias = up_bias_ref[pl.ds(pl.multiple_of(step * width + here.start, LANES), TILE)]
            value, grade = gelu_and_slope(product + bias.astype(F32).reshape(1, TILE))
            values.append(value.astype(BF))
            active[step, :, here] = values[-1]
            slope[step, :, here] = grade.astype(BF)
        values = jnp.concatenate(values, axis=1)
        for here in columns:
            total[:, here] += dot_nn(values, down_ref[:, here])

    @pl.when(step == blocks)
    def _():
        sent().wait()
        gain, shift, bias = vector(ffn_gain_ref), vector(ffn_shift_ref), vector(down_bias_ref)
        first_gain, first_shift = vector(attn_gain_ref), vector(attn_shift_ref)

        def tile(there, sums):
            hidden = unit[there] * first_gain + first_shift + (total[there] + bias)
            standard, scale = normalized(hidden)
            layer_ref[there] = (standard * gain + shift).astype(BF)
            cotangent = cotangent_all[there].astype(F32)
            pulled = norm_pulled(cotangent * gain, standard, scale)
            total[there] = pulled
            low = pulled.astype(BF)
            d_branch[there] = low
            return (
                sums[0] + column_sum(low.astype(F32)),
                sums[1] + column_sum(cotangent * standard),
                sums[2] + column_sum(cotangent),
            )

        zero = jnp.zeros((1, width), F32)
        sums = over_tiles(64, tile, (zero, zero, zero), 4)
        for row, value in zip((5, 6, 7), sums):
            small_ref[row : row + 1] = value

        for copy in returned():
            copy.start()

        def turn(there, carry):
            d_branch_t[:, there] = jnp.transpose(d_branch[there].astype(F32)).astype(BF)
            return carry

        over_tiles(TILE, turn, 0, 3)

    @pl.when(step >= blocks)
    def _():
        block = step - blocks

        columns = [slice(begin, begin + TILE) for begin in range(0, width, TILE)]
        branch = d_branch[...]
        turned = d_branch_t[...]
        following = dot_nt(branch, down_ref[columns[0]])
        values = []
        for index, here in enumerate(columns):
            product = following
            if index + 1 < len(columns):
                following = dot_nt(branch, down_ref[columns[index + 1]])
            grad_down_ref[:, here] = dot_nn(turned, active[block, :, here]).astype(BF)
            d_up = (product * slope[block, :, here].astype(F32)).astype(BF)
            small_ref[pl.ds(8 + block, 1), here] = column_sum(d_up.astype(F32))
            values.append(d_up)
        values = jnp.concatenate(values, axis=1)
        turned = normed_t[...]
        for here in columns:
            grad_up_ref[:, here] = dot_nn(turned, values[:, here]).astype(BF)
            total[:, here] += dot_nt(values, up_ref[here])

    @pl.when(step == 2 * blocks - 1)
    def _():
        store(0).start()
        for copy in returned() + [store(0), store(1), store(2)]:
            copy.wait()


def fed_forward_and_back(
    item, mixed, cotangent, out_weight, up_weight, down_weight, vectors,
):
    rows, width = item.shape
    blocks = up_weight.shape[1] // width
    whole = pl.BlockSpec(memory_space=pltpu.VMEM)
    square = lambda kind: jax.ShapeDtypeStruct((rows, width), kind)
    later = lambda i: jnp.maximum(i - blocks, 0)
    return pl.pallas_call(
        feed_kernel,
        grid=(2 * blocks,),
        in_specs=[HBM, HBM, HBM, whole]
        + [
            pl.BlockSpec((width, width), lambda i: (0, lax.rem(i, blocks))),
            pl.BlockSpec((width, width), lambda i: (lax.rem(i, blocks), 0)),
        ]
        + [HBM] * 7,
        out_specs=[HBM] * 4
        + [
            pl.BlockSpec((width, width), lambda i: (later(i), 0)),
            pl.BlockSpec((width, width), lambda i: (later(i), 0)),
            whole,
        ],
        out_shape=[
            jax.ShapeDtypeStruct((2, rows // 2, width), BF), square(F32), square(F32),
            jax.ShapeDtypeStruct((rows, LANES), F32),
            jax.ShapeDtypeStruct((blocks * width, width), BF),
            jax.ShapeDtypeStruct((blocks * width, width), BF),
            jax.ShapeDtypeStruct((16, width), F32),
        ],
        scratch_shapes=[
            pltpu.VMEM((rows, width), BF),
            pltpu.VMEM((rows, width), F32),
            pltpu.VMEM((rows, width), BF),
            pltpu.VMEM((rows, width), BF),
            pltpu.VMEM((blocks, rows, width), BF),
            pltpu.VMEM((blocks, rows, width), BF),
            pltpu.VMEM((rows, width), F32),
            pltpu.VMEM((rows, LANES), F32),
            pltpu.VMEM((rows, width), BF),
            pltpu.VMEM((width, rows), BF),
            pltpu.VMEM((rows, width), F32),
            pltpu.VMEM((rows, width), BF),
            pltpu.VMEM((width, rows), BF),
            pltpu.SemaphoreType.DMA((4,)),
            pltpu.SemaphoreType.DMA((9,)),
            pltpu.SemaphoreType.DMA((2, rows // TILE)),
            pltpu.SemaphoreType.DMA((3,)),
        ]
        + [pltpu.VMEM(vector.shape, vector.dtype) for vector in vectors],
        compiler_params=pltpu.CompilerParams(
            collective_id=2, has_side_effects=True, vmem_limit_bytes=60 * MIB
        ),
        name="feed_forward",
    )(item, mixed, cotangent, out_weight, up_weight, down_weight, *vectors)


SLOTS = 4


def finish_kernel(
    main_ref, tail_ref, input_hbm, small_ref, diagonal_ref,
    down_ref, up_ref, out_ref, qkv_ref, input_ref, *refs,
):
    singles, (main_in, tail_in, slots, input_in, input_slot, in_sems, out_sems, item_sems) = (
        refs[:12], refs[12:],
    )
    mains, width = main_in.shape[0], main_in.shape[2]
    pairs, across = tail_in.shape[0], tail_in.shape[2]
    hidden = mains // 2
    blocks = mains + pairs

    def load(block):
        if block < mains:
            source, target = main_ref.at[pl.ds(block * width, width)], main_in.at[block]
        else:
            pair = block - mains
            source, target = tail_ref.at[pl.ds(pair * TAIL_ROWS, TAIL_ROWS)], tail_in.at[pair]
        return pltpu.make_async_copy(source, target, in_sems.at[block])

    def stores(block):
        slot, sem = slots.at[block % SLOTS], out_sems.at[block % SLOTS]
        if block < hidden:
            targets = [(slot, down_ref.at[pl.ds(block * width, width)])]
        elif block < mains:
            targets = [(slot, up_ref.at[:, pl.ds((block - hidden) * width, width)])]
        else:
            pair = block - mains
            targets = [
                (
                    slot.at[:, pl.ds(part * LANES, LANES)],
                    qkv_ref.at[:, pl.ds(part * width + pair * LANES, LANES)],
                )
                for part in range(3)
            ]
            down = pl.ds(0, TAIL_ROWS - width)
            targets.append(
                (slot.at[down, pl.ds(across, across)], out_ref.at[out_spot(pair, pairs, width)])
            )
        return [
            pltpu.make_async_copy(source, target, sem.at[index])
            for index, (source, target) in enumerate(targets)
        ]

    load_input = pltpu.make_async_copy(input_hbm, input_in, item_sems.at[0])
    store_input = pltpu.make_async_copy(input_slot, input_ref, item_sems.at[1])
    for block in range(blocks):
        load(block).start()
    load_input.start()
    for block in range(blocks):
        load(block).wait()
        if block >= SLOTS:
            for copy in stores(block - SLOTS):
                copy.wait()
        slot = block % SLOTS
        if block < hidden:
            slots[slot] = jnp.transpose(main_in[block].astype(F32))
        elif block < mains:
            slots[slot] = main_in[block].astype(F32)
        else:
            slots[slot, :, :across] = tail_in[block - mains, :width].astype(F32)
            slots[slot, : TAIL_ROWS - width, across:] = tail_in[block - mains, width:].astype(F32)
        for copy in stores(block):
            copy.start()
    load_input.wait()
    input_slot[...] = input_in[...].astype(F32)
    store_input.start()
    for row in range(8):
        singles[row][...] = small_ref[row]
    for row in range(hidden):
        singles[8][row * width : row * width + width] = small_ref[8 + row]
    heads, levels = singles[9].shape
    diagonals = diagonal_ref[...]
    level = lax.broadcasted_iota(jnp.int32, (LANES, LANES), 1)
    lane = lax.broadcasted_iota(jnp.int32, (LANES, LANES), 0)
    for table, (first, size, skip) in enumerate(((0, 4, 0), (4, 2, 1), (6, 2, 1))):
        total = jnp.zeros((heads, LANES), F32)
        for row in range(size):
            distance = lane + LANES * (row + skip - 2)
            chosen = (bucket(distance) == level).astype(F32)
            total = total + jnp.dot(
                diagonals[:, first + row, :], chosen, preferred_element_type=F32,
                precision=lax.Precision.HIGHEST,
            )
        singles[9 + table][...] = total[:, :levels]
    for block in range(blocks - SLOTS, blocks):
        for copy in stores(block):
            copy.wait()
    store_input.wait()


def finished(main, tail, grad_input, small, diagonals, hidden, levels):
    width = main.shape[1]
    heads = diagonals.shape[0]
    mains = main.shape[0] // width
    pairs = tail.shape[0] // TAIL_ROWS
    single = jax.ShapeDtypeStruct((width,), F32)
    table = jax.ShapeDtypeStruct((heads, levels), F32)
    dma = pltpu.SemaphoreType.DMA
    return pl.pallas_call(
        finish_kernel,
        in_specs=[HBM, HBM, HBM, VMEM, VMEM],
        out_specs=[HBM] * 5 + [VMEM] * 12,
        out_shape=[
            jax.ShapeDtypeStruct((hidden, width), F32),
            jax.ShapeDtypeStruct((width, hidden), F32),
            jax.ShapeDtypeStruct((width, width), F32),
            jax.ShapeDtypeStruct((width, 3 * width), F32),
            jax.ShapeDtypeStruct(grad_input.shape, F32),
        ]
        + [single] * 8
        + [jax.ShapeDtypeStruct((hidden,), F32)]
        + [table] * 3,
        scratch_shapes=[
            pltpu.VMEM((mains, width, width), BF),
            pltpu.VMEM((pairs, TAIL_ROWS, tail.shape[1]), BF),
            pltpu.VMEM((SLOTS, width, width), F32),
            pltpu.VMEM(grad_input.shape, BF),
            pltpu.VMEM(grad_input.shape, F32),
            dma((mains + pairs,)),
            dma((SLOTS, 4)),
            dma((2,)),
        ],
        compiler_params=pltpu.CompilerParams(vmem_limit_bytes=56 * MIB),
        name="finished",
    )(main, tail, grad_input, small, diagonals)


PIECE = 16


class Place:
    def __init__(self, depth):
        place = lax.axis_index("dp")
        self.depth = depth
        self.group = lax.div(place, 4 * depth)
        self.z = lax.rem(lax.div(place, 4), depth)
        self.bits = {
            "x": lax.axis_index("seq"),
            "c": lax.rem(place, 2),
            "y": lax.rem(lax.div(place, 2), 2),
            "a": lax.rem(self.z, 2),
            "b": lax.div(self.z, 2),
        }

    def partner(self, letters):
        bit = {
            letter: 1 - value if letter in letters else value
            for letter, value in self.bits.items()
        }
        z = self.z
        for letter, reach in (("a", 1), ("b", 2)):
            if letter in letters:
                z = z + reach - 2 * reach * self.bits[letter]
        return (bit["x"], (self.group * self.depth + z) * 4 + bit["y"] * 2 + bit["c"])

    def greet(self, met):
        barrier = pltpu.get_barrier_semaphore()
        for letters in met:
            pl.semaphore_signal(
                barrier, inc=1, device_id=self.partner(letters), device_id_type=MESH
            )
        pl.semaphore_wait(barrier, len(met))


def letters_of(depth):
    return "xy" + "ab"[: (depth - 1).bit_length()]


def parsed(routes, depth):
    kept = letters_of(depth)
    parts = []
    for route in routes.split():
        hops = ["".join(letter for letter in hop if letter in kept) for hop in route.split(".")]
        parts.append([hop for hop in hops if hop])
    return parts


def subsets(hop):
    return [
        "".join(letter for index, letter in enumerate(hop) if mask >> index & 1)
        for mask in range(1, 2 ** len(hop))
    ]


class Chunk:
    def __init__(self, place, depth, source, out_ref, offset, spot, scratch):
        _, self.begin, rows, first, columns, _, routes, _ = spot
        self.place, self.source, self.columns = place, source, pl.ds(first, columns)
        self.out_ref, self.out_begin = out_ref, offset + self.begin
        self.parts = parsed(routes, depth)
        self.half = rows // 2
        self.share = self.half // len(self.parts)
        self.hops = max(len(part) for part in self.parts)
        self.work, self.fresh, *landing, self.sends, self.receives, self.locals = scratch
        self.landing = {}
        self.sems = {}
        count = 2
        for part, hops in enumerate(self.parts):
            for hop, letters in enumerate(hops):
                self.landing[part, hop] = landing.pop(0)
                for way in range(2):
                    for index in range(2 ** len(letters) - 1):
                        self.sems[way, part, hop, index] = count
                        count += 1

    def aligned(self, value):
        return pl.multiple_of(value, PIECE)

    def size(self, part, hop):
        return self.share >> sum(len(letters) for letters in self.parts[part][: hop + 1])

    def spot(self, part, hop, other=""):
        start = part * self.share
        for level in range(hop + 1):
            for index, letter in enumerate(self.parts[part][level]):
                bit = self.place.bits[letter]
                if level == hop and letter in other:
                    bit = 1 - bit
                start = start + bit * (self.size(part, level) << index)
        return start

    def out(self, core):
        begin = self.aligned(self.out_begin + core * self.half)
        return self.out_ref.at[pl.ds(begin, self.half), self.columns]

    def held(self, buffer, begin, size):
        return buffer.at[pl.ds(self.aligned(begin), size)]

    def copy(self, index, source, target, letters):
        return remote(
            source, target, self.sends.at[index], self.receives.at[index],
            self.place.partner(letters),
        )

    def pair_down(self):
        core = self.place.bits["c"]
        at = lambda c: self.source.at[
            pl.ds(self.aligned(self.begin + c * self.half), self.half), self.columns
        ]
        return [
            self.copy(0, at(1 - core), self.fresh, "c"),
            pltpu.make_async_copy(at(core), self.work, self.locals.at[0]),
        ]

    def pair_up(self, arriving):
        core = self.place.bits["c"]
        return [
            self.copy(1, self.fresh, self.out(1 - core if arriving else core), "c"),
            pltpu.make_async_copy(self.fresh, self.out(core), self.locals.at[1]),
        ]

    def at_hop(self, hop):
        return [
            (part, hops[hop]) for part, hops in enumerate(self.parts) if hop < len(hops)
        ]

    def down(self, hop):
        copies = []
        for part, letters in self.at_hop(hop):
            size = self.size(part, hop)
            for index, other in enumerate(subsets(letters)):
                copies.append(
                    self.copy(
                        self.sems[0, part, hop, index],
                        self.held(self.work, self.spot(part, hop, other), size),
                        self.landing[part, hop].at[index], other,
                    )
                )
        return copies

    def up(self, hop, arriving):
        copies = []
        for part, letters in self.at_hop(hop):
            mine = self.spot(part, hop)
            size = self.size(part, hop)
            for index, other in enumerate(subsets(letters)):
                target = self.spot(part, hop, other) if arriving else mine
                copies.append(
                    self.copy(
                        self.sems[1, part, hop, index], self.held(self.fresh, mine, size),
                        self.held(self.fresh, target, size), other,
                    )
                )
        return copies

    def add(self, begin, sources, size):
        step = 64 if size % 64 == 0 else 32 if size % 32 == 0 else PIECE

        def body(index, carry):
            offset = self.aligned(index * step)
            there = pl.ds(self.aligned(begin + offset), step)
            total = self.work[there]
            if len(sources) == 1:
                total = total + sources[0][pl.ds(offset, step)]
            else:
                total = total.astype(F32)
                for source in sources:
                    total = total + source[pl.ds(offset, step)].astype(F32)
            self.work[there] = total.astype(BF)
            return carry

        lax.fori_loop(0, size // step, body, 0)

    def stage(self, number):
        hops = self.hops
        ended, started = [], []
        if number == 0:
            started = self.pair_down()
        elif number == 1:
            ended = self.pair_down()
            started = self.down(0)
        elif number <= hops:
            ended = self.down(number - 2)
            started = self.down(number - 1)
        elif number == hops + 1:
            ended = self.down(hops - 1)
            started = self.up(hops - 1, False)
        elif number <= 2 * hops:
            level = 2 * hops + 1 - number
            ended = self.up(level, True)
            started = self.up(level - 1, False)
        elif number == 2 * hops + 1:
            ended = self.up(0, True)
            started = self.pair_up(False)
        else:
            ended = self.pair_up(True)
        for copy in ended:
            copy.wait()
        if number == 1:
            self.add(0, [self.fresh], self.half)
        elif 2 <= number <= hops + 1:
            hop = number - 2
            for part, letters in self.at_hop(hop):
                landing = self.landing[part, hop]
                sources = [landing.at[index] for index in range(2 ** len(letters) - 1)]
                self.add(self.spot(part, hop), sources, self.size(part, hop))
        if number == hops + 1:
            for part, route in enumerate(self.parts):
                last = len(route) - 1
                there = pl.ds(self.aligned(self.spot(part, last)), self.size(part, last))
                self.fresh[there] = self.work[there]
        for copy in started:
            copy.start()


def chunk_scratch(spot, depth):
    _, _, rows, _, columns, _, routes, _ = spot
    parts = parsed(routes, depth)
    landing = []
    copies = 2
    for hops in parts:
        size = rows // 2 // len(parts)
        for letters in hops:
            size >>= len(letters)
            others = 2 ** len(letters) - 1
            copies += 2 * others
            landing.append(pltpu.VMEM((others, size, columns), BF))
    dma = pltpu.SemaphoreType.DMA
    return (
        [pltpu.VMEM((rows // 2, columns), BF)] * 2
        + landing
        + [dma((copies,)), dma((copies,)), dma((2,))]
    )


def loads_of(hop, size):
    if "x" in hop and "y" in hop:
        return [("x", 2 * size), ("y", 2 * size)]
    if hop in ("x", "y"):
        return [(hop, size)]
    if "a" in hop and "b" in hop:
        return [("end", 3 * size), ("middle", 4 * size)]
    return [("end", size), ("middle", 2 * size)] if hop == "b" else [("end", size)]


def planned(chunks, work, depth, hop_count):
    latency, issue, link, pair = 3.5, 0.08, 100e3, 600e3
    free = {}
    now = 3.0
    chains = []
    for rows, columns, need, routes, _ in chunks:
        parts = parsed(routes, depth)
        sizes = [rows // 2 // len(parts)] * len(parts)
        down = []
        for hop in range(max(len(part) for part in parts)):
            loads, copies, added = [], 0, 0
            for index, part in enumerate(parts):
                if hop < len(part):
                    sizes[index] >>= len(part[hop])
                    others = 2 ** len(part[hop]) - 1
                    loads += loads_of(part[hop], sizes[index])
                    copies += others
                    added += sizes[index] * others
            down.append((loads, copies, added, columns))
        first = [([("core", rows // 2)], 1.5, rows // 2, columns)]
        last = [([("core", rows // 2)], 1, 0, columns)]
        chains.append((need, first + down + down[::-1] + last))
    chains.append((len(work), [([("core", 16)], 2, 0, 768)] * hop_count))
    ranks = [chunk[4] for chunk in chunks] + [0]
    position = [0] * len(chains)
    ready = [0.0] * len(chains)
    order = [[] for _ in range(len(work) + 1)]
    done = 0
    while True:
        open_ones = [
            (ranks[i], ready[i], i) for i, (need, chain) in enumerate(chains)
            if position[i] <= len(chain) and need <= done
        ]
        due = [entry for entry in open_ones if entry[1] <= now]
        if not due and done < len(work):
            now += work[done]
            done += 1
            continue
        if not open_ones:
            return order
        _, when, index = min(due) if due else min(open_ones, key=lambda entry: entry[1])
        now = max(now, when)
        chain = chains[index][1]
        stage = position[index]
        order[done].append((index, stage))
        if 0 < stage <= len(chain) // 2:
            now += 1e-6 * chain[stage - 1][2] * chain[stage - 1][3]
        if stage < len(chain):
            loads, copies, _, columns = chain[stage]
            now += issue * copies
            end = now
            for lane, rows in loads:
                rate = pair if lane == "core" else link / 2
                free[lane] = max(now, free.get(lane, 0.0)) + 2 * rows * columns / rate
                end = max(end, free[lane])
            ready[index] = end + latency
        position[index] += 1


def last_kernel(
    depth, plan, orders, counts, *refs,
):
    (meta_ref, rows_ref, projected_hbm, mixed_hbm, log_ref, first_hbm, second_hbm,
     key_image_hbm, bias_hbm, small_ref, gain_ref, item_hbm, weight_hbm, total_hbm, unit_hbm, scale_hbm,
     out_weight_hbm, grad_down_ref, grad_up_ref,
     main_out, tail_out, small_out, diagonal_out, input_out,
     *scratch) = refs
    static, scratch = scratch[:6], scratch[6:]
    (k_ref, v_ref, mixed_ref, grad_ref, first_ref, second_ref, key_image_ref, bias_ref, pair_sems,
     item_ref, weight_ref, d_hidden_ref, unit_ref, scale_ref, load_sems, d_project, item_t, tail, input_grad,
     small_in, diagonal_in, small_sems, item_sems, *scratch) = scratch
    out_weight_ref = item_t
    place = Place(depth)
    step = pl.program_id(0)
    pairs = k_ref.shape[0]
    rows, width = item_hbm.shape
    count = rows // 2
    x = place.bits["x"]
    hidden = grad_down_ref.shape[0]
    sources = ((grad_down_ref, main_out, 0), (grad_up_ref, main_out, hidden), (tail, tail_out, 0))
    chunks = []
    for spot, pieces in zip(plan, counts):
        chunks.append(Chunk(place, depth, *sources[spot[0]], spot, scratch[:pieces]))
        scratch = scratch[pieces:]
    hop_letters = "c" + letters_of(depth)
    wide_hbm = (first_hbm, second_hbm, key_image_hbm, bias_hbm)
    wide_refs = (first_ref, second_ref, key_image_ref, bias_ref)

    def pair_loads(pair):
        copies = []
        held = ((projected_hbm, k_ref, width), (projected_hbm, v_ref, 2 * width))
        for source, target, first in held:
            columns = pl.ds(pl.multiple_of(first + pair * LANES, LANES), LANES)
            copies.append((source.at[:, columns], target.at[pair]))
        heads = pl.ds(2 * pair, 2)
        for source, target in zip(wide_hbm, wide_refs):
            copies.append((source.at[heads], target.at[heads]))
        return [
            pltpu.make_async_copy(source, target, pair_sems.at[pair, index])
            for index, (source, target) in enumerate(copies)
        ]

    def loads(first):
        if first:
            copies = [
                (total_hbm, d_hidden_ref), (unit_hbm, unit_ref), (scale_hbm, scale_ref),
                (out_weight_hbm, out_weight_ref), (item_hbm, item_ref),
            ]
            copies += [
                (mixed_hbm.at[:, pl.ds(pair * LANES, LANES)], mixed_ref.at[pair])
                for pair in range(pairs)
            ]
        else:
            copies = [(weight_hbm, weight_ref)]
        return [
            pltpu.make_async_copy(source, target, load_sems.at[0 if first else 1, index])
            for index, (source, target) in enumerate(copies)
        ]

    def back_to_attention():
        gain = vector(gain_ref)

        def tile(index, sums):
            there = pl.ds(pl.multiple_of(index * 64, 64), 64)
            d_normed = d_hidden_ref[there]
            standard = unit_ref[there]
            d_hidden = norm_pulled(d_normed * gain, standard, scale_ref[there, :1])
            d_hidden_ref[there] = d_hidden
            low = d_hidden.astype(BF)
            input_grad[there] = low
            return (
                sums[0] + column_sum(low.astype(F32)),
                sums[1] + column_sum(d_normed * standard),
                sums[2] + column_sum(d_normed),
            )

        zero = jnp.zeros((1, width), F32)
        sums = lax.fori_loop(0, rows // 64, tile, (zero, zero, zero), unroll=4)
        for row, value in zip((2, 3, 4), sums):
            small_out[row : row + 1] = value
        low = input_grad[...]
        down = TAIL_ROWS - width
        for begin in range(0, width, down):
            first = begin // LANES
            several = range(first, first + down // LANES)
            d_mixed = dot_nt(low, out_weight_ref[begin : begin + down]).astype(BF)
            for index, pair in enumerate(several):
                grad_ref[pair] = d_mixed[:, index * LANES : index * LANES + LANES]
            turned = jnp.concatenate(
                [jnp.transpose(mixed_ref[pair]).astype(BF) for pair in several], axis=0
            )
            for pair in range(pairs):
                rows_of, across = out_spot(pair, pairs, width)
                if rows_of.start == begin:
                    product = dot_nn(turned, low[:, across.start : across.start + across.size])
                    base = pair * TAIL_ROWS + width
                    tail[base : base + down] = product.astype(BF)

    def input_copies():
        return [
            pltpu.make_async_copy(
                input_grad.at[pl.ds(pl.multiple_of(x * count, LANES), count)], input_out.at[x],
                item_sems.at[0],
            ),
            remote(
                input_grad.at[pl.ds(pl.multiple_of((1 - x) * count, LANES), count)],
                input_out.at[x], item_sems.at[1], item_sems.at[2], place.partner("x"),
            ),
        ]

    def small_copies(hop):
        return [
            remote(source, landing.at[hop], small_sems.at[0, kind, hop],
                   small_sems.at[1, kind, hop], place.partner(hop_letters[hop]))
            for kind, (source, landing) in enumerate(
                ((small_out, small_in), (diagonal_out, diagonal_in))
            )
        ]

    def small_stage(hop):
        if hop > 0:
            for copy in small_copies(hop - 1):
                copy.wait()
            small_out[...] = small_out[...] + small_in[hop - 1]
            diagonal_out[...] = diagonal_out[...] + diagonal_in[hop - 1]
        if hop < len(hop_letters):
            for copy in small_copies(hop):
                copy.start()

    def perform(slot):
        for index, stage in orders[slot]:
            if index == len(chunks):
                small_stage(stage)
            else:
                chunks[index].stage(stage)

    @pl.when(step == 0)
    def _():
        for copy in loads(True):
            copy.start()
        for pair in range(pairs):
            for copy in pair_loads(pair):
                copy.start()
        for copy in loads(False):
            copy.start()
        met = set(hop_letters)
        for chunk in chunks:
            for hops in chunk.parts:
                for letters in hops:
                    met.update(subsets(letters))
        place.greet(sorted(met))
        small_out[...] = small_ref[...]

    for pair in range(pairs):
        @pl.when(step == pair)
        def _(pair=pair):
            perform(pair)

    @pl.when(step == 0)
    def _():
        static_prepare(meta_ref, static)
        for copy in loads(True):
            copy.wait()
        back_to_attention()
        for tile in range(rows // TILE):
            there = slice(tile * TILE, tile * TILE + TILE)
            item_t[:, there] = jnp.transpose(item_ref[there].astype(F32)).astype(BF)

    for copy in pair_loads(step):
        copy.wait()
    (dq_even, dk_even, dv_even), (dq_odd, dk_odd, dv_odd) = [
        head_back(
            parity, step, rows_ref, wide_refs, k_ref, v_ref, mixed_ref, grad_ref, log_ref,
            static, diagonal_out,
        )
        for parity in range(2)
    ]
    even = own_lanes(0, rows)
    pieces = [
        jnp.transpose(jnp.concatenate([dq_even, dq_odd], axis=0)).astype(BF),
        jnp.where(even, dk_even, dk_odd).astype(BF),
        jnp.where(even, dv_even, dv_odd).astype(BF),
    ]
    for part, piece in enumerate(pieces):
        d_project[:, pl.ds(pl.multiple_of(part * width + step * LANES, LANES), LANES)] = piece
    slab = pl.ds(pl.multiple_of(step * TAIL_ROWS, TAIL_ROWS), width)
    tail[slab] = dot_nn(item_t[...], jnp.concatenate(pieces, axis=1)).astype(BF)

    @pl.when(step == 0)
    def _():
        for copy in loads(False):
            copy.wait()

    @pl.when(step == pairs - 1)
    def _():
        perform(pairs)
        for begin in range(0, width, TILE):
            here = slice(begin, begin + TILE)
            total = d_hidden_ref[:, here] + dot_nt(d_project[...], weight_ref[here])
            input_grad[:, here] = total.astype(BF)
        for copy in input_copies():
            copy.start()
        for begin in range(0, width, TILE):
            here = slice(begin, begin + TILE)
            there = slice(2 * width + begin, 2 * width + begin + TILE)
            small_out[0:1, here] = column_sum(d_project[:, here].astype(F32))
            small_out[1:2, here] = column_sum(d_project[:, there].astype(F32))
        perform(pairs + 1)
        for copy in input_copies():
            copy.wait()


TAIL_ROWS = 1024


def out_spot(pair, pairs, width):
    down = TAIL_ROWS - width
    across = width * width // (pairs * down)
    per_row = width // across
    return (
        pl.ds(pair // per_row * down, down),
        pl.ds(pair % per_row * across, across),
    )


def summed_with_attention_back(
    meta_columns, meta_rows, projected, mixed, logs, wide_arrays, item, qkv_weight,
    total, unit, scale, out_weight, attn_gain, small, grad_down, grad_up,
):
    size = lax.axis_size("dp")
    depth = 4 if size % 16 == 0 else size // 4
    rows, width = item.shape
    pairs = width // LANES
    hidden = grad_down.shape[0]
    hops = len(letters_of(depth)) + 1
    work = [6.8] * pairs + [4.0]
    tall, wide, slim = 1024, 3 * LANES, 2 * LANES
    plan = [
        (0, 0, 2 * tall, 0, width, 0, "a.b.x.y x.y.a.b", 1),
        (0, 2 * tall, tall, 0, width, 0, "x.a.y.b y.a.b.x", 2),
        (1, 0, 3 * tall, 0, slim, 0, "a.b.x.y y.x.a.b", 4),
        (1, 0, 3 * tall, slim, slim, 0, "y.a.x.b x.y.a.b", 0),
        (1, 0, 3 * tall, 2 * slim, slim, 0, "x.y.a.b y.x.a.b", 2),
        (2, 0, tall, 0, wide, 1, "y.x.a.b a.b.x.y", 3),
        (2, tall, tall, 0, wide, 2, "xy.a.b", 2),
        (2, 2 * tall, tall, 0, wide, 3, "x.y.ab y.ab.x", 3),
        (2, 3 * tall, tall, 0, wide, 4, "xy.a.b", 1),
        (2, 4 * tall, tall, 0, wide, 5, "xy.a.b", 1),
        (2, 5 * tall, tall, 0, wide, 6, "ab.y.x y.ab.x", 2),
    ]
    orders = planned([(spot[2],) + spot[4:] for spot in plan], work, depth, hops)

    whole = pl.BlockSpec(memory_space=pltpu.VMEM)
    diagonals = jax.ShapeDtypeStruct((2 * pairs, 8, LANES), F32)
    dma = pltpu.SemaphoreType.DMA
    scratch = []
    for spot in plan:
        scratch.append(chunk_scratch(spot, depth))
    main, tail, small, diagonals, grad_input = pl.pallas_call(
        functools.partial(last_kernel, depth, plan, orders, [len(pieces) for pieces in scratch]),
        grid=(pairs,),
        in_specs=[whole] * 2 + [HBM] * 2 + [whole] + [HBM] * 4 + [whole] * 2 + [HBM] * 8,
        out_specs=[HBM, HBM, whole, whole, HBM],
        out_shape=[
            jax.ShapeDtypeStruct((2 * hidden, width), BF),
            jax.ShapeDtypeStruct((pairs * TAIL_ROWS, 3 * LANES), BF),
            jax.ShapeDtypeStruct(small.shape, F32),
            diagonals,
            jax.ShapeDtypeStruct((2, rows // 2, width), BF),
        ],
        scratch_shapes=[pltpu.VMEM((rows, LANES), BF)] * 3
        + [pltpu.VMEM((LANES, rows), BF)] * 3
        + [pltpu.VMEM((pairs, rows, LANES), kind) for kind in (BF, BF, F32, BF)]
        + [pltpu.VMEM(array.shape, BF) for array in wide_arrays]
        + [
            dma((pairs, 6)),
            pltpu.VMEM((rows, width), BF),
            pltpu.VMEM((width, 3 * width), BF),
            pltpu.VMEM((rows, width), F32),
            pltpu.VMEM((rows, width), F32),
            pltpu.VMEM((rows, LANES), F32),
            dma((2, 5 + pairs)),
            pltpu.VMEM((rows, 3 * width), BF),
            pltpu.VMEM((width, rows), BF),
            pltpu.VMEM((pairs * TAIL_ROWS, 3 * LANES), BF),
            pltpu.VMEM((rows, width), BF),
            pltpu.VMEM((hops,) + small.shape, F32),
            pltpu.VMEM((hops,) + diagonals.shape, F32),
            dma((2, 2, hops)),
            dma((3,)),
        ]
        + [piece for pieces in scratch for piece in pieces],
        compiler_params=pltpu.CompilerParams(
            collective_id=0, has_side_effects=True, vmem_limit_bytes=62 * MIB
        ),
        name="summed_with_attention_back",
    )(meta_columns, meta_rows, projected, mixed, logs, *wide_arrays,
      small, attn_gain, item, qkv_weight, total, unit, scale, out_weight, grad_down, grad_up)
    span = 4 * depth
    if size > span:
        groups = [list(range(first, size, span)) for first in range(span)]
        main, tail, small, diagonals = lax.psum(
            (main.astype(F32), tail.astype(F32), small, diagonals), "dp",
            axis_index_groups=groups,
        )
        main, tail = main.astype(BF), tail.astype(BF)
    return main, tail, small, diagonals, grad_input


def per_device(
    layer_in, segment, key_mask, position, layout_x, layout_y,
    qkv_weight, query_bias, value_bias, out_weight, out_bias, attn_gain, attn_shift,
    up_weight, up_bias, down_weight, down_bias, ffn_gain, ffn_shift,
    text_table, horiz_table, vert_table, cotangent,
):
    width = layer_in.shape[-1]
    item, projected, meta_columns, meta_rows, table_rows = projected_item(
        layer_in, (segment, key_mask, position, layout_x, layout_y),
        qkv_weight, query_bias, value_bias, (text_table, horiz_table, vert_table),
    )
    mixed, logs, *wide_arrays = attention_forward(meta_columns, meta_rows, table_rows, projected, width)
    layer_out, total, unit, scale, grad_down, grad_up, small = fed_forward_and_back(
        item, mixed, cotangent, out_weight, up_weight, down_weight,
        (out_bias, attn_gain, attn_shift, up_bias, down_bias, ffn_gain, ffn_shift),
    )
    main, tail, small, diagonals, grad_input = summed_with_attention_back(
        meta_columns, meta_rows, projected, mixed, logs, wide_arrays, item, qkv_weight,
        total, unit, scale, out_weight, attn_gain, small, grad_down, grad_up,
    )
    done = finished(
        main, tail, grad_input, small, diagonals, up_weight.shape[1], text_table.shape[0]
    )
    sum_down, sum_up, sum_out, sum_qkv, grad_input = done[:5]
    singles, tables = done[5:14], [t.T for t in done[14:]]
    return (
        layer_out, grad_input, sum_qkv, singles[0], singles[1], sum_out, singles[2], singles[3],
        singles[4], sum_up, singles[8], sum_down, singles[5], singles[6], singles[7],
        tables[0], tables[1], tables[2],
    )


def solution(mesh):
    rows = P("dp", "seq", None)
    marks_spec = P("dp", "seq")
    return jax.shard_map(
        per_device,
        mesh=mesh,
        in_specs=(rows,) + (marks_spec,) * 5 + (P(),) * 16 + (rows,),
        out_specs=(rows, rows) + (P(),) * 16,
        check_vma=False,
    )
```

```python
import functools

import jax
import jax.numpy as jnp
from jax import lax
from jax.experimental import pallas as pl
from jax.experimental.pallas import tpu as pltpu
from jax.sharding import PartitionSpec as P

BF = jnp.bfloat16
F32 = jnp.float32
BIG = 1e30
LANES = 128
HEAD = 64
TEXT = 512
POS = 64
COORD = 48
Y0 = 64
GROUP0 = 112
MEMBER0 = 116
FLAG = 124
EVERY = 125
STRAY = 126
X_TABLE = 33
Y_TABLE = 66
NOTHING = 127


def dot_nt(a, b):
    return lax.dot_general(a, b, (((1,), (1,)), ((), ())), preferred_element_type=F32)


def dot_nn(a, b):
    return lax.dot_general(a, b, (((1,), (0,)), ((), ())), preferred_element_type=F32)


def looked_up(table_row, index):
    rows = index.shape[0]
    return jnp.take_along_axis(
        jnp.broadcast_to(table_row, (rows, LANES)), index, axis=1, mode="promise_in_bounds"
    )


def bucket(distance):
    return jnp.clip(distance, -16, 16) + 16


def between(lane, low, high):
    return (lane >= low) & (lane < high)


def columns_of(meta_ref):
    return tuple(meta_ref[:, field : field + 1] for field in range(5))


def marks(meta_ref):
    segment, key_mask, position, across, down = columns_of(meta_ref)
    rows = segment.shape[0]
    lane = lax.broadcasted_iota(jnp.int32, (rows, LANES), 1)
    row = lax.broadcasted_iota(jnp.int32, (rows, LANES), 0)
    even = between(lane, HEAD, HEAD + COORD) & (lane - HEAD == across)
    odd = (lane < COORD) & (lane == across)
    group = (segment - 1) >> 3
    member = (segment - 1) & 7
    named = segment > 0
    shared = (
        ((row < TEXT) & (lane < POS) & (lane == position))
        | (between(lane, Y0, Y0 + COORD) & (lane - Y0 == down))
        | (named & between(lane, GROUP0, MEMBER0) & (lane - GROUP0 == group))
        | (named & between(lane, MEMBER0, FLAG) & (lane - MEMBER0 == member))
        | ((lane == FLAG) & (key_mask <= 0))
        | (lane == EVERY)
        | ((lane == STRAY) & (segment < 0))
    )
    return tuple(jnp.where(m, 1.0, 0.0).astype(BF) for m in (even, odd, shared))


def square_lanes():
    shape = (LANES, LANES)
    return lax.broadcasted_iota(jnp.int32, shape, 0), lax.broadcasted_iota(jnp.int32, shape, 1)


def barred():
    row, lane = square_lanes()
    in_groups = between(lane, GROUP0, MEMBER0)
    shut = (
        (between(row, GROUP0, MEMBER0) & in_groups & (lane != row))
        | (between(row, MEMBER0, FLAG) & between(lane, MEMBER0, FLAG) & (lane != row))
        | ((row == EVERY) & (lane == FLAG))
        | ((row == STRAY) & in_groups)
    )
    return jnp.where(shut, -BIG, 0.0).astype(F32)


def table_index():
    row, lane = square_lanes()
    distance = bucket(row - lane)
    inside = lambda low, high: between(row, low, high) & between(lane, low, high)
    even = jnp.where(inside(HEAD, HEAD + COORD), distance + X_TABLE, NOTHING)
    odd = jnp.where(inside(0, COORD), distance + X_TABLE, NOTHING)
    shared = jnp.where(
        inside(0, POS), distance, jnp.where(inside(Y0, Y0 + COORD), distance + Y_TABLE, NOTHING)
    )
    return even, odd, shared


def image_query_index(meta_ref):
    position = meta_ref[TEXT:, 2:3]
    lane = lax.broadcasted_iota(jnp.int32, (position.shape[0], LANES), 1)
    return jnp.where(lane < POS, bucket(position - lane), NOTHING)


def prepare(meta_ref, mark_refs, bar_ref, index_refs, image_index_ref):
    for ref, value in zip(mark_refs, marks(meta_ref)):
        ref[...] = value
    bar_ref[...] = barred()
    for ref, value in zip(index_refs, table_index()):
        ref[...] = value
    image_index_ref[...] = image_query_index(meta_ref)


def own_lanes(parity, rows):
    lane = lax.broadcasted_iota(jnp.int32, (rows, LANES), 1)
    return (lane < HEAD) if parity == 0 else (lane >= HEAD)


def widened(parity, q, table_row, bias, bar_ref, index_refs, image_index_ref, mark_refs):
    rows = q.shape[0]
    shared = mark_refs[2][...]
    across = looked_up(table_row, index_refs[parity][...]).astype(BF)
    first = jnp.where(
        own_lanes(parity, rows), q.astype(F32) * 0.125, dot_nn(mark_refs[parity][...], across)
    )
    others = (looked_up(table_row, index_refs[2][...]) + bar_ref[...]).astype(BF)
    second = dot_nn(shared, others)
    on_images = looked_up(table_row, image_index_ref[...])
    second = jnp.concatenate([second[:TEXT], second[TEXT:] + on_images], axis=0)
    image_lane = lax.broadcasted_iota(jnp.int32, on_images.shape, 1)
    key_image = jnp.where(image_lane < POS, bias[:, :LANES].astype(BF), shared[TEXT:])
    return first.astype(BF), second.astype(BF), key_image


def joined(parity, first, second, key_image, k, marks_own, shared):
    rows = k.shape[0]
    lane = lax.broadcasted_iota(jnp.int32, (rows, LANES), 1)
    to_image = jnp.where(lane < POS, shared, second)
    key_first = jnp.where(own_lanes(parity, rows), k, marks_own)
    q_text = jnp.concatenate([first, second], axis=1)
    q_image = jnp.concatenate([first, to_image], axis=1)
    k_text = jnp.concatenate([key_first[:TEXT], shared[:TEXT]], axis=1)
    k_image = jnp.concatenate([key_first[TEXT:], key_image], axis=1)
    return q_text, q_image, k_text, k_image


def near(start, size):
    if start >= TEXT:
        return slice(0, TEXT)
    return slice(max(0, start - LANES), min(TEXT, start + size + LANES))


def image_bias(table_row, offsets):
    return jnp.concatenate(
        [looked_up(table_row, offsets[:, :LANES]), looked_up(table_row, offsets[:, LANES:])], axis=1
    )


def forward_kernel(
    meta_ref, rows_ref, table_ref, q_ref, k_ref, v_ref,
    mixed_ref, log_ref, first_ref, second_ref, key_image_ref, bias_ref,
    even_ref, odd_ref, shared_ref, bar_ref, index_even, index_odd, index_shared, image_index_ref,
):
    mark_refs = (even_ref, odd_ref, shared_ref)
    index_refs = (index_even, index_odd, index_shared)

    @pl.when(pl.program_id(0) == 0)
    def _():
        prepare(meta_ref, mark_refs, bar_ref, index_refs, image_index_ref)

    rows = q_ref.shape[0]
    images = rows - TEXT
    q, k, v = q_ref[...], k_ref[...], v_ref[...]
    offsets = bucket(rows_ref[2:3, TEXT:] - meta_ref[TEXT:, 2:3])
    tile = 256
    v_turned = transposed(v)
    heads = [None, None]

    def prepared(parity):
        table_row = table_ref[pl.ds(2 * pl.program_id(0) + parity, 1), :]
        bias = image_bias(table_row, offsets)
        first, second, key_image = widened(
            parity, q, table_row, bias, bar_ref, index_refs, image_index_ref, mark_refs
        )
        first_ref[parity] = first
        second_ref[parity] = second
        key_image_ref[parity] = key_image
        bias_ref[parity] = bias.astype(BF)
        wide = joined(
            parity, first, second, key_image, k, mark_refs[parity][...], shared_ref[...]
        )
        heads[parity] = wide + (bias,)

    def scored(parity, start):
        q_text, q_image, k_text, k_image, bias = heads[parity]
        here = slice(start, start + tile)
        on_image = dot_nt(k_image, q_image[here])
        if start >= TEXT:
            on_image = on_image + bias[:, start - TEXT : start - TEXT + tile]
        return dot_nt(k_text[near(start, tile)], q_text[here]), on_image

    spots = [(parity, start) for parity in range(2) for start in range(0, rows, tile)]
    outs = ([], [])
    prepared(0)
    following = scored(*spots[0])
    for index, (parity, start) in enumerate(spots):
        on_text, on_image = following
        if index == 1:
            prepared(1)
        if index + 1 < len(spots):
            following = scored(*spots[index + 1])
        top = jnp.maximum(
            jnp.max(on_text, axis=0, keepdims=True), jnp.max(on_image, axis=0, keepdims=True)
        )
        on_text = jnp.exp(on_text - top)
        on_image = jnp.exp(on_image - top)
        total = jnp.sum(on_text, axis=0, keepdims=True) + jnp.sum(on_image, axis=0, keepdims=True)
        own = slice(parity * HEAD, parity * HEAD + HEAD)
        out = dot_nn(v_turned[own, near(start, tile)], on_text.astype(BF)) + dot_nn(
            v_turned[own, TEXT:], on_image.astype(BF)
        )
        outs[parity].append(out * (1.0 / total))
        log_ref[0, parity : parity + 1, start : start + tile] = top + jnp.log(total)
    mixed_ref[...] = jnp.transpose(
        jnp.concatenate([jnp.concatenate(outs[parity], axis=1) for parity in range(2)], axis=0)
    )


def static_scratch(rows):
    square = (LANES, LANES)
    return [
        pltpu.VMEM((rows, LANES), BF),
        pltpu.VMEM((rows, LANES), BF),
        pltpu.VMEM((rows, LANES), BF),
        pltpu.VMEM(square, F32),
        pltpu.VMEM(square, jnp.int32),
        pltpu.VMEM(square, jnp.int32),
        pltpu.VMEM(square, jnp.int32),
        pltpu.VMEM((rows - TEXT, LANES), jnp.int32),
    ]


def attention_forward(meta_columns, meta_rows, table_rows, projected, width):
    rows = projected.shape[0]
    images = rows - TEXT
    pairs = width // LANES

    def block(part):
        return pl.BlockSpec((rows, LANES), lambda p: (0, part * pairs + p))

    whole = lambda shape: pl.BlockSpec(shape, lambda p: (0,) * len(shape))
    return pl.pallas_call(
        forward_kernel,
        grid=(pairs,),
        in_specs=[
            whole(meta_columns.shape),
            whole(meta_rows.shape),
            whole(table_rows.shape),
            block(0), block(1), block(2),
        ],
        out_specs=[
            pl.BlockSpec((rows, LANES), lambda p: (0, p)),
            pl.BlockSpec((1, 2, rows), lambda p: (p, 0, 0)),
            pl.BlockSpec((2, rows, LANES), lambda p: (p, 0, 0)),
            pl.BlockSpec((2, rows, LANES), lambda p: (p, 0, 0)),
            pl.BlockSpec((2, images, LANES), lambda p: (p, 0, 0)),
            pl.BlockSpec((2, images, images), lambda p: (p, 0, 0)),
        ],
        out_shape=[
            jax.ShapeDtypeStruct((rows, width), F32),
            jax.ShapeDtypeStruct((pairs, 2, rows), F32),
            jax.ShapeDtypeStruct((2 * pairs, rows, LANES), BF),
            jax.ShapeDtypeStruct((2 * pairs, rows, LANES), BF),
            jax.ShapeDtypeStruct((2 * pairs, images, LANES), BF),
            jax.ShapeDtypeStruct((2 * pairs, images, images), BF),
        ],
        scratch_shapes=static_scratch(rows),
        compiler_params=pltpu.CompilerParams(vmem_limit_bytes=60 * 1024 * 1024),
        name="attention_forward",
    )(meta_columns, meta_rows, table_rows, projected, projected, projected)


def skewed(block):
    size = block.shape[0]
    lane = lax.broadcasted_iota(jnp.int32, (size, LANES), 1)
    row = lax.broadcasted_iota(jnp.int32, (size, LANES), 0)
    turned = jnp.take_along_axis(
        block, (lane + row) & (LANES - 1), axis=1, mode="promise_in_bounds"
    )
    straight = lane + row < LANES
    above = jnp.sum(jnp.where(straight, turned, 0.0), axis=0, keepdims=True)
    below = jnp.sum(jnp.where(straight, 0.0, turned), axis=0, keepdims=True)
    return above, below


def transposed(array):
    return jnp.transpose(array.astype(F32)).astype(array.dtype)


def static_prepare(meta_ref, static):
    for ref, turned, value in zip(static[:3], static[3:], marks(meta_ref)):
        ref[...] = value
        turned[...] = transposed(value)


def head_back(
    parity, pair, rows_ref, wide_refs, k_ref, v_ref, mixed_ref, grad_ref, log_ref, static, diag_ref,
):
    mark_refs, turned_refs = static[:3], static[3:]
    first_ref, second_ref, key_image_ref, bias_ref = wide_refs
    head = 2 * pair + parity
    shared_t = turned_refs[2]
    rows = k_ref.shape[1]
    images = rows - TEXT
    tile = 256
    k, v, grad = k_ref[pair], v_ref[pair], grad_ref[pair]
    products = grad.astype(F32) * mixed_ref[pair]
    k_turned = transposed(k)
    is_image = rows_ref[1:2, TEXT:] > 0
    own = own_lanes(parity, rows)
    log_row = log_ref[pair, parity : parity + 1, :]
    first, shared = first_ref[head], mark_refs[2][...]
    q_text, q_image, k_text, k_image = joined(
        parity, first, second_ref[head], key_image_ref[head], k, mark_refs[parity][...], shared
    )
    bias = bias_ref[head].astype(F32)
    ones = jnp.where(own_lanes(parity, 8), 1.0, 0.0).astype(BF)
    delta = jnp.zeros((8, rows), F32)
    rest = products
    for _ in range(3):
        piece = rest.astype(BF)
        delta = delta + dot_nt(ones, piece)
        rest = rest - piece.astype(F32)
    delta = delta[0:1]
    v_own = jnp.where(own, v, jnp.zeros_like(v))
    q_marked = jnp.concatenate(
        [jnp.where(own, first, mark_refs[parity][...]), shared], axis=1
    )
    dq_text = jnp.zeros((HEAD, TEXT), F32)
    dq_image = jnp.zeros((HEAD, images), F32)
    dks = []
    dvs = []
    first_sum = jnp.zeros((LANES, LANES), F32)
    second_sum = jnp.zeros((LANES, LANES), F32)
    text_image = jnp.zeros((LANES, images), F32)

    def met(start, array, axis=0):
        text = near(start, tile)
        if axis == 0:
            return jnp.concatenate([array[text], array[TEXT:]], axis=0)
        return jnp.concatenate([array[:, text], array[:, TEXT:]], axis=1)

    def scored(start):
        here = slice(start, start + tile)
        if start < TEXT:
            scores = dot_nt(k_text[here], met(start, q_text))
        else:
            scores = dot_nt(k_image[start - TEXT : start - TEXT + tile], q_image)
            scores = jnp.concatenate([scores[:, :TEXT], scores[:, TEXT:] + bias], axis=1)
        return scores, dot_nt(v_own[here], met(start, grad))

    following = scored(0)
    for start in range(0, rows, tile):
        here = slice(start, start + tile)
        scores, prob_grad = following
        if start + tile < rows:
            following = scored(start + tile)
        soft = jnp.exp(scores - met(start, log_row, 1))
        score_grad = soft * (prob_grad - met(start, delta, 1))
        low = score_grad.astype(BF)
        dvs.append(dot_nn(soft.astype(BF), met(start, grad)))
        wide = dot_nn(low, met(start, q_marked))
        dks.append(wide[:, :LANES])
        part = dot_nn(k_turned[parity * HEAD : parity * HEAD + HEAD, here], low)
        text = near(start, tile)
        count = text.stop - text.start
        before = [jnp.zeros((HEAD, text.start), F32)] if text.start > 0 else []
        after = [jnp.zeros((HEAD, TEXT - text.stop), F32)] if text.stop < TEXT else []
        dq_text = dq_text + jnp.concatenate(before + [part[:, :count]] + after, axis=1)
        dq_image = dq_image + part[:, count:]
        rounded = wide.astype(BF)
        first_sum = first_sum + dot_nn(turned_refs[parity][:, here], rounded[:, :LANES])
        second_sum = second_sum + dot_nn(shared_t[:, here], rounded[:, LANES:])
        if start < TEXT:
            text_image = text_image + dot_nn(shared_t[:, here], low[:, count:])
        else:
            by_position = wide[:, LANES:]
            on_image = score_grad[:, TEXT:]
    dq = jnp.concatenate([dq_text, dq_image], axis=1)
    small = lax.broadcasted_iota(jnp.int32, (LANES, LANES), 1)
    small_row = lax.broadcasted_iota(jnp.int32, (LANES, LANES), 0)
    x0 = HEAD if parity == 0 else 0
    x_block = jnp.where(
        between(small, x0, x0 + COORD) & between(small_row, x0, x0 + COORD), first_sum, 0.0
    )
    y_block = jnp.where(
        between(small, Y0, Y0 + COORD) & between(small_row, Y0, Y0 + COORD), second_sum, 0.0
    )
    p_block = jnp.where((small < POS) & (small_row < POS), second_sum, 0.0)
    wide_lane = lax.broadcasted_iota(jnp.int32, (images, images), 1)
    outside = jnp.sum(jnp.where(is_image, 0.0, on_image), axis=1, keepdims=True)
    pairs = jnp.where(is_image, on_image, 0.0) + jnp.where(wide_lane == 0, outside, 0.0)
    outside_text = jnp.sum(jnp.where(is_image, 0.0, text_image), axis=1, keepdims=True)
    text_lane = lax.broadcasted_iota(jnp.int32, (LANES, images), 1)
    text_row = lax.broadcasted_iota(jnp.int32, (LANES, images), 0)
    text_image = jnp.where(is_image, text_image, 0.0) + jnp.where(
        text_lane == 0, outside_text, 0.0
    )
    text_image = jnp.where(text_row < POS, text_image, 0.0)
    first_lane = lax.broadcasted_iota(jnp.int32, (images, LANES), 1)
    left = pairs[:, :LANES] + jnp.where(first_lane < POS, by_position, 0.0)
    right = pairs[:, LANES:]
    a00, b00 = skewed(left[:LANES] + text_image[:, :LANES] + p_block)
    a01, b01 = skewed(right[:LANES] + text_image[:, LANES:])
    a10, b10 = skewed(left[LANES:])
    a11, b11 = skewed(right[LANES:])
    ax, bx = skewed(x_block)
    ay, by = skewed(y_block)
    diag_ref[head] = jnp.concatenate(
        [b10, b00 + b11 + a10, a00 + a11 + b01, a01, bx, ax, by, ay], axis=0
    )
    return dq * 0.125, jnp.concatenate(dks, axis=0), jnp.concatenate(dvs, axis=0)


MESH = pl.DeviceIdType.MESH
VMEM = pl.BlockSpec(memory_space=pltpu.VMEM)
HBM = pl.BlockSpec(memory_space=pltpu.HBM)
MIB = 1024 * 1024


def remote(src, dst, send, receive, device):
    return pltpu.make_async_remote_copy(
        src_ref=src, dst_ref=dst, send_sem=send, recv_sem=receive, device_id=device,
        device_id_type=MESH,
    )


def project_kernel(
    layer_ref, weight_hbm, *refs,
):
    small_hbm, refs = refs[:10], refs[10:]
    (item_ref, projected_out, columns_ref, rows_ref, table_ref,
     projected_ref, weight_ref, meta_send, bias_ref, sems, load_sems, store_sems), small = (
        refs[:12], refs[12:],
    )
    (segment_ref, mask_ref, position_ref, across_ref, down_ref, query_bias_ref, value_bias_ref,
     text_ref, horiz_ref, vert_ref) = small
    mine = lax.axis_index("seq")
    partner = (1 - mine, lax.axis_index("dp"))
    count, width = layer_ref.shape[1:]
    own = pl.ds(pl.multiple_of(mine * count, LANES), count)
    loads = [
        pltpu.make_async_copy(source, target, load_sems.at[index])
        for index, (source, target) in enumerate(
            list(zip(small_hbm, small))
            + [(layer_ref.at[mine], item_ref.at[own]), (weight_hbm, weight_ref)]
        )
    ]
    for load in loads:
        load.start()
    barrier = pltpu.get_barrier_semaphore()
    pl.semaphore_signal(barrier, inc=1, device_id=partner, device_id_type=MESH)
    pl.semaphore_wait(barrier, 1)
    pieces = count // LANES
    rows_out = [
        remote(
            layer_ref.at[1 - mine, pl.ds(piece * LANES, LANES)],
            item_ref.at[pl.ds(pl.multiple_of(mine * count + piece * LANES, LANES), LANES)],
            sems.at[0, piece], sems.at[1, piece], partner,
        )
        for piece in range(pieces)
    ]
    for copy in rows_out:
        copy.start()
    for load in loads[:-2]:
        load.wait()

    fields = (segment_ref, mask_ref, position_ref, across_ref, down_ref)
    blocks = [
        jnp.concatenate(
            [field[item : item + 1, :] for field in fields] + [jnp.zeros((3, count), jnp.int32)],
            axis=0,
        )
        for item in range(2)
    ]
    meta_send[...] = jnp.where(mine == 0, blocks[1], blocks[0])
    meta_out = remote(
        meta_send, rows_ref.at[:, own], sems.at[0, pieces], sems.at[1, pieces], partner
    )
    meta_out.start()
    rows_ref[:, own] = jnp.where(mine == 0, blocks[0], blocks[1])
    bias_ref[:, :width] = query_bias_ref[...].astype(F32).reshape(1, width)
    bias_ref[:, width : 2 * width] = jnp.zeros((1, width), F32)
    bias_ref[:, 2 * width :] = value_bias_ref[...].astype(F32).reshape(1, width)
    heads, levels = text_ref.shape
    spot = lax.broadcasted_iota(jnp.int32, (levels, LANES), 1)
    level = lax.broadcasted_iota(jnp.int32, (levels, LANES), 0)
    table = jnp.zeros((heads, LANES), F32)
    for source, begin in ((text_ref, 0), (horiz_ref, X_TABLE), (vert_ref, Y_TABLE)):
        table = table + dot_nn(source[...], (spot == level + begin).astype(BF))
    table_ref[...] = jnp.concatenate([table, jnp.zeros((16 - heads, LANES), F32)], axis=0)

    def project(there):
        step = 256

        def body(index, carry):
            columns = pl.ds(pl.multiple_of(index * step, step), step)
            product = dot_nn(item_ref[there], weight_ref[:, columns])
            projected_ref[there, columns] = (product + bias_ref[:, columns]).astype(BF)
            return carry

        lax.fori_loop(0, 3 * width // step, body, 0)

    def stored(index, there):
        return pltpu.make_async_copy(
            projected_ref.at[there], projected_out.at[there], store_sems.at[index]
        )

    for load in loads[-2:]:
        load.wait()
    project(own)
    stored(0, own).start()
    for piece in range(pieces):
        rows_out[piece].wait()
        there = pl.ds(pl.multiple_of((1 - mine) * count + piece * LANES, LANES), LANES)
        project(there)
        stored(1 + piece, there).start()
    meta_out.wait()
    meta = rows_ref[...].astype(F32)
    tall = jnp.concatenate([meta, jnp.zeros((LANES - 8, meta.shape[1]), F32)], axis=0)
    columns_ref[...] = jnp.transpose(tall).astype(jnp.int32)
    stored(0, own).wait()
    for piece in range(pieces):
        there = pl.ds(pl.multiple_of((1 - mine) * count + piece * LANES, LANES), LANES)
        stored(1 + piece, there).wait()


def projected_item(layer_in, fields, qkv_weight, query_bias, value_bias, tables):
    rows = 2 * layer_in.shape[1]
    width = layer_in.shape[2]
    pieces = rows // 2 // LANES
    small = list(fields) + [query_bias, value_bias] + [t.T for t in tables]
    return pl.pallas_call(
        project_kernel,
        in_specs=[HBM] * (2 + len(small)),
        out_specs=[VMEM, HBM, VMEM, VMEM, VMEM],
        out_shape=[
            jax.ShapeDtypeStruct((rows, width), BF),
            jax.ShapeDtypeStruct((rows, 3 * width), BF),
            jax.ShapeDtypeStruct((rows, LANES), jnp.int32),
            jax.ShapeDtypeStruct((8, rows), jnp.int32),
            jax.ShapeDtypeStruct((16, LANES), F32),
        ],
        scratch_shapes=[
            pltpu.VMEM((rows, 3 * width), BF),
            pltpu.VMEM((width, 3 * width), BF),
            pltpu.VMEM((8, rows // 2), jnp.int32),
            pltpu.VMEM((1, 3 * width), F32),
            pltpu.SemaphoreType.DMA((2, pieces + 1)),
            pltpu.SemaphoreType.DMA((len(small) + 2,)),
            pltpu.SemaphoreType.DMA((pieces + 1,)),
        ]
        + [pltpu.VMEM(array.shape, array.dtype) for array in small],
        compiler_params=pltpu.CompilerParams(
            collective_id=1, has_side_effects=True, vmem_limit_bytes=60 * MIB
        ),
        name="projected_item",
    )(layer_in, qkv_weight, *small)


EPSILON = 1e-05
TILE = 256


def vector(ref):
    return ref[...].astype(F32).reshape(1, ref.shape[0])


def gelu_and_slope(x):
    bell = jnp.exp2(-0.7213475204444817 * (x * x))
    rough = 1.0 + 0.23164188826 * jnp.abs(x)
    t = pl.reciprocal(rough, approx=True)
    t = t * (2.0 - rough * t)
    series = t * (
        0.127414796
        + t * (-0.142248368 + t * (0.7107068705 + t * (-0.7265760135 + t * 0.5307027145)))
    )
    tail = bell * series
    below = jnp.where(x >= 0.0, 1.0 - tail, tail)
    return x * below, below + x * (0.3989422804014327 * bell)


def row_mean(block):
    return jnp.mean(block, axis=1, keepdims=True)


def normalized(hidden):
    center = hidden - row_mean(hidden)
    scale = lax.rsqrt(row_mean(center * center) + EPSILON)
    return center * scale, scale


def norm_pulled(grad, unit, scale):
    return scale * (grad - row_mean(grad) - unit * row_mean(grad * unit))


def column_sum(block):
    return jnp.sum(block, axis=0, keepdims=True)


def feed_kernel(
    item_hbm, mixed_hbm, cotangent_ref, out_weight_ref, up_ref, down_ref, *refs,
):
    vectors_hbm, refs = refs[:7], refs[7:]
    (layer_out, total_out, unit_out, scale_out, grad_down_ref, grad_up_ref, small_ref,
     item_ref, mixed_ref, layer_ref, cotangent_all, active, slope, unit, scale_ref, normed, normed_t, total, d_branch, d_branch_t,
     sems, load_sems, tile_sems, store_sems) = refs[:24]
    vectors = refs[24:]
    (out_bias_ref, attn_gain_ref, attn_shift_ref, up_bias_ref, down_bias_ref, ffn_gain_ref,
     ffn_shift_ref) = vectors
    step = pl.program_id(0)
    blocks = pl.num_programs(0) // 2
    rows, width = item_hbm.shape
    count = rows // 2
    mine = lax.axis_index("seq")
    partner = (1 - mine, lax.axis_index("dp"))
    own = pl.ds(pl.multiple_of(mine * count, LANES), count)
    tiles = rows // TILE

    def sent():
        return remote(
            cotangent_ref.at[1 - mine], cotangent_all.at[own], sems.at[0], sems.at[1], partner
        )

    def returned():
        theirs = pl.ds(pl.multiple_of((1 - mine) * count, LANES), count)
        return [
            pltpu.make_async_copy(layer_ref.at[own], layer_out.at[mine], load_sems.at[8]),
            remote(
                layer_ref.at[theirs], layer_out.at[mine], sems.at[2], sems.at[3], partner
            ),
        ]

    def tile_loads(tile):
        there = pl.ds(tile * TILE, TILE)
        return [
            pltpu.make_async_copy(source.at[there], target.at[there], tile_sems.at[index, tile])
            for index, (source, target) in enumerate(
                ((mixed_hbm, mixed_ref), (item_hbm, item_ref))
            )
        ]

    def store(index):
        source, target = (
            (total, total_out), (unit, unit_out), (scale_ref, scale_out),
        )[index]
        return pltpu.make_async_copy(source, target, store_sems.at[index])

    def loads():
        copies = list(zip(vectors_hbm, vectors)) + [(cotangent_ref.at[mine], cotangent_all.at[own])]
        return [
            pltpu.make_async_copy(source, target, load_sems.at[index])
            for index, (source, target) in enumerate(copies)
        ]

    def over_tiles(size, body, carry, unroll=1):
        def run(index, state):
            return body(pl.ds(pl.multiple_of(index * size, size), size), state)

        return lax.fori_loop(0, rows // size, run, carry, unroll=unroll)

    @pl.when(step == 0)
    def _():
        for index in range(rows // TILE):
            for load in tile_loads(index):
                load.start()
        for load in loads():
            load.start()
        barrier = pltpu.get_barrier_semaphore()
        pl.semaphore_signal(barrier, inc=1, device_id=partner, device_id_type=MESH)
        pl.semaphore_wait(barrier, 1)
        sent().start()
        small_ref[...] = jnp.zeros_like(small_ref)
        for load in loads():
            load.wait()
        out_bias, gain, shift = vector(out_bias_ref), vector(attn_gain_ref), vector(attn_shift_ref)

        for index in range(rows // TILE):
            for load in tile_loads(index):
                load.wait()
            there = slice(index * TILE, index * TILE + TILE)
            attn = dot_nn(mixed_ref[there].astype(BF), out_weight_ref[...]) + out_bias
            standard, scale = normalized(item_ref[there].astype(F32) + attn)
            unit[there] = standard
            scale_ref[there] = jnp.broadcast_to(scale, (TILE, LANES))
            result = standard * gain + shift
            normed[there] = result.astype(BF)
            normed_t[:, there] = jnp.transpose(result).astype(BF)
        store(1).start()
        store(2).start()
        total[...] = jnp.zeros_like(total)

    @pl.when(step < blocks)
    def _():
        columns = [slice(begin, begin + TILE) for begin in range(0, width, TILE)]
        low = normed[...]
        following = dot_nn(low, up_ref[:, columns[0]])
        values = []
        for index, here in enumerate(columns):
            product = following
            if index + 1 < len(columns):
                following = dot_nn(low, up_ref[:, columns[index + 1]])
            bias = up_bias_ref[pl.ds(pl.multiple_of(step * width + here.start, LANES), TILE)]
            value, grade = gelu_and_slope(product + bias.astype(F32).reshape(1, TILE))
            values.append(value.astype(BF))
            active[step, :, here] = values[-1]
            slope[step, :, here] = grade.astype(BF)
        values = jnp.concatenate(values, axis=1)
        for here in columns:
            total[:, here] += dot_nn(values, down_ref[:, here])

    @pl.when(step == blocks)
    def _():
        sent().wait()
        gain, shift, bias = vector(ffn_gain_ref), vector(ffn_shift_ref), vector(down_bias_ref)
        first_gain, first_shift = vector(attn_gain_ref), vector(attn_shift_ref)

        def tile(there, sums):
            hidden = unit[there] * first_gain + first_shift + (total[there] + bias)
            standard, scale = normalized(hidden)
            layer_ref[there] = (standard * gain + shift).astype(BF)
            cotangent = cotangent_all[there].astype(F32)
            pulled = norm_pulled(cotangent * gain, standard, scale)
            total[there] = pulled
            low = pulled.astype(BF)
            d_branch[there] = low
            return (
                sums[0] + column_sum(low.astype(F32)),
                sums[1] + column_sum(cotangent * standard),
                sums[2] + column_sum(cotangent),
            )

        zero = jnp.zeros((1, width), F32)
        sums = over_tiles(64, tile, (zero, zero, zero), 4)
        for row, value in zip((5, 6, 7), sums):
            small_ref[row : row + 1] = value

        for copy in returned():
            copy.start()

        def turn(there, carry):
            d_branch_t[:, there] = jnp.transpose(d_branch[there].astype(F32)).astype(BF)
            return carry

        over_tiles(TILE, turn, 0, 3)

    @pl.when(step >= blocks)
    def _():
        block = step - blocks

        columns = [slice(begin, begin + TILE) for begin in range(0, width, TILE)]
        branch = d_branch[...]
        turned = d_branch_t[...]
        following = dot_nt(branch, down_ref[columns[0]])
        values = []
        for index, here in enumerate(columns):
            product = following
            if index + 1 < len(columns):
                following = dot_nt(branch, down_ref[columns[index + 1]])
            grad_down_ref[:, here] = dot_nn(turned, active[block, :, here]).astype(BF)
            d_up = (product * slope[block, :, here].astype(F32)).astype(BF)
            small_ref[pl.ds(8 + block, 1), here] = column_sum(d_up.astype(F32))
            values.append(d_up)
        values = jnp.concatenate(values, axis=1)
        turned = normed_t[...]
        for here in columns:
            grad_up_ref[:, here] = dot_nn(turned, values[:, here]).astype(BF)
            total[:, here] += dot_nt(values, up_ref[here])

    @pl.when(step == 2 * blocks - 1)
    def _():
        store(0).start()
        for copy in returned() + [store(0), store(1), store(2)]:
            copy.wait()


def fed_forward_and_back(
    item, mixed, cotangent, out_weight, up_weight, down_weight, vectors,
):
    rows, width = item.shape
    blocks = up_weight.shape[1] // width
    whole = pl.BlockSpec(memory_space=pltpu.VMEM)
    square = lambda kind: jax.ShapeDtypeStruct((rows, width), kind)
    later = lambda i: jnp.maximum(i - blocks, 0)
    return pl.pallas_call(
        feed_kernel,
        grid=(2 * blocks,),
        in_specs=[HBM, HBM, HBM, whole]
        + [
            pl.BlockSpec((width, width), lambda i: (0, lax.rem(i, blocks))),
            pl.BlockSpec((width, width), lambda i: (lax.rem(i, blocks), 0)),
        ]
        + [HBM] * 7,
        out_specs=[HBM] * 4
        + [
            pl.BlockSpec((width, width), lambda i: (later(i), 0)),
            pl.BlockSpec((width, width), lambda i: (later(i), 0)),
            whole,
        ],
        out_shape=[
            jax.ShapeDtypeStruct((2, rows // 2, width), BF), square(F32), square(F32),
            jax.ShapeDtypeStruct((rows, LANES), F32),
            jax.ShapeDtypeStruct((blocks * width, width), BF),
            jax.ShapeDtypeStruct((blocks * width, width), BF),
            jax.ShapeDtypeStruct((16, width), F32),
        ],
        scratch_shapes=[
            pltpu.VMEM((rows, width), BF),
            pltpu.VMEM((rows, width), F32),
            pltpu.VMEM((rows, width), BF),
            pltpu.VMEM((rows, width), BF),
            pltpu.VMEM((blocks, rows, width), BF),
            pltpu.VMEM((blocks, rows, width), BF),
            pltpu.VMEM((rows, width), F32),
            pltpu.VMEM((rows, LANES), F32),
            pltpu.VMEM((rows, width), BF),
            pltpu.VMEM((width, rows), BF),
            pltpu.VMEM((rows, width), F32),
            pltpu.VMEM((rows, width), BF),
            pltpu.VMEM((width, rows), BF),
            pltpu.SemaphoreType.DMA((4,)),
            pltpu.SemaphoreType.DMA((9,)),
            pltpu.SemaphoreType.DMA((2, rows // TILE)),
            pltpu.SemaphoreType.DMA((3,)),
        ]
        + [pltpu.VMEM(vector.shape, vector.dtype) for vector in vectors],
        compiler_params=pltpu.CompilerParams(
            collective_id=2, has_side_effects=True, vmem_limit_bytes=60 * MIB
        ),
        name="feed_forward",
    )(item, mixed, cotangent, out_weight, up_weight, down_weight, *vectors)


SLOTS = 4


def finish_kernel(
    main_ref, tail_ref, input_hbm, small_ref, diagonal_ref,
    down_ref, up_ref, out_ref, qkv_ref, input_ref, *refs,
):
    singles, (main_in, tail_in, slots, input_in, input_slot, in_sems, out_sems, item_sems) = (
        refs[:12], refs[12:],
    )
    mains, width = main_in.shape[0], main_in.shape[2]
    pairs, across = tail_in.shape[0], tail_in.shape[2]
    hidden = mains // 2
    blocks = mains + pairs

    def load(block):
        if block < mains:
            source, target = main_ref.at[pl.ds(block * width, width)], main_in.at[block]
        else:
            pair = block - mains
            source, target = tail_ref.at[pl.ds(pair * TAIL_ROWS, TAIL_ROWS)], tail_in.at[pair]
        return pltpu.make_async_copy(source, target, in_sems.at[block])

    def stores(block):
        slot, sem = slots.at[block % SLOTS], out_sems.at[block % SLOTS]
        if block < hidden:
            targets = [(slot, down_ref.at[pl.ds(block * width, width)])]
        elif block < mains:
            targets = [(slot, up_ref.at[:, pl.ds((block - hidden) * width, width)])]
        else:
            pair = block - mains
            targets = [
                (
                    slot.at[:, pl.ds(part * LANES, LANES)],
                    qkv_ref.at[:, pl.ds(part * width + pair * LANES, LANES)],
                )
                for part in range(3)
            ]
            down = pl.ds(0, TAIL_ROWS - width)
            targets.append(
                (slot.at[down, pl.ds(across, across)], out_ref.at[out_spot(pair, pairs, width)])
            )
        return [
            pltpu.make_async_copy(source, target, sem.at[index])
            for index, (source, target) in enumerate(targets)
        ]

    load_input = pltpu.make_async_copy(input_hbm, input_in, item_sems.at[0])
    store_input = pltpu.make_async_copy(input_slot, input_ref, item_sems.at[1])
    for block in range(blocks):
        load(block).start()
    load_input.start()
    for block in range(blocks):
        load(block).wait()
        if block >= SLOTS:
            for copy in stores(block - SLOTS):
                copy.wait()
        slot = block % SLOTS
        if block < hidden:
            slots[slot] = jnp.transpose(main_in[block].astype(F32))
        elif block < mains:
            slots[slot] = main_in[block].astype(F32)
        else:
            slots[slot, :, :across] = tail_in[block - mains, :width].astype(F32)
            slots[slot, : TAIL_ROWS - width, across:] = tail_in[block - mains, width:].astype(F32)
        for copy in stores(block):
            copy.start()
    load_input.wait()
    input_slot[...] = input_in[...].astype(F32)
    store_input.start()
    for row in range(8):
        singles[row][...] = small_ref[row]
    for row in range(hidden):
        singles[8][row * width : row * width + width] = small_ref[8 + row]
    heads, levels = singles[9].shape
    diagonals = diagonal_ref[...]
    level = lax.broadcasted_iota(jnp.int32, (LANES, LANES), 1)
    lane = lax.broadcasted_iota(jnp.int32, (LANES, LANES), 0)
    for table, (first, size, skip) in enumerate(((0, 4, 0), (4, 2, 1), (6, 2, 1))):
        total = jnp.zeros((heads, LANES), F32)
        for row in range(size):
            distance = lane + LANES * (row + skip - 2)
            chosen = (bucket(distance) == level).astype(F32)
            total = total + jnp.dot(
                diagonals[:, first + row, :], chosen, preferred_element_type=F32,
                precision=lax.Precision.HIGHEST,
            )
        singles[9 + table][...] = total[:, :levels]
    for block in range(blocks - SLOTS, blocks):
        for copy in stores(block):
            copy.wait()
    store_input.wait()


def finished(main, tail, grad_input, small, diagonals, hidden, levels):
    width = main.shape[1]
    heads = diagonals.shape[0]
    mains = main.shape[0] // width
    pairs = tail.shape[0] // TAIL_ROWS
    single = jax.ShapeDtypeStruct((width,), F32)
    table = jax.ShapeDtypeStruct((heads, levels), F32)
    dma = pltpu.SemaphoreType.DMA
    return pl.pallas_call(
        finish_kernel,
        in_specs=[HBM, HBM, HBM, VMEM, VMEM],
        out_specs=[HBM] * 5 + [VMEM] * 12,
        out_shape=[
            jax.ShapeDtypeStruct((hidden, width), F32),
            jax.ShapeDtypeStruct((width, hidden), F32),
            jax.ShapeDtypeStruct((width, width), F32),
            jax.ShapeDtypeStruct((width, 3 * width), F32),
            jax.ShapeDtypeStruct(grad_input.shape, F32),
        ]
        + [single] * 8
        + [jax.ShapeDtypeStruct((hidden,), F32)]
        + [table] * 3,
        scratch_shapes=[
            pltpu.VMEM((mains, width, width), BF),
            pltpu.VMEM((pairs, TAIL_ROWS, tail.shape[1]), BF),
            pltpu.VMEM((SLOTS, width, width), F32),
            pltpu.VMEM(grad_input.shape, BF),
            pltpu.VMEM(grad_input.shape, F32),
            dma((mains + pairs,)),
            dma((SLOTS, 4)),
            dma((2,)),
        ],
        compiler_params=pltpu.CompilerParams(vmem_limit_bytes=56 * MIB),
        name="finished",
    )(main, tail, grad_input, small, diagonals)


PIECE = 16


class Place:
    def __init__(self, depth):
        place = lax.axis_index("dp")
        self.depth = depth
        self.group = lax.div(place, 4 * depth)
        self.z = lax.rem(lax.div(place, 4), depth)
        self.bits = {
            "x": lax.axis_index("seq"),
            "c": lax.rem(place, 2),
            "y": lax.rem(lax.div(place, 2), 2),
            "a": lax.rem(self.z, 2),
            "b": lax.div(self.z, 2),
        }

    def partner(self, letters):
        bit = {
            letter: 1 - value if letter in letters else value
            for letter, value in self.bits.items()
        }
        z = self.z
        for letter, reach in (("a", 1), ("b", 2)):
            if letter in letters:
                z = z + reach - 2 * reach * self.bits[letter]
        return (bit["x"], (self.group * self.depth + z) * 4 + bit["y"] * 2 + bit["c"])

    def greet(self, met):
        barrier = pltpu.get_barrier_semaphore()
        for letters in met:
            pl.semaphore_signal(
                barrier, inc=1, device_id=self.partner(letters), device_id_type=MESH
            )
        pl.semaphore_wait(barrier, len(met))


def letters_of(depth):
    return "xy" + "ab"[: (depth - 1).bit_length()]


def parsed(routes, depth):
    kept = letters_of(depth)
    parts = []
    for route in routes.split():
        hops = ["".join(letter for letter in hop if letter in kept) for hop in route.split(".")]
        parts.append([hop for hop in hops if hop])
    return parts


def subsets(hop):
    return [
        "".join(letter for index, letter in enumerate(hop) if mask >> index & 1)
        for mask in range(1, 2 ** len(hop))
    ]


class Chunk:
    def __init__(self, place, depth, source, out_ref, offset, spot, scratch):
        _, self.begin, rows, first, columns, _, routes, _ = spot
        self.place, self.source, self.columns = place, source, pl.ds(first, columns)
        self.out_ref, self.out_begin = out_ref, offset + self.begin
        self.parts = parsed(routes, depth)
        self.half = rows // 2
        self.share = self.half // len(self.parts)
        self.hops = max(len(part) for part in self.parts)
        self.work, self.fresh, *landing, self.sends, self.receives, self.locals = scratch
        self.landing = {}
        self.sems = {}
        count = 2
        for part, hops in enumerate(self.parts):
            for hop, letters in enumerate(hops):
                self.landing[part, hop] = landing.pop(0)
                for way in range(2):
                    for index in range(2 ** len(letters) - 1):
                        self.sems[way, part, hop, index] = count
                        count += 1

    def aligned(self, value):
        return pl.multiple_of(value, PIECE)

    def size(self, part, hop):
        return self.share >> sum(len(letters) for letters in self.parts[part][: hop + 1])

    def spot(self, part, hop, other=""):
        start = part * self.share
        for level in range(hop + 1):
            for index, letter in enumerate(self.parts[part][level]):
                bit = self.place.bits[letter]
                if level == hop and letter in other:
                    bit = 1 - bit
                start = start + bit * (self.size(part, level) << index)
        return start

    def out(self, core):
        begin = self.aligned(self.out_begin + core * self.half)
        return self.out_ref.at[pl.ds(begin, self.half), self.columns]

    def held(self, buffer, begin, size):
        return buffer.at[pl.ds(self.aligned(begin), size)]

    def copy(self, index, source, target, letters):
        return remote(
            source, target, self.sends.at[index], self.receives.at[index],
            self.place.partner(letters),
        )

    def pair_down(self):
        core = self.place.bits["c"]
        at = lambda c: self.source.at[
            pl.ds(self.aligned(self.begin + c * self.half), self.half), self.columns
        ]
        return [
            self.copy(0, at(1 - core), self.fresh, "c"),
            pltpu.make_async_copy(at(core), self.work, self.locals.at[0]),
        ]

    def pair_up(self, arriving):
        core = self.place.bits["c"]
        return [
            self.copy(1, self.fresh, self.out(1 - core if arriving else core), "c"),
            pltpu.make_async_copy(self.fresh, self.out(core), self.locals.at[1]),
        ]

    def at_hop(self, hop):
        return [
            (part, hops[hop]) for part, hops in enumerate(self.parts) if hop < len(hops)
        ]

    def down(self, hop):
        copies = []
        for part, letters in self.at_hop(hop):
            size = self.size(part, hop)
            for index, other in enumerate(subsets(letters)):
                copies.append(
                    self.copy(
                        self.sems[0, part, hop, index],
                        self.held(self.work, self.spot(part, hop, other), size),
                        self.landing[part, hop].at[index], other,
                    )
                )
        return copies

    def up(self, hop, arriving):
        copies = []
        for part, letters in self.at_hop(hop):
            mine = self.spot(part, hop)
            size = self.size(part, hop)
            for index, other in enumerate(subsets(letters)):
                target = self.spot(part, hop, other) if arriving else mine
                copies.append(
                    self.copy(
                        self.sems[1, part, hop, index], self.held(self.fresh, mine, size),
                        self.held(self.fresh, target, size), other,
                    )
                )
        return copies

    def add(self, begin, sources, size):
        step = 64 if size % 64 == 0 else 32 if size % 32 == 0 else PIECE

        def body(index, carry):
            offset = self.aligned(index * step)
            there = pl.ds(self.aligned(begin + offset), step)
            total = self.work[there]
            if len(sources) == 1:
                total = total + sources[0][pl.ds(offset, step)]
            else:
                total = total.astype(F32)
                for source in sources:
                    total = total + source[pl.ds(offset, step)].astype(F32)
            self.work[there] = total.astype(BF)
            return carry

        lax.fori_loop(0, size // step, body, 0)

    def stage(self, number):
        hops = self.hops
        ended, started = [], []
        if number == 0:
            started = self.pair_down()
        elif number == 1:
            ended = self.pair_down()
            started = self.down(0)
        elif number <= hops:
            ended = self.down(number - 2)
            started = self.down(number - 1)
        elif number == hops + 1:
            ended = self.down(hops - 1)
            started = self.up(hops - 1, False)
        elif number <= 2 * hops:
            level = 2 * hops + 1 - number
            ended = self.up(level, True)
            started = self.up(level - 1, False)
        elif number == 2 * hops + 1:
            ended = self.up(0, True)
            started = self.pair_up(False)
        else:
            ended = self.pair_up(True)
        for copy in ended:
            copy.wait()
        if number == 1:
            self.add(0, [self.fresh], self.half)
        elif 2 <= number <= hops + 1:
            hop = number - 2
            for part, letters in self.at_hop(hop):
                landing = self.landing[part, hop]
                sources = [landing.at[index] for index in range(2 ** len(letters) - 1)]
                self.add(self.spot(part, hop), sources, self.size(part, hop))
        if number == hops + 1:
            for part, route in enumerate(self.parts):
                last = len(route) - 1
                there = pl.ds(self.aligned(self.spot(part, last)), self.size(part, last))
                self.fresh[there] = self.work[there]
        for copy in started:
            copy.start()


def chunk_scratch(spot, depth):
    _, _, rows, _, columns, _, routes, _ = spot
    parts = parsed(routes, depth)
    landing = []
    copies = 2
    for hops in parts:
        size = rows // 2 // len(parts)
        for letters in hops:
            size >>= len(letters)
            others = 2 ** len(letters) - 1
            copies += 2 * others
            landing.append(pltpu.VMEM((others, size, columns), BF))
    dma = pltpu.SemaphoreType.DMA
    return (
        [pltpu.VMEM((rows // 2, columns), BF)] * 2
        + landing
        + [dma((copies,)), dma((copies,)), dma((2,))]
    )


def loads_of(hop, size):
    if "x" in hop and "y" in hop:
        return [("x", 2 * size), ("y", 2 * size)]
    if hop in ("x", "y"):
        return [(hop, size)]
    if "a" in hop and "b" in hop:
        return [("end", 3 * size), ("middle", 4 * size)]
    return [("end", size), ("middle", 2 * size)] if hop == "b" else [("end", size)]


def planned(chunks, work, depth, hop_count):
    latency, issue, link, pair = 2.5, 0.08, 115e3, 600e3
    free = {}
    now = 3.0
    chains = []
    for rows, columns, need, routes, _ in chunks:
        parts = parsed(routes, depth)
        sizes = [rows // 2 // len(parts)] * len(parts)
        down = []
        for hop in range(max(len(part) for part in parts)):
            loads, copies, added = [], 0, 0
            for index, part in enumerate(parts):
                if hop < len(part):
                    sizes[index] >>= len(part[hop])
                    others = 2 ** len(part[hop]) - 1
                    loads += loads_of(part[hop], sizes[index])
                    copies += others
                    added += sizes[index] * others
            down.append((loads, copies, added, columns))
        first = [([("core", rows // 2)], 1.5, rows // 2, columns)]
        last = [([("core", rows // 2)], 1, 0, columns)]
        chains.append((need, first + down + down[::-1] + last))
    chains.append((len(work), [([("core", 16)], 2, 0, 768)] * hop_count))
    ranks = [chunk[4] for chunk in chunks] + [0]
    position = [0] * len(chains)
    ready = [0.0] * len(chains)
    order = [[] for _ in range(len(work) + 1)]
    done = 0
    while True:
        open_ones = [
            (ranks[i], ready[i], i) for i, (need, chain) in enumerate(chains)
            if position[i] <= len(chain) and need <= done
        ]
        due = [entry for entry in open_ones if entry[1] <= now]
        if not due and done < len(work):
            now += work[done]
            done += 1
            continue
        if not open_ones:
            return order
        _, when, index = min(due) if due else min(open_ones, key=lambda entry: entry[1])
        now = max(now, when)
        chain = chains[index][1]
        stage = position[index]
        order[done].append((index, stage))
        if 0 < stage <= len(chain) // 2:
            now += 1e-6 * chain[stage - 1][2] * chain[stage - 1][3]
        if stage < len(chain):
            loads, copies, _, columns = chain[stage]
            now += issue * copies
            end = now
            for lane, rows in loads:
                rate = pair if lane == "core" else link / 2
                free[lane] = max(now, free.get(lane, 0.0)) + 2 * rows * columns / rate
                end = max(end, free[lane])
            ready[index] = end + latency
        position[index] += 1


def last_kernel(
    depth, plan, orders, counts, *refs,
):
    (meta_ref, rows_ref, projected_hbm, mixed_hbm, log_ref, first_hbm, second_hbm,
     key_image_hbm, bias_hbm, small_ref, gain_ref, item_hbm, weight_hbm, total_hbm, unit_hbm, scale_hbm,
     out_weight_hbm, grad_down_ref, grad_up_ref,
     main_out, tail_out, small_out, diagonal_out, input_out,
     *scratch) = refs
    static, scratch = scratch[:6], scratch[6:]
    (k_ref, v_ref, mixed_ref, grad_ref, first_ref, second_ref, key_image_ref, bias_ref, pair_sems,
     item_ref, weight_ref, d_hidden_ref, unit_ref, scale_ref, load_sems, d_project, item_t, tail, input_grad,
     small_in, diagonal_in, small_sems, item_sems, *scratch) = scratch
    out_weight_ref = item_t
    place = Place(depth)
    step = pl.program_id(0)
    pairs = k_ref.shape[0]
    rows, width = item_hbm.shape
    count = rows // 2
    x = place.bits["x"]
    hidden = grad_down_ref.shape[0]
    sources = ((grad_down_ref, main_out, 0), (grad_up_ref, main_out, hidden), (tail, tail_out, 0))
    chunks = []
    for spot, pieces in zip(plan, counts):
        chunks.append(Chunk(place, depth, *sources[spot[0]], spot, scratch[:pieces]))
        scratch = scratch[pieces:]
    hop_letters = "c" + letters_of(depth)
    wide_hbm = (first_hbm, second_hbm, key_image_hbm, bias_hbm)
    wide_refs = (first_ref, second_ref, key_image_ref, bias_ref)

    def pair_loads(pair):
        copies = []
        held = ((projected_hbm, k_ref, width), (projected_hbm, v_ref, 2 * width))
        for source, target, first in held:
            columns = pl.ds(pl.multiple_of(first + pair * LANES, LANES), LANES)
            copies.append((source.at[:, columns], target.at[pair]))
        heads = pl.ds(2 * pair, 2)
        for source, target in zip(wide_hbm, wide_refs):
            copies.append((source.at[heads], target.at[heads]))
        return [
            pltpu.make_async_copy(source, target, pair_sems.at[pair, index])
            for index, (source, target) in enumerate(copies)
        ]

    def loads(first):
        if first:
            copies = [
                (total_hbm, d_hidden_ref), (unit_hbm, unit_ref), (scale_hbm, scale_ref),
                (out_weight_hbm, out_weight_ref), (item_hbm, item_ref),
            ]
            copies += [
                (mixed_hbm.at[:, pl.ds(pair * LANES, LANES)], mixed_ref.at[pair])
                for pair in range(pairs)
            ]
        else:
            copies = [(weight_hbm, weight_ref)]
        return [
            pltpu.make_async_copy(source, target, load_sems.at[0 if first else 1, index])
            for index, (source, target) in enumerate(copies)
        ]

    def back_to_attention():
        gain = vector(gain_ref)

        def tile(index, sums):
            there = pl.ds(pl.multiple_of(index * 64, 64), 64)
            d_normed = d_hidden_ref[there]
            standard = unit_ref[there]
            d_hidden = norm_pulled(d_normed * gain, standard, scale_ref[there, :1])
            d_hidden_ref[there] = d_hidden
            low = d_hidden.astype(BF)
            input_grad[there] = low
            return (
                sums[0] + column_sum(low.astype(F32)),
                sums[1] + column_sum(d_normed * standard),
                sums[2] + column_sum(d_normed),
            )

        zero = jnp.zeros((1, width), F32)
        sums = lax.fori_loop(0, rows // 64, tile, (zero, zero, zero), unroll=4)
        for row, value in zip((2, 3, 4), sums):
            small_out[row : row + 1] = value
        low = input_grad[...]
        down = TAIL_ROWS - width
        for begin in range(0, width, down):
            first = begin // LANES
            several = range(first, first + down // LANES)
            d_mixed = dot_nt(low, out_weight_ref[begin : begin + down]).astype(BF)
            for index, pair in enumerate(several):
                grad_ref[pair] = d_mixed[:, index * LANES : index * LANES + LANES]
            turned = jnp.concatenate(
                [jnp.transpose(mixed_ref[pair]).astype(BF) for pair in several], axis=0
            )
            for pair in range(pairs):
                rows_of, across = out_spot(pair, pairs, width)
                if rows_of.start == begin:
                    product = dot_nn(turned, low[:, across.start : across.start + across.size])
                    base = pair * TAIL_ROWS + width
                    tail[base : base + down] = product.astype(BF)

    def input_copies():
        return [
            pltpu.make_async_copy(
                input_grad.at[pl.ds(pl.multiple_of(x * count, LANES), count)], input_out.at[x],
                item_sems.at[0],
            ),
            remote(
                input_grad.at[pl.ds(pl.multiple_of((1 - x) * count, LANES), count)],
                input_out.at[x], item_sems.at[1], item_sems.at[2], place.partner("x"),
            ),
        ]

    def small_copies(hop):
        return [
            remote(source, landing.at[hop], small_sems.at[0, kind, hop],
                   small_sems.at[1, kind, hop], place.partner(hop_letters[hop]))
            for kind, (source, landing) in enumerate(
                ((small_out, small_in), (diagonal_out, diagonal_in))
            )
        ]

    def small_stage(hop):
        if hop > 0:
            for copy in small_copies(hop - 1):
                copy.wait()
            small_out[...] = small_out[...] + small_in[hop - 1]
            diagonal_out[...] = diagonal_out[...] + diagonal_in[hop - 1]
        if hop < len(hop_letters):
            for copy in small_copies(hop):
                copy.start()

    def perform(slot):
        for index, stage in orders[slot]:
            if index == len(chunks):
                small_stage(stage)
            else:
                chunks[index].stage(stage)

    @pl.when(step == 0)
    def _():
        for copy in pair_loads(0) + loads(True):
            copy.start()
        met = set(hop_letters)
        for chunk in chunks:
            for hops in chunk.parts:
                for letters in hops:
                    met.update(subsets(letters))
        place.greet(sorted(met))
        small_out[...] = small_ref[...]

    for pair in range(pairs):
        @pl.when(step == pair)
        def _(pair=pair):
            perform(pair)

    @pl.when(step == 0)
    def _():
        for pair in range(1, pairs):
            for copy in pair_loads(pair):
                copy.start()
        for copy in loads(False):
            copy.start()
        static_prepare(meta_ref, static)
        for copy in loads(True):
            copy.wait()
        back_to_attention()
        for tile in range(rows // TILE):
            there = slice(tile * TILE, tile * TILE + TILE)
            item_t[:, there] = jnp.transpose(item_ref[there].astype(F32)).astype(BF)

    for copy in pair_loads(step):
        copy.wait()
    (dq_even, dk_even, dv_even), (dq_odd, dk_odd, dv_odd) = [
        head_back(
            parity, step, rows_ref, wide_refs, k_ref, v_ref, mixed_ref, grad_ref, log_ref,
            static, diagonal_out,
        )
        for parity in range(2)
    ]
    even = own_lanes(0, rows)
    pieces = [
        jnp.transpose(jnp.concatenate([dq_even, dq_odd], axis=0)).astype(BF),
        jnp.where(even, dk_even, dk_odd).astype(BF),
        jnp.where(even, dv_even, dv_odd).astype(BF),
    ]
    for part, piece in enumerate(pieces):
        d_project[:, pl.ds(pl.multiple_of(part * width + step * LANES, LANES), LANES)] = piece
    slab = pl.ds(pl.multiple_of(step * TAIL_ROWS, TAIL_ROWS), width)
    tail[slab] = dot_nn(item_t[...], jnp.concatenate(pieces, axis=1)).astype(BF)

    @pl.when(step == 0)
    def _():
        for copy in loads(False):
            copy.wait()

    @pl.when(step == pairs - 1)
    def _():
        perform(pairs)
        for begin in range(0, width, TILE):
            here = slice(begin, begin + TILE)
            total = d_hidden_ref[:, here] + dot_nt(d_project[...], weight_ref[here])
            input_grad[:, here] = total.astype(BF)
        for copy in input_copies():
            copy.start()
        for begin in range(0, width, TILE):
            here = slice(begin, begin + TILE)
            there = slice(2 * width + begin, 2 * width + begin + TILE)
            small_out[0:1, here] = column_sum(d_project[:, here].astype(F32))
            small_out[1:2, here] = column_sum(d_project[:, there].astype(F32))
        perform(pairs + 1)
        for copy in input_copies():
            copy.wait()


TAIL_ROWS = 1024


def out_spot(pair, pairs, width):
    down = TAIL_ROWS - width
    across = width * width // (pairs * down)
    per_row = width // across
    return (
        pl.ds(pair // per_row * down, down),
        pl.ds(pair % per_row * across, across),
    )


def summed_with_attention_back(
    meta_columns, meta_rows, projected, mixed, logs, wide_arrays, item, qkv_weight,
    total, unit, scale, out_weight, attn_gain, small, grad_down, grad_up,
):
    size = lax.axis_size("dp")
    depth = 4 if size % 16 == 0 else size // 4
    rows, width = item.shape
    pairs = width // LANES
    hidden = grad_down.shape[0]
    hops = len(letters_of(depth)) + 1
    work = [6.8] * pairs + [4.0]
    tall, wide, slim = 1024, 3 * LANES, 2 * LANES
    plan = [
        (0, 0, 2 * tall, 0, width, 0, "a.b.x.y x.y.a.b", 1),
        (0, 2 * tall, tall, 0, width, 0, "x.a.y.b y.a.b.x", 2),
        (1, 0, 3 * tall, 0, slim, 0, "a.b.x.y y.x.a.b", 4),
        (1, 0, 3 * tall, slim, slim, 0, "y.a.x.b x.y.a.b", 0),
        (1, 0, 3 * tall, 2 * slim, slim, 0, "x.y.a.b y.x.a.b", 2),
        (2, 0, tall, 0, wide, 1, "y.x.a.b a.b.x.y", 3),
        (2, tall, tall, 0, wide, 2, "xy.a.b", 2),
        (2, 2 * tall, tall, 0, wide, 3, "x.y.ab y.ab.x", 3),
        (2, 3 * tall, tall, 0, wide, 4, "xy.a.b", 1),
        (2, 4 * tall, tall, 0, wide, 5, "xy.a.b", 1),
        (2, 5 * tall, tall, 0, wide, 6, "ab.y.x y.ab.x", 2),
    ]
    orders = planned([(spot[2],) + spot[4:] for spot in plan], work, depth, hops)

    whole = pl.BlockSpec(memory_space=pltpu.VMEM)
    diagonals = jax.ShapeDtypeStruct((2 * pairs, 8, LANES), F32)
    dma = pltpu.SemaphoreType.DMA
    scratch = []
    for spot in plan:
        scratch.append(chunk_scratch(spot, depth))
    main, tail, small, diagonals, grad_input = pl.pallas_call(
        functools.partial(last_kernel, depth, plan, orders, [len(pieces) for pieces in scratch]),
        grid=(pairs,),
        in_specs=[whole] * 2 + [HBM] * 2 + [whole] + [HBM] * 4 + [whole] * 2 + [HBM] * 8,
        out_specs=[HBM, HBM, whole, whole, HBM],
        out_shape=[
            jax.ShapeDtypeStruct((2 * hidden, width), BF),
            jax.ShapeDtypeStruct((pairs * TAIL_ROWS, 3 * LANES), BF),
            jax.ShapeDtypeStruct(small.shape, F32),
            diagonals,
            jax.ShapeDtypeStruct((2, rows // 2, width), BF),
        ],
        scratch_shapes=[pltpu.VMEM((rows, LANES), BF)] * 3
        + [pltpu.VMEM((LANES, rows), BF)] * 3
        + [pltpu.VMEM((pairs, rows, LANES), kind) for kind in (BF, BF, F32, BF)]
        + [pltpu.VMEM(array.shape, BF) for array in wide_arrays]
        + [
            dma((pairs, 6)),
            pltpu.VMEM((rows, width), BF),
            pltpu.VMEM((width, 3 * width), BF),
            pltpu.VMEM((rows, width), F32),
            pltpu.VMEM((rows, width), F32),
            pltpu.VMEM((rows, LANES), F32),
            dma((2, 5 + pairs)),
            pltpu.VMEM((rows, 3 * width), BF),
            pltpu.VMEM((width, rows), BF),
            pltpu.VMEM((pairs * TAIL_ROWS, 3 * LANES), BF),
            pltpu.VMEM((rows, width), BF),
            pltpu.VMEM((hops,) + small.shape, F32),
            pltpu.VMEM((hops,) + diagonals.shape, F32),
            dma((2, 2, hops)),
            dma((3,)),
        ]
        + [piece for pieces in scratch for piece in pieces],
        compiler_params=pltpu.CompilerParams(
            collective_id=0, has_side_effects=True, vmem_limit_bytes=62 * MIB
        ),
        name="summed_with_attention_back",
    )(meta_columns, meta_rows, projected, mixed, logs, *wide_arrays,
      small, attn_gain, item, qkv_weight, total, unit, scale, out_weight, grad_down, grad_up)
    span = 4 * depth
    if size > span:
        groups = [list(range(first, size, span)) for first in range(span)]
        main, tail, small, diagonals = lax.psum(
            (main.astype(F32), tail.astype(F32), small, diagonals), "dp",
            axis_index_groups=groups,
        )
        main, tail = main.astype(BF), tail.astype(BF)
    return main, tail, small, diagonals, grad_input


def per_device(
    layer_in, segment, key_mask, position, layout_x, layout_y,
    qkv_weight, query_bias, value_bias, out_weight, out_bias, attn_gain, attn_shift,
    up_weight, up_bias, down_weight, down_bias, ffn_gain, ffn_shift,
    text_table, horiz_table, vert_table, cotangent,
):
    width = layer_in.shape[-1]
    item, projected, meta_columns, meta_rows, table_rows = projected_item(
        layer_in, (segment, key_mask, position, layout_x, layout_y),
        qkv_weight, query_bias, value_bias, (text_table, horiz_table, vert_table),
    )
    mixed, logs, *wide_arrays = attention_forward(meta_columns, meta_rows, table_rows, projected, width)
    layer_out, total, unit, scale, grad_down, grad_up, small = fed_forward_and_back(
        item, mixed, cotangent, out_weight, up_weight, down_weight,
        (out_bias, attn_gain, attn_shift, up_bias, down_bias, ffn_gain, ffn_shift),
    )
    main, tail, small, diagonals, grad_input = summed_with_attention_back(
        meta_columns, meta_rows, projected, mixed, logs, wide_arrays, item, qkv_weight,
        total, unit, scale, out_weight, attn_gain, small, grad_down, grad_up,
    )
    done = finished(
        main, tail, grad_input, small, diagonals, up_weight.shape[1], text_table.shape[0]
    )
    sum_down, sum_up, sum_out, sum_qkv, grad_input = done[:5]
    singles, tables = done[5:14], [t.T for t in done[14:]]
    return (
        layer_out, grad_input, sum_qkv, singles[0], singles[1], sum_out, singles[2], singles[3],
        singles[4], sum_up, singles[8], sum_down, singles[5], singles[6], singles[7],
        tables[0], tables[1], tables[2],
    )


def solution(mesh):
    rows = P("dp", "seq", None)
    marks_spec = P("dp", "seq")
    return jax.shard_map(
        per_device,
        mesh=mesh,
        in_specs=(rows,) + (marks_spec,) * 5 + (P(),) * 16 + (rows,),
        out_specs=(rows, rows) + (P(),) * 16,
        check_vma=False,
    )
```
